32 devices in a mesh: blk: 8 (over z, x), col: 4 (over y, core).
Axes of the slice: x: 2, y: 2, z: 4, core: 2. Of those that a mesh axis runs over, the one named last changes fastest.
Arguments:
- frames: bfloat16 [4, 2048, 440], P(None, ('blk', 'col')), may hold values from -6 to 6
- labels: int32 [4, 2048], P(None, ('blk', 'col')), may hold values from 0 to 9303
- mask: int32 [4, 2048], P(None, ('blk', 'col')), may hold values from 0 to 1, as said below
- w_input: float32 [440, 2048], P(None, 'col'), may hold values from -0.25 to 0.25
- w_hidden: float32 [2048, 2048], P('blk', 'col'), may hold values from -0.125 to 0.125
- w_output: float32 [2048, 9304], P('blk', 'col'), may hold values from -0.25 to 0.25
- biases: float32 [4, 3350], P('col'), may hold values from -1 to 1
- mom_input: float32 [440, 2048], P(None, 'col'), may hold values from -2.0343273e-06 to 2.0343273e-06
- mom_hidden: float32 [2048, 2048], P('blk', 'col'), may hold values from -2.0343273e-06 to 2.0343273e-06
- out_first: float32 [2048, 9304], P('blk', 'col'), may hold values from -2.0343273e-06 to 2.0343273e-06
- out_second: float32 [2048, 9304], P('blk', 'col'), may hold values from 8.2769756e-15 to 3.3107902e-14
- bias_first: float32 [4, 3350], P('col'), may hold values from -2.0343274e-05 to 2.0343274e-05
- bias_second: float32 [4, 3350], P('col'), may hold values from 8.2769756e-13 to 3.3107902e-12
- res_input: bfloat16 [8, 440, 2048], P('blk', None, 'col'), may hold values from -6.055832e-05 to 6.055832e-05
- res_hidden: bfloat16 [8, 2048, 2048], P('blk', None, 'col'), may hold values from -6.055832e-05 to 6.055832e-05
- res_output: bfloat16 [8, 2048, 9304], P('blk', None, 'col'), may hold values from -6.055832e-05 to 6.055832e-05
Outputs:
- loss_sum: float32 [], replicated
- clip_norm: float32 [], replicated
- new_input: float32 [440, 2048], P(None, 'col')
- new_hidden: float32 [2048, 2048], P('blk', 'col')
- new_output: float32 [2048, 9304], P('blk', 'col')
- new_biases: float32 [4, 3350], P('col')
- next_mom_input: float32 [440, 2048], P(None, 'col')
- next_mom_hidden: float32 [2048, 2048], P('blk', 'col')
- next_out_first: float32 [2048, 9304], P('blk', 'col')
- next_out_second: float32 [2048, 9304], P('blk', 'col')
- next_bias_first: float32 [4, 3350], P('col')
- next_bias_second: float32 [4, 3350], P('col')
- next_res_input: float32 [8, 440, 2048], P('blk', None, 'col')
- next_res_hidden: float32 [8, 2048, 2048], P('blk', None, 'col')
- next_res_output: float32 [8, 2048, 9304], P('blk', None, 'col')
The draws below stay inside these ranges and needn't reach their ends.
Inputs may be any that keep to these rules, and one draw needn't show every extreme that they name: `mask`: each device's slots in a micro-batch hold live frames from the first slot on, with scattered dead slots among them.
All inputs are finite; a program needn't handle non-finite values. Where the reference program divides by a largest or mean magnitude, that divisor is 1e-20 or more.
Results may differ from the reference program's by a relative error of at most 0.002.
The reference program's roundings to bfloat16 on the way count: a program that leaves them out, or rounds other values in their place, can miss the bound.
Values may be sent and summed in bfloat16 or wider, within the bound.
A program may use at most 320 MiB of HBM per device.

```python
import math
import jax
import jax.numpy as jnp
import numpy as np
from jax import lax

D_IN = 440
H = 2048
S = 9304
FR_DEV = 64
MB = 4
NS = 5
STEP = 5
FRAMES = 2048
BIAS_COL = 3350
N_BLK = 8
N_COL = 4


def draw_mask(key, part):
    key = jax.random.fold_in(key, 11)
    first_key, second_key = jax.random.split(key)
    devices = N_BLK * N_COL
    device_ids = jnp.arange(devices)
    rank = device_ids // N_COL + device_ids % N_COL
    highest = N_BLK - 1 + N_COL - 1
    live_runs = FR_DEV // 4 + 3 * FR_DEV // 4 * rank // highest
    jitter = jax.random.randint(first_key, (MB, devices), 0, FR_DEV // 8 + 1)
    live_runs = jnp.minimum(live_runs[None, :] + jitter, FR_DEV)
    position = jnp.arange(FR_DEV)
    inside = position[None, None, :] < live_runs[:, :, None]
    holes = jax.random.randint(second_key, (MB, devices, FR_DEV), 0, 8) != 0
    return (inside & holes).astype(jnp.int32).reshape(MB, devices * FR_DEV)


def place_ends(array, key, least, top_value):
    shape = array.shape
    place = [jax.random.randint(jax.random.fold_in(key, axis), (), 0, shape[axis]) for axis in range(len(shape))]
    array = array.at[tuple(place)].set(least)
    longest = shape.index(max(shape))
    place[longest] = (place[longest] + 1) % shape[longest]
    return array.at[tuple(place)].set(top_value)


def shard_levels(rng, dims, cuts, smallest, top_value):
    def one(dim, blocks):
        steps = jax.random.uniform(jax.random.fold_in(jax.random.fold_in(rng, 6), dim), (blocks,), jnp.float32, smallest / len(cuts), top_value / len(cuts))
        return jnp.repeat(jnp.exp(steps), dims[dim] // blocks).reshape((-1,) + (1,) * (len(dims) - dim - 1))

    factor_of = one(*cuts[0])
    for cut in cuts[1:]:
        factor_of = factor_of * one(*cut)
    return factor_of


def cumulative_ranks(number_of, slope):
    loads = [(1 << 20) // math.isqrt(grade ** slope) + 1 for grade in range(1, number_of + 1)]
    deviation = 1 + sum(loads) // (1 << 30)
    return np.cumsum(np.array([max(1, weight // deviation) for weight in loads]))


def ranked_ids(rng, dims, count, slope):
    table = cumulative_ranks(count, slope)
    lot = jax.random.randint(jax.random.fold_in(rng, 1), dims, 0, int(table[count - 1]))
    standing = jnp.searchsorted(jnp.asarray(table, jnp.int32), lot, side="right")
    return jax.random.permutation(jax.random.fold_in(rng, 2), count)[standing].astype(jnp.int32)


def gaussian(stream_key, extent, scale, most, cuts=(), kind=jnp.bfloat16):
    array = jax.random.normal(stream_key, extent, jnp.float32) * scale
    if len(cuts) > 0:
        array = shard_levels(stream_key, extent, cuts, -0.22, 0.18) * array
    return jnp.clip(array, min=-most, max=most).astype(kind)


def setup_inputs(seed: int = 0) -> dict:
    streams_of = jax.random.split(jax.random.key(seed), 17)
    return {
        "frames": gaussian(streams_of[0], (MB, FRAMES, D_IN), 1.0, 6.0, ((1, 32),)),
        "labels": place_ends(ranked_ids(streams_of[1], (MB, FRAMES), S, 2), jax.random.fold_in(streams_of[1], 3), 0, S - 1).astype(jnp.int32),
        "mask": draw_mask(jax.random.fold_in(streams_of[16], 71), 0),
        "w_input": gaussian(streams_of[3], (D_IN, H), D_IN ** -0.5, 0.25, ((1, 4),), jnp.float32),
        "w_hidden": gaussian(streams_of[4], (H, H), H ** -0.5, 0.125, ((0, 8), (1, 4)), jnp.float32),
        "w_output": gaussian(streams_of[5], (H, S), (H // 4) ** -0.5, 0.25, ((0, 8), (1, 4)), jnp.float32),
        "biases": gaussian(streams_of[6], (N_COL, BIAS_COL), 0.2, 1.0, ((0, 4),), jnp.float32),
        "mom_input": gaussian(streams_of[7], (D_IN, H), (0.002 / (D_IN * H + H * H + H * S + 2 * H + S) ** 0.5), 2.0343272808531765e-06, ((1, 4),), jnp.float32),
        "mom_hidden": gaussian(streams_of[8], (H, H), (0.002 / (D_IN * H + H * H + H * S + 2 * H + S) ** 0.5), 2.0343272808531765e-06, ((0, 8), (1, 4)), jnp.float32),
        "out_first": gaussian(streams_of[9], (H, S), (0.002 / (D_IN * H + H * H + H * S + 2 * H + S) ** 0.5), 2.0343272808531765e-06, ((0, 8), (1, 4)), jnp.float32),
        "out_second": jnp.clip(jnp.exp(math.log(3.310790227042948e-14) - 1.3862944 * jax.random.uniform(streams_of[10], (H, S), jnp.float32) ** shard_levels(streams_of[10], (H, S), ((0, 8), (1, 4)), -0.2, 0.2)), 8.27697556760737e-15, 3.310790227042948e-14),
        "bias_first": gaussian(streams_of[11], (N_COL, BIAS_COL), (0.02 / (D_IN * H + H * H + H * S + 2 * H + S) ** 0.5), 2.0343273718026467e-05, ((0, 4),), jnp.float32),
        "bias_second": jnp.clip(jnp.exp(math.log(3.310790227042948e-12) - 1.3862944 * jax.random.uniform(streams_of[12], (N_COL, BIAS_COL), jnp.float32) ** shard_levels(streams_of[12], (N_COL, BIAS_COL), ((0, 4),), -0.2, 0.2)), 8.27697556760737e-13, 3.310790227042948e-12),
        "res_input": gaussian(streams_of[13], (N_BLK, D_IN, H), (0.3 * (N_COL * MB * FR_DEV) ** 0.5 / (N_BLK * N_COL * MB * FR_DEV) / S ** 0.5), 6.0558319091796875e-05, ((0, 8), (2, 4))),
        "res_hidden": gaussian(streams_of[14], (N_BLK, H, H), (0.3 * (N_COL * MB * FR_DEV) ** 0.5 / (N_BLK * N_COL * MB * FR_DEV) / S ** 0.5), 6.0558319091796875e-05, ((0, 8), (2, 4))),
        "res_output": gaussian(streams_of[15], (N_BLK, H, S), (0.3 * (N_COL * MB * FR_DEV) ** 0.5 / (N_BLK * N_COL * MB * FR_DEV) / S ** 0.5), 6.0558319091796875e-05, ((0, 8), (2, 4))),
    }


@jax.custom_vjp
def low(v):
    return lax.optimization_barrier(v.astype(jnp.bfloat16)).astype(jnp.float32)

@jax.custom_vjp
def low_back(v):
    return v

def low_keep(v):
    return (low(v), None)

def low_pass(kept, grad):
    return (grad,)

def back_keep(v):
    return (v, None)

def back_low(kept, grad):
    return (low(grad),)
low.defvjp(low_keep, low_pass)
low_back.defvjp(back_keep, back_low)
NS_A = 3.4445
NS_B = -4.775
NS_C = 2.0315
CLIP = 0.002
LR_MUON = 0.1
WD_MUON = 0.01
LR_ADAM = 0.03
WD_ADAM = 0.1

def precise(left_side, right_side):
    return jnp.dot(left_side, right_side, precision=lax.Precision.HIGHEST, preferred_element_type=jnp.float32)

def split_biases(biases):
    width = H // N_COL
    return (biases[:, :width].reshape(H), biases[:, width:2 * width].reshape(H), biases[:, 2 * width:].reshape(S))

def rows_loss(rounded, pieces, inputs, row_tags):
    z_one = low_back(precise(inputs, rounded[0]) + pieces[0])
    h_one = low(jax.nn.sigmoid(z_one))
    z_two = low_back(precise(h_one, rounded[1]) + pieces[1])
    h_two = low(jax.nn.sigmoid(z_two))
    logits = low_back(precise(h_two, rounded[2]) + pieces[2])
    row_top = lax.optimization_barrier(jnp.max(logits, axis=1, keepdims=True))
    log_total = row_top[:, 0] + jnp.log(lax.optimization_barrier(jnp.sum(jnp.exp(logits - row_top), axis=1)))
    picked = lax.optimization_barrier(jnp.sum(jnp.where(jnp.arange(S)[None, :] == row_tags[:, None], logits, 0.0), axis=1))
    return jnp.sum(jnp.where(row_tags >= 0, log_total - picked, 0.0))

def squash(gradient, resid):
    value = gradient + resid.astype(jnp.float32)
    scale = lax.optimization_barrier(jnp.mean(jnp.abs(value), axis=0, keepdims=True)) + 1e-12
    signed = scale * jnp.tanh(2.0 * value / scale)
    return (signed, value - signed)

def orthogonal(moment):
    iterate = moment / (jnp.sqrt(jnp.sum(moment * moment)) + 1e-07)
    for turn_index in range(NS):
        gram = precise(iterate, iterate.T)
        image = precise(gram, iterate)
        iterate = NS_A * iterate + NS_B * image + NS_C * precise(gram, image)
    return iterate

def adam_step(weight, gradient, first, second):
    first = 0.5 * first + 0.5 * gradient
    second = 0.95 * second + 0.05 * gradient * gradient
    update = first / (1.0 - 0.5 ** STEP) / (jnp.sqrt(second / (1.0 - 0.95 ** STEP)) + 1e-08)
    return (weight - LR_ADAM * (update + WD_ADAM * weight), first, second)

def reference(frames, labels, mask, w_input, w_hidden, w_output, biases, mom_input, mom_hidden, out_first, out_second, bias_first, bias_second, res_input, res_hidden, res_output):
    group = N_COL * FR_DEV
    slot_count = MB * group * N_BLK
    inputs = frames.astype(jnp.float32).reshape(MB, N_BLK, group, D_IN).transpose(1, 0, 2, 3)
    row_tags = jnp.where(mask > 0, labels, -1).reshape(MB, N_BLK, group).transpose(1, 0, 2)
    params = (w_input, w_hidden, w_output, biases)

    def worker(running, slices):
        inputs_w, tags_w, resid_one, resid_two, resid_three = slices

        def objective(weights):
            rounded = (low(weights[0]), low(weights[1]), low(weights[2]))
            pieces = split_biases(weights[3])
            total_loss = jnp.zeros((), jnp.float32)
            for micro_step in range(MB):
                total_loss = total_loss + rows_loss(rounded, pieces, inputs_w[micro_step], tags_w[micro_step])
            return total_loss
        loss_w, pullback = jax.vjp(objective, params)
        gradients = pullback(jnp.ones_like(loss_w) / slot_count)[0]
        q_one, r_one = squash(gradients[0], resid_one)
        q_two, r_two = squash(gradients[1], resid_two)
        q_three, r_three = squash(gradients[2], resid_three)
        running = (running[0] + q_one, running[1] + q_two, running[2] + q_three, running[3] + gradients[3], running[4] + loss_w)
        return (running, (r_one, r_two, r_three))
    start = (jnp.zeros_like(w_input), jnp.zeros_like(w_hidden), jnp.zeros_like(w_output), jnp.zeros_like(biases), jnp.zeros((), jnp.float32))
    running, residuals = lax.scan(worker, start, (inputs, row_tags, res_input, res_hidden, res_output))
    red_one, red_two, red_three, red_bias, loss_sum = running
    square = jnp.sum(red_one * red_one) + jnp.sum(red_two * red_two) + jnp.sum(red_three * red_three) + jnp.sum(red_bias * red_bias)
    clip_norm = jnp.sqrt(square)
    factor = jnp.minimum(1.0, CLIP / clip_norm)
    next_mom_input = 0.5 * mom_input + factor * red_one
    next_mom_hidden = 0.5 * mom_hidden + factor * red_two
    muon_scale = LR_MUON * 0.2 * math.sqrt(H)
    new_input = w_input * (1.0 - LR_MUON * WD_MUON) - muon_scale * orthogonal(next_mom_input)
    new_hidden = w_hidden * (1.0 - LR_MUON * WD_MUON) - muon_scale * orthogonal(next_mom_hidden)
    new_output, next_out_first, next_out_second = adam_step(w_output, factor * red_three, out_first, out_second)
    new_biases, next_bias_first, next_bias_second = adam_step(biases, factor * red_bias, bias_first, bias_second)
    return (loss_sum, clip_norm, new_input, new_hidden, new_output, new_biases, next_mom_input, next_mom_hidden, next_out_first, next_out_second, next_bias_first, next_bias_second, residuals[0], residuals[1], residuals[2])
```

```python
import functools
import math

import jax
import jax.numpy as jnp
from jax import lax
from jax.experimental import pallas as pl
from jax.experimental.pallas import tpu as pltpu
from jax.sharding import PartitionSpec as P

NS = 5
STEP = 5


NS_A = 3.4445
NS_B = -4.775
NS_C = 2.0315
CLIP = 0.002
LR_MUON = 0.1
WD_MUON = 0.01
LR_ADAM = 0.03
WD_ADAM = 0.1

MESH = pl.DeviceIdType.MESH
F32 = jnp.float32
BF16 = jnp.bfloat16
I16 = jnp.int16
LN2 = math.log(2.0)
TOP_CODE = 32700.0
LEVELS = 64.0


def matmul(left_side, right_side):
    return jnp.dot(left_side, right_side, preferred_element_type=jnp.float32)


def inner_rows(left_side, right_side):
    return lax.dot_general(
        left_side, right_side, (((0,), (0,)), ((), ())), preferred_element_type=jnp.float32
    )


def outer_cols(left_side, right_side):
    return lax.dot_general(
        left_side, right_side, (((1,), (1,)), ((), ())), preferred_element_type=jnp.float32
    )


def precise(left_side, right_side):
    return jnp.dot(
        left_side, right_side, precision=lax.Precision.HIGHEST, preferred_element_type=jnp.float32
    )


def spread_cols(values):
    return lax.all_gather(values, "col", axis=1, tiled=True)


def reduce_cols(values):
    return lax.psum_scatter(values, "col", scatter_dimension=1, tiled=True)


def collect_rows(values):
    return lax.all_gather(values, "blk", axis=0, tiled=True)


def squash(gradient, resid):
    value = gradient + resid.astype(jnp.float32)
    scale = jnp.mean(jnp.abs(value), axis=0, keepdims=True) + 1e-12
    signed = scale * jnp.tanh(2.0 * value / scale)
    return (signed, value - signed)


def adam_step(weight, gradient, first, second):
    first = 0.5 * first + 0.5 * gradient
    second = 0.95 * second + 0.05 * gradient * gradient
    update = first / (1.0 - 0.5**STEP) / (jnp.sqrt(second / (1.0 - 0.95**STEP)) + 1e-08)
    return (weight - LR_ADAM * (update + WD_ADAM * weight), first, second)


def halves(values):
    top = values.astype(BF16)
    return top, (values - top.astype(F32)).astype(BF16)


def dot_nn(left_side, right_side):
    return lax.dot_general(
        left_side, right_side, (((1,), (0,)), ((), ())), preferred_element_type=F32
    )


def dot_nt(left_side, right_side):
    return lax.dot_general(
        left_side, right_side, (((1,), (1,)), ((), ())), preferred_element_type=F32
    )


DIM_BITS = (2, 4, 8)
ORDERS = ((0, 1, 2), (1, 2, 0), (2, 0, 1))
PIECE = 48


def span_of(dims):
    slots = [0]
    for dim in dims:
        slots = slots + [slot | DIM_BITS[dim] for slot in slots]
    return slots


def stage_sends(stage):
    moves = []
    for piece, order in enumerate(ORDERS):
        for slot in span_of(order[:stage]):
            moves.append((piece, slot, order[stage]))
    return sorted(moves, key=lambda move: (move[1] | DIM_BITS[move[2]], move[0]))


def muon_kernel(
    xt_ref,
    xin_ref,
    hid_ref,
    inp_ref,
    codes,
    tops,
    lows,
    scales,
    xs,
    us,
    vs,
    lhs,
    xin,
    xin_top,
    xin_low,
    gram,
    back,
    send_sems,
    core_sems,
    recv_sems,
    back_send,
    back_recv,
):
    blk = lax.axis_index("blk")
    col = lax.axis_index("col")
    rows, wide = xs.shape
    other_core = {"col": col + 1 - 2 * (col % 2)}
    dims = (
        {"blk": blk + 1 - 2 * (blk % 2)},
        {"col": (col + 2) % 4},
        {"blk": blk + 2 - 4 * ((blk // 2) % 2)},
    )
    diagonal = {"blk": 4 * (blk // 4) + 3 - blk % 4}
    barrier = pltpu.get_barrier_semaphore()
    for target in (other_core, *dims, diagonal):
        pl.semaphore_signal(barrier, inc=1, device_id=target, device_id_type=MESH)

    xs[...] = xt_ref[...]
    xin[...] = xin_ref[...]
    for turn in range(2):
        codes[turn, 0, rows:, :] = jnp.zeros((codes.shape[2] - rows, wide), I16)
    eye = lax.broadcasted_iota(jnp.int32, (rows, rows), 0) == lax.broadcasted_iota(
        jnp.int32, (rows, rows), 1
    )
    pl.semaphore_wait(barrier, 5)

    stages = [stage_sends(stage) for stage in range(3)]
    numbers = {move: number for number, move in enumerate(sum(stages, []))}

    def part(turn, slot, piece):
        return codes.at[turn, slot, pl.ds(piece * PIECE, PIECE), :]

    def send(turn, move):
        piece, slot, dim = move
        return pltpu.make_async_remote_copy(
            src_ref=part(turn, slot, piece),
            dst_ref=part(turn, slot | DIM_BITS[dim], piece),
            send_sem=send_sems.at[numbers[move]],
            recv_sem=recv_sems.at[turn, slot | DIM_BITS[dim], piece],
            device_id=dims[dim],
            device_id_type=MESH,
        )

    def to_core(turn, slot, piece):
        return pltpu.make_async_remote_copy(
            src_ref=part(turn, slot, piece),
            dst_ref=part(turn, slot + 1, piece),
            send_sem=core_sems.at[slot // 2, piece],
            recv_sem=recv_sems.at[turn, slot + 1, piece],
            device_id=other_core,
            device_id_type=MESH,
        )

    def arrived(turn, slot, piece):
        pltpu.make_async_remote_copy(
            src_ref=part(turn, slot, piece),
            dst_ref=part(turn, slot, piece),
            send_sem=core_sems.at[0, 0],
            recv_sem=recv_sems.at[turn, slot, piece],
            device_id=other_core,
            device_id_type=MESH,
        ).wait_recv()

    def forward(turn, slot, piece):
        arrived(turn, slot, piece)
        to_core(turn, slot, piece).start()

    def landed(stage):
        return [(slot | DIM_BITS[dim], piece) for piece, slot, dim in stages[stage]]

    def unpack(turn, pair):
        for core in range(2):
            whole = codes[turn, 2 * pair + core, 0:rows, :].astype(jnp.int32).astype(F32)
            top, low = halves(whole)
            tops[pair, core * rows : (core + 1) * rows, :] = top
            lows[pair, core * rows : (core + 1) * rows, :] = low
            step = codes[turn, 2 * pair + core, rows : rows + 16, 0:rows].astype(jnp.int32)
            size = jnp.exp(step.astype(F32)[0:8, :] * (LN2 / LEVELS)) * (1.0 / TOP_CODE)
            scales[pair, :, core * rows : (core + 1) * rows] = size * size

    def apply_pair(pair, out):
        both = dot_nt(lhs[...], tops[pair])
        inner = both[:rows] + both[rows:] + dot_nt(lhs[0:rows, :], lows[pair])
        inner = inner * scales[pair, 0:1, :]
        top, low = halves(inner)
        stack = jnp.concatenate([top, low], axis=0)
        cut = 512
        for start in range(0, wide, cut):
            lanes = slice(start, start + cut)
            both = dot_nn(stack, tops[pair, :, lanes])
            out[:, lanes] += both[:rows] + both[rows:] + dot_nn(top, lows[pair, :, lanes])

    def set_lhs(values):
        top, low = halves(values)
        lhs[0:rows, :] = top
        lhs[rows:, :] = low

    def input_gram():
        top, low = halves(xin[...])
        xin_top[...] = top
        xin_low[...] = low
        gram[...] = (
            dot_nt(xin_top[...], xin_top[...])
            + dot_nt(xin_low[...], xin_top[...])
            + dot_nt(xin_top[...], xin_low[...])
        )

    def input_step():
        size = gram.shape[0]
        top, low = halves(gram[...])
        square = dot_nn(top, top) + dot_nn(low, top) + dot_nn(top, low)
        same = lax.broadcasted_iota(jnp.int32, (size, size), 0) == lax.broadcasted_iota(
            jnp.int32, (size, size), 1
        )
        poly = NS_B * gram[...] + NS_C * square + jnp.where(same, NS_A, 0.0)
        top, low = halves(poly)
        cut = 512
        for start in range(0, wide, cut):
            lanes = slice(start, start + cut)
            xin[:, lanes] = (
                dot_nn(top, xin_top[:, lanes])
                + dot_nn(low, xin_top[:, lanes])
                + dot_nn(top, xin_low[:, lanes])
            )

    def iteration(number, carry):
        turn = number % 2
        values = xs[...]
        largest = jnp.maximum(jnp.max(jnp.abs(values), axis=1, keepdims=True), 1e-30)
        step = jnp.ceil(jnp.log(largest) * (LEVELS / LN2))
        codes[turn, 0, 0:rows, :] = (
            jnp.round(values * (TOP_CODE / jnp.exp(step * (LN2 / LEVELS))))
            .astype(jnp.int32)
            .astype(I16)
        )
        lane_step = jnp.sum(jnp.where(eye, step, 0.0), axis=0, keepdims=True)
        codes[turn, 0, rows : rows + 16, 0:rows] = jnp.broadcast_to(
            lane_step.astype(jnp.int32), (16, rows)
        ).astype(I16)
        for move in stages[0]:
            send(turn, move).start()
        for piece in range(3):
            to_core(turn, 0, piece).start()
        set_lhs(values)
        us[...] = jnp.zeros_like(us)
        vs[...] = jnp.zeros_like(vs)

        def first_pass(pair, carry):
            @pl.when(pair == 1)
            def _():
                for slot, piece in landed(0):
                    forward(turn, slot, piece)
                for move in stages[1]:
                    send(turn, move).start()
                input_gram()
                for slot, piece in landed(1):
                    forward(turn, slot, piece)
                for move in stages[2]:
                    send(turn, move).start()
                input_step()

            for slot_pair in range(1, 8):
                mine = [(slot, piece) for slot, piece in landed(2) if slot == 2 * slot_pair]

                @pl.when(pair == max(slot_pair - 1, 1))
                def _(mine=mine):
                    for slot, piece in mine:
                        forward(turn, slot, piece)

            for piece in range(3):
                arrived(turn, 2 * pair + 1, piece)
            unpack(turn, pair)
            apply_pair(pair, us)
            return carry

        lax.fori_loop(0, 8, first_pass, 0)
        set_lhs(us[...])

        def second_pass(pair, carry):
            apply_pair(pair, vs)
            return carry

        lax.fori_loop(0, 8, second_pass, 0)
        xs[...] = NS_A * xs[...] + NS_B * us[...] + NS_C * vs[...]
        for stage in stages:
            for move in stage:
                send(turn, move).wait_send()
        for pair in range(8):
            for piece in range(3):
                to_core(turn, 2 * pair, piece).wait_send()
        return carry

    lax.fori_loop(0, NS, iteration, 0)

    place = blk % 4
    height = back.shape[2]
    copies = []
    for rel, target in ((1, dims[0]), (2, dims[2]), (3, diagonal)):
        copies.append(
            pltpu.make_async_remote_copy(
                src_ref=xs.at[:, pl.ds(pl.multiple_of(target["blk"] * height, height), height)],
                dst_ref=back.at[place],
                send_sem=back_send.at[rel - 1],
                recv_sem=back_recv.at[rel - 1],
                device_id=target,
                device_id_type=MESH,
            )
        )
        copies[-1].start()
    hid_ref[place] = xs[:, pl.ds(pl.multiple_of(blk * height, height), height)]
    part_wide = inp_ref.shape[1]
    inp_ref[...] = xin[:, pl.ds(pl.multiple_of(col * part_wide, part_wide), part_wide)]
    for copy in copies:
        copy.wait_recv()
    for target in (dims[0], dims[2], diagonal):
        other = target["blk"] % 4
        hid_ref[other] = back[other]
    for copy in copies:
        copy.wait_send()


def muon(xt, xin, height, part_wide):
    rows, wide = xt.shape
    deep = xin.shape[0]
    return pl.pallas_call(
        muon_kernel,
        out_shape=(
            jax.ShapeDtypeStruct((4, rows, height), F32),
            jax.ShapeDtypeStruct((deep, part_wide), F32),
        ),
        in_specs=[pl.BlockSpec(memory_space=pltpu.VMEM)] * 2,
        out_specs=(pl.BlockSpec(memory_space=pltpu.VMEM), pl.BlockSpec(memory_space=pltpu.VMEM)),
        scratch_shapes=[
            pltpu.VMEM((2, 16, 3 * PIECE, wide), I16),
            pltpu.VMEM((8, 2 * rows, wide), BF16),
            pltpu.VMEM((8, 2 * rows, wide), BF16),
            pltpu.VMEM((8, 8, 2 * rows), F32),
            pltpu.VMEM((rows, wide), F32),
            pltpu.VMEM((rows, wide), F32),
            pltpu.VMEM((rows, wide), F32),
            pltpu.VMEM((2 * rows, wide), BF16),
            pltpu.VMEM((deep, wide), F32),
            pltpu.VMEM((deep, wide), BF16),
            pltpu.VMEM((deep, wide), BF16),
            pltpu.VMEM((deep, deep), F32),
            pltpu.VMEM((4, rows, height), F32),
            pltpu.SemaphoreType.DMA((21,)),
            pltpu.SemaphoreType.DMA((8, 3)),
            pltpu.SemaphoreType.DMA((2, 16, 3)),
            pltpu.SemaphoreType.DMA((3,)),
            pltpu.SemaphoreType.DMA((3,)),
        ],
        compiler_params=pltpu.CompilerParams(
            collective_id=0, has_side_effects=True, vmem_limit_bytes=60 * 1024 * 1024
        ),
    )(xt, xin)


def plain_body(
    frames,
    labels,
    mask,
    w_input,
    w_hidden,
    w_output,
    biases,
    mom_input,
    mom_hidden,
    out_first,
    out_second,
    bias_first,
    bias_second,
    res_input,
    res_hidden,
    res_output,
):
    ncol = lax.axis_size("col")
    nblk = lax.axis_size("blk")
    col_index = lax.axis_index("col")
    hcol = w_input.shape[1]
    scol = w_output.shape[1]
    micro = frames.shape[0]
    slot_count = frames.shape[1] * micro * nblk * ncol
    bias_row = biases[0]
    b_one = bias_row[:hcol]
    b_two = bias_row[hcol : 2 * hcol]
    b_out = bias_row[2 * hcol :]
    low_input = w_input.astype(jnp.bfloat16)
    row_tags = jnp.where(mask > 0, labels, -1)
    grad_input = jnp.zeros(w_input.shape, jnp.float32)
    grad_hidden = jnp.zeros((w_hidden.shape[0] * nblk, hcol), jnp.float32)
    grad_output = jnp.zeros((w_output.shape[0] * nblk, scol), jnp.float32)
    grad_bias = jnp.zeros(bias_row.shape, jnp.float32)
    loss_local = jnp.zeros((), jnp.float32)
    for micro_step in range(micro):
        low_hidden, low_output = (
            lax.all_gather(w_hidden.astype(jnp.bfloat16), "blk", axis=0, tiled=True),
            lax.all_gather(w_output.astype(jnp.bfloat16), "blk", axis=0, tiled=True),
        )
        inputs = lax.all_gather(frames[micro_step], "col", axis=0, tiled=True)
        tags_group = lax.all_gather(row_tags[micro_step], "col", axis=0, tiled=True)
        sig_one = jax.nn.sigmoid(matmul(inputs, low_input) + b_one)
        h_one = spread_cols(sig_one.astype(jnp.bfloat16))
        sig_two = jax.nn.sigmoid(matmul(h_one, low_hidden) + b_two)
        h_two = spread_cols(sig_two.astype(jnp.bfloat16))
        logits = matmul(h_two, low_output) + b_out
        row_top = lax.pmax(jnp.max(logits, axis=1), "col")
        exponent = jnp.exp(logits - row_top[:, None])
        target_hit = jnp.arange(scol)[None, :] == (tags_group - col_index * scol)[:, None]
        row_total, picked = lax.psum(
            (jnp.sum(exponent, axis=1), jnp.sum(jnp.where(target_hit, logits, 0.0), axis=1)), "col"
        )
        live_rows = tags_group >= 0
        loss_local = loss_local + jnp.sum(
            jnp.where(live_rows, row_top + jnp.log(row_total) - picked, 0.0)
        )
        probs = exponent / row_total[:, None]
        d_logits = (
            jnp.where(live_rows[:, None], probs - target_hit.astype(jnp.float32), 0.0) / slot_count
        ).astype(jnp.bfloat16)
        grad_output = grad_output + inner_rows(h_two, d_logits)
        d_h_two = reduce_cols(outer_cols(d_logits, low_output))
        d_z_two = (d_h_two * sig_two * (1.0 - sig_two)).astype(jnp.bfloat16)
        grad_hidden = grad_hidden + inner_rows(h_one, d_z_two)
        d_h_one = reduce_cols(outer_cols(d_z_two, low_hidden))
        d_z_one = (d_h_one * sig_one * (1.0 - sig_one)).astype(jnp.bfloat16)
        grad_input = grad_input + inner_rows(inputs, d_z_one)
        grad_bias = grad_bias + jnp.concatenate(
            [
                jnp.sum(d_z_one.astype(jnp.float32), axis=0),
                jnp.sum(d_z_two.astype(jnp.float32), axis=0),
                jnp.sum(d_logits.astype(jnp.float32), axis=0),
            ]
        )
    q_input, next_res_input = squash(grad_input, res_input[0])
    q_hidden, next_res_hidden = squash(grad_hidden, res_hidden[0])
    q_output, next_res_output = squash(grad_output, res_output[0])
    red_hidden, red_output = (
        lax.psum_scatter(q_hidden, "blk", scatter_dimension=0, tiled=True),
        lax.psum_scatter(q_output, "blk", scatter_dimension=0, tiled=True),
    )
    red_input, red_bias, loss_sum = lax.psum((q_input, grad_bias, loss_local), "blk")
    share_blk = 1.0 / nblk
    grad_square = (
        share_blk * (jnp.sum(red_input * red_input) + jnp.sum(red_bias * red_bias))
        + jnp.sum(red_hidden * red_hidden)
        + jnp.sum(red_output * red_output)
    )
    clip_norm = jnp.sqrt(lax.psum(grad_square, ("blk", "col")))
    factor = jnp.minimum(1.0, CLIP / clip_norm)
    next_mom_input = 0.5 * mom_input + factor * red_input
    next_mom_hidden = 0.5 * mom_hidden + factor * red_hidden
    square_input, square_hidden = lax.psum(
        (
            share_blk * jnp.sum(next_mom_input * next_mom_input),
            jnp.sum(next_mom_hidden * next_mom_hidden),
        ),
        ("blk", "col"),
    )
    iter_input = next_mom_input / (jnp.sqrt(square_input) + 1e-07)
    iter_hidden = next_mom_hidden / (jnp.sqrt(square_hidden) + 1e-07)
    for turn_index in range(NS):
        rows_hidden = collect_rows(iter_hidden)
        gram_input, gram_hidden = lax.psum(
            (precise(iter_input, iter_input.T), precise(iter_hidden, rows_hidden.T)), "col"
        )
        image_input = precise(gram_input, iter_input)
        image_hidden = precise(gram_hidden, rows_hidden)
        iter_input = (
            NS_A * iter_input + NS_B * image_input + NS_C * precise(gram_input, image_input)
        )
        iter_hidden = (
            NS_A * iter_hidden
            + NS_B * image_hidden
            + NS_C * precise(gram_hidden, collect_rows(image_hidden))
        )
    muon_scale = LR_MUON * 0.2 * math.sqrt(hcol * ncol)
    new_input = w_input * (1.0 - LR_MUON * WD_MUON) - muon_scale * iter_input
    new_hidden = w_hidden * (1.0 - LR_MUON * WD_MUON) - muon_scale * iter_hidden
    new_output, next_out_first, next_out_second = adam_step(
        w_output, factor * red_output, out_first, out_second
    )
    new_biases, next_bias_first, next_bias_second = adam_step(
        biases, factor * red_bias[None, :], bias_first, bias_second
    )
    return (
        loss_sum,
        clip_norm,
        new_input,
        new_hidden,
        new_output,
        new_biases,
        next_mom_input,
        next_mom_hidden,
        next_out_first,
        next_out_second,
        next_bias_first,
        next_bias_second,
        next_res_input[None],
        next_res_hidden[None],
        next_res_output[None],
    )


def fast_body(
    frames,
    labels,
    mask,
    w_input,
    w_hidden,
    w_output,
    biases,
    mom_input,
    mom_hidden,
    out_first,
    out_second,
    bias_first,
    bias_second,
    res_input,
    res_hidden,
    res_output,
):
    ncol = lax.axis_size("col")
    nblk = lax.axis_size("blk")
    col_index = lax.axis_index("col")
    blk_index = lax.axis_index("blk")
    hcol = w_input.shape[1]
    scol = w_output.shape[1]
    micro = frames.shape[0]
    slot_count = frames.shape[1] * micro * nblk * ncol
    bias_row = biases[0]
    b_one = bias_row[:hcol]
    b_two = bias_row[hcol : 2 * hcol]
    b_out = bias_row[2 * hcol :]
    low_input = w_input.astype(jnp.bfloat16)
    own_tags = jnp.where(mask > 0, labels, -1).reshape(-1)
    own_inputs = frames.reshape(-1, frames.shape[2])
    inputs = lax.all_gather(own_inputs, "col", axis=0, tiled=True)
    tags_group = lax.all_gather(own_tags, "col", axis=0, tiled=True)
    low_hidden = collect_rows(w_hidden.astype(jnp.bfloat16))
    low_output = collect_rows(w_output.astype(jnp.bfloat16))
    sig_one = jax.nn.sigmoid(matmul(inputs, low_input) + b_one)
    h_one = spread_cols(sig_one.astype(jnp.bfloat16))
    sig_two = jax.nn.sigmoid(matmul(h_one, low_hidden) + b_two)
    h_two = spread_cols(sig_two.astype(jnp.bfloat16))
    logits = matmul(h_two, low_output) + b_out
    row_top = lax.pmax(jnp.max(logits, axis=1), "col")
    exponent = jnp.exp(logits - row_top[:, None])
    target_hit = jnp.arange(scol)[None, :] == (tags_group - col_index * scol)[:, None]
    row_total, picked = lax.psum(
        (jnp.sum(exponent, axis=1), jnp.sum(jnp.where(target_hit, logits, 0.0), axis=1)), "col"
    )
    live_rows = tags_group >= 0
    loss_local = jnp.sum(jnp.where(live_rows, row_top + jnp.log(row_total) - picked, 0.0))
    probs = exponent / row_total[:, None]
    d_logits = (
        jnp.where(live_rows[:, None], probs - target_hit.astype(jnp.float32), 0.0) / slot_count
    ).astype(jnp.bfloat16)
    grad_output = inner_rows(h_two, d_logits)
    d_h_two = reduce_cols(outer_cols(d_logits, low_output))
    d_z_two = (d_h_two * sig_two * (1.0 - sig_two)).astype(jnp.bfloat16)
    grad_hidden = inner_rows(h_one, d_z_two)
    d_h_one = reduce_cols(outer_cols(d_z_two, low_hidden))
    d_z_one = (d_h_one * sig_one * (1.0 - sig_one)).astype(jnp.bfloat16)
    grad_input = inner_rows(inputs, d_z_one)
    grad_bias = jnp.concatenate(
        [
            jnp.sum(d_z_one.astype(jnp.float32), axis=0),
            jnp.sum(d_z_two.astype(jnp.float32), axis=0),
            jnp.sum(d_logits.astype(jnp.float32), axis=0),
        ]
    )
    q_input, next_res_input = squash(grad_input, res_input[0])
    q_hidden, next_res_hidden = squash(grad_hidden, res_hidden[0])
    q_output, next_res_output = squash(grad_output, res_output[0])
    red_hidden, red_output = (
        lax.psum_scatter(q_hidden, "blk", scatter_dimension=0, tiled=True),
        lax.psum_scatter(q_output, "blk", scatter_dimension=0, tiled=True),
    )
    red_input, red_bias, loss_sum = lax.psum((q_input, grad_bias, loss_local), "blk")
    share_blk = 1.0 / nblk
    grad_square = (
        share_blk * (jnp.sum(red_input * red_input) + jnp.sum(red_bias * red_bias))
        + jnp.sum(red_hidden * red_hidden)
        + jnp.sum(red_output * red_output)
    )
    clip_norm = jnp.sqrt(lax.psum(grad_square, ("blk", "col")))
    factor = jnp.minimum(1.0, CLIP / clip_norm)
    next_mom_input = 0.5 * mom_input + factor * red_input
    next_mom_hidden = 0.5 * mom_hidden + factor * red_hidden
    square_input, square_hidden = lax.psum(
        (
            share_blk * jnp.sum(next_mom_input * next_mom_input),
            jnp.sum(next_mom_hidden * next_mom_hidden),
        ),
        ("blk", "col"),
    )
    iter_input = next_mom_input / (jnp.sqrt(square_input) + 1e-07)
    iter_hidden = next_mom_hidden / (jnp.sqrt(square_hidden) + 1e-07)
    tall = collect_rows(iter_hidden)
    piece = hcol // 4
    mine = lax.dynamic_slice_in_dim(tall, (blk_index % 4) * piece, piece, axis=1).T
    deep = w_input.shape[0]
    padded = 512
    whole_input = spread_cols(jnp.pad(iter_input, ((0, padded - deep), (0, 0))))
    done_hidden, done_input = muon(mine, whole_input, w_hidden.shape[0], hcol)
    done_hidden = done_hidden.reshape(hcol, w_hidden.shape[0]).T
    muon_scale = LR_MUON * 0.2 * math.sqrt(hcol * ncol)
    new_input = w_input * (1.0 - LR_MUON * WD_MUON) - muon_scale * done_input[:deep]
    new_hidden = w_hidden * (1.0 - LR_MUON * WD_MUON) - muon_scale * done_hidden
    new_output, next_out_first, next_out_second = adam_step(
        w_output, factor * red_output, out_first, out_second
    )
    new_biases, next_bias_first, next_bias_second = adam_step(
        biases, factor * red_bias[None, :], bias_first, bias_second
    )
    return (
        loss_sum,
        clip_norm,
        new_input,
        new_hidden,
        new_output,
        new_biases,
        next_mom_input,
        next_mom_hidden,
        next_out_first,
        next_out_second,
        next_bias_first,
        next_bias_second,
        next_res_input[None],
        next_res_hidden[None],
        next_res_output[None],
    )


def solution(mesh):
    in_specs = (
        P(None, ("blk", "col"), None),
        P(None, ("blk", "col")),
        P(None, ("blk", "col")),
        P(None, "col"),
        P("blk", "col"),
        P("blk", "col"),
        P("col", None),
        P(None, "col"),
        P("blk", "col"),
        P("blk", "col"),
        P("blk", "col"),
        P("col", None),
        P("col", None),
        P("blk", None, "col"),
        P("blk", None, "col"),
        P("blk", None, "col"),
    )
    out_specs = (
        P(),
        P(),
        P(None, "col"),
        P("blk", "col"),
        P("blk", "col"),
        P("col", None),
        P(None, "col"),
        P("blk", "col"),
        P("blk", "col"),
        P("blk", "col"),
        P("col", None),
        P("col", None),
        P("blk", None, "col"),
        P("blk", None, "col"),
        P("blk", None, "col"),
    )
    cubes = mesh.shape["blk"] == 8 and mesh.shape["col"] == 4
    body = fast_body if cubes else plain_body
    return jax.shard_map(body, mesh=mesh, in_specs=in_specs, out_specs=out_specs, check_vma=False)
```

```python
import functools
import math

import jax
import jax.numpy as jnp
from jax import lax
from jax.experimental import pallas as pl
from jax.experimental.pallas import tpu as pltpu
from jax.sharding import PartitionSpec as P

NS = 5
STEP = 5


NS_A = 3.4445
NS_B = -4.775
NS_C = 2.0315
CLIP = 0.002
LR_MUON = 0.1
WD_MUON = 0.01
LR_ADAM = 0.03
WD_ADAM = 0.1

MESH = pl.DeviceIdType.MESH
F32 = jnp.float32
BF16 = jnp.bfloat16
I16 = jnp.int16
LN2 = math.log(2.0)
TOP_CODE = 32700.0
LEVELS = 64.0


def matmul(left_side, right_side):
    return jnp.dot(left_side, right_side, preferred_element_type=jnp.float32)


def inner_rows(left_side, right_side):
    return lax.dot_general(
        left_side, right_side, (((0,), (0,)), ((), ())), preferred_element_type=jnp.float32
    )


def outer_cols(left_side, right_side):
    return lax.dot_general(
        left_side, right_side, (((1,), (1,)), ((), ())), preferred_element_type=jnp.float32
    )


def precise(left_side, right_side):
    return jnp.dot(
        left_side, right_side, precision=lax.Precision.HIGHEST, preferred_element_type=jnp.float32
    )


def spread_cols(values):
    return lax.all_gather(values, "col", axis=1, tiled=True)


def reduce_cols(values):
    return lax.psum_scatter(values, "col", scatter_dimension=1, tiled=True)


def collect_rows(values):
    return lax.all_gather(values, "blk", axis=0, tiled=True)


def squash(gradient, resid):
    value = gradient + resid.astype(jnp.float32)
    scale = jnp.mean(jnp.abs(value), axis=0, keepdims=True) + 1e-12
    signed = scale * jnp.tanh(2.0 * value / scale)
    return (signed, value - signed)


def adam_step(weight, gradient, first, second):
    first = 0.5 * first + 0.5 * gradient
    second = 0.95 * second + 0.05 * gradient * gradient
    update = first / (1.0 - 0.5**STEP) / (jnp.sqrt(second / (1.0 - 0.95**STEP)) + 1e-08)
    return (weight - LR_ADAM * (update + WD_ADAM * weight), first, second)


def halves(values):
    top = values.astype(BF16)
    return top, (values - top.astype(F32)).astype(BF16)


def dot_nn(left_side, right_side):
    return lax.dot_general(
        left_side, right_side, (((1,), (0,)), ((), ())), preferred_element_type=F32
    )


def dot_nt(left_side, right_side):
    return lax.dot_general(
        left_side, right_side, (((1,), (1,)), ((), ())), preferred_element_type=F32
    )


DIM_BITS = (2, 4, 8)
ORDERS = ((0, 1, 2), (1, 2, 0), (2, 0, 1))
PIECE = 48


def span_of(dims):
    slots = [0]
    for dim in dims:
        slots = slots + [slot | DIM_BITS[dim] for slot in slots]
    return slots


def stage_sends(stage):
    moves = []
    for piece, order in enumerate(ORDERS):
        for slot in span_of(order[:stage]):
            moves.append((piece, slot, order[stage]))
    return sorted(moves, key=lambda move: (move[1] | DIM_BITS[move[2]], move[0]))


def muon_kernel(
    xt_ref,
    xin_ref,
    hid_ref,
    inp_ref,
    codes,
    tops,
    lows,
    scales,
    xs,
    us,
    vs,
    lhs,
    xin,
    xin_top,
    xin_low,
    gram,
    back,
    send_sems,
    core_sems,
    recv_sems,
    back_send,
    back_recv,
):
    blk = lax.axis_index("blk")
    col = lax.axis_index("col")
    rows, wide = xs.shape
    other_core = {"col": col + 1 - 2 * (col % 2)}
    dims = (
        {"blk": blk + 1 - 2 * (blk % 2)},
        {"col": (col + 2) % 4},
        {"blk": blk + 2 - 4 * ((blk // 2) % 2)},
    )
    diagonal = {"blk": 4 * (blk // 4) + 3 - blk % 4}
    barrier = pltpu.get_barrier_semaphore()
    for target in (other_core, *dims, diagonal):
        pl.semaphore_signal(barrier, inc=1, device_id=target, device_id_type=MESH)

    xs[...] = xt_ref[...]
    xin[...] = xin_ref[...]
    for turn in range(2):
        codes[turn, 0, rows:, :] = jnp.zeros((codes.shape[2] - rows, wide), I16)
    eye = lax.broadcasted_iota(jnp.int32, (rows, rows), 0) == lax.broadcasted_iota(
        jnp.int32, (rows, rows), 1
    )
    pl.semaphore_wait(barrier, 5)

    stages = [stage_sends(stage) for stage in range(3)]
    numbers = {move: number for number, move in enumerate(sum(stages, []))}

    def part(turn, slot, piece):
        return codes.at[turn, slot, pl.ds(piece * PIECE, PIECE), :]

    def send(turn, move):
        piece, slot, dim = move
        return pltpu.make_async_remote_copy(
            src_ref=part(turn, slot, piece),
            dst_ref=part(turn, slot | DIM_BITS[dim], piece),
            send_sem=send_sems.at[numbers[move]],
            recv_sem=recv_sems.at[turn, slot | DIM_BITS[dim], piece],
            device_id=dims[dim],
            device_id_type=MESH,
        )

    def to_core(turn, slot, piece):
        return pltpu.make_async_remote_copy(
            src_ref=part(turn, slot, piece),
            dst_ref=part(turn, slot + 1, piece),
            send_sem=core_sems.at[slot // 2, piece],
            recv_sem=recv_sems.at[turn, slot + 1, piece],
            device_id=other_core,
            device_id_type=MESH,
        )

    def arrived(turn, slot, piece):
        pltpu.make_async_remote_copy(
            src_ref=part(turn, slot, piece),
            dst_ref=part(turn, slot, piece),
            send_sem=core_sems.at[0, 0],
            recv_sem=recv_sems.at[turn, slot, piece],
            device_id=other_core,
            device_id_type=MESH,
        ).wait_recv()

    def forward(turn, slot, piece):
        arrived(turn, slot, piece)
        to_core(turn, slot, piece).start()

    def landed(stage):
        return [(slot | DIM_BITS[dim], piece) for piece, slot, dim in stages[stage]]

    def unpack(turn, pair):
        for core in range(2):
            whole = codes[turn, 2 * pair + core, 0:rows, :].astype(jnp.int32).astype(F32)
            top, low = halves(whole)
            tops[pair, core * rows : (core + 1) * rows, :] = top
            lows[pair, core * rows : (core + 1) * rows, :] = low
            step = codes[turn, 2 * pair + core, rows : rows + 16, 0:rows].astype(jnp.int32)
            size = jnp.exp(step.astype(F32)[0:8, :] * (LN2 / LEVELS)) * (1.0 / TOP_CODE)
            scales[pair, :, core * rows : (core + 1) * rows] = size * size

    def apply_pair(pair, out):
        both = dot_nt(lhs[...], tops[pair])
        inner = both[:rows] + both[rows:] + dot_nt(lhs[0:rows, :], lows[pair])
        inner = inner * scales[pair, 0:1, :]
        top, low = halves(inner)
        stack = jnp.concatenate([top, low], axis=0)
        cut = 512
        for start in range(0, wide, cut):
            lanes = slice(start, start + cut)
            both = dot_nn(stack, tops[pair, :, lanes])
            out[:, lanes] += both[:rows] + both[rows:] + dot_nn(top, lows[pair, :, lanes])

    def set_lhs(values):
        top, low = halves(values)
        lhs[0:rows, :] = top
        lhs[rows:, :] = low

    def input_gram():
        top, low = halves(xin[...])
        xin_top[...] = top
        xin_low[...] = low
        gram[...] = (
            dot_nt(xin_top[...], xin_top[...])
            + dot_nt(xin_low[...], xin_top[...])
            + dot_nt(xin_top[...], xin_low[...])
        )

    def input_step():
        size = gram.shape[0]
        top, low = halves(gram[...])
        square = dot_nn(top, top) + dot_nn(low, top) + dot_nn(top, low)
        same = lax.broadcasted_iota(jnp.int32, (size, size), 0) == lax.broadcasted_iota(
            jnp.int32, (size, size), 1
        )
        poly = NS_B * gram[...] + NS_C * square + jnp.where(same, NS_A, 0.0)
        top, low = halves(poly)
        cut = 512
        for start in range(0, wide, cut):
            lanes = slice(start, start + cut)
            xin[:, lanes] = (
                dot_nn(top, xin_top[:, lanes])
                + dot_nn(low, xin_top[:, lanes])
                + dot_nn(top, xin_low[:, lanes])
            )

    def iteration(number, carry):
        turn = number % 2
        values = xs[...]
        largest = jnp.maximum(jnp.max(jnp.abs(values), axis=1, keepdims=True), 1e-30)
        step = jnp.ceil(jnp.log(largest) * (LEVELS / LN2))
        codes[turn, 0, 0:rows, :] = (
            jnp.round(values * (TOP_CODE / jnp.exp(step * (LN2 / LEVELS))))
            .astype(jnp.int32)
            .astype(I16)
        )
        lane_step = jnp.sum(jnp.where(eye, step, 0.0), axis=0, keepdims=True)
        codes[turn, 0, rows : rows + 16, 0:rows] = jnp.broadcast_to(
            lane_step.astype(jnp.int32), (16, rows)
        ).astype(I16)
        for move in stages[0]:
            send(turn, move).start()
        for piece in range(3):
            to_core(turn, 0, piece).start()
        set_lhs(values)
        us[...] = jnp.zeros_like(us)
        vs[...] = jnp.zeros_like(vs)

        def first_pass(pair, carry):
            @pl.when(pair == 1)
            def _():
                for slot, piece in landed(0):
                    forward(turn, slot, piece)
                for move in stages[1]:
                    send(turn, move).start()
                input_gram()
                for slot, piece in landed(1):
                    forward(turn, slot, piece)
                for move in stages[2]:
                    send(turn, move).start()
                input_step()

            for slot_pair in range(1, 8):
                mine = [(slot, piece) for slot, piece in landed(2) if slot == 2 * slot_pair]

                @pl.when(pair == max(slot_pair - 1, 1))
                def _(mine=mine):
                    for slot, piece in mine:
                        forward(turn, slot, piece)

            for piece in range(3):
                arrived(turn, 2 * pair + 1, piece)
            unpack(turn, pair)
            apply_pair(pair, us)
            return carry

        lax.fori_loop(0, 8, first_pass, 0)
        set_lhs(us[...])

        def second_pass(pair, carry):
            apply_pair(pair, vs)
            return carry

        lax.fori_loop(0, 8, second_pass, 0)
        xs[...] = NS_A * xs[...] + NS_B * us[...] + NS_C * vs[...]
        for stage in stages:
            for move in stage:
                send(turn, move).wait_send()
        for pair in range(8):
            for piece in range(3):
                to_core(turn, 2 * pair, piece).wait_send()
        return carry

    lax.fori_loop(0, NS, iteration, 0)

    place = blk % 4
    height = back.shape[2]
    copies = []
    for rel, target in ((1, dims[0]), (2, dims[2]), (3, diagonal)):
        copies.append(
            pltpu.make_async_remote_copy(
                src_ref=xs.at[:, pl.ds(pl.multiple_of(target["blk"] * height, height), height)],
                dst_ref=back.at[place],
                send_sem=back_send.at[rel - 1],
                recv_sem=back_recv.at[rel - 1],
                device_id=target,
                device_id_type=MESH,
            )
        )
        copies[-1].start()
    hid_ref[place] = xs[:, pl.ds(pl.multiple_of(blk * height, height), height)]
    part_wide = inp_ref.shape[1]
    inp_ref[...] = xin[:, pl.ds(pl.multiple_of(col * part_wide, part_wide), part_wide)]
    for copy in copies:
        copy.wait_recv()
    for target in (dims[0], dims[2], diagonal):
        other = target["blk"] % 4
        hid_ref[other] = back[other]
    for copy in copies:
        copy.wait_send()


def muon(xt, xin, height, part_wide):
    rows, wide = xt.shape
    deep = xin.shape[0]
    return pl.pallas_call(
        muon_kernel,
        out_shape=(
            jax.ShapeDtypeStruct((4, rows, height), F32),
            jax.ShapeDtypeStruct((deep, part_wide), F32),
        ),
        in_specs=[pl.BlockSpec(memory_space=pltpu.VMEM)] * 2,
        out_specs=(pl.BlockSpec(memory_space=pltpu.VMEM), pl.BlockSpec(memory_space=pltpu.VMEM)),
        scratch_shapes=[
            pltpu.VMEM((2, 16, 3 * PIECE, wide), I16),
            pltpu.VMEM((8, 2 * rows, wide), BF16),
            pltpu.VMEM((8, 2 * rows, wide), BF16),
            pltpu.VMEM((8, 8, 2 * rows), F32),
            pltpu.VMEM((rows, wide), F32),
            pltpu.VMEM((rows, wide), F32),
            pltpu.VMEM((rows, wide), F32),
            pltpu.VMEM((2 * rows, wide), BF16),
            pltpu.VMEM((deep, wide), F32),
            pltpu.VMEM((deep, wide), BF16),
            pltpu.VMEM((deep, wide), BF16),
            pltpu.VMEM((deep, deep), F32),
            pltpu.VMEM((4, rows, height), F32),
            pltpu.SemaphoreType.DMA((21,)),
            pltpu.SemaphoreType.DMA((8, 3)),
            pltpu.SemaphoreType.DMA((2, 16, 3)),
            pltpu.SemaphoreType.DMA((3,)),
            pltpu.SemaphoreType.DMA((3,)),
        ],
        compiler_params=pltpu.CompilerParams(
            collective_id=0, has_side_effects=True, vmem_limit_bytes=60 * 1024 * 1024
        ),
    )(xt, xin)


RING = 8
STEPS = RING - 1
OUT_ROWS = 592
OUT_GROUPS = 4
BLOCKS = (304, 288)
HID_ROWS = 512
SCALE_ROWS = 16


def ring_place(blk):
    odd = blk % 2
    return (blk // 2) * (1 - odd) + (7 - blk // 2) * odd


def ring_blk(place):
    back = place // 4
    return 2 * place * (1 - back) + (15 - 2 * place) * back


def scale_code(size):
    return jnp.ceil(jnp.log(jnp.maximum(size, 1e-30)) * (LEVELS / LN2))


def code_scale(code):
    return jnp.exp(code * (LN2 / LEVELS))


def to_codes(values):
    return jnp.round(values).astype(jnp.int32).astype(I16)


def from_codes(codes):
    return codes.astype(jnp.int32).astype(F32)


def reduce_kernel(
    deep,
    dl_ref,
    h_two_ref,
    res_out_ref,
    dz_two_ref,
    h_one_ref,
    res_hid_ref,
    dz_one_ref,
    x_ref,
    res_in_ref,
    vec_ref,
    next_out_ref,
    next_hid_ref,
    next_in_ref,
    red_out_ref,
    red_hid_ref,
    red_in_ref,
    vec_sum_ref,
    stats_ref,
    grad,
    stage,
    res_buf,
    marks,
    own_out,
    got_out,
    size_out,
    own_hid,
    got_hid,
    size_hid,
    own_in,
    got_in,
    size_in,
    share_in,
    vecs,
    res_sems,
    stage_sems,
    out_send,
    out_recv,
    hid_send,
    hid_recv,
    in_send,
    in_recv,
    share_send,
    share_recv,
    vec_send,
    vec_recv,
):
    blk = lax.axis_index("blk")
    here = ring_place(blk)
    total_rows = next_out_ref.shape[0]
    barrier = pltpu.get_barrier_semaphore()
    for away in range(1, RING):
        pl.semaphore_signal(
            barrier, inc=1, device_id={"blk": (blk + away) % RING}, device_id_type=MESH
        )

    starts = [sum(BLOCKS[:part]) for part in range(len(BLOCKS))]

    def res_copy(group, part):
        rows = BLOCKS[part]
        return pltpu.make_async_copy(
            res_out_ref.at[pl.ds(group * OUT_ROWS + starts[part], rows), :],
            res_buf.at[part, pl.ds(0, rows), :],
            res_sems.at[part],
        )

    def stage_copy(group, part, rows):
        return pltpu.make_async_copy(
            stage.at[pl.ds(0, rows)],
            next_out_ref.at[pl.ds(group * OUT_ROWS + starts[part], rows)],
            stage_sems.at[0],
        )

    last_rows = total_rows - (OUT_GROUPS - 1) * OUT_ROWS - starts[-1]

    def stage_start(group, part):
        if part < len(BLOCKS) - 1:
            stage_copy(group, part, BLOCKS[part]).start()
        else:

            @pl.when(group < OUT_GROUPS - 1)
            def _():
                stage_copy(group, part, BLOCKS[part]).start()

            @pl.when(group == OUT_GROUPS - 1)
            def _():
                stage_copy(group, part, last_rows).start()

    res_copy(0, 0).start()
    res_copy(0, 1).start()
    marks[...] = jnp.zeros_like(marks)
    stats_ref[...] = jnp.zeros_like(stats_ref)
    pl.semaphore_wait(barrier, RING - 1)

    vec_copies = []
    for away in range(1, RING):
        copy = pltpu.make_async_remote_copy(
            src_ref=vec_ref,
            dst_ref=vecs.at[blk],
            send_sem=vec_send.at[away - 1],
            recv_sem=vec_recv.at[away - 1],
            device_id={"blk": (blk + away) % RING},
            device_id_type=MESH,
        )
        copy.start()
        vec_copies.append(copy)

    def row_scale(value, count):
        size = jnp.sum(jnp.abs(value), axis=1, keepdims=True) * (1.0 / count) + 1e-12
        code = scale_code(size)
        return size, code, size * (TOP_CODE / code_scale(code))

    def lane_codes(first):
        return jnp.transpose(marks[first : first + 128, :])[0:1, :]

    def set_sizes(rows, own, sizes):
        parts = [lane_codes(first) for first in range(0, rows, 128)]
        parts.append(jnp.zeros((SCALE_ROWS - len(parts), 128), F32))
        codes = jnp.concatenate(parts, axis=0)
        sizes[...] = code_scale(codes[0:8, :])
        for number in range(2 * RING):
            own[number, rows : rows + SCALE_ROWS, :] = codes.astype(jnp.int32).astype(I16)

    def squash_rows(first, count, own, first_own, read_res, write_next):
        def some(number, carry):
            row = pl.multiple_of(number * 16, 16)
            value = grad[pl.ds(row, 16), :] + read_res(row)
            size, code, factor = row_scale(value, value.shape[1])
            grad[pl.ds(row, 16), :] = value
            marks[pl.ds(first_own + row, 16), :] = jnp.broadcast_to(code, (16, 128))
            steep = 2.0 / size
            for lane in range(0, value.shape[1], 128):
                piece = grad[pl.ds(row, 16), lane : lane + 128]
                curve = jnp.tanh(piece * steep)
                number_of = lane // 256
                chunk = number_of // 2 if number_of % 2 == 0 else 7 - number_of // 2
                own[2 * chunk + lane // 128 % 2, pl.ds(first_own + row, 16), :] = to_codes(
                    curve * factor
                )
                write_next(row, lane, piece - size * curve)
            return carry

        lax.fori_loop(0, count // 16, some, 0)

    def out_group(group):
        for part, rows in enumerate(BLOCKS):
            base = pl.multiple_of(group * OUT_ROWS + starts[part], 16)
            for lane in range(0, grad.shape[1], 512):
                grad[0:rows, lane : lane + 512] = dot_nn(
                    dl_ref[pl.ds(base, rows), :], h_two_ref[:, lane : lane + 512]
                )
            res_copy(group, part).wait()
            if part == 0:

                @pl.when(group > 0)
                def _():
                    stage_copy(group - 1, len(BLOCKS) - 1, BLOCKS[-1]).wait()

            else:
                stage_copy(group, part - 1, BLOCKS[part - 1]).wait()

            def write_next(row, lane, values):
                stage[pl.ds(row, 16), 0, lane : lane + 128] = values

            squash_rows(
                0,
                rows,
                own_out.at[group],
                starts[part],
                lambda row, part=part: res_buf[part, pl.ds(row, 16), :].astype(F32),
                write_next,
            )
            stage_start(group, part)

            @pl.when(group < OUT_GROUPS - 1)
            def _(part=part):
                res_copy(group + 1, part).start()

        set_sizes(OUT_ROWS, own_out.at[group], size_out.at[group])

    def hid_group():
        for first in range(0, HID_ROWS, 256):
            for lane in range(0, grad.shape[1], 512):
                grad[0:256, lane : lane + 512] = dot_nn(
                    dz_two_ref[first : first + 256, :], h_one_ref[:, lane : lane + 512]
                )

            def write_next(row, lane, values, first=first):
                next_hid_ref[pl.ds(first + row, 16), lane : lane + 128] = values

            squash_rows(
                0,
                256,
                own_hid,
                first,
                lambda row, first=first: res_hid_ref[pl.ds(first + row, 16), :].astype(F32),
                write_next,
            )
        set_sizes(HID_ROWS, own_hid, size_hid)

    def in_group():
        wide = x_ref.shape[1]
        for first in range(0, HID_ROWS, 256):
            grad[0:256, 0:wide] = dot_nn(dz_one_ref[first : first + 256, :], x_ref[...])

            def some(number, carry, first=first):
                row = pl.multiple_of(number * 16, 16)
                place = pl.multiple_of(first + row, 16)
                value = grad[pl.ds(row, 16), 0:wide] + res_in_ref[pl.ds(place, 16), :].astype(F32)
                size, code, factor = row_scale(value, deep)
                curve = jnp.tanh(value * (2.0 / size))
                next_in_ref[pl.ds(place, 16), :] = value - size * curve
                marks[pl.ds(place, 16), :] = jnp.broadcast_to(code, (16, 128))
                chunk = first // 64 + number // 4
                inside = pl.multiple_of(number % 4 * 16, 16)
                codes = to_codes(curve * factor)
                for way in range(2):
                    own_in[2 * chunk + way, pl.ds(inside, 16), :] = codes[
                        :, way * 256 : (way + 1) * 256
                    ]
                return carry

            lax.fori_loop(0, 16, some, 0)
        for chunk in range(RING):
            codes = jnp.concatenate(
                [lane_codes(64 * chunk), jnp.zeros((SCALE_ROWS - 1, 128), F32)], axis=0
            )
            size_in[chunk] = code_scale(codes[0:8, :])
            for way in range(2):
                own_in[2 * chunk + way, 64 : 64 + SCALE_ROWS, 0:128] = codes.astype(
                    jnp.int32
                ).astype(I16)
                own_in[2 * chunk + way, 64 : 64 + SCALE_ROWS, 128:256] = jnp.zeros(
                    (SCALE_ROWS, 128), I16
                )

    def towards(way):
        return {"blk": ring_blk((here + 1 - 2 * way + RING) % RING)}

    def move(src, got, step, way, send_sem, recv_sem):
        return pltpu.make_async_remote_copy(
            src_ref=src,
            dst_ref=got.at[way, step],
            send_sem=send_sem.at[way, step],
            recv_sem=recv_sem.at[way, step],
            device_id=towards(way),
            device_id_type=MESH,
        )

    def first_moves(own, got, send_sem, recv_sem):
        for way in range(2):
            chunk = (here - 1 + 2 * way + RING) % RING
            move(own.at[2 * chunk + way], got, 0, way, send_sem, recv_sem).start()

    def hop(rows, own, got, own_sizes, step, way, send_sem, recv_sem, keep):
        message = got.at[way, step]
        move(message, got, step, way, send_sem, recv_sem).wait_recv()
        ahead = here - 2 - step + way * (4 + 2 * step) + 2 * RING
        chunk = ahead % RING
        mine = own.at[2 * chunk + way]
        size = own_sizes(chunk)
        came = code_scale(from_codes(message[rows : rows + SCALE_ROWS, 0:128])[0:8, :])
        code = scale_code(came + size)
        whole = code_scale(code)
        blank = jnp.zeros((112, 128), F32)
        wide = message.shape[1]

        @pl.when(step < STEPS - 1)
        def _():
            shares = jnp.transpose(jnp.concatenate([came / whole, size / whole, blank], axis=0))
            for number, first in enumerate(range(0, rows, 128)):
                count = min(128, rows - first)
                there = slice(first, first + count)
                message[there, :] = to_codes(
                    from_codes(message[there, :]) * shares[0:count, number : number + 1]
                    + from_codes(mine[there, :]) * shares[0:count, 8 + number : 9 + number]
                )
            codes = jnp.concatenate([code, jnp.zeros((SCALE_ROWS - 8, 128), F32)], axis=0)
            message[rows : rows + SCALE_ROWS, 0:128] = codes.astype(jnp.int32).astype(I16)
            move(message, got, step + 1, way, send_sem, recv_sem).start()

        @pl.when(step == STEPS - 1)
        def _():
            shares = jnp.transpose(
                jnp.concatenate([came * (1.0 / TOP_CODE), size * (1.0 / TOP_CODE), blank], axis=0)
            )
            square = jnp.zeros((1, wide), F32)
            for number, first in enumerate(range(0, rows, 128)):
                count = min(128, rows - first)
                there = slice(first, first + count)
                value = (
                    from_codes(message[there, :]) * shares[0:count, number : number + 1]
                    + from_codes(mine[there, :]) * shares[0:count, 8 + number : 9 + number]
                )
                keep(first, count, value)
                square = square + jnp.sum(value * value, axis=0, keepdims=True)
            for lane in range(0, wide, 128):
                stats_ref[0:1, :] += square[:, lane : lane + 128]

    def out_hop(group, step, way):
        def keep(first, count, value):
            row = pl.multiple_of(group * OUT_ROWS + first, 16)

            @pl.when(way == 0)
            def _():
                red_out_ref[pl.ds(row, count), 0:128] = value

            @pl.when(way == 1)
            def _():
                red_out_ref[pl.ds(row, count), 128:256] = value

        hop(
            OUT_ROWS,
            own_out.at[group],
            got_out.at[group],
            lambda chunk: size_out[group],
            step,
            way,
            out_send.at[group],
            out_recv.at[group],
            keep,
        )

    def hid_hop(step, way):
        def keep(first, count, value):
            @pl.when(way == 0)
            def _():
                red_hid_ref[first : first + count, 0:128] = value

            @pl.when(way == 1)
            def _():
                red_hid_ref[first : first + count, 128:256] = value

        hop(
            HID_ROWS, own_hid, got_hid, lambda chunk: size_hid[...], step, way, hid_send, hid_recv, keep
        )

    def share_move(step, way):
        place = (here - step + 2 * step * way + 2 * RING) % RING
        return pltpu.make_async_remote_copy(
            src_ref=share_in.at[way, place],
            dst_ref=share_in.at[way, place],
            send_sem=share_send.at[way, step],
            recv_sem=share_recv.at[way, step],
            device_id=towards(way),
            device_id_type=MESH,
        )

    def in_hop(step, way):
        def keep(first, count, value):
            share_in[way, here] = value

        hop(64, own_in, got_in, lambda chunk: size_in[chunk], step, way, in_send, in_recv, keep)

        @pl.when(step == STEPS - 1)
        def _():
            share_move(0, way).start()

    def share_hop(step, way):
        share_move(step, way).wait_recv()

        @pl.when(step < STEPS - 1)
        def _():
            share_move(step + 1, way).start()

    def wave(number, carry):
        @pl.when(number == 0)
        def _():
            in_group()
            first_moves(own_in, got_in, in_send, in_recv)
            hid_group()
            first_moves(own_hid, got_hid, hid_send, hid_recv)

        @pl.when(number < OUT_GROUPS)
        def _():
            out_group(number)
            first_moves(own_out.at[number], got_out.at[number], out_send.at[number], out_recv.at[number])

        def both(way, carry):
            @pl.when((number >= 1) & (number <= STEPS))
            def _():
                in_hop(number - 1, way)
                hid_hop(number - 1, way)

            @pl.when(number > STEPS)
            def _():
                share_hop(2 * (number - STEPS - 1), way)

                @pl.when(number < STEPS + 4)
                def _():
                    share_hop(2 * (number - STEPS - 1) + 1, way)

            def outs(group, carry):
                step = number - 1 - group

                @pl.when((step >= 0) & (step < STEPS))
                def _():
                    out_hop(group, step, way)

                return carry

            lax.fori_loop(0, OUT_GROUPS, outs, 0)
            return carry

        lax.fori_loop(0, 2, both, 0)
        return carry

    lax.fori_loop(0, STEPS + OUT_GROUPS + 1, wave, 0)

    for place in range(RING):
        for way in range(2):
            red_in_ref[place * 64 : (place + 1) * 64, way * 256 : (way + 1) * 256] = share_in[
                way, place
            ]
    for copy in vec_copies:
        copy.wait_recv()
    vecs[blk] = vec_ref[...]
    total = vecs[0]
    for number in range(1, RING):
        total = total + vecs[number]
    vec_sum_ref[...] = total
    for copy in vec_copies:
        copy.wait_send()
    stage_copy(OUT_GROUPS - 1, len(BLOCKS) - 1, last_rows).wait()
    for way in range(2):
        for step in range(STEPS):
            for group in range(OUT_GROUPS):
                move(
                    got_out.at[group, way, step],
                    got_out.at[group],
                    step,
                    way,
                    out_send.at[group],
                    out_recv.at[group],
                ).wait_send()
            move(got_hid.at[way, step], got_hid, step, way, hid_send, hid_recv).wait_send()
            move(got_in.at[way, step], got_in, step, way, in_send, in_recv).wait_send()
            share_move(step, way).wait_send()


def reduce_grads(dl, h_two, res_out, dz_two, h_one, res_hid, dz_one, x, res_in, vec, senones, deep):
    wide = h_two.shape[1]
    in_wide = x.shape[1]
    vmem = pl.BlockSpec(memory_space=pltpu.VMEM)
    hbm = pl.BlockSpec(memory_space=pl.ANY)
    message = OUT_ROWS + SCALE_ROWS
    hid_message = HID_ROWS + SCALE_ROWS
    in_message = 64 + SCALE_ROWS
    sem = pltpu.SemaphoreType.DMA
    return pl.pallas_call(
        functools.partial(reduce_kernel, deep),
        out_shape=(
            jax.ShapeDtypeStruct((senones, 1, wide), F32),
            jax.ShapeDtypeStruct((HID_ROWS, wide), F32),
            jax.ShapeDtypeStruct((HID_ROWS, in_wide), F32),
            jax.ShapeDtypeStruct((OUT_GROUPS * OUT_ROWS, 256), F32),
            jax.ShapeDtypeStruct((HID_ROWS, 256), F32),
            jax.ShapeDtypeStruct((HID_ROWS, in_wide), F32),
            jax.ShapeDtypeStruct(vec.shape, F32),
            jax.ShapeDtypeStruct((8, 128), F32),
        ),
        in_specs=[vmem, vmem, hbm] + [vmem] * 7,
        out_specs=(hbm,) + (vmem,) * 7,
        scratch_shapes=[
            pltpu.VMEM((BLOCKS[0], wide), F32),
            pltpu.VMEM((BLOCKS[0], 1, wide), F32),
            pltpu.VMEM((2, BLOCKS[0], wide), BF16),
            pltpu.VMEM((640, 128), F32),
            pltpu.VMEM((OUT_GROUPS, 2 * RING, message, 128), I16),
            pltpu.VMEM((OUT_GROUPS, 2, STEPS, message, 128), I16),
            pltpu.VMEM((OUT_GROUPS, 8, 128), F32),
            pltpu.VMEM((2 * RING, hid_message, 128), I16),
            pltpu.VMEM((2, STEPS, hid_message, 128), I16),
            pltpu.VMEM((8, 128), F32),
            pltpu.VMEM((2 * RING, in_message, 256), I16),
            pltpu.VMEM((2, STEPS, in_message, 256), I16),
            pltpu.VMEM((RING, 8, 128), F32),
            pltpu.VMEM((2, RING, 64, 256), F32),
            pltpu.VMEM((RING,) + vec.shape, F32),
            sem((2,)),
            sem((1,)),
            sem((OUT_GROUPS, 2, STEPS)),
            sem((OUT_GROUPS, 2, STEPS)),
            sem((2, STEPS)),
            sem((2, STEPS)),
            sem((2, STEPS)),
            sem((2, STEPS)),
            sem((2, STEPS)),
            sem((2, STEPS)),
            sem((STEPS,)),
            sem((STEPS,)),
        ],
        compiler_params=pltpu.CompilerParams(
            collective_id=1, has_side_effects=True, vmem_limit_bytes=62 * 1024 * 1024
        ),
    )(dl, h_two, res_out, dz_two, h_one, res_hid, dz_one, x, res_in, vec)


def plain_body(
    frames,
    labels,
    mask,
    w_input,
    w_hidden,
    w_output,
    biases,
    mom_input,
    mom_hidden,
    out_first,
    out_second,
    bias_first,
    bias_second,
    res_input,
    res_hidden,
    res_output,
):
    ncol = lax.axis_size("col")
    nblk = lax.axis_size("blk")
    col_index = lax.axis_index("col")
    hcol = w_input.shape[1]
    scol = w_output.shape[1]
    micro = frames.shape[0]
    slot_count = frames.shape[1] * micro * nblk * ncol
    bias_row = biases[0]
    b_one = bias_row[:hcol]
    b_two = bias_row[hcol : 2 * hcol]
    b_out = bias_row[2 * hcol :]
    low_input = w_input.astype(jnp.bfloat16)
    row_tags = jnp.where(mask > 0, labels, -1)
    grad_input = jnp.zeros(w_input.shape, jnp.float32)
    grad_hidden = jnp.zeros((w_hidden.shape[0] * nblk, hcol), jnp.float32)
    grad_output = jnp.zeros((w_output.shape[0] * nblk, scol), jnp.float32)
    grad_bias = jnp.zeros(bias_row.shape, jnp.float32)
    loss_local = jnp.zeros((), jnp.float32)
    for micro_step in range(micro):
        low_hidden, low_output = (
            lax.all_gather(w_hidden.astype(jnp.bfloat16), "blk", axis=0, tiled=True),
            lax.all_gather(w_output.astype(jnp.bfloat16), "blk", axis=0, tiled=True),
        )
        inputs = lax.all_gather(frames[micro_step], "col", axis=0, tiled=True)
        tags_group = lax.all_gather(row_tags[micro_step], "col", axis=0, tiled=True)
        sig_one = jax.nn.sigmoid(matmul(inputs, low_input) + b_one)
        h_one = spread_cols(sig_one.astype(jnp.bfloat16))
        sig_two = jax.nn.sigmoid(matmul(h_one, low_hidden) + b_two)
        h_two = spread_cols(sig_two.astype(jnp.bfloat16))
        logits = matmul(h_two, low_output) + b_out
        row_top = lax.pmax(jnp.max(logits, axis=1), "col")
        exponent = jnp.exp(logits - row_top[:, None])
        target_hit = jnp.arange(scol)[None, :] == (tags_group - col_index * scol)[:, None]
        row_total, picked = lax.psum(
            (jnp.sum(exponent, axis=1), jnp.sum(jnp.where(target_hit, logits, 0.0), axis=1)), "col"
        )
        live_rows = tags_group >= 0
        loss_local = loss_local + jnp.sum(
            jnp.where(live_rows, row_top + jnp.log(row_total) - picked, 0.0)
        )
        probs = exponent / row_total[:, None]
        d_logits = (
            jnp.where(live_rows[:, None], probs - target_hit.astype(jnp.float32), 0.0) / slot_count
        ).astype(jnp.bfloat16)
        grad_output = grad_output + inner_rows(h_two, d_logits)
        d_h_two = reduce_cols(outer_cols(d_logits, low_output))
        d_z_two = (d_h_two * sig_two * (1.0 - sig_two)).astype(jnp.bfloat16)
        grad_hidden = grad_hidden + inner_rows(h_one, d_z_two)
        d_h_one = reduce_cols(outer_cols(d_z_two, low_hidden))
        d_z_one = (d_h_one * sig_one * (1.0 - sig_one)).astype(jnp.bfloat16)
        grad_input = grad_input + inner_rows(inputs, d_z_one)
        grad_bias = grad_bias + jnp.concatenate(
            [
                jnp.sum(d_z_one.astype(jnp.float32), axis=0),
                jnp.sum(d_z_two.astype(jnp.float32), axis=0),
                jnp.sum(d_logits.astype(jnp.float32), axis=0),
            ]
        )
    q_input, next_res_input = squash(grad_input, res_input[0])
    q_hidden, next_res_hidden = squash(grad_hidden, res_hidden[0])
    q_output, next_res_output = squash(grad_output, res_output[0])
    red_hidden, red_output = (
        lax.psum_scatter(q_hidden, "blk", scatter_dimension=0, tiled=True),
        lax.psum_scatter(q_output, "blk", scatter_dimension=0, tiled=True),
    )
    red_input, red_bias, loss_sum = lax.psum((q_input, grad_bias, loss_local), "blk")
    share_blk = 1.0 / nblk
    grad_square = (
        share_blk * (jnp.sum(red_input * red_input) + jnp.sum(red_bias * red_bias))
        + jnp.sum(red_hidden * red_hidden)
        + jnp.sum(red_output * red_output)
    )
    clip_norm = jnp.sqrt(lax.psum(grad_square, ("blk", "col")))
    factor = jnp.minimum(1.0, CLIP / clip_norm)
    next_mom_input = 0.5 * mom_input + factor * red_input
    next_mom_hidden = 0.5 * mom_hidden + factor * red_hidden
    square_input, square_hidden = lax.psum(
        (
            share_blk * jnp.sum(next_mom_input * next_mom_input),
            jnp.sum(next_mom_hidden * next_mom_hidden),
        ),
        ("blk", "col"),
    )
    iter_input = next_mom_input / (jnp.sqrt(square_input) + 1e-07)
    iter_hidden = next_mom_hidden / (jnp.sqrt(square_hidden) + 1e-07)
    for turn_index in range(NS):
        rows_hidden = collect_rows(iter_hidden)
        gram_input, gram_hidden = lax.psum(
            (precise(iter_input, iter_input.T), precise(iter_hidden, rows_hidden.T)), "col"
        )
        image_input = precise(gram_input, iter_input)
        image_hidden = precise(gram_hidden, rows_hidden)
        iter_input = (
            NS_A * iter_input + NS_B * image_input + NS_C * precise(gram_input, image_input)
        )
        iter_hidden = (
            NS_A * iter_hidden
            + NS_B * image_hidden
            + NS_C * precise(gram_hidden, collect_rows(image_hidden))
        )
    muon_scale = LR_MUON * 0.2 * math.sqrt(hcol * ncol)
    new_input = w_input * (1.0 - LR_MUON * WD_MUON) - muon_scale * iter_input
    new_hidden = w_hidden * (1.0 - LR_MUON * WD_MUON) - muon_scale * iter_hidden
    new_output, next_out_first, next_out_second = adam_step(
        w_output, factor * red_output, out_first, out_second
    )
    new_biases, next_bias_first, next_bias_second = adam_step(
        biases, factor * red_bias[None, :], bias_first, bias_second
    )
    return (
        loss_sum,
        clip_norm,
        new_input,
        new_hidden,
        new_output,
        new_biases,
        next_mom_input,
        next_mom_hidden,
        next_out_first,
        next_out_second,
        next_bias_first,
        next_bias_second,
        next_res_input[None],
        next_res_hidden[None],
        next_res_output[None],
    )


def fast_body(
    frames,
    labels,
    mask,
    w_input,
    w_hidden,
    w_output,
    biases,
    mom_input,
    mom_hidden,
    out_first,
    out_second,
    bias_first,
    bias_second,
    res_input,
    res_hidden,
    res_output,
):
    ncol = lax.axis_size("col")
    nblk = lax.axis_size("blk")
    col_index = lax.axis_index("col")
    blk_index = lax.axis_index("blk")
    hcol = w_input.shape[1]
    scol = w_output.shape[1]
    micro = frames.shape[0]
    slot_count = frames.shape[1] * micro * nblk * ncol
    bias_row = biases[0]
    b_one = bias_row[:hcol]
    b_two = bias_row[hcol : 2 * hcol]
    b_out = bias_row[2 * hcol :]
    low_input = w_input.astype(jnp.bfloat16)
    own_tags = jnp.where(mask > 0, labels, -1).reshape(-1)
    own_inputs = frames.reshape(-1, frames.shape[2])
    inputs = lax.all_gather(own_inputs, "col", axis=0, tiled=True)
    tags_group = lax.all_gather(own_tags, "col", axis=0, tiled=True)
    low_hidden = collect_rows(w_hidden.astype(jnp.bfloat16))
    low_output = collect_rows(w_output.astype(jnp.bfloat16))
    sig_one = jax.nn.sigmoid(matmul(inputs, low_input) + b_one)
    h_one = spread_cols(sig_one.astype(jnp.bfloat16))
    sig_two = jax.nn.sigmoid(matmul(h_one, low_hidden) + b_two)
    h_two = spread_cols(sig_two.astype(jnp.bfloat16))
    logits = matmul(h_two, low_output) + b_out
    row_top = lax.pmax(jnp.max(logits, axis=1), "col")
    exponent = jnp.exp(logits - row_top[:, None])
    target_hit = jnp.arange(scol)[None, :] == (tags_group - col_index * scol)[:, None]
    row_total, picked = lax.psum(
        (jnp.sum(exponent, axis=1), jnp.sum(jnp.where(target_hit, logits, 0.0), axis=1)), "col"
    )
    live_rows = tags_group >= 0
    loss_local = jnp.sum(jnp.where(live_rows, row_top + jnp.log(row_total) - picked, 0.0))
    probs = exponent / row_total[:, None]
    d_logits = (
        jnp.where(live_rows[:, None], probs - target_hit.astype(jnp.float32), 0.0) / slot_count
    ).astype(jnp.bfloat16)
    d_h_two = reduce_cols(outer_cols(d_logits, low_output))
    d_z_two = (d_h_two * sig_two * (1.0 - sig_two)).astype(jnp.bfloat16)
    d_h_one = reduce_cols(outer_cols(d_z_two, low_hidden))
    d_z_one = (d_h_one * sig_one * (1.0 - sig_one)).astype(jnp.bfloat16)
    grad_bias = jnp.concatenate(
        [
            jnp.sum(d_z_one.astype(jnp.float32), axis=0),
            jnp.sum(d_z_two.astype(jnp.float32), axis=0),
            jnp.sum(d_logits.astype(jnp.float32), axis=0),
        ]
    )
    deep = w_input.shape[0]
    padded = 512
    rows_out = OUT_GROUPS * OUT_ROWS
    vec = jnp.concatenate([grad_bias, loss_local[None]])
    vec = jnp.pad(vec, (0, 4096 - vec.shape[0])).reshape(32, 128)
    next_out, next_hid, next_in, red_out, red_hid, red_in, vec_sum, stats = reduce_grads(
        jnp.pad(d_logits, ((0, 0), (0, rows_out - scol))).T,
        h_two,
        jnp.pad(res_output[0], ((0, 0), (0, rows_out - scol))).T,
        d_z_two.T,
        h_one,
        res_hidden[0].T,
        d_z_one.T,
        jnp.pad(inputs, ((0, 0), (0, padded - deep))),
        jnp.pad(res_input[0], ((0, padded - deep), (0, 0))).T,
        vec,
        scol,
        deep,
    )
    next_res_output = next_out.transpose(1, 2, 0)
    next_res_hidden = next_hid.T
    next_res_input = next_in[:, :deep].T
    red_output = red_out[:scol].T
    red_hidden = red_hid.T
    red_input = red_in[:, :deep].T
    vec_sum = vec_sum.reshape(-1)
    red_bias = vec_sum[: bias_row.shape[0]]
    loss_sum = vec_sum[bias_row.shape[0]]
    share_blk = 1.0 / nblk
    grad_square = share_blk * jnp.sum(red_bias * red_bias) + jnp.sum(stats)
    clip_norm = jnp.sqrt(lax.psum(grad_square, ("blk", "col")))
    factor = jnp.minimum(1.0, CLIP / clip_norm)
    next_mom_input = 0.5 * mom_input + factor * red_input
    next_mom_hidden = 0.5 * mom_hidden + factor * red_hidden
    square_input, square_hidden = lax.psum(
        (
            share_blk * jnp.sum(next_mom_input * next_mom_input),
            jnp.sum(next_mom_hidden * next_mom_hidden),
        ),
        ("blk", "col"),
    )
    iter_input = next_mom_input / (jnp.sqrt(square_input) + 1e-07)
    iter_hidden = next_mom_hidden / (jnp.sqrt(square_hidden) + 1e-07)
    tall = collect_rows(iter_hidden)
    piece = hcol // 4
    mine = lax.dynamic_slice_in_dim(tall, (blk_index % 4) * piece, piece, axis=1).T
    whole_input = spread_cols(jnp.pad(iter_input, ((0, padded - deep), (0, 0))))
    done_hidden, done_input = muon(mine, whole_input, w_hidden.shape[0], hcol)
    done_hidden = done_hidden.reshape(hcol, w_hidden.shape[0]).T
    muon_scale = LR_MUON * 0.2 * math.sqrt(hcol * ncol)
    new_input = w_input * (1.0 - LR_MUON * WD_MUON) - muon_scale * done_input[:deep]
    new_hidden = w_hidden * (1.0 - LR_MUON * WD_MUON) - muon_scale * done_hidden
    new_output, next_out_first, next_out_second = adam_step(
        w_output, factor * red_output, out_first, out_second
    )
    new_biases, next_bias_first, next_bias_second = adam_step(
        biases, factor * red_bias[None, :], bias_first, bias_second
    )
    return (
        loss_sum,
        clip_norm,
        new_input,
        new_hidden,
        new_output,
        new_biases,
        next_mom_input,
        next_mom_hidden,
        next_out_first,
        next_out_second,
        next_bias_first,
        next_bias_second,
        next_res_input[None],
        next_res_hidden[None],
        next_res_output,
    )


def solution(mesh):
    in_specs = (
        P(None, ("blk", "col"), None),
        P(None, ("blk", "col")),
        P(None, ("blk", "col")),
        P(None, "col"),
        P("blk", "col"),
        P("blk", "col"),
        P("col", None),
        P(None, "col"),
        P("blk", "col"),
        P("blk", "col"),
        P("blk", "col"),
        P("col", None),
        P("col", None),
        P("blk", None, "col"),
        P("blk", None, "col"),
        P("blk", None, "col"),
    )
    out_specs = (
        P(),
        P(),
        P(None, "col"),
        P("blk", "col"),
        P("blk", "col"),
        P("col", None),
        P(None, "col"),
        P("blk", "col"),
        P("blk", "col"),
        P("blk", "col"),
        P("col", None),
        P("col", None),
        P("blk", None, "col"),
        P("blk", None, "col"),
        P("blk", None, "col"),
    )
    cubes = mesh.shape["blk"] == 8 and mesh.shape["col"] == 4
    body = fast_body if cubes else plain_body
    return jax.shard_map(body, mesh=mesh, in_specs=in_specs, out_specs=out_specs, check_vma=False)
```

```python
import functools
import math

import jax
import jax.numpy as jnp
from jax import lax
from jax.experimental import pallas as pl
from jax.experimental.pallas import tpu as pltpu
from jax.sharding import PartitionSpec as P

NS = 5
STEP = 5


NS_A = 3.4445
NS_B = -4.775
NS_C = 2.0315
CLIP = 0.002
LR_MUON = 0.1
WD_MUON = 0.01
LR_ADAM = 0.03
WD_ADAM = 0.1

MESH = pl.DeviceIdType.MESH
F32 = jnp.float32
BF16 = jnp.bfloat16
I16 = jnp.int16
LN2 = math.log(2.0)
TOP_CODE = 32700.0
LEVELS = 64.0


def matmul(left_side, right_side):
    return jnp.dot(left_side, right_side, preferred_element_type=jnp.float32)


def inner_rows(left_side, right_side):
    return lax.dot_general(
        left_side, right_side, (((0,), (0,)), ((), ())), preferred_element_type=jnp.float32
    )


def outer_cols(left_side, right_side):
    return lax.dot_general(
        left_side, right_side, (((1,), (1,)), ((), ())), preferred_element_type=jnp.float32
    )


def precise(left_side, right_side):
    return jnp.dot(
        left_side, right_side, precision=lax.Precision.HIGHEST, preferred_element_type=jnp.float32
    )


def spread_cols(values):
    return lax.all_gather(values, "col", axis=1, tiled=True)


def reduce_cols(values):
    return lax.psum_scatter(values, "col", scatter_dimension=1, tiled=True)


def collect_rows(values):
    return lax.all_gather(values, "blk", axis=0, tiled=True)


def squash(gradient, resid):
    value = gradient + resid.astype(jnp.float32)
    scale = jnp.mean(jnp.abs(value), axis=0, keepdims=True) + 1e-12
    signed = scale * jnp.tanh(2.0 * value / scale)
    return (signed, value - signed)


def adam_step(weight, gradient, first, second):
    first = 0.5 * first + 0.5 * gradient
    second = 0.95 * second + 0.05 * gradient * gradient
    update = first / (1.0 - 0.5**STEP) / (jnp.sqrt(second / (1.0 - 0.95**STEP)) + 1e-08)
    return (weight - LR_ADAM * (update + WD_ADAM * weight), first, second)


def halves(values):
    top = values.astype(BF16)
    return top, (values - top.astype(F32)).astype(BF16)


def dot_nn(left_side, right_side):
    return lax.dot_general(
        left_side, right_side, (((1,), (0,)), ((), ())), preferred_element_type=F32
    )


def dot_nt(left_side, right_side):
    return lax.dot_general(
        left_side, right_side, (((1,), (1,)), ((), ())), preferred_element_type=F32
    )


RING = 8
STEPS = RING - 1
OUT_ROWS = 592
OUT_GROUPS = 4
BLOCKS = (304, 288)
HID_ROWS = 512
SCALE_ROWS = 16


def ring_place(blk):
    odd = blk % 2
    return (blk // 2) * (1 - odd) + (7 - blk // 2) * odd


def ring_blk(place):
    back = place // 4
    return 2 * place * (1 - back) + (15 - 2 * place) * back


def scale_code(size):
    return jnp.ceil(jnp.log(jnp.maximum(size, 1e-30)) * (LEVELS / LN2))


def code_scale(code):
    return jnp.exp(code * (LN2 / LEVELS))


def to_codes(values):
    return jnp.round(values).astype(jnp.int32).astype(I16)


def from_codes(codes):
    return codes.astype(jnp.int32).astype(F32)


def reduce_kernel(
    deep,
    dl_ref,
    h_two_ref,
    res_out_ref,
    dz_two_ref,
    h_one_ref,
    res_hid_ref,
    dz_one_ref,
    x_ref,
    res_in_ref,
    vec_ref,
    next_out_ref,
    next_hid_ref,
    next_in_ref,
    red_out_ref,
    red_hid_ref,
    red_in_ref,
    vec_sum_ref,
    stats_ref,
    grad,
    stage,
    res_buf,
    marks,
    own_out,
    got_out,
    size_out,
    own_hid,
    got_hid,
    size_hid,
    own_in,
    got_in,
    size_in,
    share_in,
    vecs,
    res_sems,
    stage_sems,
    out_send,
    out_recv,
    hid_send,
    hid_recv,
    in_send,
    in_recv,
    share_send,
    share_recv,
    vec_send,
    vec_recv,
):
    blk = lax.axis_index("blk")
    here = ring_place(blk)
    total_rows = next_out_ref.shape[0]
    barrier = pltpu.get_barrier_semaphore()
    for away in range(1, RING):
        pl.semaphore_signal(
            barrier, inc=1, device_id={"blk": (blk + away) % RING}, device_id_type=MESH
        )

    starts = [sum(BLOCKS[:part]) for part in range(len(BLOCKS))]

    def res_copy(group, part):
        rows = BLOCKS[part]
        return pltpu.make_async_copy(
            res_out_ref.at[pl.ds(group * OUT_ROWS + starts[part], rows), :],
            res_buf.at[part, pl.ds(0, rows), :],
            res_sems.at[part],
        )

    def stage_copy(group, part, rows):
        return pltpu.make_async_copy(
            stage.at[pl.ds(0, rows)],
            next_out_ref.at[pl.ds(group * OUT_ROWS + starts[part], rows)],
            stage_sems.at[0],
        )

    last_rows = total_rows - (OUT_GROUPS - 1) * OUT_ROWS - starts[-1]

    def stage_start(group, part):
        if part < len(BLOCKS) - 1:
            stage_copy(group, part, BLOCKS[part]).start()
        else:

            @pl.when(group < OUT_GROUPS - 1)
            def _():
                stage_copy(group, part, BLOCKS[part]).start()

            @pl.when(group == OUT_GROUPS - 1)
            def _():
                stage_copy(group, part, last_rows).start()

    res_copy(0, 0).start()
    res_copy(0, 1).start()
    marks[...] = jnp.zeros_like(marks)
    stats_ref[...] = jnp.zeros_like(stats_ref)
    pl.semaphore_wait(barrier, RING - 1)

    vec_copies = []
    for away in range(1, RING):
        copy = pltpu.make_async_remote_copy(
            src_ref=vec_ref,
            dst_ref=vecs.at[blk],
            send_sem=vec_send.at[away - 1],
            recv_sem=vec_recv.at[away - 1],
            device_id={"blk": (blk + away) % RING},
            device_id_type=MESH,
        )
        copy.start()
        vec_copies.append(copy)

    def row_scale(value, count):
        size = jnp.sum(jnp.abs(value), axis=1, keepdims=True) * (1.0 / count) + 1e-12
        code = scale_code(size)
        return size, code, size * (TOP_CODE / code_scale(code))

    def lane_codes(first):
        return jnp.transpose(marks[first : first + 128, :])[0:1, :]

    def set_sizes(rows, own, sizes):
        parts = [lane_codes(first) for first in range(0, rows, 128)]
        parts.append(jnp.zeros((SCALE_ROWS - len(parts), 128), F32))
        codes = jnp.concatenate(parts, axis=0)
        sizes[...] = code_scale(codes[0:8, :])
        for number in range(2 * RING):
            own[number, rows : rows + SCALE_ROWS, :] = codes.astype(jnp.int32).astype(I16)

    def squash_rows(first, count, own, first_own, read_res, write_next):
        def some(number, carry):
            row = pl.multiple_of(number * 16, 16)
            value = grad[pl.ds(row, 16), :] + read_res(row)
            size, code, factor = row_scale(value, value.shape[1])
            grad[pl.ds(row, 16), :] = value
            marks[pl.ds(first_own + row, 16), :] = jnp.broadcast_to(code, (16, 128))
            steep = 2.0 / size
            for lane in range(0, value.shape[1], 128):
                piece = grad[pl.ds(row, 16), lane : lane + 128]
                curve = jnp.tanh(piece * steep)
                number_of = lane // 256
                chunk = number_of // 2 if number_of % 2 == 0 else 7 - number_of // 2
                own[2 * chunk + lane // 128 % 2, pl.ds(first_own + row, 16), :] = to_codes(
                    curve * factor
                )
                write_next(row, lane, piece - size * curve)
            return carry

        lax.fori_loop(0, count // 16, some, 0)

    def out_group(group):
        for part, rows in enumerate(BLOCKS):
            base = pl.multiple_of(group * OUT_ROWS + starts[part], 16)
            for lane in range(0, grad.shape[1], 512):
                grad[0:rows, lane : lane + 512] = dot_nn(
                    dl_ref[pl.ds(base, rows), :], h_two_ref[:, lane : lane + 512]
                )
            res_copy(group, part).wait()
            if part == 0:

                @pl.when(group > 0)
                def _():
                    stage_copy(group - 1, len(BLOCKS) - 1, BLOCKS[-1]).wait()

            else:
                stage_copy(group, part - 1, BLOCKS[part - 1]).wait()

            def write_next(row, lane, values):
                stage[pl.ds(row, 16), 0, lane : lane + 128] = values

            squash_rows(
                0,
                rows,
                own_out.at[group],
                starts[part],
                lambda row, part=part: res_buf[part, pl.ds(row, 16), :].astype(F32),
                write_next,
            )
            stage_start(group, part)

            @pl.when(group < OUT_GROUPS - 1)
            def _(part=part):
                res_copy(group + 1, part).start()

        set_sizes(OUT_ROWS, own_out.at[group], size_out.at[group])

    def hid_group():
        for first in range(0, HID_ROWS, 256):
            for lane in range(0, grad.shape[1], 512):
                grad[0:256, lane : lane + 512] = dot_nn(
                    dz_two_ref[first : first + 256, :], h_one_ref[:, lane : lane + 512]
                )

            def write_next(row, lane, values, first=first):
                next_hid_ref[pl.ds(first + row, 16), lane : lane + 128] = values

            squash_rows(
                0,
                256,
                own_hid,
                first,
                lambda row, first=first: res_hid_ref[pl.ds(first + row, 16), :].astype(F32),
                write_next,
            )
        set_sizes(HID_ROWS, own_hid, size_hid)

    def in_group():
        wide = x_ref.shape[1]
        for first in range(0, HID_ROWS, 256):
            grad[0:256, 0:wide] = dot_nn(dz_one_ref[first : first + 256, :], x_ref[...])

            def some(number, carry, first=first):
                row = pl.multiple_of(number * 16, 16)
                place = pl.multiple_of(first + row, 16)
                value = grad[pl.ds(row, 16), 0:wide] + res_in_ref[pl.ds(place, 16), :].astype(F32)
                size, code, factor = row_scale(value, deep)
                curve = jnp.tanh(value * (2.0 / size))
                next_in_ref[pl.ds(place, 16), :] = value - size * curve
                marks[pl.ds(place, 16), :] = jnp.broadcast_to(code, (16, 128))
                chunk = first // 64 + number // 4
                inside = pl.multiple_of(number % 4 * 16, 16)
                codes = to_codes(curve * factor)
                for way in range(2):
                    own_in[2 * chunk + way, pl.ds(inside, 16), :] = codes[
                        :, way * 256 : (way + 1) * 256
                    ]
                return carry

            lax.fori_loop(0, 16, some, 0)
        for chunk in range(RING):
            codes = jnp.concatenate(
                [lane_codes(64 * chunk), jnp.zeros((SCALE_ROWS - 1, 128), F32)], axis=0
            )
            size_in[chunk] = code_scale(codes[0:8, :])
            for way in range(2):
                own_in[2 * chunk + way, 64 : 64 + SCALE_ROWS, 0:128] = codes.astype(
                    jnp.int32
                ).astype(I16)
                own_in[2 * chunk + way, 64 : 64 + SCALE_ROWS, 128:256] = jnp.zeros(
                    (SCALE_ROWS, 128), I16
                )

    def towards(way):
        return {"blk": ring_blk((here + 1 - 2 * way + RING) % RING)}

    def move(src, got, step, way, send_sem, recv_sem):
        return pltpu.make_async_remote_copy(
            src_ref=src,
            dst_ref=got.at[way, step],
            send_sem=send_sem.at[way, step],
            recv_sem=recv_sem.at[way, step],
            device_id=towards(way),
            device_id_type=MESH,
        )

    def first_moves(own, got, send_sem, recv_sem):
        for way in range(2):
            chunk = (here - 1 + 2 * way + RING) % RING
            move(own.at[2 * chunk + way], got, 0, way, send_sem, recv_sem).start()

    def hop(rows, own, got, own_sizes, step, way, send_sem, recv_sem, keep):
        message = got.at[way, step]
        move(message, got, step, way, send_sem, recv_sem).wait_recv()
        ahead = here - 2 - step + way * (4 + 2 * step) + 2 * RING
        chunk = ahead % RING
        mine = own.at[2 * chunk + way]
        size = own_sizes(chunk)
        came = code_scale(from_codes(message[rows : rows + SCALE_ROWS, 0:128])[0:8, :])
        code = scale_code(came + size)
        whole = code_scale(code)
        blank = jnp.zeros((112, 128), F32)
        wide = message.shape[1]

        @pl.when(step < STEPS - 1)
        def _():
            shares = jnp.transpose(jnp.concatenate([came / whole, size / whole, blank], axis=0))
            for number, first in enumerate(range(0, rows, 128)):
                count = min(128, rows - first)
                there = slice(first, first + count)
                message[there, :] = to_codes(
                    from_codes(message[there, :]) * shares[0:count, number : number + 1]
                    + from_codes(mine[there, :]) * shares[0:count, 8 + number : 9 + number]
                )
            codes = jnp.concatenate([code, jnp.zeros((SCALE_ROWS - 8, 128), F32)], axis=0)
            message[rows : rows + SCALE_ROWS, 0:128] = codes.astype(jnp.int32).astype(I16)
            move(message, got, step + 1, way, send_sem, recv_sem).start()

        @pl.when(step == STEPS - 1)
        def _():
            shares = jnp.transpose(
                jnp.concatenate([came * (1.0 / TOP_CODE), size * (1.0 / TOP_CODE), blank], axis=0)
            )
            square = jnp.zeros((1, wide), F32)
            for number, first in enumerate(range(0, rows, 128)):
                count = min(128, rows - first)
                there = slice(first, first + count)
                value = (
                    from_codes(message[there, :]) * shares[0:count, number : number + 1]
                    + from_codes(mine[there, :]) * shares[0:count, 8 + number : 9 + number]
                )
                keep(first, count, value)
                square = square + jnp.sum(value * value, axis=0, keepdims=True)
            for lane in range(0, wide, 128):
                stats_ref[0:1, :] += square[:, lane : lane + 128]

    def out_hop(group, step, way):
        def keep(first, count, value):
            row = pl.multiple_of(group * OUT_ROWS + first, 16)

            @pl.when(way == 0)
            def _():
                red_out_ref[pl.ds(row, count), 0:128] = value

            @pl.when(way == 1)
            def _():
                red_out_ref[pl.ds(row, count), 128:256] = value

        hop(
            OUT_ROWS,
            own_out.at[group],
            got_out.at[group],
            lambda chunk: size_out[group],
            step,
            way,
            out_send.at[group],
            out_recv.at[group],
            keep,
        )

    def hid_hop(step, way):
        def keep(first, count, value):
            @pl.when(way == 0)
            def _():
                red_hid_ref[first : first + count, 0:128] = value

            @pl.when(way == 1)
            def _():
                red_hid_ref[first : first + count, 128:256] = value

        hop(
            HID_ROWS, own_hid, got_hid, lambda chunk: size_hid[...], step, way, hid_send, hid_recv, keep
        )

    def share_move(step, way):
        place = (here - step + 2 * step * way + 2 * RING) % RING
        return pltpu.make_async_remote_copy(
            src_ref=share_in.at[way, place],
            dst_ref=share_in.at[way, place],
            send_sem=share_send.at[way, step],
            recv_sem=share_recv.at[way, step],
            device_id=towards(way),
            device_id_type=MESH,
        )

    def in_hop(step, way):
        def keep(first, count, value):
            share_in[way, here] = value

        hop(64, own_in, got_in, lambda chunk: size_in[chunk], step, way, in_send, in_recv, keep)

        @pl.when(step == STEPS - 1)
        def _():
            share_move(0, way).start()

    def share_hop(step, way):
        share_move(step, way).wait_recv()

        @pl.when(step < STEPS - 1)
        def _():
            share_move(step + 1, way).start()

    def wave(number, carry):
        @pl.when(number == 0)
        def _():
            in_group()
            first_moves(own_in, got_in, in_send, in_recv)
            hid_group()
            first_moves(own_hid, got_hid, hid_send, hid_recv)

        @pl.when(number < OUT_GROUPS)
        def _():
            out_group(number)
            first_moves(own_out.at[number], got_out.at[number], out_send.at[number], out_recv.at[number])

        def both(way, carry):
            @pl.when((number >= 1) & (number <= STEPS))
            def _():
                in_hop(number - 1, way)
                hid_hop(number - 1, way)

            @pl.when(number > STEPS)
            def _():
                share_hop(2 * (number - STEPS - 1), way)

                @pl.when(number < STEPS + 4)
                def _():
                    share_hop(2 * (number - STEPS - 1) + 1, way)

            def outs(group, carry):
                step = number - 1 - group

                @pl.when((step >= 0) & (step < STEPS))
                def _():
                    out_hop(group, step, way)

                return carry

            lax.fori_loop(0, OUT_GROUPS, outs, 0)
            return carry

        lax.fori_loop(0, 2, both, 0)
        return carry

    lax.fori_loop(0, STEPS + OUT_GROUPS + 1, wave, 0)

    for place in range(RING):
        for way in range(2):
            red_in_ref[place * 64 : (place + 1) * 64, way * 256 : (way + 1) * 256] = share_in[
                way, place
            ]
    for copy in vec_copies:
        copy.wait_recv()
    vecs[blk] = vec_ref[...]
    total = vecs[0]
    for number in range(1, RING):
        total = total + vecs[number]
    vec_sum_ref[...] = total
    for copy in vec_copies:
        copy.wait_send()
    stage_copy(OUT_GROUPS - 1, len(BLOCKS) - 1, last_rows).wait()
    for way in range(2):
        for step in range(STEPS):
            for group in range(OUT_GROUPS):
                move(
                    got_out.at[group, way, step],
                    got_out.at[group],
                    step,
                    way,
                    out_send.at[group],
                    out_recv.at[group],
                ).wait_send()
            move(got_hid.at[way, step], got_hid, step, way, hid_send, hid_recv).wait_send()
            move(got_in.at[way, step], got_in, step, way, in_send, in_recv).wait_send()
            share_move(step, way).wait_send()


def reduce_grads(dl, h_two, res_out, dz_two, h_one, res_hid, dz_one, x, res_in, vec, senones, deep):
    wide = h_two.shape[1]
    in_wide = x.shape[1]
    vmem = pl.BlockSpec(memory_space=pltpu.VMEM)
    hbm = pl.BlockSpec(memory_space=pl.ANY)
    message = OUT_ROWS + SCALE_ROWS
    hid_message = HID_ROWS + SCALE_ROWS
    in_message = 64 + SCALE_ROWS
    sem = pltpu.SemaphoreType.DMA
    return pl.pallas_call(
        functools.partial(reduce_kernel, deep),
        out_shape=(
            jax.ShapeDtypeStruct((senones, 1, wide), F32),
            jax.ShapeDtypeStruct((HID_ROWS, wide), F32),
            jax.ShapeDtypeStruct((HID_ROWS, in_wide), F32),
            jax.ShapeDtypeStruct((OUT_GROUPS * OUT_ROWS, 256), F32),
            jax.ShapeDtypeStruct((HID_ROWS, 256), F32),
            jax.ShapeDtypeStruct((HID_ROWS, in_wide), F32),
            jax.ShapeDtypeStruct(vec.shape, F32),
            jax.ShapeDtypeStruct((8, 128), F32),
        ),
        in_specs=[vmem, vmem, hbm] + [vmem] * 7,
        out_specs=(hbm,) + (vmem,) * 7,
        scratch_shapes=[
            pltpu.VMEM((BLOCKS[0], wide), F32),
            pltpu.VMEM((BLOCKS[0], 1, wide), F32),
            pltpu.VMEM((2, BLOCKS[0], wide), BF16),
            pltpu.VMEM((640, 128), F32),
            pltpu.VMEM((OUT_GROUPS, 2 * RING, message, 128), I16),
            pltpu.VMEM((OUT_GROUPS, 2, STEPS, message, 128), I16),
            pltpu.VMEM((OUT_GROUPS, 8, 128), F32),
            pltpu.VMEM((2 * RING, hid_message, 128), I16),
            pltpu.VMEM((2, STEPS, hid_message, 128), I16),
            pltpu.VMEM((8, 128), F32),
            pltpu.VMEM((2 * RING, in_message, 256), I16),
            pltpu.VMEM((2, STEPS, in_message, 256), I16),
            pltpu.VMEM((RING, 8, 128), F32),
            pltpu.VMEM((2, RING, 64, 256), F32),
            pltpu.VMEM((RING,) + vec.shape, F32),
            sem((2,)),
            sem((1,)),
            sem((OUT_GROUPS, 2, STEPS)),
            sem((OUT_GROUPS, 2, STEPS)),
            sem((2, STEPS)),
            sem((2, STEPS)),
            sem((2, STEPS)),
            sem((2, STEPS)),
            sem((2, STEPS)),
            sem((2, STEPS)),
            sem((STEPS,)),
            sem((STEPS,)),
        ],
        compiler_params=pltpu.CompilerParams(
            collective_id=1, has_side_effects=True, vmem_limit_bytes=62 * 1024 * 1024
        ),
    )(dl, h_two, res_out, dz_two, h_one, res_hid, dz_one, x, res_in, vec)


DIM_BITS = (2, 4, 8)
ORDERS = ((0, 1, 2), (1, 2, 0), (2, 0, 1))
PIECE = 48
LIGHT_HID = 3
LIGHT_IN = 2


def stage_sends(stage, sources):
    moves = []
    for piece, order in enumerate(ORDERS):
        slot = sum(DIM_BITS[order[index]] for index in sources)
        moves.append((piece, slot, order[stage]))
    return moves


def landed(moves):
    return [(slot | DIM_BITS[dim], piece) for piece, slot, dim in moves]


FIRST = stage_sends(0, ())
SECOND = stage_sends(1, ())
SECOND_ON = stage_sends(1, (0,))
THIRD = stage_sends(2, ())
THIRD_A = stage_sends(2, (0,))
THIRD_B = stage_sends(2, (1,))
THIRD_C = stage_sends(2, (0, 1))
MOVES = FIRST + SECOND + SECOND_ON + THIRD + THIRD_A + THIRD_B + THIRD_C


def muon_kernel(
    stats_ref,
    red_hid_ref,
    mom_hid_ref,
    red_in_ref,
    mom_in_ref,
    hid_ref,
    inp_ref,
    next_hid_ref,
    next_in_ref,
    norm_ref,
    codes,
    tops,
    lows,
    scales,
    xs,
    us,
    vs,
    lhs,
    xin,
    xin_top,
    xin_low,
    gram,
    gram_got,
    back,
    sums,
    sums_got,
    send_sems,
    core_sems,
    recv_sems,
    back_send,
    back_recv,
    sums_send,
    sums_recv,
    spread_send,
    spread_recv,
    pair_send,
    pair_recv,
):
    blk = lax.axis_index("blk")
    col = lax.axis_index("col")
    rows, wide = xs.shape
    height = back.shape[2]
    part_wide = inp_ref.shape[1]
    other_core = {"col": col + 1 - 2 * (col % 2)}
    dims = (
        {"blk": blk + 1 - 2 * (blk % 2)},
        {"col": (col + 2) % 4},
        {"blk": blk + 2 - 4 * ((blk // 2) % 2)},
    )
    far = {"blk": (blk + 4) % 8}
    diagonal = {"blk": 4 * (blk // 4) + 3 - blk % 4}
    barrier = pltpu.get_barrier_semaphore()
    for target in (other_core, dims[1], *({"blk": (blk + away) % 8} for away in range(1, 8))):
        pl.semaphore_signal(barrier, inc=1, device_id=target, device_id_type=MESH)

    def fold(values):
        line = jnp.sum(values, axis=0, keepdims=True)
        return sum(line[:, lane : lane + 128] for lane in range(0, line.shape[1], 128))

    share = 0.125
    sums[0, 0:1, :] = fold(stats_ref[...])
    sums[0, 1:2, :] = fold(mom_hid_ref[...] * mom_hid_ref[...])
    sums[0, 2:3, :] = fold(mom_hid_ref[...] * red_hid_ref[...])
    sums[0, 3:4, :] = fold(red_hid_ref[...] * red_hid_ref[...])
    sums[0, 4:5, :] = fold(mom_in_ref[...] * mom_in_ref[...]) * share
    sums[0, 5:6, :] = fold(mom_in_ref[...] * red_in_ref[...]) * share
    sums[0, 6:7, :] = fold(red_in_ref[...] * red_in_ref[...]) * share
    sums[0, 7:8, :] = jnp.zeros((1, 128), F32)
    for turn in range(2):
        codes[turn, 0, rows:, :] = jnp.zeros((codes.shape[2] - rows, wide), I16)
    eye = lax.broadcasted_iota(jnp.int32, (rows, rows), 0) == lax.broadcasted_iota(
        jnp.int32, (rows, rows), 1
    )
    pl.semaphore_wait(barrier, 9)

    for number, target in enumerate((other_core, *dims, far)):
        copy = pltpu.make_async_remote_copy(
            src_ref=sums.at[number],
            dst_ref=sums_got.at[number],
            send_sem=sums_send.at[number],
            recv_sem=sums_recv.at[number],
            device_id=target,
            device_id_type=MESH,
        )
        copy.start()
        copy.wait()
        sums[number + 1] = sums[number] + sums_got[number]
    whole = jnp.sum(sums[5], axis=1, keepdims=True)
    clip = jnp.sqrt(whole[0:1])
    factor = jnp.minimum(1.0, CLIP / clip)

    def norm_of(first):
        square = (
            0.25 * whole[first : first + 1]
            + factor * whole[first + 1 : first + 2]
            + factor * factor * whole[first + 2 : first + 3]
        )
        return 1.0 / (jnp.sqrt(jnp.maximum(square, 0.0)) + 1e-07)

    norm_ref[0:4, :] = jnp.broadcast_to(clip, (4, 128))
    norm_ref[4:8, :] = jnp.broadcast_to(factor, (4, 128))
    next_hid_ref[...] = 0.5 * mom_hid_ref[...] + factor * red_hid_ref[...]
    next_in_ref[...] = 0.5 * mom_in_ref[...] + factor * red_in_ref[...]

    my_lanes = pl.ds(pl.multiple_of(blk * height, height), height)
    spread = []
    for away in range(1, 8):
        target = (blk + away) % 8
        spread.append(
            pltpu.make_async_remote_copy(
                src_ref=next_hid_ref.at[
                    pl.ds(pl.multiple_of(target % 4 * rows, rows), rows), :
                ],
                dst_ref=xs.at[:, my_lanes],
                send_sem=spread_send.at[away - 1],
                recv_sem=spread_recv.at[away - 1],
                device_id={"blk": target},
                device_id_type=MESH,
            )
        )
        spread[-1].start()
    high = col // 2
    my_half = pl.ds(pl.multiple_of(high * part_wide, part_wide), part_wide)
    half_copy = pltpu.make_async_remote_copy(
        src_ref=next_in_ref,
        dst_ref=xin.at[:, my_half],
        send_sem=pair_send.at[0],
        recv_sem=pair_recv.at[0],
        device_id=dims[1],
        device_id_type=MESH,
    )
    half_copy.start()
    xs[:, my_lanes] = next_hid_ref[pl.ds(pl.multiple_of(blk % 4 * rows, rows), rows), :]
    xin[:, my_half] = next_in_ref[...]
    for copy in spread:
        copy.wait_recv()
    xs[...] = xs[...] * norm_of(1)
    in_scale = norm_of(4)

    numbers = {move: number for number, move in enumerate(MOVES)}

    def part(turn, slot, piece):
        return codes.at[turn, slot, pl.ds(piece * PIECE, PIECE), :]

    def send(turn, move):
        piece, slot, dim = move
        return pltpu.make_async_remote_copy(
            src_ref=part(turn, slot, piece),
            dst_ref=part(turn, slot | DIM_BITS[dim], piece),
            send_sem=send_sems.at[numbers[move]],
            recv_sem=recv_sems.at[turn, slot | DIM_BITS[dim], piece],
            device_id=dims[dim],
            device_id_type=MESH,
        )

    def send_all(turn, moves):
        for move in moves:
            send(turn, move).start()

    def to_core(turn, slot, piece):
        return pltpu.make_async_remote_copy(
            src_ref=part(turn, slot, piece),
            dst_ref=part(turn, slot + 1, piece),
            send_sem=core_sems.at[slot // 2, piece],
            recv_sem=recv_sems.at[turn, slot + 1, piece],
            device_id=other_core,
            device_id_type=MESH,
        )

    def arrived(turn, slot, piece):
        pltpu.make_async_remote_copy(
            src_ref=part(turn, slot, piece),
            dst_ref=part(turn, slot, piece),
            send_sem=core_sems.at[0, 0],
            recv_sem=recv_sems.at[turn, slot, piece],
            device_id=other_core,
            device_id_type=MESH,
        ).wait_recv()

    def forward(turn, moves, on=()):
        for number, (slot, piece) in enumerate(landed(moves)):
            arrived(turn, slot, piece)
            to_core(turn, slot, piece).start()
            if on:
                send(turn, on[number]).start()

    def gram_copy():
        return pltpu.make_async_remote_copy(
            src_ref=gram,
            dst_ref=gram_got,
            send_sem=pair_send.at[1],
            recv_sem=pair_recv.at[1],
            device_id=other_core,
            device_id_type=MESH,
        )

    def unpack(turn, pair, light):
        for core in range(2):
            here = slice(core * rows, (core + 1) * rows)
            whole = from_codes(codes[turn, 2 * pair + core, 0:rows, :])
            if light:
                tops[pair, here, :] = whole.astype(BF16)
            else:
                top, low = halves(whole)
                tops[pair, here, :] = top
                lows[pair, here, :] = low
            step = from_codes(codes[turn, 2 * pair + core, rows : rows + 16, 0:rows])
            size = code_scale(step[0:8, :]) * (1.0 / TOP_CODE)
            scales[pair, :, here] = size * size

    def apply_pair(pair, out, light):
        cut = 512
        if light:
            inner = (dot_nt(lhs[0:rows, :], tops[pair]) * scales[pair, 0:1, :]).astype(BF16)
            for start in range(0, wide, cut):
                lanes = slice(start, start + cut)
                out[:, lanes] += dot_nn(inner, tops[pair, :, lanes])
            return
        both = dot_nt(lhs[...], tops[pair])
        inner = both[:rows] + both[rows:] + dot_nt(lhs[0:rows, :], lows[pair])
        inner = inner * scales[pair, 0:1, :]
        top, low = halves(inner)
        stack = jnp.concatenate([top, low], axis=0)
        for start in range(0, wide, cut):
            lanes = slice(start, start + cut)
            both = dot_nn(stack, tops[pair, :, lanes])
            out[:, lanes] += both[:rows] + both[rows:] + dot_nn(top, lows[pair, :, lanes])

    def set_lhs(values):
        top, low = halves(values)
        lhs[0:rows, :] = top
        lhs[rows:, :] = low

    def input_gram(light):
        top, low = halves(xin[...])
        xin_top[...] = top
        if light:
            gram[...] = dot_nt(xin_top[...], xin_top[...])
        else:
            xin_low[...] = low
            cross = dot_nt(xin_top[...], xin_low[...])
            gram[...] = dot_nt(xin_top[...], xin_top[...]) + (cross + jnp.transpose(cross))
        gram_copy().start()

    def input_step(light):
        gram_copy().wait()
        square_of = gram[...] + gram_got[...]
        top, low = halves(square_of)
        if light:
            poly = NS_B * square_of + NS_C * dot_nn(top, top)
        else:
            cross = dot_nn(top, low)
            poly = NS_B * square_of + NS_C * (dot_nn(top, top) + (cross + jnp.transpose(cross)))
        top, low = halves(poly)
        cut = 512
        for start in range(0, xin.shape[1], cut):
            lanes = slice(start, start + cut)
            change = dot_nn(top, xin_top[:, lanes])
            if not light:
                change = change + dot_nn(low, xin_top[:, lanes]) + dot_nn(top, xin_low[:, lanes])
            xin[:, lanes] = NS_A * xin[:, lanes] + change

    def by_weight(number, limit, work):
        @pl.when(number < limit)
        def _():
            work(True)

        @pl.when(number >= limit)
        def _():
            work(False)

    def iteration(number, carry):
        turn = number % 2
        values = xs[...]
        largest = jnp.max(jnp.abs(values), axis=1, keepdims=True)
        step = scale_code(largest)
        codes[turn, 0, 0:rows, :] = to_codes(values * (TOP_CODE / code_scale(step)))
        lane_step = jnp.sum(jnp.where(eye, step, 0.0), axis=0, keepdims=True)
        codes[turn, 0, rows : rows + 16, 0:rows] = jnp.broadcast_to(
            lane_step.astype(jnp.int32), (16, rows)
        ).astype(I16)
        send_all(turn, FIRST)
        for piece in range(3):
            to_core(turn, 0, piece).start()
        send_all(turn, SECOND)
        set_lhs(values)
        us[...] = jnp.zeros_like(us)
        vs[...] = jnp.zeros_like(vs)

        def first_pass(index, carry):
            pair = index + (index // 3) * (1 - index // 4) - (index // 4) * (1 - index // 5)

            @pl.when(index == 1)
            def _():
                forward(turn, FIRST, SECOND_ON)
                send_all(turn, THIRD)
                send_all(turn, THIRD_A)

                @pl.when(number > 0)
                def _():
                    by_weight(number, LIGHT_IN, input_gram)

                forward(turn, SECOND, THIRD_B)
                forward(turn, SECOND_ON, THIRD_C)

                @pl.when(number > 0)
                def _():
                    by_weight(number, LIGHT_IN, input_step)

                forward(turn, THIRD)

            @pl.when(index == 4)
            def _():
                forward(turn, THIRD_A)
                forward(turn, THIRD_B)

            @pl.when((index == 6) & (number == 0))
            def _():
                half_copy.wait()
                xin[...] = xin[...] * in_scale
                input_gram(True)
                input_step(True)

            @pl.when(index == 7)
            def _():
                forward(turn, THIRD_C)

            for piece in range(3):
                arrived(turn, 2 * pair + 1, piece)

            def work(light):
                unpack(turn, pair, light)
                apply_pair(pair, us, light)

            by_weight(number, LIGHT_HID, work)
            return carry

        lax.fori_loop(0, 8, first_pass, 0)
        set_lhs(us[...])

        def second_pass(pair, carry):
            by_weight(number, LIGHT_HID, lambda light: apply_pair(pair, vs, light))
            return carry

        lax.fori_loop(0, 8, second_pass, 0)
        xs[...] = NS_A * xs[...] + NS_B * us[...] + NS_C * vs[...]
        for move in MOVES:
            send(turn, move).wait_send()
        for pair in range(8):
            for piece in range(3):
                to_core(turn, 2 * pair, piece).wait_send()
        return carry

    lax.fori_loop(0, NS, iteration, 0)

    place = blk % 4
    copies = []
    for rel, target in ((1, dims[0]), (2, dims[2]), (3, diagonal)):
        copies.append(
            pltpu.make_async_remote_copy(
                src_ref=xs.at[:, pl.ds(pl.multiple_of(target["blk"] * height, height), height)],
                dst_ref=back.at[place],
                send_sem=back_send.at[rel - 1],
                recv_sem=back_recv.at[rel - 1],
                device_id=target,
                device_id_type=MESH,
            )
        )
        copies[-1].start()
    hid_ref[place] = xs[:, my_lanes]
    inp_ref[...] = xin[:, my_half]
    for copy in copies:
        copy.wait_recv()
    for target in (dims[0], dims[2], diagonal):
        other = target["blk"] % 4
        hid_ref[other] = back[other]
    for copy in copies + spread:
        copy.wait_send()


def muon(stats, red_hid, mom_hid, red_in, mom_in, wide):
    rows = red_hid.shape[0] // 4
    height = red_hid.shape[1]
    deep, part_wide = red_in.shape
    vmem = pl.BlockSpec(memory_space=pltpu.VMEM)
    sem = pltpu.SemaphoreType.DMA
    return pl.pallas_call(
        muon_kernel,
        out_shape=(
            jax.ShapeDtypeStruct((4, rows, height), F32),
            jax.ShapeDtypeStruct((deep, part_wide), F32),
            jax.ShapeDtypeStruct(red_hid.shape, F32),
            jax.ShapeDtypeStruct(red_in.shape, F32),
            jax.ShapeDtypeStruct((8, 128), F32),
        ),
        in_specs=[vmem] * 5,
        out_specs=(vmem,) * 5,
        scratch_shapes=[
            pltpu.VMEM((2, 16, 3 * PIECE, wide), I16),
            pltpu.VMEM((8, 2 * rows, wide), BF16),
            pltpu.VMEM((8, 2 * rows, wide), BF16),
            pltpu.VMEM((8, 8, 2 * rows), F32),
            pltpu.VMEM((rows, wide), F32),
            pltpu.VMEM((rows, wide), F32),
            pltpu.VMEM((rows, wide), F32),
            pltpu.VMEM((2 * rows, wide), BF16),
            pltpu.VMEM((deep, 2 * part_wide), F32),
            pltpu.VMEM((deep, 2 * part_wide), BF16),
            pltpu.VMEM((deep, 2 * part_wide), BF16),
            pltpu.VMEM((deep, deep), F32),
            pltpu.VMEM((deep, deep), F32),
            pltpu.VMEM((4, rows, height), F32),
            pltpu.VMEM((6, 8, 128), F32),
            pltpu.VMEM((5, 8, 128), F32),
            sem((len(MOVES),)),
            sem((8, 3)),
            sem((2, 16, 3)),
            sem((3,)),
            sem((3,)),
            sem((5,)),
            sem((5,)),
            sem((7,)),
            sem((7,)),
            sem((2,)),
            sem((2,)),
        ],
        compiler_params=pltpu.CompilerParams(
            collective_id=0, has_side_effects=True, vmem_limit_bytes=60 * 1024 * 1024
        ),
    )(stats, red_hid, mom_hid, red_in, mom_in)


def plain_body(
    frames,
    labels,
    mask,
    w_input,
    w_hidden,
    w_output,
    biases,
    mom_input,
    mom_hidden,
    out_first,
    out_second,
    bias_first,
    bias_second,
    res_input,
    res_hidden,
    res_output,
):
    ncol = lax.axis_size("col")
    nblk = lax.axis_size("blk")
    col_index = lax.axis_index("col")
    hcol = w_input.shape[1]
    scol = w_output.shape[1]
    micro = frames.shape[0]
    slot_count = frames.shape[1] * micro * nblk * ncol
    bias_row = biases[0]
    b_one = bias_row[:hcol]
    b_two = bias_row[hcol : 2 * hcol]
    b_out = bias_row[2 * hcol :]
    low_input = w_input.astype(jnp.bfloat16)
    row_tags = jnp.where(mask > 0, labels, -1)
    grad_input = jnp.zeros(w_input.shape, jnp.float32)
    grad_hidden = jnp.zeros((w_hidden.shape[0] * nblk, hcol), jnp.float32)
    grad_output = jnp.zeros((w_output.shape[0] * nblk, scol), jnp.float32)
    grad_bias = jnp.zeros(bias_row.shape, jnp.float32)
    loss_local = jnp.zeros((), jnp.float32)
    for micro_step in range(micro):
        low_hidden, low_output = (
            lax.all_gather(w_hidden.astype(jnp.bfloat16), "blk", axis=0, tiled=True),
            lax.all_gather(w_output.astype(jnp.bfloat16), "blk", axis=0, tiled=True),
        )
        inputs = lax.all_gather(frames[micro_step], "col", axis=0, tiled=True)
        tags_group = lax.all_gather(row_tags[micro_step], "col", axis=0, tiled=True)
        sig_one = jax.nn.sigmoid(matmul(inputs, low_input) + b_one)
        h_one = spread_cols(sig_one.astype(jnp.bfloat16))
        sig_two = jax.nn.sigmoid(matmul(h_one, low_hidden) + b_two)
        h_two = spread_cols(sig_two.astype(jnp.bfloat16))
        logits = matmul(h_two, low_output) + b_out
        row_top = lax.pmax(jnp.max(logits, axis=1), "col")
        exponent = jnp.exp(logits - row_top[:, None])
        target_hit = jnp.arange(scol)[None, :] == (tags_group - col_index * scol)[:, None]
        row_total, picked = lax.psum(
            (jnp.sum(exponent, axis=1), jnp.sum(jnp.where(target_hit, logits, 0.0), axis=1)), "col"
        )
        live_rows = tags_group >= 0
        loss_local = loss_local + jnp.sum(
            jnp.where(live_rows, row_top + jnp.log(row_total) - picked, 0.0)
        )
        probs = exponent / row_total[:, None]
        d_logits = (
            jnp.where(live_rows[:, None], probs - target_hit.astype(jnp.float32), 0.0) / slot_count
        ).astype(jnp.bfloat16)
        grad_output = grad_output + inner_rows(h_two, d_logits)
        d_h_two = reduce_cols(outer_cols(d_logits, low_output))
        d_z_two = (d_h_two * sig_two * (1.0 - sig_two)).astype(jnp.bfloat16)
        grad_hidden = grad_hidden + inner_rows(h_one, d_z_two)
        d_h_one = reduce_cols(outer_cols(d_z_two, low_hidden))
        d_z_one = (d_h_one * sig_one * (1.0 - sig_one)).astype(jnp.bfloat16)
        grad_input = grad_input + inner_rows(inputs, d_z_one)
        grad_bias = grad_bias + jnp.concatenate(
            [
                jnp.sum(d_z_one.astype(jnp.float32), axis=0),
                jnp.sum(d_z_two.astype(jnp.float32), axis=0),
                jnp.sum(d_logits.astype(jnp.float32), axis=0),
            ]
        )
    q_input, next_res_input = squash(grad_input, res_input[0])
    q_hidden, next_res_hidden = squash(grad_hidden, res_hidden[0])
    q_output, next_res_output = squash(grad_output, res_output[0])
    red_hidden, red_output = (
        lax.psum_scatter(q_hidden, "blk", scatter_dimension=0, tiled=True),
        lax.psum_scatter(q_output, "blk", scatter_dimension=0, tiled=True),
    )
    red_input, red_bias, loss_sum = lax.psum((q_input, grad_bias, loss_local), "blk")
    share_blk = 1.0 / nblk
    grad_square = (
        share_blk * (jnp.sum(red_input * red_input) + jnp.sum(red_bias * red_bias))
        + jnp.sum(red_hidden * red_hidden)
        + jnp.sum(red_output * red_output)
    )
    clip_norm = jnp.sqrt(lax.psum(grad_square, ("blk", "col")))
    factor = jnp.minimum(1.0, CLIP / clip_norm)
    next_mom_input = 0.5 * mom_input + factor * red_input
    next_mom_hidden = 0.5 * mom_hidden + factor * red_hidden
    square_input, square_hidden = lax.psum(
        (
            share_blk * jnp.sum(next_mom_input * next_mom_input),
            jnp.sum(next_mom_hidden * next_mom_hidden),
        ),
        ("blk", "col"),
    )
    iter_input = next_mom_input / (jnp.sqrt(square_input) + 1e-07)
    iter_hidden = next_mom_hidden / (jnp.sqrt(square_hidden) + 1e-07)
    for turn_index in range(NS):
        rows_hidden = collect_rows(iter_hidden)
        gram_input, gram_hidden = lax.psum(
            (precise(iter_input, iter_input.T), precise(iter_hidden, rows_hidden.T)), "col"
        )
        image_input = precise(gram_input, iter_input)
        image_hidden = precise(gram_hidden, rows_hidden)
        iter_input = (
            NS_A * iter_input + NS_B * image_input + NS_C * precise(gram_input, image_input)
        )
        iter_hidden = (
            NS_A * iter_hidden
            + NS_B * image_hidden
            + NS_C * precise(gram_hidden, collect_rows(image_hidden))
        )
    muon_scale = LR_MUON * 0.2 * math.sqrt(hcol * ncol)
    new_input = w_input * (1.0 - LR_MUON * WD_MUON) - muon_scale * iter_input
    new_hidden = w_hidden * (1.0 - LR_MUON * WD_MUON) - muon_scale * iter_hidden
    new_output, next_out_first, next_out_second = adam_step(
        w_output, factor * red_output, out_first, out_second
    )
    new_biases, next_bias_first, next_bias_second = adam_step(
        biases, factor * red_bias[None, :], bias_first, bias_second
    )
    return (
        loss_sum,
        clip_norm,
        new_input,
        new_hidden,
        new_output,
        new_biases,
        next_mom_input,
        next_mom_hidden,
        next_out_first,
        next_out_second,
        next_bias_first,
        next_bias_second,
        next_res_input[None],
        next_res_hidden[None],
        next_res_output[None],
    )


def fast_body(
    frames,
    labels,
    mask,
    w_input,
    w_hidden,
    w_output,
    biases,
    mom_input,
    mom_hidden,
    out_first,
    out_second,
    bias_first,
    bias_second,
    res_input,
    res_hidden,
    res_output,
):
    ncol = lax.axis_size("col")
    nblk = lax.axis_size("blk")
    col_index = lax.axis_index("col")
    blk_index = lax.axis_index("blk")
    hcol = w_input.shape[1]
    scol = w_output.shape[1]
    micro = frames.shape[0]
    slot_count = frames.shape[1] * micro * nblk * ncol
    bias_row = biases[0]
    b_one = bias_row[:hcol]
    b_two = bias_row[hcol : 2 * hcol]
    b_out = bias_row[2 * hcol :]
    low_input = w_input.astype(jnp.bfloat16)
    own_tags = jnp.where(mask > 0, labels, -1).reshape(-1)
    own_inputs = frames.reshape(-1, frames.shape[2])
    inputs = lax.all_gather(own_inputs, "col", axis=0, tiled=True)
    tags_group = lax.all_gather(own_tags, "col", axis=0, tiled=True)
    low_hidden = collect_rows(w_hidden.astype(jnp.bfloat16))
    low_output = collect_rows(w_output.astype(jnp.bfloat16))
    sig_one = jax.nn.sigmoid(matmul(inputs, low_input) + b_one)
    h_one = spread_cols(sig_one.astype(jnp.bfloat16))
    sig_two = jax.nn.sigmoid(matmul(h_one, low_hidden) + b_two)
    h_two = spread_cols(sig_two.astype(jnp.bfloat16))
    logits = matmul(h_two, low_output) + b_out
    row_top = lax.pmax(jnp.max(logits, axis=1), "col")
    exponent = jnp.exp(logits - row_top[:, None])
    target_hit = jnp.arange(scol)[None, :] == (tags_group - col_index * scol)[:, None]
    row_total, picked = lax.psum(
        (jnp.sum(exponent, axis=1), jnp.sum(jnp.where(target_hit, logits, 0.0), axis=1)), "col"
    )
    live_rows = tags_group >= 0
    loss_local = jnp.sum(jnp.where(live_rows, row_top + jnp.log(row_total) - picked, 0.0))
    probs = exponent / row_total[:, None]
    d_logits = (
        jnp.where(live_rows[:, None], probs - target_hit.astype(jnp.float32), 0.0) / slot_count
    ).astype(jnp.bfloat16)
    d_h_two = reduce_cols(outer_cols(d_logits, low_output))
    d_z_two = (d_h_two * sig_two * (1.0 - sig_two)).astype(jnp.bfloat16)
    d_h_one = reduce_cols(outer_cols(d_z_two, low_hidden))
    d_z_one = (d_h_one * sig_one * (1.0 - sig_one)).astype(jnp.bfloat16)
    grad_bias = jnp.concatenate(
        [
            jnp.sum(d_z_one.astype(jnp.float32), axis=0),
            jnp.sum(d_z_two.astype(jnp.float32), axis=0),
            jnp.sum(d_logits.astype(jnp.float32), axis=0),
        ]
    )
    deep = w_input.shape[0]
    padded = 512
    rows_out = OUT_GROUPS * OUT_ROWS
    vec = jnp.concatenate([grad_bias, loss_local[None]])
    vec = jnp.pad(vec, (0, 4096 - vec.shape[0])).reshape(32, 128)
    next_out, next_hid, next_in, red_out, red_hid, red_in, vec_sum, stats = reduce_grads(
        jnp.pad(d_logits, ((0, 0), (0, rows_out - scol))).T,
        h_two,
        jnp.pad(res_output[0], ((0, 0), (0, rows_out - scol))).T,
        d_z_two.T,
        h_one,
        res_hidden[0].T,
        d_z_one.T,
        jnp.pad(inputs, ((0, 0), (0, padded - deep))),
        jnp.pad(res_input[0], ((0, padded - deep), (0, 0))).T,
        vec,
        scol,
        deep,
    )
    next_res_output = next_out.transpose(1, 2, 0)
    next_res_hidden = next_hid.T
    next_res_input = next_in[:, :deep].T
    red_output = red_out[:scol].T
    vec_sum = vec_sum.reshape(-1)
    red_bias = vec_sum[: bias_row.shape[0]]
    loss_sum = vec_sum[bias_row.shape[0]]
    stats = stats.at[1, 0].set(jnp.sum(red_bias * red_bias) / nblk)
    done_hidden, done_input, mom_hid_next, mom_in_next, norms = muon(
        stats,
        red_hid,
        mom_hidden.T,
        red_in.T,
        jnp.pad(mom_input, ((0, padded - deep), (0, 0))),
        hcol * ncol,
    )
    clip_norm = norms[0, 0]
    factor = norms[4, 0]
    next_mom_hidden = mom_hid_next.T
    next_mom_input = mom_in_next[:deep]
    done_hidden = done_hidden.reshape(hcol, w_hidden.shape[0]).T
    muon_scale = LR_MUON * 0.2 * math.sqrt(hcol * ncol)
    new_input = w_input * (1.0 - LR_MUON * WD_MUON) - muon_scale * done_input[:deep]
    new_hidden = w_hidden * (1.0 - LR_MUON * WD_MUON) - muon_scale * done_hidden
    new_output, next_out_first, next_out_second = adam_step(
        w_output, factor * red_output, out_first, out_second
    )
    new_biases, next_bias_first, next_bias_second = adam_step(
        biases, factor * red_bias[None, :], bias_first, bias_second
    )
    return (
        loss_sum,
        clip_norm,
        new_input,
        new_hidden,
        new_output,
        new_biases,
        next_mom_input,
        next_mom_hidden,
        next_out_first,
        next_out_second,
        next_bias_first,
        next_bias_second,
        next_res_input[None],
        next_res_hidden[None],
        next_res_output,
    )


def solution(mesh):
    in_specs = (
        P(None, ("blk", "col"), None),
        P(None, ("blk", "col")),
        P(None, ("blk", "col")),
        P(None, "col"),
        P("blk", "col"),
        P("blk", "col"),
        P("col", None),
        P(None, "col"),
        P("blk", "col"),
        P("blk", "col"),
        P("blk", "col"),
        P("col", None),
        P("col", None),
        P("blk", None, "col"),
        P("blk", None, "col"),
        P("blk", None, "col"),
    )
    out_specs = (
        P(),
        P(),
        P(None, "col"),
        P("blk", "col"),
        P("blk", "col"),
        P("col", None),
        P(None, "col"),
        P("blk", "col"),
        P("blk", "col"),
        P("blk", "col"),
        P("col", None),
        P("col", None),
        P("blk", None, "col"),
        P("blk", None, "col"),
        P("blk", None, "col"),
    )
    cubes = mesh.shape["blk"] == 8 and mesh.shape["col"] == 4
    body = fast_body if cubes else plain_body
    return jax.shard_map(body, mesh=mesh, in_specs=in_specs, out_specs=out_specs, check_vma=False)
```

```python
import functools
import math

import jax
import jax.numpy as jnp
from jax import lax
from jax.experimental import pallas as pl
from jax.experimental.pallas import tpu as pltpu
from jax.sharding import PartitionSpec as P

NS = 5
STEP = 5


NS_A = 3.4445
NS_B = -4.775
NS_C = 2.0315
CLIP = 0.002
LR_MUON = 0.1
WD_MUON = 0.01
LR_ADAM = 0.03
WD_ADAM = 0.1

MESH = pl.DeviceIdType.MESH
F32 = jnp.float32
BF16 = jnp.bfloat16
I16 = jnp.int16
LN2 = math.log(2.0)
TOP_CODE = 32700.0
LEVELS = 64.0


def matmul(left_side, right_side):
    return jnp.dot(left_side, right_side, preferred_element_type=jnp.float32)


def inner_rows(left_side, right_side):
    return lax.dot_general(
        left_side, right_side, (((0,), (0,)), ((), ())), preferred_element_type=jnp.float32
    )


def outer_cols(left_side, right_side):
    return lax.dot_general(
        left_side, right_side, (((1,), (1,)), ((), ())), preferred_element_type=jnp.float32
    )


def precise(left_side, right_side):
    return jnp.dot(
        left_side, right_side, precision=lax.Precision.HIGHEST, preferred_element_type=jnp.float32
    )


def spread_cols(values):
    return lax.all_gather(values, "col", axis=1, tiled=True)


def reduce_cols(values):
    return lax.psum_scatter(values, "col", scatter_dimension=1, tiled=True)


def collect_rows(values):
    return lax.all_gather(values, "blk", axis=0, tiled=True)


def squash(gradient, resid):
    value = gradient + resid.astype(jnp.float32)
    scale = jnp.mean(jnp.abs(value), axis=0, keepdims=True) + 1e-12
    signed = scale * jnp.tanh(2.0 * value / scale)
    return (signed, value - signed)


def adam_step(weight, gradient, first, second):
    first = 0.5 * first + 0.5 * gradient
    second = 0.95 * second + 0.05 * gradient * gradient
    update = first / (1.0 - 0.5**STEP) / (jnp.sqrt(second / (1.0 - 0.95**STEP)) + 1e-08)
    return (weight - LR_ADAM * (update + WD_ADAM * weight), first, second)


def halves(values):
    top = values.astype(BF16)
    return top, (values - top.astype(F32)).astype(BF16)


def dot_nn(left_side, right_side):
    return lax.dot_general(
        left_side, right_side, (((1,), (0,)), ((), ())), preferred_element_type=F32
    )


def dot_nt(left_side, right_side):
    return lax.dot_general(
        left_side, right_side, (((1,), (1,)), ((), ())), preferred_element_type=F32
    )


RING = 8
STEPS = RING - 1
OUT_ROWS = 592
OUT_GROUPS = 4
BLOCKS = (304, 288)
HID_ROWS = 512
SCALE_ROWS = 16


def ring_place(blk):
    odd = blk % 2
    return (blk // 2) * (1 - odd) + (7 - blk // 2) * odd


def ring_blk(place):
    back = place // 4
    return 2 * place * (1 - back) + (15 - 2 * place) * back


def scale_code(size):
    return jnp.ceil(jnp.log(jnp.maximum(size, 1e-30)) * (LEVELS / LN2))


def code_scale(code):
    return jnp.exp(code * (LN2 / LEVELS))


def to_codes(values):
    return jnp.round(values).astype(jnp.int32).astype(I16)


def from_codes(codes):
    return codes.astype(jnp.int32).astype(F32)


def reduce_kernel(
    deep,
    dl_ref,
    h_two_ref,
    res_out_ref,
    dz_two_ref,
    h_one_ref,
    res_hid_ref,
    dz_one_ref,
    x_ref,
    res_in_ref,
    vec_ref,
    next_out_ref,
    next_hid_ref,
    next_in_ref,
    red_out_ref,
    red_hid_ref,
    red_in_ref,
    vec_sum_ref,
    stats_ref,
    grad,
    stage,
    res_buf,
    marks,
    own_out,
    got_out,
    size_out,
    own_hid,
    got_hid,
    size_hid,
    own_in,
    got_in,
    size_in,
    share_in,
    vecs,
    res_sems,
    stage_sems,
    out_send,
    out_recv,
    hid_send,
    hid_recv,
    in_send,
    in_recv,
    share_send,
    share_recv,
    vec_send,
    vec_recv,
):
    blk = lax.axis_index("blk")
    here = ring_place(blk)
    total_rows = next_out_ref.shape[0]
    barrier = pltpu.get_barrier_semaphore()
    for away in range(1, RING):
        pl.semaphore_signal(
            barrier, inc=1, device_id={"blk": (blk + away) % RING}, device_id_type=MESH
        )

    starts = [sum(BLOCKS[:part]) for part in range(len(BLOCKS))]

    def res_copy(group, part):
        rows = BLOCKS[part]
        return pltpu.make_async_copy(
            res_out_ref.at[pl.ds(group * OUT_ROWS + starts[part], rows), :],
            res_buf.at[part, pl.ds(0, rows), :],
            res_sems.at[part],
        )

    def stage_copy(group, part, rows):
        return pltpu.make_async_copy(
            stage.at[pl.ds(0, rows)],
            next_out_ref.at[pl.ds(group * OUT_ROWS + starts[part], rows)],
            stage_sems.at[0],
        )

    last_rows = total_rows - (OUT_GROUPS - 1) * OUT_ROWS - starts[-1]

    def stage_start(group, part):
        if part < len(BLOCKS) - 1:
            stage_copy(group, part, BLOCKS[part]).start()
        else:

            @pl.when(group < OUT_GROUPS - 1)
            def _():
                stage_copy(group, part, BLOCKS[part]).start()

            @pl.when(group == OUT_GROUPS - 1)
            def _():
                stage_copy(group, part, last_rows).start()

    res_copy(0, 0).start()
    res_copy(0, 1).start()
    marks[...] = jnp.zeros_like(marks)
    stats_ref[...] = jnp.zeros_like(stats_ref)
    pl.semaphore_wait(barrier, RING - 1)

    vec_copies = []
    for away in range(1, RING):
        copy = pltpu.make_async_remote_copy(
            src_ref=vec_ref,
            dst_ref=vecs.at[blk],
            send_sem=vec_send.at[away - 1],
            recv_sem=vec_recv.at[away - 1],
            device_id={"blk": (blk + away) % RING},
            device_id_type=MESH,
        )
        copy.start()
        vec_copies.append(copy)

    def row_scale(value, count):
        size = jnp.sum(jnp.abs(value), axis=1, keepdims=True) * (1.0 / count) + 1e-12
        code = scale_code(size)
        return size, code, size * (TOP_CODE / code_scale(code))

    def lane_codes(first):
        return jnp.transpose(marks[first : first + 128, :])[0:1, :]

    def set_sizes(rows, own, sizes):
        parts = [lane_codes(first) for first in range(0, rows, 128)]
        parts.append(jnp.zeros((SCALE_ROWS - len(parts), 128), F32))
        codes = jnp.concatenate(parts, axis=0)
        sizes[...] = code_scale(codes[0:8, :])
        for number in range(2 * RING):
            own[number, rows : rows + SCALE_ROWS, :] = codes.astype(jnp.int32).astype(I16)

    def squash_rows(first, count, own, first_own, read_res, write_next):
        def some(number, carry):
            row = pl.multiple_of(number * 16, 16)
            value = grad[pl.ds(row, 16), :] + read_res(row)
            size, code, factor = row_scale(value, value.shape[1])
            grad[pl.ds(row, 16), :] = value
            marks[pl.ds(first_own + row, 16), :] = jnp.broadcast_to(code, (16, 128))
            steep = 2.0 / size
            for lane in range(0, value.shape[1], 128):
                piece = grad[pl.ds(row, 16), lane : lane + 128]
                curve = jnp.tanh(piece * steep)
                number_of = lane // 256
                chunk = number_of // 2 if number_of % 2 == 0 else 7 - number_of // 2
                own[2 * chunk + lane // 128 % 2, pl.ds(first_own + row, 16), :] = to_codes(
                    curve * factor
                )
                write_next(row, lane, piece - size * curve)
            return carry

        lax.fori_loop(0, count // 16, some, 0)

    def out_group(group):
        for part, rows in enumerate(BLOCKS):
            base = pl.multiple_of(group * OUT_ROWS + starts[part], 16)
            for lane in range(0, grad.shape[1], 512):
                grad[0:rows, lane : lane + 512] = dot_nn(
                    dl_ref[pl.ds(base, rows), :], h_two_ref[:, lane : lane + 512]
                )
            res_copy(group, part).wait()
            if part == 0:

                @pl.when(group > 0)
                def _():
                    stage_copy(group - 1, len(BLOCKS) - 1, BLOCKS[-1]).wait()

            else:
                stage_copy(group, part - 1, BLOCKS[part - 1]).wait()

            def write_next(row, lane, values):
                stage[pl.ds(row, 16), 0, lane : lane + 128] = values

            squash_rows(
                0,
                rows,
                own_out.at[group],
                starts[part],
                lambda row, part=part: res_buf[part, pl.ds(row, 16), :].astype(F32),
                write_next,
            )
            stage_start(group, part)

            @pl.when(group < OUT_GROUPS - 1)
            def _(part=part):
                res_copy(group + 1, part).start()

        set_sizes(OUT_ROWS, own_out.at[group], size_out.at[group])

    def hid_group():
        for first in range(0, HID_ROWS, 256):
            for lane in range(0, grad.shape[1], 512):
                grad[0:256, lane : lane + 512] = dot_nn(
                    dz_two_ref[first : first + 256, :], h_one_ref[:, lane : lane + 512]
                )

            def write_next(row, lane, values, first=first):
                next_hid_ref[pl.ds(first + row, 16), lane : lane + 128] = values

            squash_rows(
                0,
                256,
                own_hid,
                first,
                lambda row, first=first: res_hid_ref[pl.ds(first + row, 16), :].astype(F32),
                write_next,
            )
        set_sizes(HID_ROWS, own_hid, size_hid)

    def in_group():
        wide = x_ref.shape[1]
        for first in range(0, HID_ROWS, 256):
            grad[0:256, 0:wide] = dot_nn(dz_one_ref[first : first + 256, :], x_ref[...])

            def some(number, carry, first=first):
                row = pl.multiple_of(number * 16, 16)
                place = pl.multiple_of(first + row, 16)
                value = grad[pl.ds(row, 16), 0:wide] + res_in_ref[pl.ds(place, 16), :].astype(F32)
                size, code, factor = row_scale(value, deep)
                curve = jnp.tanh(value * (2.0 / size))
                next_in_ref[pl.ds(place, 16), :] = value - size * curve
                marks[pl.ds(place, 16), :] = jnp.broadcast_to(code, (16, 128))
                chunk = first // 64 + number // 4
                inside = pl.multiple_of(number % 4 * 16, 16)
                codes = to_codes(curve * factor)
                for way in range(2):
                    own_in[2 * chunk + way, pl.ds(inside, 16), :] = codes[
                        :, way * 256 : (way + 1) * 256
                    ]
                return carry

            lax.fori_loop(0, 16, some, 0)
        for chunk in range(RING):
            codes = jnp.concatenate(
                [lane_codes(64 * chunk), jnp.zeros((SCALE_ROWS - 1, 128), F32)], axis=0
            )
            size_in[chunk] = code_scale(codes[0:8, :])
            for way in range(2):
                own_in[2 * chunk + way, 64 : 64 + SCALE_ROWS, 0:128] = codes.astype(
                    jnp.int32
                ).astype(I16)
                own_in[2 * chunk + way, 64 : 64 + SCALE_ROWS, 128:256] = jnp.zeros(
                    (SCALE_ROWS, 128), I16
                )

    def towards(way):
        return {"blk": ring_blk((here + 1 - 2 * way + RING) % RING)}

    def move(src, got, step, way, send_sem, recv_sem):
        return pltpu.make_async_remote_copy(
            src_ref=src,
            dst_ref=got.at[way, step],
            send_sem=send_sem.at[way, step],
            recv_sem=recv_sem.at[way, step],
            device_id=towards(way),
            device_id_type=MESH,
        )

    def first_moves(own, got, send_sem, recv_sem):
        for way in range(2):
            chunk = (here - 1 + 2 * way + RING) % RING
            move(own.at[2 * chunk + way], got, 0, way, send_sem, recv_sem).start()

    def hop(rows, own, got, own_sizes, step, way, send_sem, recv_sem, keep):
        message = got.at[way, step]
        move(message, got, step, way, send_sem, recv_sem).wait_recv()
        ahead = here - 2 - step + way * (4 + 2 * step) + 2 * RING
        chunk = ahead % RING
        mine = own.at[2 * chunk + way]
        size = own_sizes(chunk)
        came = code_scale(from_codes(message[rows : rows + SCALE_ROWS, 0:128])[0:8, :])
        code = scale_code(came + size)
        whole = code_scale(code)
        blank = jnp.zeros((112, 128), F32)
        wide = message.shape[1]

        @pl.when(step < STEPS - 1)
        def _():
            shares = jnp.transpose(jnp.concatenate([came / whole, size / whole, blank], axis=0))
            for number, first in enumerate(range(0, rows, 128)):
                count = min(128, rows - first)
                there = slice(first, first + count)
                message[there, :] = to_codes(
                    from_codes(message[there, :]) * shares[0:count, number : number + 1]
                    + from_codes(mine[there, :]) * shares[0:count, 8 + number : 9 + number]
                )
            codes = jnp.concatenate([code, jnp.zeros((SCALE_ROWS - 8, 128), F32)], axis=0)
            message[rows : rows + SCALE_ROWS, 0:128] = codes.astype(jnp.int32).astype(I16)
            move(message, got, step + 1, way, send_sem, recv_sem).start()

        @pl.when(step == STEPS - 1)
        def _():
            shares = jnp.transpose(
                jnp.concatenate([came * (1.0 / TOP_CODE), size * (1.0 / TOP_CODE), blank], axis=0)
            )
            square = jnp.zeros((1, wide), F32)
            for number, first in enumerate(range(0, rows, 128)):
                count = min(128, rows - first)
                there = slice(first, first + count)
                value = (
                    from_codes(message[there, :]) * shares[0:count, number : number + 1]
                    + from_codes(mine[there, :]) * shares[0:count, 8 + number : 9 + number]
                )
                keep(first, count, value)
                square = square + jnp.sum(value * value, axis=0, keepdims=True)
            for lane in range(0, wide, 128):
                stats_ref[0:1, :] += square[:, lane : lane + 128]

    def out_hop(group, step, way):
        def keep(first, count, value):
            row = pl.multiple_of(group * OUT_ROWS + first, 16)

            @pl.when(way == 0)
            def _():
                red_out_ref[pl.ds(row, count), 0:128] = value

            @pl.when(way == 1)
            def _():
                red_out_ref[pl.ds(row, count), 128:256] = value

        hop(
            OUT_ROWS,
            own_out.at[group],
            got_out.at[group],
            lambda chunk: size_out[group],
            step,
            way,
            out_send.at[group],
            out_recv.at[group],
            keep,
        )

    def hid_hop(step, way):
        def keep(first, count, value):
            @pl.when(way == 0)
            def _():
                red_hid_ref[first : first + count, 0:128] = value

            @pl.when(way == 1)
            def _():
                red_hid_ref[first : first + count, 128:256] = value

        hop(
            HID_ROWS, own_hid, got_hid, lambda chunk: size_hid[...], step, way, hid_send, hid_recv, keep
        )

    def share_move(step, way):
        place = (here - step + 2 * step * way + 2 * RING) % RING
        return pltpu.make_async_remote_copy(
            src_ref=share_in.at[way, place],
            dst_ref=share_in.at[way, place],
            send_sem=share_send.at[way, step],
            recv_sem=share_recv.at[way, step],
            device_id=towards(way),
            device_id_type=MESH,
        )

    def in_hop(step, way):
        def keep(first, count, value):
            share_in[way, here] = value

        hop(64, own_in, got_in, lambda chunk: size_in[chunk], step, way, in_send, in_recv, keep)

        @pl.when(step == STEPS - 1)
        def _():
            share_move(0, way).start()

    def share_hop(step, way):
        share_move(step, way).wait_recv()

        @pl.when(step < STEPS - 1)
        def _():
            share_move(step + 1, way).start()

    def wave(number, carry):
        @pl.when(number == 0)
        def _():
            in_group()
            first_moves(own_in, got_in, in_send, in_recv)
            hid_group()
            first_moves(own_hid, got_hid, hid_send, hid_recv)

        @pl.when(number < OUT_GROUPS)
        def _():
            out_group(number)
            first_moves(own_out.at[number], got_out.at[number], out_send.at[number], out_recv.at[number])

        def both(way, carry):
            @pl.when((number >= 1) & (number <= STEPS))
            def _():
                in_hop(number - 1, way)
                hid_hop(number - 1, way)

            @pl.when(number > STEPS)
            def _():
                share_hop(2 * (number - STEPS - 1), way)

                @pl.when(number < STEPS + 4)
                def _():
                    share_hop(2 * (number - STEPS - 1) + 1, way)

            def outs(group, carry):
                step = number - 1 - group

                @pl.when((step >= 0) & (step < STEPS))
                def _():
                    out_hop(group, step, way)

                return carry

            lax.fori_loop(0, OUT_GROUPS, outs, 0)
            return carry

        lax.fori_loop(0, 2, both, 0)
        return carry

    lax.fori_loop(0, STEPS + OUT_GROUPS + 1, wave, 0)

    for place in range(RING):
        for way in range(2):
            red_in_ref[place * 64 : (place + 1) * 64, way * 256 : (way + 1) * 256] = share_in[
                way, place
            ]
    for copy in vec_copies:
        copy.wait_recv()
    vecs[blk] = vec_ref[...]
    total = vecs[0]
    for number in range(1, RING):
        total = total + vecs[number]
    vec_sum_ref[...] = total
    for copy in vec_copies:
        copy.wait_send()
    stage_copy(OUT_GROUPS - 1, len(BLOCKS) - 1, last_rows).wait()
    for way in range(2):
        for step in range(STEPS):
            for group in range(OUT_GROUPS):
                move(
                    got_out.at[group, way, step],
                    got_out.at[group],
                    step,
                    way,
                    out_send.at[group],
                    out_recv.at[group],
                ).wait_send()
            move(got_hid.at[way, step], got_hid, step, way, hid_send, hid_recv).wait_send()
            move(got_in.at[way, step], got_in, step, way, in_send, in_recv).wait_send()
            share_move(step, way).wait_send()


def reduce_grads(dl, h_two, res_out, dz_two, h_one, res_hid, dz_one, x, res_in, vec, senones, deep):
    wide = h_two.shape[1]
    in_wide = x.shape[1]
    vmem = pl.BlockSpec(memory_space=pltpu.VMEM)
    hbm = pl.BlockSpec(memory_space=pl.ANY)
    message = OUT_ROWS + SCALE_ROWS
    hid_message = HID_ROWS + SCALE_ROWS
    in_message = 64 + SCALE_ROWS
    sem = pltpu.SemaphoreType.DMA
    return pl.pallas_call(
        functools.partial(reduce_kernel, deep),
        out_shape=(
            jax.ShapeDtypeStruct((senones, 1, wide), F32),
            jax.ShapeDtypeStruct((HID_ROWS, wide), F32),
            jax.ShapeDtypeStruct((HID_ROWS, in_wide), F32),
            jax.ShapeDtypeStruct((OUT_GROUPS * OUT_ROWS, 256), F32),
            jax.ShapeDtypeStruct((HID_ROWS, 256), F32),
            jax.ShapeDtypeStruct((HID_ROWS, in_wide), F32),
            jax.ShapeDtypeStruct(vec.shape, F32),
            jax.ShapeDtypeStruct((8, 128), F32),
        ),
        in_specs=[vmem, vmem, hbm] + [vmem] * 7,
        out_specs=(hbm,) + (vmem,) * 7,
        scratch_shapes=[
            pltpu.VMEM((BLOCKS[0], wide), F32),
            pltpu.VMEM((BLOCKS[0], 1, wide), F32),
            pltpu.VMEM((2, BLOCKS[0], wide), BF16),
            pltpu.VMEM((640, 128), F32),
            pltpu.VMEM((OUT_GROUPS, 2 * RING, message, 128), I16),
            pltpu.VMEM((OUT_GROUPS, 2, STEPS, message, 128), I16),
            pltpu.VMEM((OUT_GROUPS, 8, 128), F32),
            pltpu.VMEM((2 * RING, hid_message, 128), I16),
            pltpu.VMEM((2, STEPS, hid_message, 128), I16),
            pltpu.VMEM((8, 128), F32),
            pltpu.VMEM((2 * RING, in_message, 256), I16),
            pltpu.VMEM((2, STEPS, in_message, 256), I16),
            pltpu.VMEM((RING, 8, 128), F32),
            pltpu.VMEM((2, RING, 64, 256), F32),
            pltpu.VMEM((RING,) + vec.shape, F32),
            sem((2,)),
            sem((1,)),
            sem((OUT_GROUPS, 2, STEPS)),
            sem((OUT_GROUPS, 2, STEPS)),
            sem((2, STEPS)),
            sem((2, STEPS)),
            sem((2, STEPS)),
            sem((2, STEPS)),
            sem((2, STEPS)),
            sem((2, STEPS)),
            sem((STEPS,)),
            sem((STEPS,)),
        ],
        compiler_params=pltpu.CompilerParams(
            collective_id=1, has_side_effects=True, vmem_limit_bytes=62 * 1024 * 1024
        ),
    )(dl, h_two, res_out, dz_two, h_one, res_hid, dz_one, x, res_in, vec)


RING_STARTS = (0, 2, 5, 7, 9)
LAYER_TWO_WAVE = 7
LOGIT_WAVES = (11, 12, 14, 16)


def forward_kernel(
    slot_count,
    x_ref,
    tags_ref,
    w_in_ref,
    w_hid_ref,
    w_out_ref,
    bias_ref,
    bias_out_ref,
    x_out,
    h_one_out,
    h_two_out,
    slope_one_out,
    slope_two_out,
    w_hid_out,
    w_out_out,
    dl_ref,
    bias_sum_ref,
    loss_ref,
    x_all,
    h_one,
    h_two,
    slope_one,
    slope_two,
    w_in,
    w_hid,
    w_out,
    curve,
    bias_col,
    tags,
    sums,
    ring_send,
    ring_recv,
    x_send,
    x_recv,
    h_send,
    h_recv,
    tag_send,
    tag_recv,
    sum_send,
    sum_recv,
    out_sems,
):
    blk = lax.axis_index("blk")
    col = lax.axis_index("col")
    here = ring_place(blk)
    senones, depth = w_out_ref.shape
    own_rows, deep = x_ref.shape
    units = w_hid_ref.shape[1]
    frames = x_all.shape[0]
    cores = {"col": col + 1 - 2 * (col % 2)}
    across = {"col": (col + 2) % 4}
    corner = {"col": (col + 2) % 4 + 1 - 2 * (col % 2)}
    others = (cores, across, corner)

    barrier = pltpu.get_barrier_semaphore()
    for target in others + tuple({"blk": ring_blk((here + way) % RING)} for way in (1, 7)):
        pl.semaphore_signal(barrier, inc=1, device_id=target, device_id_type=MESH)

    w_hid[pl.ds(pl.multiple_of(blk * depth, depth), depth), :] = w_hid_ref[...].astype(BF16)
    own_lanes = pl.ds(pl.multiple_of(blk * depth, depth), depth)
    w_out[senones // 16 * 16 :, own_lanes] = jnp.zeros(
        (w_out.shape[0] - senones // 16 * 16, depth), BF16
    )
    w_out[0:senones, own_lanes] = w_out_ref[...].astype(BF16)
    own_frames = pl.ds(pl.multiple_of(col * own_rows, own_rows), own_rows)
    x_all[own_frames, :] = jnp.zeros((own_rows, x_all.shape[1]), BF16)
    x_all[own_frames, 0:deep] = x_ref[...]
    tags[col] = tags_ref[...]
    sums[...] = jnp.zeros_like(sums)
    pl.semaphore_wait(barrier, 5)

    def ring_part(group, origin, way):
        start = pl.multiple_of(origin * depth + way * 128, 128)
        if group == 0:
            return w_hid.at[pl.ds(start, 128), :]
        return w_out.at[pl.ds((group - 1) * OUT_ROWS, OUT_ROWS), pl.ds(start, 128)]

    def ring_move(group, step, way):
        origin = ring_blk((here - step + 2 * step * way + RING) % RING)
        part = ring_part(group, origin, way)
        return pltpu.make_async_remote_copy(
            src_ref=part,
            dst_ref=part,
            send_sem=ring_send.at[group, way, step],
            recv_sem=ring_recv.at[group, way, step],
            device_id={"blk": ring_blk((here + 1 - 2 * way + RING) % RING)},
            device_id_type=MESH,
        )

    def ring_wave(wave):
        for group, start in enumerate(RING_STARTS):
            step = wave - 1 - start
            for way in range(2):
                if step == -1:
                    ring_move(group, 0, way).start()
                if 0 <= step < STEPS:
                    ring_move(group, step, way).wait_recv()
                    if step < STEPS - 1:
                        ring_move(group, step + 1, way).start()

    def copy_to(target, src, send_sem, recv_sem):
        return pltpu.make_async_remote_copy(
            src_ref=src,
            dst_ref=src,
            send_sem=send_sem,
            recv_sem=recv_sem,
            device_id=target,
            device_id_type=MESH,
        )

    def rows_of(owner):
        return pl.ds(pl.multiple_of(owner * own_rows, own_rows), own_rows)

    def lanes_of(owner):
        return pl.ds(pl.multiple_of(owner * units, units), units)

    def x_move(number):
        owner = across["col"] if number == 2 else col
        target = across if number == 1 else cores
        return copy_to(target, x_all.at[rows_of(owner), :], x_send.at[number], x_recv.at[number])

    def h_move(layer, number, block):
        owner = across["col"] if number == 2 else col
        target = across if number == 1 else cores
        whole = (h_one, h_two)[layer]
        part = whole.at[pl.ds(block * own_rows, own_rows), lanes_of(owner)]
        return copy_to(
            target, part, h_send.at[layer, number, block], h_recv.at[layer, number, block]
        )

    def h_start(layer, block):
        h_move(layer, 0, block).start()
        h_move(layer, 1, block).start()

    def h_forward(layer, block):
        h_move(layer, 1, block).wait_recv()
        h_move(layer, 2, block).start()

    def h_ready(layer, block):
        h_move(layer, 0, block).wait_recv()
        h_move(layer, 2, block).wait_recv()

    ring_wave(0)
    x_move(0).start()
    x_move(1).start()
    tag_copies = [
        copy_to(target, tags.at[col], tag_send.at[number], tag_recv.at[number])
        for number, target in enumerate(others)
    ]
    for copy in tag_copies:
        copy.start()
    w_in[...] = jnp.zeros_like(w_in)
    w_in[0:deep, :] = w_in_ref[...].astype(BF16)
    for number in range(bias_out_ref.shape[0]):
        line = jnp.broadcast_to(bias_out_ref[number : number + 1, :], (128, 128))
        bias_col[number * 128 : (number + 1) * 128, :] = jnp.transpose(line)
    ring_wave(1)
    x_move(1).wait_recv()
    x_move(2).start()
    x_move(0).wait_recv()
    x_move(2).wait_recv()

    def layer(number, block, inputs, weights, whole, slopes):
        there = slice(block * own_rows, (block + 1) * own_rows)
        value = jax.nn.sigmoid(
            dot_nn(inputs[there, :], weights[...]) + bias_ref[number : number + 1, :]
        )
        slopes[there, :] = value * (1.0 - value)
        whole[there, lanes_of(col)] = value.astype(BF16)
        h_start(number, block)

    outs = []

    def put(src, dst):
        copy = pltpu.make_async_copy(src, dst, out_sems.at[len(outs)])
        copy.start()
        outs.append(copy)

    for block in range(4):
        layer(0, block, x_all, w_in, h_one, slope_one)
    put(x_all, x_out)
    put(slope_one, slope_one_out)

    def all_tags():
        return jnp.concatenate([tags[owner, 0:1, :] for owner in range(4)], axis=1)

    def own_row(line):
        line = line - col * senones
        return jnp.where(line < senones, line, -1)

    def logits(group):
        first = group * OUT_ROWS
        half = frames // 2
        for part in range(2):
            curve[first : first + OUT_ROWS, part * half : (part + 1) * half] = dot_nt(
                w_out[first : first + OUT_ROWS, :], h_two[part * half : (part + 1) * half, :]
            )
        base = lax.broadcasted_iota(jnp.int32, (16, frames), 0)

        def largest(number, top):
            row = pl.multiple_of(first + number * 16, 16)
            value = curve[pl.ds(row, 16), :] + bias_col[pl.ds(row, 16), 0:1]
            if group == OUT_GROUPS - 1:
                value = jnp.where(base + row < senones, value, -1e30)
            curve[pl.ds(row, 16), :] = value
            return jnp.maximum(top, value)

        top = lax.fori_loop(0, OUT_ROWS // 16, largest, jnp.full((16, frames), -1e30, F32))
        top = jnp.max(top, axis=0, keepdims=True)
        line = jnp.broadcast_to(own_row(all_tags()), (16, frames))

        def exponents(number, carry):
            total, picked = carry
            row = pl.multiple_of(first + number * 16, 16)
            value = curve[pl.ds(row, 16), :]
            power = jnp.exp(value - top)
            curve[pl.ds(row, 16), :] = power
            return total + power, picked + jnp.where(base + row == line, value, 0.0)

        blank = jnp.zeros((16, frames), F32)
        total, picked = lax.fori_loop(0, OUT_ROWS // 16, exponents, (blank, blank))
        sums[col, group : group + 1, :] = top
        sums[col, 4 + group : 5 + group, :] = jnp.sum(total, axis=0, keepdims=True)
        sums[col, 8 + group : 9 + group, :] = jnp.sum(picked, axis=0, keepdims=True)

    last_wave = RING_STARTS[-1] + STEPS
    for wave in range(2, last_wave + 1):
        ring_wave(wave)
        if 2 <= wave < 6:
            h_forward(0, wave - 2)
        if wave == LAYER_TWO_WAVE:
            for block in range(4):
                h_ready(0, block)
                layer(1, block, h_one, w_hid, h_two, slope_two)
            put(h_one, h_one_out)
            put(slope_two, slope_two_out)
            put(w_hid, w_hid_out)
        if LAYER_TWO_WAVE < wave <= LAYER_TWO_WAVE + 4:
            h_forward(1, wave - LAYER_TWO_WAVE - 1)
        for group, when in enumerate(LOGIT_WAVES):
            if wave == when:
                if group == 0:
                    for block in range(4):
                        h_ready(1, block)
                    put(h_two, h_two_out)
                    for copy in tag_copies:
                        copy.wait_recv()
                rows = pl.ds(group * OUT_ROWS, OUT_ROWS)
                put(w_out.at[rows, :], w_out_out.at[rows, :])
                logits(group)

    sum_copies = [
        copy_to(target, sums.at[col], sum_send.at[number], sum_recv.at[number])
        for number, target in enumerate(others)
    ]
    for copy in sum_copies:
        copy.start()
    for copy in sum_copies:
        copy.wait_recv()

    def lines(first):
        return [sums[owner, first + group : first + group + 1, :] for owner in range(4) for group in range(4)]

    tops = lines(0)
    top = functools.reduce(jnp.maximum, tops)
    total = functools.reduce(
        jnp.add, [size * jnp.exp(own - top) for own, size in zip(tops, lines(4), strict=True)]
    )
    picked = functools.reduce(jnp.add, lines(8))
    line = all_tags()
    live = line >= 0
    loss = jnp.where(live, top + jnp.log(total) - picked, 0.0)
    loss_ref[...] = jnp.zeros_like(loss_ref)
    loss_ref[0:1, :] = functools.reduce(
        jnp.add, [loss[:, lane : lane + 128] for lane in range(0, frames, 128)]
    )
    weight = jnp.where(live, 1.0 / slot_count, 0.0)
    line = jnp.broadcast_to(own_row(line), (16, frames))
    hit_weight = jnp.broadcast_to(weight, (16, frames))
    base = lax.broadcasted_iota(jnp.int32, (16, frames), 0)
    bias_col[...] = jnp.zeros_like(bias_col)
    for group in range(OUT_GROUPS):
        share = jnp.exp(sums[col, group : group + 1, :] - top) / total * weight

        def gradient(number, carry, first=group * OUT_ROWS, share=share):
            row = pl.multiple_of(first + number * 16, 16)
            value = curve[pl.ds(row, 16), :] * share - jnp.where(base + row == line, hit_weight, 0.0)
            value = value.astype(BF16)
            dl_ref[pl.ds(row, 16), :] = value
            bias_col[pl.ds(row, 16), :] = jnp.broadcast_to(
                jnp.sum(value.astype(F32), axis=1, keepdims=True), (16, 128)
            )
            return carry

        lax.fori_loop(0, OUT_ROWS // 16, gradient, 0)
    bias_sum_ref[...] = jnp.zeros_like(bias_sum_ref)
    for number in range(bias_out_ref.shape[0]):
        block = jnp.transpose(bias_col[number * 128 : (number + 1) * 128, :])
        bias_sum_ref[number : number + 1, :] = block[0:1, :]

    for group in range(len(RING_STARTS)):
        for way in range(2):
            for step in range(STEPS):
                ring_move(group, step, way).wait_send()
    for number in range(3):
        x_move(number).wait_send()
        for block in range(4):
            h_move(0, number, block).wait_send()
            h_move(1, number, block).wait_send()
    for copy in tag_copies + sum_copies:
        copy.wait_send()
    for copy in outs:
        copy.wait()


def forward_pass(x, tags, w_in, w_hid, w_out, bias, bias_out, slot_count):
    own_rows = x.shape[0]
    units = w_hid.shape[1]
    frames = 4 * own_rows
    wide = 4 * units
    rows = OUT_GROUPS * OUT_ROWS
    blocks = bias_out.shape[0]
    vmem = pl.BlockSpec(memory_space=pltpu.VMEM)
    hbm = pl.BlockSpec(memory_space=pl.ANY)
    sem = pltpu.SemaphoreType.DMA
    kept = (
        ((frames, 512), BF16),
        ((frames, wide), BF16),
        ((frames, wide), BF16),
        ((frames, units), F32),
        ((frames, units), F32),
        ((wide, units), BF16),
        ((rows, wide), BF16),
    )
    return pl.pallas_call(
        functools.partial(forward_kernel, slot_count),
        out_shape=tuple(jax.ShapeDtypeStruct(shape, kind) for shape, kind in kept)
        + (
            jax.ShapeDtypeStruct((rows, frames), BF16),
            jax.ShapeDtypeStruct((24, 128), F32),
            jax.ShapeDtypeStruct((8, 128), F32),
        ),
        in_specs=[vmem] * 7,
        out_specs=(hbm,) * 7 + (vmem,) * 3,
        scratch_shapes=[pltpu.VMEM(shape, kind) for shape, kind in kept[:5]]
        + [
            pltpu.VMEM((512, units), BF16),
            pltpu.VMEM((wide, units), BF16),
            pltpu.VMEM((rows, wide), BF16),
            pltpu.VMEM((rows, frames), F32),
            pltpu.VMEM((blocks * 128, 128), F32),
            pltpu.VMEM((4,) + tags.shape, jnp.int32),
            pltpu.VMEM((4, 16, frames), F32),
            sem((5, 2, STEPS)),
            sem((5, 2, STEPS)),
            sem((3,)),
            sem((3,)),
            sem((2, 3, 4)),
            sem((2, 3, 4)),
            sem((3,)),
            sem((3,)),
            sem((3,)),
            sem((3,)),
            sem((16,)),
        ],
        compiler_params=pltpu.CompilerParams(
            collective_id=2, has_side_effects=True, vmem_limit_bytes=60 * 1024 * 1024
        ),
    )(x, tags, w_in, w_hid, w_out, bias, bias_out)


DIM_BITS = (2, 4, 8)
ORDERS = ((0, 1, 2), (1, 2, 0), (2, 0, 1))
PIECE = 48
LIGHT_HID = 3
LIGHT_IN = 2


def stage_sends(stage, sources):
    moves = []
    for piece, order in enumerate(ORDERS):
        slot = sum(DIM_BITS[order[index]] for index in sources)
        moves.append((piece, slot, order[stage]))
    return moves


def landed(moves):
    return [(slot | DIM_BITS[dim], piece) for piece, slot, dim in moves]


FIRST = stage_sends(0, ())
SECOND = stage_sends(1, ())
SECOND_ON = stage_sends(1, (0,))
THIRD = stage_sends(2, ())
THIRD_A = stage_sends(2, (0,))
THIRD_B = stage_sends(2, (1,))
THIRD_C = stage_sends(2, (0, 1))
MOVES = FIRST + SECOND + SECOND_ON + THIRD + THIRD_A + THIRD_B + THIRD_C


def muon_kernel(
    stats_ref,
    red_hid_ref,
    mom_hid_ref,
    red_in_ref,
    mom_in_ref,
    hid_ref,
    inp_ref,
    next_hid_ref,
    next_in_ref,
    norm_ref,
    codes,
    tops,
    lows,
    scales,
    xs,
    us,
    vs,
    lhs,
    xin,
    xin_top,
    xin_low,
    gram,
    gram_got,
    back,
    sums,
    sums_got,
    send_sems,
    core_sems,
    recv_sems,
    back_send,
    back_recv,
    sums_send,
    sums_recv,
    spread_send,
    spread_recv,
    pair_send,
    pair_recv,
):
    blk = lax.axis_index("blk")
    col = lax.axis_index("col")
    rows, wide = xs.shape
    height = back.shape[2]
    part_wide = inp_ref.shape[1]
    other_core = {"col": col + 1 - 2 * (col % 2)}
    dims = (
        {"blk": blk + 1 - 2 * (blk % 2)},
        {"col": (col + 2) % 4},
        {"blk": blk + 2 - 4 * ((blk // 2) % 2)},
    )
    far = {"blk": (blk + 4) % 8}
    diagonal = {"blk": 4 * (blk // 4) + 3 - blk % 4}
    barrier = pltpu.get_barrier_semaphore()
    for target in (other_core, dims[1], *({"blk": (blk + away) % 8} for away in range(1, 8))):
        pl.semaphore_signal(barrier, inc=1, device_id=target, device_id_type=MESH)

    def fold(values):
        line = jnp.sum(values, axis=0, keepdims=True)
        return sum(line[:, lane : lane + 128] for lane in range(0, line.shape[1], 128))

    share = 0.125
    sums[0, 0:1, :] = fold(stats_ref[...])
    sums[0, 1:2, :] = fold(mom_hid_ref[...] * mom_hid_ref[...])
    sums[0, 2:3, :] = fold(mom_hid_ref[...] * red_hid_ref[...])
    sums[0, 3:4, :] = fold(red_hid_ref[...] * red_hid_ref[...])
    sums[0, 4:5, :] = fold(mom_in_ref[...] * mom_in_ref[...]) * share
    sums[0, 5:6, :] = fold(mom_in_ref[...] * red_in_ref[...]) * share
    sums[0, 6:7, :] = fold(red_in_ref[...] * red_in_ref[...]) * share
    sums[0, 7:8, :] = jnp.zeros((1, 128), F32)
    for turn in range(2):
        codes[turn, 0, rows:, :] = jnp.zeros((codes.shape[2] - rows, wide), I16)
    eye = lax.broadcasted_iota(jnp.int32, (rows, rows), 0) == lax.broadcasted_iota(
        jnp.int32, (rows, rows), 1
    )
    pl.semaphore_wait(barrier, 9)

    for number, target in enumerate((other_core, *dims, far)):
        copy = pltpu.make_async_remote_copy(
            src_ref=sums.at[number],
            dst_ref=sums_got.at[number],
            send_sem=sums_send.at[number],
            recv_sem=sums_recv.at[number],
            device_id=target,
            device_id_type=MESH,
        )
        copy.start()
        copy.wait()
        sums[number + 1] = sums[number] + sums_got[number]
    whole = jnp.sum(sums[5], axis=1, keepdims=True)
    clip = jnp.sqrt(whole[0:1])
    factor = jnp.minimum(1.0, CLIP / clip)

    def norm_of(first):
        square = (
            0.25 * whole[first : first + 1]
            + factor * whole[first + 1 : first + 2]
            + factor * factor * whole[first + 2 : first + 3]
        )
        return 1.0 / (jnp.sqrt(jnp.maximum(square, 0.0)) + 1e-07)

    norm_ref[0:4, :] = jnp.broadcast_to(clip, (4, 128))
    norm_ref[4:8, :] = jnp.broadcast_to(factor, (4, 128))
    next_hid_ref[...] = 0.5 * mom_hid_ref[...] + factor * red_hid_ref[...]
    next_in_ref[...] = 0.5 * mom_in_ref[...] + factor * red_in_ref[...]

    my_lanes = pl.ds(pl.multiple_of(blk * height, height), height)
    spread = []
    for away in range(1, 8):
        target = (blk + away) % 8
        spread.append(
            pltpu.make_async_remote_copy(
                src_ref=next_hid_ref.at[
                    pl.ds(pl.multiple_of(target % 4 * rows, rows), rows), :
                ],
                dst_ref=xs.at[:, my_lanes],
                send_sem=spread_send.at[away - 1],
                recv_sem=spread_recv.at[away - 1],
                device_id={"blk": target},
                device_id_type=MESH,
            )
        )
        spread[-1].start()
    high = col // 2
    my_half = pl.ds(pl.multiple_of(high * part_wide, part_wide), part_wide)
    half_copy = pltpu.make_async_remote_copy(
        src_ref=next_in_ref,
        dst_ref=xin.at[:, my_half],
        send_sem=pair_send.at[0],
        recv_sem=pair_recv.at[0],
        device_id=dims[1],
        device_id_type=MESH,
    )
    half_copy.start()
    xs[:, my_lanes] = next_hid_ref[pl.ds(pl.multiple_of(blk % 4 * rows, rows), rows), :]
    xin[:, my_half] = next_in_ref[...]
    for copy in spread:
        copy.wait_recv()
    xs[...] = xs[...] * norm_of(1)
    in_scale = norm_of(4)

    numbers = {move: number for number, move in enumerate(MOVES)}

    def part(turn, slot, piece):
        return codes.at[turn, slot, pl.ds(piece * PIECE, PIECE), :]

    def send(turn, move):
        piece, slot, dim = move
        return pltpu.make_async_remote_copy(
            src_ref=part(turn, slot, piece),
            dst_ref=part(turn, slot | DIM_BITS[dim], piece),
            send_sem=send_sems.at[numbers[move]],
            recv_sem=recv_sems.at[turn, slot | DIM_BITS[dim], piece],
            device_id=dims[dim],
            device_id_type=MESH,
        )

    def send_all(turn, moves):
        for move in moves:
            send(turn, move).start()

    def to_core(turn, slot, piece):
        return pltpu.make_async_remote_copy(
            src_ref=part(turn, slot, piece),
            dst_ref=part(turn, slot + 1, piece),
            send_sem=core_sems.at[slot // 2, piece],
            recv_sem=recv_sems.at[turn, slot + 1, piece],
            device_id=other_core,
            device_id_type=MESH,
        )

    def arrived(turn, slot, piece):
        pltpu.make_async_remote_copy(
            src_ref=part(turn, slot, piece),
            dst_ref=part(turn, slot, piece),
            send_sem=core_sems.at[0, 0],
            recv_sem=recv_sems.at[turn, slot, piece],
            device_id=other_core,
            device_id_type=MESH,
        ).wait_recv()

    def forward(turn, moves, on=()):
        for number, (slot, piece) in enumerate(landed(moves)):
            arrived(turn, slot, piece)
            to_core(turn, slot, piece).start()
            if on:
                send(turn, on[number]).start()

    def gram_copy():
        return pltpu.make_async_remote_copy(
            src_ref=gram,
            dst_ref=gram_got,
            send_sem=pair_send.at[1],
            recv_sem=pair_recv.at[1],
            device_id=other_core,
            device_id_type=MESH,
        )

    def unpack(turn, pair, light):
        for core in range(2):
            here = slice(core * rows, (core + 1) * rows)
            whole = from_codes(codes[turn, 2 * pair + core, 0:rows, :])
            if light:
                tops[pair, here, :] = whole.astype(BF16)
            else:
                top, low = halves(whole)
                tops[pair, here, :] = top
                lows[pair, here, :] = low
            step = from_codes(codes[turn, 2 * pair + core, rows : rows + 16, 0:rows])
            size = code_scale(step[0:8, :]) * (1.0 / TOP_CODE)
            scales[pair, :, here] = size * size

    def apply_pair(pair, out, light):
        cut = 512
        if light:
            inner = (dot_nt(lhs[0:rows, :], tops[pair]) * scales[pair, 0:1, :]).astype(BF16)
            for start in range(0, wide, cut):
                lanes = slice(start, start + cut)
                out[:, lanes] += dot_nn(inner, tops[pair, :, lanes])
            return
        both = dot_nt(lhs[...], tops[pair])
        inner = both[:rows] + both[rows:] + dot_nt(lhs[0:rows, :], lows[pair])
        inner = inner * scales[pair, 0:1, :]
        top, low = halves(inner)
        stack = jnp.concatenate([top, low], axis=0)
        for start in range(0, wide, cut):
            lanes = slice(start, start + cut)
            both = dot_nn(stack, tops[pair, :, lanes])
            out[:, lanes] += both[:rows] + both[rows:] + dot_nn(top, lows[pair, :, lanes])

    def set_lhs(values):
        top, low = halves(values)
        lhs[0:rows, :] = top
        lhs[rows:, :] = low

    def input_gram(light):
        top, low = halves(xin[...])
        xin_top[...] = top
        if light:
            gram[...] = dot_nt(xin_top[...], xin_top[...])
        else:
            xin_low[...] = low
            cross = dot_nt(xin_top[...], xin_low[...])
            gram[...] = dot_nt(xin_top[...], xin_top[...]) + (cross + jnp.transpose(cross))
        gram_copy().start()

    def input_step(light):
        gram_copy().wait()
        square_of = gram[...] + gram_got[...]
        top, low = halves(square_of)
        if light:
            poly = NS_B * square_of + NS_C * dot_nn(top, top)
        else:
            cross = dot_nn(top, low)
            poly = NS_B * square_of + NS_C * (dot_nn(top, top) + (cross + jnp.transpose(cross)))
        top, low = halves(poly)
        cut = 512
        for start in range(0, xin.shape[1], cut):
            lanes = slice(start, start + cut)
            change = dot_nn(top, xin_top[:, lanes])
            if not light:
                change = change + dot_nn(low, xin_top[:, lanes]) + dot_nn(top, xin_low[:, lanes])
            xin[:, lanes] = NS_A * xin[:, lanes] + change

    def by_weight(number, limit, work):
        @pl.when(number < limit)
        def _():
            work(True)

        @pl.when(number >= limit)
        def _():
            work(False)

    def iteration(number, carry):
        turn = number % 2
        values = xs[...]
        largest = jnp.max(jnp.abs(values), axis=1, keepdims=True)
        step = scale_code(largest)
        codes[turn, 0, 0:rows, :] = to_codes(values * (TOP_CODE / code_scale(step)))
        lane_step = jnp.sum(jnp.where(eye, step, 0.0), axis=0, keepdims=True)
        codes[turn, 0, rows : rows + 16, 0:rows] = jnp.broadcast_to(
            lane_step.astype(jnp.int32), (16, rows)
        ).astype(I16)
        send_all(turn, FIRST)
        for piece in range(3):
            to_core(turn, 0, piece).start()
        send_all(turn, SECOND)
        set_lhs(values)
        us[...] = jnp.zeros_like(us)
        vs[...] = jnp.zeros_like(vs)

        def first_pass(index, carry):
            pair = index + (index // 3) * (1 - index // 4) - (index // 4) * (1 - index // 5)

            @pl.when(index == 1)
            def _():
                forward(turn, FIRST, SECOND_ON)
                send_all(turn, THIRD)
                send_all(turn, THIRD_A)

                @pl.when(number > 0)
                def _():
                    by_weight(number, LIGHT_IN, input_gram)

                forward(turn, SECOND, THIRD_B)
                forward(turn, SECOND_ON, THIRD_C)

                @pl.when(number > 0)
                def _():
                    by_weight(number, LIGHT_IN, input_step)

                forward(turn, THIRD)

            @pl.when(index == 4)
            def _():
                forward(turn, THIRD_A)
                forward(turn, THIRD_B)

            @pl.when((index == 6) & (number == 0))
            def _():
                half_copy.wait()
                xin[...] = xin[...] * in_scale
                input_gram(True)
                input_step(True)

            @pl.when(index == 7)
            def _():
                forward(turn, THIRD_C)

            for piece in range(3):
                arrived(turn, 2 * pair + 1, piece)

            def work(light):
                unpack(turn, pair, light)
                apply_pair(pair, us, light)

            by_weight(number, LIGHT_HID, work)
            return carry

        lax.fori_loop(0, 8, first_pass, 0)
        set_lhs(us[...])

        def second_pass(pair, carry):
            by_weight(number, LIGHT_HID, lambda light: apply_pair(pair, vs, light))
            return carry

        lax.fori_loop(0, 8, second_pass, 0)
        xs[...] = NS_A * xs[...] + NS_B * us[...] + NS_C * vs[...]
        for move in MOVES:
            send(turn, move).wait_send()
        for pair in range(8):
            for piece in range(3):
                to_core(turn, 2 * pair, piece).wait_send()
        return carry

    lax.fori_loop(0, NS, iteration, 0)

    place = blk % 4
    copies = []
    for rel, target in ((1, dims[0]), (2, dims[2]), (3, diagonal)):
        copies.append(
            pltpu.make_async_remote_copy(
                src_ref=xs.at[:, pl.ds(pl.multiple_of(target["blk"] * height, height), height)],
                dst_ref=back.at[place],
                send_sem=back_send.at[rel - 1],
                recv_sem=back_recv.at[rel - 1],
                device_id=target,
                device_id_type=MESH,
            )
        )
        copies[-1].start()
    hid_ref[place] = xs[:, my_lanes]
    inp_ref[...] = xin[:, my_half]
    for copy in copies:
        copy.wait_recv()
    for target in (dims[0], dims[2], diagonal):
        other = target["blk"] % 4
        hid_ref[other] = back[other]
    for copy in copies + spread:
        copy.wait_send()


def muon(stats, red_hid, mom_hid, red_in, mom_in, wide):
    rows = red_hid.shape[0] // 4
    height = red_hid.shape[1]
    deep, part_wide = red_in.shape
    vmem = pl.BlockSpec(memory_space=pltpu.VMEM)
    sem = pltpu.SemaphoreType.DMA
    return pl.pallas_call(
        muon_kernel,
        out_shape=(
            jax.ShapeDtypeStruct((4, rows, height), F32),
            jax.ShapeDtypeStruct((deep, part_wide), F32),
            jax.ShapeDtypeStruct(red_hid.shape, F32),
            jax.ShapeDtypeStruct(red_in.shape, F32),
            jax.ShapeDtypeStruct((8, 128), F32),
        ),
        in_specs=[vmem] * 5,
        out_specs=(vmem,) * 5,
        scratch_shapes=[
            pltpu.VMEM((2, 16, 3 * PIECE, wide), I16),
            pltpu.VMEM((8, 2 * rows, wide), BF16),
            pltpu.VMEM((8, 2 * rows, wide), BF16),
            pltpu.VMEM((8, 8, 2 * rows), F32),
            pltpu.VMEM((rows, wide), F32),
            pltpu.VMEM((rows, wide), F32),
            pltpu.VMEM((rows, wide), F32),
            pltpu.VMEM((2 * rows, wide), BF16),
            pltpu.VMEM((deep, 2 * part_wide), F32),
            pltpu.VMEM((deep, 2 * part_wide), BF16),
            pltpu.VMEM((deep, 2 * part_wide), BF16),
            pltpu.VMEM((deep, deep), F32),
            pltpu.VMEM((deep, deep), F32),
            pltpu.VMEM((4, rows, height), F32),
            pltpu.VMEM((6, 8, 128), F32),
            pltpu.VMEM((5, 8, 128), F32),
            sem((len(MOVES),)),
            sem((8, 3)),
            sem((2, 16, 3)),
            sem((3,)),
            sem((3,)),
            sem((5,)),
            sem((5,)),
            sem((7,)),
            sem((7,)),
            sem((2,)),
            sem((2,)),
        ],
        compiler_params=pltpu.CompilerParams(
            collective_id=0, has_side_effects=True, vmem_limit_bytes=60 * 1024 * 1024
        ),
    )(stats, red_hid, mom_hid, red_in, mom_in)


def plain_body(
    frames,
    labels,
    mask,
    w_input,
    w_hidden,
    w_output,
    biases,
    mom_input,
    mom_hidden,
    out_first,
    out_second,
    bias_first,
    bias_second,
    res_input,
    res_hidden,
    res_output,
):
    ncol = lax.axis_size("col")
    nblk = lax.axis_size("blk")
    col_index = lax.axis_index("col")
    hcol = w_input.shape[1]
    scol = w_output.shape[1]
    micro = frames.shape[0]
    slot_count = frames.shape[1] * micro * nblk * ncol
    bias_row = biases[0]
    b_one = bias_row[:hcol]
    b_two = bias_row[hcol : 2 * hcol]
    b_out = bias_row[2 * hcol :]
    low_input = w_input.astype(jnp.bfloat16)
    row_tags = jnp.where(mask > 0, labels, -1)
    grad_input = jnp.zeros(w_input.shape, jnp.float32)
    grad_hidden = jnp.zeros((w_hidden.shape[0] * nblk, hcol), jnp.float32)
    grad_output = jnp.zeros((w_output.shape[0] * nblk, scol), jnp.float32)
    grad_bias = jnp.zeros(bias_row.shape, jnp.float32)
    loss_local = jnp.zeros((), jnp.float32)
    for micro_step in range(micro):
        low_hidden, low_output = (
            lax.all_gather(w_hidden.astype(jnp.bfloat16), "blk", axis=0, tiled=True),
            lax.all_gather(w_output.astype(jnp.bfloat16), "blk", axis=0, tiled=True),
        )
        inputs = lax.all_gather(frames[micro_step], "col", axis=0, tiled=True)
        tags_group = lax.all_gather(row_tags[micro_step], "col", axis=0, tiled=True)
        sig_one = jax.nn.sigmoid(matmul(inputs, low_input) + b_one)
        h_one = spread_cols(sig_one.astype(jnp.bfloat16))
        sig_two = jax.nn.sigmoid(matmul(h_one, low_hidden) + b_two)
        h_two = spread_cols(sig_two.astype(jnp.bfloat16))
        logits = matmul(h_two, low_output) + b_out
        row_top = lax.pmax(jnp.max(logits, axis=1), "col")
        exponent = jnp.exp(logits - row_top[:, None])
        target_hit = jnp.arange(scol)[None, :] == (tags_group - col_index * scol)[:, None]
        row_total, picked = lax.psum(
            (jnp.sum(exponent, axis=1), jnp.sum(jnp.where(target_hit, logits, 0.0), axis=1)), "col"
        )
        live_rows = tags_group >= 0
        loss_local = loss_local + jnp.sum(
            jnp.where(live_rows, row_top + jnp.log(row_total) - picked, 0.0)
        )
        probs = exponent / row_total[:, None]
        d_logits = (
            jnp.where(live_rows[:, None], probs - target_hit.astype(jnp.float32), 0.0) / slot_count
        ).astype(jnp.bfloat16)
        grad_output = grad_output + inner_rows(h_two, d_logits)
        d_h_two = reduce_cols(outer_cols(d_logits, low_output))
        d_z_two = (d_h_two * sig_two * (1.0 - sig_two)).astype(jnp.bfloat16)
        grad_hidden = grad_hidden + inner_rows(h_one, d_z_two)
        d_h_one = reduce_cols(outer_cols(d_z_two, low_hidden))
        d_z_one = (d_h_one * sig_one * (1.0 - sig_one)).astype(jnp.bfloat16)
        grad_input = grad_input + inner_rows(inputs, d_z_one)
        grad_bias = grad_bias + jnp.concatenate(
            [
                jnp.sum(d_z_one.astype(jnp.float32), axis=0),
                jnp.sum(d_z_two.astype(jnp.float32), axis=0),
                jnp.sum(d_logits.astype(jnp.float32), axis=0),
            ]
        )
    q_input, next_res_input = squash(grad_input, res_input[0])
    q_hidden, next_res_hidden = squash(grad_hidden, res_hidden[0])
    q_output, next_res_output = squash(grad_output, res_output[0])
    red_hidden, red_output = (
        lax.psum_scatter(q_hidden, "blk", scatter_dimension=0, tiled=True),
        lax.psum_scatter(q_output, "blk", scatter_dimension=0, tiled=True),
    )
    red_input, red_bias, loss_sum = lax.psum((q_input, grad_bias, loss_local), "blk")
    share_blk = 1.0 / nblk
    grad_square = (
        share_blk * (jnp.sum(red_input * red_input) + jnp.sum(red_bias * red_bias))
        + jnp.sum(red_hidden * red_hidden)
        + jnp.sum(red_output * red_output)
    )
    clip_norm = jnp.sqrt(lax.psum(grad_square, ("blk", "col")))
    factor = jnp.minimum(1.0, CLIP / clip_norm)
    next_mom_input = 0.5 * mom_input + factor * red_input
    next_mom_hidden = 0.5 * mom_hidden + factor * red_hidden
    square_input, square_hidden = lax.psum(
        (
            share_blk * jnp.sum(next_mom_input * next_mom_input),
            jnp.sum(next_mom_hidden * next_mom_hidden),
        ),
        ("blk", "col"),
    )
    iter_input = next_mom_input / (jnp.sqrt(square_input) + 1e-07)
    iter_hidden = next_mom_hidden / (jnp.sqrt(square_hidden) + 1e-07)
    for turn_index in range(NS):
        rows_hidden = collect_rows(iter_hidden)
        gram_input, gram_hidden = lax.psum(
            (precise(iter_input, iter_input.T), precise(iter_hidden, rows_hidden.T)), "col"
        )
        image_input = precise(gram_input, iter_input)
        image_hidden = precise(gram_hidden, rows_hidden)
        iter_input = (
            NS_A * iter_input + NS_B * image_input + NS_C * precise(gram_input, image_input)
        )
        iter_hidden = (
            NS_A * iter_hidden
            + NS_B * image_hidden
            + NS_C * precise(gram_hidden, collect_rows(image_hidden))
        )
    muon_scale = LR_MUON * 0.2 * math.sqrt(hcol * ncol)
    new_input = w_input * (1.0 - LR_MUON * WD_MUON) - muon_scale * iter_input
    new_hidden = w_hidden * (1.0 - LR_MUON * WD_MUON) - muon_scale * iter_hidden
    new_output, next_out_first, next_out_second = adam_step(
        w_output, factor * red_output, out_first, out_second
    )
    new_biases, next_bias_first, next_bias_second = adam_step(
        biases, factor * red_bias[None, :], bias_first, bias_second
    )
    return (
        loss_sum,
        clip_norm,
        new_input,
        new_hidden,
        new_output,
        new_biases,
        next_mom_input,
        next_mom_hidden,
        next_out_first,
        next_out_second,
        next_bias_first,
        next_bias_second,
        next_res_input[None],
        next_res_hidden[None],
        next_res_output[None],
    )


def fast_body(
    frames,
    labels,
    mask,
    w_input,
    w_hidden,
    w_output,
    biases,
    mom_input,
    mom_hidden,
    out_first,
    out_second,
    bias_first,
    bias_second,
    res_input,
    res_hidden,
    res_output,
):
    ncol = lax.axis_size("col")
    nblk = lax.axis_size("blk")
    col_index = lax.axis_index("col")
    blk_index = lax.axis_index("blk")
    hcol = w_input.shape[1]
    scol = w_output.shape[1]
    micro = frames.shape[0]
    slot_count = frames.shape[1] * micro * nblk * ncol
    bias_row = biases[0]
    deep = w_input.shape[0]
    padded = 512
    rows_out = OUT_GROUPS * OUT_ROWS
    own_tags = jnp.where(mask > 0, labels, -1).reshape(1, -1)
    layer_biases = jnp.pad(bias_row[: 2 * hcol].reshape(2, hcol), ((0, 6), (0, 0)))
    blocks = -(-rows_out // 128)
    out_biases = jnp.pad(bias_row[2 * hcol :], (0, blocks * 128 - scol)).reshape(blocks, 128)
    inputs, h_one, h_two, slope_one, slope_two, low_hidden, low_output, d_logits, bias_sums, losses = (
        forward_pass(
            frames.reshape(-1, deep),
            jnp.broadcast_to(own_tags, (8, own_tags.shape[1])),
            w_input,
            w_hidden,
            w_output.T,
            layer_biases,
            out_biases,
            slot_count,
        )
    )
    loss_local = jnp.sum(losses)
    d_h_two = reduce_cols(inner_rows(d_logits, low_output))
    d_z_two = (d_h_two * slope_two).astype(jnp.bfloat16)
    d_h_one = reduce_cols(outer_cols(d_z_two, low_hidden))
    d_z_one = (d_h_one * slope_one).astype(jnp.bfloat16)
    grad_bias = jnp.concatenate(
        [
            jnp.sum(d_z_one.astype(jnp.float32), axis=0),
            jnp.sum(d_z_two.astype(jnp.float32), axis=0),
            bias_sums.reshape(-1)[:scol],
        ]
    )
    vec = jnp.concatenate([grad_bias, loss_local[None]])
    vec = jnp.pad(vec, (0, 4096 - vec.shape[0])).reshape(32, 128)
    next_out, next_hid, next_in, red_out, red_hid, red_in, vec_sum, stats = reduce_grads(
        d_logits,
        h_two,
        jnp.pad(res_output[0], ((0, 0), (0, rows_out - scol))).T,
        d_z_two.T,
        h_one,
        res_hidden[0].T,
        d_z_one.T,
        inputs,
        jnp.pad(res_input[0], ((0, padded - deep), (0, 0))).T,
        vec,
        scol,
        deep,
    )
    next_res_output = next_out.transpose(1, 2, 0)
    next_res_hidden = next_hid.T
    next_res_input = next_in[:, :deep].T
    red_output = red_out[:scol].T
    vec_sum = vec_sum.reshape(-1)
    red_bias = vec_sum[: bias_row.shape[0]]
    loss_sum = vec_sum[bias_row.shape[0]]
    stats = stats.at[1, 0].set(jnp.sum(red_bias * red_bias) / nblk)
    done_hidden, done_input, mom_hid_next, mom_in_next, norms = muon(
        stats,
        red_hid,
        mom_hidden.T,
        red_in.T,
        jnp.pad(mom_input, ((0, padded - deep), (0, 0))),
        hcol * ncol,
    )
    clip_norm = norms[0, 0]
    factor = norms[4, 0]
    next_mom_hidden = mom_hid_next.T
    next_mom_input = mom_in_next[:deep]
    done_hidden = done_hidden.reshape(hcol, w_hidden.shape[0]).T
    muon_scale = LR_MUON * 0.2 * math.sqrt(hcol * ncol)
    new_input = w_input * (1.0 - LR_MUON * WD_MUON) - muon_scale * done_input[:deep]
    new_hidden = w_hidden * (1.0 - LR_MUON * WD_MUON) - muon_scale * done_hidden
    new_output, next_out_first, next_out_second = adam_step(
        w_output, factor * red_output, out_first, out_second
    )
    new_biases, next_bias_first, next_bias_second = adam_step(
        biases, factor * red_bias[None, :], bias_first, bias_second
    )
    return (
        loss_sum,
        clip_norm,
        new_input,
        new_hidden,
        new_output,
        new_biases,
        next_mom_input,
        next_mom_hidden,
        next_out_first,
        next_out_second,
        next_bias_first,
        next_bias_second,
        next_res_input[None],
        next_res_hidden[None],
        next_res_output,
    )


def solution(mesh):
    in_specs = (
        P(None, ("blk", "col"), None),
        P(None, ("blk", "col")),
        P(None, ("blk", "col")),
        P(None, "col"),
        P("blk", "col"),
        P("blk", "col"),
        P("col", None),
        P(None, "col"),
        P("blk", "col"),
        P("blk", "col"),
        P("blk", "col"),
        P("col", None),
        P("col", None),
        P("blk", None, "col"),
        P("blk", None, "col"),
        P("blk", None, "col"),
    )
    out_specs = (
        P(),
        P(),
        P(None, "col"),
        P("blk", "col"),
        P("blk", "col"),
        P("col", None),
        P(None, "col"),
        P("blk", "col"),
        P("blk", "col"),
        P("blk", "col"),
        P("col", None),
        P("col", None),
        P("blk", None, "col"),
        P("blk", None, "col"),
        P("blk", None, "col"),
    )
    cubes = mesh.shape["blk"] == 8 and mesh.shape["col"] == 4
    body = fast_body if cubes else plain_body
    return jax.shard_map(body, mesh=mesh, in_specs=in_specs, out_specs=out_specs, check_vma=False)
```

```python
import functools
import math

import jax
import jax.numpy as jnp
from jax import lax
from jax.experimental import pallas as pl
from jax.experimental.pallas import tpu as pltpu
from jax.sharding import PartitionSpec as P

NS = 5
STEP = 5


NS_A = 3.4445
NS_B = -4.775
NS_C = 2.0315
CLIP = 0.002
LR_MUON = 0.1
WD_MUON = 0.01
LR_ADAM = 0.03
WD_ADAM = 0.1

MESH = pl.DeviceIdType.MESH
F32 = jnp.float32
BF16 = jnp.bfloat16
I16 = jnp.int16
LN2 = math.log(2.0)
TOP_CODE = 32700.0
LEVELS = 64.0


def matmul(left_side, right_side):
    return jnp.dot(left_side, right_side, preferred_element_type=jnp.float32)


def inner_rows(left_side, right_side):
    return lax.dot_general(
        left_side, right_side, (((0,), (0,)), ((), ())), preferred_element_type=jnp.float32
    )


def outer_cols(left_side, right_side):
    return lax.dot_general(
        left_side, right_side, (((1,), (1,)), ((), ())), preferred_element_type=jnp.float32
    )


def precise(left_side, right_side):
    return jnp.dot(
        left_side, right_side, precision=lax.Precision.HIGHEST, preferred_element_type=jnp.float32
    )


def spread_cols(values):
    return lax.all_gather(values, "col", axis=1, tiled=True)


def reduce_cols(values):
    return lax.psum_scatter(values, "col", scatter_dimension=1, tiled=True)


def collect_rows(values):
    return lax.all_gather(values, "blk", axis=0, tiled=True)


def squash(gradient, resid):
    value = gradient + resid.astype(jnp.float32)
    scale = jnp.mean(jnp.abs(value), axis=0, keepdims=True) + 1e-12
    signed = scale * jnp.tanh(2.0 * value / scale)
    return (signed, value - signed)


def adam_step(weight, gradient, first, second):
    first = 0.5 * first + 0.5 * gradient
    second = 0.95 * second + 0.05 * gradient * gradient
    update = first / (1.0 - 0.5**STEP) / (jnp.sqrt(second / (1.0 - 0.95**STEP)) + 1e-08)
    return (weight - LR_ADAM * (update + WD_ADAM * weight), first, second)


def halves(values):
    top = values.astype(BF16)
    return top, (values - top.astype(F32)).astype(BF16)


def dot_nn(left_side, right_side):
    return lax.dot_general(
        left_side, right_side, (((1,), (0,)), ((), ())), preferred_element_type=F32
    )


def dot_nt(left_side, right_side):
    return lax.dot_general(
        left_side, right_side, (((1,), (1,)), ((), ())), preferred_element_type=F32
    )


RING = 8
STEPS = RING - 1
OUT_ROWS = 592
OUT_GROUPS = 4
BLOCKS = (304, 288)
HID_ROWS = 512
SCALE_ROWS = 16
HID_WAVE = 4
IN_WAVE = 6


def ring_place(blk):
    odd = blk % 2
    return (blk // 2) * (1 - odd) + (7 - blk // 2) * odd


def ring_blk(place):
    back = place // 4
    return 2 * place * (1 - back) + (15 - 2 * place) * back


def scale_code(size):
    return jnp.ceil(jnp.log(jnp.maximum(size, 1e-30)) * (LEVELS / LN2))


def code_scale(code):
    return jnp.exp(code * (LN2 / LEVELS))


def to_codes(values):
    return jnp.round(values).astype(jnp.int32).astype(I16)


def from_codes(codes):
    return codes.astype(jnp.int32).astype(F32)


def reduce_kernel(
    deep,
    dl_ref,
    h_two_ref,
    h_one_ref,
    x_ref,
    part_ref,
    slope_two_ref,
    slope_one_ref,
    w_hid_ref,
    res_out_ref,
    res_hid_ref,
    res_in_ref,
    vec_ref,
    next_out_ref,
    next_hid_ref,
    next_in_ref,
    red_out_ref,
    red_hid_ref,
    red_in_ref,
    vec_sum_ref,
    stats_ref,
    grad,
    stage,
    res_buf,
    dl_buf,
    h_buf,
    slope_buf,
    marks,
    keep_sums,
    dz,
    dz_two,
    dz_one,
    core_out,
    core_got,
    far_out,
    far_got,
    own_out,
    got_out,
    size_out,
    own_hid,
    got_hid,
    size_hid,
    own_in,
    got_in,
    size_in,
    share_in,
    vec,
    vecs,
    res_sems,
    dl_sems,
    load_sems,
    stage_sems,
    slope_sems,
    core_send,
    core_recv,
    far_send,
    far_recv,
    out_send,
    out_recv,
    hid_send,
    hid_recv,
    in_send,
    in_recv,
    share_send,
    share_recv,
    vec_send,
    vec_recv,
):
    blk = lax.axis_index("blk")
    col = lax.axis_index("col")
    here = ring_place(blk)
    total_rows = next_out_ref.shape[0]
    core, high = col % 2, col // 2
    cores = {"col": col + 1 - 2 * core}
    across = {"col": (col + 2) % 4}
    barrier = pltpu.get_barrier_semaphore()
    for target in (cores, across, *({"blk": (blk + away) % RING} for away in range(1, RING))):
        pl.semaphore_signal(barrier, inc=1, device_id=target, device_id_type=MESH)

    starts = [sum(BLOCKS[:part]) for part in range(len(BLOCKS))]

    def res_copy(group, part):
        rows = BLOCKS[part]
        return pltpu.make_async_copy(
            res_out_ref.at[pl.ds(group * OUT_ROWS + starts[part], rows), :],
            res_buf.at[part, pl.ds(0, rows), :],
            res_sems.at[part],
        )

    def dl_copy(group, part):
        rows = BLOCKS[part]
        return pltpu.make_async_copy(
            dl_ref.at[pl.ds(group * OUT_ROWS + starts[part], rows), :],
            dl_buf.at[part, pl.ds(0, rows), :],
            dl_sems.at[part],
        )

    def hid_res_copy(part):
        return pltpu.make_async_copy(
            res_hid_ref.at[pl.ds(part * 256, 256), :],
            res_buf.at[part, pl.ds(0, 256), :],
            res_sems.at[part],
        )

    def hid_next_copy(part):
        return pltpu.make_async_copy(
            grad.at[pl.ds(0, 256), :], next_hid_ref.at[pl.ds(part * 256, 256), :], load_sems.at[1]
        )

    def load(src, dst):
        return pltpu.make_async_copy(src, dst, load_sems.at[0])

    def stage_copy(group, part, rows):
        return pltpu.make_async_copy(
            stage.at[pl.ds(0, rows)],
            next_out_ref.at[pl.ds(group * OUT_ROWS + starts[part], rows)],
            stage_sems.at[0],
        )

    last_rows = total_rows - (OUT_GROUPS - 1) * OUT_ROWS - starts[-1]

    def stage_start(group, part):
        if part < len(BLOCKS) - 1:
            stage_copy(group, part, BLOCKS[part]).start()
        else:

            @pl.when(group < OUT_GROUPS - 1)
            def _():
                stage_copy(group, part, BLOCKS[part]).start()

            @pl.when(group == OUT_GROUPS - 1)
            def _():
                stage_copy(group, part, last_rows).start()

    for part in range(2):
        res_copy(0, part).start()
        dl_copy(0, part).start()
    load(h_two_ref, h_buf).start()
    marks[...] = jnp.zeros_like(marks)
    stats_ref[...] = jnp.zeros_like(stats_ref)
    vec[...] = vec_ref[...]
    pl.semaphore_wait(barrier, RING + 1)

    CHUNK = 256
    units = slope_buf.shape[2]

    def slope_copy(layer, block):
        rows = pl.ds(pl.multiple_of(block * CHUNK, CHUNK), CHUNK)
        src = (slope_two_ref, slope_one_ref)[layer]
        return pltpu.make_async_copy(src.at[rows, :], slope_buf.at[block % 2], slope_sems.at[block % 2])

    def core_move(layer, block):
        return pltpu.make_async_remote_copy(
            src_ref=core_out.at[block % 2],
            dst_ref=core_got.at[layer, block],
            send_sem=core_send.at[block % 2],
            recv_sem=core_recv.at[layer, block],
            device_id=cores,
            device_id_type=MESH,
        )

    def far_move(layer, block):
        return pltpu.make_async_remote_copy(
            src_ref=far_out.at[block % 2],
            dst_ref=far_got.at[layer, block],
            send_sem=far_send.at[block % 2],
            recv_sem=far_recv.at[layer, block],
            device_id=across,
            device_id_type=MESH,
        )

    def lanes_of(number):
        return pl.ds(pl.multiple_of(number * units, units), units)

    def rows_at(number):
        return pl.ds(pl.multiple_of(number * 16, 16), 16)

    def free(copy, layer, block):
        @pl.when((layer > 0) | (block >= 2))
        def _():
            copy.wait_send()

    def lane_codes(first):
        return jnp.transpose(marks[first : first + 128, :])[0:1, :]

    def row_codes(values, rows):
        top = functools.reduce(
            jnp.maximum, [jnp.max(jnp.abs(value), axis=1, keepdims=True) for value in values]
        )
        code = scale_code(top)
        marks[rows, :] = jnp.broadcast_to(code, (16, 128))
        factor = TOP_CODE / code_scale(code)
        return [to_codes(value * factor) for value in values]

    def put_scale(out):
        codes = jnp.concatenate(
            [lane_codes(0), lane_codes(128), jnp.zeros((14, 128), F32)], axis=0
        )
        out[CHUNK : CHUNK + 16, 0:128] = codes.astype(jnp.int32).astype(I16)

    def read_scale(got):
        step = code_scale(from_codes(got[CHUNK : CHUNK + 16, 0:128])) * (1.0 / TOP_CODE)
        step = jnp.transpose(jnp.concatenate([step, jnp.zeros((112, 128), F32)], axis=0))
        for up in range(2):
            marks[CHUNK + up * 128 : CHUNK + (up + 1) * 128, :] = jnp.broadcast_to(
                step[:, up : up + 1], (128, 128)
            )

    def step_at(number):
        return marks[pl.ds(pl.multiple_of(CHUNK + number * 16, 16), 16), 0:1]

    def split(layer, block):
        free(core_move(layer, block), layer, block)

        def write(number, carry):
            rows = rows_at(number)
            parts = row_codes(
                [grad[rows, lanes_of(2 * half + 1 - core)] for half in range(2)], rows
            )
            for half in range(2):
                there = slice(half * units, (half + 1) * units)
                core_out[block % 2, rows, there] = parts[half]
                keep_sums[block, rows, there] = grad[rows, lanes_of(2 * half + core)]
            return carry

        lax.fori_loop(0, CHUNK // 16, write, 0)
        put_scale(core_out.at[block % 2])
        core_move(layer, block).start()

    def cross(layer, block):
        core_move(layer, block).wait_recv()
        free(far_move(layer, block), layer, block)
        got = core_got.at[layer, block]
        read_scale(got)

        def add(number, carry):
            rows = rows_at(number)
            near, away = lanes_of(high), lanes_of(1 - high)
            step = step_at(number)
            keep_sums[block, rows, near] += from_codes(got[rows, near]) * step
            value = keep_sums[block, rows, away] + from_codes(got[rows, away]) * step
            far_out[block % 2, rows, :] = row_codes([value], rows)[0]
            return carry

        lax.fori_loop(0, CHUNK // 16, add, 0)
        put_scale(far_out.at[block % 2])
        far_move(layer, block).start()

    def finish(layer, block):
        far_move(layer, block).wait_recv()
        slope_copy(layer, block).wait()
        got = far_got.at[layer, block]
        read_scale(got)

        def one(number, total):
            rows = rows_at(number)
            value = keep_sums[block, rows, lanes_of(high)] + from_codes(got[rows, :]) * step_at(number)
            value = (value * slope_buf[block % 2, rows, :]).astype(BF16)
            dz[rows, :] = value
            return total + value.astype(F32)

        total = lax.fori_loop(0, CHUNK // 16, one, jnp.zeros((16, units), F32))
        if layer == 0:

            @pl.when(block < 2)
            def _():
                slope_copy(0, block + 2).start()

            @pl.when(block >= 2)
            def _():
                slope_copy(1, block - 2).start()

        else:

            @pl.when(block < 2)
            def _():
                slope_copy(1, block + 2).start()

        total = jnp.sum(total, axis=0, keepdims=True)
        for number in range(units // 128):
            row = 4 * (1 - layer) + number
            vec[row : row + 1, :] += total[:, number * 128 : (number + 1) * 128]
        flipped = (dz_two, dz_one)[layer]
        for up in range(CHUNK // 128):
            there = pl.ds(pl.multiple_of(block * CHUNK + up * 128, 128), 128)
            for number in range(units // 128):
                tile = dz[up * 128 : (up + 1) * 128, number * 128 : (number + 1) * 128]
                flipped[number * 128 : (number + 1) * 128, there] = jnp.transpose(
                    tile.astype(F32)
                ).astype(BF16)

    def blocks(first, last, work):
        def one(block, carry):
            work(block)
            return carry

        lax.fori_loop(first, last, one, 0)

    def start_block(block):
        rows = pl.ds(pl.multiple_of(block * CHUNK, CHUNK), CHUNK)
        copy = pltpu.make_async_copy(part_ref.at[rows, :], grad.at[pl.ds(0, CHUNK), :], load_sems.at[1])
        copy.start()
        copy.wait()
        split(0, block)

    def turn_block(block):
        finish(0, block)
        for lane in range(0, grad.shape[1], 512):
            grad[0:CHUNK, lane : lane + 512] = dot_nt(dz[...], w_hid_ref[lane : lane + 512, :])
        split(1, block)

    core_out[:, CHUNK:, :] = jnp.zeros((2, 16, 2 * units), I16)
    far_out[:, CHUNK:, :] = jnp.zeros((2, 16, units), I16)
    slope_copy(0, 0).start()
    slope_copy(0, 1).start()
    blocks(0, 4, start_block)
    blocks(0, 4, lambda block: cross(0, block))

    def vec_copy(away):
        return pltpu.make_async_remote_copy(
            src_ref=vec,
            dst_ref=vecs.at[blk],
            send_sem=vec_send.at[away - 1],
            recv_sem=vec_recv.at[away - 1],
            device_id={"blk": (blk + away) % RING},
            device_id_type=MESH,
        )

    def row_scale(value, count):
        size = jnp.sum(jnp.abs(value), axis=1, keepdims=True) * (1.0 / count) + 1e-12
        code = scale_code(size)
        return size, code, size * (TOP_CODE / code_scale(code))

    def set_sizes(rows, own, sizes):
        parts = [lane_codes(first) for first in range(0, rows, 128)]
        parts.append(jnp.zeros((SCALE_ROWS - len(parts), 128), F32))
        codes = jnp.concatenate(parts, axis=0)
        sizes[...] = code_scale(codes[0:8, :])
        for number in range(2 * RING):
            own[number, rows : rows + SCALE_ROWS, :] = codes.astype(jnp.int32).astype(I16)

    def squash_rows(first, count, own, first_own, read_res, write_next):
        def some(number, carry):
            row = pl.multiple_of(number * 16, 16)
            value = grad[pl.ds(row, 16), :] + read_res(row)
            size, code, factor = row_scale(value, value.shape[1])
            grad[pl.ds(row, 16), :] = value
            marks[pl.ds(first_own + row, 16), :] = jnp.broadcast_to(code, (16, 128))
            steep = 2.0 / size
            for lane in range(0, value.shape[1], 128):
                piece = grad[pl.ds(row, 16), lane : lane + 128]
                curve = jnp.tanh(piece * steep)
                number_of = lane // 256
                chunk = number_of // 2 if number_of % 2 == 0 else 7 - number_of // 2
                own[2 * chunk + lane // 128 % 2, pl.ds(first_own + row, 16), :] = to_codes(
                    curve * factor
                )
                write_next(row, lane, piece - size * curve)
            return carry

        lax.fori_loop(0, count // 16, some, 0)

    def out_group(group):
        for part, rows in enumerate(BLOCKS):
            dl_copy(group, part).wait()
            if part == 0:

                @pl.when(group == 0)
                def _():
                    load(h_two_ref, h_buf).wait()

            for lane in range(0, grad.shape[1], 512):
                grad[0:rows, lane : lane + 512] = dot_nn(
                    dl_buf[part, 0:rows, :], h_buf[:, lane : lane + 512]
                )
            res_copy(group, part).wait()
            if part == 0:

                @pl.when(group > 0)
                def _():
                    stage_copy(group - 1, len(BLOCKS) - 1, BLOCKS[-1]).wait()

            else:
                stage_copy(group, part - 1, BLOCKS[part - 1]).wait()

            def write_next(row, lane, values):
                stage[pl.ds(row, 16), 0, lane : lane + 128] = values

            squash_rows(
                0,
                rows,
                own_out.at[group],
                starts[part],
                lambda row, part=part: res_buf[part, pl.ds(row, 16), :].astype(F32),
                write_next,
            )
            stage_start(group, part)

            @pl.when(group < OUT_GROUPS - 1)
            def _(part=part):
                res_copy(group + 1, part).start()
                dl_copy(group + 1, part).start()

            @pl.when(group == OUT_GROUPS - 1)
            def _(part=part):
                hid_res_copy(part).start()
                if part == len(BLOCKS) - 1:
                    load(h_one_ref, h_buf).start()

        set_sizes(OUT_ROWS, own_out.at[group], size_out.at[group])

    def hid_group():
        load(h_one_ref, h_buf).wait()
        for part in range(2):
            first = part * 256
            if part:
                hid_next_copy(part - 1).wait()
            for lane in range(0, grad.shape[1], 512):
                grad[0:256, lane : lane + 512] = dot_nn(
                    dz_two[first : first + 256, :], h_buf[:, lane : lane + 512]
                )
            hid_res_copy(part).wait()

            def write_next(row, lane, values):
                grad[pl.ds(row, 16), lane : lane + 128] = values

            squash_rows(
                0,
                256,
                own_hid,
                first,
                lambda row, part=part: res_buf[part, pl.ds(row, 16), :].astype(F32),
                write_next,
            )
            hid_next_copy(part).start()
        load(x_ref, h_buf.at[:, pl.ds(0, x_ref.shape[1])]).start()
        set_sizes(HID_ROWS, own_hid, size_hid)
        hid_next_copy(1).wait()

    def in_group():
        wide = x_ref.shape[1]
        load(x_ref, h_buf.at[:, pl.ds(0, wide)]).wait()
        for first in range(0, HID_ROWS, 256):
            grad[0:256, 0:wide] = dot_nn(dz_one[first : first + 256, :], h_buf[:, 0:wide])

            def some(number, carry, first=first):
                row = pl.multiple_of(number * 16, 16)
                place = pl.multiple_of(first + row, 16)
                value = grad[pl.ds(row, 16), 0:wide] + res_in_ref[pl.ds(place, 16), :].astype(F32)
                size, code, factor = row_scale(value, deep)
                curve = jnp.tanh(value * (2.0 / size))
                next_in_ref[pl.ds(place, 16), :] = value - size * curve
                marks[pl.ds(place, 16), :] = jnp.broadcast_to(code, (16, 128))
                chunk = first // 64 + number // 4
                inside = pl.multiple_of(number % 4 * 16, 16)
                codes = to_codes(curve * factor)
                for way in range(2):
                    own_in[2 * chunk + way, pl.ds(inside, 16), :] = codes[
                        :, way * 256 : (way + 1) * 256
                    ]
                return carry

            lax.fori_loop(0, 16, some, 0)
        for chunk in range(RING):
            codes = jnp.concatenate(
                [lane_codes(64 * chunk), jnp.zeros((SCALE_ROWS - 1, 128), F32)], axis=0
            )
            size_in[chunk] = code_scale(codes[0:8, :])
            for way in range(2):
                own_in[2 * chunk + way, 64 : 64 + SCALE_ROWS, 0:128] = codes.astype(
                    jnp.int32
                ).astype(I16)
                own_in[2 * chunk + way, 64 : 64 + SCALE_ROWS, 128:256] = jnp.zeros(
                    (SCALE_ROWS, 128), I16
                )

    def towards(way):
        return {"blk": ring_blk((here + 1 - 2 * way + RING) % RING)}

    def move(src, got, step, way, send_sem, recv_sem):
        return pltpu.make_async_remote_copy(
            src_ref=src,
            dst_ref=got.at[way, step],
            send_sem=send_sem.at[way, step],
            recv_sem=recv_sem.at[way, step],
            device_id=towards(way),
            device_id_type=MESH,
        )

    def first_moves(own, got, send_sem, recv_sem):
        for way in range(2):
            chunk = (here - 1 + 2 * way + RING) % RING
            move(own.at[2 * chunk + way], got, 0, way, send_sem, recv_sem).start()

    def hop(rows, own, got, own_sizes, step, way, send_sem, recv_sem, keep):
        message = got.at[way, step]
        move(message, got, step, way, send_sem, recv_sem).wait_recv()
        ahead = here - 2 - step + way * (4 + 2 * step) + 2 * RING
        chunk = ahead % RING
        mine = own.at[2 * chunk + way]
        size = own_sizes(chunk)
        came = code_scale(from_codes(message[rows : rows + SCALE_ROWS, 0:128])[0:8, :])
        code = scale_code(came + size)
        whole = code_scale(code)
        blank = jnp.zeros((112, 128), F32)
        wide = message.shape[1]

        @pl.when(step < STEPS - 1)
        def _():
            shares = jnp.transpose(jnp.concatenate([came / whole, size / whole, blank], axis=0))
            for number, first in enumerate(range(0, rows, 128)):
                count = min(128, rows - first)
                there = slice(first, first + count)
                message[there, :] = to_codes(
                    from_codes(message[there, :]) * shares[0:count, number : number + 1]
                    + from_codes(mine[there, :]) * shares[0:count, 8 + number : 9 + number]
                )
            codes = jnp.concatenate([code, jnp.zeros((SCALE_ROWS - 8, 128), F32)], axis=0)
            message[rows : rows + SCALE_ROWS, 0:128] = codes.astype(jnp.int32).astype(I16)
            move(message, got, step + 1, way, send_sem, recv_sem).start()

        @pl.when(step == STEPS - 1)
        def _():
            shares = jnp.transpose(
                jnp.concatenate([came * (1.0 / TOP_CODE), size * (1.0 / TOP_CODE), blank], axis=0)
            )
            square = jnp.zeros((1, wide), F32)
            for number, first in enumerate(range(0, rows, 128)):
                count = min(128, rows - first)
                there = slice(first, first + count)
                value = (
                    from_codes(message[there, :]) * shares[0:count, number : number + 1]
                    + from_codes(mine[there, :]) * shares[0:count, 8 + number : 9 + number]
                )
                keep(first, count, value)
                square = square + jnp.sum(value * value, axis=0, keepdims=True)
            for lane in range(0, wide, 128):
                stats_ref[0:1, :] += square[:, lane : lane + 128]

    def out_hop(group, step, way):
        def keep(first, count, value):
            row = pl.multiple_of(group * OUT_ROWS + first, 16)

            @pl.when(way == 0)
            def _():
                red_out_ref[pl.ds(row, count), 0:128] = value

            @pl.when(way == 1)
            def _():
                red_out_ref[pl.ds(row, count), 128:256] = value

        hop(
            OUT_ROWS,
            own_out.at[group],
            got_out.at[group],
            lambda chunk: size_out[group],
            step,
            way,
            out_send.at[group],
            out_recv.at[group],
            keep,
        )

    def hid_hop(step, way):
        def keep(first, count, value):
            @pl.when(way == 0)
            def _():
                red_hid_ref[first : first + count, 0:128] = value

            @pl.when(way == 1)
            def _():
                red_hid_ref[first : first + count, 128:256] = value

        hop(
            HID_ROWS, own_hid, got_hid, lambda chunk: size_hid[...], step, way, hid_send, hid_recv, keep
        )

    def share_move(step, way):
        place = (here - step + 2 * step * way + 2 * RING) % RING
        return pltpu.make_async_remote_copy(
            src_ref=share_in.at[way, place],
            dst_ref=share_in.at[way, place],
            send_sem=share_send.at[way, step],
            recv_sem=share_recv.at[way, step],
            device_id=towards(way),
            device_id_type=MESH,
        )

    def in_hop(step, way):
        def keep(first, count, value):
            share_in[way, here] = value

        hop(64, own_in, got_in, lambda chunk: size_in[chunk], step, way, in_send, in_recv, keep)

        @pl.when(step == STEPS - 1)
        def _():
            share_move(0, way).start()

    def share_hop(step, way):
        share_move(step, way).wait_recv()

        @pl.when(step < STEPS - 1)
        def _():
            share_move(step + 1, way).start()

    def in_step(index, way):
        @pl.when((index >= 0) & (index < STEPS))
        def _():
            in_hop(index, way)

        @pl.when((index >= STEPS) & (index < 2 * STEPS))
        def _():
            share_hop(index - STEPS, way)

    def ways(work):
        def one(way, carry):
            work(way)
            return carry

        lax.fori_loop(0, 2, one, 0)

    def wave(number, carry):
        @pl.when(number < OUT_GROUPS)
        def _():
            out_group(number)
            first_moves(own_out.at[number], got_out.at[number], out_send.at[number], out_recv.at[number])

        @pl.when(number == HID_WAVE)
        def _():
            hid_group()
            first_moves(own_hid, got_hid, hid_send, hid_recv)

        index = 2 * (number - IN_WAVE - 1)
        ways(lambda way: in_step(index, way))

        def both(way):
            @pl.when((number > HID_WAVE) & (number <= HID_WAVE + STEPS))
            def _():
                hid_hop(number - HID_WAVE - 1, way)

            def outs(group, carry):
                step = number - 1 - group

                @pl.when((step >= 0) & (step < STEPS))
                def _():
                    out_hop(group, step, way)

                return carry

            lax.fori_loop(0, OUT_GROUPS, outs, 0)

        ways(both)

        @pl.when((number == 1) | (number == 2))
        def _():
            blocks(2 * number - 2, 2 * number, turn_block)

        @pl.when(number == 3)
        def _():
            blocks(0, 4, lambda block: cross(1, block))

        @pl.when(number == IN_WAVE)
        def _():
            blocks(0, 4, lambda block: finish(1, block))
            in_group()
            first_moves(own_in, got_in, in_send, in_recv)
            for away in range(1, RING):
                vec_copy(away).start()

        ways(lambda way: in_step(index + 1, way))
        return carry

    lax.fori_loop(0, IN_WAVE + 1 + STEPS, wave, 0)

    for place in range(RING):
        for way in range(2):
            red_in_ref[place * 64 : (place + 1) * 64, way * 256 : (way + 1) * 256] = share_in[
                way, place
            ]
    for away in range(1, RING):
        vec_copy(away).wait_recv()
    vecs[blk] = vec[...]
    total = vecs[0]
    for number in range(1, RING):
        total = total + vecs[number]
    vec_sum_ref[...] = total
    for away in range(1, RING):
        vec_copy(away).wait_send()
    for slot in range(2):
        core_move(1, 2 + slot).wait_send()
        far_move(1, 2 + slot).wait_send()
    stage_copy(OUT_GROUPS - 1, len(BLOCKS) - 1, last_rows).wait()
    for way in range(2):
        for step in range(STEPS):
            for group in range(OUT_GROUPS):
                move(
                    got_out.at[group, way, step],
                    got_out.at[group],
                    step,
                    way,
                    out_send.at[group],
                    out_recv.at[group],
                ).wait_send()
            move(got_hid.at[way, step], got_hid, step, way, hid_send, hid_recv).wait_send()
            move(got_in.at[way, step], got_in, step, way, in_send, in_recv).wait_send()
            share_move(step, way).wait_send()


def reduce_grads(
    dl, h_two, h_one, x, part, slope_two, slope_one, w_hid, res_out, res_hid, res_in, vec, senones, deep
):
    frames, wide = h_two.shape
    in_wide = x.shape[1]
    units = w_hid.shape[1]
    vmem = pl.BlockSpec(memory_space=pltpu.VMEM)
    hbm = pl.BlockSpec(memory_space=pl.ANY)
    message = OUT_ROWS + SCALE_ROWS
    hid_message = HID_ROWS + SCALE_ROWS
    in_message = 64 + SCALE_ROWS
    sem = pltpu.SemaphoreType.DMA
    return pl.pallas_call(
        functools.partial(reduce_kernel, deep),
        out_shape=(
            jax.ShapeDtypeStruct((senones, 1, wide), F32),
            jax.ShapeDtypeStruct((HID_ROWS, wide), F32),
            jax.ShapeDtypeStruct((HID_ROWS, in_wide), F32),
            jax.ShapeDtypeStruct((OUT_GROUPS * OUT_ROWS, 256), F32),
            jax.ShapeDtypeStruct((HID_ROWS, 256), F32),
            jax.ShapeDtypeStruct((HID_ROWS, in_wide), F32),
            jax.ShapeDtypeStruct(vec.shape, F32),
            jax.ShapeDtypeStruct((8, 128), F32),
        ),
        in_specs=[hbm] * 7 + [vmem] + [hbm] * 2 + [vmem] * 2,
        out_specs=(hbm, hbm) + (vmem,) * 6,
        scratch_shapes=[
            pltpu.VMEM((BLOCKS[0], wide), F32),
            pltpu.VMEM((BLOCKS[0], 1, wide), F32),
            pltpu.VMEM((2, BLOCKS[0], wide), BF16),
            pltpu.VMEM((2, BLOCKS[0], frames), BF16),
            pltpu.VMEM((frames, wide), BF16),
            pltpu.VMEM((2, 256, units), F32),
            pltpu.VMEM((640, 128), F32),
            pltpu.VMEM((4, 256, 2 * units), F32),
            pltpu.VMEM((256, units), BF16),
            pltpu.VMEM((units, frames), BF16),
            pltpu.VMEM((units, frames), BF16),
            pltpu.VMEM((2, 272, 2 * units), I16),
            pltpu.VMEM((2, 4, 272, 2 * units), I16),
            pltpu.VMEM((2, 272, units), I16),
            pltpu.VMEM((2, 4, 272, units), I16),
            pltpu.VMEM((OUT_GROUPS, 2 * RING, message, 128), I16),
            pltpu.VMEM((OUT_GROUPS, 2, STEPS, message, 128), I16),
            pltpu.VMEM((OUT_GROUPS, 8, 128), F32),
            pltpu.VMEM((2 * RING, hid_message, 128), I16),
            pltpu.VMEM((2, STEPS, hid_message, 128), I16),
            pltpu.VMEM((8, 128), F32),
            pltpu.VMEM((2 * RING, in_message, 256), I16),
            pltpu.VMEM((2, STEPS, in_message, 256), I16),
            pltpu.VMEM((RING, 8, 128), F32),
            pltpu.VMEM((2, RING, 64, 256), F32),
            pltpu.VMEM(vec.shape, F32),
            pltpu.VMEM((RING,) + vec.shape, F32),
            sem((2,)),
            sem((2,)),
            sem((2,)),
            sem((1,)),
            sem((2,)),
            sem((2,)),
            sem((2, 4)),
            sem((2,)),
            sem((2, 4)),
            sem((OUT_GROUPS, 2, STEPS)),
            sem((OUT_GROUPS, 2, STEPS)),
            sem((2, STEPS)),
            sem((2, STEPS)),
            sem((2, STEPS)),
            sem((2, STEPS)),
            sem((2, STEPS)),
            sem((2, STEPS)),
            sem((STEPS,)),
            sem((STEPS,)),
        ],
        compiler_params=pltpu.CompilerParams(
            collective_id=1, has_side_effects=True, vmem_limit_bytes=63 * 1024 * 1024
        ),
    )(dl, h_two, h_one, x, part, slope_two, slope_one, w_hid, res_out, res_hid, res_in, vec)


RING_STARTS = (0, 2, 5, 7, 9)
LAYER_TWO_WAVE = 7
LOGIT_WAVES = (11, 12, 14, 16)


def forward_kernel(
    slot_count,
    x_ref,
    tags_ref,
    w_in_ref,
    w_hid_ref,
    w_out_ref,
    bias_ref,
    bias_out_ref,
    x_out,
    h_one_out,
    h_two_out,
    slope_one_out,
    slope_two_out,
    w_hid_out,
    w_out_out,
    dl_ref,
    bias_sum_ref,
    loss_ref,
    x_all,
    h_one,
    h_two,
    slope_one,
    slope_two,
    w_in,
    w_hid,
    w_out,
    curve,
    bias_col,
    tags,
    sums,
    ring_send,
    ring_recv,
    x_send,
    x_recv,
    h_send,
    h_recv,
    tag_send,
    tag_recv,
    sum_send,
    sum_recv,
    out_sems,
):
    blk = lax.axis_index("blk")
    col = lax.axis_index("col")
    here = ring_place(blk)
    senones, depth = w_out_ref.shape
    own_rows, deep = x_ref.shape
    units = w_hid_ref.shape[1]
    frames = x_all.shape[0]
    cores = {"col": col + 1 - 2 * (col % 2)}
    across = {"col": (col + 2) % 4}
    corner = {"col": (col + 2) % 4 + 1 - 2 * (col % 2)}
    others = (cores, across, corner)

    barrier = pltpu.get_barrier_semaphore()
    for target in others + tuple({"blk": ring_blk((here + way) % RING)} for way in (1, 7)):
        pl.semaphore_signal(barrier, inc=1, device_id=target, device_id_type=MESH)

    w_hid[pl.ds(pl.multiple_of(blk * depth, depth), depth), :] = w_hid_ref[...].astype(BF16)
    own_lanes = pl.ds(pl.multiple_of(blk * depth, depth), depth)
    w_out[senones // 16 * 16 :, own_lanes] = jnp.zeros(
        (w_out.shape[0] - senones // 16 * 16, depth), BF16
    )
    w_out[0:senones, own_lanes] = w_out_ref[...].astype(BF16)
    own_frames = pl.ds(pl.multiple_of(col * own_rows, own_rows), own_rows)
    x_all[own_frames, :] = jnp.zeros((own_rows, x_all.shape[1]), BF16)
    x_all[own_frames, 0:deep] = x_ref[...]
    tags[col] = tags_ref[...]
    sums[...] = jnp.zeros_like(sums)
    pl.semaphore_wait(barrier, 5)

    def ring_part(group, origin, way):
        start = pl.multiple_of(origin * depth + way * 128, 128)
        if group == 0:
            return w_hid.at[pl.ds(start, 128), :]
        return w_out.at[pl.ds((group - 1) * OUT_ROWS, OUT_ROWS), pl.ds(start, 128)]

    def ring_move(group, step, way):
        origin = ring_blk((here - step + 2 * step * way + RING) % RING)
        part = ring_part(group, origin, way)
        return pltpu.make_async_remote_copy(
            src_ref=part,
            dst_ref=part,
            send_sem=ring_send.at[group, way, step],
            recv_sem=ring_recv.at[group, way, step],
            device_id={"blk": ring_blk((here + 1 - 2 * way + RING) % RING)},
            device_id_type=MESH,
        )

    def ring_wave(wave):
        for group, start in enumerate(RING_STARTS):
            step = wave - 1 - start
            for way in range(2):
                if step == -1:
                    ring_move(group, 0, way).start()
                if 0 <= step < STEPS:
                    ring_move(group, step, way).wait_recv()
                    if step < STEPS - 1:
                        ring_move(group, step + 1, way).start()

    def copy_to(target, src, send_sem, recv_sem):
        return pltpu.make_async_remote_copy(
            src_ref=src,
            dst_ref=src,
            send_sem=send_sem,
            recv_sem=recv_sem,
            device_id=target,
            device_id_type=MESH,
        )

    def rows_of(owner):
        return pl.ds(pl.multiple_of(owner * own_rows, own_rows), own_rows)

    def lanes_of(owner):
        return pl.ds(pl.multiple_of(owner * units, units), units)

    def x_move(number):
        owner = across["col"] if number == 2 else col
        target = across if number == 1 else cores
        return copy_to(target, x_all.at[rows_of(owner), :], x_send.at[number], x_recv.at[number])

    def h_move(layer, number, block):
        owner = across["col"] if number == 2 else col
        target = across if number == 1 else cores
        whole = (h_one, h_two)[layer]
        part = whole.at[pl.ds(block * own_rows, own_rows), lanes_of(owner)]
        return copy_to(
            target, part, h_send.at[layer, number, block], h_recv.at[layer, number, block]
        )

    def h_start(layer, block):
        h_move(layer, 0, block).start()
        h_move(layer, 1, block).start()

    def h_forward(layer, block):
        h_move(layer, 1, block).wait_recv()
        h_move(layer, 2, block).start()

    def h_ready(layer, block):
        h_move(layer, 0, block).wait_recv()
        h_move(layer, 2, block).wait_recv()

    ring_wave(0)
    x_move(0).start()
    x_move(1).start()
    tag_copies = [
        copy_to(target, tags.at[col], tag_send.at[number], tag_recv.at[number])
        for number, target in enumerate(others)
    ]
    for copy in tag_copies:
        copy.start()
    w_in[...] = jnp.zeros_like(w_in)
    w_in[0:deep, :] = w_in_ref[...].astype(BF16)
    for number in range(bias_out_ref.shape[0]):
        line = jnp.broadcast_to(bias_out_ref[number : number + 1, :], (128, 128))
        bias_col[number * 128 : (number + 1) * 128, :] = jnp.transpose(line)
    ring_wave(1)
    x_move(1).wait_recv()
    x_move(2).start()
    x_move(0).wait_recv()
    x_move(2).wait_recv()

    def layer(number, block, inputs, weights, whole, slopes):
        there = slice(block * own_rows, (block + 1) * own_rows)
        value = jax.nn.sigmoid(
            dot_nn(inputs[there, :], weights[...]) + bias_ref[number : number + 1, :]
        )
        slopes[there, :] = value * (1.0 - value)
        whole[there, lanes_of(col)] = value.astype(BF16)
        h_start(number, block)

    outs = []

    def put(src, dst):
        copy = pltpu.make_async_copy(src, dst, out_sems.at[len(outs)])
        copy.start()
        outs.append(copy)

    for block in range(4):
        layer(0, block, x_all, w_in, h_one, slope_one)
    put(x_all, x_out)
    put(slope_one, slope_one_out)

    def all_tags():
        return jnp.concatenate([tags[owner, 0:1, :] for owner in range(4)], axis=1)

    def own_row(line):
        line = line - col * senones
        return jnp.where(line < senones, line, -1)

    def logits(group):
        first = group * OUT_ROWS
        half = frames // 2
        for part in range(2):
            curve[first : first + OUT_ROWS, part * half : (part + 1) * half] = dot_nt(
                w_out[first : first + OUT_ROWS, :], h_two[part * half : (part + 1) * half, :]
            )
        base = lax.broadcasted_iota(jnp.int32, (16, frames), 0)

        def largest(number, top):
            row = pl.multiple_of(first + number * 16, 16)
            value = curve[pl.ds(row, 16), :] + bias_col[pl.ds(row, 16), 0:1]
            if group == OUT_GROUPS - 1:
                value = jnp.where(base + row < senones, value, -1e30)
            curve[pl.ds(row, 16), :] = value
            return jnp.maximum(top, value)

        top = lax.fori_loop(0, OUT_ROWS // 16, largest, jnp.full((16, frames), -1e30, F32))
        top = jnp.max(top, axis=0, keepdims=True)
        line = jnp.broadcast_to(own_row(all_tags()), (16, frames))

        def exponents(number, carry):
            total, picked = carry
            row = pl.multiple_of(first + number * 16, 16)
            value = curve[pl.ds(row, 16), :]
            power = jnp.exp(value - top)
            curve[pl.ds(row, 16), :] = power
            return total + power, picked + jnp.where(base + row == line, value, 0.0)

        blank = jnp.zeros((16, frames), F32)
        total, picked = lax.fori_loop(0, OUT_ROWS // 16, exponents, (blank, blank))
        sums[col, group : group + 1, :] = top
        sums[col, 4 + group : 5 + group, :] = jnp.sum(total, axis=0, keepdims=True)
        sums[col, 8 + group : 9 + group, :] = jnp.sum(picked, axis=0, keepdims=True)

    last_wave = RING_STARTS[-1] + STEPS
    for wave in range(2, last_wave + 1):
        ring_wave(wave)
        if 2 <= wave < 6:
            h_forward(0, wave - 2)
        if wave == LAYER_TWO_WAVE:
            for block in range(4):
                h_ready(0, block)
                layer(1, block, h_one, w_hid, h_two, slope_two)
            put(h_one, h_one_out)
            put(slope_two, slope_two_out)
            put(w_hid, w_hid_out)
        if LAYER_TWO_WAVE < wave <= LAYER_TWO_WAVE + 4:
            h_forward(1, wave - LAYER_TWO_WAVE - 1)
        for group, when in enumerate(LOGIT_WAVES):
            if wave == when:
                if group == 0:
                    for block in range(4):
                        h_ready(1, block)
                    put(h_two, h_two_out)
                    for copy in tag_copies:
                        copy.wait_recv()
                rows = pl.ds(group * OUT_ROWS, OUT_ROWS)
                put(w_out.at[rows, :], w_out_out.at[rows, :])
                logits(group)

    sum_copies = [
        copy_to(target, sums.at[col], sum_send.at[number], sum_recv.at[number])
        for number, target in enumerate(others)
    ]
    for copy in sum_copies:
        copy.start()
    for copy in sum_copies:
        copy.wait_recv()

    def lines(first):
        return [sums[owner, first + group : first + group + 1, :] for owner in range(4) for group in range(4)]

    tops = lines(0)
    top = functools.reduce(jnp.maximum, tops)
    total = functools.reduce(
        jnp.add, [size * jnp.exp(own - top) for own, size in zip(tops, lines(4), strict=True)]
    )
    picked = functools.reduce(jnp.add, lines(8))
    line = all_tags()
    live = line >= 0
    loss = jnp.where(live, top + jnp.log(total) - picked, 0.0)
    loss_ref[...] = jnp.zeros_like(loss_ref)
    loss_ref[0:1, :] = functools.reduce(
        jnp.add, [loss[:, lane : lane + 128] for lane in range(0, frames, 128)]
    )
    weight = jnp.where(live, 1.0 / slot_count, 0.0)
    line = jnp.broadcast_to(own_row(line), (16, frames))
    hit_weight = jnp.broadcast_to(weight, (16, frames))
    base = lax.broadcasted_iota(jnp.int32, (16, frames), 0)
    bias_col[...] = jnp.zeros_like(bias_col)
    for group in range(OUT_GROUPS):
        share = jnp.exp(sums[col, group : group + 1, :] - top) / total * weight

        def gradient(number, carry, first=group * OUT_ROWS, share=share):
            row = pl.multiple_of(first + number * 16, 16)
            value = curve[pl.ds(row, 16), :] * share - jnp.where(base + row == line, hit_weight, 0.0)
            value = value.astype(BF16)
            dl_ref[pl.ds(row, 16), :] = value
            bias_col[pl.ds(row, 16), :] = jnp.broadcast_to(
                jnp.sum(value.astype(F32), axis=1, keepdims=True), (16, 128)
            )
            return carry

        lax.fori_loop(0, OUT_ROWS // 16, gradient, 0)
    bias_sum_ref[...] = jnp.zeros_like(bias_sum_ref)
    for number in range(bias_out_ref.shape[0]):
        block = jnp.transpose(bias_col[number * 128 : (number + 1) * 128, :])
        bias_sum_ref[number : number + 1, :] = block[0:1, :]

    for group in range(len(RING_STARTS)):
        for way in range(2):
            for step in range(STEPS):
                ring_move(group, step, way).wait_send()
    for number in range(3):
        x_move(number).wait_send()
        for block in range(4):
            h_move(0, number, block).wait_send()
            h_move(1, number, block).wait_send()
    for copy in tag_copies + sum_copies:
        copy.wait_send()
    for copy in outs:
        copy.wait()


def forward_pass(x, tags, w_in, w_hid, w_out, bias, bias_out, slot_count):
    own_rows = x.shape[0]
    units = w_hid.shape[1]
    frames = 4 * own_rows
    wide = 4 * units
    rows = OUT_GROUPS * OUT_ROWS
    blocks = bias_out.shape[0]
    vmem = pl.BlockSpec(memory_space=pltpu.VMEM)
    hbm = pl.BlockSpec(memory_space=pl.ANY)
    sem = pltpu.SemaphoreType.DMA
    kept = (
        ((frames, 512), BF16),
        ((frames, wide), BF16),
        ((frames, wide), BF16),
        ((frames, units), F32),
        ((frames, units), F32),
        ((wide, units), BF16),
        ((rows, wide), BF16),
    )
    return pl.pallas_call(
        functools.partial(forward_kernel, slot_count),
        out_shape=tuple(jax.ShapeDtypeStruct(shape, kind) for shape, kind in kept)
        + (
            jax.ShapeDtypeStruct((rows, frames), BF16),
            jax.ShapeDtypeStruct((24, 128), F32),
            jax.ShapeDtypeStruct((8, 128), F32),
        ),
        in_specs=[vmem] * 7,
        out_specs=(hbm,) * 7 + (vmem,) * 3,
        scratch_shapes=[pltpu.VMEM(shape, kind) for shape, kind in kept[:5]]
        + [
            pltpu.VMEM((512, units), BF16),
            pltpu.VMEM((wide, units), BF16),
            pltpu.VMEM((rows, wide), BF16),
            pltpu.VMEM((rows, frames), F32),
            pltpu.VMEM((blocks * 128, 128), F32),
            pltpu.VMEM((4,) + tags.shape, jnp.int32),
            pltpu.VMEM((4, 16, frames), F32),
            sem((5, 2, STEPS)),
            sem((5, 2, STEPS)),
            sem((3,)),
            sem((3,)),
            sem((2, 3, 4)),
            sem((2, 3, 4)),
            sem((3,)),
            sem((3,)),
            sem((3,)),
            sem((3,)),
            sem((16,)),
        ],
        compiler_params=pltpu.CompilerParams(
            collective_id=2, has_side_effects=True, vmem_limit_bytes=60 * 1024 * 1024
        ),
    )(x, tags, w_in, w_hid, w_out, bias, bias_out)


DIM_BITS = (2, 4, 8)
ORDERS = ((0, 1, 2), (1, 2, 0), (2, 0, 1))
PIECE = 48
LIGHT_HID = 3
LIGHT_IN = 2


def stage_sends(stage, sources):
    moves = []
    for piece, order in enumerate(ORDERS):
        slot = sum(DIM_BITS[order[index]] for index in sources)
        moves.append((piece, slot, order[stage]))
    return moves


def landed(moves):
    return [(slot | DIM_BITS[dim], piece) for piece, slot, dim in moves]


FIRST = stage_sends(0, ())
SECOND = stage_sends(1, ())
SECOND_ON = stage_sends(1, (0,))
THIRD = stage_sends(2, ())
THIRD_A = stage_sends(2, (0,))
THIRD_B = stage_sends(2, (1,))
THIRD_C = stage_sends(2, (0, 1))
MOVES = FIRST + SECOND + SECOND_ON + THIRD + THIRD_A + THIRD_B + THIRD_C


def muon_kernel(
    stats_ref,
    red_hid_ref,
    mom_hid_ref,
    red_in_ref,
    mom_in_ref,
    hid_ref,
    inp_ref,
    next_hid_ref,
    next_in_ref,
    norm_ref,
    codes,
    tops,
    lows,
    scales,
    xs,
    us,
    vs,
    lhs,
    xin,
    xin_top,
    xin_low,
    gram,
    gram_got,
    back,
    sums,
    sums_got,
    send_sems,
    core_sems,
    recv_sems,
    back_send,
    back_recv,
    sums_send,
    sums_recv,
    spread_send,
    spread_recv,
    pair_send,
    pair_recv,
):
    blk = lax.axis_index("blk")
    col = lax.axis_index("col")
    rows, wide = xs.shape
    height = back.shape[2]
    part_wide = inp_ref.shape[1]
    other_core = {"col": col + 1 - 2 * (col % 2)}
    dims = (
        {"blk": blk + 1 - 2 * (blk % 2)},
        {"col": (col + 2) % 4},
        {"blk": blk + 2 - 4 * ((blk // 2) % 2)},
    )
    far = {"blk": (blk + 4) % 8}
    diagonal = {"blk": 4 * (blk // 4) + 3 - blk % 4}
    barrier = pltpu.get_barrier_semaphore()
    for target in (other_core, dims[1], *({"blk": (blk + away) % 8} for away in range(1, 8))):
        pl.semaphore_signal(barrier, inc=1, device_id=target, device_id_type=MESH)

    def fold(values):
        line = jnp.sum(values, axis=0, keepdims=True)
        return sum(line[:, lane : lane + 128] for lane in range(0, line.shape[1], 128))

    share = 0.125
    sums[0, 0:1, :] = fold(stats_ref[...])
    sums[0, 1:2, :] = fold(mom_hid_ref[...] * mom_hid_ref[...])
    sums[0, 2:3, :] = fold(mom_hid_ref[...] * red_hid_ref[...])
    sums[0, 3:4, :] = fold(red_hid_ref[...] * red_hid_ref[...])
    sums[0, 4:5, :] = fold(mom_in_ref[...] * mom_in_ref[...]) * share
    sums[0, 5:6, :] = fold(mom_in_ref[...] * red_in_ref[...]) * share
    sums[0, 6:7, :] = fold(red_in_ref[...] * red_in_ref[...]) * share
    sums[0, 7:8, :] = jnp.zeros((1, 128), F32)
    for turn in range(2):
        codes[turn, 0, rows:, :] = jnp.zeros((codes.shape[2] - rows, wide), I16)
    eye = lax.broadcasted_iota(jnp.int32, (rows, rows), 0) == lax.broadcasted_iota(
        jnp.int32, (rows, rows), 1
    )
    pl.semaphore_wait(barrier, 9)

    for number, target in enumerate((other_core, *dims, far)):
        copy = pltpu.make_async_remote_copy(
            src_ref=sums.at[number],
            dst_ref=sums_got.at[number],
            send_sem=sums_send.at[number],
            recv_sem=sums_recv.at[number],
            device_id=target,
            device_id_type=MESH,
        )
        copy.start()
        copy.wait()
        sums[number + 1] = sums[number] + sums_got[number]
    whole = jnp.sum(sums[5], axis=1, keepdims=True)
    clip = jnp.sqrt(whole[0:1])
    factor = jnp.minimum(1.0, CLIP / clip)

    def norm_of(first):
        square = (
            0.25 * whole[first : first + 1]
            + factor * whole[first + 1 : first + 2]
            + factor * factor * whole[first + 2 : first + 3]
        )
        return 1.0 / (jnp.sqrt(jnp.maximum(square, 0.0)) + 1e-07)

    norm_ref[0:4, :] = jnp.broadcast_to(clip, (4, 128))
    norm_ref[4:8, :] = jnp.broadcast_to(factor, (4, 128))
    next_hid_ref[...] = 0.5 * mom_hid_ref[...] + factor * red_hid_ref[...]
    next_in_ref[...] = 0.5 * mom_in_ref[...] + factor * red_in_ref[...]

    my_lanes = pl.ds(pl.multiple_of(blk * height, height), height)
    spread = []
    for away in range(1, 8):
        target = (blk + away) % 8
        spread.append(
            pltpu.make_async_remote_copy(
                src_ref=next_hid_ref.at[
                    pl.ds(pl.multiple_of(target % 4 * rows, rows), rows), :
                ],
                dst_ref=xs.at[:, my_lanes],
                send_sem=spread_send.at[away - 1],
                recv_sem=spread_recv.at[away - 1],
                device_id={"blk": target},
                device_id_type=MESH,
            )
        )
        spread[-1].start()
    high = col // 2
    my_half = pl.ds(pl.multiple_of(high * part_wide, part_wide), part_wide)
    half_copy = pltpu.make_async_remote_copy(
        src_ref=next_in_ref,
        dst_ref=xin.at[:, my_half],
        send_sem=pair_send.at[0],
        recv_sem=pair_recv.at[0],
        device_id=dims[1],
        device_id_type=MESH,
    )
    half_copy.start()
    xs[:, my_lanes] = next_hid_ref[pl.ds(pl.multiple_of(blk % 4 * rows, rows), rows), :]
    xin[:, my_half] = next_in_ref[...]
    for copy in spread:
        copy.wait_recv()
    xs[...] = xs[...] * norm_of(1)
    in_scale = norm_of(4)

    numbers = {move: number for number, move in enumerate(MOVES)}

    def part(turn, slot, piece):
        return codes.at[turn, slot, pl.ds(piece * PIECE, PIECE), :]

    def send(turn, move):
        piece, slot, dim = move
        return pltpu.make_async_remote_copy(
            src_ref=part(turn, slot, piece),
            dst_ref=part(turn, slot | DIM_BITS[dim], piece),
            send_sem=send_sems.at[numbers[move]],
            recv_sem=recv_sems.at[turn, slot | DIM_BITS[dim], piece],
            device_id=dims[dim],
            device_id_type=MESH,
        )

    def send_all(turn, moves):
        for move in moves:
            send(turn, move).start()

    def to_core(turn, slot, piece):
        return pltpu.make_async_remote_copy(
            src_ref=part(turn, slot, piece),
            dst_ref=part(turn, slot + 1, piece),
            send_sem=core_sems.at[slot // 2, piece],
            recv_sem=recv_sems.at[turn, slot + 1, piece],
            device_id=other_core,
            device_id_type=MESH,
        )

    def arrived(turn, slot, piece):
        pltpu.make_async_remote_copy(
            src_ref=part(turn, slot, piece),
            dst_ref=part(turn, slot, piece),
            send_sem=core_sems.at[0, 0],
            recv_sem=recv_sems.at[turn, slot, piece],
            device_id=other_core,
            device_id_type=MESH,
        ).wait_recv()

    def forward(turn, moves, on=()):
        for number, (slot, piece) in enumerate(landed(moves)):
            arrived(turn, slot, piece)
            to_core(turn, slot, piece).start()
            if on:
                send(turn, on[number]).start()

    def gram_copy():
        return pltpu.make_async_remote_copy(
            src_ref=gram,
            dst_ref=gram_got,
            send_sem=pair_send.at[1],
            recv_sem=pair_recv.at[1],
            device_id=other_core,
            device_id_type=MESH,
        )

    def unpack(turn, pair, light):
        for core in range(2):
            here = slice(core * rows, (core + 1) * rows)
            whole = from_codes(codes[turn, 2 * pair + core, 0:rows, :])
            if light:
                tops[pair, here, :] = whole.astype(BF16)
            else:
                top, low = halves(whole)
                tops[pair, here, :] = top
                lows[pair, here, :] = low
            step = from_codes(codes[turn, 2 * pair + core, rows : rows + 16, 0:rows])
            size = code_scale(step[0:8, :]) * (1.0 / TOP_CODE)
            scales[pair, :, here] = size * size

    def apply_pair(pair, out, light):
        cut = 512
        if light:
            inner = (dot_nt(lhs[0:rows, :], tops[pair]) * scales[pair, 0:1, :]).astype(BF16)
            for start in range(0, wide, cut):
                lanes = slice(start, start + cut)
                out[:, lanes] += dot_nn(inner, tops[pair, :, lanes])
            return
        both = dot_nt(lhs[...], tops[pair])
        inner = both[:rows] + both[rows:] + dot_nt(lhs[0:rows, :], lows[pair])
        inner = inner * scales[pair, 0:1, :]
        top, low = halves(inner)
        stack = jnp.concatenate([top, low], axis=0)
        for start in range(0, wide, cut):
            lanes = slice(start, start + cut)
            both = dot_nn(stack, tops[pair, :, lanes])
            out[:, lanes] += both[:rows] + both[rows:] + dot_nn(top, lows[pair, :, lanes])

    def set_lhs(values):
        top, low = halves(values)
        lhs[0:rows, :] = top
        lhs[rows:, :] = low

    def input_gram(light):
        top, low = halves(xin[...])
        xin_top[...] = top
        if light:
            gram[...] = dot_nt(xin_top[...], xin_top[...])
        else:
            xin_low[...] = low
            cross = dot_nt(xin_top[...], xin_low[...])
            gram[...] = dot_nt(xin_top[...], xin_top[...]) + (cross + jnp.transpose(cross))
        gram_copy().start()

    def input_step(light):
        gram_copy().wait()
        square_of = gram[...] + gram_got[...]
        top, low = halves(square_of)
        if light:
            poly = NS_B * square_of + NS_C * dot_nn(top, top)
        else:
            cross = dot_nn(top, low)
            poly = NS_B * square_of + NS_C * (dot_nn(top, top) + (cross + jnp.transpose(cross)))
        top, low = halves(poly)
        cut = 512
        for start in range(0, xin.shape[1], cut):
            lanes = slice(start, start + cut)
            change = dot_nn(top, xin_top[:, lanes])
            if not light:
                change = change + dot_nn(low, xin_top[:, lanes]) + dot_nn(top, xin_low[:, lanes])
            xin[:, lanes] = NS_A * xin[:, lanes] + change

    def by_weight(number, limit, work):
        @pl.when(number < limit)
        def _():
            work(True)

        @pl.when(number >= limit)
        def _():
            work(False)

    def iteration(number, carry):
        turn = number % 2
        values = xs[...]
        largest = jnp.max(jnp.abs(values), axis=1, keepdims=True)
        step = scale_code(largest)
        codes[turn, 0, 0:rows, :] = to_codes(values * (TOP_CODE / code_scale(step)))
        lane_step = jnp.sum(jnp.where(eye, step, 0.0), axis=0, keepdims=True)
        codes[turn, 0, rows : rows + 16, 0:rows] = jnp.broadcast_to(
            lane_step.astype(jnp.int32), (16, rows)
        ).astype(I16)
        send_all(turn, FIRST)
        for piece in range(3):
            to_core(turn, 0, piece).start()
        send_all(turn, SECOND)
        set_lhs(values)
        us[...] = jnp.zeros_like(us)
        vs[...] = jnp.zeros_like(vs)

        def first_pass(index, carry):
            pair = index + (index // 3) * (1 - index // 4) - (index // 4) * (1 - index // 5)

            @pl.when(index == 1)
            def _():
                forward(turn, FIRST, SECOND_ON)
                send_all(turn, THIRD)
                send_all(turn, THIRD_A)

                @pl.when(number > 0)
                def _():
                    by_weight(number, LIGHT_IN, input_gram)

                forward(turn, SECOND, THIRD_B)
                forward(turn, SECOND_ON, THIRD_C)

                @pl.when(number > 0)
                def _():
                    by_weight(number, LIGHT_IN, input_step)

                forward(turn, THIRD)

            @pl.when(index == 4)
            def _():
                forward(turn, THIRD_A)
                forward(turn, THIRD_B)

            @pl.when((index == 6) & (number == 0))
            def _():
                half_copy.wait()
                xin[...] = xin[...] * in_scale
                input_gram(True)
                input_step(True)

            @pl.when(index == 7)
            def _():
                forward(turn, THIRD_C)

            for piece in range(3):
                arrived(turn, 2 * pair + 1, piece)

            def work(light):
                unpack(turn, pair, light)
                apply_pair(pair, us, light)

            by_weight(number, LIGHT_HID, work)
            return carry

        lax.fori_loop(0, 8, first_pass, 0)
        set_lhs(us[...])

        def second_pass(pair, carry):
            by_weight(number, LIGHT_HID, lambda light: apply_pair(pair, vs, light))
            return carry

        lax.fori_loop(0, 8, second_pass, 0)
        xs[...] = NS_A * xs[...] + NS_B * us[...] + NS_C * vs[...]
        for move in MOVES:
            send(turn, move).wait_send()
        for pair in range(8):
            for piece in range(3):
                to_core(turn, 2 * pair, piece).wait_send()
        return carry

    lax.fori_loop(0, NS, iteration, 0)

    place = blk % 4
    copies = []
    for rel, target in ((1, dims[0]), (2, dims[2]), (3, diagonal)):
        copies.append(
            pltpu.make_async_remote_copy(
                src_ref=xs.at[:, pl.ds(pl.multiple_of(target["blk"] * height, height), height)],
                dst_ref=back.at[place],
                send_sem=back_send.at[rel - 1],
                recv_sem=back_recv.at[rel - 1],
                device_id=target,
                device_id_type=MESH,
            )
        )
        copies[-1].start()
    hid_ref[place] = xs[:, my_lanes]
    inp_ref[...] = xin[:, my_half]
    for copy in copies:
        copy.wait_recv()
    for target in (dims[0], dims[2], diagonal):
        other = target["blk"] % 4
        hid_ref[other] = back[other]
    for copy in copies + spread:
        copy.wait_send()


def muon(stats, red_hid, mom_hid, red_in, mom_in, wide):
    rows = red_hid.shape[0] // 4
    height = red_hid.shape[1]
    deep, part_wide = red_in.shape
    vmem = pl.BlockSpec(memory_space=pltpu.VMEM)
    sem = pltpu.SemaphoreType.DMA
    return pl.pallas_call(
        muon_kernel,
        out_shape=(
            jax.ShapeDtypeStruct((4, rows, height), F32),
            jax.ShapeDtypeStruct((deep, part_wide), F32),
            jax.ShapeDtypeStruct(red_hid.shape, F32),
            jax.ShapeDtypeStruct(red_in.shape, F32),
            jax.ShapeDtypeStruct((8, 128), F32),
        ),
        in_specs=[vmem] * 5,
        out_specs=(vmem,) * 5,
        scratch_shapes=[
            pltpu.VMEM((2, 16, 3 * PIECE, wide), I16),
            pltpu.VMEM((8, 2 * rows, wide), BF16),
            pltpu.VMEM((8, 2 * rows, wide), BF16),
            pltpu.VMEM((8, 8, 2 * rows), F32),
            pltpu.VMEM((rows, wide), F32),
            pltpu.VMEM((rows, wide), F32),
            pltpu.VMEM((rows, wide), F32),
            pltpu.VMEM((2 * rows, wide), BF16),
            pltpu.VMEM((deep, 2 * part_wide), F32),
            pltpu.VMEM((deep, 2 * part_wide), BF16),
            pltpu.VMEM((deep, 2 * part_wide), BF16),
            pltpu.VMEM((deep, deep), F32),
            pltpu.VMEM((deep, deep), F32),
            pltpu.VMEM((4, rows, height), F32),
            pltpu.VMEM((6, 8, 128), F32),
            pltpu.VMEM((5, 8, 128), F32),
            sem((len(MOVES),)),
            sem((8, 3)),
            sem((2, 16, 3)),
            sem((3,)),
            sem((3,)),
            sem((5,)),
            sem((5,)),
            sem((7,)),
            sem((7,)),
            sem((2,)),
            sem((2,)),
        ],
        compiler_params=pltpu.CompilerParams(
            collective_id=0, has_side_effects=True, vmem_limit_bytes=60 * 1024 * 1024
        ),
    )(stats, red_hid, mom_hid, red_in, mom_in)


def plain_body(
    frames,
    labels,
    mask,
    w_input,
    w_hidden,
    w_output,
    biases,
    mom_input,
    mom_hidden,
    out_first,
    out_second,
    bias_first,
    bias_second,
    res_input,
    res_hidden,
    res_output,
):
    ncol = lax.axis_size("col")
    nblk = lax.axis_size("blk")
    col_index = lax.axis_index("col")
    hcol = w_input.shape[1]
    scol = w_output.shape[1]
    micro = frames.shape[0]
    slot_count = frames.shape[1] * micro * nblk * ncol
    bias_row = biases[0]
    b_one = bias_row[:hcol]
    b_two = bias_row[hcol : 2 * hcol]
    b_out = bias_row[2 * hcol :]
    low_input = w_input.astype(jnp.bfloat16)
    row_tags = jnp.where(mask > 0, labels, -1)
    grad_input = jnp.zeros(w_input.shape, jnp.float32)
    grad_hidden = jnp.zeros((w_hidden.shape[0] * nblk, hcol), jnp.float32)
    grad_output = jnp.zeros((w_output.shape[0] * nblk, scol), jnp.float32)
    grad_bias = jnp.zeros(bias_row.shape, jnp.float32)
    loss_local = jnp.zeros((), jnp.float32)
    for micro_step in range(micro):
        low_hidden, low_output = (
            lax.all_gather(w_hidden.astype(jnp.bfloat16), "blk", axis=0, tiled=True),
            lax.all_gather(w_output.astype(jnp.bfloat16), "blk", axis=0, tiled=True),
        )
        inputs = lax.all_gather(frames[micro_step], "col", axis=0, tiled=True)
        tags_group = lax.all_gather(row_tags[micro_step], "col", axis=0, tiled=True)
        sig_one = jax.nn.sigmoid(matmul(inputs, low_input) + b_one)
        h_one = spread_cols(sig_one.astype(jnp.bfloat16))
        sig_two = jax.nn.sigmoid(matmul(h_one, low_hidden) + b_two)
        h_two = spread_cols(sig_two.astype(jnp.bfloat16))
        logits = matmul(h_two, low_output) + b_out
        row_top = lax.pmax(jnp.max(logits, axis=1), "col")
        exponent = jnp.exp(logits - row_top[:, None])
        target_hit = jnp.arange(scol)[None, :] == (tags_group - col_index * scol)[:, None]
        row_total, picked = lax.psum(
            (jnp.sum(exponent, axis=1), jnp.sum(jnp.where(target_hit, logits, 0.0), axis=1)), "col"
        )
        live_rows = tags_group >= 0
        loss_local = loss_local + jnp.sum(
            jnp.where(live_rows, row_top + jnp.log(row_total) - picked, 0.0)
        )
        probs = exponent / row_total[:, None]
        d_logits = (
            jnp.where(live_rows[:, None], probs - target_hit.astype(jnp.float32), 0.0) / slot_count
        ).astype(jnp.bfloat16)
        grad_output = grad_output + inner_rows(h_two, d_logits)
        d_h_two = reduce_cols(outer_cols(d_logits, low_output))
        d_z_two = (d_h_two * sig_two * (1.0 - sig_two)).astype(jnp.bfloat16)
        grad_hidden = grad_hidden + inner_rows(h_one, d_z_two)
        d_h_one = reduce_cols(outer_cols(d_z_two, low_hidden))
        d_z_one = (d_h_one * sig_one * (1.0 - sig_one)).astype(jnp.bfloat16)
        grad_input = grad_input + inner_rows(inputs, d_z_one)
        grad_bias = grad_bias + jnp.concatenate(
            [
                jnp.sum(d_z_one.astype(jnp.float32), axis=0),
                jnp.sum(d_z_two.astype(jnp.float32), axis=0),
                jnp.sum(d_logits.astype(jnp.float32), axis=0),
            ]
        )
    q_input, next_res_input = squash(grad_input, res_input[0])
    q_hidden, next_res_hidden = squash(grad_hidden, res_hidden[0])
    q_output, next_res_output = squash(grad_output, res_output[0])
    red_hidden, red_output = (
        lax.psum_scatter(q_hidden, "blk", scatter_dimension=0, tiled=True),
        lax.psum_scatter(q_output, "blk", scatter_dimension=0, tiled=True),
    )
    red_input, red_bias, loss_sum = lax.psum((q_input, grad_bias, loss_local), "blk")
    share_blk = 1.0 / nblk
    grad_square = (
        share_blk * (jnp.sum(red_input * red_input) + jnp.sum(red_bias * red_bias))
        + jnp.sum(red_hidden * red_hidden)
        + jnp.sum(red_output * red_output)
    )
    clip_norm = jnp.sqrt(lax.psum(grad_square, ("blk", "col")))
    factor = jnp.minimum(1.0, CLIP / clip_norm)
    next_mom_input = 0.5 * mom_input + factor * red_input
    next_mom_hidden = 0.5 * mom_hidden + factor * red_hidden
    square_input, square_hidden = lax.psum(
        (
            share_blk * jnp.sum(next_mom_input * next_mom_input),
            jnp.sum(next_mom_hidden * next_mom_hidden),
        ),
        ("blk", "col"),
    )
    iter_input = next_mom_input / (jnp.sqrt(square_input) + 1e-07)
    iter_hidden = next_mom_hidden / (jnp.sqrt(square_hidden) + 1e-07)
    for turn_index in range(NS):
        rows_hidden = collect_rows(iter_hidden)
        gram_input, gram_hidden = lax.psum(
            (precise(iter_input, iter_input.T), precise(iter_hidden, rows_hidden.T)), "col"
        )
        image_input = precise(gram_input, iter_input)
        image_hidden = precise(gram_hidden, rows_hidden)
        iter_input = (
            NS_A * iter_input + NS_B * image_input + NS_C * precise(gram_input, image_input)
        )
        iter_hidden = (
            NS_A * iter_hidden
            + NS_B * image_hidden
            + NS_C * precise(gram_hidden, collect_rows(image_hidden))
        )
    muon_scale = LR_MUON * 0.2 * math.sqrt(hcol * ncol)
    new_input = w_input * (1.0 - LR_MUON * WD_MUON) - muon_scale * iter_input
    new_hidden = w_hidden * (1.0 - LR_MUON * WD_MUON) - muon_scale * iter_hidden
    new_output, next_out_first, next_out_second = adam_step(
        w_output, factor * red_output, out_first, out_second
    )
    new_biases, next_bias_first, next_bias_second = adam_step(
        biases, factor * red_bias[None, :], bias_first, bias_second
    )
    return (
        loss_sum,
        clip_norm,
        new_input,
        new_hidden,
        new_output,
        new_biases,
        next_mom_input,
        next_mom_hidden,
        next_out_first,
        next_out_second,
        next_bias_first,
        next_bias_second,
        next_res_input[None],
        next_res_hidden[None],
        next_res_output[None],
    )


def fast_body(
    frames,
    labels,
    mask,
    w_input,
    w_hidden,
    w_output,
    biases,
    mom_input,
    mom_hidden,
    out_first,
    out_second,
    bias_first,
    bias_second,
    res_input,
    res_hidden,
    res_output,
):
    ncol = lax.axis_size("col")
    nblk = lax.axis_size("blk")
    col_index = lax.axis_index("col")
    blk_index = lax.axis_index("blk")
    hcol = w_input.shape[1]
    scol = w_output.shape[1]
    micro = frames.shape[0]
    slot_count = frames.shape[1] * micro * nblk * ncol
    bias_row = biases[0]
    deep = w_input.shape[0]
    padded = 512
    rows_out = OUT_GROUPS * OUT_ROWS
    own_tags = jnp.where(mask > 0, labels, -1).reshape(1, -1)
    layer_biases = jnp.pad(bias_row[: 2 * hcol].reshape(2, hcol), ((0, 6), (0, 0)))
    blocks = -(-rows_out // 128)
    out_biases = jnp.pad(bias_row[2 * hcol :], (0, blocks * 128 - scol)).reshape(blocks, 128)
    inputs, h_one, h_two, slope_one, slope_two, low_hidden, low_output, d_logits, bias_sums, losses = (
        forward_pass(
            frames.reshape(-1, deep),
            jnp.broadcast_to(own_tags, (8, own_tags.shape[1])),
            w_input,
            w_hidden,
            w_output.T,
            layer_biases,
            out_biases,
            slot_count,
        )
    )
    loss_local = jnp.sum(losses)
    partial = inner_rows(d_logits, low_output)
    vec = jnp.concatenate([jnp.zeros((2 * hcol,), F32), bias_sums.reshape(-1)[:scol], loss_local[None]])
    vec = jnp.pad(vec, (0, 4096 - vec.shape[0])).reshape(32, 128)
    next_out, next_hid, next_in, red_out, red_hid, red_in, vec_sum, stats = reduce_grads(
        d_logits,
        h_two,
        h_one,
        inputs,
        partial,
        slope_two,
        slope_one,
        low_hidden,
        jnp.pad(res_output[0], ((0, 0), (0, rows_out - scol))).T,
        res_hidden[0].T,
        jnp.pad(res_input[0], ((0, padded - deep), (0, 0))).T,
        vec,
        scol,
        deep,
    )
    next_res_output = next_out.transpose(1, 2, 0)
    next_res_hidden = next_hid.T
    next_res_input = next_in[:, :deep].T
    red_output = red_out[:scol].T
    vec_sum = vec_sum.reshape(-1)
    red_bias = vec_sum[: bias_row.shape[0]]
    loss_sum = vec_sum[bias_row.shape[0]]
    stats = stats.at[1, 0].set(jnp.sum(red_bias * red_bias) / nblk)
    done_hidden, done_input, mom_hid_next, mom_in_next, norms = muon(
        stats,
        red_hid,
        mom_hidden.T,
        red_in.T,
        jnp.pad(mom_input, ((0, padded - deep), (0, 0))),
        hcol * ncol,
    )
    clip_norm = norms[0, 0]
    factor = norms[4, 0]
    next_mom_hidden = mom_hid_next.T
    next_mom_input = mom_in_next[:deep]
    done_hidden = done_hidden.reshape(hcol, w_hidden.shape[0]).T
    muon_scale = LR_MUON * 0.2 * math.sqrt(hcol * ncol)
    new_input = w_input * (1.0 - LR_MUON * WD_MUON) - muon_scale * done_input[:deep]
    new_hidden = w_hidden * (1.0 - LR_MUON * WD_MUON) - muon_scale * done_hidden
    new_output, next_out_first, next_out_second = adam_step(
        w_output, factor * red_output, out_first, out_second
    )
    new_biases, next_bias_first, next_bias_second = adam_step(
        biases, factor * red_bias[None, :], bias_first, bias_second
    )
    return (
        loss_sum,
        clip_norm,
        new_input,
        new_hidden,
        new_output,
        new_biases,
        next_mom_input,
        next_mom_hidden,
        next_out_first,
        next_out_second,
        next_bias_first,
        next_bias_second,
        next_res_input[None],
        next_res_hidden[None],
        next_res_output,
    )


def solution(mesh):
    in_specs = (
        P(None, ("blk", "col"), None),
        P(None, ("blk", "col")),
        P(None, ("blk", "col")),
        P(None, "col"),
        P("blk", "col"),
        P("blk", "col"),
        P("col", None),
        P(None, "col"),
        P("blk", "col"),
        P("blk", "col"),
        P("blk", "col"),
        P("col", None),
        P("col", None),
        P("blk", None, "col"),
        P("blk", None, "col"),
        P("blk", None, "col"),
    )
    out_specs = (
        P(),
        P(),
        P(None, "col"),
        P("blk", "col"),
        P("blk", "col"),
        P("col", None),
        P(None, "col"),
        P("blk", "col"),
        P("blk", "col"),
        P("blk", "col"),
        P("col", None),
        P("col", None),
        P("blk", None, "col"),
        P("blk", None, "col"),
        P("blk", None, "col"),
    )
    cubes = mesh.shape["blk"] == 8 and mesh.shape["col"] == 4
    body = fast_body if cubes else plain_body
    return jax.shard_map(body, mesh=mesh, in_specs=in_specs, out_specs=out_specs, check_vma=False)
```

```python
import functools
import math

import jax
import jax.numpy as jnp
from jax import lax
from jax.experimental import pallas as pl
from jax.experimental.pallas import tpu as pltpu
from jax.sharding import PartitionSpec as P

NS = 5
STEP = 5


NS_A = 3.4445
NS_B = -4.775
NS_C = 2.0315
CLIP = 0.002
LR_MUON = 0.1
WD_MUON = 0.01
LR_ADAM = 0.03
WD_ADAM = 0.1

MESH = pl.DeviceIdType.MESH
F32 = jnp.float32
BF16 = jnp.bfloat16
I16 = jnp.int16
LN2 = math.log(2.0)
TOP_CODE = 32700.0
LEVELS = 64.0


def matmul(left_side, right_side):
    return jnp.dot(left_side, right_side, preferred_element_type=jnp.float32)


def inner_rows(left_side, right_side):
    return lax.dot_general(
        left_side, right_side, (((0,), (0,)), ((), ())), preferred_element_type=jnp.float32
    )


def outer_cols(left_side, right_side):
    return lax.dot_general(
        left_side, right_side, (((1,), (1,)), ((), ())), preferred_element_type=jnp.float32
    )


def precise(left_side, right_side):
    return jnp.dot(
        left_side, right_side, precision=lax.Precision.HIGHEST, preferred_element_type=jnp.float32
    )


def spread_cols(values):
    return lax.all_gather(values, "col", axis=1, tiled=True)


def reduce_cols(values):
    return lax.psum_scatter(values, "col", scatter_dimension=1, tiled=True)


def collect_rows(values):
    return lax.all_gather(values, "blk", axis=0, tiled=True)


def squash(gradient, resid):
    value = gradient + resid.astype(jnp.float32)
    scale = jnp.mean(jnp.abs(value), axis=0, keepdims=True) + 1e-12
    signed = scale * jnp.tanh(2.0 * value / scale)
    return (signed, value - signed)


def adam_step(weight, gradient, first, second):
    first = 0.5 * first + 0.5 * gradient
    second = 0.95 * second + 0.05 * gradient * gradient
    update = first / (1.0 - 0.5**STEP) / (jnp.sqrt(second / (1.0 - 0.95**STEP)) + 1e-08)
    return (weight - LR_ADAM * (update + WD_ADAM * weight), first, second)


def halves(values):
    top = values.astype(BF16)
    return top, (values - top.astype(F32)).astype(BF16)


def dot_nn(left_side, right_side):
    return lax.dot_general(
        left_side, right_side, (((1,), (0,)), ((), ())), preferred_element_type=F32
    )


def dot_nt(left_side, right_side):
    return lax.dot_general(
        left_side, right_side, (((1,), (1,)), ((), ())), preferred_element_type=F32
    )


RING = 8
STEPS = RING - 1
OUT_ROWS = 592
OUT_GROUPS = 4
BLOCKS = (304, 288)
HID_ROWS = 512
HID_GROUP = 4
IN_GROUP = 5
HID_WAVE = 4
IN_WAVE = 6


def ring_place(blk):
    odd = blk % 2
    return (blk // 2) * (1 - odd) + (7 - blk // 2) * odd


def ring_blk(place):
    back = place // 4
    return 2 * place * (1 - back) + (15 - 2 * place) * back


def scale_code(size):
    return jnp.ceil(jnp.log(jnp.maximum(size, 1e-30)) * (LEVELS / LN2))


def code_scale(code):
    return jnp.exp(code * (LN2 / LEVELS))


def to_codes(values):
    return jnp.round(values).astype(jnp.int32).astype(I16)


def from_codes(codes):
    return codes.astype(jnp.int32).astype(F32)


def reduce_kernel(
    deep,
    dl_ref,
    h_two_ref,
    h_one_ref,
    x_ref,
    part_ref,
    slope_two_ref,
    slope_one_ref,
    w_hid_ref,
    res_out_ref,
    res_hid_ref,
    res_in_ref,
    res_tail_ref,
    vec_ref,
    next_out_ref,
    next_hid_ref,
    next_in_ref,
    red_out_ref,
    red_hid_ref,
    red_in_ref,
    vec_sum_ref,
    stats_ref,
    grad,
    stage,
    res_buf,
    dl_buf,
    h_buf,
    slope_buf,
    marks,
    cols,
    keep_sums,
    dz,
    dz_two,
    dz_one,
    core_out,
    core_got,
    far_out,
    far_got,
    own_out,
    got_out,
    own_hid,
    got_hid,
    own_in,
    got_in,
    share_in,
    sizes,
    shares,
    vec,
    vecs,
    res_sems,
    dl_sems,
    load_sems,
    stage_sems,
    slope_sems,
    core_send,
    core_recv,
    far_send,
    far_recv,
    out_send,
    out_recv,
    hid_send,
    hid_recv,
    in_send,
    in_recv,
    share_send,
    share_recv,
    vec_send,
    vec_recv,
    size_send,
    size_recv,
):
    blk = lax.axis_index("blk")
    col = lax.axis_index("col")
    here = ring_place(blk)
    total_rows = next_out_ref.shape[0]
    core, high = col % 2, col // 2
    cores = {"col": col + 1 - 2 * core}
    across = {"col": (col + 2) % 4}
    barrier = pltpu.get_barrier_semaphore()
    for target in (cores, across, *({"blk": (blk + away) % RING} for away in range(1, RING))):
        pl.semaphore_signal(barrier, inc=1, device_id=target, device_id_type=MESH)

    starts = [sum(BLOCKS[:part]) for part in range(len(BLOCKS))]

    def res_copy(group, part, rows=None):
        rows = rows or BLOCKS[part]
        return pltpu.make_async_copy(
            res_out_ref.at[pl.ds(group * OUT_ROWS + starts[part], rows), :],
            res_buf.at[part, pl.ds(0, rows), :],
            res_sems.at[part],
        )

    def dl_copy(group, part):
        rows = BLOCKS[part]
        return pltpu.make_async_copy(
            dl_ref.at[pl.ds(group * OUT_ROWS + starts[part], rows), :],
            dl_buf.at[part, pl.ds(0, rows), :],
            dl_sems.at[part],
        )

    def hid_res_copy(part):
        return pltpu.make_async_copy(
            res_hid_ref.at[pl.ds(part * 256, 256), :],
            res_buf.at[part, pl.ds(0, 256), :],
            res_sems.at[part],
        )

    def hid_next_copy(part):
        return pltpu.make_async_copy(
            grad.at[pl.ds(0, 256), :], next_hid_ref.at[pl.ds(part * 256, 256), :], load_sems.at[1]
        )

    def load(src, dst):
        return pltpu.make_async_copy(src, dst, load_sems.at[0])

    def stage_copy(group, part, rows):
        return pltpu.make_async_copy(
            stage.at[pl.ds(0, rows)],
            next_out_ref.at[pl.ds(group * OUT_ROWS + starts[part], rows)],
            stage_sems.at[0],
        )

    last_rows = total_rows - (OUT_GROUPS - 1) * OUT_ROWS - starts[-1]
    whole_rows = last_rows // 16 * 16

    def stage_start(group, part):
        if part < len(BLOCKS) - 1:
            stage_copy(group, part, BLOCKS[part]).start()
        else:

            @pl.when(group < OUT_GROUPS - 1)
            def _():
                stage_copy(group, part, BLOCKS[part]).start()

            @pl.when(group == OUT_GROUPS - 1)
            def _():
                stage_copy(group, part, last_rows).start()

    for part in range(2):
        res_copy(0, part).start()
        dl_copy(0, part).start()
    load(h_two_ref, h_buf).start()
    marks[...] = jnp.zeros_like(marks)
    stats_ref[...] = jnp.zeros_like(stats_ref)
    vec[...] = vec_ref[...]
    pl.semaphore_wait(barrier, RING + 1)

    CHUNK = 256
    units = slope_buf.shape[2]

    def slope_copy(layer, block):
        rows = pl.ds(pl.multiple_of(block * CHUNK, CHUNK), CHUNK)
        src = (slope_two_ref, slope_one_ref)[layer]
        return pltpu.make_async_copy(src.at[rows, :], slope_buf.at[block % 2], slope_sems.at[block % 2])

    def core_move(layer, block):
        return pltpu.make_async_remote_copy(
            src_ref=core_out.at[block % 2],
            dst_ref=core_got.at[layer, block],
            send_sem=core_send.at[block % 2],
            recv_sem=core_recv.at[layer, block],
            device_id=cores,
            device_id_type=MESH,
        )

    def far_move(layer, block):
        return pltpu.make_async_remote_copy(
            src_ref=far_out.at[block % 2],
            dst_ref=far_got.at[layer, block],
            send_sem=far_send.at[block % 2],
            recv_sem=far_recv.at[layer, block],
            device_id=across,
            device_id_type=MESH,
        )

    def lanes_of(number):
        return pl.ds(pl.multiple_of(number * units, units), units)

    def rows_at(number):
        return pl.ds(pl.multiple_of(number * 16, 16), 16)

    def free(copy, layer, block):
        @pl.when((layer > 0) | (block >= 2))
        def _():
            copy.wait_send()

    def lane_codes(first):
        return jnp.transpose(marks[first : first + 128, :])[0:1, :]

    def set_factors():
        top = jnp.max(cols[0, 0:CHUNK, :], axis=1, keepdims=True)
        code = scale_code(top)
        marks[0:CHUNK, :] = jnp.broadcast_to(code, (CHUNK, 128))
        cols[1, 0:CHUNK, :] = jnp.broadcast_to(TOP_CODE / code_scale(code), (CHUNK, 128))

    def largest(values):
        return functools.reduce(
            jnp.maximum,
            [
                jnp.abs(value[:, lane : lane + 128])
                for value in values
                for lane in range(0, value.shape[1], 128)
            ],
        )

    def scaled(values, factor):
        return jnp.concatenate(
            [values[:, lane : lane + 128] * factor for lane in range(0, values.shape[1], 128)], axis=1
        )

    def put_scale(out):
        codes = jnp.concatenate(
            [lane_codes(0), lane_codes(128), jnp.zeros((14, 128), F32)], axis=0
        )
        out[CHUNK : CHUNK + 16, 0:128] = codes.astype(jnp.int32).astype(I16)

    def read_scale(got):
        step = code_scale(from_codes(got[CHUNK : CHUNK + 16, 0:128])) * (1.0 / TOP_CODE)
        step = jnp.transpose(jnp.concatenate([step, jnp.zeros((112, 128), F32)], axis=0))
        for up in range(2):
            marks[CHUNK + up * 128 : CHUNK + (up + 1) * 128, :] = jnp.broadcast_to(
                step[:, up : up + 1], (128, 128)
            )

    def step_at(number):
        return marks[pl.ds(pl.multiple_of(CHUNK + number * 16, 16), 16), :]

    def split(layer, block):
        free(core_move(layer, block), layer, block)

        def measure(number, carry):
            rows = rows_at(number)
            cols[0, rows, :] = largest(
                [grad[rows, lanes_of(2 * half + 1 - core)] for half in range(2)]
            )
            return carry

        lax.fori_loop(0, CHUNK // 16, measure, 0)
        set_factors()

        def write(number, carry):
            rows = rows_at(number)
            factor = cols[1, rows, :]
            for half in range(2):
                there = slice(half * units, (half + 1) * units)
                core_out[block % 2, rows, there] = to_codes(
                    scaled(grad[rows, lanes_of(2 * half + 1 - core)], factor)
                )
                keep_sums[block, rows, there] = grad[rows, lanes_of(2 * half + core)]
            return carry

        lax.fori_loop(0, CHUNK // 16, write, 0)
        put_scale(core_out.at[block % 2])
        core_move(layer, block).start()

    def cross(layer, block):
        core_move(layer, block).wait_recv()
        free(far_move(layer, block), layer, block)
        got = core_got.at[layer, block]
        read_scale(got)

        def add(number, carry):
            rows = rows_at(number)
            near, away = lanes_of(high), lanes_of(1 - high)
            step = step_at(number)
            keep_sums[block, rows, near] += scaled(from_codes(got[rows, near]), step)
            value = keep_sums[block, rows, away] + scaled(from_codes(got[rows, away]), step)
            keep_sums[block, rows, away] = value
            cols[0, rows, :] = largest([value])
            return carry

        lax.fori_loop(0, CHUNK // 16, add, 0)
        set_factors()

        def write(number, carry):
            rows = rows_at(number)
            far_out[block % 2, rows, :] = to_codes(
                scaled(keep_sums[block, rows, lanes_of(1 - high)], cols[1, rows, :])
            )
            return carry

        lax.fori_loop(0, CHUNK // 16, write, 0)
        put_scale(far_out.at[block % 2])
        far_move(layer, block).start()

    def finish(layer, block):
        far_move(layer, block).wait_recv()
        slope_copy(layer, block).wait()
        got = far_got.at[layer, block]
        read_scale(got)

        def one(number, total):
            rows = rows_at(number)
            value = keep_sums[block, rows, lanes_of(high)] + scaled(
                from_codes(got[rows, :]), step_at(number)
            )
            value = (value * slope_buf[block % 2, rows, :]).astype(BF16)
            dz[rows, :] = value
            return total + value.astype(F32)

        total = lax.fori_loop(0, CHUNK // 16, one, jnp.zeros((16, units), F32))
        if layer == 0:

            @pl.when(block < 2)
            def _():
                slope_copy(0, block + 2).start()

            @pl.when(block >= 2)
            def _():
                slope_copy(1, block - 2).start()

        else:

            @pl.when(block < 2)
            def _():
                slope_copy(1, block + 2).start()

        total = jnp.sum(total, axis=0, keepdims=True)
        for number in range(units // 128):
            row = 4 * (1 - layer) + number
            vec[row : row + 1, :] += total[:, number * 128 : (number + 1) * 128]
        flipped = (dz_two, dz_one)[layer]
        for up in range(CHUNK // 128):
            there = pl.ds(pl.multiple_of(block * CHUNK + up * 128, 128), 128)
            for number in range(units // 128):
                tile = dz[up * 128 : (up + 1) * 128, number * 128 : (number + 1) * 128]
                flipped[number * 128 : (number + 1) * 128, there] = jnp.transpose(
                    tile.astype(F32)
                ).astype(BF16)

    def blocks(first, last, work):
        def one(block, carry):
            work(block)
            return carry

        lax.fori_loop(first, last, one, 0)

    def start_block(block):
        rows = pl.ds(pl.multiple_of(block * CHUNK, CHUNK), CHUNK)
        copy = pltpu.make_async_copy(part_ref.at[rows, :], grad.at[pl.ds(0, CHUNK), :], load_sems.at[1])
        copy.start()
        copy.wait()
        split(0, block)

    def turn_block(block):
        finish(0, block)
        for lane in range(0, grad.shape[1], 512):
            grad[0:CHUNK, lane : lane + 512] = dot_nt(dz[...], w_hid_ref[lane : lane + 512, :])
        split(1, block)

    core_out[:, CHUNK:, :] = jnp.zeros((2, 16, 2 * units), I16)
    far_out[:, CHUNK:, :] = jnp.zeros((2, 16, units), I16)
    slope_copy(0, 0).start()
    slope_copy(0, 1).start()
    blocks(0, 4, start_block)
    blocks(0, 4, lambda block: cross(0, block))

    def vec_copy(away):
        return pltpu.make_async_remote_copy(
            src_ref=vec,
            dst_ref=vecs.at[blk],
            send_sem=vec_send.at[away - 1],
            recv_sem=vec_recv.at[away - 1],
            device_id={"blk": (blk + away) % RING},
            device_id_type=MESH,
        )

    def set_rows(count, first_own, size):
        size = jnp.broadcast_to(size, (count, 128))
        marks[first_own : first_own + count, :] = size
        cols[0, 0:count, :] = size
        cols[1, 0:count, :] = 2.0 / size

    def tell_sizes(group):
        for away in range(1, RING):
            size_copy(group, away).start()

    def size_copy(group, away):
        return pltpu.make_async_remote_copy(
            src_ref=sizes.at[group, here],
            dst_ref=sizes.at[group, here],
            send_sem=size_send.at[group, away - 1],
            recv_sem=size_recv.at[group, away - 1],
            device_id={"blk": ring_blk((here + away) % RING)},
            device_id_type=MESH,
        )

    def set_sizes(rows, group):
        parts = [lane_codes(first) for first in range(0, rows, 128)]
        parts.append(jnp.zeros((8 - len(parts), 128), F32))
        sizes[group, here] = jnp.concatenate(parts, axis=0)
        tell_sizes(group)

    def make_shares(group, row_of):
        for away in range(1, RING):
            size_copy(group, away).wait_recv()
        for way in range(2):
            tiles = []
            for step in range(STEPS):
                mine = row_of(here, step, way)
                came = mine * 0.0
                for back in range(step + 1):
                    came = came + row_of((here - 1 - back + (2 + 2 * back) * way + RING) % RING, step, way)
                if step < STEPS - 1:
                    whole = 1.0 / jnp.maximum(came + mine, 1e-30)
                else:
                    whole = 1.0 / TOP_CODE
                tiles += [came * whole, mine * whole]
            tiles.append(jnp.zeros((16, 128), F32))
            shares[group, way] = jnp.transpose(jnp.concatenate(tiles, axis=0))

    def squash_rows(count, own, first_own, read_res, write_next):
        wide = grad.shape[1]

        def add(number, carry):
            row = pl.multiple_of(number * 16, 16)
            value = grad[pl.ds(row, 16), :] + read_res(row)
            grad[pl.ds(row, 16), :] = value
            value = jnp.abs(value)
            cols[0, pl.ds(row, 16), :] = functools.reduce(
                jnp.add, [value[:, lane : lane + 128] for lane in range(0, wide, 128)]
            )
            return carry

        lax.fori_loop(0, count // 16, add, 0)
        set_rows(
            count,
            first_own,
            jnp.sum(cols[0, 0:count, :], axis=1, keepdims=True) * (1.0 / wide) + 1e-12,
        )

        def some(number, carry):
            row = pl.multiple_of(number * 16, 16)
            size = cols[0, pl.ds(row, 16), :]
            steep = cols[1, pl.ds(row, 16), :]
            for lane in range(0, wide, 128):
                piece = grad[pl.ds(row, 16), lane : lane + 128]
                curve = jnp.tanh(piece * steep)
                number_of = lane // 256
                chunk = number_of // 2 if number_of % 2 == 0 else 7 - number_of // 2
                own[2 * chunk + lane // 128 % 2, pl.ds(first_own + row, 16), :] = to_codes(
                    curve * TOP_CODE
                )
                write_next(row, lane, piece - size * curve)
            return carry

        lax.fori_loop(0, count // 16, some, 0)

    def out_group(group):
        for part, rows in enumerate(BLOCKS):
            dl_copy(group, part).wait()
            if part == 0:

                @pl.when(group == 0)
                def _():
                    load(h_two_ref, h_buf).wait()

            for lane in range(0, grad.shape[1], 512):
                grad[0:rows, lane : lane + 512] = dot_nn(
                    dl_buf[part, 0:rows, :], h_buf[:, lane : lane + 512]
                )
            if part == 0:
                res_copy(group, part).wait()
            else:

                @pl.when(group < OUT_GROUPS - 1)
                def _():
                    res_copy(group, 1).wait()

                @pl.when(group == OUT_GROUPS - 1)
                def _():
                    res_copy(group, 1, whole_rows).wait()
                    res_buf[1, whole_rows : whole_rows + 16, :] = res_tail_ref[...]
                    res_buf[1, whole_rows + 16 : BLOCKS[1], :] = jnp.zeros(
                        (BLOCKS[1] - whole_rows - 16, res_buf.shape[2]), BF16
                    )

            if part == 0:

                @pl.when(group > 0)
                def _():
                    stage_copy(group - 1, len(BLOCKS) - 1, BLOCKS[-1]).wait()

            else:
                stage_copy(group, part - 1, BLOCKS[part - 1]).wait()

            def write_next(row, lane, values):
                stage[pl.ds(row, 16), 0, lane : lane + 128] = values

            squash_rows(
                rows,
                own_out.at[group],
                starts[part],
                lambda row, part=part: res_buf[part, pl.ds(row, 16), :].astype(F32),
                write_next,
            )
            stage_start(group, part)

            @pl.when(group < OUT_GROUPS - 1)
            def _(part=part):
                if part == 0:
                    res_copy(group + 1, 0).start()
                else:

                    @pl.when(group < OUT_GROUPS - 2)
                    def _():
                        res_copy(group + 1, 1).start()

                    @pl.when(group == OUT_GROUPS - 2)
                    def _():
                        res_copy(group + 1, 1, whole_rows).start()

                dl_copy(group + 1, part).start()

            @pl.when(group == OUT_GROUPS - 1)
            def _(part=part):
                hid_res_copy(part).start()
                if part == len(BLOCKS) - 1:
                    load(h_one_ref, h_buf).start()

        set_sizes(OUT_ROWS, group)

    def hid_group():
        load(h_one_ref, h_buf).wait()
        for part in range(2):
            first = part * 256
            if part:
                hid_next_copy(part - 1).wait()
            for lane in range(0, grad.shape[1], 512):
                grad[0:256, lane : lane + 512] = dot_nn(
                    dz_two[first : first + 256, :], h_buf[:, lane : lane + 512]
                )
            hid_res_copy(part).wait()

            def write_next(row, lane, values):
                grad[pl.ds(row, 16), lane : lane + 128] = values

            squash_rows(
                256,
                own_hid,
                first,
                lambda row, part=part: res_buf[part, pl.ds(row, 16), :].astype(F32),
                write_next,
            )
            hid_next_copy(part).start()
        load(x_ref, h_buf.at[:, pl.ds(0, x_ref.shape[1])]).start()
        set_sizes(HID_ROWS, HID_GROUP)
        hid_next_copy(1).wait()

    def in_group():
        wide = x_ref.shape[1]
        load(x_ref, h_buf.at[:, pl.ds(0, wide)]).wait()
        for first in range(0, HID_ROWS, 256):
            grad[0:256, 0:wide] = dot_nn(dz_one[first : first + 256, :], h_buf[:, 0:wide])

            def add(number, carry, first=first):
                row = pl.multiple_of(number * 16, 16)
                place = pl.multiple_of(first + row, 16)
                value = grad[pl.ds(row, 16), 0:wide] + res_in_ref[pl.ds(place, 16), :].astype(F32)
                grad[pl.ds(row, 16), 0:wide] = value
                value = jnp.abs(value)
                cols[0, pl.ds(row, 16), :] = functools.reduce(
                    jnp.add, [value[:, lane : lane + 128] for lane in range(0, wide, 128)]
                )
                return carry

            lax.fori_loop(0, 16, add, 0)
            set_rows(
                256,
                first,
                jnp.sum(cols[0, 0:256, :], axis=1, keepdims=True) * (1.0 / deep) + 1e-12,
            )

            def some(number, carry, first=first):
                row = pl.multiple_of(number * 16, 16)
                place = pl.multiple_of(first + row, 16)
                size = cols[0, pl.ds(row, 16), :]
                steep = cols[1, pl.ds(row, 16), :]
                chunk = first // 64 + number // 4
                inside = pl.multiple_of(number % 4 * 16, 16)
                for lane in range(0, wide, 128):
                    piece = grad[pl.ds(row, 16), lane : lane + 128]
                    curve = jnp.tanh(piece * steep)
                    next_in_ref[pl.ds(place, 16), lane : lane + 128] = piece - size * curve
                    own_in[
                        2 * chunk + lane // 256, pl.ds(inside, 16), lane % 256 : lane % 256 + 128
                    ] = to_codes(curve * TOP_CODE)
                return carry

            lax.fori_loop(0, 16, some, 0)
        sizes[IN_GROUP, here] = jnp.concatenate(
            [lane_codes(64 * chunk) for chunk in range(RING)], axis=0
        )
        tell_sizes(IN_GROUP)

    def towards(way):
        return {"blk": ring_blk((here + 1 - 2 * way + RING) % RING)}

    def move(src, got, step, way, send_sem, recv_sem):
        return pltpu.make_async_remote_copy(
            src_ref=src,
            dst_ref=got.at[way, step],
            send_sem=send_sem.at[way, step],
            recv_sem=recv_sem.at[way, step],
            device_id=towards(way),
            device_id_type=MESH,
        )

    def first_moves(own, got, send_sem, recv_sem):
        for way in range(2):
            chunk = (here - 1 + 2 * way + RING) % RING
            move(own.at[2 * chunk + way], got, 0, way, send_sem, recv_sem).start()

    def hop(rows, own, got, group, step, send_sem, recv_sem, keep):
        for way in range(2):
            move(got.at[way, step], got, step, way, send_sem, recv_sem).wait_recv()

        def add(way, result):
            message = got.at[way, step]
            ahead = here - 2 - step + way * (4 + 2 * step) + 2 * RING
            mine = own.at[2 * (ahead % RING) + way]
            share = pltpu.roll(shares[group, way], (128 - 16 * step) % 128, 1)
            for number, first in enumerate(range(0, rows, 128)):
                count = min(128, rows - first)
                there = slice(first, first + count)
                result(
                    first,
                    count,
                    from_codes(message[there, :]) * share[0:count, number : number + 1]
                    + from_codes(mine[there, :]) * share[0:count, 8 + number : 9 + number],
                )

        @pl.when(step < STEPS - 1)
        def _():
            for way in range(2):

                def write(first, count, value, way=way):
                    got[way, step, first : first + count, :] = to_codes(value)

                add(way, write)
            for way in range(2):
                move(got.at[way, step], got, step + 1, way, send_sem, recv_sem).start()

        @pl.when(step == STEPS - 1)
        def _():
            for way in range(2):

                def finish_rows(first, count, value, way=way):
                    keep(way, first, count, value)
                    square = jnp.sum(value * value, axis=0, keepdims=True)
                    for lane in range(0, value.shape[1], 128):
                        stats_ref[0:1, :] += square[:, lane : lane + 128]

                add(way, finish_rows)

    def out_hop(group, step):
        def keep(way, first, count, value):
            row = pl.multiple_of(group * OUT_ROWS + first, 16)
            red_out_ref[pl.ds(row, count), way * 128 : (way + 1) * 128] = value

        hop(
            OUT_ROWS,
            own_out.at[group],
            got_out.at[group],
            group,
            step,
            out_send.at[group],
            out_recv.at[group],
            keep,
        )

    def hid_hop(step):
        def keep(way, first, count, value):
            red_hid_ref[first : first + count, way * 128 : (way + 1) * 128] = value

        hop(HID_ROWS, own_hid, got_hid, HID_GROUP, step, hid_send, hid_recv, keep)

    def share_move(step, way):
        place = (here - step + 2 * step * way + 2 * RING) % RING
        return pltpu.make_async_remote_copy(
            src_ref=share_in.at[way, place],
            dst_ref=share_in.at[way, place],
            send_sem=share_send.at[way, step],
            recv_sem=share_recv.at[way, step],
            device_id=towards(way),
            device_id_type=MESH,
        )

    def in_hop(step):
        def keep(way, first, count, value):
            share_in[way, here] = value

        hop(64, own_in, got_in, IN_GROUP, step, in_send, in_recv, keep)

        @pl.when(step == STEPS - 1)
        def _():
            for way in range(2):
                share_move(0, way).start()

    def share_hop(step):
        for way in range(2):
            share_move(step, way).wait_recv()

        @pl.when(step < STEPS - 1)
        def _():
            for way in range(2):
                share_move(step + 1, way).start()

    def in_step(index):
        @pl.when((index >= 0) & (index < STEPS))
        def _():
            in_hop(index)

        @pl.when((index >= STEPS) & (index < 2 * STEPS))
        def _():
            share_hop(index - STEPS)

    def chunk_row(place, step, way):
        chunk = (here - 2 - step + way * (4 + 2 * step) + 2 * RING) % RING
        line = sizes[IN_GROUP, place, pl.ds(chunk, 1), :]
        return jnp.broadcast_to(line, (8, 128))

    def wave(number, carry):
        @pl.when(number < OUT_GROUPS)
        def _():
            out_group(number)
            first_moves(own_out.at[number], got_out.at[number], out_send.at[number], out_recv.at[number])

        @pl.when(number == HID_WAVE)
        def _():
            hid_group()
            first_moves(own_hid, got_hid, hid_send, hid_recv)

        @pl.when((number >= 1) & (number <= OUT_GROUPS))
        def _():
            group = number - 1
            make_shares(group, lambda place, step, way: sizes[group, place])

        @pl.when(number == HID_WAVE + 1)
        def _():
            make_shares(HID_GROUP, lambda place, step, way: sizes[HID_GROUP, place])

        @pl.when(number == IN_WAVE + 1)
        def _():
            make_shares(IN_GROUP, chunk_row)

        index = 2 * (number - IN_WAVE - 1)
        in_step(index)

        @pl.when((number > HID_WAVE) & (number <= HID_WAVE + STEPS))
        def _():
            hid_hop(number - HID_WAVE - 1)

        def outs(group, carry):
            step = number - 1 - group

            @pl.when((step >= 0) & (step < STEPS))
            def _():
                out_hop(group, step)

            return carry

        lax.fori_loop(0, OUT_GROUPS, outs, 0)

        @pl.when((number == 1) | (number == 2))
        def _():
            blocks(2 * number - 2, 2 * number, turn_block)

        @pl.when(number == 3)
        def _():
            blocks(0, 4, lambda block: cross(1, block))

        @pl.when(number == IN_WAVE)
        def _():
            blocks(0, 4, lambda block: finish(1, block))
            in_group()
            first_moves(own_in, got_in, in_send, in_recv)
            for away in range(1, RING):
                vec_copy(away).start()

        in_step(index + 1)
        return carry

    lax.fori_loop(0, IN_WAVE + 1 + STEPS, wave, 0)

    for place in range(RING):
        for way in range(2):
            red_in_ref[place * 64 : (place + 1) * 64, way * 256 : (way + 1) * 256] = share_in[
                way, place
            ]
    for away in range(1, RING):
        vec_copy(away).wait_recv()
    vecs[blk] = vec[...]
    total = vecs[0]
    for number in range(1, RING):
        total = total + vecs[number]
    vec_sum_ref[...] = total
    for away in range(1, RING):
        vec_copy(away).wait_send()
        for group in range(OUT_GROUPS + 2):
            size_copy(group, away).wait_send()
    for slot in range(2):
        core_move(1, 2 + slot).wait_send()
        far_move(1, 2 + slot).wait_send()
    stage_copy(OUT_GROUPS - 1, len(BLOCKS) - 1, last_rows).wait()
    for way in range(2):
        for step in range(STEPS):
            for group in range(OUT_GROUPS):
                move(
                    got_out.at[group, way, step],
                    got_out.at[group],
                    step,
                    way,
                    out_send.at[group],
                    out_recv.at[group],
                ).wait_send()
            move(got_hid.at[way, step], got_hid, step, way, hid_send, hid_recv).wait_send()
            move(got_in.at[way, step], got_in, step, way, in_send, in_recv).wait_send()
            share_move(step, way).wait_send()


def reduce_grads(
    dl, h_two, h_one, x, part, slope_two, slope_one, w_hid, res_out, res_hid, res_in, res_tail, vec, senones, deep
):
    frames, wide = h_two.shape
    in_wide = x.shape[1]
    units = w_hid.shape[1]
    vmem = pl.BlockSpec(memory_space=pltpu.VMEM)
    hbm = pl.BlockSpec(memory_space=pl.ANY)
    message = OUT_ROWS
    hid_message = HID_ROWS
    in_message = 64
    sem = pltpu.SemaphoreType.DMA
    return pl.pallas_call(
        functools.partial(reduce_kernel, deep),
        out_shape=(
            jax.ShapeDtypeStruct((senones, 1, wide), F32),
            jax.ShapeDtypeStruct((HID_ROWS, wide), F32),
            jax.ShapeDtypeStruct((HID_ROWS, in_wide), F32),
            jax.ShapeDtypeStruct((OUT_GROUPS * OUT_ROWS, 256), F32),
            jax.ShapeDtypeStruct((HID_ROWS, 256), F32),
            jax.ShapeDtypeStruct((HID_ROWS, in_wide), F32),
            jax.ShapeDtypeStruct(vec.shape, F32),
            jax.ShapeDtypeStruct((8, 128), F32),
        ),
        in_specs=[hbm] * 7 + [vmem] + [hbm] * 2 + [vmem] * 3,
        out_specs=(hbm, hbm) + (vmem,) * 6,
        scratch_shapes=[
            pltpu.VMEM((BLOCKS[0], wide), F32),
            pltpu.VMEM((BLOCKS[0], 1, wide), F32),
            pltpu.VMEM((2, BLOCKS[0], wide), BF16),
            pltpu.VMEM((2, BLOCKS[0], frames), BF16),
            pltpu.VMEM((frames, wide), BF16),
            pltpu.VMEM((2, 256, units), F32),
            pltpu.VMEM((640, 128), F32),
            pltpu.VMEM((2, BLOCKS[0], 128), F32),
            pltpu.VMEM((4, 256, 2 * units), F32),
            pltpu.VMEM((256, units), BF16),
            pltpu.VMEM((units, frames), BF16),
            pltpu.VMEM((units, frames), BF16),
            pltpu.VMEM((2, 272, 2 * units), I16),
            pltpu.VMEM((2, 4, 272, 2 * units), I16),
            pltpu.VMEM((2, 272, units), I16),
            pltpu.VMEM((2, 4, 272, units), I16),
            pltpu.VMEM((OUT_GROUPS, 2 * RING, message, 128), I16),
            pltpu.VMEM((OUT_GROUPS, 2, STEPS, message, 128), I16),
            pltpu.VMEM((2 * RING, hid_message, 128), I16),
            pltpu.VMEM((2, STEPS, hid_message, 128), I16),
            pltpu.VMEM((2 * RING, in_message, 256), I16),
            pltpu.VMEM((2, STEPS, in_message, 256), I16),
            pltpu.VMEM((2, RING, 64, 256), F32),
            pltpu.VMEM((OUT_GROUPS + 2, RING, 8, 128), F32),
            pltpu.VMEM((OUT_GROUPS + 2, 2, 128, 128), F32),
            pltpu.VMEM(vec.shape, F32),
            pltpu.VMEM((RING,) + vec.shape, F32),
            sem((2,)),
            sem((2,)),
            sem((2,)),
            sem((1,)),
            sem((2,)),
            sem((2,)),
            sem((2, 4)),
            sem((2,)),
            sem((2, 4)),
            sem((OUT_GROUPS, 2, STEPS)),
            sem((OUT_GROUPS, 2, STEPS)),
            sem((2, STEPS)),
            sem((2, STEPS)),
            sem((2, STEPS)),
            sem((2, STEPS)),
            sem((2, STEPS)),
            sem((2, STEPS)),
            sem((STEPS,)),
            sem((STEPS,)),
            sem((OUT_GROUPS + 2, STEPS)),
            sem((OUT_GROUPS + 2, STEPS)),
        ],
        compiler_params=pltpu.CompilerParams(
            collective_id=1, has_side_effects=True, vmem_limit_bytes=63 * 1024 * 1024
        ),
    )(dl, h_two, h_one, x, part, slope_two, slope_one, w_hid, res_out, res_hid, res_in, res_tail, vec)


RING_STARTS = (0, 2, 5, 7, 9)
LAYER_TWO_WAVE = 7
LOGIT_WAVES = (11, 12, 14, 16)


def forward_kernel(
    slot_count,
    x_ref,
    tags_ref,
    w_in_ref,
    w_hid_ref,
    w_out_ref,
    bias_ref,
    bias_out_ref,
    x_out,
    h_one_out,
    h_two_out,
    slope_one_out,
    slope_two_out,
    w_hid_out,
    w_out_out,
    dl_ref,
    bias_sum_ref,
    loss_ref,
    x_all,
    h_one,
    h_two,
    slope_one,
    slope_two,
    w_in,
    w_hid,
    w_out,
    curve,
    bias_col,
    tags,
    sums,
    ring_send,
    ring_recv,
    x_send,
    x_recv,
    h_send,
    h_recv,
    tag_send,
    tag_recv,
    sum_send,
    sum_recv,
    out_sems,
):
    blk = lax.axis_index("blk")
    col = lax.axis_index("col")
    here = ring_place(blk)
    senones, depth = w_out_ref.shape
    own_rows, deep = x_ref.shape
    units = w_hid_ref.shape[1]
    frames = x_all.shape[0]
    cores = {"col": col + 1 - 2 * (col % 2)}
    across = {"col": (col + 2) % 4}
    corner = {"col": (col + 2) % 4 + 1 - 2 * (col % 2)}
    others = (cores, across, corner)

    barrier = pltpu.get_barrier_semaphore()
    for target in others + tuple({"blk": ring_blk((here + way) % RING)} for way in (1, 7)):
        pl.semaphore_signal(barrier, inc=1, device_id=target, device_id_type=MESH)

    w_hid[pl.ds(pl.multiple_of(blk * depth, depth), depth), :] = w_hid_ref[...].astype(BF16)
    own_lanes = pl.ds(pl.multiple_of(blk * depth, depth), depth)
    w_out[senones // 16 * 16 :, own_lanes] = jnp.zeros(
        (w_out.shape[0] - senones // 16 * 16, depth), BF16
    )
    w_out[0:senones, own_lanes] = w_out_ref[...].astype(BF16)
    own_frames = pl.ds(pl.multiple_of(col * own_rows, own_rows), own_rows)
    x_all[own_frames, :] = jnp.zeros((own_rows, x_all.shape[1]), BF16)
    x_all[own_frames, 0:deep] = x_ref[...]
    tags[col] = tags_ref[...]
    sums[...] = jnp.zeros_like(sums)
    pl.semaphore_wait(barrier, 5)

    def ring_part(group, origin, way):
        start = pl.multiple_of(origin * depth + way * 128, 128)
        if group == 0:
            return w_hid.at[pl.ds(start, 128), :]
        return w_out.at[pl.ds((group - 1) * OUT_ROWS, OUT_ROWS), pl.ds(start, 128)]

    def ring_move(group, step, way):
        origin = ring_blk((here - step + 2 * step * way + RING) % RING)
        part = ring_part(group, origin, way)
        return pltpu.make_async_remote_copy(
            src_ref=part,
            dst_ref=part,
            send_sem=ring_send.at[group, way, step],
            recv_sem=ring_recv.at[group, way, step],
            device_id={"blk": ring_blk((here + 1 - 2 * way + RING) % RING)},
            device_id_type=MESH,
        )

    def ring_wave(wave):
        for group, start in enumerate(RING_STARTS):
            step = wave - 1 - start
            for way in range(2):
                if step == -1:
                    ring_move(group, 0, way).start()
                if 0 <= step < STEPS:
                    ring_move(group, step, way).wait_recv()
                    if step < STEPS - 1:
                        ring_move(group, step + 1, way).start()

    def copy_to(target, src, send_sem, recv_sem):
        return pltpu.make_async_remote_copy(
            src_ref=src,
            dst_ref=src,
            send_sem=send_sem,
            recv_sem=recv_sem,
            device_id=target,
            device_id_type=MESH,
        )

    def rows_of(owner):
        return pl.ds(pl.multiple_of(owner * own_rows, own_rows), own_rows)

    def lanes_of(owner):
        return pl.ds(pl.multiple_of(owner * units, units), units)

    def x_move(number):
        owner = across["col"] if number == 2 else col
        target = across if number == 1 else cores
        return copy_to(target, x_all.at[rows_of(owner), :], x_send.at[number], x_recv.at[number])

    def h_move(layer, number, block):
        owner = across["col"] if number == 2 else col
        target = across if number == 1 else cores
        whole = (h_one, h_two)[layer]
        part = whole.at[pl.ds(block * own_rows, own_rows), lanes_of(owner)]
        return copy_to(
            target, part, h_send.at[layer, number, block], h_recv.at[layer, number, block]
        )

    def h_start(layer, block):
        h_move(layer, 0, block).start()
        h_move(layer, 1, block).start()

    def h_forward(layer, block):
        h_move(layer, 1, block).wait_recv()
        h_move(layer, 2, block).start()

    def h_ready(layer, block):
        h_move(layer, 0, block).wait_recv()
        h_move(layer, 2, block).wait_recv()

    ring_wave(0)
    x_move(0).start()
    x_move(1).start()
    tag_copies = [
        copy_to(target, tags.at[col], tag_send.at[number], tag_recv.at[number])
        for number, target in enumerate(others)
    ]
    for copy in tag_copies:
        copy.start()
    w_in[...] = jnp.zeros_like(w_in)
    w_in[0:deep, :] = w_in_ref[...].astype(BF16)
    for number in range(bias_out_ref.shape[0]):
        line = jnp.broadcast_to(bias_out_ref[number : number + 1, :], (128, 128))
        bias_col[number * 128 : (number + 1) * 128, :] = jnp.transpose(line)
    ring_wave(1)
    x_move(1).wait_recv()
    x_move(2).start()
    x_move(0).wait_recv()
    x_move(2).wait_recv()

    def layer(number, block, inputs, weights, whole, slopes):
        there = slice(block * own_rows, (block + 1) * own_rows)
        value = jax.nn.sigmoid(
            dot_nn(inputs[there, :], weights[...]) + bias_ref[number : number + 1, :]
        )
        slopes[there, :] = value * (1.0 - value)
        whole[there, lanes_of(col)] = value.astype(BF16)
        h_start(number, block)

    outs = []

    def put(src, dst):
        copy = pltpu.make_async_copy(src, dst, out_sems.at[len(outs)])
        copy.start()
        outs.append(copy)

    for block in range(4):
        layer(0, block, x_all, w_in, h_one, slope_one)
    put(x_all, x_out)
    put(slope_one, slope_one_out)

    def all_tags():
        return jnp.concatenate([tags[owner, 0:1, :] for owner in range(4)], axis=1)

    def own_row(line):
        line = line - col * senones
        return jnp.where(line < senones, line, -1)

    def logits(group):
        first = group * OUT_ROWS
        half = frames // 2
        for part in range(2):
            curve[first : first + OUT_ROWS, part * half : (part + 1) * half] = dot_nt(
                w_out[first : first + OUT_ROWS, :], h_two[part * half : (part + 1) * half, :]
            )
        base = lax.broadcasted_iota(jnp.int32, (16, frames), 0)

        def largest(number, top):
            row = pl.multiple_of(first + number * 16, 16)
            value = curve[pl.ds(row, 16), :] + bias_col[pl.ds(row, 16), 0:1]
            if group == OUT_GROUPS - 1:
                value = jnp.where(base + row < senones, value, -1e30)
            curve[pl.ds(row, 16), :] = value
            return jnp.maximum(top, value)

        top = lax.fori_loop(0, OUT_ROWS // 16, largest, jnp.full((16, frames), -1e30, F32))
        top = jnp.max(top, axis=0, keepdims=True)
        line = jnp.broadcast_to(own_row(all_tags()), (16, frames))

        def exponents(number, carry):
            total, picked = carry
            row = pl.multiple_of(first + number * 16, 16)
            value = curve[pl.ds(row, 16), :]
            power = jnp.exp(value - top)
            curve[pl.ds(row, 16), :] = power
            return total + power, picked + jnp.where(base + row == line, value, 0.0)

        blank = jnp.zeros((16, frames), F32)
        total, picked = lax.fori_loop(0, OUT_ROWS // 16, exponents, (blank, blank))
        sums[col, group : group + 1, :] = top
        sums[col, 4 + group : 5 + group, :] = jnp.sum(total, axis=0, keepdims=True)
        sums[col, 8 + group : 9 + group, :] = jnp.sum(picked, axis=0, keepdims=True)

    last_wave = RING_STARTS[-1] + STEPS
    for wave in range(2, last_wave + 1):
        ring_wave(wave)
        if 2 <= wave < 6:
            h_forward(0, wave - 2)
        if wave == LAYER_TWO_WAVE:
            for block in range(4):
                h_ready(0, block)
                layer(1, block, h_one, w_hid, h_two, slope_two)
            put(h_one, h_one_out)
            put(slope_two, slope_two_out)
            put(w_hid, w_hid_out)
        if LAYER_TWO_WAVE < wave <= LAYER_TWO_WAVE + 4:
            h_forward(1, wave - LAYER_TWO_WAVE - 1)
        for group, when in enumerate(LOGIT_WAVES):
            if wave == when:
                if group == 0:
                    for block in range(4):
                        h_ready(1, block)
                    put(h_two, h_two_out)
                    for copy in tag_copies:
                        copy.wait_recv()
                rows = pl.ds(group * OUT_ROWS, OUT_ROWS)
                put(w_out.at[rows, :], w_out_out.at[rows, :])
                logits(group)

    sum_copies = [
        copy_to(target, sums.at[col], sum_send.at[number], sum_recv.at[number])
        for number, target in enumerate(others)
    ]
    for copy in sum_copies:
        copy.start()
    for copy in sum_copies:
        copy.wait_recv()

    def lines(first):
        return [sums[owner, first + group : first + group + 1, :] for owner in range(4) for group in range(4)]

    tops = lines(0)
    top = functools.reduce(jnp.maximum, tops)
    total = functools.reduce(
        jnp.add, [size * jnp.exp(own - top) for own, size in zip(tops, lines(4), strict=True)]
    )
    picked = functools.reduce(jnp.add, lines(8))
    line = all_tags()
    live = line >= 0
    loss = jnp.where(live, top + jnp.log(total) - picked, 0.0)
    loss_ref[...] = jnp.zeros_like(loss_ref)
    loss_ref[0:1, :] = functools.reduce(
        jnp.add, [loss[:, lane : lane + 128] for lane in range(0, frames, 128)]
    )
    weight = jnp.where(live, 1.0 / slot_count, 0.0)
    line = jnp.broadcast_to(own_row(line), (16, frames))
    hit_weight = jnp.broadcast_to(weight, (16, frames))
    base = lax.broadcasted_iota(jnp.int32, (16, frames), 0)
    bias_col[...] = jnp.zeros_like(bias_col)
    for group in range(OUT_GROUPS):
        share = jnp.exp(sums[col, group : group + 1, :] - top) / total * weight

        def gradient(number, carry, first=group * OUT_ROWS, share=share):
            row = pl.multiple_of(first + number * 16, 16)
            value = curve[pl.ds(row, 16), :] * share - jnp.where(base + row == line, hit_weight, 0.0)
            value = value.astype(BF16)
            dl_ref[pl.ds(row, 16), :] = value
            bias_col[pl.ds(row, 16), :] = jnp.broadcast_to(
                jnp.sum(value.astype(F32), axis=1, keepdims=True), (16, 128)
            )
            return carry

        lax.fori_loop(0, OUT_ROWS // 16, gradient, 0)
    bias_sum_ref[...] = jnp.zeros_like(bias_sum_ref)
    for number in range(bias_out_ref.shape[0]):
        block = jnp.transpose(bias_col[number * 128 : (number + 1) * 128, :])
        bias_sum_ref[number : number + 1, :] = block[0:1, :]

    for group in range(len(RING_STARTS)):
        for way in range(2):
            for step in range(STEPS):
                ring_move(group, step, way).wait_send()
    for number in range(3):
        x_move(number).wait_send()
        for block in range(4):
            h_move(0, number, block).wait_send()
            h_move(1, number, block).wait_send()
    for copy in tag_copies + sum_copies:
        copy.wait_send()
    for copy in outs:
        copy.wait()


def forward_pass(x, tags, w_in, w_hid, w_out, bias, bias_out, slot_count):
    own_rows = x.shape[0]
    units = w_hid.shape[1]
    frames = 4 * own_rows
    wide = 4 * units
    rows = OUT_GROUPS * OUT_ROWS
    blocks = bias_out.shape[0]
    vmem = pl.BlockSpec(memory_space=pltpu.VMEM)
    hbm = pl.BlockSpec(memory_space=pl.ANY)
    sem = pltpu.SemaphoreType.DMA
    kept = (
        ((frames, 512), BF16),
        ((frames, wide), BF16),
        ((frames, wide), BF16),
        ((frames, units), F32),
        ((frames, units), F32),
        ((wide, units), BF16),
        ((rows, wide), BF16),
    )
    return pl.pallas_call(
        functools.partial(forward_kernel, slot_count),
        out_shape=tuple(jax.ShapeDtypeStruct(shape, kind) for shape, kind in kept)
        + (
            jax.ShapeDtypeStruct((rows, frames), BF16),
            jax.ShapeDtypeStruct((24, 128), F32),
            jax.ShapeDtypeStruct((8, 128), F32),
        ),
        in_specs=[vmem] * 7,
        out_specs=(hbm,) * 7 + (vmem,) * 3,
        scratch_shapes=[pltpu.VMEM(shape, kind) for shape, kind in kept[:5]]
        + [
            pltpu.VMEM((512, units), BF16),
            pltpu.VMEM((wide, units), BF16),
            pltpu.VMEM((rows, wide), BF16),
            pltpu.VMEM((rows, frames), F32),
            pltpu.VMEM((blocks * 128, 128), F32),
            pltpu.VMEM((4,) + tags.shape, jnp.int32),
            pltpu.VMEM((4, 16, frames), F32),
            sem((5, 2, STEPS)),
            sem((5, 2, STEPS)),
            sem((3,)),
            sem((3,)),
            sem((2, 3, 4)),
            sem((2, 3, 4)),
            sem((3,)),
            sem((3,)),
            sem((3,)),
            sem((3,)),
            sem((16,)),
        ],
        compiler_params=pltpu.CompilerParams(
            collective_id=2, has_side_effects=True, vmem_limit_bytes=60 * 1024 * 1024
        ),
    )(x, tags, w_in, w_hid, w_out, bias, bias_out)


DIM_BITS = (2, 4, 8)
ORDERS = ((0, 1, 2), (1, 2, 0), (2, 0, 1))
PIECES = ((0, 48), (48, 48), (96, 32))
SIZE_PIECE = 2
LIGHT_HID = 3
LIGHT_IN = 2


def stage_sends(stage, sources):
    moves = []
    for piece, order in enumerate(ORDERS):
        slot = sum(DIM_BITS[order[index]] for index in sources)
        moves.append((piece, slot, order[stage]))
    return moves


def landed(moves):
    return [(slot | DIM_BITS[dim], piece) for piece, slot, dim in moves]


FIRST = stage_sends(0, ())
SECOND = stage_sends(1, ())
SECOND_ON = stage_sends(1, (0,))
THIRD = stage_sends(2, ())
THIRD_A = stage_sends(2, (0,))
THIRD_B = stage_sends(2, (1,))
THIRD_C = stage_sends(2, (0, 1))
MOVES = FIRST + SECOND + SECOND_ON + THIRD + THIRD_A + THIRD_B + THIRD_C


def muon_kernel(
    stats_ref,
    red_hid_ref,
    mom_hid_ref,
    red_in_ref,
    mom_in_ref,
    hid_ref,
    inp_ref,
    next_hid_ref,
    next_in_ref,
    norm_ref,
    codes,
    sizes,
    tops,
    lows,
    scales,
    weights,
    xs,
    us,
    vs,
    lhs,
    xin,
    xin_top,
    xin_low,
    gram,
    gram_got,
    back,
    sums,
    sums_got,
    send_sems,
    core_sems,
    recv_sems,
    back_send,
    back_recv,
    sums_send,
    sums_recv,
    spread_send,
    spread_recv,
    pair_send,
    pair_recv,
    size_send,
    size_recv,
):
    blk = lax.axis_index("blk")
    col = lax.axis_index("col")
    rows, wide = xs.shape
    height = back.shape[2]
    part_wide = inp_ref.shape[1]
    other_core = {"col": col + 1 - 2 * (col % 2)}
    dims = (
        {"blk": blk + 1 - 2 * (blk % 2)},
        {"col": (col + 2) % 4},
        {"blk": blk + 2 - 4 * ((blk // 2) % 2)},
    )
    far = {"blk": (blk + 4) % 8}
    diagonal = {"blk": 4 * (blk // 4) + 3 - blk % 4}
    barrier = pltpu.get_barrier_semaphore()
    for target in (other_core, dims[1], *({"blk": (blk + away) % 8} for away in range(1, 8))):
        pl.semaphore_signal(barrier, inc=1, device_id=target, device_id_type=MESH)

    def fold(values):
        line = jnp.sum(values, axis=0, keepdims=True)
        return sum(line[:, lane : lane + 128] for lane in range(0, line.shape[1], 128))

    share = 0.125
    sums[0, 0:1, :] = fold(stats_ref[...])
    sums[0, 1:2, :] = fold(mom_hid_ref[...] * mom_hid_ref[...])
    sums[0, 2:3, :] = fold(mom_hid_ref[...] * red_hid_ref[...])
    sums[0, 3:4, :] = fold(red_hid_ref[...] * red_hid_ref[...])
    sums[0, 4:5, :] = fold(mom_in_ref[...] * mom_in_ref[...]) * share
    sums[0, 5:6, :] = fold(mom_in_ref[...] * red_in_ref[...]) * share
    sums[0, 6:7, :] = fold(red_in_ref[...] * red_in_ref[...]) * share
    sums[0, 7:8, :] = jnp.zeros((1, 128), F32)
    eye = lax.broadcasted_iota(jnp.int32, (rows, rows), 0) == lax.broadcasted_iota(
        jnp.int32, (rows, rows), 1
    )
    pl.semaphore_wait(barrier, 9)

    for number, target in enumerate((other_core, *dims, far)):
        copy = pltpu.make_async_remote_copy(
            src_ref=sums.at[number],
            dst_ref=sums_got.at[number],
            send_sem=sums_send.at[number],
            recv_sem=sums_recv.at[number],
            device_id=target,
            device_id_type=MESH,
        )
        copy.start()
        copy.wait()
        sums[number + 1] = sums[number] + sums_got[number]
    whole = jnp.sum(sums[5], axis=1, keepdims=True)
    clip = jnp.sqrt(whole[0:1])
    factor = jnp.minimum(1.0, CLIP / clip)

    def norm_of(first):
        square = (
            0.25 * whole[first : first + 1]
            + factor * whole[first + 1 : first + 2]
            + factor * factor * whole[first + 2 : first + 3]
        )
        return 1.0 / (jnp.sqrt(jnp.maximum(square, 0.0)) + 1e-07)

    norm_ref[0:4, :] = jnp.broadcast_to(clip, (4, 128))
    norm_ref[4:8, :] = jnp.broadcast_to(factor, (4, 128))
    next_hid_ref[...] = 0.5 * mom_hid_ref[...] + factor * red_hid_ref[...]
    next_in_ref[...] = 0.5 * mom_in_ref[...] + factor * red_in_ref[...]

    my_lanes = pl.ds(pl.multiple_of(blk * height, height), height)
    spread = []
    for away in range(1, 8):
        target = (blk + away) % 8
        spread.append(
            pltpu.make_async_remote_copy(
                src_ref=next_hid_ref.at[
                    pl.ds(pl.multiple_of(target % 4 * rows, rows), rows), :
                ],
                dst_ref=xs.at[:, my_lanes],
                send_sem=spread_send.at[away - 1],
                recv_sem=spread_recv.at[away - 1],
                device_id={"blk": target},
                device_id_type=MESH,
            )
        )
        spread[-1].start()
    high = col // 2
    my_half = pl.ds(pl.multiple_of(high * part_wide, part_wide), part_wide)
    half_copy = pltpu.make_async_remote_copy(
        src_ref=next_in_ref,
        dst_ref=xin.at[:, my_half],
        send_sem=pair_send.at[0],
        recv_sem=pair_recv.at[0],
        device_id=dims[1],
        device_id_type=MESH,
    )
    half_copy.start()
    xs[:, my_lanes] = next_hid_ref[pl.ds(pl.multiple_of(blk % 4 * rows, rows), rows), :]
    xin[:, my_half] = next_in_ref[...]
    for copy in spread:
        copy.wait_recv()
    xs[...] = xs[...] * norm_of(1)
    in_scale = norm_of(4)

    numbers = {move: number for number, move in enumerate(MOVES)}

    def part(turn, slot, piece):
        first, count = PIECES[piece]
        return codes.at[turn, slot, pl.ds(first, count), :]

    def send(turn, move):
        piece, slot, dim = move
        there = slot | DIM_BITS[dim]
        copies = [
            pltpu.make_async_remote_copy(
                src_ref=part(turn, slot, piece),
                dst_ref=part(turn, there, piece),
                send_sem=send_sems.at[numbers[move]],
                recv_sem=recv_sems.at[turn, there, piece],
                device_id=dims[dim],
                device_id_type=MESH,
            )
        ]
        if piece == SIZE_PIECE:
            copies.append(
                pltpu.make_async_remote_copy(
                    src_ref=sizes.at[turn, slot],
                    dst_ref=sizes.at[turn, there],
                    send_sem=size_send.at[numbers[move]],
                    recv_sem=size_recv.at[turn, there],
                    device_id=dims[dim],
                    device_id_type=MESH,
                )
            )
        return copies

    def send_all(turn, moves):
        for move in moves:
            for copy in send(turn, move):
                copy.start()

    def to_core(turn, slot, piece):
        copies = [
            pltpu.make_async_remote_copy(
                src_ref=part(turn, slot, piece),
                dst_ref=part(turn, slot + 1, piece),
                send_sem=core_sems.at[slot // 2, piece],
                recv_sem=recv_sems.at[turn, slot + 1, piece],
                device_id=other_core,
                device_id_type=MESH,
            )
        ]
        if piece == SIZE_PIECE:
            copies.append(
                pltpu.make_async_remote_copy(
                    src_ref=sizes.at[turn, slot],
                    dst_ref=sizes.at[turn, slot + 1],
                    send_sem=core_sems.at[slot // 2, 3],
                    recv_sem=size_recv.at[turn, slot + 1],
                    device_id=other_core,
                    device_id_type=MESH,
                )
            )
        return copies

    def arrived(turn, slot, piece):
        def wait(ref, sem):
            pltpu.make_async_remote_copy(
                src_ref=ref,
                dst_ref=ref,
                send_sem=core_sems.at[0, 0],
                recv_sem=sem,
                device_id=other_core,
                device_id_type=MESH,
            ).wait_recv()

        wait(part(turn, slot, piece), recv_sems.at[turn, slot, piece])
        if piece == SIZE_PIECE:
            wait(sizes.at[turn, slot], size_recv.at[turn, slot])

    def forward(turn, moves, on=()):
        for number, (slot, piece) in enumerate(landed(moves)):
            arrived(turn, slot, piece)
            for copy in to_core(turn, slot, piece):
                copy.start()
            if on:
                send_all(turn, on[number : number + 1])

    def gram_copy():
        return pltpu.make_async_remote_copy(
            src_ref=gram,
            dst_ref=gram_got,
            send_sem=pair_send.at[1],
            recv_sem=pair_recv.at[1],
            device_id=other_core,
            device_id_type=MESH,
        )

    def unpack(turn, index, pair, light):
        for core in range(2):
            here = pl.ds(pl.multiple_of(index * 2 * rows + core * rows, rows), rows)
            slot = 2 * pair + core
            if light:
                tops[here, :] = from_codes(codes[turn, slot]).astype(BF16)
            else:
                top, low = halves(from_codes(codes[turn, slot]))
                tops[here, :] = top
                lows[here, :] = low
            size = sizes[turn, slot]
            scales[:, here] = size * size

    def inner(first, count, light):
        here = pl.ds(first, count)
        if light:
            values = dot_nt(lhs[0:rows, :], tops[here, :])
            weights[0:rows, here] = (values * scales[0:1, here]).astype(BF16)
        else:
            both = dot_nt(lhs[...], tops[here, :])
            values = both[:rows] + both[rows:] + dot_nt(lhs[0:rows, :], lows[here, :])
            top, low = halves(values * scales[0:1, here])
            weights[0:rows, here] = top
            weights[rows:, here] = low

    def outer(first, count, out, add, light):
        cut = 512
        here = slice(first, first + count)
        for start in range(0, wide, cut):
            lanes = slice(start, start + cut)
            if light:
                value = dot_nn(weights[0:rows, here], tops[here, lanes])
            else:
                both = dot_nn(weights[:, here], tops[here, lanes])
                value = both[:rows] + both[rows:] + dot_nn(weights[0:rows, here], lows[here, lanes])
            if add:
                value = value + out[:, lanes]
            out[:, lanes] = value

    def set_lhs(values):
        top, low = halves(values)
        lhs[0:rows, :] = top
        lhs[rows:, :] = low

    def input_gram(light):
        top, low = halves(xin[...])
        xin_top[...] = top
        if light:
            gram[...] = dot_nt(xin_top[...], xin_top[...])
        else:
            xin_low[...] = low
            cross = dot_nt(xin_top[...], xin_low[...])
            gram[...] = dot_nt(xin_top[...], xin_top[...]) + (cross + jnp.transpose(cross))
        gram_copy().start()

    def input_step(light):
        gram_copy().wait()
        square_of = gram[...] + gram_got[...]
        top, low = halves(square_of)
        if light:
            poly = NS_B * square_of + NS_C * dot_nn(top, top)
        else:
            cross = dot_nn(top, low)
            poly = NS_B * square_of + NS_C * (dot_nn(top, top) + (cross + jnp.transpose(cross)))
        top, low = halves(poly)
        cut = 512
        for start in range(0, xin.shape[1], cut):
            lanes = slice(start, start + cut)
            change = dot_nn(top, xin_top[:, lanes])
            if not light:
                change = change + dot_nn(low, xin_top[:, lanes]) + dot_nn(top, xin_low[:, lanes])
            xin[:, lanes] = NS_A * xin[:, lanes] + change

    def by_weight(number, limit, work):
        @pl.when(number < limit)
        def _():
            work(True)

        @pl.when(number >= limit)
        def _():
            work(False)

    def iteration(number, carry):
        turn = number % 2
        values = xs[...]
        largest = jnp.maximum(jnp.max(jnp.abs(values), axis=1, keepdims=True), 1e-30)
        codes[turn, 0] = to_codes(values * (TOP_CODE / largest))
        lane_size = jnp.sum(jnp.where(eye, largest, 0.0), axis=0, keepdims=True)
        sizes[turn, 0] = jnp.broadcast_to(lane_size * (1.0 / TOP_CODE), (8, rows))
        send_all(turn, FIRST)
        for piece in range(3):
            for copy in to_core(turn, 0, piece):
                copy.start()
        send_all(turn, SECOND)
        set_lhs(values)

        def first_pass(index, carry):
            pair = index + (index // 3) * (1 - index // 4) - (index // 4) * (1 - index // 5)

            @pl.when(index == 1)
            def _():
                forward(turn, FIRST, SECOND_ON)
                send_all(turn, THIRD)
                send_all(turn, THIRD_A)

                @pl.when(number > 0)
                def _():
                    by_weight(number, LIGHT_IN, input_gram)

                forward(turn, SECOND, THIRD_B)
                forward(turn, SECOND_ON, THIRD_C)

                @pl.when(number > 0)
                def _():
                    by_weight(number, LIGHT_IN, input_step)

                forward(turn, THIRD)

            @pl.when(index == 4)
            def _():
                forward(turn, THIRD_A)
                forward(turn, THIRD_B)

            @pl.when((index == 6) & (number == 0))
            def _():
                half_copy.wait()
                xin[...] = xin[...] * in_scale
                input_gram(True)
                input_step(True)

            @pl.when(index == 7)
            def _():
                forward(turn, THIRD_C)

            for piece in range(3):
                arrived(turn, 2 * pair + 1, piece)

            def work(light):
                unpack(turn, index, pair, light)
                inner(pl.multiple_of(index * 2 * rows, 2 * rows), 2 * rows, light)

            by_weight(number, LIGHT_HID, work)

            @pl.when(index == 3)
            def _():
                by_weight(number, LIGHT_HID, lambda light: outer(0, wide // 2, us, False, light))

            return carry

        lax.fori_loop(0, 8, first_pass, 0)

        def second_pass(light):
            outer(wide // 2, wide // 2, us, True, light)
            set_lhs(us[...])
            for first in range(0, wide, 512):
                inner(first, 512, light)
            outer(0, wide, vs, False, light)

        by_weight(number, LIGHT_HID, second_pass)
        xs[...] = NS_A * xs[...] + NS_B * us[...] + NS_C * vs[...]
        for move in MOVES:
            for copy in send(turn, move):
                copy.wait_send()
        for pair in range(8):
            for piece in range(3):
                for copy in to_core(turn, 2 * pair, piece):
                    copy.wait_send()
        return carry

    lax.fori_loop(0, NS, iteration, 0)

    place = blk % 4
    copies = []
    for rel, target in ((1, dims[0]), (2, dims[2]), (3, diagonal)):
        copies.append(
            pltpu.make_async_remote_copy(
                src_ref=xs.at[:, pl.ds(pl.multiple_of(target["blk"] * height, height), height)],
                dst_ref=back.at[place],
                send_sem=back_send.at[rel - 1],
                recv_sem=back_recv.at[rel - 1],
                device_id=target,
                device_id_type=MESH,
            )
        )
        copies[-1].start()
    hid_ref[place] = xs[:, my_lanes]
    inp_ref[...] = xin[:, my_half]
    for copy in copies:
        copy.wait_recv()
    for target in (dims[0], dims[2], diagonal):
        other = target["blk"] % 4
        hid_ref[other] = back[other]
    for copy in copies + spread:
        copy.wait_send()


def muon(stats, red_hid, mom_hid, red_in, mom_in, wide):
    rows = red_hid.shape[0] // 4
    height = red_hid.shape[1]
    deep, part_wide = red_in.shape
    vmem = pl.BlockSpec(memory_space=pltpu.VMEM)
    sem = pltpu.SemaphoreType.DMA
    return pl.pallas_call(
        muon_kernel,
        out_shape=(
            jax.ShapeDtypeStruct((4, rows, height), F32),
            jax.ShapeDtypeStruct((deep, part_wide), F32),
            jax.ShapeDtypeStruct(red_hid.shape, F32),
            jax.ShapeDtypeStruct(red_in.shape, F32),
            jax.ShapeDtypeStruct((8, 128), F32),
        ),
        in_specs=[vmem] * 5,
        out_specs=(vmem,) * 5,
        scratch_shapes=[
            pltpu.VMEM((2, 16, rows, wide), I16),
            pltpu.VMEM((2, 16, 8, rows), F32),
            pltpu.VMEM((wide, wide), BF16),
            pltpu.VMEM((wide, wide), BF16),
            pltpu.VMEM((8, wide), F32),
            pltpu.VMEM((2 * rows, wide), BF16),
            pltpu.VMEM((rows, wide), F32),
            pltpu.VMEM((rows, wide), F32),
            pltpu.VMEM((rows, wide), F32),
            pltpu.VMEM((2 * rows, wide), BF16),
            pltpu.VMEM((deep, 2 * part_wide), F32),
            pltpu.VMEM((deep, 2 * part_wide), BF16),
            pltpu.VMEM((deep, 2 * part_wide), BF16),
            pltpu.VMEM((deep, deep), F32),
            pltpu.VMEM((deep, deep), F32),
            pltpu.VMEM((4, rows, height), F32),
            pltpu.VMEM((6, 8, 128), F32),
            pltpu.VMEM((5, 8, 128), F32),
            sem((len(MOVES),)),
            sem((8, 4)),
            sem((2, 16, 3)),
            sem((3,)),
            sem((3,)),
            sem((5,)),
            sem((5,)),
            sem((7,)),
            sem((7,)),
            sem((2,)),
            sem((2,)),
            sem((len(MOVES),)),
            sem((2, 16)),
        ],
        compiler_params=pltpu.CompilerParams(
            collective_id=0, has_side_effects=True, vmem_limit_bytes=60 * 1024 * 1024
        ),
    )(stats, red_hid, mom_hid, red_in, mom_in)


def plain_body(
    frames,
    labels,
    mask,
    w_input,
    w_hidden,
    w_output,
    biases,
    mom_input,
    mom_hidden,
    out_first,
    out_second,
    bias_first,
    bias_second,
    res_input,
    res_hidden,
    res_output,
):
    ncol = lax.axis_size("col")
    nblk = lax.axis_size("blk")
    col_index = lax.axis_index("col")
    hcol = w_input.shape[1]
    scol = w_output.shape[1]
    micro = frames.shape[0]
    slot_count = frames.shape[1] * micro * nblk * ncol
    bias_row = biases[0]
    b_one = bias_row[:hcol]
    b_two = bias_row[hcol : 2 * hcol]
    b_out = bias_row[2 * hcol :]
    low_input = w_input.astype(jnp.bfloat16)
    row_tags = jnp.where(mask > 0, labels, -1)
    grad_input = jnp.zeros(w_input.shape, jnp.float32)
    grad_hidden = jnp.zeros((w_hidden.shape[0] * nblk, hcol), jnp.float32)
    grad_output = jnp.zeros((w_output.shape[0] * nblk, scol), jnp.float32)
    grad_bias = jnp.zeros(bias_row.shape, jnp.float32)
    loss_local = jnp.zeros((), jnp.float32)
    for micro_step in range(micro):
        low_hidden, low_output = (
            lax.all_gather(w_hidden.astype(jnp.bfloat16), "blk", axis=0, tiled=True),
            lax.all_gather(w_output.astype(jnp.bfloat16), "blk", axis=0, tiled=True),
        )
        inputs = lax.all_gather(frames[micro_step], "col", axis=0, tiled=True)
        tags_group = lax.all_gather(row_tags[micro_step], "col", axis=0, tiled=True)
        sig_one = jax.nn.sigmoid(matmul(inputs, low_input) + b_one)
        h_one = spread_cols(sig_one.astype(jnp.bfloat16))
        sig_two = jax.nn.sigmoid(matmul(h_one, low_hidden) + b_two)
        h_two = spread_cols(sig_two.astype(jnp.bfloat16))
        logits = matmul(h_two, low_output) + b_out
        row_top = lax.pmax(jnp.max(logits, axis=1), "col")
        exponent = jnp.exp(logits - row_top[:, None])
        target_hit = jnp.arange(scol)[None, :] == (tags_group - col_index * scol)[:, None]
        row_total, picked = lax.psum(
            (jnp.sum(exponent, axis=1), jnp.sum(jnp.where(target_hit, logits, 0.0), axis=1)), "col"
        )
        live_rows = tags_group >= 0
        loss_local = loss_local + jnp.sum(
            jnp.where(live_rows, row_top + jnp.log(row_total) - picked, 0.0)
        )
        probs = exponent / row_total[:, None]
        d_logits = (
            jnp.where(live_rows[:, None], probs - target_hit.astype(jnp.float32), 0.0) / slot_count
        ).astype(jnp.bfloat16)
        grad_output = grad_output + inner_rows(h_two, d_logits)
        d_h_two = reduce_cols(outer_cols(d_logits, low_output))
        d_z_two = (d_h_two * sig_two * (1.0 - sig_two)).astype(jnp.bfloat16)
        grad_hidden = grad_hidden + inner_rows(h_one, d_z_two)
        d_h_one = reduce_cols(outer_cols(d_z_two, low_hidden))
        d_z_one = (d_h_one * sig_one * (1.0 - sig_one)).astype(jnp.bfloat16)
        grad_input = grad_input + inner_rows(inputs, d_z_one)
        grad_bias = grad_bias + jnp.concatenate(
            [
                jnp.sum(d_z_one.astype(jnp.float32), axis=0),
                jnp.sum(d_z_two.astype(jnp.float32), axis=0),
                jnp.sum(d_logits.astype(jnp.float32), axis=0),
            ]
        )
    q_input, next_res_input = squash(grad_input, res_input[0])
    q_hidden, next_res_hidden = squash(grad_hidden, res_hidden[0])
    q_output, next_res_output = squash(grad_output, res_output[0])
    red_hidden, red_output = (
        lax.psum_scatter(q_hidden, "blk", scatter_dimension=0, tiled=True),
        lax.psum_scatter(q_output, "blk", scatter_dimension=0, tiled=True),
    )
    red_input, red_bias, loss_sum = lax.psum((q_input, grad_bias, loss_local), "blk")
    share_blk = 1.0 / nblk
    grad_square = (
        share_blk * (jnp.sum(red_input * red_input) + jnp.sum(red_bias * red_bias))
        + jnp.sum(red_hidden * red_hidden)
        + jnp.sum(red_output * red_output)
    )
    clip_norm = jnp.sqrt(lax.psum(grad_square, ("blk", "col")))
    factor = jnp.minimum(1.0, CLIP / clip_norm)
    next_mom_input = 0.5 * mom_input + factor * red_input
    next_mom_hidden = 0.5 * mom_hidden + factor * red_hidden
    square_input, square_hidden = lax.psum(
        (
            share_blk * jnp.sum(next_mom_input * next_mom_input),
            jnp.sum(next_mom_hidden * next_mom_hidden),
        ),
        ("blk", "col"),
    )
    iter_input = next_mom_input / (jnp.sqrt(square_input) + 1e-07)
    iter_hidden = next_mom_hidden / (jnp.sqrt(square_hidden) + 1e-07)
    for turn_index in range(NS):
        rows_hidden = collect_rows(iter_hidden)
        gram_input, gram_hidden = lax.psum(
            (precise(iter_input, iter_input.T), precise(iter_hidden, rows_hidden.T)), "col"
        )
        image_input = precise(gram_input, iter_input)
        image_hidden = precise(gram_hidden, rows_hidden)
        iter_input = (
            NS_A * iter_input + NS_B * image_input + NS_C * precise(gram_input, image_input)
        )
        iter_hidden = (
            NS_A * iter_hidden
            + NS_B * image_hidden
            + NS_C * precise(gram_hidden, collect_rows(image_hidden))
        )
    muon_scale = LR_MUON * 0.2 * math.sqrt(hcol * ncol)
    new_input = w_input * (1.0 - LR_MUON * WD_MUON) - muon_scale * iter_input
    new_hidden = w_hidden * (1.0 - LR_MUON * WD_MUON) - muon_scale * iter_hidden
    new_output, next_out_first, next_out_second = adam_step(
        w_output, factor * red_output, out_first, out_second
    )
    new_biases, next_bias_first, next_bias_second = adam_step(
        biases, factor * red_bias[None, :], bias_first, bias_second
    )
    return (
        loss_sum,
        clip_norm,
        new_input,
        new_hidden,
        new_output,
        new_biases,
        next_mom_input,
        next_mom_hidden,
        next_out_first,
        next_out_second,
        next_bias_first,
        next_bias_second,
        next_res_input[None],
        next_res_hidden[None],
        next_res_output[None],
    )


def fast_body(
    frames,
    labels,
    mask,
    w_input,
    w_hidden,
    w_output,
    biases,
    mom_input,
    mom_hidden,
    out_first,
    out_second,
    bias_first,
    bias_second,
    res_input,
    res_hidden,
    res_output,
):
    ncol = lax.axis_size("col")
    nblk = lax.axis_size("blk")
    col_index = lax.axis_index("col")
    blk_index = lax.axis_index("blk")
    hcol = w_input.shape[1]
    scol = w_output.shape[1]
    micro = frames.shape[0]
    slot_count = frames.shape[1] * micro * nblk * ncol
    bias_row = biases[0]
    deep = w_input.shape[0]
    padded = 512
    rows_out = OUT_GROUPS * OUT_ROWS
    own_tags = jnp.where(mask > 0, labels, -1).reshape(1, -1)
    layer_biases = jnp.pad(bias_row[: 2 * hcol].reshape(2, hcol), ((0, 6), (0, 0)))
    blocks = -(-rows_out // 128)
    out_biases = jnp.pad(bias_row[2 * hcol :], (0, blocks * 128 - scol)).reshape(blocks, 128)
    inputs, h_one, h_two, slope_one, slope_two, low_hidden, low_output, d_logits, bias_sums, losses = (
        forward_pass(
            frames.reshape(-1, deep),
            jnp.broadcast_to(own_tags, (8, own_tags.shape[1])),
            w_input,
            w_hidden,
            w_output.T,
            layer_biases,
            out_biases,
            slot_count,
        )
    )
    loss_local = jnp.sum(losses)
    partial = inner_rows(d_logits, low_output)
    vec = jnp.concatenate([jnp.zeros((2 * hcol,), F32), bias_sums.reshape(-1)[:scol], loss_local[None]])
    vec = jnp.pad(vec, (0, 4096 - vec.shape[0])).reshape(32, 128)
    next_out, next_hid, next_in, red_out, red_hid, red_in, vec_sum, stats = reduce_grads(
        d_logits,
        h_two,
        h_one,
        inputs,
        partial,
        slope_two,
        slope_one,
        low_hidden,
        res_output[0].T,
        res_hidden[0].T,
        jnp.pad(res_input[0], ((0, padded - deep), (0, 0))).T,
        jnp.pad(res_output[0, :, scol // 16 * 16 :], ((0, 0), (0, 16 - scol % 16))).T,
        vec,
        scol,
        deep,
    )
    next_res_output = next_out.transpose(1, 2, 0)
    next_res_hidden = next_hid.T
    next_res_input = next_in[:, :deep].T
    red_output = red_out[:scol].T
    vec_sum = vec_sum.reshape(-1)
    red_bias = vec_sum[: bias_row.shape[0]]
    loss_sum = vec_sum[bias_row.shape[0]]
    stats = stats.at[1, 0].set(jnp.sum(red_bias * red_bias) / nblk)
    done_hidden, done_input, mom_hid_next, mom_in_next, norms = muon(
        stats,
        red_hid,
        mom_hidden.T,
        red_in.T,
        jnp.pad(mom_input, ((0, padded - deep), (0, 0))),
        hcol * ncol,
    )
    clip_norm = norms[0, 0]
    factor = norms[4, 0]
    next_mom_hidden = mom_hid_next.T
    next_mom_input = mom_in_next[:deep]
    done_hidden = done_hidden.reshape(hcol, w_hidden.shape[0]).T
    muon_scale = LR_MUON * 0.2 * math.sqrt(hcol * ncol)
    new_input = w_input * (1.0 - LR_MUON * WD_MUON) - muon_scale * done_input[:deep]
    new_hidden = w_hidden * (1.0 - LR_MUON * WD_MUON) - muon_scale * done_hidden
    new_output, next_out_first, next_out_second = adam_step(
        w_output, factor * red_output, out_first, out_second
    )
    new_biases, next_bias_first, next_bias_second = adam_step(
        biases, factor * red_bias[None, :], bias_first, bias_second
    )
    return (
        loss_sum,
        clip_norm,
        new_input,
        new_hidden,
        new_output,
        new_biases,
        next_mom_input,
        next_mom_hidden,
        next_out_first,
        next_out_second,
        next_bias_first,
        next_bias_second,
        next_res_input[None],
        next_res_hidden[None],
        next_res_output,
    )


def solution(mesh):
    in_specs = (
        P(None, ("blk", "col"), None),
        P(None, ("blk", "col")),
        P(None, ("blk", "col")),
        P(None, "col"),
        P("blk", "col"),
        P("blk", "col"),
        P("col", None),
        P(None, "col"),
        P("blk", "col"),
        P("blk", "col"),
        P("blk", "col"),
        P("col", None),
        P("col", None),
        P("blk", None, "col"),
        P("blk", None, "col"),
        P("blk", None, "col"),
    )
    out_specs = (
        P(),
        P(),
        P(None, "col"),
        P("blk", "col"),
        P("blk", "col"),
        P("col", None),
        P(None, "col"),
        P("blk", "col"),
        P("blk", "col"),
        P("blk", "col"),
        P("col", None),
        P("col", None),
        P("blk", None, "col"),
        P("blk", None, "col"),
        P("blk", None, "col"),
    )
    cubes = mesh.shape["blk"] == 8 and mesh.shape["col"] == 4
    body = fast_body if cubes else plain_body
    return jax.shard_map(body, mesh=mesh, in_specs=in_specs, out_specs=out_specs, check_vma=False)
```

```python
import functools
import math

import jax
import jax.numpy as jnp
from jax import lax
from jax.experimental import pallas as pl
from jax.experimental.pallas import tpu as pltpu
from jax.sharding import PartitionSpec as P

NS = 5
STEP = 5


NS_A = 3.4445
NS_B = -4.775
NS_C = 2.0315
CLIP = 0.002
LR_MUON = 0.1
WD_MUON = 0.01
LR_ADAM = 0.03
WD_ADAM = 0.1

MESH = pl.DeviceIdType.MESH
F32 = jnp.float32
BF16 = jnp.bfloat16
I16 = jnp.int16
LN2 = math.log(2.0)
TOP_CODE = 32700.0
LEVELS = 64.0


def matmul(left_side, right_side):
    return jnp.dot(left_side, right_side, preferred_element_type=jnp.float32)


def inner_rows(left_side, right_side):
    return lax.dot_general(
        left_side, right_side, (((0,), (0,)), ((), ())), preferred_element_type=jnp.float32
    )


def outer_cols(left_side, right_side):
    return lax.dot_general(
        left_side, right_side, (((1,), (1,)), ((), ())), preferred_element_type=jnp.float32
    )


def precise(left_side, right_side):
    return jnp.dot(
        left_side, right_side, precision=lax.Precision.HIGHEST, preferred_element_type=jnp.float32
    )


def spread_cols(values):
    return lax.all_gather(values, "col", axis=1, tiled=True)


def reduce_cols(values):
    return lax.psum_scatter(values, "col", scatter_dimension=1, tiled=True)


def collect_rows(values):
    return lax.all_gather(values, "blk", axis=0, tiled=True)


def squash(gradient, resid):
    value = gradient + resid.astype(jnp.float32)
    scale = jnp.mean(jnp.abs(value), axis=0, keepdims=True) + 1e-12
    signed = scale * jnp.tanh(2.0 * value / scale)
    return (signed, value - signed)


def adam_step(weight, gradient, first, second):
    first = 0.5 * first + 0.5 * gradient
    second = 0.95 * second + 0.05 * gradient * gradient
    update = first / (1.0 - 0.5**STEP) / (jnp.sqrt(second / (1.0 - 0.95**STEP)) + 1e-08)
    return (weight - LR_ADAM * (update + WD_ADAM * weight), first, second)


def halves(values):
    top = values.astype(BF16)
    return top, (values - top.astype(F32)).astype(BF16)


def dot_nn(left_side, right_side):
    return lax.dot_general(
        left_side, right_side, (((1,), (0,)), ((), ())), preferred_element_type=F32
    )


def dot_nt(left_side, right_side):
    return lax.dot_general(
        left_side, right_side, (((1,), (1,)), ((), ())), preferred_element_type=F32
    )


RING = 8
STEPS = RING - 1
OUT_ROWS = 592
OUT_GROUPS = 4
BLOCKS = (304, 288)
HID_ROWS = 512
HID_GROUP = 4
IN_GROUP = 5
HID_WAVE = 6
IN_WAVE = 6


def ring_place(blk):
    odd = blk % 2
    return (blk // 2) * (1 - odd) + (7 - blk // 2) * odd


def ring_blk(place):
    back = place // 4
    return 2 * place * (1 - back) + (15 - 2 * place) * back


def scale_code(size):
    return jnp.ceil(jnp.log(jnp.maximum(size, 1e-30)) * (LEVELS / LN2))


def code_scale(code):
    return jnp.exp(code * (LN2 / LEVELS))


def to_codes(values):
    return jnp.round(values).astype(jnp.int32).astype(I16)


def from_codes(codes):
    return codes.astype(jnp.int32).astype(F32)


def reduce_kernel(
    deep,
    dl_ref,
    h_two_ref,
    h_one_ref,
    x_ref,
    part_ref,
    slope_two_ref,
    slope_one_ref,
    w_hid_ref,
    res_out_ref,
    res_hid_ref,
    res_in_ref,
    res_tail_ref,
    vec_ref,
    next_out_ref,
    next_hid_ref,
    next_in_ref,
    red_out_ref,
    red_hid_ref,
    red_in_ref,
    red_far_ref,
    vec_sum_ref,
    stats_ref,
    grad,
    stage,
    res_buf,
    dl_buf,
    h_buf,
    slope_buf,
    marks,
    cols,
    keep_sums,
    dz,
    dz_two,
    dz_one,
    core_out,
    core_got,
    far_out,
    far_got,
    own_out,
    got_out,
    own_hid,
    got_hid,
    own_in,
    got_in,
    share_in,
    share_far,
    sizes,
    shares,
    vec,
    vecs,
    res_sems,
    dl_sems,
    load_sems,
    stage_sems,
    slope_sems,
    core_send,
    core_recv,
    far_send,
    far_recv,
    out_send,
    out_recv,
    hid_send,
    hid_recv,
    in_send,
    in_recv,
    share_send,
    share_recv,
    vec_send,
    vec_recv,
    size_send,
    size_recv,
    share_far_send,
    share_far_recv,
):
    blk = lax.axis_index("blk")
    col = lax.axis_index("col")
    here = ring_place(blk)
    total_rows = next_out_ref.shape[0]
    core, high = col % 2, col // 2
    cores = {"col": col + 1 - 2 * core}
    across = {"col": (col + 2) % 4}
    barrier = pltpu.get_barrier_semaphore()
    for target in (cores, across, *({"blk": (blk + away) % RING} for away in range(1, RING))):
        pl.semaphore_signal(barrier, inc=1, device_id=target, device_id_type=MESH)

    starts = [sum(BLOCKS[:part]) for part in range(len(BLOCKS))]

    def res_copy(group, part, rows=None):
        rows = rows or BLOCKS[part]
        return pltpu.make_async_copy(
            res_out_ref.at[pl.ds(group * OUT_ROWS + starts[part], rows), :],
            res_buf.at[part, pl.ds(0, rows), :],
            res_sems.at[part],
        )

    def dl_copy(group, part):
        rows = BLOCKS[part]
        return pltpu.make_async_copy(
            dl_ref.at[pl.ds(group * OUT_ROWS + starts[part], rows), :],
            dl_buf.at[part, pl.ds(0, rows), :],
            dl_sems.at[part],
        )

    def hid_res_copy(part):
        return pltpu.make_async_copy(
            res_hid_ref.at[pl.ds(part * 256, 256), :],
            res_buf.at[part, pl.ds(0, 256), :],
            res_sems.at[part],
        )

    def hid_next_copy(part):
        return pltpu.make_async_copy(
            grad.at[pl.ds(0, 256), :], next_hid_ref.at[pl.ds(part * 256, 256), :], load_sems.at[1]
        )

    def load(src, dst):
        return pltpu.make_async_copy(src, dst, load_sems.at[0])

    def stage_copy(group, part, rows):
        return pltpu.make_async_copy(
            stage.at[pl.ds(0, rows)],
            next_out_ref.at[pl.ds(group * OUT_ROWS + starts[part], rows)],
            stage_sems.at[0],
        )

    last_rows = total_rows - (OUT_GROUPS - 1) * OUT_ROWS - starts[-1]
    whole_rows = last_rows // 16 * 16

    def stage_start(group, part):
        if part < len(BLOCKS) - 1:
            stage_copy(group, part, BLOCKS[part]).start()
        else:

            @pl.when(group < OUT_GROUPS - 1)
            def _():
                stage_copy(group, part, BLOCKS[part]).start()

            @pl.when(group == OUT_GROUPS - 1)
            def _():
                stage_copy(group, part, last_rows).start()

    for part in range(2):
        res_copy(0, part).start()
        dl_copy(0, part).start()
    load(h_two_ref, h_buf).start()
    marks[...] = jnp.zeros_like(marks)
    stats_ref[...] = jnp.zeros_like(stats_ref)
    vec[...] = vec_ref[...]
    pl.semaphore_wait(barrier, RING + 1)

    CHUNK = 256
    units = slope_buf.shape[2]

    def slope_copy(layer, block):
        rows = pl.ds(pl.multiple_of(block * CHUNK, CHUNK), CHUNK)
        src = (slope_two_ref, slope_one_ref)[layer]
        return pltpu.make_async_copy(src.at[rows, :], slope_buf.at[block % 2], slope_sems.at[block % 2])

    def core_move(layer, block):
        return pltpu.make_async_remote_copy(
            src_ref=core_out.at[block % 2],
            dst_ref=core_got.at[layer, block],
            send_sem=core_send.at[block % 2],
            recv_sem=core_recv.at[layer, block],
            device_id=cores,
            device_id_type=MESH,
        )

    def far_move(layer, block):
        return pltpu.make_async_remote_copy(
            src_ref=far_out.at[block % 2],
            dst_ref=far_got.at[layer, block],
            send_sem=far_send.at[block % 2],
            recv_sem=far_recv.at[layer, block],
            device_id=across,
            device_id_type=MESH,
        )

    def lanes_of(number):
        return pl.ds(pl.multiple_of(number * units, units), units)

    def rows_at(number):
        return pl.ds(pl.multiple_of(number * 16, 16), 16)

    def free(copy, layer, block):
        @pl.when((layer > 0) | (block >= 2))
        def _():
            copy.wait_send()

    def lane_codes(first):
        return jnp.transpose(marks[first : first + 128, :])[0:1, :]

    def set_factors():
        top = jnp.max(cols[0, 0:CHUNK, :], axis=1, keepdims=True)
        code = scale_code(top)
        marks[0:CHUNK, :] = jnp.broadcast_to(code, (CHUNK, 128))
        cols[1, 0:CHUNK, :] = jnp.broadcast_to(TOP_CODE / code_scale(code), (CHUNK, 128))

    def largest(values):
        return functools.reduce(
            jnp.maximum,
            [
                jnp.abs(value[:, lane : lane + 128])
                for value in values
                for lane in range(0, value.shape[1], 128)
            ],
        )

    def scaled(values, factor):
        return jnp.concatenate(
            [values[:, lane : lane + 128] * factor for lane in range(0, values.shape[1], 128)], axis=1
        )

    def put_scale(out):
        codes = jnp.concatenate(
            [lane_codes(0), lane_codes(128), jnp.zeros((14, 128), F32)], axis=0
        )
        out[CHUNK : CHUNK + 16, 0:128] = codes.astype(jnp.int32).astype(I16)

    def read_scale(got):
        step = code_scale(from_codes(got[CHUNK : CHUNK + 16, 0:128])) * (1.0 / TOP_CODE)
        step = jnp.transpose(jnp.concatenate([step, jnp.zeros((112, 128), F32)], axis=0))
        for up in range(2):
            marks[CHUNK + up * 128 : CHUNK + (up + 1) * 128, :] = jnp.broadcast_to(
                step[:, up : up + 1], (128, 128)
            )

    def step_at(number):
        return marks[pl.ds(pl.multiple_of(CHUNK + number * 16, 16), 16), :]

    def split(layer, block):
        free(core_move(layer, block), layer, block)

        def measure(number, carry):
            rows = rows_at(number)
            cols[0, rows, :] = largest(
                [grad[rows, lanes_of(2 * half + 1 - core)] for half in range(2)]
            )
            return carry

        lax.fori_loop(0, CHUNK // 16, measure, 0)
        set_factors()

        def write(number, carry):
            rows = rows_at(number)
            factor = cols[1, rows, :]
            for half in range(2):
                there = slice(half * units, (half + 1) * units)
                core_out[block % 2, rows, there] = to_codes(
                    scaled(grad[rows, lanes_of(2 * half + 1 - core)], factor)
                )
                keep_sums[block, rows, there] = grad[rows, lanes_of(2 * half + core)]
            return carry

        lax.fori_loop(0, CHUNK // 16, write, 0)
        put_scale(core_out.at[block % 2])
        core_move(layer, block).start()

    def cross(layer, block):
        core_move(layer, block).wait_recv()
        free(far_move(layer, block), layer, block)
        got = core_got.at[layer, block]
        read_scale(got)

        def add(number, carry):
            rows = rows_at(number)
            near, away = lanes_of(high), lanes_of(1 - high)
            step = step_at(number)
            keep_sums[block, rows, near] += scaled(from_codes(got[rows, near]), step)
            value = keep_sums[block, rows, away] + scaled(from_codes(got[rows, away]), step)
            keep_sums[block, rows, away] = value
            cols[0, rows, :] = largest([value])
            return carry

        lax.fori_loop(0, CHUNK // 16, add, 0)
        set_factors()

        def write(number, carry):
            rows = rows_at(number)
            far_out[block % 2, rows, :] = to_codes(
                scaled(keep_sums[block, rows, lanes_of(1 - high)], cols[1, rows, :])
            )
            return carry

        lax.fori_loop(0, CHUNK // 16, write, 0)
        put_scale(far_out.at[block % 2])
        far_move(layer, block).start()

    def finish(layer, block):
        far_move(layer, block).wait_recv()
        slope_copy(layer, block).wait()
        got = far_got.at[layer, block]
        read_scale(got)

        def one(number, total):
            rows = rows_at(number)
            value = keep_sums[block, rows, lanes_of(high)] + scaled(
                from_codes(got[rows, :]), step_at(number)
            )
            value = (value * slope_buf[block % 2, rows, :]).astype(BF16)
            dz[rows, :] = value
            return total + value.astype(F32)

        total = lax.fori_loop(0, CHUNK // 16, one, jnp.zeros((16, units), F32))
        if layer == 0:

            @pl.when(block < 2)
            def _():
                slope_copy(0, block + 2).start()

            @pl.when(block >= 2)
            def _():
                slope_copy(1, block - 2).start()

        else:

            @pl.when(block < 2)
            def _():
                slope_copy(1, block + 2).start()

        total = jnp.sum(total, axis=0, keepdims=True)
        for number in range(units // 128):
            row = 4 * (1 - layer) + number
            vec[row : row + 1, :] += total[:, number * 128 : (number + 1) * 128]
        flipped = (dz_two, dz_one)[layer]
        for up in range(CHUNK // 128):
            there = pl.ds(pl.multiple_of(block * CHUNK + up * 128, 128), 128)
            for number in range(units // 128):
                tile = dz[up * 128 : (up + 1) * 128, number * 128 : (number + 1) * 128]
                flipped[number * 128 : (number + 1) * 128, there] = jnp.transpose(
                    tile.astype(F32)
                ).astype(BF16)

    def blocks(first, last, work):
        def one(block, carry):
            work(block)
            return carry

        lax.fori_loop(first, last, one, 0)

    def start_block(block):
        rows = pl.ds(pl.multiple_of(block * CHUNK, CHUNK), CHUNK)
        copy = pltpu.make_async_copy(part_ref.at[rows, :], grad.at[pl.ds(0, CHUNK), :], load_sems.at[1])
        copy.start()
        copy.wait()
        split(0, block)

    def turn_block(block):
        finish(0, block)
        for lane in range(0, grad.shape[1], 512):
            grad[0:CHUNK, lane : lane + 512] = dot_nt(dz[...], w_hid_ref[lane : lane + 512, :])
        split(1, block)

    core_out[:, CHUNK:, :] = jnp.zeros((2, 16, 2 * units), I16)
    far_out[:, CHUNK:, :] = jnp.zeros((2, 16, units), I16)
    slope_copy(0, 0).start()
    slope_copy(0, 1).start()
    def vec_copy(away):
        return pltpu.make_async_remote_copy(
            src_ref=vec,
            dst_ref=vecs.at[blk],
            send_sem=vec_send.at[away - 1],
            recv_sem=vec_recv.at[away - 1],
            device_id={"blk": (blk + away) % RING},
            device_id_type=MESH,
        )

    def set_rows(count, first_own, size):
        size = jnp.broadcast_to(size, (count, 128))
        marks[first_own : first_own + count, :] = size
        cols[0, 0:count, :] = size
        cols[1, 0:count, :] = 2.0 / size

    def tell_sizes(group):
        for away in range(1, RING):
            size_copy(group, away).start()

    def size_copy(group, away):
        return pltpu.make_async_remote_copy(
            src_ref=sizes.at[group, here],
            dst_ref=sizes.at[group, here],
            send_sem=size_send.at[group, away - 1],
            recv_sem=size_recv.at[group, away - 1],
            device_id={"blk": ring_blk((here + away) % RING)},
            device_id_type=MESH,
        )

    def set_sizes(rows, group):
        parts = [lane_codes(first) for first in range(0, rows, 128)]
        parts.append(jnp.zeros((8 - len(parts), 128), F32))
        sizes[group, here] = jnp.concatenate(parts, axis=0)
        tell_sizes(group)

    def make_shares(group, row_of):
        for away in range(1, RING):
            size_copy(group, away).wait_recv()
        for way in range(2):
            tiles = []
            for step in range(STEPS):
                mine = row_of(here, step, way)
                came = mine * 0.0
                for back in range(step + 1):
                    came = came + row_of((here - 1 - back + (2 + 2 * back) * way + RING) % RING, step, way)
                if step < STEPS - 1:
                    whole = 1.0 / jnp.maximum(came + mine, 1e-30)
                else:
                    whole = 1.0 / TOP_CODE
                tiles += [came * whole, mine * whole]
            tiles.append(jnp.zeros((16, 128), F32))
            shares[group, way] = jnp.transpose(jnp.concatenate(tiles, axis=0))

    def squash_rows(count, own, first_own, read_res, write_next):
        wide = grad.shape[1]

        def add(number, carry):
            row = pl.multiple_of(number * 16, 16)
            value = grad[pl.ds(row, 16), :] + read_res(row)
            grad[pl.ds(row, 16), :] = value
            value = jnp.abs(value)
            cols[0, pl.ds(row, 16), :] = functools.reduce(
                jnp.add, [value[:, lane : lane + 128] for lane in range(0, wide, 128)]
            )
            return carry

        lax.fori_loop(0, count // 16, add, 0)
        set_rows(
            count,
            first_own,
            jnp.sum(cols[0, 0:count, :], axis=1, keepdims=True) * (1.0 / wide) + 1e-12,
        )

        def some(number, carry):
            row = pl.multiple_of(number * 16, 16)
            size = cols[0, pl.ds(row, 16), :]
            steep = cols[1, pl.ds(row, 16), :]
            for lane in range(0, wide, 128):
                piece = grad[pl.ds(row, 16), lane : lane + 128]
                curve = jnp.tanh(piece * steep)
                number_of = lane // 256
                chunk = number_of // 2 if number_of % 2 == 0 else 7 - number_of // 2
                own[2 * chunk + lane // 128 % 2, pl.ds(first_own + row, 16), :] = to_codes(
                    curve * TOP_CODE
                )
                write_next(row, lane, piece - size * curve)
            return carry

        lax.fori_loop(0, count // 16, some, 0)

    def out_group(group):
        for part, rows in enumerate(BLOCKS):
            dl_copy(group, part).wait()
            if part == 0:

                @pl.when(group == 0)
                def _():
                    load(h_two_ref, h_buf).wait()

            for lane in range(0, grad.shape[1], 512):
                grad[0:rows, lane : lane + 512] = dot_nn(
                    dl_buf[part, 0:rows, :], h_buf[:, lane : lane + 512]
                )
            if part == 0:
                res_copy(group, part).wait()
            else:

                @pl.when(group < OUT_GROUPS - 1)
                def _():
                    res_copy(group, 1).wait()

                @pl.when(group == OUT_GROUPS - 1)
                def _():
                    res_copy(group, 1, whole_rows).wait()
                    res_buf[1, whole_rows : whole_rows + 16, :] = res_tail_ref[...]
                    res_buf[1, whole_rows + 16 : BLOCKS[1], :] = jnp.zeros(
                        (BLOCKS[1] - whole_rows - 16, res_buf.shape[2]), BF16
                    )

            if part == 0:

                @pl.when(group > 0)
                def _():
                    stage_copy(group - 1, len(BLOCKS) - 1, BLOCKS[-1]).wait()

            else:
                stage_copy(group, part - 1, BLOCKS[part - 1]).wait()

            def write_next(row, lane, values):
                stage[pl.ds(row, 16), 0, lane : lane + 128] = values

            squash_rows(
                rows,
                own_out.at[group],
                starts[part],
                lambda row, part=part: res_buf[part, pl.ds(row, 16), :].astype(F32),
                write_next,
            )
            stage_start(group, part)

            @pl.when(group < OUT_GROUPS - 1)
            def _(part=part):
                if part == 0:
                    res_copy(group + 1, 0).start()
                else:

                    @pl.when(group < OUT_GROUPS - 2)
                    def _():
                        res_copy(group + 1, 1).start()

                    @pl.when(group == OUT_GROUPS - 2)
                    def _():
                        res_copy(group + 1, 1, whole_rows).start()

                dl_copy(group + 1, part).start()

            @pl.when(group == OUT_GROUPS - 1)
            def _(part=part):
                hid_res_copy(part).start()
                if part == len(BLOCKS) - 1:
                    load(h_one_ref, h_buf).start()

        set_sizes(OUT_ROWS, group)

    def hid_group():
        load(h_one_ref, h_buf).wait()
        for part in range(2):
            first = part * 256
            if part:
                hid_next_copy(part - 1).wait()
            for lane in range(0, grad.shape[1], 512):
                grad[0:256, lane : lane + 512] = dot_nn(
                    dz_two[first : first + 256, :], h_buf[:, lane : lane + 512]
                )
            hid_res_copy(part).wait()

            def write_next(row, lane, values):
                grad[pl.ds(row, 16), lane : lane + 128] = values

            squash_rows(
                256,
                own_hid,
                first,
                lambda row, part=part: res_buf[part, pl.ds(row, 16), :].astype(F32),
                write_next,
            )
            hid_next_copy(part).start()
        load(x_ref, h_buf.at[:, pl.ds(0, x_ref.shape[1])]).start()
        set_sizes(HID_ROWS, HID_GROUP)
        hid_next_copy(1).wait()

    def in_group():
        wide = x_ref.shape[1]
        load(x_ref, h_buf.at[:, pl.ds(0, wide)]).wait()
        for first in range(0, HID_ROWS, 256):
            grad[0:256, 0:wide] = dot_nn(dz_one[first : first + 256, :], h_buf[:, 0:wide])

            def add(number, carry, first=first):
                row = pl.multiple_of(number * 16, 16)
                place = pl.multiple_of(first + row, 16)
                value = grad[pl.ds(row, 16), 0:wide] + res_in_ref[pl.ds(place, 16), :].astype(F32)
                grad[pl.ds(row, 16), 0:wide] = value
                value = jnp.abs(value)
                cols[0, pl.ds(row, 16), :] = functools.reduce(
                    jnp.add, [value[:, lane : lane + 128] for lane in range(0, wide, 128)]
                )
                return carry

            lax.fori_loop(0, 16, add, 0)
            set_rows(
                256,
                first,
                jnp.sum(cols[0, 0:256, :], axis=1, keepdims=True) * (1.0 / deep) + 1e-12,
            )

            def some(number, carry, first=first):
                row = pl.multiple_of(number * 16, 16)
                place = pl.multiple_of(first + row, 16)
                size = cols[0, pl.ds(row, 16), :]
                steep = cols[1, pl.ds(row, 16), :]
                chunk = first // 64 + number // 4
                inside = pl.multiple_of(number % 4 * 16, 16)
                for lane in range(0, wide, 128):
                    piece = grad[pl.ds(row, 16), lane : lane + 128]
                    curve = jnp.tanh(piece * steep)
                    next_in_ref[pl.ds(place, 16), lane : lane + 128] = piece - size * curve
                    own_in[
                        2 * chunk + lane // 256, pl.ds(inside, 16), lane % 256 : lane % 256 + 128
                    ] = to_codes(curve * TOP_CODE)
                return carry

            lax.fori_loop(0, 16, some, 0)
        sizes[IN_GROUP, here] = jnp.concatenate(
            [lane_codes(64 * chunk) for chunk in range(RING)], axis=0
        )
        tell_sizes(IN_GROUP)

    def towards(way):
        return {"blk": ring_blk((here + 1 - 2 * way + RING) % RING)}

    def move(src, got, step, way, send_sem, recv_sem):
        return pltpu.make_async_remote_copy(
            src_ref=src,
            dst_ref=got.at[way, step],
            send_sem=send_sem.at[way, step],
            recv_sem=recv_sem.at[way, step],
            device_id=towards(way),
            device_id_type=MESH,
        )

    def first_moves(own, got, send_sem, recv_sem):
        for way in range(2):
            chunk = (here - 1 + 2 * way + RING) % RING
            move(own.at[2 * chunk + way], got, 0, way, send_sem, recv_sem).start()

    def hop(rows, own, got, group, step, send_sem, recv_sem, keep):
        for way in range(2):
            move(got.at[way, step], got, step, way, send_sem, recv_sem).wait_recv()

        def add(way, result):
            message = got.at[way, step]
            ahead = here - 2 - step + way * (4 + 2 * step) + 2 * RING
            mine = own.at[2 * (ahead % RING) + way]
            share = pltpu.roll(shares[group, way], (128 - 16 * step) % 128, 1)
            for number, first in enumerate(range(0, rows, 128)):
                count = min(128, rows - first)
                there = slice(first, first + count)
                result(
                    first,
                    count,
                    from_codes(message[there, :]) * share[0:count, number : number + 1]
                    + from_codes(mine[there, :]) * share[0:count, 8 + number : 9 + number],
                )

        @pl.when(step < STEPS - 1)
        def _():
            for way in range(2):

                def write(first, count, value, way=way):
                    got[way, step, first : first + count, :] = to_codes(value)

                add(way, write)
            for way in range(2):
                move(got.at[way, step], got, step + 1, way, send_sem, recv_sem).start()

        @pl.when(step == STEPS - 1)
        def _():
            for way in range(2):

                def finish_rows(first, count, value, way=way):
                    keep(way, first, count, value)
                    square = jnp.sum(value * value, axis=0, keepdims=True)
                    for lane in range(0, value.shape[1], 128):
                        stats_ref[0:1, :] += square[:, lane : lane + 128]

                add(way, finish_rows)

    def out_hop(group, step):
        def keep(way, first, count, value):
            row = pl.multiple_of(group * OUT_ROWS + first, 16)
            red_out_ref[pl.ds(row, count), way * 128 : (way + 1) * 128] = value

        hop(
            OUT_ROWS,
            own_out.at[group],
            got_out.at[group],
            group,
            step,
            out_send.at[group],
            out_recv.at[group],
            keep,
        )

    def hid_hop(step):
        def keep(way, first, count, value):
            red_hid_ref[first : first + count, way * 128 : (way + 1) * 128] = value

        hop(HID_ROWS, own_hid, got_hid, HID_GROUP, step, hid_send, hid_recv, keep)

    def share_move(step, way):
        place = (here - step + 2 * step * way + 2 * RING) % RING
        return pltpu.make_async_remote_copy(
            src_ref=share_in.at[way, place],
            dst_ref=share_in.at[way, place],
            send_sem=share_send.at[way, step],
            recv_sem=share_recv.at[way, step],
            device_id=towards(way),
            device_id_type=MESH,
        )

    def share_across(way, place):
        return pltpu.make_async_remote_copy(
            src_ref=share_in.at[way, place],
            dst_ref=share_far.at[way, place],
            send_sem=share_far_send.at[way, place],
            recv_sem=share_far_recv.at[way, place],
            device_id=across,
            device_id_type=MESH,
        )

    def in_hop(step):
        def keep(way, first, count, value):
            share_in[way, here] = value

        hop(64, own_in, got_in, IN_GROUP, step, in_send, in_recv, keep)

        @pl.when(step == STEPS - 1)
        def _():
            for way in range(2):
                share_move(0, way).start()
                share_across(way, here).start()

    def share_hop(step):
        for way in range(2):
            share_move(step, way).wait_recv()
            share_across(way, (here - 1 - step + (2 + 2 * step) * way + RING) % RING).start()

        @pl.when(step < STEPS - 1)
        def _():
            for way in range(2):
                share_move(step + 1, way).start()

    def in_step(index):
        @pl.when((index >= 0) & (index < STEPS))
        def _():
            in_hop(index)

        @pl.when((index >= STEPS) & (index < 2 * STEPS))
        def _():
            share_hop(index - STEPS)

    def chunk_row(place, step, way):
        chunk = (here - 2 - step + way * (4 + 2 * step) + 2 * RING) % RING
        line = sizes[IN_GROUP, place, pl.ds(chunk, 1), :]
        return jnp.broadcast_to(line, (8, 128))

    def wave(number, carry):
        @pl.when(number < OUT_GROUPS)
        def _():
            out_group(number)
            first_moves(own_out.at[number], got_out.at[number], out_send.at[number], out_recv.at[number])

        @pl.when(number == HID_WAVE)
        def _():
            hid_group()
            first_moves(own_hid, got_hid, hid_send, hid_recv)

        @pl.when((number >= 1) & (number <= OUT_GROUPS))
        def _():
            group = number - 1
            make_shares(group, lambda place, step, way: sizes[group, place])

        @pl.when(number == HID_WAVE + 1)
        def _():
            make_shares(HID_GROUP, lambda place, step, way: sizes[HID_GROUP, place])

        @pl.when(number == IN_WAVE + 1)
        def _():
            make_shares(IN_GROUP, chunk_row)

        index = 2 * (number - IN_WAVE - 1)
        in_step(index)

        @pl.when((number > HID_WAVE) & (number <= HID_WAVE + STEPS))
        def _():
            hid_hop(number - HID_WAVE - 1)

        def outs(group, carry):
            step = number - 1 - group

            @pl.when((step >= 0) & (step < STEPS))
            def _():
                out_hop(group, step)

            return carry

        lax.fori_loop(0, OUT_GROUPS, outs, 0)

        @pl.when(number == 1)
        def _():
            blocks(0, 4, start_block)

        @pl.when(number == 2)
        def _():
            blocks(0, 4, lambda block: cross(0, block))

        @pl.when((number == 3) | (number == 4))
        def _():
            blocks(2 * number - 6, 2 * number - 4, turn_block)

        @pl.when(number == 4)
        def _():
            blocks(0, 4, lambda block: cross(1, block))

        @pl.when(number == IN_WAVE)
        def _():
            blocks(0, 4, lambda block: finish(1, block))
            in_group()
            first_moves(own_in, got_in, in_send, in_recv)
            for away in range(1, RING):
                vec_copy(away).start()

        in_step(index + 1)
        return carry

    lax.fori_loop(0, IN_WAVE + 1 + STEPS, wave, 0)

    def unfold(shares_of, out):
        for place in range(0, RING, 2):
            for way in range(2):
                for lane in range(0, 256, 128):
                    tile = jnp.concatenate(
                        [shares_of[way, place + more, :, lane : lane + 128] for more in range(2)],
                        axis=0,
                    )
                    first = way * 256 + lane
                    out[first : first + 128, place * 64 : place * 64 + 128] = jnp.transpose(tile)

    unfold(share_in, red_in_ref)
    for place in range(RING):
        for way in range(2):
            share_across(way, place).wait_recv()
    unfold(share_far, red_far_ref)
    for away in range(1, RING):
        vec_copy(away).wait_recv()
    vecs[blk] = vec[...]
    total = vecs[0]
    for number in range(1, RING):
        total = total + vecs[number]
    vec_sum_ref[...] = total
    flat = 128 * lax.broadcasted_iota(jnp.int32, total.shape, 0) + lax.broadcasted_iota(
        jnp.int32, total.shape, 1
    )
    total = jnp.where(flat < 2 * units + total_rows, total, 0.0)
    stats_ref[1:2, :] = jnp.sum(total * total, axis=0, keepdims=True) * (1.0 / RING)
    for away in range(1, RING):
        vec_copy(away).wait_send()
        for group in range(OUT_GROUPS + 2):
            size_copy(group, away).wait_send()
    for slot in range(2):
        core_move(1, 2 + slot).wait_send()
        far_move(1, 2 + slot).wait_send()
    stage_copy(OUT_GROUPS - 1, len(BLOCKS) - 1, last_rows).wait()
    for way in range(2):
        for step in range(STEPS):
            for group in range(OUT_GROUPS):
                move(
                    got_out.at[group, way, step],
                    got_out.at[group],
                    step,
                    way,
                    out_send.at[group],
                    out_recv.at[group],
                ).wait_send()
            move(got_hid.at[way, step], got_hid, step, way, hid_send, hid_recv).wait_send()
            move(got_in.at[way, step], got_in, step, way, in_send, in_recv).wait_send()
            share_move(step, way).wait_send()
        for place in range(RING):
            share_across(way, place).wait_send()


def reduce_grads(
    dl, h_two, h_one, x, part, slope_two, slope_one, w_hid, res_out, res_hid, res_in, res_tail, vec, senones, deep
):
    frames, wide = h_two.shape
    in_wide = x.shape[1]
    units = w_hid.shape[1]
    vmem = pl.BlockSpec(memory_space=pltpu.VMEM)
    hbm = pl.BlockSpec(memory_space=pl.ANY)
    message = OUT_ROWS
    hid_message = HID_ROWS
    in_message = 64
    sem = pltpu.SemaphoreType.DMA
    return pl.pallas_call(
        functools.partial(reduce_kernel, deep),
        out_shape=(
            jax.ShapeDtypeStruct((senones, 1, wide), F32),
            jax.ShapeDtypeStruct((HID_ROWS, wide), F32),
            jax.ShapeDtypeStruct((HID_ROWS, in_wide), F32),
            jax.ShapeDtypeStruct((OUT_GROUPS * OUT_ROWS, 256), F32),
            jax.ShapeDtypeStruct((HID_ROWS, 256), F32),
            jax.ShapeDtypeStruct((in_wide, HID_ROWS), F32),
            jax.ShapeDtypeStruct((in_wide, HID_ROWS), F32),
            jax.ShapeDtypeStruct(vec.shape, F32),
            jax.ShapeDtypeStruct((8, 128), F32),
        ),
        in_specs=[hbm] * 7 + [vmem] + [hbm] * 2 + [vmem] * 3,
        out_specs=(hbm, hbm) + (vmem,) * 7,
        scratch_shapes=[
            pltpu.VMEM((BLOCKS[0], wide), F32),
            pltpu.VMEM((BLOCKS[0], 1, wide), F32),
            pltpu.VMEM((2, BLOCKS[0], wide), BF16),
            pltpu.VMEM((2, BLOCKS[0], frames), BF16),
            pltpu.VMEM((frames, wide), BF16),
            pltpu.VMEM((2, 256, units), F32),
            pltpu.VMEM((640, 128), F32),
            pltpu.VMEM((2, BLOCKS[0], 128), F32),
            pltpu.VMEM((4, 256, 2 * units), F32),
            pltpu.VMEM((256, units), BF16),
            pltpu.VMEM((units, frames), BF16),
            pltpu.VMEM((units, frames), BF16),
            pltpu.VMEM((2, 272, 2 * units), I16),
            pltpu.VMEM((2, 4, 272, 2 * units), I16),
            pltpu.VMEM((2, 272, units), I16),
            pltpu.VMEM((2, 4, 272, units), I16),
            pltpu.VMEM((OUT_GROUPS, 2 * RING, message, 128), I16),
            pltpu.VMEM((OUT_GROUPS, 2, STEPS, message, 128), I16),
            pltpu.VMEM((2 * RING, hid_message, 128), I16),
            pltpu.VMEM((2, STEPS, hid_message, 128), I16),
            pltpu.VMEM((2 * RING, in_message, 256), I16),
            pltpu.VMEM((2, STEPS, in_message, 256), I16),
            pltpu.VMEM((2, RING, 64, 256), F32),
            pltpu.VMEM((2, RING, 64, 256), F32),
            pltpu.VMEM((OUT_GROUPS + 2, RING, 8, 128), F32),
            pltpu.VMEM((OUT_GROUPS + 2, 2, 128, 128), F32),
            pltpu.VMEM(vec.shape, F32),
            pltpu.VMEM((RING,) + vec.shape, F32),
            sem((2,)),
            sem((2,)),
            sem((2,)),
            sem((1,)),
            sem((2,)),
            sem((2,)),
            sem((2, 4)),
            sem((2,)),
            sem((2, 4)),
            sem((OUT_GROUPS, 2, STEPS)),
            sem((OUT_GROUPS, 2, STEPS)),
            sem((2, STEPS)),
            sem((2, STEPS)),
            sem((2, STEPS)),
            sem((2, STEPS)),
            sem((2, STEPS)),
            sem((2, STEPS)),
            sem((STEPS,)),
            sem((STEPS,)),
            sem((OUT_GROUPS + 2, STEPS)),
            sem((OUT_GROUPS + 2, STEPS)),
            sem((2, RING)),
            sem((2, RING)),
        ],
        compiler_params=pltpu.CompilerParams(
            collective_id=1, has_side_effects=True, vmem_limit_bytes=63 * 1024 * 1024
        ),
    )(dl, h_two, h_one, x, part, slope_two, slope_one, w_hid, res_out, res_hid, res_in, res_tail, vec)


RING_STARTS = (0, 2, 5, 7, 9)
LAYER_TWO_WAVE = 7
LOGIT_WAVES = (11, 12, 14, 16)


def forward_kernel(
    slot_count,
    x_ref,
    tags_ref,
    w_in_ref,
    w_hid_ref,
    w_out_ref,
    bias_ref,
    bias_out_ref,
    mom_ref,
    x_out,
    h_one_out,
    h_two_out,
    slope_one_out,
    slope_two_out,
    w_hid_out,
    w_out_out,
    mom_far_ref,
    dl_ref,
    bias_sum_ref,
    loss_ref,
    x_all,
    h_one,
    h_two,
    slope_one,
    slope_two,
    w_in,
    w_hid,
    w_out,
    curve,
    bias_col,
    tags,
    sums,
    ring_send,
    ring_recv,
    x_send,
    x_recv,
    h_send,
    h_recv,
    tag_send,
    tag_recv,
    sum_send,
    sum_recv,
    out_sems,
    mom_sems,
):
    blk = lax.axis_index("blk")
    col = lax.axis_index("col")
    here = ring_place(blk)
    senones, depth = w_out_ref.shape
    own_rows, deep = x_ref.shape
    units = w_hid_ref.shape[1]
    frames = x_all.shape[0]
    cores = {"col": col + 1 - 2 * (col % 2)}
    across = {"col": (col + 2) % 4}
    corner = {"col": (col + 2) % 4 + 1 - 2 * (col % 2)}
    others = (cores, across, corner)

    barrier = pltpu.get_barrier_semaphore()
    for target in others + tuple({"blk": ring_blk((here + way) % RING)} for way in (1, 7)):
        pl.semaphore_signal(barrier, inc=1, device_id=target, device_id_type=MESH)

    w_hid[pl.ds(pl.multiple_of(blk * depth, depth), depth), :] = w_hid_ref[...].astype(BF16)
    own_lanes = pl.ds(pl.multiple_of(blk * depth, depth), depth)
    w_out[senones // 16 * 16 :, own_lanes] = jnp.zeros(
        (w_out.shape[0] - senones // 16 * 16, depth), BF16
    )
    w_out[0:senones, own_lanes] = w_out_ref[...].astype(BF16)
    own_frames = pl.ds(pl.multiple_of(col * own_rows, own_rows), own_rows)
    x_all[own_frames, :] = jnp.zeros((own_rows, x_all.shape[1]), BF16)
    x_all[own_frames, 0:deep] = x_ref[...]
    tags[col] = tags_ref[...]
    sums[...] = jnp.zeros_like(sums)
    pl.semaphore_wait(barrier, 5)

    def ring_part(group, origin, way):
        start = pl.multiple_of(origin * depth + way * 128, 128)
        if group == 0:
            return w_hid.at[pl.ds(start, 128), :]
        return w_out.at[pl.ds((group - 1) * OUT_ROWS, OUT_ROWS), pl.ds(start, 128)]

    def ring_move(group, step, way):
        origin = ring_blk((here - step + 2 * step * way + RING) % RING)
        part = ring_part(group, origin, way)
        return pltpu.make_async_remote_copy(
            src_ref=part,
            dst_ref=part,
            send_sem=ring_send.at[group, way, step],
            recv_sem=ring_recv.at[group, way, step],
            device_id={"blk": ring_blk((here + 1 - 2 * way + RING) % RING)},
            device_id_type=MESH,
        )

    def ring_wave(wave):
        for group, start in enumerate(RING_STARTS):
            step = wave - 1 - start
            for way in range(2):
                if step == -1:
                    ring_move(group, 0, way).start()
                if 0 <= step < STEPS:
                    ring_move(group, step, way).wait_recv()
                    if step < STEPS - 1:
                        ring_move(group, step + 1, way).start()

    def copy_to(target, src, send_sem, recv_sem):
        return pltpu.make_async_remote_copy(
            src_ref=src,
            dst_ref=src,
            send_sem=send_sem,
            recv_sem=recv_sem,
            device_id=target,
            device_id_type=MESH,
        )

    def rows_of(owner):
        return pl.ds(pl.multiple_of(owner * own_rows, own_rows), own_rows)

    def lanes_of(owner):
        return pl.ds(pl.multiple_of(owner * units, units), units)

    def x_move(number):
        owner = across["col"] if number == 2 else col
        target = across if number == 1 else cores
        return copy_to(target, x_all.at[rows_of(owner), :], x_send.at[number], x_recv.at[number])

    def h_move(layer, number, block):
        owner = across["col"] if number == 2 else col
        target = across if number == 1 else cores
        whole = (h_one, h_two)[layer]
        part = whole.at[pl.ds(block * own_rows, own_rows), lanes_of(owner)]
        return copy_to(
            target, part, h_send.at[layer, number, block], h_recv.at[layer, number, block]
        )

    def h_start(layer, block):
        h_move(layer, 0, block).start()
        h_move(layer, 1, block).start()

    def h_forward(layer, block):
        h_move(layer, 1, block).wait_recv()
        h_move(layer, 2, block).start()

    def h_ready(layer, block):
        h_move(layer, 0, block).wait_recv()
        h_move(layer, 2, block).wait_recv()

    ring_wave(0)
    x_move(0).start()
    x_move(1).start()
    tag_copies = [
        copy_to(target, tags.at[col], tag_send.at[number], tag_recv.at[number])
        for number, target in enumerate(others)
    ]
    for copy in tag_copies:
        copy.start()
    w_in[...] = jnp.zeros_like(w_in)
    w_in[0:deep, :] = w_in_ref[...].astype(BF16)
    for number in range(bias_out_ref.shape[0]):
        line = jnp.broadcast_to(bias_out_ref[number : number + 1, :], (128, 128))
        bias_col[number * 128 : (number + 1) * 128, :] = jnp.transpose(line)
    ring_wave(1)
    x_move(1).wait_recv()
    x_move(2).start()
    x_move(0).wait_recv()
    x_move(2).wait_recv()

    def layer(number, block, inputs, weights, whole, slopes):
        there = slice(block * own_rows, (block + 1) * own_rows)
        value = jax.nn.sigmoid(
            dot_nn(inputs[there, :], weights[...]) + bias_ref[number : number + 1, :]
        )
        slopes[there, :] = value * (1.0 - value)
        whole[there, lanes_of(col)] = value.astype(BF16)
        h_start(number, block)

    outs = []

    def put(src, dst):
        copy = pltpu.make_async_copy(src, dst, out_sems.at[len(outs)])
        copy.start()
        outs.append(copy)

    for block in range(4):
        layer(0, block, x_all, w_in, h_one, slope_one)
    put(x_all, x_out)
    put(slope_one, slope_one_out)

    def all_tags():
        return jnp.concatenate([tags[owner, 0:1, :] for owner in range(4)], axis=1)

    def own_row(line):
        line = line - col * senones
        return jnp.where(line < senones, line, -1)

    def logits(group):
        first = group * OUT_ROWS
        half = frames // 2
        for part in range(2):
            curve[first : first + OUT_ROWS, part * half : (part + 1) * half] = dot_nt(
                w_out[first : first + OUT_ROWS, :], h_two[part * half : (part + 1) * half, :]
            )
        base = lax.broadcasted_iota(jnp.int32, (16, frames), 0)

        def largest(number, top):
            row = pl.multiple_of(first + number * 16, 16)
            value = curve[pl.ds(row, 16), :] + bias_col[pl.ds(row, 16), 0:1]
            if group == OUT_GROUPS - 1:
                value = jnp.where(base + row < senones, value, -1e30)
            curve[pl.ds(row, 16), :] = value
            return jnp.maximum(top, value)

        top = lax.fori_loop(0, OUT_ROWS // 16, largest, jnp.full((16, frames), -1e30, F32))
        top = jnp.max(top, axis=0, keepdims=True)
        line = jnp.broadcast_to(own_row(all_tags()), (16, frames))

        def exponents(number, carry):
            total, picked = carry
            row = pl.multiple_of(first + number * 16, 16)
            value = curve[pl.ds(row, 16), :]
            power = jnp.exp(value - top)
            curve[pl.ds(row, 16), :] = power
            return total + power, picked + jnp.where(base + row == line, value, 0.0)

        blank = jnp.zeros((16, frames), F32)
        total, picked = lax.fori_loop(0, OUT_ROWS // 16, exponents, (blank, blank))
        sums[col, group : group + 1, :] = top
        sums[col, 4 + group : 5 + group, :] = jnp.sum(total, axis=0, keepdims=True)
        sums[col, 8 + group : 9 + group, :] = jnp.sum(picked, axis=0, keepdims=True)

    mom_copy = pltpu.make_async_remote_copy(
        src_ref=mom_ref,
        dst_ref=mom_far_ref,
        send_sem=mom_sems.at[0],
        recv_sem=mom_sems.at[1],
        device_id=across,
        device_id_type=MESH,
    )
    last_wave = RING_STARTS[-1] + STEPS
    for wave in range(2, last_wave + 1):
        ring_wave(wave)
        if 2 <= wave < 6:
            h_forward(0, wave - 2)
        if wave == LAYER_TWO_WAVE:
            for block in range(4):
                h_ready(0, block)
                layer(1, block, h_one, w_hid, h_two, slope_two)
            put(h_one, h_one_out)
            put(slope_two, slope_two_out)
            put(w_hid, w_hid_out)
        if LAYER_TWO_WAVE < wave <= LAYER_TWO_WAVE + 4:
            h_forward(1, wave - LAYER_TWO_WAVE - 1)
        for group, when in enumerate(LOGIT_WAVES):
            if wave == when:
                if group == 0:
                    for block in range(4):
                        h_ready(1, block)
                    put(h_two, h_two_out)
                    mom_copy.start()
                    for copy in tag_copies:
                        copy.wait_recv()
                rows = pl.ds(group * OUT_ROWS, OUT_ROWS)
                put(w_out.at[rows, :], w_out_out.at[rows, :])
                logits(group)

    sum_copies = [
        copy_to(target, sums.at[col], sum_send.at[number], sum_recv.at[number])
        for number, target in enumerate(others)
    ]
    for copy in sum_copies:
        copy.start()
    for copy in sum_copies:
        copy.wait_recv()

    def lines(first):
        return [sums[owner, first + group : first + group + 1, :] for owner in range(4) for group in range(4)]

    tops = lines(0)
    top = functools.reduce(jnp.maximum, tops)
    total = functools.reduce(
        jnp.add, [size * jnp.exp(own - top) for own, size in zip(tops, lines(4), strict=True)]
    )
    picked = functools.reduce(jnp.add, lines(8))
    line = all_tags()
    live = line >= 0
    loss = jnp.where(live, top + jnp.log(total) - picked, 0.0)
    loss_ref[...] = jnp.zeros_like(loss_ref)
    loss_ref[0:1, :] = functools.reduce(
        jnp.add, [loss[:, lane : lane + 128] for lane in range(0, frames, 128)]
    )
    weight = jnp.where(live, 1.0 / slot_count, 0.0)
    line = jnp.broadcast_to(own_row(line), (16, frames))
    hit_weight = jnp.broadcast_to(weight, (16, frames))
    base = lax.broadcasted_iota(jnp.int32, (16, frames), 0)
    bias_col[...] = jnp.zeros_like(bias_col)
    for group in range(OUT_GROUPS):
        share = jnp.exp(sums[col, group : group + 1, :] - top) / total * weight

        def gradient(number, carry, first=group * OUT_ROWS, share=share):
            row = pl.multiple_of(first + number * 16, 16)
            value = curve[pl.ds(row, 16), :] * share - jnp.where(base + row == line, hit_weight, 0.0)
            value = value.astype(BF16)
            dl_ref[pl.ds(row, 16), :] = value
            value = value.astype(F32)
            bias_col[pl.ds(row, 16), :] = functools.reduce(
                jnp.add, [value[:, lane : lane + 128] for lane in range(0, frames, 128)]
            )
            return carry

        lax.fori_loop(0, OUT_ROWS // 16, gradient, 0)
    bias_sum_ref[...] = jnp.zeros_like(bias_sum_ref)
    for number in range(bias_out_ref.shape[0]):
        block = jnp.transpose(bias_col[number * 128 : (number + 1) * 128, :])
        bias_sum_ref[number : number + 1, :] = jnp.sum(block, axis=0, keepdims=True)

    for group in range(len(RING_STARTS)):
        for way in range(2):
            for step in range(STEPS):
                ring_move(group, step, way).wait_send()
    for number in range(3):
        x_move(number).wait_send()
        for block in range(4):
            h_move(0, number, block).wait_send()
            h_move(1, number, block).wait_send()
    for copy in tag_copies + sum_copies:
        copy.wait_send()
    mom_copy.wait()
    for copy in outs:
        copy.wait()


def forward_pass(x, tags, w_in, w_hid, w_out, bias, bias_out, mom, slot_count):
    own_rows = x.shape[0]
    units = w_hid.shape[1]
    frames = 4 * own_rows
    wide = 4 * units
    rows = OUT_GROUPS * OUT_ROWS
    blocks = bias_out.shape[0]
    vmem = pl.BlockSpec(memory_space=pltpu.VMEM)
    hbm = pl.BlockSpec(memory_space=pl.ANY)
    sem = pltpu.SemaphoreType.DMA
    kept = (
        ((frames, 512), BF16),
        ((frames, wide), BF16),
        ((frames, wide), BF16),
        ((frames, units), F32),
        ((frames, units), F32),
        ((wide, units), BF16),
        ((rows, wide), BF16),
    )
    return pl.pallas_call(
        functools.partial(forward_kernel, slot_count),
        out_shape=tuple(jax.ShapeDtypeStruct(shape, kind) for shape, kind in kept)
        + (
            jax.ShapeDtypeStruct(mom.shape, F32),
            jax.ShapeDtypeStruct((rows, frames), BF16),
            jax.ShapeDtypeStruct((24, 128), F32),
            jax.ShapeDtypeStruct((8, 128), F32),
        ),
        in_specs=[vmem] * 7 + [hbm],
        out_specs=(hbm,) * 8 + (vmem,) * 3,
        scratch_shapes=[pltpu.VMEM(shape, kind) for shape, kind in kept[:5]]
        + [
            pltpu.VMEM((512, units), BF16),
            pltpu.VMEM((wide, units), BF16),
            pltpu.VMEM((rows, wide), BF16),
            pltpu.VMEM((rows, frames), F32),
            pltpu.VMEM((blocks * 128, 128), F32),
            pltpu.VMEM((4,) + tags.shape, jnp.int32),
            pltpu.VMEM((4, 16, frames), F32),
            sem((5, 2, STEPS)),
            sem((5, 2, STEPS)),
            sem((3,)),
            sem((3,)),
            sem((2, 3, 4)),
            sem((2, 3, 4)),
            sem((3,)),
            sem((3,)),
            sem((3,)),
            sem((3,)),
            sem((16,)),
            sem((2,)),
        ],
        compiler_params=pltpu.CompilerParams(
            collective_id=2, has_side_effects=True, vmem_limit_bytes=60 * 1024 * 1024
        ),
    )(x, tags, w_in, w_hid, w_out, bias, bias_out, mom)


DIM_BITS = (2, 4, 8)
ORDERS = ((0, 1, 2), (1, 2, 0), (2, 0, 1))
PIECES = ((0, 48), (48, 48), (96, 32))
SIZE_PIECE = 2
LIGHT_HID = 3
LIGHT_IN = 2


def stage_sends(stage, sources):
    moves = []
    for piece, order in enumerate(ORDERS):
        slot = sum(DIM_BITS[order[index]] for index in sources)
        moves.append((piece, slot, order[stage]))
    return moves


def landed(moves):
    return [(slot | DIM_BITS[dim], piece) for piece, slot, dim in moves]


FIRST = stage_sends(0, ())
SECOND = stage_sends(1, ())
SECOND_ON = stage_sends(1, (0,))
THIRD = stage_sends(2, ())
THIRD_A = stage_sends(2, (0,))
THIRD_B = stage_sends(2, (1,))
THIRD_C = stage_sends(2, (0, 1))
MOVES = FIRST + SECOND + SECOND_ON + THIRD + THIRD_A + THIRD_B + THIRD_C


def muon_kernel(
    stats_ref,
    red_hid_ref,
    mom_hid_ref,
    red_in_ref,
    mom_in_ref,
    red_far_ref,
    mom_far_ref,
    hid_ref,
    inp_ref,
    next_hid_ref,
    next_in_ref,
    norm_ref,
    codes,
    sizes,
    tops,
    lows,
    scales,
    weights,
    xs,
    us,
    vs,
    lhs,
    xin,
    xin_top,
    xin_low,
    gram,
    gram_got,
    back,
    sums,
    sums_got,
    spread_out,
    spread_got,
    spread_size_out,
    spread_size_got,
    send_sems,
    core_sems,
    recv_sems,
    back_send,
    back_recv,
    sums_send,
    sums_recv,
    spread_send,
    spread_recv,
    pair_send,
    pair_recv,
    size_send,
    size_recv,
):
    blk = lax.axis_index("blk")
    col = lax.axis_index("col")
    rows, wide = xs.shape
    height = back.shape[2]
    part_wide = inp_ref.shape[1]
    other_core = {"col": col + 1 - 2 * (col % 2)}
    dims = (
        {"blk": blk + 1 - 2 * (blk % 2)},
        {"col": (col + 2) % 4},
        {"blk": blk + 2 - 4 * ((blk // 2) % 2)},
    )
    diagonal = {"blk": 4 * (blk // 4) + 3 - blk % 4}
    barrier = pltpu.get_barrier_semaphore()
    corner = {"col": (col + 2) % 4 + 1 - 2 * (col % 2)}
    cols = (other_core, dims[1], corner)
    for target in (*cols, *({"blk": (blk + away) % 8} for away in range(1, 8))):
        pl.semaphore_signal(barrier, inc=1, device_id=target, device_id_type=MESH)

    def fold(values):
        line = jnp.sum(values, axis=0, keepdims=True)
        return sum(line[:, lane : lane + 128] for lane in range(0, line.shape[1], 128))

    share = 0.125
    sums[blk, 0:1, :] = fold(stats_ref[...])
    sums[blk, 1:2, :] = fold(mom_hid_ref[...] * mom_hid_ref[...])
    sums[blk, 2:3, :] = fold(mom_hid_ref[...] * red_hid_ref[...])
    sums[blk, 3:4, :] = fold(red_hid_ref[...] * red_hid_ref[...])
    sums[blk, 4:5, :] = fold(mom_in_ref[...] * mom_in_ref[...]) * share
    sums[blk, 5:6, :] = fold(mom_in_ref[...] * red_in_ref[...]) * share
    sums[blk, 6:7, :] = fold(red_in_ref[...] * red_in_ref[...]) * share
    sums[blk, 7:8, :] = jnp.zeros((1, 128), F32)
    eye = lax.broadcasted_iota(jnp.int32, (rows, rows), 0) == lax.broadcasted_iota(
        jnp.int32, (rows, rows), 1
    )
    pl.semaphore_wait(barrier, 10)

    def tell(own, targets, first):
        copies = []
        for number, target in enumerate(targets, start=first):
            copies.append(
                pltpu.make_async_remote_copy(
                    src_ref=own,
                    dst_ref=own,
                    send_sem=sums_send.at[number],
                    recv_sem=sums_recv.at[number],
                    device_id=target,
                    device_id_type=MESH,
                )
            )
            copies[-1].start()
        for copy in copies:
            copy.wait_recv()
        return copies

    told = tell(sums.at[blk], [{"blk": (blk + away) % 8} for away in range(1, 8)], 0)
    sums_got[col] = functools.reduce(jnp.add, [sums[number] for number in range(8)])
    told += tell(sums_got.at[col], cols, 7)
    whole = functools.reduce(jnp.add, [sums_got[number] for number in range(4)])
    whole = jnp.sum(whole, axis=1, keepdims=True)
    clip = jnp.sqrt(whole[0:1])
    factor = jnp.minimum(1.0, CLIP / clip)

    def norm_of(first):
        square = (
            0.25 * whole[first : first + 1]
            + factor * whole[first + 1 : first + 2]
            + factor * factor * whole[first + 2 : first + 3]
        )
        return 1.0 / (jnp.sqrt(jnp.maximum(square, 0.0)) + 1e-07)

    norm_ref[0:4, :] = jnp.broadcast_to(clip, (4, 128))
    norm_ref[4:8, :] = jnp.broadcast_to(factor, (4, 128))
    next_hid_ref[...] = 0.5 * mom_hid_ref[...] + factor * red_hid_ref[...]
    next_in_ref[...] = 0.5 * mom_in_ref[...] + factor * red_in_ref[...]

    my_lanes = pl.ds(pl.multiple_of(blk * height, height), height)
    for number in range(4):
        there = slice(number * rows, (number + 1) * rows)
        value = next_hid_ref[there, :]
        largest = jnp.maximum(jnp.max(jnp.abs(value), axis=1, keepdims=True), 1e-30)
        spread_out[number] = to_codes(value * (TOP_CODE / largest))
        line = jnp.sum(jnp.where(eye, largest, 0.0), axis=0, keepdims=True)
        spread_size_out[number] = jnp.broadcast_to(line * (1.0 / TOP_CODE), (8, rows))
    spread = []
    for away in range(1, 8):
        target = (blk + away) % 8
        for kind, (src, dst) in enumerate(
            ((spread_out, spread_got), (spread_size_out, spread_size_got))
        ):
            spread.append(
                pltpu.make_async_remote_copy(
                    src_ref=src.at[target % 4],
                    dst_ref=dst.at[blk],
                    send_sem=spread_send.at[kind, away - 1],
                    recv_sem=spread_recv.at[kind, away - 1],
                    device_id={"blk": target},
                    device_id_type=MESH,
                )
            )
            spread[-1].start()
    high = col // 2
    my_half = pl.ds(pl.multiple_of(high * part_wide, part_wide), part_wide)
    far_half = pl.ds(pl.multiple_of((1 - high) * part_wide, part_wide), part_wide)
    in_scale = norm_of(4)
    xin[:, my_half] = next_in_ref[...] * in_scale
    xin[:, far_half] = (0.5 * mom_far_ref[...] + factor * red_far_ref[...]) * in_scale
    spread_got[blk] = spread_out[blk % 4]
    spread_size_got[blk] = spread_size_out[blk % 4]
    for copy in spread:
        copy.wait_recv()
    hid_scale = norm_of(1)
    for number in range(8):
        size = jnp.broadcast_to(spread_size_got[number, 0:1, :], (rows, rows))
        size = jnp.transpose(size) * hid_scale
        for lane in range(0, height, 128):
            xs[:, number * height + lane : number * height + lane + 128] = (
                from_codes(spread_got[number, :, lane : lane + 128]) * size
            )

    numbers = {move: number for number, move in enumerate(MOVES)}

    def part(turn, slot, piece):
        first, count = PIECES[piece]
        return codes.at[turn, slot, pl.ds(first, count), :]

    def send(turn, move):
        piece, slot, dim = move
        there = slot | DIM_BITS[dim]
        copies = [
            pltpu.make_async_remote_copy(
                src_ref=part(turn, slot, piece),
                dst_ref=part(turn, there, piece),
                send_sem=send_sems.at[numbers[move]],
                recv_sem=recv_sems.at[turn, there, piece],
                device_id=dims[dim],
                device_id_type=MESH,
            )
        ]
        if piece == SIZE_PIECE:
            copies.append(
                pltpu.make_async_remote_copy(
                    src_ref=sizes.at[turn, slot],
                    dst_ref=sizes.at[turn, there],
                    send_sem=size_send.at[numbers[move]],
                    recv_sem=size_recv.at[turn, there],
                    device_id=dims[dim],
                    device_id_type=MESH,
                )
            )
        return copies

    def send_all(turn, moves):
        for move in moves:
            for copy in send(turn, move):
                copy.start()

    def to_core(turn, slot, piece):
        copies = [
            pltpu.make_async_remote_copy(
                src_ref=part(turn, slot, piece),
                dst_ref=part(turn, slot + 1, piece),
                send_sem=core_sems.at[slot // 2, piece],
                recv_sem=recv_sems.at[turn, slot + 1, piece],
                device_id=other_core,
                device_id_type=MESH,
            )
        ]
        if piece == SIZE_PIECE:
            copies.append(
                pltpu.make_async_remote_copy(
                    src_ref=sizes.at[turn, slot],
                    dst_ref=sizes.at[turn, slot + 1],
                    send_sem=core_sems.at[slot // 2, 3],
                    recv_sem=size_recv.at[turn, slot + 1],
                    device_id=other_core,
                    device_id_type=MESH,
                )
            )
        return copies

    def arrived(turn, slot, piece):
        def wait(ref, sem):
            pltpu.make_async_remote_copy(
                src_ref=ref,
                dst_ref=ref,
                send_sem=core_sems.at[0, 0],
                recv_sem=sem,
                device_id=other_core,
                device_id_type=MESH,
            ).wait_recv()

        wait(part(turn, slot, piece), recv_sems.at[turn, slot, piece])
        if piece == SIZE_PIECE:
            wait(sizes.at[turn, slot], size_recv.at[turn, slot])

    def forward(turn, moves, on=()):
        for number, (slot, piece) in enumerate(landed(moves)):
            arrived(turn, slot, piece)
            for copy in to_core(turn, slot, piece):
                copy.start()
            if on:
                send_all(turn, on[number : number + 1])

    def gram_copy():
        return pltpu.make_async_remote_copy(
            src_ref=gram,
            dst_ref=gram_got,
            send_sem=pair_send.at[1],
            recv_sem=pair_recv.at[1],
            device_id=other_core,
            device_id_type=MESH,
        )

    def unpack(turn, index, pair, light):
        for core in range(2):
            here = pl.ds(pl.multiple_of(index * 2 * rows + core * rows, rows), rows)
            slot = 2 * pair + core
            if light:
                tops[here, :] = from_codes(codes[turn, slot]).astype(BF16)
            else:
                top, low = halves(from_codes(codes[turn, slot]))
                tops[here, :] = top
                lows[here, :] = low
            size = sizes[turn, slot]
            scales[:, here] = size * size

    def inner(first, count, light):
        here = pl.ds(first, count)
        if light:
            values = dot_nt(lhs[0:rows, :], tops[here, :])
            weights[0:rows, here] = (values * scales[0:1, here]).astype(BF16)
        else:
            both = dot_nt(lhs[...], tops[here, :])
            values = both[:rows] + both[rows:] + dot_nt(lhs[0:rows, :], lows[here, :])
            top, low = halves(values * scales[0:1, here])
            weights[0:rows, here] = top
            weights[rows:, here] = low

    def outer(first, count, out, add, light):
        cut = 512
        here = slice(first, first + count)
        for start in range(0, wide, cut):
            lanes = slice(start, start + cut)
            if light:
                value = dot_nn(weights[0:rows, here], tops[here, lanes])
            else:
                both = dot_nn(weights[:, here], tops[here, lanes])
                value = both[:rows] + both[rows:] + dot_nn(weights[0:rows, here], lows[here, lanes])
            if add:
                value = value + out[:, lanes]
            out[:, lanes] = value

    def set_lhs(values):
        top, low = halves(values)
        lhs[0:rows, :] = top
        lhs[rows:, :] = low

    def input_gram(light):
        top, low = halves(xin[...])
        xin_top[...] = top
        if light:
            gram[...] = dot_nt(xin_top[...], xin_top[...])
        else:
            xin_low[...] = low
            cross = dot_nt(xin_top[...], xin_low[...])
            gram[...] = dot_nt(xin_top[...], xin_top[...]) + (cross + jnp.transpose(cross))
        gram_copy().start()

    def input_step(light):
        gram_copy().wait()
        square_of = gram[...] + gram_got[...]
        top, low = halves(square_of)
        if light:
            poly = NS_B * square_of + NS_C * dot_nn(top, top)
        else:
            cross = dot_nn(top, low)
            poly = NS_B * square_of + NS_C * (dot_nn(top, top) + (cross + jnp.transpose(cross)))
        top, low = halves(poly)
        cut = 512
        for start in range(0, xin.shape[1], cut):
            lanes = slice(start, start + cut)
            change = dot_nn(top, xin_top[:, lanes])
            if not light:
                change = change + dot_nn(low, xin_top[:, lanes]) + dot_nn(top, xin_low[:, lanes])
            xin[:, lanes] = NS_A * xin[:, lanes] + change

    def by_weight(number, limit, work):
        @pl.when(number < limit)
        def _():
            work(True)

        @pl.when(number >= limit)
        def _():
            work(False)

    def iteration(number, carry):
        turn = number % 2
        values = xs[...]
        largest = jnp.maximum(jnp.max(jnp.abs(values), axis=1, keepdims=True), 1e-30)
        codes[turn, 0] = to_codes(values * (TOP_CODE / largest))
        lane_size = jnp.sum(jnp.where(eye, largest, 0.0), axis=0, keepdims=True)
        sizes[turn, 0] = jnp.broadcast_to(lane_size * (1.0 / TOP_CODE), (8, rows))
        send_all(turn, FIRST)
        for piece in range(3):
            for copy in to_core(turn, 0, piece):
                copy.start()
        send_all(turn, SECOND)
        set_lhs(values)

        def first_pass(index, carry):
            pair = index + (index // 3) * (1 - index // 4) - (index // 4) * (1 - index // 5)

            @pl.when(index == 1)
            def _():
                forward(turn, FIRST, SECOND_ON)
                send_all(turn, THIRD)
                send_all(turn, THIRD_A)

                by_weight(number, LIGHT_IN, input_gram)

                forward(turn, SECOND, THIRD_B)
                forward(turn, SECOND_ON, THIRD_C)

                by_weight(number, LIGHT_IN, input_step)

                forward(turn, THIRD)

            @pl.when(index == 4)
            def _():
                forward(turn, THIRD_A)
                forward(turn, THIRD_B)

            @pl.when(index == 7)
            def _():
                forward(turn, THIRD_C)

            for piece in range(3):
                arrived(turn, 2 * pair + 1, piece)

            def work(light):
                unpack(turn, index, pair, light)
                inner(pl.multiple_of(index * 2 * rows, 2 * rows), 2 * rows, light)

            by_weight(number, LIGHT_HID, work)

            @pl.when(index == 3)
            def _():
                by_weight(number, LIGHT_HID, lambda light: outer(0, wide // 2, us, False, light))

            return carry

        lax.fori_loop(0, 8, first_pass, 0)

        def second_pass(light):
            outer(wide // 2, wide // 2, us, True, light)
            set_lhs(us[...])
            for first in range(0, wide, 512):
                inner(first, 512, light)
            outer(0, wide, vs, False, light)

        by_weight(number, LIGHT_HID, second_pass)
        xs[...] = NS_A * xs[...] + NS_B * us[...] + NS_C * vs[...]
        for move in MOVES:
            for copy in send(turn, move):
                copy.wait_send()
        for pair in range(8):
            for piece in range(3):
                for copy in to_core(turn, 2 * pair, piece):
                    copy.wait_send()
        return carry

    lax.fori_loop(0, NS, iteration, 0)

    place = blk % 4
    copies = []
    for rel, target in ((1, dims[0]), (2, dims[2]), (3, diagonal)):
        copies.append(
            pltpu.make_async_remote_copy(
                src_ref=xs.at[:, pl.ds(pl.multiple_of(target["blk"] * height, height), height)],
                dst_ref=back.at[place],
                send_sem=back_send.at[rel - 1],
                recv_sem=back_recv.at[rel - 1],
                device_id=target,
                device_id_type=MESH,
            )
        )
        copies[-1].start()
    hid_ref[place] = xs[:, my_lanes]
    inp_ref[...] = xin[:, my_half]
    for copy in copies:
        copy.wait_recv()
    for target in (dims[0], dims[2], diagonal):
        other = target["blk"] % 4
        hid_ref[other] = back[other]
    for copy in copies + spread + told:
        copy.wait_send()


def muon(stats, red_hid, mom_hid, red_in, mom_in, red_far, mom_far, wide):
    rows = red_hid.shape[0] // 4
    height = red_hid.shape[1]
    deep, part_wide = red_in.shape
    vmem = pl.BlockSpec(memory_space=pltpu.VMEM)
    sem = pltpu.SemaphoreType.DMA
    return pl.pallas_call(
        muon_kernel,
        out_shape=(
            jax.ShapeDtypeStruct((4, rows, height), F32),
            jax.ShapeDtypeStruct((deep, part_wide), F32),
            jax.ShapeDtypeStruct(red_hid.shape, F32),
            jax.ShapeDtypeStruct(red_in.shape, F32),
            jax.ShapeDtypeStruct((8, 128), F32),
        ),
        in_specs=[vmem] * 7,
        out_specs=(vmem,) * 5,
        scratch_shapes=[
            pltpu.VMEM((2, 16, rows, wide), I16),
            pltpu.VMEM((2, 16, 8, rows), F32),
            pltpu.VMEM((wide, wide), BF16),
            pltpu.VMEM((wide, wide), BF16),
            pltpu.VMEM((8, wide), F32),
            pltpu.VMEM((2 * rows, wide), BF16),
            pltpu.VMEM((rows, wide), F32),
            pltpu.VMEM((rows, wide), F32),
            pltpu.VMEM((rows, wide), F32),
            pltpu.VMEM((2 * rows, wide), BF16),
            pltpu.VMEM((deep, 2 * part_wide), F32),
            pltpu.VMEM((deep, 2 * part_wide), BF16),
            pltpu.VMEM((deep, 2 * part_wide), BF16),
            pltpu.VMEM((deep, deep), F32),
            pltpu.VMEM((deep, deep), F32),
            pltpu.VMEM((4, rows, height), F32),
            pltpu.VMEM((8, 8, 128), F32),
            pltpu.VMEM((4, 8, 128), F32),
            pltpu.VMEM((4, rows, height), I16),
            pltpu.VMEM((8, rows, height), I16),
            pltpu.VMEM((4, 8, rows), F32),
            pltpu.VMEM((8, 8, rows), F32),
            sem((len(MOVES),)),
            sem((8, 4)),
            sem((2, 16, 3)),
            sem((3,)),
            sem((3,)),
            sem((10,)),
            sem((10,)),
            sem((2, 7)),
            sem((2, 7)),
            sem((2,)),
            sem((2,)),
            sem((len(MOVES),)),
            sem((2, 16)),
        ],
        compiler_params=pltpu.CompilerParams(
            collective_id=0, has_side_effects=True, vmem_limit_bytes=60 * 1024 * 1024
        ),
    )(stats, red_hid, mom_hid, red_in, mom_in, red_far, mom_far)


def plain_body(
    frames,
    labels,
    mask,
    w_input,
    w_hidden,
    w_output,
    biases,
    mom_input,
    mom_hidden,
    out_first,
    out_second,
    bias_first,
    bias_second,
    res_input,
    res_hidden,
    res_output,
):
    ncol = lax.axis_size("col")
    nblk = lax.axis_size("blk")
    col_index = lax.axis_index("col")
    hcol = w_input.shape[1]
    scol = w_output.shape[1]
    micro = frames.shape[0]
    slot_count = frames.shape[1] * micro * nblk * ncol
    bias_row = biases[0]
    b_one = bias_row[:hcol]
    b_two = bias_row[hcol : 2 * hcol]
    b_out = bias_row[2 * hcol :]
    low_input = w_input.astype(jnp.bfloat16)
    row_tags = jnp.where(mask > 0, labels, -1)
    grad_input = jnp.zeros(w_input.shape, jnp.float32)
    grad_hidden = jnp.zeros((w_hidden.shape[0] * nblk, hcol), jnp.float32)
    grad_output = jnp.zeros((w_output.shape[0] * nblk, scol), jnp.float32)
    grad_bias = jnp.zeros(bias_row.shape, jnp.float32)
    loss_local = jnp.zeros((), jnp.float32)
    for micro_step in range(micro):
        low_hidden, low_output = (
            lax.all_gather(w_hidden.astype(jnp.bfloat16), "blk", axis=0, tiled=True),
            lax.all_gather(w_output.astype(jnp.bfloat16), "blk", axis=0, tiled=True),
        )
        inputs = lax.all_gather(frames[micro_step], "col", axis=0, tiled=True)
        tags_group = lax.all_gather(row_tags[micro_step], "col", axis=0, tiled=True)
        sig_one = jax.nn.sigmoid(matmul(inputs, low_input) + b_one)
        h_one = spread_cols(sig_one.astype(jnp.bfloat16))
        sig_two = jax.nn.sigmoid(matmul(h_one, low_hidden) + b_two)
        h_two = spread_cols(sig_two.astype(jnp.bfloat16))
        logits = matmul(h_two, low_output) + b_out
        row_top = lax.pmax(jnp.max(logits, axis=1), "col")
        exponent = jnp.exp(logits - row_top[:, None])
        target_hit = jnp.arange(scol)[None, :] == (tags_group - col_index * scol)[:, None]
        row_total, picked = lax.psum(
            (jnp.sum(exponent, axis=1), jnp.sum(jnp.where(target_hit, logits, 0.0), axis=1)), "col"
        )
        live_rows = tags_group >= 0
        loss_local = loss_local + jnp.sum(
            jnp.where(live_rows, row_top + jnp.log(row_total) - picked, 0.0)
        )
        probs = exponent / row_total[:, None]
        d_logits = (
            jnp.where(live_rows[:, None], probs - target_hit.astype(jnp.float32), 0.0) / slot_count
        ).astype(jnp.bfloat16)
        grad_output = grad_output + inner_rows(h_two, d_logits)
        d_h_two = reduce_cols(outer_cols(d_logits, low_output))
        d_z_two = (d_h_two * sig_two * (1.0 - sig_two)).astype(jnp.bfloat16)
        grad_hidden = grad_hidden + inner_rows(h_one, d_z_two)
        d_h_one = reduce_cols(outer_cols(d_z_two, low_hidden))
        d_z_one = (d_h_one * sig_one * (1.0 - sig_one)).astype(jnp.bfloat16)
        grad_input = grad_input + inner_rows(inputs, d_z_one)
        grad_bias = grad_bias + jnp.concatenate(
            [
                jnp.sum(d_z_one.astype(jnp.float32), axis=0),
                jnp.sum(d_z_two.astype(jnp.float32), axis=0),
                jnp.sum(d_logits.astype(jnp.float32), axis=0),
            ]
        )
    q_input, next_res_input = squash(grad_input, res_input[0])
    q_hidden, next_res_hidden = squash(grad_hidden, res_hidden[0])
    q_output, next_res_output = squash(grad_output, res_output[0])
    red_hidden, red_output = (
        lax.psum_scatter(q_hidden, "blk", scatter_dimension=0, tiled=True),
        lax.psum_scatter(q_output, "blk", scatter_dimension=0, tiled=True),
    )
    red_input, red_bias, loss_sum = lax.psum((q_input, grad_bias, loss_local), "blk")
    share_blk = 1.0 / nblk
    grad_square = (
        share_blk * (jnp.sum(red_input * red_input) + jnp.sum(red_bias * red_bias))
        + jnp.sum(red_hidden * red_hidden)
        + jnp.sum(red_output * red_output)
    )
    clip_norm = jnp.sqrt(lax.psum(grad_square, ("blk", "col")))
    factor = jnp.minimum(1.0, CLIP / clip_norm)
    next_mom_input = 0.5 * mom_input + factor * red_input
    next_mom_hidden = 0.5 * mom_hidden + factor * red_hidden
    square_input, square_hidden = lax.psum(
        (
            share_blk * jnp.sum(next_mom_input * next_mom_input),
            jnp.sum(next_mom_hidden * next_mom_hidden),
        ),
        ("blk", "col"),
    )
    iter_input = next_mom_input / (jnp.sqrt(square_input) + 1e-07)
    iter_hidden = next_mom_hidden / (jnp.sqrt(square_hidden) + 1e-07)
    for turn_index in range(NS):
        rows_hidden = collect_rows(iter_hidden)
        gram_input, gram_hidden = lax.psum(
            (precise(iter_input, iter_input.T), precise(iter_hidden, rows_hidden.T)), "col"
        )
        image_input = precise(gram_input, iter_input)
        image_hidden = precise(gram_hidden, rows_hidden)
        iter_input = (
            NS_A * iter_input + NS_B * image_input + NS_C * precise(gram_input, image_input)
        )
        iter_hidden = (
            NS_A * iter_hidden
            + NS_B * image_hidden
            + NS_C * precise(gram_hidden, collect_rows(image_hidden))
        )
    muon_scale = LR_MUON * 0.2 * math.sqrt(hcol * ncol)
    new_input = w_input * (1.0 - LR_MUON * WD_MUON) - muon_scale * iter_input
    new_hidden = w_hidden * (1.0 - LR_MUON * WD_MUON) - muon_scale * iter_hidden
    new_output, next_out_first, next_out_second = adam_step(
        w_output, factor * red_output, out_first, out_second
    )
    new_biases, next_bias_first, next_bias_second = adam_step(
        biases, factor * red_bias[None, :], bias_first, bias_second
    )
    return (
        loss_sum,
        clip_norm,
        new_input,
        new_hidden,
        new_output,
        new_biases,
        next_mom_input,
        next_mom_hidden,
        next_out_first,
        next_out_second,
        next_bias_first,
        next_bias_second,
        next_res_input[None],
        next_res_hidden[None],
        next_res_output[None],
    )


def fast_body(
    frames,
    labels,
    mask,
    w_input,
    w_hidden,
    w_output,
    biases,
    mom_input,
    mom_hidden,
    out_first,
    out_second,
    bias_first,
    bias_second,
    res_input,
    res_hidden,
    res_output,
):
    ncol = lax.axis_size("col")
    nblk = lax.axis_size("blk")
    col_index = lax.axis_index("col")
    blk_index = lax.axis_index("blk")
    hcol = w_input.shape[1]
    scol = w_output.shape[1]
    micro = frames.shape[0]
    slot_count = frames.shape[1] * micro * nblk * ncol
    bias_row = biases[0]
    deep = w_input.shape[0]
    padded = 512
    rows_out = OUT_GROUPS * OUT_ROWS
    mom_in_padded = jnp.pad(mom_input, ((0, padded - deep), (0, 0)))
    own_tags = jnp.where(mask > 0, labels, -1).reshape(1, -1)
    layer_biases = jnp.pad(bias_row[: 2 * hcol].reshape(2, hcol), ((0, 6), (0, 0)))
    blocks = -(-rows_out // 128)
    out_biases = jnp.pad(bias_row[2 * hcol :], (0, blocks * 128 - scol)).reshape(blocks, 128)
    inputs, h_one, h_two, slope_one, slope_two, low_hidden, low_output, mom_far, d_logits, bias_sums, losses = (
        forward_pass(
            frames.reshape(-1, deep),
            jnp.broadcast_to(own_tags, (8, own_tags.shape[1])),
            w_input,
            w_hidden,
            w_output.T,
            layer_biases,
            out_biases,
            mom_in_padded,
            slot_count,
        )
    )
    loss_local = jnp.sum(losses)
    partial = inner_rows(d_logits, low_output)
    vec = jnp.concatenate([jnp.zeros((2 * hcol,), F32), bias_sums.reshape(-1)[:scol], loss_local[None]])
    vec = jnp.pad(vec, (0, 4096 - vec.shape[0])).reshape(32, 128)
    next_out, next_hid, next_in, red_out, red_hid, red_in, red_far, vec_sum, stats = reduce_grads(
        d_logits,
        h_two,
        h_one,
        inputs,
        partial,
        slope_two,
        slope_one,
        low_hidden,
        res_output[0].T,
        res_hidden[0].T,
        jnp.pad(res_input[0], ((0, padded - deep), (0, 0))).T,
        jnp.pad(res_output[0, :, scol // 16 * 16 :], ((0, 0), (0, 16 - scol % 16))).T,
        vec,
        scol,
        deep,
    )
    next_res_output = next_out.transpose(1, 2, 0)
    next_res_hidden = next_hid.T
    next_res_input = next_in[:, :deep].T
    red_output = red_out[:scol].T
    vec_sum = vec_sum.reshape(-1)
    red_bias = vec_sum[: bias_row.shape[0]]
    loss_sum = vec_sum[bias_row.shape[0]]
    done_hidden, done_input, mom_hid_next, mom_in_next, norms = muon(
        stats,
        red_hid,
        mom_hidden.T,
        red_in,
        mom_in_padded,
        red_far,
        mom_far,
        hcol * ncol,
    )
    clip_norm = norms[0, 0]
    factor = norms[4, 0]
    next_mom_hidden = mom_hid_next.T
    next_mom_input = mom_in_next[:deep]
    done_hidden = done_hidden.reshape(hcol, w_hidden.shape[0]).T
    muon_scale = LR_MUON * 0.2 * math.sqrt(hcol * ncol)
    new_input = w_input * (1.0 - LR_MUON * WD_MUON) - muon_scale * done_input[:deep]
    new_hidden = w_hidden * (1.0 - LR_MUON * WD_MUON) - muon_scale * done_hidden
    new_output, next_out_first, next_out_second = adam_step(
        w_output, factor * red_output, out_first, out_second
    )
    new_biases, next_bias_first, next_bias_second = adam_step(
        biases, factor * red_bias[None, :], bias_first, bias_second
    )
    return (
        loss_sum,
        clip_norm,
        new_input,
        new_hidden,
        new_output,
        new_biases,
        next_mom_input,
        next_mom_hidden,
        next_out_first,
        next_out_second,
        next_bias_first,
        next_bias_second,
        next_res_input[None],
        next_res_hidden[None],
        next_res_output,
    )


def solution(mesh):
    in_specs = (
        P(None, ("blk", "col"), None),
        P(None, ("blk", "col")),
        P(None, ("blk", "col")),
        P(None, "col"),
        P("blk", "col"),
        P("blk", "col"),
        P("col", None),
        P(None, "col"),
        P("blk", "col"),
        P("blk", "col"),
        P("blk", "col"),
        P("col", None),
        P("col", None),
        P("blk", None, "col"),
        P("blk", None, "col"),
        P("blk", None, "col"),
    )
    out_specs = (
        P(),
        P(),
        P(None, "col"),
        P("blk", "col"),
        P("blk", "col"),
        P("col", None),
        P(None, "col"),
        P("blk", "col"),
        P("blk", "col"),
        P("blk", "col"),
        P("col", None),
        P("col", None),
        P("blk", None, "col"),
        P("blk", None, "col"),
        P("blk", None, "col"),
    )
    cubes = mesh.shape["blk"] == 8 and mesh.shape["col"] == 4
    body = fast_body if cubes else plain_body
    return jax.shard_map(body, mesh=mesh, in_specs=in_specs, out_specs=out_specs, check_vma=False)
```

```python
import functools
import math

import jax
import jax.numpy as jnp
from jax import lax
from jax.experimental import pallas as pl
from jax.experimental.pallas import tpu as pltpu
from jax.sharding import PartitionSpec as P

NS = 5
STEP = 5


NS_A = 3.4445
NS_B = -4.775
NS_C = 2.0315
CLIP = 0.002
LR_MUON = 0.1
WD_MUON = 0.01
LR_ADAM = 0.03
WD_ADAM = 0.1

MESH = pl.DeviceIdType.MESH
F32 = jnp.float32
BF16 = jnp.bfloat16
I16 = jnp.int16
LN2 = math.log(2.0)
TOP_CODE = 32700.0
LEVELS = 64.0


def matmul(left_side, right_side):
    return jnp.dot(left_side, right_side, preferred_element_type=jnp.float32)


def inner_rows(left_side, right_side):
    return lax.dot_general(
        left_side, right_side, (((0,), (0,)), ((), ())), preferred_element_type=jnp.float32
    )


def outer_cols(left_side, right_side):
    return lax.dot_general(
        left_side, right_side, (((1,), (1,)), ((), ())), preferred_element_type=jnp.float32
    )


def precise(left_side, right_side):
    return jnp.dot(
        left_side, right_side, precision=lax.Precision.HIGHEST, preferred_element_type=jnp.float32
    )


def spread_cols(values):
    return lax.all_gather(values, "col", axis=1, tiled=True)


def reduce_cols(values):
    return lax.psum_scatter(values, "col", scatter_dimension=1, tiled=True)


def collect_rows(values):
    return lax.all_gather(values, "blk", axis=0, tiled=True)


def squash(gradient, resid):
    value = gradient + resid.astype(jnp.float32)
    scale = jnp.mean(jnp.abs(value), axis=0, keepdims=True) + 1e-12
    signed = scale * jnp.tanh(2.0 * value / scale)
    return (signed, value - signed)


def adam_step(weight, gradient, first, second):
    first = 0.5 * first + 0.5 * gradient
    second = 0.95 * second + 0.05 * gradient * gradient
    update = first / (1.0 - 0.5**STEP) / (jnp.sqrt(second / (1.0 - 0.95**STEP)) + 1e-08)
    return (weight - LR_ADAM * (update + WD_ADAM * weight), first, second)


def halves(values):
    top = values.astype(BF16)
    return top, (values - top.astype(F32)).astype(BF16)


def dot_nn(left_side, right_side):
    return lax.dot_general(
        left_side, right_side, (((1,), (0,)), ((), ())), preferred_element_type=F32
    )


def dot_nt(left_side, right_side):
    return lax.dot_general(
        left_side, right_side, (((1,), (1,)), ((), ())), preferred_element_type=F32
    )


RING = 8
STEPS = RING - 1
OUT_ROWS = 592
OUT_GROUPS = 4
HID_ROWS = 512
HID_GROUP = 4
IN_GROUP = 5
TURN_AT = 5
CROSS_AT = 6
HID_AT = 13
FINISH_AT = 14
IN_AT = 20
HID_HOP = 3


def ring_place(blk):
    odd = blk % 2
    return (blk // 2) * (1 - odd) + (7 - blk // 2) * odd


def ring_blk(place):
    back = place // 4
    return 2 * place * (1 - back) + (15 - 2 * place) * back


def scale_code(size):
    return jnp.ceil(jnp.log(jnp.maximum(size, 1e-30)) * (LEVELS / LN2))


def code_scale(code):
    return jnp.exp(code * (LN2 / LEVELS))


def to_codes(values):
    return jnp.round(values).astype(jnp.int32).astype(I16)


def from_codes(codes):
    return codes.astype(jnp.int32).astype(F32)


def chunk_of(lane):
    number = lane // 256
    return number // 2 if number % 2 == 0 else 7 - number // 2


def squash_kernel(senones, dl_ref, h_ref, res_ref, next_ref, codes_ref, size_ref, grad, cols, marks):
    group = pl.program_id(0)
    rows, wide = grad.shape
    valid = senones - group * rows
    for first, count in ((0, rows // 32 * 16), (rows // 32 * 16, rows - rows // 32 * 16)):
        there = slice(first, first + count)
        total = jnp.zeros((count, 128), F32)
        for lane in range(0, wide, 512):
            value = dot_nn(dl_ref[there, :], h_ref[:, lane : lane + 512])
            value = value + res_ref[there, lane : lane + 512].astype(F32)
            row = first + lax.broadcasted_iota(jnp.int32, value.shape, 0)
            value = jnp.where(row < valid, value, 0.0)
            grad[there, lane : lane + 512] = value
            value = jnp.abs(value)
            for part in range(0, 512, 128):
                total = total + value[:, part : part + 128]
        size = jnp.sum(total, axis=1, keepdims=True) * (1.0 / wide) + 1e-12
        size = jnp.broadcast_to(size, (count, 128))
        marks[there, :] = size
        cols[0, there, :] = size
        cols[1, there, :] = 2.0 / size

    def some(number, carry):
        row = pl.multiple_of(number * 16, 16)
        size = cols[0, pl.ds(row, 16), :]
        steep = cols[1, pl.ds(row, 16), :]
        for lane in range(0, wide, 128):
            piece = grad[pl.ds(row, 16), lane : lane + 128]
            curve = jnp.tanh(piece * steep)
            codes_ref[0, 2 * chunk_of(lane) + lane // 128 % 2, pl.ds(row, 16), :] = to_codes(
                curve * TOP_CODE
            )
            next_ref[pl.ds(row, 16), 0, lane : lane + 128] = piece - size * curve
        return carry

    lax.fori_loop(0, rows // 16, some, 0)
    marks[rows:, :] = jnp.zeros((marks.shape[0] - rows, 128), F32)
    lines = [jnp.transpose(marks[first : first + 128, :])[0:1, :] for first in range(0, rows, 128)]
    lines.append(jnp.zeros((8 - len(lines), 128), F32))
    size_ref[0] = jnp.concatenate(lines, axis=0)


def squash_out(dl, h_two, res_out):
    senones, wide = res_out.shape
    frames = dl.shape[1]
    return pl.pallas_call(
        functools.partial(squash_kernel, senones),
        grid=(OUT_GROUPS,),
        out_shape=(
            jax.ShapeDtypeStruct((senones, 1, wide), F32),
            jax.ShapeDtypeStruct((OUT_GROUPS, 2 * RING, OUT_ROWS, 128), I16),
            jax.ShapeDtypeStruct((OUT_GROUPS, 8, 128), F32),
        ),
        in_specs=[
            pl.BlockSpec((OUT_ROWS, frames), lambda group: (group, 0)),
            pl.BlockSpec((frames, wide), lambda group: (0, 0)),
            pl.BlockSpec((OUT_ROWS, wide), lambda group: (group, 0)),
        ],
        out_specs=(
            pl.BlockSpec((OUT_ROWS, 1, wide), lambda group: (group, 0, 0)),
            pl.BlockSpec((1, 2 * RING, OUT_ROWS, 128), lambda group: (group, 0, 0, 0)),
            pl.BlockSpec((1, 8, 128), lambda group: (group, 0, 0)),
        ),
        scratch_shapes=[
            pltpu.VMEM((OUT_ROWS, wide), F32),
            pltpu.VMEM((2, OUT_ROWS, 128), F32),
            pltpu.VMEM((640, 128), F32),
        ],
        compiler_params=pltpu.CompilerParams(vmem_limit_bytes=60 * 1024 * 1024),
    )(dl, h_two, res_out)


def reduce_kernel(
    deep,
    senones,
    codes_ref,
    sizes_ref,
    h_one_ref,
    x_ref,
    part_ref,
    slope_two_ref,
    slope_one_ref,
    w_hid_ref,
    res_hid_ref,
    res_in_ref,
    vec_ref,
    next_hid_ref,
    next_in_ref,
    red_out_ref,
    red_hid_ref,
    red_in_ref,
    red_far_ref,
    vec_sum_ref,
    stats_ref,
    grad,
    res_buf,
    h_buf,
    slope_buf,
    marks,
    cols,
    keep_sums,
    dz,
    dz_two,
    dz_one,
    core_out,
    core_got,
    far_out,
    far_got,
    own_out,
    got_out,
    own_hid,
    got_hid,
    own_in,
    got_in,
    share_in,
    share_far,
    sizes,
    shares,
    vec,
    vecs,
    res_sems,
    load_sems,
    code_sems,
    slope_sems,
    core_send,
    core_recv,
    far_send,
    far_recv,
    out_send,
    out_recv,
    hid_send,
    hid_recv,
    in_send,
    in_recv,
    share_send,
    share_recv,
    vec_send,
    vec_recv,
    size_send,
    size_recv,
    share_far_send,
    share_far_recv,
):
    blk = lax.axis_index("blk")
    col = lax.axis_index("col")
    here = ring_place(blk)
    core, high = col % 2, col // 2
    cores = {"col": col + 1 - 2 * core}
    across = {"col": (col + 2) % 4}
    barrier = pltpu.get_barrier_semaphore()
    for target in (cores, across, *({"blk": (blk + away) % RING} for away in range(1, RING))):
        pl.semaphore_signal(barrier, inc=1, device_id=target, device_id_type=MESH)

    def code_copy(group):
        return pltpu.make_async_copy(codes_ref.at[group], own_out.at[group], code_sems.at[group])

    def hid_res_copy(part):
        return pltpu.make_async_copy(
            res_hid_ref.at[pl.ds(part * 256, 256), :],
            res_buf.at[part, pl.ds(0, 256), :],
            res_sems.at[part],
        )

    def hid_next_copy(part):
        return pltpu.make_async_copy(
            grad.at[pl.ds(0, 256), :], next_hid_ref.at[pl.ds(part * 256, 256), :], load_sems.at[1]
        )

    def load(src, dst):
        return pltpu.make_async_copy(src, dst, load_sems.at[0])

    for group in range(OUT_GROUPS):
        code_copy(group).start()
    for part in range(2):
        hid_res_copy(part).start()
    load(h_one_ref, h_buf).start()
    marks[...] = jnp.zeros_like(marks)
    stats_ref[...] = jnp.zeros_like(stats_ref)
    vec[...] = vec_ref[...]
    pl.semaphore_wait(barrier, RING + 1)

    CHUNK = 256
    units = slope_buf.shape[2]

    def slope_copy(layer, block):
        rows = pl.ds(pl.multiple_of(block * CHUNK, CHUNK), CHUNK)
        src = (slope_two_ref, slope_one_ref)[layer]
        return pltpu.make_async_copy(src.at[rows, :], slope_buf.at[block % 2], slope_sems.at[block % 2])

    def core_move(layer, block):
        return pltpu.make_async_remote_copy(
            src_ref=core_out.at[block % 2],
            dst_ref=core_got.at[layer, block],
            send_sem=core_send.at[block % 2],
            recv_sem=core_recv.at[layer, block],
            device_id=cores,
            device_id_type=MESH,
        )

    def far_move(layer, block):
        return pltpu.make_async_remote_copy(
            src_ref=far_out.at[block % 2],
            dst_ref=far_got.at[layer, block],
            send_sem=far_send.at[block % 2],
            recv_sem=far_recv.at[layer, block],
            device_id=across,
            device_id_type=MESH,
        )

    def lanes_of(number):
        return pl.ds(pl.multiple_of(number * units, units), units)

    def rows_at(number):
        return pl.ds(pl.multiple_of(number * 16, 16), 16)

    def free(copy, layer, block):
        @pl.when((layer > 0) | (block >= 2))
        def _():
            copy.wait_send()

    def lane_codes(first):
        return jnp.transpose(marks[first : first + 128, :])[0:1, :]

    def set_factors():
        top = jnp.max(cols[0, 0:CHUNK, :], axis=1, keepdims=True)
        code = scale_code(top)
        marks[0:CHUNK, :] = jnp.broadcast_to(code, (CHUNK, 128))
        cols[1, 0:CHUNK, :] = jnp.broadcast_to(TOP_CODE / code_scale(code), (CHUNK, 128))

    def largest(values):
        return functools.reduce(
            jnp.maximum,
            [
                jnp.abs(value[:, lane : lane + 128])
                for value in values
                for lane in range(0, value.shape[1], 128)
            ],
        )

    def scaled(values, factor):
        return jnp.concatenate(
            [values[:, lane : lane + 128] * factor for lane in range(0, values.shape[1], 128)], axis=1
        )

    def put_scale(out):
        codes = jnp.concatenate(
            [lane_codes(0), lane_codes(128), jnp.zeros((14, 128), F32)], axis=0
        )
        out[CHUNK : CHUNK + 16, 0:128] = codes.astype(jnp.int32).astype(I16)

    def read_scale(got):
        step = code_scale(from_codes(got[CHUNK : CHUNK + 16, 0:128])) * (1.0 / TOP_CODE)
        step = jnp.transpose(jnp.concatenate([step, jnp.zeros((112, 128), F32)], axis=0))
        for up in range(2):
            marks[CHUNK + up * 128 : CHUNK + (up + 1) * 128, :] = jnp.broadcast_to(
                step[:, up : up + 1], (128, 128)
            )

    def step_at(number):
        return marks[pl.ds(pl.multiple_of(CHUNK + number * 16, 16), 16), :]

    def split(layer, block):
        free(core_move(layer, block), layer, block)

        def measure(number, carry):
            rows = rows_at(number)
            cols[0, rows, :] = largest(
                [grad[rows, lanes_of(2 * half + 1 - core)] for half in range(2)]
            )
            return carry

        lax.fori_loop(0, CHUNK // 16, measure, 0)
        set_factors()

        def write(number, carry):
            rows = rows_at(number)
            factor = cols[1, rows, :]
            for half in range(2):
                there = slice(half * units, (half + 1) * units)
                core_out[block % 2, rows, there] = to_codes(
                    scaled(grad[rows, lanes_of(2 * half + 1 - core)], factor)
                )
                keep_sums[block, rows, there] = grad[rows, lanes_of(2 * half + core)]
            return carry

        lax.fori_loop(0, CHUNK // 16, write, 0)
        put_scale(core_out.at[block % 2])
        core_move(layer, block).start()

    def cross(layer, block):
        core_move(layer, block).wait_recv()
        free(far_move(layer, block), layer, block)
        got = core_got.at[layer, block]
        read_scale(got)

        def add(number, carry):
            rows = rows_at(number)
            near, away = lanes_of(high), lanes_of(1 - high)
            step = step_at(number)
            keep_sums[block, rows, near] += scaled(from_codes(got[rows, near]), step)
            value = keep_sums[block, rows, away] + scaled(from_codes(got[rows, away]), step)
            keep_sums[block, rows, away] = value
            cols[0, rows, :] = largest([value])
            return carry

        lax.fori_loop(0, CHUNK // 16, add, 0)
        set_factors()

        def write(number, carry):
            rows = rows_at(number)
            far_out[block % 2, rows, :] = to_codes(
                scaled(keep_sums[block, rows, lanes_of(1 - high)], cols[1, rows, :])
            )
            return carry

        lax.fori_loop(0, CHUNK // 16, write, 0)
        put_scale(far_out.at[block % 2])
        far_move(layer, block).start()

    def finish(layer, block):
        far_move(layer, block).wait_recv()
        slope_copy(layer, block).wait()
        got = far_got.at[layer, block]
        read_scale(got)

        def one(number, total):
            rows = rows_at(number)
            value = keep_sums[block, rows, lanes_of(high)] + scaled(
                from_codes(got[rows, :]), step_at(number)
            )
            value = (value * slope_buf[block % 2, rows, :]).astype(BF16)
            dz[rows, :] = value
            return total + value.astype(F32)

        total = lax.fori_loop(0, CHUNK // 16, one, jnp.zeros((16, units), F32))
        if layer == 0:

            @pl.when(block < 2)
            def _():
                slope_copy(0, block + 2).start()

            @pl.when(block >= 2)
            def _():
                slope_copy(1, block - 2).start()

        else:

            @pl.when(block < 2)
            def _():
                slope_copy(1, block + 2).start()

        total = jnp.sum(total, axis=0, keepdims=True)
        for number in range(units // 128):
            row = 4 * (1 - layer) + number
            vec[row : row + 1, :] += total[:, number * 128 : (number + 1) * 128]
        flipped = (dz_two, dz_one)[layer]
        for up in range(CHUNK // 128):
            there = pl.ds(pl.multiple_of(block * CHUNK + up * 128, 128), 128)
            for number in range(units // 128):
                tile = dz[up * 128 : (up + 1) * 128, number * 128 : (number + 1) * 128]
                flipped[number * 128 : (number + 1) * 128, there] = jnp.transpose(
                    tile.astype(F32)
                ).astype(BF16)

    def blocks(first, last, work):
        def one(block, carry):
            work(block)
            return carry

        lax.fori_loop(first, last, one, 0)

    def start_block(block):
        rows = pl.ds(pl.multiple_of(block * CHUNK, CHUNK), CHUNK)
        copy = pltpu.make_async_copy(part_ref.at[rows, :], grad.at[pl.ds(0, CHUNK), :], load_sems.at[1])
        copy.start()
        copy.wait()
        split(0, block)

    def turn_block(block):
        finish(0, block)
        for lane in range(0, grad.shape[1], 512):
            grad[0:CHUNK, lane : lane + 512] = dot_nt(dz[...], w_hid_ref[lane : lane + 512, :])
        split(1, block)

    core_out[:, CHUNK:, :] = jnp.zeros((2, 16, 2 * units), I16)
    far_out[:, CHUNK:, :] = jnp.zeros((2, 16, units), I16)
    slope_copy(0, 0).start()
    slope_copy(0, 1).start()
    def vec_copy(away):
        return pltpu.make_async_remote_copy(
            src_ref=vec,
            dst_ref=vecs.at[blk],
            send_sem=vec_send.at[away - 1],
            recv_sem=vec_recv.at[away - 1],
            device_id={"blk": (blk + away) % RING},
            device_id_type=MESH,
        )

    def set_rows(count, first_own, size):
        size = jnp.broadcast_to(size, (count, 128))
        marks[first_own : first_own + count, :] = size
        cols[0, 0:count, :] = size
        cols[1, 0:count, :] = 2.0 / size

    def tell_sizes(group):
        for away in range(1, RING):
            size_copy(group, away).start()

    def size_copy(group, away):
        return pltpu.make_async_remote_copy(
            src_ref=sizes.at[group, here],
            dst_ref=sizes.at[group, here],
            send_sem=size_send.at[group, away - 1],
            recv_sem=size_recv.at[group, away - 1],
            device_id={"blk": ring_blk((here + away) % RING)},
            device_id_type=MESH,
        )

    def set_sizes(rows, group):
        parts = [lane_codes(first) for first in range(0, rows, 128)]
        parts.append(jnp.zeros((8 - len(parts), 128), F32))
        sizes[group, here] = jnp.concatenate(parts, axis=0)
        tell_sizes(group)

    def make_shares(group, row_of):
        for away in range(1, RING):
            size_copy(group, away).wait_recv()
        for way in range(2):
            tiles = []
            for step in range(STEPS):
                mine = row_of(here, step, way)
                came = mine * 0.0
                for back in range(step + 1):
                    came = came + row_of((here - 1 - back + (2 + 2 * back) * way + RING) % RING, step, way)
                if step < STEPS - 1:
                    whole = 1.0 / jnp.maximum(came + mine, 1e-30)
                else:
                    whole = 1.0 / TOP_CODE
                tiles += [came * whole, mine * whole]
            tiles.append(jnp.zeros((16, 128), F32))
            shares[group, way] = jnp.transpose(jnp.concatenate(tiles, axis=0))

    def hid_group():
        load(h_one_ref, h_buf).wait()
        wide = grad.shape[1]
        for part in range(2):
            first = part * 256
            hid_res_copy(part).wait()
            if part:
                hid_next_copy(part - 1).wait()
            total = jnp.zeros((256, 128), F32)
            for lane in range(0, wide, 512):
                value = dot_nn(dz_two[first : first + 256, :], h_buf[:, lane : lane + 512])
                value = value + res_buf[part, :, lane : lane + 512].astype(F32)
                grad[:, lane : lane + 512] = value
                value = jnp.abs(value)
                for more in range(0, 512, 128):
                    total = total + value[:, more : more + 128]
            set_rows(
                256, first, jnp.sum(total, axis=1, keepdims=True) * (1.0 / wide) + 1e-12
            )

            def some(number, carry, first=first):
                row = pl.multiple_of(number * 16, 16)
                size = cols[0, pl.ds(row, 16), :]
                steep = cols[1, pl.ds(row, 16), :]
                for lane in range(0, wide, 128):
                    piece = grad[pl.ds(row, 16), lane : lane + 128]
                    curve = jnp.tanh(piece * steep)
                    own_hid[2 * chunk_of(lane) + lane // 128 % 2, pl.ds(first + row, 16), :] = (
                        to_codes(curve * TOP_CODE)
                    )
                    grad[pl.ds(row, 16), lane : lane + 128] = piece - size * curve
                return carry

            lax.fori_loop(0, 16, some, 0)
            hid_next_copy(part).start()
        load(x_ref, h_buf.at[:, pl.ds(0, x_ref.shape[1])]).start()
        set_sizes(HID_ROWS, HID_GROUP)
        hid_next_copy(1).wait()

    def in_group():
        wide = x_ref.shape[1]
        load(x_ref, h_buf.at[:, pl.ds(0, wide)]).wait()
        for first in range(0, HID_ROWS, 256):
            grad[0:256, 0:wide] = dot_nn(dz_one[first : first + 256, :], h_buf[:, 0:wide])

            def add(number, carry, first=first):
                row = pl.multiple_of(number * 16, 16)
                place = pl.multiple_of(first + row, 16)
                value = grad[pl.ds(row, 16), 0:wide] + res_in_ref[pl.ds(place, 16), :].astype(F32)
                grad[pl.ds(row, 16), 0:wide] = value
                value = jnp.abs(value)
                cols[0, pl.ds(row, 16), :] = functools.reduce(
                    jnp.add, [value[:, lane : lane + 128] for lane in range(0, wide, 128)]
                )
                return carry

            lax.fori_loop(0, 16, add, 0)
            set_rows(
                256,
                first,
                jnp.sum(cols[0, 0:256, :], axis=1, keepdims=True) * (1.0 / deep) + 1e-12,
            )

            def some(number, carry, first=first):
                row = pl.multiple_of(number * 16, 16)
                place = pl.multiple_of(first + row, 16)
                size = cols[0, pl.ds(row, 16), :]
                steep = cols[1, pl.ds(row, 16), :]
                chunk = first // 64 + number // 4
                inside = pl.multiple_of(number % 4 * 16, 16)
                for lane in range(0, wide, 128):
                    piece = grad[pl.ds(row, 16), lane : lane + 128]
                    curve = jnp.tanh(piece * steep)
                    next_in_ref[pl.ds(place, 16), lane : lane + 128] = piece - size * curve
                    own_in[
                        2 * chunk + lane // 256, pl.ds(inside, 16), lane % 256 : lane % 256 + 128
                    ] = to_codes(curve * TOP_CODE)
                return carry

            lax.fori_loop(0, 16, some, 0)
        sizes[IN_GROUP, here] = jnp.concatenate(
            [lane_codes(64 * chunk) for chunk in range(RING)], axis=0
        )
        tell_sizes(IN_GROUP)

    def towards(way):
        return {"blk": ring_blk((here + 1 - 2 * way + RING) % RING)}

    def move(src, got, step, way, send_sem, recv_sem):
        return pltpu.make_async_remote_copy(
            src_ref=src,
            dst_ref=got.at[way, step],
            send_sem=send_sem.at[way, step],
            recv_sem=recv_sem.at[way, step],
            device_id=towards(way),
            device_id_type=MESH,
        )

    def first_moves(own, got, send_sem, recv_sem):
        for way in range(2):
            chunk = (here - 1 + 2 * way + RING) % RING
            move(own.at[2 * chunk + way], got, 0, way, send_sem, recv_sem).start()

    def hop(rows, own, got, group, step, send_sem, recv_sem, keep):
        for way in range(2):
            move(got.at[way, step], got, step, way, send_sem, recv_sem).wait_recv()

        def add(way, result):
            message = got.at[way, step]
            ahead = here - 2 - step + way * (4 + 2 * step) + 2 * RING
            mine = own.at[2 * (ahead % RING) + way]
            share = pltpu.roll(shares[group, way], (128 - 16 * step) % 128, 1)
            for number, first in enumerate(range(0, rows, 128)):
                count = min(128, rows - first)
                there = slice(first, first + count)
                result(
                    first,
                    count,
                    from_codes(message[there, :]) * share[0:count, number : number + 1]
                    + from_codes(mine[there, :]) * share[0:count, 8 + number : 9 + number],
                )

        @pl.when(step < STEPS - 1)
        def _():
            for way in range(2):

                def write(first, count, value, way=way):
                    got[way, step, first : first + count, :] = to_codes(value)

                add(way, write)
            for way in range(2):
                move(got.at[way, step], got, step + 1, way, send_sem, recv_sem).start()

        @pl.when(step == STEPS - 1)
        def _():
            for way in range(2):

                def finish_rows(first, count, value, way=way):
                    keep(way, first, count, value)
                    square = jnp.sum(value * value, axis=0, keepdims=True)
                    for lane in range(0, value.shape[1], 128):
                        stats_ref[0:1, :] += square[:, lane : lane + 128]

                add(way, finish_rows)

    def out_hop(group, step):
        def keep(way, first, count, value):
            row = pl.multiple_of(group * OUT_ROWS + first, 16)
            red_out_ref[pl.ds(row, count), way * 128 : (way + 1) * 128] = value

        hop(
            OUT_ROWS,
            own_out.at[group],
            got_out.at[group],
            group,
            step,
            out_send.at[group],
            out_recv.at[group],
            keep,
        )

    def hid_hop(step):
        def keep(way, first, count, value):
            red_hid_ref[first : first + count, way * 128 : (way + 1) * 128] = value

        hop(HID_ROWS, own_hid, got_hid, HID_GROUP, step, hid_send, hid_recv, keep)

    def share_move(step, way):
        place = (here - step + 2 * step * way + 2 * RING) % RING
        return pltpu.make_async_remote_copy(
            src_ref=share_in.at[way, place],
            dst_ref=share_in.at[way, place],
            send_sem=share_send.at[way, step],
            recv_sem=share_recv.at[way, step],
            device_id=towards(way),
            device_id_type=MESH,
        )

    def share_across(way, place):
        return pltpu.make_async_remote_copy(
            src_ref=share_in.at[way, place],
            dst_ref=share_far.at[way, place],
            send_sem=share_far_send.at[way, place],
            recv_sem=share_far_recv.at[way, place],
            device_id=across,
            device_id_type=MESH,
        )

    def in_hop(step):
        def keep(way, first, count, value):
            share_in[way, here] = value

        hop(64, own_in, got_in, IN_GROUP, step, in_send, in_recv, keep)

        @pl.when(step == STEPS - 1)
        def _():
            for way in range(2):
                share_move(0, way).start()
                share_across(way, here).start()

    def share_hop(step):
        for way in range(2):
            share_move(step, way).wait_recv()
            share_across(way, (here - 1 - step + (2 + 2 * step) * way + RING) % RING).start()

        @pl.when(step < STEPS - 1)
        def _():
            for way in range(2):
                share_move(step + 1, way).start()

    def in_step(index):
        @pl.when((index >= 0) & (index < STEPS))
        def _():
            in_hop(index)

        @pl.when((index >= STEPS) & (index < 2 * STEPS))
        def _():
            share_hop(index - STEPS)

    def chunk_row(place, step, way):
        chunk = (here - 2 - step + way * (4 + 2 * step) + 2 * RING) % RING
        line = sizes[IN_GROUP, place, pl.ds(chunk, 1), :]
        return jnp.broadcast_to(line, (8, 128))

    for group in range(OUT_GROUPS):
        sizes[group, here] = sizes_ref[group]
        tell_sizes(group)
        code_copy(group).wait()
        first_moves(own_out.at[group], got_out.at[group], out_send.at[group], out_recv.at[group])
    blocks(0, 4, start_block)

    def each(number, first, spacing, count, work):
        after = number - first

        @pl.when((after >= 0) & (after < spacing * count) & (after % spacing == 0))
        def _():
            work(after // spacing)

    def turn(number, carry):
        @pl.when(number < OUT_GROUPS)
        def _():
            make_shares(number, lambda place, step, way: sizes[number, place])

        @pl.when(number < OUT_GROUPS * STEPS)
        def _():
            out_hop(number % OUT_GROUPS, number // OUT_GROUPS)

        @pl.when(number == HID_AT + HID_HOP)
        def _():
            make_shares(HID_GROUP, lambda place, step, way: sizes[HID_GROUP, place])

        each(number, HID_AT + HID_HOP, HID_HOP, STEPS, hid_hop)

        @pl.when(number == IN_AT + 1)
        def _():
            make_shares(IN_GROUP, chunk_row)

        in_step(number - IN_AT - 1)
        each(number, 0, 1, 4, lambda block: cross(0, block))
        each(number, TURN_AT, 2, 4, turn_block)
        each(number, CROSS_AT, 2, 4, lambda block: cross(1, block))

        @pl.when(number == HID_AT)
        def _():
            hid_group()
            first_moves(own_hid, got_hid, hid_send, hid_recv)

        each(number, FINISH_AT, 2, 4, lambda block: finish(1, block))

        @pl.when(number == IN_AT)
        def _():
            in_group()
            first_moves(own_in, got_in, in_send, in_recv)
            for away in range(1, RING):
                vec_copy(away).start()

        return carry

    turns = max(IN_AT + 1 + 2 * STEPS, HID_AT + HID_HOP * STEPS + 1, OUT_GROUPS * STEPS)
    lax.fori_loop(0, turns, turn, 0)

    def unfold(shares_of, out):
        for place in range(0, RING, 2):
            for way in range(2):
                for lane in range(0, 256, 128):
                    tile = jnp.concatenate(
                        [shares_of[way, place + more, :, lane : lane + 128] for more in range(2)],
                        axis=0,
                    )
                    first = way * 256 + lane
                    out[first : first + 128, place * 64 : place * 64 + 128] = jnp.transpose(tile)

    unfold(share_in, red_in_ref)
    for place in range(RING):
        for way in range(2):
            share_across(way, place).wait_recv()
    unfold(share_far, red_far_ref)
    for away in range(1, RING):
        vec_copy(away).wait_recv()
    vecs[blk] = vec[...]
    total = vecs[0]
    for number in range(1, RING):
        total = total + vecs[number]
    vec_sum_ref[...] = total
    flat = 128 * lax.broadcasted_iota(jnp.int32, total.shape, 0) + lax.broadcasted_iota(
        jnp.int32, total.shape, 1
    )
    total = jnp.where(flat < 2 * units + senones, total, 0.0)
    stats_ref[1:2, :] = jnp.sum(total * total, axis=0, keepdims=True) * (1.0 / RING)
    for away in range(1, RING):
        vec_copy(away).wait_send()
        for group in range(OUT_GROUPS + 2):
            size_copy(group, away).wait_send()
    for slot in range(2):
        core_move(1, 2 + slot).wait_send()
        far_move(1, 2 + slot).wait_send()
    for way in range(2):
        for step in range(STEPS):
            for group in range(OUT_GROUPS):
                move(
                    got_out.at[group, way, step],
                    got_out.at[group],
                    step,
                    way,
                    out_send.at[group],
                    out_recv.at[group],
                ).wait_send()
            move(got_hid.at[way, step], got_hid, step, way, hid_send, hid_recv).wait_send()
            move(got_in.at[way, step], got_in, step, way, in_send, in_recv).wait_send()
            share_move(step, way).wait_send()
        for place in range(RING):
            share_across(way, place).wait_send()


def reduce_grads(
    codes, sizes, h_one, x, part, slope_two, slope_one, w_hid, res_hid, res_in, vec, senones, deep
):
    frames, wide = h_one.shape
    in_wide = x.shape[1]
    units = w_hid.shape[1]
    vmem = pl.BlockSpec(memory_space=pltpu.VMEM)
    hbm = pl.BlockSpec(memory_space=pl.ANY)
    message = OUT_ROWS
    hid_message = HID_ROWS
    in_message = 64
    sem = pltpu.SemaphoreType.DMA
    return pl.pallas_call(
        functools.partial(reduce_kernel, deep, senones),
        out_shape=(
            jax.ShapeDtypeStruct((HID_ROWS, wide), F32),
            jax.ShapeDtypeStruct((HID_ROWS, in_wide), F32),
            jax.ShapeDtypeStruct((OUT_GROUPS * OUT_ROWS, 256), F32),
            jax.ShapeDtypeStruct((HID_ROWS, 256), F32),
            jax.ShapeDtypeStruct((in_wide, HID_ROWS), F32),
            jax.ShapeDtypeStruct((in_wide, HID_ROWS), F32),
            jax.ShapeDtypeStruct(vec.shape, F32),
            jax.ShapeDtypeStruct((8, 128), F32),
        ),
        in_specs=[hbm, vmem] + [hbm] * 5 + [vmem, hbm, vmem, vmem],
        out_specs=(hbm,) + (vmem,) * 7,
        scratch_shapes=[
            pltpu.VMEM((256, wide), F32),
            pltpu.VMEM((2, 256, wide), BF16),
            pltpu.VMEM((frames, wide), BF16),
            pltpu.VMEM((2, 256, units), F32),
            pltpu.VMEM((640, 128), F32),
            pltpu.VMEM((2, 256, 128), F32),
            pltpu.VMEM((4, 256, 2 * units), F32),
            pltpu.VMEM((256, units), BF16),
            pltpu.VMEM((units, frames), BF16),
            pltpu.VMEM((units, frames), BF16),
            pltpu.VMEM((2, 272, 2 * units), I16),
            pltpu.VMEM((2, 4, 272, 2 * units), I16),
            pltpu.VMEM((2, 272, units), I16),
            pltpu.VMEM((2, 4, 272, units), I16),
            pltpu.VMEM((OUT_GROUPS, 2 * RING, message, 128), I16),
            pltpu.VMEM((OUT_GROUPS, 2, STEPS, message, 128), I16),
            pltpu.VMEM((2 * RING, hid_message, 128), I16),
            pltpu.VMEM((2, STEPS, hid_message, 128), I16),
            pltpu.VMEM((2 * RING, in_message, 256), I16),
            pltpu.VMEM((2, STEPS, in_message, 256), I16),
            pltpu.VMEM((2, RING, 64, 256), F32),
            pltpu.VMEM((2, RING, 64, 256), F32),
            pltpu.VMEM((OUT_GROUPS + 2, RING, 8, 128), F32),
            pltpu.VMEM((OUT_GROUPS + 2, 2, 128, 128), F32),
            pltpu.VMEM(vec.shape, F32),
            pltpu.VMEM((RING,) + vec.shape, F32),
            sem((2,)),
            sem((2,)),
            sem((OUT_GROUPS,)),
            sem((2,)),
            sem((2,)),
            sem((2, 4)),
            sem((2,)),
            sem((2, 4)),
            sem((OUT_GROUPS, 2, STEPS)),
            sem((OUT_GROUPS, 2, STEPS)),
            sem((2, STEPS)),
            sem((2, STEPS)),
            sem((2, STEPS)),
            sem((2, STEPS)),
            sem((2, STEPS)),
            sem((2, STEPS)),
            sem((STEPS,)),
            sem((STEPS,)),
            sem((OUT_GROUPS + 2, STEPS)),
            sem((OUT_GROUPS + 2, STEPS)),
            sem((2, RING)),
            sem((2, RING)),
        ],
        compiler_params=pltpu.CompilerParams(
            collective_id=1, has_side_effects=True, vmem_limit_bytes=63 * 1024 * 1024
        ),
    )(codes, sizes, h_one, x, part, slope_two, slope_one, w_hid, res_hid, res_in, vec)


RING_STARTS = (0, 2, 5, 7, 9)
LAYER_TWO_WAVE = 7
LOGIT_WAVES = (11, 12, 14, 16)


def forward_kernel(
    slot_count,
    x_ref,
    tags_ref,
    w_in_ref,
    w_hid_ref,
    w_out_ref,
    bias_ref,
    bias_out_ref,
    mom_ref,
    x_out,
    h_one_out,
    h_two_out,
    slope_one_out,
    slope_two_out,
    w_hid_out,
    w_out_out,
    mom_far_ref,
    dl_ref,
    bias_sum_ref,
    loss_ref,
    x_all,
    h_one,
    h_two,
    slope_one,
    slope_two,
    w_in,
    w_hid,
    w_out,
    curve,
    bias_col,
    tags,
    sums,
    ring_send,
    ring_recv,
    x_send,
    x_recv,
    h_send,
    h_recv,
    tag_send,
    tag_recv,
    sum_send,
    sum_recv,
    out_sems,
    mom_sems,
):
    blk = lax.axis_index("blk")
    col = lax.axis_index("col")
    here = ring_place(blk)
    senones, depth = w_out_ref.shape
    own_rows, deep = x_ref.shape
    units = w_hid_ref.shape[1]
    frames = x_all.shape[0]
    cores = {"col": col + 1 - 2 * (col % 2)}
    across = {"col": (col + 2) % 4}
    corner = {"col": (col + 2) % 4 + 1 - 2 * (col % 2)}
    others = (cores, across, corner)

    barrier = pltpu.get_barrier_semaphore()
    for target in others + tuple({"blk": ring_blk((here + way) % RING)} for way in (1, 7)):
        pl.semaphore_signal(barrier, inc=1, device_id=target, device_id_type=MESH)

    w_hid[pl.ds(pl.multiple_of(blk * depth, depth), depth), :] = w_hid_ref[...].astype(BF16)
    own_lanes = pl.ds(pl.multiple_of(blk * depth, depth), depth)
    w_out[senones // 16 * 16 :, own_lanes] = jnp.zeros(
        (w_out.shape[0] - senones // 16 * 16, depth), BF16
    )
    w_out[0:senones, own_lanes] = w_out_ref[...].astype(BF16)
    own_frames = pl.ds(pl.multiple_of(col * own_rows, own_rows), own_rows)
    x_all[own_frames, :] = jnp.zeros((own_rows, x_all.shape[1]), BF16)
    x_all[own_frames, 0:deep] = x_ref[...]
    tags[col] = tags_ref[...]
    sums[...] = jnp.zeros_like(sums)
    pl.semaphore_wait(barrier, 5)

    def ring_part(group, origin, way):
        start = pl.multiple_of(origin * depth + way * 128, 128)
        if group == 0:
            return w_hid.at[pl.ds(start, 128), :]
        return w_out.at[pl.ds((group - 1) * OUT_ROWS, OUT_ROWS), pl.ds(start, 128)]

    def ring_move(group, step, way):
        origin = ring_blk((here - step + 2 * step * way + RING) % RING)
        part = ring_part(group, origin, way)
        return pltpu.make_async_remote_copy(
            src_ref=part,
            dst_ref=part,
            send_sem=ring_send.at[group, way, step],
            recv_sem=ring_recv.at[group, way, step],
            device_id={"blk": ring_blk((here + 1 - 2 * way + RING) % RING)},
            device_id_type=MESH,
        )

    def ring_wave(wave):
        for group, start in enumerate(RING_STARTS):
            step = wave - 1 - start
            for way in range(2):
                if step == -1:
                    ring_move(group, 0, way).start()
                if 0 <= step < STEPS:
                    ring_move(group, step, way).wait_recv()
                    if step < STEPS - 1:
                        ring_move(group, step + 1, way).start()

    def copy_to(target, src, send_sem, recv_sem):
        return pltpu.make_async_remote_copy(
            src_ref=src,
            dst_ref=src,
            send_sem=send_sem,
            recv_sem=recv_sem,
            device_id=target,
            device_id_type=MESH,
        )

    def rows_of(owner):
        return pl.ds(pl.multiple_of(owner * own_rows, own_rows), own_rows)

    def lanes_of(owner):
        return pl.ds(pl.multiple_of(owner * units, units), units)

    def x_move(number):
        owner = across["col"] if number == 2 else col
        target = across if number == 1 else cores
        return copy_to(target, x_all.at[rows_of(owner), :], x_send.at[number], x_recv.at[number])

    def h_move(layer, number, block):
        owner = across["col"] if number == 2 else col
        target = across if number == 1 else cores
        whole = (h_one, h_two)[layer]
        part = whole.at[pl.ds(block * own_rows, own_rows), lanes_of(owner)]
        return copy_to(
            target, part, h_send.at[layer, number, block], h_recv.at[layer, number, block]
        )

    def h_start(layer, block):
        h_move(layer, 0, block).start()
        h_move(layer, 1, block).start()

    def h_forward(layer, block):
        h_move(layer, 1, block).wait_recv()
        h_move(layer, 2, block).start()

    def h_ready(layer, block):
        h_move(layer, 0, block).wait_recv()
        h_move(layer, 2, block).wait_recv()

    ring_wave(0)
    x_move(0).start()
    x_move(1).start()
    tag_copies = [
        copy_to(target, tags.at[col], tag_send.at[number], tag_recv.at[number])
        for number, target in enumerate(others)
    ]
    for copy in tag_copies:
        copy.start()
    w_in[...] = jnp.zeros_like(w_in)
    w_in[0:deep, :] = w_in_ref[...].astype(BF16)
    for number in range(bias_out_ref.shape[0]):
        line = jnp.broadcast_to(bias_out_ref[number : number + 1, :], (128, 128))
        bias_col[number * 128 : (number + 1) * 128, :] = jnp.transpose(line)
    ring_wave(1)
    x_move(1).wait_recv()
    x_move(2).start()
    x_move(0).wait_recv()
    x_move(2).wait_recv()

    def layer(number, block, inputs, weights, whole, slopes):
        there = slice(block * own_rows, (block + 1) * own_rows)
        value = jax.nn.sigmoid(
            dot_nn(inputs[there, :], weights[...]) + bias_ref[number : number + 1, :]
        )
        slopes[there, :] = value * (1.0 - value)
        whole[there, lanes_of(col)] = value.astype(BF16)
        h_start(number, block)

    outs = []

    def put(src, dst):
        copy = pltpu.make_async_copy(src, dst, out_sems.at[len(outs)])
        copy.start()
        outs.append(copy)

    for block in range(4):
        layer(0, block, x_all, w_in, h_one, slope_one)
    put(x_all, x_out)
    put(slope_one, slope_one_out)

    def all_tags():
        return jnp.concatenate([tags[owner, 0:1, :] for owner in range(4)], axis=1)

    def own_row(line):
        line = line - col * senones
        return jnp.where(line < senones, line, -1)

    def logits(group):
        first = group * OUT_ROWS
        half = frames // 2
        for part in range(2):
            curve[first : first + OUT_ROWS, part * half : (part + 1) * half] = dot_nt(
                w_out[first : first + OUT_ROWS, :], h_two[part * half : (part + 1) * half, :]
            )
        base = lax.broadcasted_iota(jnp.int32, (16, frames), 0)

        def largest(number, top):
            row = pl.multiple_of(first + number * 16, 16)
            value = curve[pl.ds(row, 16), :] + bias_col[pl.ds(row, 16), 0:1]
            if group == OUT_GROUPS - 1:
                value = jnp.where(base + row < senones, value, -1e30)
            curve[pl.ds(row, 16), :] = value
            return jnp.maximum(top, value)

        top = lax.fori_loop(0, OUT_ROWS // 16, largest, jnp.full((16, frames), -1e30, F32))
        top = jnp.max(top, axis=0, keepdims=True)
        line = jnp.broadcast_to(own_row(all_tags()), (16, frames))

        def exponents(number, carry):
            total, picked = carry
            row = pl.multiple_of(first + number * 16, 16)
            value = curve[pl.ds(row, 16), :]
            power = jnp.exp(value - top)
            curve[pl.ds(row, 16), :] = power
            return total + power, picked + jnp.where(base + row == line, value, 0.0)

        blank = jnp.zeros((16, frames), F32)
        total, picked = lax.fori_loop(0, OUT_ROWS // 16, exponents, (blank, blank))
        sums[col, group : group + 1, :] = top
        sums[col, 4 + group : 5 + group, :] = jnp.sum(total, axis=0, keepdims=True)
        sums[col, 8 + group : 9 + group, :] = jnp.sum(picked, axis=0, keepdims=True)

    mom_copy = pltpu.make_async_remote_copy(
        src_ref=mom_ref,
        dst_ref=mom_far_ref,
        send_sem=mom_sems.at[0],
        recv_sem=mom_sems.at[1],
        device_id=across,
        device_id_type=MESH,
    )
    last_wave = RING_STARTS[-1] + STEPS
    for wave in range(2, last_wave + 1):
        ring_wave(wave)
        if 2 <= wave < 6:
            h_forward(0, wave - 2)
        if wave == LAYER_TWO_WAVE:
            for block in range(4):
                h_ready(0, block)
                layer(1, block, h_one, w_hid, h_two, slope_two)
            put(h_one, h_one_out)
            put(slope_two, slope_two_out)
            put(w_hid, w_hid_out)
        if LAYER_TWO_WAVE < wave <= LAYER_TWO_WAVE + 4:
            h_forward(1, wave - LAYER_TWO_WAVE - 1)
        for group, when in enumerate(LOGIT_WAVES):
            if wave == when:
                if group == 0:
                    for block in range(4):
                        h_ready(1, block)
                    put(h_two, h_two_out)
                    mom_copy.start()
                    for copy in tag_copies:
                        copy.wait_recv()
                rows = pl.ds(group * OUT_ROWS, OUT_ROWS)
                put(w_out.at[rows, :], w_out_out.at[rows, :])
                logits(group)

    sum_copies = [
        copy_to(target, sums.at[col], sum_send.at[number], sum_recv.at[number])
        for number, target in enumerate(others)
    ]
    for copy in sum_copies:
        copy.start()
    for copy in sum_copies:
        copy.wait_recv()

    def lines(first):
        return [sums[owner, first + group : first + group + 1, :] for owner in range(4) for group in range(4)]

    tops = lines(0)
    top = functools.reduce(jnp.maximum, tops)
    total = functools.reduce(
        jnp.add, [size * jnp.exp(own - top) for own, size in zip(tops, lines(4), strict=True)]
    )
    picked = functools.reduce(jnp.add, lines(8))
    line = all_tags()
    live = line >= 0
    loss = jnp.where(live, top + jnp.log(total) - picked, 0.0)
    loss_ref[...] = jnp.zeros_like(loss_ref)
    loss_ref[0:1, :] = functools.reduce(
        jnp.add, [loss[:, lane : lane + 128] for lane in range(0, frames, 128)]
    )
    weight = jnp.where(live, 1.0 / slot_count, 0.0)
    line = jnp.broadcast_to(own_row(line), (16, frames))
    hit_weight = jnp.broadcast_to(weight, (16, frames))
    base = lax.broadcasted_iota(jnp.int32, (16, frames), 0)
    bias_col[...] = jnp.zeros_like(bias_col)
    for group in range(OUT_GROUPS):
        share = jnp.exp(sums[col, group : group + 1, :] - top) / total * weight

        def gradient(number, carry, first=group * OUT_ROWS, share=share):
            row = pl.multiple_of(first + number * 16, 16)
            value = curve[pl.ds(row, 16), :] * share - jnp.where(base + row == line, hit_weight, 0.0)
            value = value.astype(BF16)
            dl_ref[pl.ds(row, 16), :] = value
            value = value.astype(F32)
            bias_col[pl.ds(row, 16), :] = functools.reduce(
                jnp.add, [value[:, lane : lane + 128] for lane in range(0, frames, 128)]
            )
            return carry

        lax.fori_loop(0, OUT_ROWS // 16, gradient, 0)
    bias_sum_ref[...] = jnp.zeros_like(bias_sum_ref)
    for number in range(bias_out_ref.shape[0]):
        block = jnp.transpose(bias_col[number * 128 : (number + 1) * 128, :])
        bias_sum_ref[number : number + 1, :] = jnp.sum(block, axis=0, keepdims=True)

    for group in range(len(RING_STARTS)):
        for way in range(2):
            for step in range(STEPS):
                ring_move(group, step, way).wait_send()
    for number in range(3):
        x_move(number).wait_send()
        for block in range(4):
            h_move(0, number, block).wait_send()
            h_move(1, number, block).wait_send()
    for copy in tag_copies + sum_copies:
        copy.wait_send()
    mom_copy.wait()
    for copy in outs:
        copy.wait()


def forward_pass(x, tags, w_in, w_hid, w_out, bias, bias_out, mom, slot_count):
    own_rows = x.shape[0]
    units = w_hid.shape[1]
    frames = 4 * own_rows
    wide = 4 * units
    rows = OUT_GROUPS * OUT_ROWS
    blocks = bias_out.shape[0]
    vmem = pl.BlockSpec(memory_space=pltpu.VMEM)
    hbm = pl.BlockSpec(memory_space=pl.ANY)
    sem = pltpu.SemaphoreType.DMA
    kept = (
        ((frames, 512), BF16),
        ((frames, wide), BF16),
        ((frames, wide), BF16),
        ((frames, units), F32),
        ((frames, units), F32),
        ((wide, units), BF16),
        ((rows, wide), BF16),
    )
    return pl.pallas_call(
        functools.partial(forward_kernel, slot_count),
        out_shape=tuple(jax.ShapeDtypeStruct(shape, kind) for shape, kind in kept)
        + (
            jax.ShapeDtypeStruct(mom.shape, F32),
            jax.ShapeDtypeStruct((rows, frames), BF16),
            jax.ShapeDtypeStruct((24, 128), F32),
            jax.ShapeDtypeStruct((8, 128), F32),
        ),
        in_specs=[vmem] * 7 + [hbm],
        out_specs=(hbm,) * 8 + (vmem,) * 3,
        scratch_shapes=[pltpu.VMEM(shape, kind) for shape, kind in kept[:5]]
        + [
            pltpu.VMEM((512, units), BF16),
            pltpu.VMEM((wide, units), BF16),
            pltpu.VMEM((rows, wide), BF16),
            pltpu.VMEM((rows, frames), F32),
            pltpu.VMEM((blocks * 128, 128), F32),
            pltpu.VMEM((4,) + tags.shape, jnp.int32),
            pltpu.VMEM((4, 16, frames), F32),
            sem((5, 2, STEPS)),
            sem((5, 2, STEPS)),
            sem((3,)),
            sem((3,)),
            sem((2, 3, 4)),
            sem((2, 3, 4)),
            sem((3,)),
            sem((3,)),
            sem((3,)),
            sem((3,)),
            sem((16,)),
            sem((2,)),
        ],
        compiler_params=pltpu.CompilerParams(
            collective_id=2, has_side_effects=True, vmem_limit_bytes=60 * 1024 * 1024
        ),
    )(x, tags, w_in, w_hid, w_out, bias, bias_out, mom)


DIM_BITS = (2, 4, 8)
ORDERS = ((0, 1, 2), (1, 2, 0), (2, 0, 1))
PIECES = ((0, 48), (48, 48), (96, 32))
SIZE_PIECE = 2
LIGHT_HID = 3
LIGHT_IN = 2


def stage_sends(stage, sources):
    moves = []
    for piece, order in enumerate(ORDERS):
        slot = sum(DIM_BITS[order[index]] for index in sources)
        moves.append((piece, slot, order[stage]))
    return moves


def landed(moves):
    return [(slot | DIM_BITS[dim], piece) for piece, slot, dim in moves]


FIRST = stage_sends(0, ())
SECOND = stage_sends(1, ())
SECOND_ON = stage_sends(1, (0,))
THIRD = stage_sends(2, ())
THIRD_A = stage_sends(2, (0,))
THIRD_B = stage_sends(2, (1,))
THIRD_C = stage_sends(2, (0, 1))
MOVES = FIRST + SECOND + SECOND_ON + THIRD + THIRD_A + THIRD_B + THIRD_C


def muon_kernel(
    stats_ref,
    red_hid_ref,
    mom_hid_ref,
    red_in_ref,
    mom_in_ref,
    red_far_ref,
    mom_far_ref,
    hid_ref,
    inp_ref,
    next_hid_ref,
    next_in_ref,
    norm_ref,
    codes,
    sizes,
    tops,
    lows,
    scales,
    weights,
    xs,
    us,
    vs,
    lhs,
    xin,
    xin_top,
    xin_low,
    gram,
    gram_got,
    back,
    sums,
    sums_got,
    spread_out,
    spread_got,
    spread_size_out,
    spread_size_got,
    send_sems,
    core_sems,
    recv_sems,
    back_send,
    back_recv,
    sums_send,
    sums_recv,
    spread_send,
    spread_recv,
    pair_send,
    pair_recv,
    size_send,
    size_recv,
):
    blk = lax.axis_index("blk")
    col = lax.axis_index("col")
    rows, wide = xs.shape
    height = back.shape[2]
    part_wide = inp_ref.shape[1]
    other_core = {"col": col + 1 - 2 * (col % 2)}
    dims = (
        {"blk": blk + 1 - 2 * (blk % 2)},
        {"col": (col + 2) % 4},
        {"blk": blk + 2 - 4 * ((blk // 2) % 2)},
    )
    diagonal = {"blk": 4 * (blk // 4) + 3 - blk % 4}
    barrier = pltpu.get_barrier_semaphore()
    corner = {"col": (col + 2) % 4 + 1 - 2 * (col % 2)}
    cols = (other_core, dims[1], corner)
    for target in (*cols, *({"blk": (blk + away) % 8} for away in range(1, 8))):
        pl.semaphore_signal(barrier, inc=1, device_id=target, device_id_type=MESH)

    def fold(values):
        line = jnp.sum(values, axis=0, keepdims=True)
        return sum(line[:, lane : lane + 128] for lane in range(0, line.shape[1], 128))

    share = 0.125
    sums[blk, 0:1, :] = fold(stats_ref[...])
    sums[blk, 1:2, :] = fold(mom_hid_ref[...] * mom_hid_ref[...])
    sums[blk, 2:3, :] = fold(mom_hid_ref[...] * red_hid_ref[...])
    sums[blk, 3:4, :] = fold(red_hid_ref[...] * red_hid_ref[...])
    sums[blk, 4:5, :] = fold(mom_in_ref[...] * mom_in_ref[...]) * share
    sums[blk, 5:6, :] = fold(mom_in_ref[...] * red_in_ref[...]) * share
    sums[blk, 6:7, :] = fold(red_in_ref[...] * red_in_ref[...]) * share
    sums[blk, 7:8, :] = jnp.zeros((1, 128), F32)
    eye = lax.broadcasted_iota(jnp.int32, (rows, rows), 0) == lax.broadcasted_iota(
        jnp.int32, (rows, rows), 1
    )
    pl.semaphore_wait(barrier, 10)

    def tell(own, targets, first):
        copies = []
        for number, target in enumerate(targets, start=first):
            copies.append(
                pltpu.make_async_remote_copy(
                    src_ref=own,
                    dst_ref=own,
                    send_sem=sums_send.at[number],
                    recv_sem=sums_recv.at[number],
                    device_id=target,
                    device_id_type=MESH,
                )
            )
            copies[-1].start()
        for copy in copies:
            copy.wait_recv()
        return copies

    told = tell(sums.at[blk], [{"blk": (blk + away) % 8} for away in range(1, 8)], 0)
    sums_got[col] = functools.reduce(jnp.add, [sums[number] for number in range(8)])
    told += tell(sums_got.at[col], cols, 7)
    whole = functools.reduce(jnp.add, [sums_got[number] for number in range(4)])
    whole = jnp.sum(whole, axis=1, keepdims=True)
    clip = jnp.sqrt(whole[0:1])
    factor = jnp.minimum(1.0, CLIP / clip)

    def norm_of(first):
        square = (
            0.25 * whole[first : first + 1]
            + factor * whole[first + 1 : first + 2]
            + factor * factor * whole[first + 2 : first + 3]
        )
        return 1.0 / (jnp.sqrt(jnp.maximum(square, 0.0)) + 1e-07)

    norm_ref[0:4, :] = jnp.broadcast_to(clip, (4, 128))
    norm_ref[4:8, :] = jnp.broadcast_to(factor, (4, 128))
    next_hid_ref[...] = 0.5 * mom_hid_ref[...] + factor * red_hid_ref[...]
    next_in_ref[...] = 0.5 * mom_in_ref[...] + factor * red_in_ref[...]

    my_lanes = pl.ds(pl.multiple_of(blk * height, height), height)
    for number in range(4):
        there = slice(number * rows, (number + 1) * rows)
        value = next_hid_ref[there, :]
        largest = jnp.maximum(jnp.max(jnp.abs(value), axis=1, keepdims=True), 1e-30)
        spread_out[number] = to_codes(value * (TOP_CODE / largest))
        line = jnp.sum(jnp.where(eye, largest, 0.0), axis=0, keepdims=True)
        spread_size_out[number] = jnp.broadcast_to(line * (1.0 / TOP_CODE), (8, rows))
    spread = []
    for away in range(1, 8):
        target = (blk + away) % 8
        for kind, (src, dst) in enumerate(
            ((spread_out, spread_got), (spread_size_out, spread_size_got))
        ):
            spread.append(
                pltpu.make_async_remote_copy(
                    src_ref=src.at[target % 4],
                    dst_ref=dst.at[blk],
                    send_sem=spread_send.at[kind, away - 1],
                    recv_sem=spread_recv.at[kind, away - 1],
                    device_id={"blk": target},
                    device_id_type=MESH,
                )
            )
            spread[-1].start()
    high = col // 2
    my_half = pl.ds(pl.multiple_of(high * part_wide, part_wide), part_wide)
    far_half = pl.ds(pl.multiple_of((1 - high) * part_wide, part_wide), part_wide)
    in_scale = norm_of(4)
    xin[:, my_half] = next_in_ref[...] * in_scale
    xin[:, far_half] = (0.5 * mom_far_ref[...] + factor * red_far_ref[...]) * in_scale
    spread_got[blk] = spread_out[blk % 4]
    spread_size_got[blk] = spread_size_out[blk % 4]
    for copy in spread:
        copy.wait_recv()
    hid_scale = norm_of(1)
    for number in range(8):
        size = jnp.broadcast_to(spread_size_got[number, 0:1, :], (rows, rows))
        size = jnp.transpose(size) * hid_scale
        for lane in range(0, height, 128):
            xs[:, number * height + lane : number * height + lane + 128] = (
                from_codes(spread_got[number, :, lane : lane + 128]) * size
            )

    numbers = {move: number for number, move in enumerate(MOVES)}

    def part(turn, slot, piece):
        first, count = PIECES[piece]
        return codes.at[turn, slot, pl.ds(first, count), :]

    def send(turn, move):
        piece, slot, dim = move
        there = slot | DIM_BITS[dim]
        copies = [
            pltpu.make_async_remote_copy(
                src_ref=part(turn, slot, piece),
                dst_ref=part(turn, there, piece),
                send_sem=send_sems.at[numbers[move]],
                recv_sem=recv_sems.at[turn, there, piece],
                device_id=dims[dim],
                device_id_type=MESH,
            )
        ]
        if piece == SIZE_PIECE:
            copies.append(
                pltpu.make_async_remote_copy(
                    src_ref=sizes.at[turn, slot],
                    dst_ref=sizes.at[turn, there],
                    send_sem=size_send.at[numbers[move]],
                    recv_sem=size_recv.at[turn, there],
                    device_id=dims[dim],
                    device_id_type=MESH,
                )
            )
        return copies

    def send_all(turn, moves):
        for move in moves:
            for copy in send(turn, move):
                copy.start()

    def to_core(turn, slot, piece):
        copies = [
            pltpu.make_async_remote_copy(
                src_ref=part(turn, slot, piece),
                dst_ref=part(turn, slot + 1, piece),
                send_sem=core_sems.at[slot // 2, piece],
                recv_sem=recv_sems.at[turn, slot + 1, piece],
                device_id=other_core,
                device_id_type=MESH,
            )
        ]
        if piece == SIZE_PIECE:
            copies.append(
                pltpu.make_async_remote_copy(
                    src_ref=sizes.at[turn, slot],
                    dst_ref=sizes.at[turn, slot + 1],
                    send_sem=core_sems.at[slot // 2, 3],
                    recv_sem=size_recv.at[turn, slot + 1],
                    device_id=other_core,
                    device_id_type=MESH,
                )
            )
        return copies

    def arrived(turn, slot, piece):
        def wait(ref, sem):
            pltpu.make_async_remote_copy(
                src_ref=ref,
                dst_ref=ref,
                send_sem=core_sems.at[0, 0],
                recv_sem=sem,
                device_id=other_core,
                device_id_type=MESH,
            ).wait_recv()

        wait(part(turn, slot, piece), recv_sems.at[turn, slot, piece])
        if piece == SIZE_PIECE:
            wait(sizes.at[turn, slot], size_recv.at[turn, slot])

    def forward(turn, moves, on=()):
        for number, (slot, piece) in enumerate(landed(moves)):
            arrived(turn, slot, piece)
            for copy in to_core(turn, slot, piece):
                copy.start()
            if on:
                send_all(turn, on[number : number + 1])

    def gram_copy():
        return pltpu.make_async_remote_copy(
            src_ref=gram,
            dst_ref=gram_got,
            send_sem=pair_send.at[1],
            recv_sem=pair_recv.at[1],
            device_id=other_core,
            device_id_type=MESH,
        )

    def unpack(turn, index, pair, light):
        for core in range(2):
            here = pl.ds(pl.multiple_of(index * 2 * rows + core * rows, rows), rows)
            slot = 2 * pair + core
            if light:
                tops[here, :] = from_codes(codes[turn, slot]).astype(BF16)
            else:
                top, low = halves(from_codes(codes[turn, slot]))
                tops[here, :] = top
                lows[here, :] = low
            size = sizes[turn, slot]
            scales[:, here] = size * size

    def inner(first, count, light):
        here = pl.ds(first, count)
        if light:
            values = dot_nt(lhs[0:rows, :], tops[here, :])
            weights[0:rows, here] = (values * scales[0:1, here]).astype(BF16)
        else:
            both = dot_nt(lhs[...], tops[here, :])
            values = both[:rows] + both[rows:] + dot_nt(lhs[0:rows, :], lows[here, :])
            top, low = halves(values * scales[0:1, here])
            weights[0:rows, here] = top
            weights[rows:, here] = low

    def outer(first, count, out, add, light):
        cut = 512
        here = slice(first, first + count)
        for start in range(0, wide, cut):
            lanes = slice(start, start + cut)
            if light:
                value = dot_nn(weights[0:rows, here], tops[here, lanes])
            else:
                both = dot_nn(weights[:, here], tops[here, lanes])
                value = both[:rows] + both[rows:] + dot_nn(weights[0:rows, here], lows[here, lanes])
            if add:
                value = value + out[:, lanes]
            out[:, lanes] = value

    def set_lhs(values):
        top, low = halves(values)
        lhs[0:rows, :] = top
        lhs[rows:, :] = low

    def input_gram(light):
        top, low = halves(xin[...])
        xin_top[...] = top
        if light:
            gram[...] = dot_nt(xin_top[...], xin_top[...])
        else:
            xin_low[...] = low
            cross = dot_nt(xin_top[...], xin_low[...])
            gram[...] = dot_nt(xin_top[...], xin_top[...]) + (cross + jnp.transpose(cross))
        gram_copy().start()

    def input_step(light):
        gram_copy().wait()
        square_of = gram[...] + gram_got[...]
        top, low = halves(square_of)
        if light:
            poly = NS_B * square_of + NS_C * dot_nn(top, top)
        else:
            cross = dot_nn(top, low)
            poly = NS_B * square_of + NS_C * (dot_nn(top, top) + (cross + jnp.transpose(cross)))
        top, low = halves(poly)
        cut = 512
        for start in range(0, xin.shape[1], cut):
            lanes = slice(start, start + cut)
            change = dot_nn(top, xin_top[:, lanes])
            if not light:
                change = change + dot_nn(low, xin_top[:, lanes]) + dot_nn(top, xin_low[:, lanes])
            xin[:, lanes] = NS_A * xin[:, lanes] + change

    def by_weight(number, limit, work):
        @pl.when(number < limit)
        def _():
            work(True)

        @pl.when(number >= limit)
        def _():
            work(False)

    def iteration(number, carry):
        turn = number % 2
        values = xs[...]
        largest = jnp.maximum(jnp.max(jnp.abs(values), axis=1, keepdims=True), 1e-30)
        codes[turn, 0] = to_codes(values * (TOP_CODE / largest))
        lane_size = jnp.sum(jnp.where(eye, largest, 0.0), axis=0, keepdims=True)
        sizes[turn, 0] = jnp.broadcast_to(lane_size * (1.0 / TOP_CODE), (8, rows))
        send_all(turn, FIRST)
        for piece in range(3):
            for copy in to_core(turn, 0, piece):
                copy.start()
        send_all(turn, SECOND)
        set_lhs(values)

        def first_pass(index, carry):
            pair = index + (index // 3) * (1 - index // 4) - (index // 4) * (1 - index // 5)

            @pl.when(index == 1)
            def _():
                forward(turn, FIRST, SECOND_ON)
                send_all(turn, THIRD)
                send_all(turn, THIRD_A)

                by_weight(number, LIGHT_IN, input_gram)

                forward(turn, SECOND, THIRD_B)
                forward(turn, SECOND_ON, THIRD_C)

                by_weight(number, LIGHT_IN, input_step)

                forward(turn, THIRD)

            @pl.when(index == 4)
            def _():
                forward(turn, THIRD_A)
                forward(turn, THIRD_B)

            @pl.when(index == 7)
            def _():
                forward(turn, THIRD_C)

            for piece in range(3):
                arrived(turn, 2 * pair + 1, piece)

            def work(light):
                unpack(turn, index, pair, light)
                inner(pl.multiple_of(index * 2 * rows, 2 * rows), 2 * rows, light)

            by_weight(number, LIGHT_HID, work)

            @pl.when(index == 3)
            def _():
                by_weight(number, LIGHT_HID, lambda light: outer(0, wide // 2, us, False, light))

            return carry

        lax.fori_loop(0, 8, first_pass, 0)

        def second_pass(light):
            outer(wide // 2, wide // 2, us, True, light)
            set_lhs(us[...])
            for first in range(0, wide, 512):
                inner(first, 512, light)
            outer(0, wide, vs, False, light)

        by_weight(number, LIGHT_HID, second_pass)
        xs[...] = NS_A * xs[...] + NS_B * us[...] + NS_C * vs[...]
        for move in MOVES:
            for copy in send(turn, move):
                copy.wait_send()
        for pair in range(8):
            for piece in range(3):
                for copy in to_core(turn, 2 * pair, piece):
                    copy.wait_send()
        return carry

    lax.fori_loop(0, NS, iteration, 0)

    place = blk % 4
    copies = []
    for rel, target in ((1, dims[0]), (2, dims[2]), (3, diagonal)):
        copies.append(
            pltpu.make_async_remote_copy(
                src_ref=xs.at[:, pl.ds(pl.multiple_of(target["blk"] * height, height), height)],
                dst_ref=back.at[place],
                send_sem=back_send.at[rel - 1],
                recv_sem=back_recv.at[rel - 1],
                device_id=target,
                device_id_type=MESH,
            )
        )
        copies[-1].start()
    hid_ref[place] = xs[:, my_lanes]
    inp_ref[...] = xin[:, my_half]
    for copy in copies:
        copy.wait_recv()
    for target in (dims[0], dims[2], diagonal):
        other = target["blk"] % 4
        hid_ref[other] = back[other]
    for copy in copies + spread + told:
        copy.wait_send()


def muon(stats, red_hid, mom_hid, red_in, mom_in, red_far, mom_far, wide):
    rows = red_hid.shape[0] // 4
    height = red_hid.shape[1]
    deep, part_wide = red_in.shape
    vmem = pl.BlockSpec(memory_space=pltpu.VMEM)
    sem = pltpu.SemaphoreType.DMA
    return pl.pallas_call(
        muon_kernel,
        out_shape=(
            jax.ShapeDtypeStruct((4, rows, height), F32),
            jax.ShapeDtypeStruct((deep, part_wide), F32),
            jax.ShapeDtypeStruct(red_hid.shape, F32),
            jax.ShapeDtypeStruct(red_in.shape, F32),
            jax.ShapeDtypeStruct((8, 128), F32),
        ),
        in_specs=[vmem] * 7,
        out_specs=(vmem,) * 5,
        scratch_shapes=[
            pltpu.VMEM((2, 16, rows, wide), I16),
            pltpu.VMEM((2, 16, 8, rows), F32),
            pltpu.VMEM((wide, wide), BF16),
            pltpu.VMEM((wide, wide), BF16),
            pltpu.VMEM((8, wide), F32),
            pltpu.VMEM((2 * rows, wide), BF16),
            pltpu.VMEM((rows, wide), F32),
            pltpu.VMEM((rows, wide), F32),
            pltpu.VMEM((rows, wide), F32),
            pltpu.VMEM((2 * rows, wide), BF16),
            pltpu.VMEM((deep, 2 * part_wide), F32),
            pltpu.VMEM((deep, 2 * part_wide), BF16),
            pltpu.VMEM((deep, 2 * part_wide), BF16),
            pltpu.VMEM((deep, deep), F32),
            pltpu.VMEM((deep, deep), F32),
            pltpu.VMEM((4, rows, height), F32),
            pltpu.VMEM((8, 8, 128), F32),
            pltpu.VMEM((4, 8, 128), F32),
            pltpu.VMEM((4, rows, height), I16),
            pltpu.VMEM((8, rows, height), I16),
            pltpu.VMEM((4, 8, rows), F32),
            pltpu.VMEM((8, 8, rows), F32),
            sem((len(MOVES),)),
            sem((8, 4)),
            sem((2, 16, 3)),
            sem((3,)),
            sem((3,)),
            sem((10,)),
            sem((10,)),
            sem((2, 7)),
            sem((2, 7)),
            sem((2,)),
            sem((2,)),
            sem((len(MOVES),)),
            sem((2, 16)),
        ],
        compiler_params=pltpu.CompilerParams(
            collective_id=0, has_side_effects=True, vmem_limit_bytes=60 * 1024 * 1024
        ),
    )(stats, red_hid, mom_hid, red_in, mom_in, red_far, mom_far)


def plain_body(
    frames,
    labels,
    mask,
    w_input,
    w_hidden,
    w_output,
    biases,
    mom_input,
    mom_hidden,
    out_first,
    out_second,
    bias_first,
    bias_second,
    res_input,
    res_hidden,
    res_output,
):
    ncol = lax.axis_size("col")
    nblk = lax.axis_size("blk")
    col_index = lax.axis_index("col")
    hcol = w_input.shape[1]
    scol = w_output.shape[1]
    micro = frames.shape[0]
    slot_count = frames.shape[1] * micro * nblk * ncol
    bias_row = biases[0]
    b_one = bias_row[:hcol]
    b_two = bias_row[hcol : 2 * hcol]
    b_out = bias_row[2 * hcol :]
    low_input = w_input.astype(jnp.bfloat16)
    row_tags = jnp.where(mask > 0, labels, -1)
    grad_input = jnp.zeros(w_input.shape, jnp.float32)
    grad_hidden = jnp.zeros((w_hidden.shape[0] * nblk, hcol), jnp.float32)
    grad_output = jnp.zeros((w_output.shape[0] * nblk, scol), jnp.float32)
    grad_bias = jnp.zeros(bias_row.shape, jnp.float32)
    loss_local = jnp.zeros((), jnp.float32)
    for micro_step in range(micro):
        low_hidden, low_output = (
            lax.all_gather(w_hidden.astype(jnp.bfloat16), "blk", axis=0, tiled=True),
            lax.all_gather(w_output.astype(jnp.bfloat16), "blk", axis=0, tiled=True),
        )
        inputs = lax.all_gather(frames[micro_step], "col", axis=0, tiled=True)
        tags_group = lax.all_gather(row_tags[micro_step], "col", axis=0, tiled=True)
        sig_one = jax.nn.sigmoid(matmul(inputs, low_input) + b_one)
        h_one = spread_cols(sig_one.astype(jnp.bfloat16))
        sig_two = jax.nn.sigmoid(matmul(h_one, low_hidden) + b_two)
        h_two = spread_cols(sig_two.astype(jnp.bfloat16))
        logits = matmul(h_two, low_output) + b_out
        row_top = lax.pmax(jnp.max(logits, axis=1), "col")
        exponent = jnp.exp(logits - row_top[:, None])
        target_hit = jnp.arange(scol)[None, :] == (tags_group - col_index * scol)[:, None]
        row_total, picked = lax.psum(
            (jnp.sum(exponent, axis=1), jnp.sum(jnp.where(target_hit, logits, 0.0), axis=1)), "col"
        )
        live_rows = tags_group >= 0
        loss_local = loss_local + jnp.sum(
            jnp.where(live_rows, row_top + jnp.log(row_total) - picked, 0.0)
        )
        probs = exponent / row_total[:, None]
        d_logits = (
            jnp.where(live_rows[:, None], probs - target_hit.astype(jnp.float32), 0.0) / slot_count
        ).astype(jnp.bfloat16)
        grad_output = grad_output + inner_rows(h_two, d_logits)
        d_h_two = reduce_cols(outer_cols(d_logits, low_output))
        d_z_two = (d_h_two * sig_two * (1.0 - sig_two)).astype(jnp.bfloat16)
        grad_hidden = grad_hidden + inner_rows(h_one, d_z_two)
        d_h_one = reduce_cols(outer_cols(d_z_two, low_hidden))
        d_z_one = (d_h_one * sig_one * (1.0 - sig_one)).astype(jnp.bfloat16)
        grad_input = grad_input + inner_rows(inputs, d_z_one)
        grad_bias = grad_bias + jnp.concatenate(
            [
                jnp.sum(d_z_one.astype(jnp.float32), axis=0),
                jnp.sum(d_z_two.astype(jnp.float32), axis=0),
                jnp.sum(d_logits.astype(jnp.float32), axis=0),
            ]
        )
    q_input, next_res_input = squash(grad_input, res_input[0])
    q_hidden, next_res_hidden = squash(grad_hidden, res_hidden[0])
    q_output, next_res_output = squash(grad_output, res_output[0])
    red_hidden, red_output = (
        lax.psum_scatter(q_hidden, "blk", scatter_dimension=0, tiled=True),
        lax.psum_scatter(q_output, "blk", scatter_dimension=0, tiled=True),
    )
    red_input, red_bias, loss_sum = lax.psum((q_input, grad_bias, loss_local), "blk")
    share_blk = 1.0 / nblk
    grad_square = (
        share_blk * (jnp.sum(red_input * red_input) + jnp.sum(red_bias * red_bias))
        + jnp.sum(red_hidden * red_hidden)
        + jnp.sum(red_output * red_output)
    )
    clip_norm = jnp.sqrt(lax.psum(grad_square, ("blk", "col")))
    factor = jnp.minimum(1.0, CLIP / clip_norm)
    next_mom_input = 0.5 * mom_input + factor * red_input
    next_mom_hidden = 0.5 * mom_hidden + factor * red_hidden
    square_input, square_hidden = lax.psum(
        (
            share_blk * jnp.sum(next_mom_input * next_mom_input),
            jnp.sum(next_mom_hidden * next_mom_hidden),
        ),
        ("blk", "col"),
    )
    iter_input = next_mom_input / (jnp.sqrt(square_input) + 1e-07)
    iter_hidden = next_mom_hidden / (jnp.sqrt(square_hidden) + 1e-07)
    for turn_index in range(NS):
        rows_hidden = collect_rows(iter_hidden)
        gram_input, gram_hidden = lax.psum(
            (precise(iter_input, iter_input.T), precise(iter_hidden, rows_hidden.T)), "col"
        )
        image_input = precise(gram_input, iter_input)
        image_hidden = precise(gram_hidden, rows_hidden)
        iter_input = (
            NS_A * iter_input + NS_B * image_input + NS_C * precise(gram_input, image_input)
        )
        iter_hidden = (
            NS_A * iter_hidden
            + NS_B * image_hidden
            + NS_C * precise(gram_hidden, collect_rows(image_hidden))
        )
    muon_scale = LR_MUON * 0.2 * math.sqrt(hcol * ncol)
    new_input = w_input * (1.0 - LR_MUON * WD_MUON) - muon_scale * iter_input
    new_hidden = w_hidden * (1.0 - LR_MUON * WD_MUON) - muon_scale * iter_hidden
    new_output, next_out_first, next_out_second = adam_step(
        w_output, factor * red_output, out_first, out_second
    )
    new_biases, next_bias_first, next_bias_second = adam_step(
        biases, factor * red_bias[None, :], bias_first, bias_second
    )
    return (
        loss_sum,
        clip_norm,
        new_input,
        new_hidden,
        new_output,
        new_biases,
        next_mom_input,
        next_mom_hidden,
        next_out_first,
        next_out_second,
        next_bias_first,
        next_bias_second,
        next_res_input[None],
        next_res_hidden[None],
        next_res_output[None],
    )


def fast_body(
    frames,
    labels,
    mask,
    w_input,
    w_hidden,
    w_output,
    biases,
    mom_input,
    mom_hidden,
    out_first,
    out_second,
    bias_first,
    bias_second,
    res_input,
    res_hidden,
    res_output,
):
    ncol = lax.axis_size("col")
    nblk = lax.axis_size("blk")
    col_index = lax.axis_index("col")
    blk_index = lax.axis_index("blk")
    hcol = w_input.shape[1]
    scol = w_output.shape[1]
    micro = frames.shape[0]
    slot_count = frames.shape[1] * micro * nblk * ncol
    bias_row = biases[0]
    deep = w_input.shape[0]
    padded = 512
    rows_out = OUT_GROUPS * OUT_ROWS
    mom_in_padded = jnp.pad(mom_input, ((0, padded - deep), (0, 0)))
    own_tags = jnp.where(mask > 0, labels, -1).reshape(1, -1)
    layer_biases = jnp.pad(bias_row[: 2 * hcol].reshape(2, hcol), ((0, 6), (0, 0)))
    blocks = -(-rows_out // 128)
    out_biases = jnp.pad(bias_row[2 * hcol :], (0, blocks * 128 - scol)).reshape(blocks, 128)
    inputs, h_one, h_two, slope_one, slope_two, low_hidden, low_output, mom_far, d_logits, bias_sums, losses = (
        forward_pass(
            frames.reshape(-1, deep),
            jnp.broadcast_to(own_tags, (8, own_tags.shape[1])),
            w_input,
            w_hidden,
            w_output.T,
            layer_biases,
            out_biases,
            mom_in_padded,
            slot_count,
        )
    )
    loss_local = jnp.sum(losses)
    partial = inner_rows(d_logits, low_output)
    vec = jnp.concatenate([jnp.zeros((2 * hcol,), F32), bias_sums.reshape(-1)[:scol], loss_local[None]])
    vec = jnp.pad(vec, (0, 4096 - vec.shape[0])).reshape(32, 128)
    next_out, codes, sizes = squash_out(d_logits, h_two, res_output[0].T)
    next_hid, next_in, red_out, red_hid, red_in, red_far, vec_sum, stats = reduce_grads(
        codes,
        sizes,
        h_one,
        inputs,
        partial,
        slope_two,
        slope_one,
        low_hidden,
        res_hidden[0].T,
        jnp.pad(res_input[0], ((0, padded - deep), (0, 0))).T,
        vec,
        scol,
        deep,
    )
    next_res_output = next_out.transpose(1, 2, 0)
    next_res_hidden = next_hid.T
    next_res_input = next_in[:, :deep].T
    red_output = red_out[:scol].T
    vec_sum = vec_sum.reshape(-1)
    red_bias = vec_sum[: bias_row.shape[0]]
    loss_sum = vec_sum[bias_row.shape[0]]
    done_hidden, done_input, mom_hid_next, mom_in_next, norms = muon(
        stats,
        red_hid,
        mom_hidden.T,
        red_in,
        mom_in_padded,
        red_far,
        mom_far,
        hcol * ncol,
    )
    clip_norm = norms[0, 0]
    factor = norms[4, 0]
    next_mom_hidden = mom_hid_next.T
    next_mom_input = mom_in_next[:deep]
    done_hidden = done_hidden.reshape(hcol, w_hidden.shape[0]).T
    muon_scale = LR_MUON * 0.2 * math.sqrt(hcol * ncol)
    new_input = w_input * (1.0 - LR_MUON * WD_MUON) - muon_scale * done_input[:deep]
    new_hidden = w_hidden * (1.0 - LR_MUON * WD_MUON) - muon_scale * done_hidden
    new_output, next_out_first, next_out_second = adam_step(
        w_output, factor * red_output, out_first, out_second
    )
    new_biases, next_bias_first, next_bias_second = adam_step(
        biases, factor * red_bias[None, :], bias_first, bias_second
    )
    return (
        loss_sum,
        clip_norm,
        new_input,
        new_hidden,
        new_output,
        new_biases,
        next_mom_input,
        next_mom_hidden,
        next_out_first,
        next_out_second,
        next_bias_first,
        next_bias_second,
        next_res_input[None],
        next_res_hidden[None],
        next_res_output,
    )


def solution(mesh):
    in_specs = (
        P(None, ("blk", "col"), None),
        P(None, ("blk", "col")),
        P(None, ("blk", "col")),
        P(None, "col"),
        P("blk", "col"),
        P("blk", "col"),
        P("col", None),
        P(None, "col"),
        P("blk", "col"),
        P("blk", "col"),
        P("blk", "col"),
        P("col", None),
        P("col", None),
        P("blk", None, "col"),
        P("blk", None, "col"),
        P("blk", None, "col"),
    )
    out_specs = (
        P(),
        P(),
        P(None, "col"),
        P("blk", "col"),
        P("blk", "col"),
        P("col", None),
        P(None, "col"),
        P("blk", "col"),
        P("blk", "col"),
        P("blk", "col"),
        P("col", None),
        P("col", None),
        P("blk", None, "col"),
        P("blk", None, "col"),
        P("blk", None, "col"),
    )
    cubes = mesh.shape["blk"] == 8 and mesh.shape["col"] == 4
    body = fast_body if cubes else plain_body
    return jax.shard_map(body, mesh=mesh, in_specs=in_specs, out_specs=out_specs, check_vma=False)
```

```python
import functools
import math

import jax
import jax.numpy as jnp
from jax import lax
from jax.experimental import pallas as pl
from jax.experimental.pallas import tpu as pltpu
from jax.sharding import PartitionSpec as P

NS = 5
STEP = 5


NS_A = 3.4445
NS_B = -4.775
NS_C = 2.0315
CLIP = 0.002
LR_MUON = 0.1
WD_MUON = 0.01
LR_ADAM = 0.03
WD_ADAM = 0.1

MESH = pl.DeviceIdType.MESH
F32 = jnp.float32
BF16 = jnp.bfloat16
I16 = jnp.int16
LN2 = math.log(2.0)
TOP_CODE = 32700.0
LEVELS = 64.0


def matmul(left_side, right_side):
    return jnp.dot(left_side, right_side, preferred_element_type=jnp.float32)


def inner_rows(left_side, right_side):
    return lax.dot_general(
        left_side, right_side, (((0,), (0,)), ((), ())), preferred_element_type=jnp.float32
    )


def outer_cols(left_side, right_side):
    return lax.dot_general(
        left_side, right_side, (((1,), (1,)), ((), ())), preferred_element_type=jnp.float32
    )


def precise(left_side, right_side):
    return jnp.dot(
        left_side, right_side, precision=lax.Precision.HIGHEST, preferred_element_type=jnp.float32
    )


def spread_cols(values):
    return lax.all_gather(values, "col", axis=1, tiled=True)


def reduce_cols(values):
    return lax.psum_scatter(values, "col", scatter_dimension=1, tiled=True)


def collect_rows(values):
    return lax.all_gather(values, "blk", axis=0, tiled=True)


def squash(gradient, resid):
    value = gradient + resid.astype(jnp.float32)
    scale = jnp.mean(jnp.abs(value), axis=0, keepdims=True) + 1e-12
    signed = scale * jnp.tanh(2.0 * value / scale)
    return (signed, value - signed)


def adam_step(weight, gradient, first, second):
    first = 0.5 * first + 0.5 * gradient
    second = 0.95 * second + 0.05 * gradient * gradient
    update = first / (1.0 - 0.5**STEP) / (jnp.sqrt(second / (1.0 - 0.95**STEP)) + 1e-08)
    return (weight - LR_ADAM * (update + WD_ADAM * weight), first, second)


def halves(values):
    top = values.astype(BF16)
    return top, (values - top.astype(F32)).astype(BF16)


def dot_nn(left_side, right_side):
    return lax.dot_general(
        left_side, right_side, (((1,), (0,)), ((), ())), preferred_element_type=F32
    )


def dot_nt(left_side, right_side):
    return lax.dot_general(
        left_side, right_side, (((1,), (1,)), ((), ())), preferred_element_type=F32
    )


RING = 8
STEPS = RING - 1
OUT_ROWS = 592
OUT_GROUPS = 4
HID_ROWS = 512
HID_GROUP = 4
IN_GROUP = 5
TURN_AT = 5
CROSS_AT = 6
HID_AT = 13
FINISH_AT = 14
IN_AT = 20
HID_HOP = 3


def ring_place(blk):
    odd = blk % 2
    return (blk // 2) * (1 - odd) + (7 - blk // 2) * odd


def ring_blk(place):
    back = place // 4
    return 2 * place * (1 - back) + (15 - 2 * place) * back


def scale_code(size):
    return jnp.ceil(jnp.log(jnp.maximum(size, 1e-30)) * (LEVELS / LN2))


def code_scale(code):
    return jnp.exp(code * (LN2 / LEVELS))


def to_codes(values):
    return jnp.round(values).astype(jnp.int32).astype(I16)


def from_codes(codes):
    return codes.astype(jnp.int32).astype(F32)


def chunk_of(lane):
    number = lane // 256
    return number // 2 if number % 2 == 0 else 7 - number // 2


def squash_kernel(senones, dl_ref, h_ref, res_ref, next_ref, codes_ref, size_ref, grad, cols, marks):
    group = pl.program_id(0)
    rows, wide = grad.shape
    valid = senones - group * rows
    for first, count in ((0, rows // 32 * 16), (rows // 32 * 16, rows - rows // 32 * 16)):
        there = slice(first, first + count)
        total = jnp.zeros((count, 128), F32)
        for lane in range(0, wide, 512):
            value = dot_nn(dl_ref[there, :], h_ref[:, lane : lane + 512])
            value = value + res_ref[there, lane : lane + 512].astype(F32)
            row = first + lax.broadcasted_iota(jnp.int32, value.shape, 0)
            value = jnp.where(row < valid, value, 0.0)
            grad[there, lane : lane + 512] = value
            value = jnp.abs(value)
            for part in range(0, 512, 128):
                total = total + value[:, part : part + 128]
        size = jnp.sum(total, axis=1, keepdims=True) * (1.0 / wide) + 1e-12
        size = jnp.broadcast_to(size, (count, 128))
        marks[there, :] = size
        cols[0, there, :] = size
        cols[1, there, :] = 2.0 / size

    def some(number, carry):
        row = pl.multiple_of(number * 16, 16)
        size = cols[0, pl.ds(row, 16), :]
        steep = cols[1, pl.ds(row, 16), :]
        for lane in range(0, wide, 128):
            piece = grad[pl.ds(row, 16), lane : lane + 128]
            curve = jnp.tanh(piece * steep)
            codes_ref[0, 2 * chunk_of(lane) + lane // 128 % 2, pl.ds(row, 16), :] = to_codes(
                curve * TOP_CODE
            )
            next_ref[pl.ds(row, 16), 0, lane : lane + 128] = piece - size * curve
        return carry

    lax.fori_loop(0, rows // 16, some, 0)
    marks[rows:, :] = jnp.zeros((marks.shape[0] - rows, 128), F32)
    lines = [jnp.transpose(marks[first : first + 128, :])[0:1, :] for first in range(0, rows, 128)]
    lines.append(jnp.zeros((8 - len(lines), 128), F32))
    size_ref[0] = jnp.concatenate(lines, axis=0)


def squash_out(dl, h_two, res_out):
    senones, wide = res_out.shape
    frames = dl.shape[1]
    return pl.pallas_call(
        functools.partial(squash_kernel, senones),
        grid=(OUT_GROUPS,),
        out_shape=(
            jax.ShapeDtypeStruct((senones, 1, wide), F32),
            jax.ShapeDtypeStruct((OUT_GROUPS, 2 * RING, OUT_ROWS, 128), I16),
            jax.ShapeDtypeStruct((OUT_GROUPS, 8, 128), F32),
        ),
        in_specs=[
            pl.BlockSpec((OUT_ROWS, frames), lambda group: (group, 0)),
            pl.BlockSpec((frames, wide), lambda group: (0, 0)),
            pl.BlockSpec((OUT_ROWS, wide), lambda group: (group, 0)),
        ],
        out_specs=(
            pl.BlockSpec((OUT_ROWS, 1, wide), lambda group: (group, 0, 0)),
            pl.BlockSpec((1, 2 * RING, OUT_ROWS, 128), lambda group: (group, 0, 0, 0)),
            pl.BlockSpec((1, 8, 128), lambda group: (group, 0, 0)),
        ),
        scratch_shapes=[
            pltpu.VMEM((OUT_ROWS, wide), F32),
            pltpu.VMEM((2, OUT_ROWS, 128), F32),
            pltpu.VMEM((640, 128), F32),
        ],
        compiler_params=pltpu.CompilerParams(vmem_limit_bytes=60 * 1024 * 1024),
    )(dl, h_two, res_out)


def reduce_kernel(
    deep,
    senones,
    codes_ref,
    sizes_ref,
    h_one_ref,
    x_ref,
    part_ref,
    slope_two_ref,
    slope_one_ref,
    w_hid_ref,
    res_hid_ref,
    res_in_ref,
    vec_ref,
    next_hid_ref,
    next_in_ref,
    red_out_ref,
    red_hid_ref,
    red_in_ref,
    red_far_ref,
    vec_sum_ref,
    stats_ref,
    grad,
    turned,
    res_buf,
    h_buf,
    slope_buf,
    marks,
    cols,
    keep_sums,
    dz,
    dz_two,
    dz_one,
    core_out,
    core_got,
    far_out,
    far_got,
    own_out,
    got_out,
    own_hid,
    got_hid,
    own_in,
    got_in,
    share_in,
    share_far,
    sizes,
    shares,
    vec,
    vecs,
    res_sems,
    load_sems,
    code_sems,
    slope_sems,
    core_send,
    core_recv,
    far_send,
    far_recv,
    out_send,
    out_recv,
    hid_send,
    hid_recv,
    in_send,
    in_recv,
    share_send,
    share_recv,
    vec_send,
    vec_recv,
    size_send,
    size_recv,
    share_far_send,
    share_far_recv,
):
    blk = lax.axis_index("blk")
    col = lax.axis_index("col")
    here = ring_place(blk)
    core, high = col % 2, col // 2
    cores = {"col": col + 1 - 2 * core}
    across = {"col": (col + 2) % 4}
    barrier = pltpu.get_barrier_semaphore()
    for target in (cores, across, *({"blk": (blk + away) % RING} for away in range(1, RING))):
        pl.semaphore_signal(barrier, inc=1, device_id=target, device_id_type=MESH)

    def code_copy(group):
        return pltpu.make_async_copy(codes_ref.at[group], own_out.at[group], code_sems.at[group])

    def hid_res_copy(part):
        return pltpu.make_async_copy(
            res_hid_ref.at[:, pl.ds(part * 256, 256)],
            res_buf.at[part],
            res_sems.at[part],
        )

    def hid_next_copy(part):
        return pltpu.make_async_copy(
            turned, next_hid_ref.at[:, pl.ds(part * 256, 256)], load_sems.at[1]
        )

    def load(src, dst):
        return pltpu.make_async_copy(src, dst, load_sems.at[0])

    for group in range(OUT_GROUPS):
        code_copy(group).start()
    for part in range(2):
        hid_res_copy(part).start()
    load(h_one_ref, h_buf).start()
    marks[...] = jnp.zeros_like(marks)
    stats_ref[...] = jnp.zeros_like(stats_ref)
    vec[...] = vec_ref[...]
    pl.semaphore_wait(barrier, RING + 1)

    CHUNK = 256
    units = slope_buf.shape[2]

    def slope_copy(layer, block):
        rows = pl.ds(pl.multiple_of(block * CHUNK, CHUNK), CHUNK)
        src = (slope_two_ref, slope_one_ref)[layer]
        return pltpu.make_async_copy(src.at[rows, :], slope_buf.at[block % 2], slope_sems.at[block % 2])

    def core_move(layer, block):
        return pltpu.make_async_remote_copy(
            src_ref=core_out.at[block % 2],
            dst_ref=core_got.at[layer, block],
            send_sem=core_send.at[block % 2],
            recv_sem=core_recv.at[layer, block],
            device_id=cores,
            device_id_type=MESH,
        )

    def far_move(layer, block):
        return pltpu.make_async_remote_copy(
            src_ref=far_out.at[block % 2],
            dst_ref=far_got.at[layer, block],
            send_sem=far_send.at[block % 2],
            recv_sem=far_recv.at[layer, block],
            device_id=across,
            device_id_type=MESH,
        )

    def lanes_of(number):
        return pl.ds(pl.multiple_of(number * units, units), units)

    def rows_at(number):
        return pl.ds(pl.multiple_of(number * 16, 16), 16)

    def free(copy, layer, block):
        @pl.when((layer > 0) | (block >= 2))
        def _():
            copy.wait_send()

    def lane_codes(first):
        return jnp.transpose(marks[first : first + 128, :])[0:1, :]

    def set_factors():
        top = jnp.max(cols[0, 0:CHUNK, :], axis=1, keepdims=True)
        code = scale_code(top)
        marks[0:CHUNK, :] = jnp.broadcast_to(code, (CHUNK, 128))
        cols[1, 0:CHUNK, :] = jnp.broadcast_to(TOP_CODE / code_scale(code), (CHUNK, 128))

    def largest(values):
        return functools.reduce(
            jnp.maximum,
            [
                jnp.abs(value[:, lane : lane + 128])
                for value in values
                for lane in range(0, value.shape[1], 128)
            ],
        )

    def scaled(values, factor):
        return jnp.concatenate(
            [values[:, lane : lane + 128] * factor for lane in range(0, values.shape[1], 128)], axis=1
        )

    def put_scale(out):
        codes = jnp.concatenate(
            [lane_codes(0), lane_codes(128), jnp.zeros((14, 128), F32)], axis=0
        )
        out[CHUNK : CHUNK + 16, 0:128] = codes.astype(jnp.int32).astype(I16)

    def read_scale(got):
        step = code_scale(from_codes(got[CHUNK : CHUNK + 16, 0:128])) * (1.0 / TOP_CODE)
        step = jnp.transpose(jnp.concatenate([step, jnp.zeros((112, 128), F32)], axis=0))
        for up in range(2):
            marks[CHUNK + up * 128 : CHUNK + (up + 1) * 128, :] = jnp.broadcast_to(
                step[:, up : up + 1], (128, 128)
            )

    def step_at(number):
        return marks[pl.ds(pl.multiple_of(CHUNK + number * 16, 16), 16), :]

    def split(layer, block):
        free(core_move(layer, block), layer, block)

        def measure(number, carry):
            rows = rows_at(number)
            cols[0, rows, :] = largest(
                [grad[rows, lanes_of(2 * half + 1 - core)] for half in range(2)]
            )
            return carry

        lax.fori_loop(0, CHUNK // 16, measure, 0)
        set_factors()

        def write(number, carry):
            rows = rows_at(number)
            factor = cols[1, rows, :]
            for half in range(2):
                there = slice(half * units, (half + 1) * units)
                core_out[block % 2, rows, there] = to_codes(
                    scaled(grad[rows, lanes_of(2 * half + 1 - core)], factor)
                )
                keep_sums[block, rows, there] = grad[rows, lanes_of(2 * half + core)]
            return carry

        lax.fori_loop(0, CHUNK // 16, write, 0)
        put_scale(core_out.at[block % 2])
        core_move(layer, block).start()

    def cross(layer, block):
        core_move(layer, block).wait_recv()
        free(far_move(layer, block), layer, block)
        got = core_got.at[layer, block]
        read_scale(got)

        def add(number, carry):
            rows = rows_at(number)
            near, away = lanes_of(high), lanes_of(1 - high)
            step = step_at(number)
            keep_sums[block, rows, near] += scaled(from_codes(got[rows, near]), step)
            value = keep_sums[block, rows, away] + scaled(from_codes(got[rows, away]), step)
            keep_sums[block, rows, away] = value
            cols[0, rows, :] = largest([value])
            return carry

        lax.fori_loop(0, CHUNK // 16, add, 0)
        set_factors()

        def write(number, carry):
            rows = rows_at(number)
            far_out[block % 2, rows, :] = to_codes(
                scaled(keep_sums[block, rows, lanes_of(1 - high)], cols[1, rows, :])
            )
            return carry

        lax.fori_loop(0, CHUNK // 16, write, 0)
        put_scale(far_out.at[block % 2])
        far_move(layer, block).start()

    def finish(layer, block):
        far_move(layer, block).wait_recv()
        slope_copy(layer, block).wait()
        got = far_got.at[layer, block]
        read_scale(got)

        def one(number, total):
            rows = rows_at(number)
            value = keep_sums[block, rows, lanes_of(high)] + scaled(
                from_codes(got[rows, :]), step_at(number)
            )
            value = (value * slope_buf[block % 2, rows, :]).astype(BF16)
            dz[rows, :] = value
            return total + value.astype(F32)

        total = lax.fori_loop(0, CHUNK // 16, one, jnp.zeros((16, units), F32))
        if layer == 0:

            @pl.when(block < 2)
            def _():
                slope_copy(0, block + 2).start()

            @pl.when(block >= 2)
            def _():
                slope_copy(1, block - 2).start()

        else:

            @pl.when(block < 2)
            def _():
                slope_copy(1, block + 2).start()

        total = jnp.sum(total, axis=0, keepdims=True)
        for number in range(units // 128):
            row = 4 * (1 - layer) + number
            vec[row : row + 1, :] += total[:, number * 128 : (number + 1) * 128]
        flipped = (dz_two, dz_one)[layer]
        for up in range(CHUNK // 128):
            there = pl.ds(pl.multiple_of(block * CHUNK + up * 128, 128), 128)
            for number in range(units // 128):
                tile = dz[up * 128 : (up + 1) * 128, number * 128 : (number + 1) * 128]
                flipped[number * 128 : (number + 1) * 128, there] = jnp.transpose(
                    tile.astype(F32)
                ).astype(BF16)

    def blocks(first, last, work):
        def one(block, carry):
            work(block)
            return carry

        lax.fori_loop(first, last, one, 0)

    def start_block(block):
        rows = pl.ds(pl.multiple_of(block * CHUNK, CHUNK), CHUNK)
        copy = pltpu.make_async_copy(part_ref.at[rows, :], grad.at[pl.ds(0, CHUNK), :], load_sems.at[1])
        copy.start()
        copy.wait()
        split(0, block)

    def turn_block(block):
        finish(0, block)
        for lane in range(0, grad.shape[1], 512):
            grad[0:CHUNK, lane : lane + 512] = dot_nt(dz[...], w_hid_ref[lane : lane + 512, :])
        split(1, block)

    core_out[:, CHUNK:, :] = jnp.zeros((2, 16, 2 * units), I16)
    far_out[:, CHUNK:, :] = jnp.zeros((2, 16, units), I16)
    slope_copy(0, 0).start()
    slope_copy(0, 1).start()
    def vec_copy(away):
        return pltpu.make_async_remote_copy(
            src_ref=vec,
            dst_ref=vecs.at[blk],
            send_sem=vec_send.at[away - 1],
            recv_sem=vec_recv.at[away - 1],
            device_id={"blk": (blk + away) % RING},
            device_id_type=MESH,
        )

    def set_rows(count, first_own, size):
        size = jnp.broadcast_to(size, (count, 128))
        marks[first_own : first_own + count, :] = size
        cols[0, 0:count, :] = size
        cols[1, 0:count, :] = 2.0 / size

    def tell_sizes(group):
        for away in range(1, RING):
            size_copy(group, away).start()

    def size_copy(group, away):
        return pltpu.make_async_remote_copy(
            src_ref=sizes.at[group, here],
            dst_ref=sizes.at[group, here],
            send_sem=size_send.at[group, away - 1],
            recv_sem=size_recv.at[group, away - 1],
            device_id={"blk": ring_blk((here + away) % RING)},
            device_id_type=MESH,
        )

    def set_sizes(rows, group):
        parts = [lane_codes(first) for first in range(0, rows, 128)]
        parts.append(jnp.zeros((8 - len(parts), 128), F32))
        sizes[group, here] = jnp.concatenate(parts, axis=0)
        tell_sizes(group)

    def make_shares(group, row_of):
        for away in range(1, RING):
            size_copy(group, away).wait_recv()
        for way in range(2):
            tiles = []
            for step in range(STEPS):
                mine = row_of(here, step, way)
                came = mine * 0.0
                for back in range(step + 1):
                    came = came + row_of((here - 1 - back + (2 + 2 * back) * way + RING) % RING, step, way)
                if step < STEPS - 1:
                    whole = 1.0 / jnp.maximum(came + mine, 1e-30)
                else:
                    whole = 1.0 / TOP_CODE
                tiles += [came * whole, mine * whole]
            tiles.append(jnp.zeros((16, 128), F32))
            shares[group, way] = jnp.transpose(jnp.concatenate(tiles, axis=0))

    def hid_group():
        load(h_one_ref, h_buf).wait()
        wide = grad.shape[1]
        for part in range(2):
            first = part * 256
            hid_res_copy(part).wait()
            total = jnp.zeros((256, 128), F32)
            for lane in range(0, wide, 512):
                value = dot_nn(dz_two[first : first + 256, :], h_buf[:, lane : lane + 512])
                value = value + jnp.transpose(res_buf[part, lane : lane + 512, :].astype(F32))
                grad[:, lane : lane + 512] = value
                value = jnp.abs(value)
                for more in range(0, 512, 128):
                    total = total + value[:, more : more + 128]
            set_rows(
                256, first, jnp.sum(total, axis=1, keepdims=True) * (1.0 / wide) + 1e-12
            )

            def some(number, carry, first=first):
                row = pl.multiple_of(number * 16, 16)
                size = cols[0, pl.ds(row, 16), :]
                steep = cols[1, pl.ds(row, 16), :]
                for lane in range(0, wide, 128):
                    piece = grad[pl.ds(row, 16), lane : lane + 128]
                    curve = jnp.tanh(piece * steep)
                    own_hid[2 * chunk_of(lane) + lane // 128 % 2, pl.ds(first + row, 16), :] = (
                        to_codes(curve * TOP_CODE)
                    )
                    grad[pl.ds(row, 16), lane : lane + 128] = piece - size * curve
                return carry

            lax.fori_loop(0, 16, some, 0)
            if part:
                hid_next_copy(part - 1).wait()
            for lane in range(0, wide, 128):
                turned[lane : lane + 128, :] = jnp.transpose(grad[:, lane : lane + 128])
            hid_next_copy(part).start()
        load(x_ref, h_buf.at[:, pl.ds(0, x_ref.shape[1])]).start()
        set_sizes(HID_ROWS, HID_GROUP)
        hid_next_copy(1).wait()

    def in_group():
        wide = x_ref.shape[1]
        load(x_ref, h_buf.at[:, pl.ds(0, wide)]).wait()
        for first in range(0, HID_ROWS, 256):
            grad[0:256, 0:wide] = dot_nn(dz_one[first : first + 256, :], h_buf[:, 0:wide])

            def add(number, carry, first=first):
                row = pl.multiple_of(number * 16, 16)
                place = pl.multiple_of(first + row, 16)
                value = grad[pl.ds(row, 16), 0:wide] + res_in_ref[pl.ds(place, 16), :].astype(F32)
                grad[pl.ds(row, 16), 0:wide] = value
                value = jnp.abs(value)
                cols[0, pl.ds(row, 16), :] = functools.reduce(
                    jnp.add, [value[:, lane : lane + 128] for lane in range(0, wide, 128)]
                )
                return carry

            lax.fori_loop(0, 16, add, 0)
            set_rows(
                256,
                first,
                jnp.sum(cols[0, 0:256, :], axis=1, keepdims=True) * (1.0 / deep) + 1e-12,
            )

            def some(number, carry, first=first):
                row = pl.multiple_of(number * 16, 16)
                place = pl.multiple_of(first + row, 16)
                size = cols[0, pl.ds(row, 16), :]
                steep = cols[1, pl.ds(row, 16), :]
                chunk = first // 64 + number // 4
                inside = pl.multiple_of(number % 4 * 16, 16)
                for lane in range(0, wide, 128):
                    piece = grad[pl.ds(row, 16), lane : lane + 128]
                    curve = jnp.tanh(piece * steep)
                    next_in_ref[pl.ds(place, 16), lane : lane + 128] = piece - size * curve
                    own_in[
                        2 * chunk + lane // 256, pl.ds(inside, 16), lane % 256 : lane % 256 + 128
                    ] = to_codes(curve * TOP_CODE)
                return carry

            lax.fori_loop(0, 16, some, 0)
        sizes[IN_GROUP, here] = jnp.concatenate(
            [lane_codes(64 * chunk) for chunk in range(RING)], axis=0
        )
        tell_sizes(IN_GROUP)

    def towards(way):
        return {"blk": ring_blk((here + 1 - 2 * way + RING) % RING)}

    def move(src, got, step, way, send_sem, recv_sem):
        return pltpu.make_async_remote_copy(
            src_ref=src,
            dst_ref=got.at[way, step],
            send_sem=send_sem.at[way, step],
            recv_sem=recv_sem.at[way, step],
            device_id=towards(way),
            device_id_type=MESH,
        )

    def first_moves(own, got, send_sem, recv_sem):
        for way in range(2):
            chunk = (here - 1 + 2 * way + RING) % RING
            move(own.at[2 * chunk + way], got, 0, way, send_sem, recv_sem).start()

    def hop(rows, own, got, group, step, send_sem, recv_sem, keep):
        for way in range(2):
            move(got.at[way, step], got, step, way, send_sem, recv_sem).wait_recv()

        def add(way, result):
            message = got.at[way, step]
            ahead = here - 2 - step + way * (4 + 2 * step) + 2 * RING
            mine = own.at[2 * (ahead % RING) + way]
            share = pltpu.roll(shares[group, way], (128 - 16 * step) % 128, 1)
            for number, first in enumerate(range(0, rows, 128)):
                count = min(128, rows - first)
                there = slice(first, first + count)
                result(
                    first,
                    count,
                    from_codes(message[there, :]) * share[0:count, number : number + 1]
                    + from_codes(mine[there, :]) * share[0:count, 8 + number : 9 + number],
                )

        @pl.when(step < STEPS - 1)
        def _():
            for way in range(2):

                def write(first, count, value, way=way):
                    got[way, step, first : first + count, :] = to_codes(value)

                add(way, write)
            for way in range(2):
                move(got.at[way, step], got, step + 1, way, send_sem, recv_sem).start()

        @pl.when(step == STEPS - 1)
        def _():
            for way in range(2):

                def finish_rows(first, count, value, way=way):
                    keep(way, first, count, value)
                    square = jnp.sum(value * value, axis=0, keepdims=True)
                    for lane in range(0, value.shape[1], 128):
                        stats_ref[0:1, :] += square[:, lane : lane + 128]

                add(way, finish_rows)

    def out_hop(group, step):
        def keep(way, first, count, value):
            row = pl.multiple_of(group * OUT_ROWS + first, 16)
            red_out_ref[pl.ds(row, count), way * 128 : (way + 1) * 128] = value

        hop(
            OUT_ROWS,
            own_out.at[group],
            got_out.at[group],
            group,
            step,
            out_send.at[group],
            out_recv.at[group],
            keep,
        )

    def hid_hop(step):
        def keep(way, first, count, value):
            red_hid_ref[first : first + count, way * 128 : (way + 1) * 128] = value

        hop(HID_ROWS, own_hid, got_hid, HID_GROUP, step, hid_send, hid_recv, keep)

    def share_move(step, way):
        place = (here - step + 2 * step * way + 2 * RING) % RING
        return pltpu.make_async_remote_copy(
            src_ref=share_in.at[way, place],
            dst_ref=share_in.at[way, place],
            send_sem=share_send.at[way, step],
            recv_sem=share_recv.at[way, step],
            device_id=towards(way),
            device_id_type=MESH,
        )

    def share_across(way, place):
        return pltpu.make_async_remote_copy(
            src_ref=share_in.at[way, place],
            dst_ref=share_far.at[way, place],
            send_sem=share_far_send.at[way, place],
            recv_sem=share_far_recv.at[way, place],
            device_id=across,
            device_id_type=MESH,
        )

    def in_hop(step):
        def keep(way, first, count, value):
            share_in[way, here] = value

        hop(64, own_in, got_in, IN_GROUP, step, in_send, in_recv, keep)

        @pl.when(step == STEPS - 1)
        def _():
            for way in range(2):
                share_move(0, way).start()
                share_across(way, here).start()

    def share_hop(step):
        for way in range(2):
            share_move(step, way).wait_recv()
            share_across(way, (here - 1 - step + (2 + 2 * step) * way + RING) % RING).start()

        @pl.when(step < STEPS - 1)
        def _():
            for way in range(2):
                share_move(step + 1, way).start()

    def in_step(index):
        @pl.when((index >= 0) & (index < STEPS))
        def _():
            in_hop(index)

        @pl.when((index >= STEPS) & (index < 2 * STEPS))
        def _():
            share_hop(index - STEPS)

    def chunk_row(place, step, way):
        chunk = (here - 2 - step + way * (4 + 2 * step) + 2 * RING) % RING
        line = sizes[IN_GROUP, place, pl.ds(chunk, 1), :]
        return jnp.broadcast_to(line, (8, 128))

    for group in range(OUT_GROUPS):
        sizes[group, here] = sizes_ref[group]
        tell_sizes(group)
        code_copy(group).wait()
        first_moves(own_out.at[group], got_out.at[group], out_send.at[group], out_recv.at[group])
    blocks(0, 4, start_block)

    def each(number, first, spacing, count, work):
        after = number - first

        @pl.when((after >= 0) & (after < spacing * count) & (after % spacing == 0))
        def _():
            work(after // spacing)

    def turn(number, carry):
        @pl.when(number < OUT_GROUPS)
        def _():
            make_shares(number, lambda place, step, way: sizes[number, place])

        @pl.when(number < OUT_GROUPS * STEPS)
        def _():
            out_hop(number % OUT_GROUPS, number // OUT_GROUPS)

        @pl.when(number == HID_AT + HID_HOP)
        def _():
            make_shares(HID_GROUP, lambda place, step, way: sizes[HID_GROUP, place])

        each(number, HID_AT + HID_HOP, HID_HOP, STEPS, hid_hop)

        @pl.when(number == IN_AT + 1)
        def _():
            make_shares(IN_GROUP, chunk_row)

        in_step(number - IN_AT - 1)
        each(number, 0, 1, 4, lambda block: cross(0, block))
        each(number, TURN_AT, 2, 4, turn_block)
        each(number, CROSS_AT, 2, 4, lambda block: cross(1, block))

        @pl.when(number == HID_AT)
        def _():
            hid_group()
            first_moves(own_hid, got_hid, hid_send, hid_recv)

        each(number, FINISH_AT, 2, 4, lambda block: finish(1, block))

        @pl.when(number == IN_AT)
        def _():
            in_group()
            first_moves(own_in, got_in, in_send, in_recv)
            for away in range(1, RING):
                vec_copy(away).start()

        return carry

    turns = max(IN_AT + 1 + 2 * STEPS, HID_AT + HID_HOP * STEPS + 1, OUT_GROUPS * STEPS)
    lax.fori_loop(0, turns, turn, 0)

    def unfold(shares_of, out):
        for place in range(0, RING, 2):
            for way in range(2):
                for lane in range(0, 256, 128):
                    tile = jnp.concatenate(
                        [shares_of[way, place + more, :, lane : lane + 128] for more in range(2)],
                        axis=0,
                    )
                    first = way * 256 + lane
                    out[first : first + 128, place * 64 : place * 64 + 128] = jnp.transpose(tile)

    unfold(share_in, red_in_ref)
    for place in range(RING):
        for way in range(2):
            share_across(way, place).wait_recv()
    unfold(share_far, red_far_ref)
    for away in range(1, RING):
        vec_copy(away).wait_recv()
    vecs[blk] = vec[...]
    total = vecs[0]
    for number in range(1, RING):
        total = total + vecs[number]
    vec_sum_ref[...] = total
    flat = 128 * lax.broadcasted_iota(jnp.int32, total.shape, 0) + lax.broadcasted_iota(
        jnp.int32, total.shape, 1
    )
    total = jnp.where(flat < 2 * units + senones, total, 0.0)
    stats_ref[1:2, :] = jnp.sum(total * total, axis=0, keepdims=True) * (1.0 / RING)
    for away in range(1, RING):
        vec_copy(away).wait_send()
        for group in range(OUT_GROUPS + 2):
            size_copy(group, away).wait_send()
    for slot in range(2):
        core_move(1, 2 + slot).wait_send()
        far_move(1, 2 + slot).wait_send()
    for way in range(2):
        for step in range(STEPS):
            for group in range(OUT_GROUPS):
                move(
                    got_out.at[group, way, step],
                    got_out.at[group],
                    step,
                    way,
                    out_send.at[group],
                    out_recv.at[group],
                ).wait_send()
            move(got_hid.at[way, step], got_hid, step, way, hid_send, hid_recv).wait_send()
            move(got_in.at[way, step], got_in, step, way, in_send, in_recv).wait_send()
            share_move(step, way).wait_send()
        for place in range(RING):
            share_across(way, place).wait_send()


def reduce_grads(
    codes, sizes, h_one, x, part, slope_two, slope_one, w_hid, res_hid, res_in, vec, senones, deep
):
    frames, wide = h_one.shape
    in_wide = x.shape[1]
    units = w_hid.shape[1]
    vmem = pl.BlockSpec(memory_space=pltpu.VMEM)
    hbm = pl.BlockSpec(memory_space=pl.ANY)
    message = OUT_ROWS
    hid_message = HID_ROWS
    in_message = 64
    sem = pltpu.SemaphoreType.DMA
    return pl.pallas_call(
        functools.partial(reduce_kernel, deep, senones),
        out_shape=(
            jax.ShapeDtypeStruct((wide, HID_ROWS), F32),
            jax.ShapeDtypeStruct((HID_ROWS, in_wide), F32),
            jax.ShapeDtypeStruct((OUT_GROUPS * OUT_ROWS, 256), F32),
            jax.ShapeDtypeStruct((HID_ROWS, 256), F32),
            jax.ShapeDtypeStruct((in_wide, HID_ROWS), F32),
            jax.ShapeDtypeStruct((in_wide, HID_ROWS), F32),
            jax.ShapeDtypeStruct(vec.shape, F32),
            jax.ShapeDtypeStruct((8, 128), F32),
        ),
        in_specs=[hbm, vmem] + [hbm] * 5 + [vmem, hbm, vmem, vmem],
        out_specs=(hbm,) + (vmem,) * 7,
        scratch_shapes=[
            pltpu.VMEM((256, wide), F32),
            pltpu.VMEM((wide, 256), F32),
            pltpu.VMEM((2, wide, 256), BF16),
            pltpu.VMEM((frames, wide), BF16),
            pltpu.VMEM((2, 256, units), F32),
            pltpu.VMEM((640, 128), F32),
            pltpu.VMEM((2, 256, 128), F32),
            pltpu.VMEM((4, 256, 2 * units), F32),
            pltpu.VMEM((256, units), BF16),
            pltpu.VMEM((units, frames), BF16),
            pltpu.VMEM((units, frames), BF16),
            pltpu.VMEM((2, 272, 2 * units), I16),
            pltpu.VMEM((2, 4, 272, 2 * units), I16),
            pltpu.VMEM((2, 272, units), I16),
            pltpu.VMEM((2, 4, 272, units), I16),
            pltpu.VMEM((OUT_GROUPS, 2 * RING, message, 128), I16),
            pltpu.VMEM((OUT_GROUPS, 2, STEPS, message, 128), I16),
            pltpu.VMEM((2 * RING, hid_message, 128), I16),
            pltpu.VMEM((2, STEPS, hid_message, 128), I16),
            pltpu.VMEM((2 * RING, in_message, 256), I16),
            pltpu.VMEM((2, STEPS, in_message, 256), I16),
            pltpu.VMEM((2, RING, 64, 256), F32),
            pltpu.VMEM((2, RING, 64, 256), F32),
            pltpu.VMEM((OUT_GROUPS + 2, RING, 8, 128), F32),
            pltpu.VMEM((OUT_GROUPS + 2, 2, 128, 128), F32),
            pltpu.VMEM(vec.shape, F32),
            pltpu.VMEM((RING,) + vec.shape, F32),
            sem((2,)),
            sem((2,)),
            sem((OUT_GROUPS,)),
            sem((2,)),
            sem((2,)),
            sem((2, 4)),
            sem((2,)),
            sem((2, 4)),
            sem((OUT_GROUPS, 2, STEPS)),
            sem((OUT_GROUPS, 2, STEPS)),
            sem((2, STEPS)),
            sem((2, STEPS)),
            sem((2, STEPS)),
            sem((2, STEPS)),
            sem((2, STEPS)),
            sem((2, STEPS)),
            sem((STEPS,)),
            sem((STEPS,)),
            sem((OUT_GROUPS + 2, STEPS)),
            sem((OUT_GROUPS + 2, STEPS)),
            sem((2, RING)),
            sem((2, RING)),
        ],
        compiler_params=pltpu.CompilerParams(
            collective_id=1, has_side_effects=True, vmem_limit_bytes=63 * 1024 * 1024
        ),
    )(codes, sizes, h_one, x, part, slope_two, slope_one, w_hid, res_hid, res_in, vec)


RING_STARTS = (0, 0, 5, 6, 7)
LAYER_TWO_WAVE = 7
LOGIT_WAVES = (11, 12, 13, 14)


def forward_kernel(
    slot_count,
    x_ref,
    tags_ref,
    w_in_ref,
    w_hid_ref,
    w_out_ref,
    bias_ref,
    bias_out_ref,
    mom_ref,
    x_out,
    h_one_out,
    h_two_out,
    slope_one_out,
    slope_two_out,
    w_hid_out,
    w_out_out,
    mom_far_ref,
    dl_ref,
    vec_ref,
    x_all,
    h_one,
    h_two,
    slope_one,
    slope_two,
    w_in,
    w_hid,
    w_out,
    curve,
    bias_col,
    tags,
    sums,
    ring_send,
    ring_recv,
    x_send,
    x_recv,
    h_send,
    h_recv,
    tag_send,
    tag_recv,
    sum_send,
    sum_recv,
    out_sems,
    mom_sems,
):
    blk = lax.axis_index("blk")
    col = lax.axis_index("col")
    here = ring_place(blk)
    senones, depth = w_out_ref.shape
    own_rows, deep = x_ref.shape
    units = w_hid_ref.shape[1]
    frames = x_all.shape[0]
    cores = {"col": col + 1 - 2 * (col % 2)}
    across = {"col": (col + 2) % 4}
    corner = {"col": (col + 2) % 4 + 1 - 2 * (col % 2)}
    others = (cores, across, corner)

    barrier = pltpu.get_barrier_semaphore()
    for target in others + tuple({"blk": ring_blk((here + way) % RING)} for way in (1, 7)):
        pl.semaphore_signal(barrier, inc=1, device_id=target, device_id_type=MESH)

    w_hid[pl.ds(pl.multiple_of(blk * depth, depth), depth), :] = w_hid_ref[...].astype(BF16)
    own_lanes = pl.ds(pl.multiple_of(blk * depth, depth), depth)
    w_out[senones // 16 * 16 :, own_lanes] = jnp.zeros(
        (w_out.shape[0] - senones // 16 * 16, depth), BF16
    )
    w_out[0:senones, own_lanes] = w_out_ref[...].astype(BF16)
    own_frames = pl.ds(pl.multiple_of(col * own_rows, own_rows), own_rows)
    x_all[own_frames, :] = jnp.zeros((own_rows, x_all.shape[1]), BF16)
    x_all[own_frames, 0:deep] = x_ref[...]
    tags[col] = tags_ref[...]
    sums[...] = jnp.zeros_like(sums)
    pl.semaphore_wait(barrier, 5)

    def ring_part(group, origin, way):
        start = pl.multiple_of(origin * depth + way * 128, 128)
        if group == 0:
            return w_hid.at[pl.ds(start, 128), :]
        return w_out.at[pl.ds((group - 1) * OUT_ROWS, OUT_ROWS), pl.ds(start, 128)]

    def ring_move(group, step, way):
        origin = ring_blk((here - step + 2 * step * way + RING) % RING)
        part = ring_part(group, origin, way)
        return pltpu.make_async_remote_copy(
            src_ref=part,
            dst_ref=part,
            send_sem=ring_send.at[group, way, step],
            recv_sem=ring_recv.at[group, way, step],
            device_id={"blk": ring_blk((here + 1 - 2 * way + RING) % RING)},
            device_id_type=MESH,
        )

    def ring_wave(wave):
        for group, start in enumerate(RING_STARTS):
            step = wave - 1 - start
            for way in range(2):
                if step == -1:
                    ring_move(group, 0, way).start()
                if 0 <= step < STEPS:
                    ring_move(group, step, way).wait_recv()
                    if step < STEPS - 1:
                        ring_move(group, step + 1, way).start()

    def copy_to(target, src, send_sem, recv_sem):
        return pltpu.make_async_remote_copy(
            src_ref=src,
            dst_ref=src,
            send_sem=send_sem,
            recv_sem=recv_sem,
            device_id=target,
            device_id_type=MESH,
        )

    def rows_of(owner):
        return pl.ds(pl.multiple_of(owner * own_rows, own_rows), own_rows)

    def lanes_of(owner):
        return pl.ds(pl.multiple_of(owner * units, units), units)

    def x_move(number):
        owner = across["col"] if number == 2 else col
        target = across if number == 1 else cores
        return copy_to(target, x_all.at[rows_of(owner), :], x_send.at[number], x_recv.at[number])

    def h_move(layer, number, block):
        owner = across["col"] if number == 2 else col
        target = across if number == 1 else cores
        whole = (h_one, h_two)[layer]
        part = whole.at[pl.ds(block * own_rows, own_rows), lanes_of(owner)]
        return copy_to(
            target, part, h_send.at[layer, number, block], h_recv.at[layer, number, block]
        )

    def h_start(layer, block):
        h_move(layer, 0, block).start()
        h_move(layer, 1, block).start()

    def h_forward(layer, block):
        h_move(layer, 1, block).wait_recv()
        h_move(layer, 2, block).start()

    def h_ready(layer, block):
        h_move(layer, 0, block).wait_recv()
        h_move(layer, 2, block).wait_recv()

    ring_wave(0)
    x_move(0).start()
    x_move(1).start()
    tag_copies = [
        copy_to(target, tags.at[col], tag_send.at[number], tag_recv.at[number])
        for number, target in enumerate(others)
    ]
    for copy in tag_copies:
        copy.start()
    w_in[...] = jnp.zeros_like(w_in)
    w_in[0:deep, :] = w_in_ref[...].astype(BF16)
    for number in range(bias_out_ref.shape[0]):
        line = jnp.broadcast_to(bias_out_ref[number : number + 1, :], (128, 128))
        bias_col[number * 128 : (number + 1) * 128, :] = jnp.transpose(line)
    ring_wave(1)
    x_move(1).wait_recv()
    x_move(2).start()
    x_move(0).wait_recv()
    x_move(2).wait_recv()

    def layer(number, block, inputs, weights, whole, slopes):
        there = slice(block * own_rows, (block + 1) * own_rows)
        value = jax.nn.sigmoid(
            dot_nn(inputs[there, :], weights[...]) + bias_ref[number : number + 1, :]
        )
        slopes[there, :] = value * (1.0 - value)
        whole[there, lanes_of(col)] = value.astype(BF16)
        h_start(number, block)

    outs = []

    def put(src, dst):
        copy = pltpu.make_async_copy(src, dst, out_sems.at[len(outs)])
        copy.start()
        outs.append(copy)

    for block in range(4):
        layer(0, block, x_all, w_in, h_one, slope_one)
    put(x_all, x_out)
    put(slope_one, slope_one_out)

    def all_tags():
        return jnp.concatenate([tags[owner, 0:1, :] for owner in range(4)], axis=1)

    def own_row(line):
        line = line - col * senones
        return jnp.where(line < senones, line, -1)

    def logits(group):
        first = group * OUT_ROWS
        half = frames // 2
        for part in range(2):
            curve[first : first + OUT_ROWS, part * half : (part + 1) * half] = dot_nt(
                w_out[first : first + OUT_ROWS, :], h_two[part * half : (part + 1) * half, :]
            )
        base = lax.broadcasted_iota(jnp.int32, (16, frames), 0)

        def largest(number, top):
            row = pl.multiple_of(first + number * 16, 16)
            value = curve[pl.ds(row, 16), :] + bias_col[pl.ds(row, 16), 0:1]
            if group == OUT_GROUPS - 1:
                value = jnp.where(base + row < senones, value, -1e30)
            curve[pl.ds(row, 16), :] = value
            return jnp.maximum(top, value)

        top = lax.fori_loop(0, OUT_ROWS // 16, largest, jnp.full((16, frames), -1e30, F32))
        top = jnp.max(top, axis=0, keepdims=True)
        line = jnp.broadcast_to(own_row(all_tags()), (16, frames))

        def exponents(number, carry):
            total, picked = carry
            row = pl.multiple_of(first + number * 16, 16)
            value = curve[pl.ds(row, 16), :]
            power = jnp.exp(value - top)
            curve[pl.ds(row, 16), :] = power
            return total + power, picked + jnp.where(base + row == line, value, 0.0)

        blank = jnp.zeros((16, frames), F32)
        total, picked = lax.fori_loop(0, OUT_ROWS // 16, exponents, (blank, blank))
        sums[col, group : group + 1, :] = top
        sums[col, 4 + group : 5 + group, :] = jnp.sum(total, axis=0, keepdims=True)
        sums[col, 8 + group : 9 + group, :] = jnp.sum(picked, axis=0, keepdims=True)

    mom_copy = pltpu.make_async_remote_copy(
        src_ref=mom_ref,
        dst_ref=mom_far_ref,
        send_sem=mom_sems.at[0],
        recv_sem=mom_sems.at[1],
        device_id=across,
        device_id_type=MESH,
    )
    last_wave = RING_STARTS[-1] + STEPS
    for wave in range(2, last_wave + 1):
        ring_wave(wave)
        if 2 <= wave < 6:
            h_forward(0, wave - 2)
        if wave == LAYER_TWO_WAVE:
            for block in range(4):
                h_ready(0, block)
                layer(1, block, h_one, w_hid, h_two, slope_two)
            put(h_one, h_one_out)
            put(slope_two, slope_two_out)
            put(w_hid, w_hid_out)
        if LAYER_TWO_WAVE < wave <= LAYER_TWO_WAVE + 4:
            h_forward(1, wave - LAYER_TWO_WAVE - 1)
        for group, when in enumerate(LOGIT_WAVES):
            if wave == when:
                if group == 0:
                    for block in range(4):
                        h_ready(1, block)
                    put(h_two, h_two_out)
                    mom_copy.start()
                    for copy in tag_copies:
                        copy.wait_recv()
                rows = pl.ds(group * OUT_ROWS, OUT_ROWS)
                put(w_out.at[rows, :], w_out_out.at[rows, :])
                logits(group)

    sum_copies = [
        copy_to(target, sums.at[col], sum_send.at[number], sum_recv.at[number])
        for number, target in enumerate(others)
    ]
    for copy in sum_copies:
        copy.start()
    for copy in sum_copies:
        copy.wait_recv()

    def lines(first):
        return [sums[owner, first + group : first + group + 1, :] for owner in range(4) for group in range(4)]

    tops = lines(0)
    top = functools.reduce(jnp.maximum, tops)
    total = functools.reduce(
        jnp.add, [size * jnp.exp(own - top) for own, size in zip(tops, lines(4), strict=True)]
    )
    picked = functools.reduce(jnp.add, lines(8))
    line = all_tags()
    live = line >= 0
    loss = jnp.where(live, top + jnp.log(total) - picked, 0.0)
    loss = jnp.sum(loss, axis=1, keepdims=True)
    weight = jnp.where(live, 1.0 / slot_count, 0.0)
    line = jnp.broadcast_to(own_row(line), (16, frames))
    hit_weight = jnp.broadcast_to(weight, (16, frames))
    base = lax.broadcasted_iota(jnp.int32, (16, frames), 0)
    bias_col[...] = jnp.zeros_like(bias_col)
    for group in range(OUT_GROUPS):
        share = jnp.exp(sums[col, group : group + 1, :] - top) / total * weight

        def gradient(number, carry, first=group * OUT_ROWS, share=share):
            row = pl.multiple_of(first + number * 16, 16)
            value = curve[pl.ds(row, 16), :] * share - jnp.where(base + row == line, hit_weight, 0.0)
            value = value.astype(BF16)
            dl_ref[pl.ds(row, 16), :] = value
            value = value.astype(F32)
            bias_col[pl.ds(row, 16), :] = functools.reduce(
                jnp.add, [value[:, lane : lane + 128] for lane in range(0, frames, 128)]
            )
            return carry

        lax.fori_loop(0, OUT_ROWS // 16, gradient, 0)
    vec_ref[...] = jnp.zeros_like(vec_ref)
    row = 2 * units // 128
    for number in range(bias_out_ref.shape[0]):
        line = jnp.transpose(bias_col[number * 128 : (number + 1) * 128, :])
        line = jnp.sum(line, axis=0, keepdims=True)
        place = 128 * number + lax.broadcasted_iota(jnp.int32, line.shape, 1)
        line = jnp.where(place < senones, line, jnp.where(place == senones, loss, 0.0))
        vec_ref[row + number : row + number + 1, :] = line

    for group in range(len(RING_STARTS)):
        for way in range(2):
            for step in range(STEPS):
                ring_move(group, step, way).wait_send()
    for number in range(3):
        x_move(number).wait_send()
        for block in range(4):
            h_move(0, number, block).wait_send()
            h_move(1, number, block).wait_send()
    for copy in tag_copies + sum_copies:
        copy.wait_send()
    mom_copy.wait()
    for copy in outs:
        copy.wait()


def forward_pass(x, tags, w_in, w_hid, w_out, bias, bias_out, mom, slot_count):
    own_rows = x.shape[0]
    units = w_hid.shape[1]
    frames = 4 * own_rows
    wide = 4 * units
    rows = OUT_GROUPS * OUT_ROWS
    blocks = bias_out.shape[0]
    vmem = pl.BlockSpec(memory_space=pltpu.VMEM)
    hbm = pl.BlockSpec(memory_space=pl.ANY)
    sem = pltpu.SemaphoreType.DMA
    kept = (
        ((frames, 512), BF16),
        ((frames, wide), BF16),
        ((frames, wide), BF16),
        ((frames, units), F32),
        ((frames, units), F32),
        ((wide, units), BF16),
        ((rows, wide), BF16),
    )
    return pl.pallas_call(
        functools.partial(forward_kernel, slot_count),
        out_shape=tuple(jax.ShapeDtypeStruct(shape, kind) for shape, kind in kept)
        + (
            jax.ShapeDtypeStruct(mom.shape, F32),
            jax.ShapeDtypeStruct((rows, frames), BF16),
            jax.ShapeDtypeStruct((32, 128), F32),
        ),
        in_specs=[vmem] * 7 + [hbm],
        out_specs=(hbm,) * 8 + (vmem,) * 2,
        scratch_shapes=[pltpu.VMEM(shape, kind) for shape, kind in kept[:5]]
        + [
            pltpu.VMEM((512, units), BF16),
            pltpu.VMEM((wide, units), BF16),
            pltpu.VMEM((rows, wide), BF16),
            pltpu.VMEM((rows, frames), F32),
            pltpu.VMEM((blocks * 128, 128), F32),
            pltpu.VMEM((4,) + tags.shape, jnp.int32),
            pltpu.VMEM((4, 16, frames), F32),
            sem((5, 2, STEPS)),
            sem((5, 2, STEPS)),
            sem((3,)),
            sem((3,)),
            sem((2, 3, 4)),
            sem((2, 3, 4)),
            sem((3,)),
            sem((3,)),
            sem((3,)),
            sem((3,)),
            sem((16,)),
            sem((2,)),
        ],
        compiler_params=pltpu.CompilerParams(
            collective_id=2, has_side_effects=True, vmem_limit_bytes=60 * 1024 * 1024
        ),
    )(x, tags, w_in, w_hid, w_out, bias, bias_out, mom)


DIM_BITS = (2, 4, 8)
ORDERS = ((0, 1, 2), (1, 2, 0), (2, 0, 1))
PIECES = (
    ((0, 48, 0, 1792),),
    ((48, 96, 0, 1792),),
    ((96, 128, 0, 2048), (0, 96, 1792, 2048)),
)
SIZE_PIECE = 2
LIGHT_HID = 3
LIGHT_IN = 2


def stage_sends(stage, sources):
    moves = []
    for piece, order in enumerate(ORDERS):
        slot = sum(DIM_BITS[order[index]] for index in sources)
        moves.append((piece, slot, order[stage]))
    return moves


def landed(moves):
    return [(slot | DIM_BITS[dim], piece) for piece, slot, dim in moves]


FIRST = stage_sends(0, ())
SECOND = stage_sends(1, ())
SECOND_ON = stage_sends(1, (0,))
THIRD = stage_sends(2, ())
THIRD_A = stage_sends(2, (0,))
THIRD_B = stage_sends(2, (1,))
THIRD_C = stage_sends(2, (0, 1))
MOVES = FIRST + SECOND + SECOND_ON + THIRD + THIRD_A + THIRD_B + THIRD_C


def muon_kernel(
    stats_ref,
    red_hid_ref,
    mom_hid_ref,
    red_in_ref,
    mom_in_ref,
    red_far_ref,
    mom_far_ref,
    hid_ref,
    inp_ref,
    next_hid_ref,
    next_in_ref,
    norm_ref,
    codes,
    sizes,
    tops,
    lows,
    scales,
    weights,
    xs,
    us,
    vs,
    lhs,
    xin,
    xin_top,
    xin_low,
    gram,
    gram_got,
    back,
    sums,
    sums_got,
    spread_out,
    spread_got,
    spread_size_out,
    spread_size_got,
    send_sems,
    core_sems,
    recv_sems,
    back_send,
    back_recv,
    sums_send,
    sums_recv,
    spread_send,
    spread_recv,
    pair_send,
    pair_recv,
):
    blk = lax.axis_index("blk")
    col = lax.axis_index("col")
    rows, wide = xs.shape
    height = back.shape[2]
    deep = mom_in_ref.shape[0]
    part_wide = inp_ref.shape[1]
    other_core = {"col": col + 1 - 2 * (col % 2)}
    dims = (
        {"blk": blk + 1 - 2 * (blk % 2)},
        {"col": (col + 2) % 4},
        {"blk": blk + 2 - 4 * ((blk // 2) % 2)},
    )
    diagonal = {"blk": 4 * (blk // 4) + 3 - blk % 4}
    barrier = pltpu.get_barrier_semaphore()
    corner = {"col": (col + 2) % 4 + 1 - 2 * (col % 2)}
    cols = (other_core, dims[1], corner)
    for target in (*cols, *({"blk": (blk + away) % 8} for away in range(1, 8))):
        pl.semaphore_signal(barrier, inc=1, device_id=target, device_id_type=MESH)

    def fold(values):
        line = jnp.sum(values, axis=0, keepdims=True)
        return sum(line[:, lane : lane + 128] for lane in range(0, line.shape[1], 128))

    share = 0.125
    sums[blk, 0:1, :] = fold(stats_ref[...])
    sums[blk, 1:2, :] = fold(mom_hid_ref[...] * mom_hid_ref[...])
    red_hid = jnp.transpose(red_hid_ref[...])
    sums[blk, 2:3, :] = fold(mom_hid_ref[...] * red_hid)
    sums[blk, 3:4, :] = fold(red_hid_ref[...] * red_hid_ref[...])
    sums[blk, 4:5, :] = fold(mom_in_ref[...] * mom_in_ref[...]) * share
    sums[blk, 5:6, :] = fold(mom_in_ref[...] * red_in_ref[0:deep, :]) * share
    sums[blk, 6:7, :] = fold(red_in_ref[0:deep, :] * red_in_ref[0:deep, :]) * share
    sums[blk, 7:8, :] = jnp.zeros((1, 128), F32)
    eye = lax.broadcasted_iota(jnp.int32, (rows, rows), 0) == lax.broadcasted_iota(
        jnp.int32, (rows, rows), 1
    )
    pl.semaphore_wait(barrier, 10)

    def tell(own, targets, first):
        copies = []
        for number, target in enumerate(targets, start=first):
            copies.append(
                pltpu.make_async_remote_copy(
                    src_ref=own,
                    dst_ref=own,
                    send_sem=sums_send.at[number],
                    recv_sem=sums_recv.at[number],
                    device_id=target,
                    device_id_type=MESH,
                )
            )
            copies[-1].start()
        for copy in copies:
            copy.wait_recv()
        return copies

    told = tell(sums.at[blk], [{"blk": (blk + away) % 8} for away in range(1, 8)], 0)
    sums_got[col] = functools.reduce(jnp.add, [sums[number] for number in range(8)])
    told += tell(sums_got.at[col], cols, 7)
    whole = functools.reduce(jnp.add, [sums_got[number] for number in range(4)])
    whole = jnp.sum(whole, axis=1, keepdims=True)
    clip = jnp.sqrt(whole[0:1])
    factor = jnp.minimum(1.0, CLIP / clip)

    def norm_of(first):
        square = (
            0.25 * whole[first : first + 1]
            + factor * whole[first + 1 : first + 2]
            + factor * factor * whole[first + 2 : first + 3]
        )
        return 1.0 / (jnp.sqrt(jnp.maximum(square, 0.0)) + 1e-07)

    norm_ref[0:4, :] = jnp.broadcast_to(clip, (4, 128))
    norm_ref[4:8, :] = jnp.broadcast_to(factor, (4, 128))
    next_hid_ref[...] = 0.5 * mom_hid_ref[...] + factor * jnp.transpose(red_hid_ref[...])
    next_in_ref[...] = 0.5 * mom_in_ref[...] + factor * red_in_ref[0:deep, :]

    my_lanes = pl.ds(pl.multiple_of(blk * height, height), height)
    for number in range(4):
        there = slice(number * rows, (number + 1) * rows)
        value = jnp.transpose(next_hid_ref[:, there])
        largest = jnp.maximum(jnp.max(jnp.abs(value), axis=1, keepdims=True), 1e-30)
        spread_out[number] = to_codes(value * (TOP_CODE / largest))
        line = jnp.sum(jnp.where(eye, largest, 0.0), axis=0, keepdims=True)
        spread_size_out[number] = jnp.broadcast_to(line * (1.0 / TOP_CODE), (8, rows))
    spread = []
    for away in range(1, 8):
        target = (blk + away) % 8
        for kind, (src, dst) in enumerate(
            ((spread_out, spread_got), (spread_size_out, spread_size_got))
        ):
            spread.append(
                pltpu.make_async_remote_copy(
                    src_ref=src.at[target % 4],
                    dst_ref=dst.at[blk],
                    send_sem=spread_send.at[kind, away - 1],
                    recv_sem=spread_recv.at[kind, away - 1],
                    device_id={"blk": target},
                    device_id_type=MESH,
                )
            )
            spread[-1].start()
    high = col // 2
    my_half = pl.ds(pl.multiple_of(high * part_wide, part_wide), part_wide)
    far_half = pl.ds(pl.multiple_of((1 - high) * part_wide, part_wide), part_wide)
    in_scale = norm_of(4)
    xin[deep:, :] = jnp.zeros((xin.shape[0] - deep, xin.shape[1]), F32)
    xin[0:deep, my_half] = next_in_ref[...] * in_scale
    xin[0:deep, far_half] = (
        0.5 * mom_far_ref[...] + factor * red_far_ref[0:deep, :]
    ) * in_scale
    spread_got[blk] = spread_out[blk % 4]
    spread_size_got[blk] = spread_size_out[blk % 4]
    for copy in spread:
        copy.wait_recv()
    hid_scale = norm_of(1)
    for number in range(8):
        size = jnp.broadcast_to(spread_size_got[number, 0:1, :], (rows, rows))
        size = jnp.transpose(size) * hid_scale
        for lane in range(0, height, 128):
            xs[:, number * height + lane : number * height + lane + 128] = (
                from_codes(spread_got[number, :, lane : lane + 128]) * size
            )

    numbers = {move: number for number, move in enumerate(MOVES)}

    def parts(turn, slot, piece):
        refs = [
            codes.at[turn, slot, pl.ds(top, low - top), pl.ds(left, right - left)]
            for top, low, left, right in PIECES[piece]
        ]
        numbered = [(piece, refs[0])]
        if piece == SIZE_PIECE:
            numbered += [(3, refs[1]), (4, sizes.at[turn, slot])]
        return numbered

    def send(turn, move):
        piece, slot, dim = move
        there = slot | DIM_BITS[dim]
        return [
            pltpu.make_async_remote_copy(
                src_ref=src,
                dst_ref=dst,
                send_sem=send_sems.at[numbers[move], max(number - 2, 0)],
                recv_sem=recv_sems.at[turn, there, number],
                device_id=dims[dim],
                device_id_type=MESH,
            )
            for (number, src), (_, dst) in zip(
                parts(turn, slot, piece), parts(turn, there, piece), strict=True
            )
        ]

    def send_all(turn, moves):
        for move in moves:
            for copy in send(turn, move):
                copy.start()

    def to_core(turn, slot, piece):
        return [
            pltpu.make_async_remote_copy(
                src_ref=src,
                dst_ref=dst,
                send_sem=core_sems.at[slot // 2, number],
                recv_sem=recv_sems.at[turn, slot + 1, number],
                device_id=other_core,
                device_id_type=MESH,
            )
            for (number, src), (_, dst) in zip(
                parts(turn, slot, piece), parts(turn, slot + 1, piece), strict=True
            )
        ]

    def arrived(turn, slot, piece):
        for number, ref in parts(turn, slot, piece):
            pltpu.make_async_remote_copy(
                src_ref=ref,
                dst_ref=ref,
                send_sem=core_sems.at[0, 0],
                recv_sem=recv_sems.at[turn, slot, number],
                device_id=other_core,
                device_id_type=MESH,
            ).wait_recv()

    def forward(turn, moves, on=()):
        for number, (slot, piece) in enumerate(landed(moves)):
            arrived(turn, slot, piece)
            for copy in to_core(turn, slot, piece):
                copy.start()
            if on:
                send_all(turn, on[number : number + 1])

    def gram_copy():
        return pltpu.make_async_remote_copy(
            src_ref=gram,
            dst_ref=gram_got,
            send_sem=pair_send.at[1],
            recv_sem=pair_recv.at[1],
            device_id=other_core,
            device_id_type=MESH,
        )

    def unpack(turn, index, pair, light):
        for core in range(2):
            here = pl.ds(pl.multiple_of(index * 2 * rows + core * rows, rows), rows)
            slot = 2 * pair + core
            if light:
                tops[here, :] = from_codes(codes[turn, slot]).astype(BF16)
            else:
                top, low = halves(from_codes(codes[turn, slot]))
                tops[here, :] = top
                lows[here, :] = low
            size = sizes[turn, slot]
            scales[:, here] = size * size

    def inner(first, count, light):
        here = pl.ds(first, count)
        if light:
            values = dot_nt(lhs[0:rows, :], tops[here, :])
            weights[0:rows, here] = (values * scales[0:1, here]).astype(BF16)
        else:
            both = dot_nt(lhs[...], tops[here, :])
            values = both[:rows] + both[rows:] + dot_nt(lhs[0:rows, :], lows[here, :])
            top, low = halves(values * scales[0:1, here])
            weights[0:rows, here] = top
            weights[rows:, here] = low

    def outer(first, count, out, add, light):
        cut = 512
        here = slice(first, first + count)
        for start in range(0, wide, cut):
            lanes = slice(start, start + cut)
            if light:
                value = dot_nn(weights[0:rows, here], tops[here, lanes])
            else:
                both = dot_nn(weights[:, here], tops[here, lanes])
                value = both[:rows] + both[rows:] + dot_nn(weights[0:rows, here], lows[here, lanes])
            if add:
                value = value + out[:, lanes]
            out[:, lanes] = value

    def set_lhs(values):
        top, low = halves(values)
        lhs[0:rows, :] = top
        lhs[rows:, :] = low

    def input_gram(light):
        top, low = halves(xin[...])
        xin_top[...] = top
        if light:
            gram[...] = dot_nt(xin_top[...], xin_top[...])
        else:
            xin_low[...] = low
            cross = dot_nt(xin_top[...], xin_low[...])
            gram[...] = dot_nt(xin_top[...], xin_top[...]) + (cross + jnp.transpose(cross))
        gram_copy().start()

    def input_step(light):
        gram_copy().wait()
        square_of = gram[...] + gram_got[...]
        top, low = halves(square_of)
        if light:
            poly = NS_B * square_of + NS_C * dot_nn(top, top)
        else:
            cross = dot_nn(top, low)
            poly = NS_B * square_of + NS_C * (dot_nn(top, top) + (cross + jnp.transpose(cross)))
        top, low = halves(poly)
        cut = 512
        for start in range(0, xin.shape[1], cut):
            lanes = slice(start, start + cut)
            change = dot_nn(top, xin_top[:, lanes])
            if not light:
                change = change + dot_nn(low, xin_top[:, lanes]) + dot_nn(top, xin_low[:, lanes])
            xin[:, lanes] = NS_A * xin[:, lanes] + change

    def by_weight(number, limit, work):
        @pl.when(number < limit)
        def _():
            work(True)

        @pl.when(number >= limit)
        def _():
            work(False)

    def iteration(number, carry):
        turn = number % 2
        values = xs[...]
        largest = jnp.maximum(jnp.max(jnp.abs(values), axis=1, keepdims=True), 1e-30)
        codes[turn, 0] = to_codes(values * (TOP_CODE / largest))
        lane_size = jnp.sum(jnp.where(eye, largest, 0.0), axis=0, keepdims=True)
        sizes[turn, 0] = jnp.broadcast_to(lane_size * (1.0 / TOP_CODE), (8, rows))
        send_all(turn, FIRST)
        for piece in range(3):
            for copy in to_core(turn, 0, piece):
                copy.start()
        send_all(turn, SECOND)
        set_lhs(values)

        def first_pass(index, carry):
            pair = index + (index // 3) * (1 - index // 4) - (index // 4) * (1 - index // 5)

            @pl.when(index == 1)
            def _():
                forward(turn, FIRST, SECOND_ON)
                send_all(turn, THIRD)
                send_all(turn, THIRD_A)

                by_weight(number, LIGHT_IN, input_gram)

                forward(turn, SECOND, THIRD_B)
                forward(turn, SECOND_ON, THIRD_C)

                by_weight(number, LIGHT_IN, input_step)

                forward(turn, THIRD)

            @pl.when(index == 4)
            def _():
                forward(turn, THIRD_A)
                forward(turn, THIRD_B)

            @pl.when(index == 7)
            def _():
                forward(turn, THIRD_C)

            for piece in range(3):
                arrived(turn, 2 * pair + 1, piece)

            def work(light):
                unpack(turn, index, pair, light)
                inner(pl.multiple_of(index * 2 * rows, 2 * rows), 2 * rows, light)

            by_weight(number, LIGHT_HID, work)

            @pl.when(index == 3)
            def _():
                by_weight(number, LIGHT_HID, lambda light: outer(0, wide // 2, us, False, light))

            return carry

        lax.fori_loop(0, 8, first_pass, 0)

        def second_pass(light):
            outer(wide // 2, wide // 2, us, True, light)
            set_lhs(us[...])
            for first in range(0, wide, 512):
                inner(first, 512, light)
            outer(0, wide, vs, False, light)

        by_weight(number, LIGHT_HID, second_pass)
        xs[...] = NS_A * xs[...] + NS_B * us[...] + NS_C * vs[...]
        for move in MOVES:
            for copy in send(turn, move):
                copy.wait_send()
        for pair in range(8):
            for piece in range(3):
                for copy in to_core(turn, 2 * pair, piece):
                    copy.wait_send()
        return carry

    lax.fori_loop(0, NS, iteration, 0)

    place = blk % 4
    copies = []
    for rel, target in ((1, dims[0]), (2, dims[2]), (3, diagonal)):
        copies.append(
            pltpu.make_async_remote_copy(
                src_ref=xs.at[:, pl.ds(pl.multiple_of(target["blk"] * height, height), height)],
                dst_ref=back.at[place],
                send_sem=back_send.at[rel - 1],
                recv_sem=back_recv.at[rel - 1],
                device_id=target,
                device_id_type=MESH,
            )
        )
        copies[-1].start()
    back[place] = xs[:, my_lanes]
    inp_ref[...] = xin[0:deep, my_half]
    for copy in copies:
        copy.wait_recv()
    for number in range(4):
        hid_ref[:, number * rows : (number + 1) * rows] = jnp.transpose(back[number])
    for copy in copies + spread + told:
        copy.wait_send()


def muon(stats, red_hid, mom_hid, red_in, mom_in, red_far, mom_far, wide):
    rows = red_hid.shape[0] // 4
    height = red_hid.shape[1]
    deep, part_wide = red_in.shape
    vmem = pl.BlockSpec(memory_space=pltpu.VMEM)
    sem = pltpu.SemaphoreType.DMA
    return pl.pallas_call(
        muon_kernel,
        out_shape=(
            jax.ShapeDtypeStruct(mom_hid.shape, F32),
            jax.ShapeDtypeStruct(mom_in.shape, F32),
            jax.ShapeDtypeStruct(mom_hid.shape, F32),
            jax.ShapeDtypeStruct(mom_in.shape, F32),
            jax.ShapeDtypeStruct((8, 128), F32),
        ),
        in_specs=[vmem] * 7,
        out_specs=(vmem,) * 5,
        scratch_shapes=[
            pltpu.VMEM((2, 16, rows, wide), I16),
            pltpu.VMEM((2, 16, 8, rows), F32),
            pltpu.VMEM((wide, wide), BF16),
            pltpu.VMEM((wide, wide), BF16),
            pltpu.VMEM((8, wide), F32),
            pltpu.VMEM((2 * rows, wide), BF16),
            pltpu.VMEM((rows, wide), F32),
            pltpu.VMEM((rows, wide), F32),
            pltpu.VMEM((rows, wide), F32),
            pltpu.VMEM((2 * rows, wide), BF16),
            pltpu.VMEM((deep, 2 * part_wide), F32),
            pltpu.VMEM((deep, 2 * part_wide), BF16),
            pltpu.VMEM((deep, 2 * part_wide), BF16),
            pltpu.VMEM((deep, deep), F32),
            pltpu.VMEM((deep, deep), F32),
            pltpu.VMEM((4, rows, height), F32),
            pltpu.VMEM((8, 8, 128), F32),
            pltpu.VMEM((4, 8, 128), F32),
            pltpu.VMEM((4, rows, height), I16),
            pltpu.VMEM((8, rows, height), I16),
            pltpu.VMEM((4, 8, rows), F32),
            pltpu.VMEM((8, 8, rows), F32),
            sem((len(MOVES), 3)),
            sem((8, 5)),
            sem((2, 16, 5)),
            sem((3,)),
            sem((3,)),
            sem((10,)),
            sem((10,)),
            sem((2, 7)),
            sem((2, 7)),
            sem((2,)),
            sem((2,)),
        ],
        compiler_params=pltpu.CompilerParams(
            collective_id=0, has_side_effects=True, vmem_limit_bytes=60 * 1024 * 1024
        ),
    )(stats, red_hid, mom_hid, red_in, mom_in, red_far, mom_far)


def plain_body(
    frames,
    labels,
    mask,
    w_input,
    w_hidden,
    w_output,
    biases,
    mom_input,
    mom_hidden,
    out_first,
    out_second,
    bias_first,
    bias_second,
    res_input,
    res_hidden,
    res_output,
):
    ncol = lax.axis_size("col")
    nblk = lax.axis_size("blk")
    col_index = lax.axis_index("col")
    hcol = w_input.shape[1]
    scol = w_output.shape[1]
    micro = frames.shape[0]
    slot_count = frames.shape[1] * micro * nblk * ncol
    bias_row = biases[0]
    b_one = bias_row[:hcol]
    b_two = bias_row[hcol : 2 * hcol]
    b_out = bias_row[2 * hcol :]
    low_input = w_input.astype(jnp.bfloat16)
    row_tags = jnp.where(mask > 0, labels, -1)
    grad_input = jnp.zeros(w_input.shape, jnp.float32)
    grad_hidden = jnp.zeros((w_hidden.shape[0] * nblk, hcol), jnp.float32)
    grad_output = jnp.zeros((w_output.shape[0] * nblk, scol), jnp.float32)
    grad_bias = jnp.zeros(bias_row.shape, jnp.float32)
    loss_local = jnp.zeros((), jnp.float32)
    for micro_step in range(micro):
        low_hidden, low_output = (
            lax.all_gather(w_hidden.astype(jnp.bfloat16), "blk", axis=0, tiled=True),
            lax.all_gather(w_output.astype(jnp.bfloat16), "blk", axis=0, tiled=True),
        )
        inputs = lax.all_gather(frames[micro_step], "col", axis=0, tiled=True)
        tags_group = lax.all_gather(row_tags[micro_step], "col", axis=0, tiled=True)
        sig_one = jax.nn.sigmoid(matmul(inputs, low_input) + b_one)
        h_one = spread_cols(sig_one.astype(jnp.bfloat16))
        sig_two = jax.nn.sigmoid(matmul(h_one, low_hidden) + b_two)
        h_two = spread_cols(sig_two.astype(jnp.bfloat16))
        logits = matmul(h_two, low_output) + b_out
        row_top = lax.pmax(jnp.max(logits, axis=1), "col")
        exponent = jnp.exp(logits - row_top[:, None])
        target_hit = jnp.arange(scol)[None, :] == (tags_group - col_index * scol)[:, None]
        row_total, picked = lax.psum(
            (jnp.sum(exponent, axis=1), jnp.sum(jnp.where(target_hit, logits, 0.0), axis=1)), "col"
        )
        live_rows = tags_group >= 0
        loss_local = loss_local + jnp.sum(
            jnp.where(live_rows, row_top + jnp.log(row_total) - picked, 0.0)
        )
        probs = exponent / row_total[:, None]
        d_logits = (
            jnp.where(live_rows[:, None], probs - target_hit.astype(jnp.float32), 0.0) / slot_count
        ).astype(jnp.bfloat16)
        grad_output = grad_output + inner_rows(h_two, d_logits)
        d_h_two = reduce_cols(outer_cols(d_logits, low_output))
        d_z_two = (d_h_two * sig_two * (1.0 - sig_two)).astype(jnp.bfloat16)
        grad_hidden = grad_hidden + inner_rows(h_one, d_z_two)
        d_h_one = reduce_cols(outer_cols(d_z_two, low_hidden))
        d_z_one = (d_h_one * sig_one * (1.0 - sig_one)).astype(jnp.bfloat16)
        grad_input = grad_input + inner_rows(inputs, d_z_one)
        grad_bias = grad_bias + jnp.concatenate(
            [
                jnp.sum(d_z_one.astype(jnp.float32), axis=0),
                jnp.sum(d_z_two.astype(jnp.float32), axis=0),
                jnp.sum(d_logits.astype(jnp.float32), axis=0),
            ]
        )
    q_input, next_res_input = squash(grad_input, res_input[0])
    q_hidden, next_res_hidden = squash(grad_hidden, res_hidden[0])
    q_output, next_res_output = squash(grad_output, res_output[0])
    red_hidden, red_output = (
        lax.psum_scatter(q_hidden, "blk", scatter_dimension=0, tiled=True),
        lax.psum_scatter(q_output, "blk", scatter_dimension=0, tiled=True),
    )
    red_input, red_bias, loss_sum = lax.psum((q_input, grad_bias, loss_local), "blk")
    share_blk = 1.0 / nblk
    grad_square = (
        share_blk * (jnp.sum(red_input * red_input) + jnp.sum(red_bias * red_bias))
        + jnp.sum(red_hidden * red_hidden)
        + jnp.sum(red_output * red_output)
    )
    clip_norm = jnp.sqrt(lax.psum(grad_square, ("blk", "col")))
    factor = jnp.minimum(1.0, CLIP / clip_norm)
    next_mom_input = 0.5 * mom_input + factor * red_input
    next_mom_hidden = 0.5 * mom_hidden + factor * red_hidden
    square_input, square_hidden = lax.psum(
        (
            share_blk * jnp.sum(next_mom_input * next_mom_input),
            jnp.sum(next_mom_hidden * next_mom_hidden),
        ),
        ("blk", "col"),
    )
    iter_input = next_mom_input / (jnp.sqrt(square_input) + 1e-07)
    iter_hidden = next_mom_hidden / (jnp.sqrt(square_hidden) + 1e-07)
    for turn_index in range(NS):
        rows_hidden = collect_rows(iter_hidden)
        gram_input, gram_hidden = lax.psum(
            (precise(iter_input, iter_input.T), precise(iter_hidden, rows_hidden.T)), "col"
        )
        image_input = precise(gram_input, iter_input)
        image_hidden = precise(gram_hidden, rows_hidden)
        iter_input = (
            NS_A * iter_input + NS_B * image_input + NS_C * precise(gram_input, image_input)
        )
        iter_hidden = (
            NS_A * iter_hidden
            + NS_B * image_hidden
            + NS_C * precise(gram_hidden, collect_rows(image_hidden))
        )
    muon_scale = LR_MUON * 0.2 * math.sqrt(hcol * ncol)
    new_input = w_input * (1.0 - LR_MUON * WD_MUON) - muon_scale * iter_input
    new_hidden = w_hidden * (1.0 - LR_MUON * WD_MUON) - muon_scale * iter_hidden
    new_output, next_out_first, next_out_second = adam_step(
        w_output, factor * red_output, out_first, out_second
    )
    new_biases, next_bias_first, next_bias_second = adam_step(
        biases, factor * red_bias[None, :], bias_first, bias_second
    )
    return (
        loss_sum,
        clip_norm,
        new_input,
        new_hidden,
        new_output,
        new_biases,
        next_mom_input,
        next_mom_hidden,
        next_out_first,
        next_out_second,
        next_bias_first,
        next_bias_second,
        next_res_input[None],
        next_res_hidden[None],
        next_res_output[None],
    )


def fast_body(
    frames,
    labels,
    mask,
    w_input,
    w_hidden,
    w_output,
    biases,
    mom_input,
    mom_hidden,
    out_first,
    out_second,
    bias_first,
    bias_second,
    res_input,
    res_hidden,
    res_output,
):
    ncol = lax.axis_size("col")
    nblk = lax.axis_size("blk")
    col_index = lax.axis_index("col")
    blk_index = lax.axis_index("blk")
    hcol = w_input.shape[1]
    scol = w_output.shape[1]
    micro = frames.shape[0]
    slot_count = frames.shape[1] * micro * nblk * ncol
    bias_row = biases[0]
    deep = w_input.shape[0]
    padded = 512
    rows_out = OUT_GROUPS * OUT_ROWS
    own_tags = jnp.where(mask > 0, labels, -1).reshape(1, -1)
    layer_biases = jnp.pad(bias_row[: 2 * hcol].reshape(2, hcol), ((0, 6), (0, 0)))
    blocks = -(-rows_out // 128)
    out_biases = jnp.pad(bias_row[2 * hcol :], (0, blocks * 128 - scol)).reshape(blocks, 128)
    inputs, h_one, h_two, slope_one, slope_two, low_hidden, low_output, mom_far, d_logits, vec = (
        forward_pass(
            frames.reshape(-1, deep),
            jnp.broadcast_to(own_tags, (8, own_tags.shape[1])),
            w_input,
            w_hidden,
            w_output.T,
            layer_biases,
            out_biases,
            mom_input,
            slot_count,
        )
    )
    partial = inner_rows(d_logits, low_output)
    next_out, codes, sizes = squash_out(d_logits, h_two, res_output[0].T)
    next_hid, next_in, red_out, red_hid, red_in, red_far, vec_sum, stats = reduce_grads(
        codes,
        sizes,
        h_one,
        inputs,
        partial,
        slope_two,
        slope_one,
        low_hidden,
        res_hidden[0],
        jnp.pad(res_input[0], ((0, padded - deep), (0, 0))).T,
        vec,
        scol,
        deep,
    )
    next_res_output = next_out.transpose(1, 2, 0)
    next_res_hidden = next_hid
    next_res_input = next_in[:, :deep].T
    red_output = red_out[:scol].T
    vec_sum = vec_sum.reshape(-1)
    red_bias = vec_sum[: bias_row.shape[0]]
    loss_sum = vec_sum[bias_row.shape[0]]
    done_hidden, done_input, next_mom_hidden, next_mom_input, norms = muon(
        stats,
        red_hid,
        mom_hidden,
        red_in,
        mom_input,
        red_far,
        mom_far,
        hcol * ncol,
    )
    clip_norm = norms[0, 0]
    factor = norms[4, 0]
    muon_scale = LR_MUON * 0.2 * math.sqrt(hcol * ncol)
    new_input = w_input * (1.0 - LR_MUON * WD_MUON) - muon_scale * done_input
    new_hidden = w_hidden * (1.0 - LR_MUON * WD_MUON) - muon_scale * done_hidden
    new_output, next_out_first, next_out_second = adam_step(
        w_output, factor * red_output, out_first, out_second
    )
    new_biases, next_bias_first, next_bias_second = adam_step(
        biases, factor * red_bias[None, :], bias_first, bias_second
    )
    return (
        loss_sum,
        clip_norm,
        new_input,
        new_hidden,
        new_output,
        new_biases,
        next_mom_input,
        next_mom_hidden,
        next_out_first,
        next_out_second,
        next_bias_first,
        next_bias_second,
        next_res_input[None],
        next_res_hidden[None],
        next_res_output,
    )


def solution(mesh):
    in_specs = (
        P(None, ("blk", "col"), None),
        P(None, ("blk", "col")),
        P(None, ("blk", "col")),
        P(None, "col"),
        P("blk", "col"),
        P("blk", "col"),
        P("col", None),
        P(None, "col"),
        P("blk", "col"),
        P("blk", "col"),
        P("blk", "col"),
        P("col", None),
        P("col", None),
        P("blk", None, "col"),
        P("blk", None, "col"),
        P("blk", None, "col"),
    )
    out_specs = (
        P(),
        P(),
        P(None, "col"),
        P("blk", "col"),
        P("blk", "col"),
        P("col", None),
        P(None, "col"),
        P("blk", "col"),
        P("blk", "col"),
        P("blk", "col"),
        P("col", None),
        P("col", None),
        P("blk", None, "col"),
        P("blk", None, "col"),
        P("blk", None, "col"),
    )
    cubes = mesh.shape["blk"] == 8 and mesh.shape["col"] == 4
    body = fast_body if cubes else plain_body
    return jax.shard_map(body, mesh=mesh, in_specs=in_specs, out_specs=out_specs, check_vma=False)
```

```python
import functools
import math

import jax
import jax.numpy as jnp
from jax import lax
from jax.experimental import pallas as pl
from jax.experimental.pallas import tpu as pltpu
from jax.sharding import PartitionSpec as P

NS = 5
STEP = 5


NS_A = 3.4445
NS_B = -4.775
NS_C = 2.0315
CLIP = 0.002
LR_MUON = 0.1
WD_MUON = 0.01
LR_ADAM = 0.03
WD_ADAM = 0.1

MESH = pl.DeviceIdType.MESH
F32 = jnp.float32
BF16 = jnp.bfloat16
I16 = jnp.int16
LN2 = math.log(2.0)
TOP_CODE = 32700.0
LEVELS = 64.0


def matmul(left_side, right_side):
    return jnp.dot(left_side, right_side, preferred_element_type=jnp.float32)


def inner_rows(left_side, right_side):
    return lax.dot_general(
        left_side, right_side, (((0,), (0,)), ((), ())), preferred_element_type=jnp.float32
    )


def outer_cols(left_side, right_side):
    return lax.dot_general(
        left_side, right_side, (((1,), (1,)), ((), ())), preferred_element_type=jnp.float32
    )


def precise(left_side, right_side):
    return jnp.dot(
        left_side, right_side, precision=lax.Precision.HIGHEST, preferred_element_type=jnp.float32
    )


def spread_cols(values):
    return lax.all_gather(values, "col", axis=1, tiled=True)


def reduce_cols(values):
    return lax.psum_scatter(values, "col", scatter_dimension=1, tiled=True)


def collect_rows(values):
    return lax.all_gather(values, "blk", axis=0, tiled=True)


def squash(gradient, resid):
    value = gradient + resid.astype(jnp.float32)
    scale = jnp.mean(jnp.abs(value), axis=0, keepdims=True) + 1e-12
    signed = scale * jnp.tanh(2.0 * value / scale)
    return (signed, value - signed)


def adam_step(weight, gradient, first, second):
    first = 0.5 * first + 0.5 * gradient
    second = 0.95 * second + 0.05 * gradient * gradient
    update = first / (1.0 - 0.5**STEP) / (jnp.sqrt(second / (1.0 - 0.95**STEP)) + 1e-08)
    return (weight - LR_ADAM * (update + WD_ADAM * weight), first, second)


def halves(values):
    top = values.astype(BF16)
    return top, (values - top.astype(F32)).astype(BF16)


def dot_nn(left_side, right_side):
    return lax.dot_general(
        left_side, right_side, (((1,), (0,)), ((), ())), preferred_element_type=F32
    )


def dot_nt(left_side, right_side):
    return lax.dot_general(
        left_side, right_side, (((1,), (1,)), ((), ())), preferred_element_type=F32
    )


RING = 8
STEPS = RING - 1
OUT_ROWS = 592
OUT_GROUPS = 4
HID_ROWS = 512
HID_GROUP = 4
IN_GROUP = 5
TURN_AT = 4
CROSS_AT = 5
HID_AT = 11
FINISH_AT = 12
IN_AT = 18
HID_HOP = 3


def ring_place(blk):
    odd = blk % 2
    return (blk // 2) * (1 - odd) + (7 - blk // 2) * odd


def ring_blk(place):
    back = place // 4
    return 2 * place * (1 - back) + (15 - 2 * place) * back


def scale_code(size):
    return jnp.ceil(jnp.log(jnp.maximum(size, 1e-30)) * (LEVELS / LN2))


def code_scale(code):
    return jnp.exp(code * (LN2 / LEVELS))


def to_codes(values):
    return jnp.round(values).astype(jnp.int32).astype(I16)


def from_codes(codes):
    return codes.astype(jnp.int32).astype(F32)


def chunk_of(lane):
    number = lane // 256
    return number // 2 if number % 2 == 0 else 7 - number // 2


def squash_kernel(
    senones,
    dl_ref,
    h_ref,
    res_ref,
    w_ref,
    next_ref,
    codes_ref,
    size_ref,
    part_ref,
    grad,
    cols,
    marks,
    flipped,
    total_part,
    part_sem,
):
    group = pl.program_id(0)
    rows, wide = grad.shape
    valid = senones - group * rows
    for first, count in ((0, rows // 32 * 16), (rows // 32 * 16, rows - rows // 32 * 16)):
        there = slice(first, first + count)
        total = jnp.zeros((count, 128), F32)
        for lane in range(0, wide, 512):
            value = dot_nn(dl_ref[there, :], h_ref[:, lane : lane + 512])
            value = value + res_ref[there, lane : lane + 512].astype(F32)
            row = first + lax.broadcasted_iota(jnp.int32, value.shape, 0)
            value = jnp.where(row < valid, value, 0.0)
            grad[there, lane : lane + 512] = value
            value = jnp.abs(value)
            for part in range(0, 512, 128):
                total = total + value[:, part : part + 128]
        size = jnp.sum(total, axis=1, keepdims=True) * (1.0 / wide) + 1e-12
        size = jnp.broadcast_to(size, (count, 128))
        marks[there, :] = size
        cols[0, there, :] = size
        cols[1, there, :] = 2.0 / size

    frames = dl_ref.shape[1]
    for first in range(0, rows, 128):
        count = min(128, rows - first)
        for lane in range(0, frames, 128):
            tile = dl_ref[first : first + count, lane : lane + 128].astype(F32)
            if count < 128:
                tile = jnp.concatenate([tile, jnp.zeros((128 - count, 128), F32)], axis=0)
            flipped[lane : lane + 128, first : first + 128] = jnp.transpose(tile).astype(BF16)

    @pl.when(group == 0)
    def _():
        total_part[...] = jnp.zeros_like(total_part)

    def some(number):
        row = pl.multiple_of(number * 16, 16)
        size = cols[0, pl.ds(row, 16), :]
        steep = cols[1, pl.ds(row, 16), :]
        for lane in range(0, wide, 128):
            piece = grad[pl.ds(row, 16), lane : lane + 128]
            curve = jnp.tanh(piece * steep)
            codes_ref[0, 2 * chunk_of(lane) + lane // 128 % 2, pl.ds(row, 16), :] = to_codes(
                curve * TOP_CODE
            )
            next_ref[pl.ds(row, 16), 0, lane : lane + 128] = piece - size * curve

    parts = wide // 256
    each = rows // 16 // parts

    def beside(number, carry):
        lanes = pl.ds(pl.multiple_of(number * 256, 256), 256)
        total_part[:, lanes] += dot_nn(flipped[:, 0:rows], w_ref[:, lanes])
        for more in range(each):
            some(number * each + more)
        return carry

    lax.fori_loop(0, parts, beside, 0)
    for number in range(parts * each, rows // 16):
        some(number)
    copy = pltpu.make_async_copy(total_part, part_ref, part_sem.at[0])

    @pl.when(group == OUT_GROUPS - 1)
    def _():
        copy.start()

    marks[rows:, :] = jnp.zeros((marks.shape[0] - rows, 128), F32)
    lines = [jnp.transpose(marks[first : first + 128, :])[0:1, :] for first in range(0, rows, 128)]
    lines.append(jnp.zeros((8 - len(lines), 128), F32))
    size_ref[0] = jnp.concatenate(lines, axis=0)

    @pl.when(group == OUT_GROUPS - 1)
    def _():
        copy.wait()


def squash_out(dl, h_two, res_out, w_out):
    senones, wide = res_out.shape
    frames = dl.shape[1]
    return pl.pallas_call(
        functools.partial(squash_kernel, senones),
        grid=(OUT_GROUPS,),
        out_shape=(
            jax.ShapeDtypeStruct((senones, 1, wide), F32),
            jax.ShapeDtypeStruct((OUT_GROUPS, 2 * RING, OUT_ROWS, 128), I16),
            jax.ShapeDtypeStruct((OUT_GROUPS, 8, 128), F32),
            jax.ShapeDtypeStruct((frames, wide), F32),
        ),
        in_specs=[
            pl.BlockSpec((OUT_ROWS, frames), lambda group: (group, 0)),
            pl.BlockSpec((frames, wide), lambda group: (0, 0)),
            pl.BlockSpec((OUT_ROWS, wide), lambda group: (group, 0)),
            pl.BlockSpec((OUT_ROWS, wide), lambda group: (group, 0)),
        ],
        out_specs=(
            pl.BlockSpec((OUT_ROWS, 1, wide), lambda group: (group, 0, 0)),
            pl.BlockSpec((1, 2 * RING, OUT_ROWS, 128), lambda group: (group, 0, 0, 0)),
            pl.BlockSpec((1, 8, 128), lambda group: (group, 0, 0)),
            pl.BlockSpec(memory_space=pl.ANY),
        ),
        scratch_shapes=[
            pltpu.VMEM((OUT_ROWS, wide), F32),
            pltpu.VMEM((2, OUT_ROWS, 128), F32),
            pltpu.VMEM((640, 128), F32),
            pltpu.VMEM((frames, 640), BF16),
            pltpu.VMEM((frames, wide), F32),
            pltpu.SemaphoreType.DMA((1,)),
        ],
        compiler_params=pltpu.CompilerParams(vmem_limit_bytes=60 * 1024 * 1024),
    )(dl, h_two, res_out, w_out)


def reduce_kernel(
    deep,
    senones,
    codes_ref,
    sizes_ref,
    h_one_ref,
    x_ref,
    part_ref,
    slope_two_ref,
    slope_one_ref,
    w_hid_ref,
    res_hid_ref,
    res_in_ref,
    vec_ref,
    next_hid_ref,
    next_in_ref,
    red_out_ref,
    red_hid_ref,
    red_in_ref,
    red_far_ref,
    vec_sum_ref,
    stats_ref,
    grad,
    turned,
    res_buf,
    h_buf,
    slope_buf,
    marks,
    cols,
    keep_sums,
    dz,
    dz_two,
    dz_one,
    core_out,
    core_got,
    far_out,
    far_got,
    own_out,
    got_out,
    own_hid,
    got_hid,
    own_in,
    got_in,
    share_in,
    share_far,
    sizes,
    shares,
    vec,
    vecs,
    res_sems,
    load_sems,
    code_sems,
    slope_sems,
    core_send,
    core_recv,
    far_send,
    far_recv,
    out_send,
    out_recv,
    hid_send,
    hid_recv,
    in_send,
    in_recv,
    share_send,
    share_recv,
    vec_send,
    vec_recv,
    size_send,
    size_recv,
    share_far_send,
    share_far_recv,
):
    blk = lax.axis_index("blk")
    col = lax.axis_index("col")
    here = ring_place(blk)
    core, high = col % 2, col // 2
    cores = {"col": col + 1 - 2 * core}
    across = {"col": (col + 2) % 4}
    barrier = pltpu.get_barrier_semaphore()
    for target in (cores, across, *({"blk": (blk + away) % RING} for away in range(1, RING))):
        pl.semaphore_signal(barrier, inc=1, device_id=target, device_id_type=MESH)

    def code_copy(group):
        return pltpu.make_async_copy(codes_ref.at[group], own_out.at[group], code_sems.at[group])

    def hid_res_copy(part):
        return pltpu.make_async_copy(
            res_hid_ref.at[:, pl.ds(part * 256, 256)],
            res_buf.at[part],
            res_sems.at[part],
        )

    def hid_next_copy(part):
        return pltpu.make_async_copy(
            turned, next_hid_ref.at[:, pl.ds(part * 256, 256)], load_sems.at[1]
        )

    def load(src, dst):
        return pltpu.make_async_copy(src, dst, load_sems.at[0])

    for group in range(OUT_GROUPS):
        code_copy(group).start()
    for part in range(2):
        hid_res_copy(part).start()
    load(h_one_ref, h_buf).start()
    marks[...] = jnp.zeros_like(marks)
    stats_ref[...] = jnp.zeros_like(stats_ref)
    vec[...] = vec_ref[...]
    pl.semaphore_wait(barrier, RING + 1)

    CHUNK = 256
    units = slope_buf.shape[2]

    def slope_copy(layer, block):
        rows = pl.ds(pl.multiple_of(block * CHUNK, CHUNK), CHUNK)
        src = (slope_two_ref, slope_one_ref)[layer]
        return pltpu.make_async_copy(src.at[rows, :], slope_buf.at[block % 2], slope_sems.at[block % 2])

    def core_move(layer, block):
        return pltpu.make_async_remote_copy(
            src_ref=core_out.at[block % 2],
            dst_ref=core_got.at[layer, block],
            send_sem=core_send.at[block % 2],
            recv_sem=core_recv.at[layer, block],
            device_id=cores,
            device_id_type=MESH,
        )

    def far_move(layer, block):
        return pltpu.make_async_remote_copy(
            src_ref=far_out.at[block % 2],
            dst_ref=far_got.at[layer, block],
            send_sem=far_send.at[block % 2],
            recv_sem=far_recv.at[layer, block],
            device_id=across,
            device_id_type=MESH,
        )

    def lanes_of(number):
        return pl.ds(pl.multiple_of(number * units, units), units)

    def rows_at(number):
        return pl.ds(pl.multiple_of(number * 16, 16), 16)

    def free(copy, layer, block):
        @pl.when((layer > 0) | (block >= 2))
        def _():
            copy.wait_send()

    def lane_codes(first):
        return jnp.transpose(marks[first : first + 128, :])[0:1, :]

    def set_factors():
        top = jnp.max(cols[0, 0:CHUNK, :], axis=1, keepdims=True)
        code = scale_code(top)
        marks[0:CHUNK, :] = jnp.broadcast_to(code, (CHUNK, 128))
        cols[1, 0:CHUNK, :] = jnp.broadcast_to(TOP_CODE / code_scale(code), (CHUNK, 128))

    def largest(values):
        return functools.reduce(
            jnp.maximum,
            [
                jnp.abs(value[:, lane : lane + 128])
                for value in values
                for lane in range(0, value.shape[1], 128)
            ],
        )

    def scaled(values, factor):
        return jnp.concatenate(
            [values[:, lane : lane + 128] * factor for lane in range(0, values.shape[1], 128)], axis=1
        )

    def put_scale(out):
        codes = jnp.concatenate(
            [lane_codes(0), lane_codes(128), jnp.zeros((14, 128), F32)], axis=0
        )
        out[CHUNK : CHUNK + 16, 0:128] = codes.astype(jnp.int32).astype(I16)

    def read_scale(got):
        step = code_scale(from_codes(got[CHUNK : CHUNK + 16, 0:128])) * (1.0 / TOP_CODE)
        step = jnp.transpose(jnp.concatenate([step, jnp.zeros((112, 128), F32)], axis=0))
        for up in range(2):
            marks[CHUNK + up * 128 : CHUNK + (up + 1) * 128, :] = jnp.broadcast_to(
                step[:, up : up + 1], (128, 128)
            )

    def step_at(number):
        return marks[pl.ds(pl.multiple_of(CHUNK + number * 16, 16), 16), :]

    def split(layer, block):
        free(core_move(layer, block), layer, block)

        def measure(number, carry):
            rows = rows_at(number)
            cols[0, rows, :] = largest(
                [grad[rows, lanes_of(2 * half + 1 - core)] for half in range(2)]
            )
            return carry

        lax.fori_loop(0, CHUNK // 16, measure, 0)
        set_factors()

        def write(number, carry):
            rows = rows_at(number)
            factor = cols[1, rows, :]
            for half in range(2):
                there = slice(half * units, (half + 1) * units)
                core_out[block % 2, rows, there] = to_codes(
                    scaled(grad[rows, lanes_of(2 * half + 1 - core)], factor)
                )
                keep_sums[block, rows, there] = grad[rows, lanes_of(2 * half + core)]
            return carry

        lax.fori_loop(0, CHUNK // 16, write, 0)
        put_scale(core_out.at[block % 2])
        core_move(layer, block).start()

    def cross(layer, block):
        core_move(layer, block).wait_recv()
        free(far_move(layer, block), layer, block)
        got = core_got.at[layer, block]
        read_scale(got)

        def add(number, carry):
            rows = rows_at(number)
            near, away = lanes_of(high), lanes_of(1 - high)
            step = step_at(number)
            keep_sums[block, rows, near] += scaled(from_codes(got[rows, near]), step)
            value = keep_sums[block, rows, away] + scaled(from_codes(got[rows, away]), step)
            keep_sums[block, rows, away] = value
            cols[0, rows, :] = largest([value])
            return carry

        lax.fori_loop(0, CHUNK // 16, add, 0)
        set_factors()

        def write(number, carry):
            rows = rows_at(number)
            far_out[block % 2, rows, :] = to_codes(
                scaled(keep_sums[block, rows, lanes_of(1 - high)], cols[1, rows, :])
            )
            return carry

        lax.fori_loop(0, CHUNK // 16, write, 0)
        put_scale(far_out.at[block % 2])
        far_move(layer, block).start()

    def finish(layer, block):
        far_move(layer, block).wait_recv()
        slope_copy(layer, block).wait()
        got = far_got.at[layer, block]
        read_scale(got)

        def one(number, total):
            rows = rows_at(number)
            value = keep_sums[block, rows, lanes_of(high)] + scaled(
                from_codes(got[rows, :]), step_at(number)
            )
            value = (value * slope_buf[block % 2, rows, :]).astype(BF16)
            dz[rows, :] = value
            return total + value.astype(F32)

        total = lax.fori_loop(0, CHUNK // 16, one, jnp.zeros((16, units), F32))
        if layer == 0:

            @pl.when(block < 2)
            def _():
                slope_copy(0, block + 2).start()

            @pl.when(block >= 2)
            def _():
                slope_copy(1, block - 2).start()

        else:

            @pl.when(block < 2)
            def _():
                slope_copy(1, block + 2).start()

        total = jnp.sum(total, axis=0, keepdims=True)
        for number in range(units // 128):
            row = 4 * (1 - layer) + number
            vec[row : row + 1, :] += total[:, number * 128 : (number + 1) * 128]
        flipped = (dz_two, dz_one)[layer]
        for up in range(CHUNK // 128):
            there = pl.ds(pl.multiple_of(block * CHUNK + up * 128, 128), 128)
            for number in range(units // 128):
                tile = dz[up * 128 : (up + 1) * 128, number * 128 : (number + 1) * 128]
                flipped[number * 128 : (number + 1) * 128, there] = jnp.transpose(
                    tile.astype(F32)
                ).astype(BF16)

    def blocks(first, last, work):
        def one(block, carry):
            work(block)
            return carry

        lax.fori_loop(first, last, one, 0)

    def start_block(block):
        rows = pl.ds(pl.multiple_of(block * CHUNK, CHUNK), CHUNK)
        copy = pltpu.make_async_copy(part_ref.at[rows, :], grad.at[pl.ds(0, CHUNK), :], load_sems.at[1])
        copy.start()
        copy.wait()
        split(0, block)

    def turn_block(block):
        finish(0, block)
        for lane in range(0, grad.shape[1], 512):
            grad[0:CHUNK, lane : lane + 512] = dot_nt(dz[...], w_hid_ref[lane : lane + 512, :])
        split(1, block)

    core_out[:, CHUNK:, :] = jnp.zeros((2, 16, 2 * units), I16)
    far_out[:, CHUNK:, :] = jnp.zeros((2, 16, units), I16)
    slope_copy(0, 0).start()
    slope_copy(0, 1).start()
    def vec_copy(away):
        return pltpu.make_async_remote_copy(
            src_ref=vec,
            dst_ref=vecs.at[blk],
            send_sem=vec_send.at[away - 1],
            recv_sem=vec_recv.at[away - 1],
            device_id={"blk": (blk + away) % RING},
            device_id_type=MESH,
        )

    def set_rows(count, first_own, size):
        size = jnp.broadcast_to(size, (count, 128))
        marks[first_own : first_own + count, :] = size
        cols[0, 0:count, :] = size
        cols[1, 0:count, :] = 2.0 / size

    def tell_sizes(group):
        for away in range(1, RING):
            size_copy(group, away).start()

    def size_copy(group, away):
        return pltpu.make_async_remote_copy(
            src_ref=sizes.at[group, here],
            dst_ref=sizes.at[group, here],
            send_sem=size_send.at[group, away - 1],
            recv_sem=size_recv.at[group, away - 1],
            device_id={"blk": ring_blk((here + away) % RING)},
            device_id_type=MESH,
        )

    def set_sizes(rows, group):
        parts = [lane_codes(first) for first in range(0, rows, 128)]
        parts.append(jnp.zeros((8 - len(parts), 128), F32))
        sizes[group, here] = jnp.concatenate(parts, axis=0)
        tell_sizes(group)

    def make_shares(group, row_of):
        for away in range(1, RING):
            size_copy(group, away).wait_recv()
        for way in range(2):
            tiles = []
            for step in range(STEPS):
                mine = row_of(here, step, way)
                came = mine * 0.0
                for back in range(step + 1):
                    came = came + row_of((here - 1 - back + (2 + 2 * back) * way + RING) % RING, step, way)
                if step < STEPS - 1:
                    whole = 1.0 / jnp.maximum(came + mine, 1e-30)
                else:
                    whole = 1.0 / TOP_CODE
                tiles += [came * whole, mine * whole]
            tiles.append(jnp.zeros((16, 128), F32))
            shares[group, way] = jnp.transpose(jnp.concatenate(tiles, axis=0))

    def hid_group():
        load(h_one_ref, h_buf).wait()
        wide = grad.shape[1]
        for part in range(2):
            first = part * 256
            hid_res_copy(part).wait()
            total = jnp.zeros((256, 128), F32)
            for lane in range(0, wide, 512):
                value = dot_nn(dz_two[first : first + 256, :], h_buf[:, lane : lane + 512])
                value = value + jnp.transpose(res_buf[part, lane : lane + 512, :].astype(F32))
                grad[:, lane : lane + 512] = value
                value = jnp.abs(value)
                for more in range(0, 512, 128):
                    total = total + value[:, more : more + 128]
            set_rows(
                256, first, jnp.sum(total, axis=1, keepdims=True) * (1.0 / wide) + 1e-12
            )

            def some(number, carry, first=first):
                row = pl.multiple_of(number * 16, 16)
                size = cols[0, pl.ds(row, 16), :]
                steep = cols[1, pl.ds(row, 16), :]
                for lane in range(0, wide, 128):
                    piece = grad[pl.ds(row, 16), lane : lane + 128]
                    curve = jnp.tanh(piece * steep)
                    own_hid[2 * chunk_of(lane) + lane // 128 % 2, pl.ds(first + row, 16), :] = (
                        to_codes(curve * TOP_CODE)
                    )
                    grad[pl.ds(row, 16), lane : lane + 128] = piece - size * curve
                return carry

            lax.fori_loop(0, 16, some, 0)
            if part:
                hid_next_copy(part - 1).wait()
            for lane in range(0, wide, 128):
                turned[lane : lane + 128, :] = jnp.transpose(grad[:, lane : lane + 128])
            hid_next_copy(part).start()
        load(x_ref, h_buf.at[:, pl.ds(0, x_ref.shape[1])]).start()
        set_sizes(HID_ROWS, HID_GROUP)
        hid_next_copy(1).wait()

    def in_group():
        wide = x_ref.shape[1]
        load(x_ref, h_buf.at[:, pl.ds(0, wide)]).wait()
        for first in range(0, HID_ROWS, 256):
            grad[0:256, 0:wide] = dot_nn(dz_one[first : first + 256, :], h_buf[:, 0:wide])

            def add(number, carry, first=first):
                row = pl.multiple_of(number * 16, 16)
                place = pl.multiple_of(first + row, 16)
                value = grad[pl.ds(row, 16), 0:wide] + res_in_ref[pl.ds(place, 16), :].astype(F32)
                grad[pl.ds(row, 16), 0:wide] = value
                value = jnp.abs(value)
                cols[0, pl.ds(row, 16), :] = functools.reduce(
                    jnp.add, [value[:, lane : lane + 128] for lane in range(0, wide, 128)]
                )
                return carry

            lax.fori_loop(0, 16, add, 0)
            set_rows(
                256,
                first,
                jnp.sum(cols[0, 0:256, :], axis=1, keepdims=True) * (1.0 / deep) + 1e-12,
            )

            def some(number, carry, first=first):
                row = pl.multiple_of(number * 16, 16)
                place = pl.multiple_of(first + row, 16)
                size = cols[0, pl.ds(row, 16), :]
                steep = cols[1, pl.ds(row, 16), :]
                chunk = first // 64 + number // 4
                inside = pl.multiple_of(number % 4 * 16, 16)
                for lane in range(0, wide, 128):
                    piece = grad[pl.ds(row, 16), lane : lane + 128]
                    curve = jnp.tanh(piece * steep)
                    next_in_ref[pl.ds(place, 16), lane : lane + 128] = piece - size * curve
                    own_in[
                        2 * chunk + lane // 256, pl.ds(inside, 16), lane % 256 : lane % 256 + 128
                    ] = to_codes(curve * TOP_CODE)
                return carry

            lax.fori_loop(0, 16, some, 0)
        sizes[IN_GROUP, here] = jnp.concatenate(
            [lane_codes(64 * chunk) for chunk in range(RING)], axis=0
        )
        tell_sizes(IN_GROUP)

    def towards(way):
        return {"blk": ring_blk((here + 1 - 2 * way + RING) % RING)}

    def move(src, got, step, way, send_sem, recv_sem):
        return pltpu.make_async_remote_copy(
            src_ref=src,
            dst_ref=got.at[way, step],
            send_sem=send_sem.at[way, step],
            recv_sem=recv_sem.at[way, step],
            device_id=towards(way),
            device_id_type=MESH,
        )

    def first_moves(own, got, send_sem, recv_sem):
        for way in range(2):
            chunk = (here - 1 + 2 * way + RING) % RING
            move(own.at[2 * chunk + way], got, 0, way, send_sem, recv_sem).start()

    def hop(rows, own, got, group, step, send_sem, recv_sem, keep):
        for way in range(2):
            move(got.at[way, step], got, step, way, send_sem, recv_sem).wait_recv()

        def add(way, result):
            message = got.at[way, step]
            ahead = here - 2 - step + way * (4 + 2 * step) + 2 * RING
            mine = own.at[2 * (ahead % RING) + way]
            share = pltpu.roll(shares[group, way], (128 - 16 * step) % 128, 1)
            for number, first in enumerate(range(0, rows, 128)):
                count = min(128, rows - first)
                there = slice(first, first + count)
                result(
                    first,
                    count,
                    from_codes(message[there, :]) * share[0:count, number : number + 1]
                    + from_codes(mine[there, :]) * share[0:count, 8 + number : 9 + number],
                )

        @pl.when(step < STEPS - 1)
        def _():
            for way in range(2):

                def write(first, count, value, way=way):
                    got[way, step, first : first + count, :] = to_codes(value)

                add(way, write)
            for way in range(2):
                move(got.at[way, step], got, step + 1, way, send_sem, recv_sem).start()

        @pl.when(step == STEPS - 1)
        def _():
            for way in range(2):

                def finish_rows(first, count, value, way=way):
                    keep(way, first, count, value)
                    square = jnp.sum(value * value, axis=0, keepdims=True)
                    for lane in range(0, value.shape[1], 128):
                        stats_ref[0:1, :] += square[:, lane : lane + 128]

                add(way, finish_rows)

    def out_hop(group, step):
        def keep(way, first, count, value):
            row = pl.multiple_of(group * OUT_ROWS + first, 16)
            red_out_ref[pl.ds(row, count), way * 128 : (way + 1) * 128] = value

        hop(
            OUT_ROWS,
            own_out.at[group],
            got_out.at[group],
            group,
            step,
            out_send.at[group],
            out_recv.at[group],
            keep,
        )

    def hid_hop(step):
        def keep(way, first, count, value):
            red_hid_ref[first : first + count, way * 128 : (way + 1) * 128] = value

        hop(HID_ROWS, own_hid, got_hid, HID_GROUP, step, hid_send, hid_recv, keep)

    def share_move(step, way):
        place = (here - step + 2 * step * way + 2 * RING) % RING
        return pltpu.make_async_remote_copy(
            src_ref=share_in.at[way, place],
            dst_ref=share_in.at[way, place],
            send_sem=share_send.at[way, step],
            recv_sem=share_recv.at[way, step],
            device_id=towards(way),
            device_id_type=MESH,
        )

    def share_across(way, place):
        return pltpu.make_async_remote_copy(
            src_ref=share_in.at[way, place],
            dst_ref=share_far.at[way, place],
            send_sem=share_far_send.at[way, place],
            recv_sem=share_far_recv.at[way, place],
            device_id=across,
            device_id_type=MESH,
        )

    def in_hop(step):
        def keep(way, first, count, value):
            share_in[way, here] = value

        hop(64, own_in, got_in, IN_GROUP, step, in_send, in_recv, keep)

        @pl.when(step == STEPS - 1)
        def _():
            for way in range(2):
                share_move(0, way).start()
                share_across(way, here).start()

    def share_hop(step):
        for way in range(2):
            share_move(step, way).wait_recv()
            share_across(way, (here - 1 - step + (2 + 2 * step) * way + RING) % RING).start()

        @pl.when(step < STEPS - 1)
        def _():
            for way in range(2):
                share_move(step + 1, way).start()

    def in_step(index):
        @pl.when((index >= 0) & (index < STEPS))
        def _():
            in_hop(index)

        @pl.when((index >= STEPS) & (index < 2 * STEPS))
        def _():
            share_hop(index - STEPS)

    def chunk_row(place, step, way):
        chunk = (here - 2 - step + way * (4 + 2 * step) + 2 * RING) % RING
        line = sizes[IN_GROUP, place, pl.ds(chunk, 1), :]
        return jnp.broadcast_to(line, (8, 128))

    for group in range(OUT_GROUPS):
        sizes[group, here] = sizes_ref[group]
        tell_sizes(group)
        code_copy(group).wait()
        first_moves(own_out.at[group], got_out.at[group], out_send.at[group], out_recv.at[group])
    blocks(0, 4, start_block)

    def each(number, first, spacing, count, work):
        after = number - first

        @pl.when((after >= 0) & (after < spacing * count) & (after % spacing == 0))
        def _():
            work(after // spacing)

    def turn(number, carry):
        @pl.when(number < OUT_GROUPS)
        def _():
            make_shares(number, lambda place, step, way: sizes[number, place])

        @pl.when(number < OUT_GROUPS * STEPS)
        def _():
            out_hop(number % OUT_GROUPS, number // OUT_GROUPS)

        @pl.when(number == HID_AT + HID_HOP)
        def _():
            make_shares(HID_GROUP, lambda place, step, way: sizes[HID_GROUP, place])

        each(number, HID_AT + HID_HOP, HID_HOP, STEPS, hid_hop)

        @pl.when(number == IN_AT + 1)
        def _():
            make_shares(IN_GROUP, chunk_row)

        in_step(number - IN_AT - 1)
        each(number, 0, 1, 4, lambda block: cross(0, block))
        each(number, TURN_AT, 2, 4, turn_block)
        each(number, CROSS_AT, 2, 4, lambda block: cross(1, block))

        @pl.when(number == HID_AT)
        def _():
            hid_group()
            first_moves(own_hid, got_hid, hid_send, hid_recv)

        each(number, FINISH_AT, 2, 4, lambda block: finish(1, block))

        @pl.when(number == IN_AT)
        def _():
            in_group()
            first_moves(own_in, got_in, in_send, in_recv)
            for away in range(1, RING):
                vec_copy(away).start()

        return carry

    turns = max(IN_AT + 1 + 2 * STEPS, HID_AT + HID_HOP * STEPS + 1, OUT_GROUPS * STEPS)
    lax.fori_loop(0, turns, turn, 0)

    def unfold(shares_of, out):
        for place in range(0, RING, 2):
            for way in range(2):
                for lane in range(0, 256, 128):
                    tile = jnp.concatenate(
                        [shares_of[way, place + more, :, lane : lane + 128] for more in range(2)],
                        axis=0,
                    )
                    first = way * 256 + lane
                    out[first : first + 128, place * 64 : place * 64 + 128] = jnp.transpose(tile)

    unfold(share_in, red_in_ref)
    for place in range(RING):
        for way in range(2):
            share_across(way, place).wait_recv()
    unfold(share_far, red_far_ref)
    for away in range(1, RING):
        vec_copy(away).wait_recv()
    vecs[blk] = vec[...]
    total = vecs[0]
    for number in range(1, RING):
        total = total + vecs[number]
    vec_sum_ref[...] = total
    flat = 128 * lax.broadcasted_iota(jnp.int32, total.shape, 0) + lax.broadcasted_iota(
        jnp.int32, total.shape, 1
    )
    total = jnp.where(flat < 2 * units + senones, total, 0.0)
    stats_ref[1:2, :] = jnp.sum(total * total, axis=0, keepdims=True) * (1.0 / RING)
    for away in range(1, RING):
        vec_copy(away).wait_send()
        for group in range(OUT_GROUPS + 2):
            size_copy(group, away).wait_send()
    for slot in range(2):
        core_move(1, 2 + slot).wait_send()
        far_move(1, 2 + slot).wait_send()
    for way in range(2):
        for step in range(STEPS):
            for group in range(OUT_GROUPS):
                move(
                    got_out.at[group, way, step],
                    got_out.at[group],
                    step,
                    way,
                    out_send.at[group],
                    out_recv.at[group],
                ).wait_send()
            move(got_hid.at[way, step], got_hid, step, way, hid_send, hid_recv).wait_send()
            move(got_in.at[way, step], got_in, step, way, in_send, in_recv).wait_send()
            share_move(step, way).wait_send()
        for place in range(RING):
            share_across(way, place).wait_send()


def reduce_grads(
    codes, sizes, h_one, x, part, slope_two, slope_one, w_hid, res_hid, res_in, vec, senones, deep
):
    frames, wide = h_one.shape
    in_wide = x.shape[1]
    units = w_hid.shape[1]
    vmem = pl.BlockSpec(memory_space=pltpu.VMEM)
    hbm = pl.BlockSpec(memory_space=pl.ANY)
    message = OUT_ROWS
    hid_message = HID_ROWS
    in_message = 64
    sem = pltpu.SemaphoreType.DMA
    return pl.pallas_call(
        functools.partial(reduce_kernel, deep, senones),
        out_shape=(
            jax.ShapeDtypeStruct((wide, HID_ROWS), F32),
            jax.ShapeDtypeStruct((HID_ROWS, in_wide), F32),
            jax.ShapeDtypeStruct((OUT_GROUPS * OUT_ROWS, 256), F32),
            jax.ShapeDtypeStruct((HID_ROWS, 256), F32),
            jax.ShapeDtypeStruct((in_wide, HID_ROWS), F32),
            jax.ShapeDtypeStruct((in_wide, HID_ROWS), F32),
            jax.ShapeDtypeStruct(vec.shape, F32),
            jax.ShapeDtypeStruct((8, 128), F32),
        ),
        in_specs=[hbm, vmem] + [hbm] * 5 + [vmem, hbm, vmem, vmem],
        out_specs=(hbm,) + (vmem,) * 7,
        scratch_shapes=[
            pltpu.VMEM((256, wide), F32),
            pltpu.VMEM((wide, 256), F32),
            pltpu.VMEM((2, wide, 256), BF16),
            pltpu.VMEM((frames, wide), BF16),
            pltpu.VMEM((2, 256, units), F32),
            pltpu.VMEM((640, 128), F32),
            pltpu.VMEM((2, 256, 128), F32),
            pltpu.VMEM((4, 256, 2 * units), F32),
            pltpu.VMEM((256, units), BF16),
            pltpu.VMEM((units, frames), BF16),
            pltpu.VMEM((units, frames), BF16),
            pltpu.VMEM((2, 272, 2 * units), I16),
            pltpu.VMEM((2, 4, 272, 2 * units), I16),
            pltpu.VMEM((2, 272, units), I16),
            pltpu.VMEM((2, 4, 272, units), I16),
            pltpu.VMEM((OUT_GROUPS, 2 * RING, message, 128), I16),
            pltpu.VMEM((OUT_GROUPS, 2, STEPS, message, 128), I16),
            pltpu.VMEM((2 * RING, hid_message, 128), I16),
            pltpu.VMEM((2, STEPS, hid_message, 128), I16),
            pltpu.VMEM((2 * RING, in_message, 256), I16),
            pltpu.VMEM((2, STEPS, in_message, 256), I16),
            pltpu.VMEM((2, RING, 64, 256), F32),
            pltpu.VMEM((2, RING, 64, 256), F32),
            pltpu.VMEM((OUT_GROUPS + 2, RING, 8, 128), F32),
            pltpu.VMEM((OUT_GROUPS + 2, 2, 128, 128), F32),
            pltpu.VMEM(vec.shape, F32),
            pltpu.VMEM((RING,) + vec.shape, F32),
            sem((2,)),
            sem((2,)),
            sem((OUT_GROUPS,)),
            sem((2,)),
            sem((2,)),
            sem((2, 4)),
            sem((2,)),
            sem((2, 4)),
            sem((OUT_GROUPS, 2, STEPS)),
            sem((OUT_GROUPS, 2, STEPS)),
            sem((2, STEPS)),
            sem((2, STEPS)),
            sem((2, STEPS)),
            sem((2, STEPS)),
            sem((2, STEPS)),
            sem((2, STEPS)),
            sem((STEPS,)),
            sem((STEPS,)),
            sem((OUT_GROUPS + 2, STEPS)),
            sem((OUT_GROUPS + 2, STEPS)),
            sem((2, RING)),
            sem((2, RING)),
        ],
        compiler_params=pltpu.CompilerParams(
            collective_id=1, has_side_effects=True, vmem_limit_bytes=63 * 1024 * 1024
        ),
    )(codes, sizes, h_one, x, part, slope_two, slope_one, w_hid, res_hid, res_in, vec)


RING_STARTS = (0, 0, 5, 6, 7)
LAYER_TWO_WAVE = 7
LOGIT_WAVES = (11, 12, 13, 14)


def forward_kernel(
    slot_count,
    x_ref,
    tags_ref,
    w_in_ref,
    w_hid_ref,
    w_out_ref,
    bias_ref,
    bias_out_ref,
    mom_ref,
    x_out,
    h_one_out,
    h_two_out,
    slope_one_out,
    slope_two_out,
    w_hid_out,
    w_out_out,
    mom_far_ref,
    dl_ref,
    vec_ref,
    x_all,
    h_one,
    h_two,
    slope_one,
    slope_two,
    w_in,
    w_hid,
    w_out,
    curve,
    bias_col,
    tags,
    sums,
    ring_send,
    ring_recv,
    x_send,
    x_recv,
    h_send,
    h_recv,
    tag_send,
    tag_recv,
    sum_send,
    sum_recv,
    out_sems,
    mom_sems,
):
    blk = lax.axis_index("blk")
    col = lax.axis_index("col")
    here = ring_place(blk)
    senones, depth = w_out_ref.shape
    own_rows, deep = x_ref.shape
    units = w_hid_ref.shape[1]
    frames = x_all.shape[0]
    cores = {"col": col + 1 - 2 * (col % 2)}
    across = {"col": (col + 2) % 4}
    corner = {"col": (col + 2) % 4 + 1 - 2 * (col % 2)}
    others = (cores, across, corner)

    barrier = pltpu.get_barrier_semaphore()
    for target in others + tuple({"blk": ring_blk((here + way) % RING)} for way in (1, 7)):
        pl.semaphore_signal(barrier, inc=1, device_id=target, device_id_type=MESH)

    w_hid[pl.ds(pl.multiple_of(blk * depth, depth), depth), :] = w_hid_ref[...].astype(BF16)
    own_lanes = pl.ds(pl.multiple_of(blk * depth, depth), depth)
    w_out[senones // 16 * 16 :, own_lanes] = jnp.zeros(
        (w_out.shape[0] - senones // 16 * 16, depth), BF16
    )
    w_out[0:senones, own_lanes] = w_out_ref[...].astype(BF16)
    own_frames = pl.ds(pl.multiple_of(col * own_rows, own_rows), own_rows)
    x_all[own_frames, :] = jnp.zeros((own_rows, x_all.shape[1]), BF16)
    x_all[own_frames, 0:deep] = x_ref[...]
    tags[col] = tags_ref[...]
    sums[...] = jnp.zeros_like(sums)
    pl.semaphore_wait(barrier, 5)

    def ring_part(group, origin, way):
        start = pl.multiple_of(origin * depth + way * 128, 128)
        if group == 0:
            return w_hid.at[pl.ds(start, 128), :]
        return w_out.at[pl.ds((group - 1) * OUT_ROWS, OUT_ROWS), pl.ds(start, 128)]

    def ring_move(group, step, way):
        origin = ring_blk((here - step + 2 * step * way + RING) % RING)
        part = ring_part(group, origin, way)
        return pltpu.make_async_remote_copy(
            src_ref=part,
            dst_ref=part,
            send_sem=ring_send.at[group, way, step],
            recv_sem=ring_recv.at[group, way, step],
            device_id={"blk": ring_blk((here + 1 - 2 * way + RING) % RING)},
            device_id_type=MESH,
        )

    def ring_wave(wave):
        for group, start in enumerate(RING_STARTS):
            step = wave - 1 - start
            for way in range(2):
                if step == -1:
                    ring_move(group, 0, way).start()
                if 0 <= step < STEPS:
                    ring_move(group, step, way).wait_recv()
                    if step < STEPS - 1:
                        ring_move(group, step + 1, way).start()

    def copy_to(target, src, send_sem, recv_sem):
        return pltpu.make_async_remote_copy(
            src_ref=src,
            dst_ref=src,
            send_sem=send_sem,
            recv_sem=recv_sem,
            device_id=target,
            device_id_type=MESH,
        )

    def rows_of(owner):
        return pl.ds(pl.multiple_of(owner * own_rows, own_rows), own_rows)

    def lanes_of(owner):
        return pl.ds(pl.multiple_of(owner * units, units), units)

    def x_move(number):
        owner = across["col"] if number == 2 else col
        target = across if number == 1 else cores
        return copy_to(target, x_all.at[rows_of(owner), :], x_send.at[number], x_recv.at[number])

    def h_move(layer, number, block):
        owner = across["col"] if number == 2 else col
        target = across if number == 1 else cores
        whole = (h_one, h_two)[layer]
        part = whole.at[pl.ds(block * own_rows, own_rows), lanes_of(owner)]
        return copy_to(
            target, part, h_send.at[layer, number, block], h_recv.at[layer, number, block]
        )

    def h_start(layer, block):
        h_move(layer, 0, block).start()
        h_move(layer, 1, block).start()

    def h_forward(layer, block):
        h_move(layer, 1, block).wait_recv()
        h_move(layer, 2, block).start()

    def h_ready(layer, block):
        h_move(layer, 0, block).wait_recv()
        h_move(layer, 2, block).wait_recv()

    ring_wave(0)
    x_move(0).start()
    x_move(1).start()
    tag_copies = [
        copy_to(target, tags.at[col], tag_send.at[number], tag_recv.at[number])
        for number, target in enumerate(others)
    ]
    for copy in tag_copies:
        copy.start()
    w_in[...] = jnp.zeros_like(w_in)
    w_in[0:deep, :] = w_in_ref[...].astype(BF16)
    for number in range(bias_out_ref.shape[0]):
        line = jnp.broadcast_to(bias_out_ref[number : number + 1, :], (128, 128))
        bias_col[number * 128 : (number + 1) * 128, :] = jnp.transpose(line)
    ring_wave(1)
    x_move(1).wait_recv()
    x_move(2).start()
    x_move(0).wait_recv()
    x_move(2).wait_recv()

    def layer(number, block, inputs, weights, whole, slopes):
        there = slice(block * own_rows, (block + 1) * own_rows)
        value = jax.nn.sigmoid(
            dot_nn(inputs[there, :], weights[...]) + bias_ref[number : number + 1, :]
        )
        slopes[there, :] = value * (1.0 - value)
        whole[there, lanes_of(col)] = value.astype(BF16)
        h_start(number, block)

    outs = []

    def put(src, dst):
        copy = pltpu.make_async_copy(src, dst, out_sems.at[len(outs)])
        copy.start()
        outs.append(copy)

    for block in range(4):
        layer(0, block, x_all, w_in, h_one, slope_one)
    put(x_all, x_out)
    put(slope_one, slope_one_out)

    def all_tags():
        return jnp.concatenate([tags[owner, 0:1, :] for owner in range(4)], axis=1)

    def own_row(line):
        line = line - col * senones
        return jnp.where(line < senones, line, -1)

    def logits(group):
        first = group * OUT_ROWS
        half = frames // 2
        for part in range(2):
            curve[first : first + OUT_ROWS, part * half : (part + 1) * half] = dot_nt(
                w_out[first : first + OUT_ROWS, :], h_two[part * half : (part + 1) * half, :]
            )
        base = lax.broadcasted_iota(jnp.int32, (16, frames), 0)

        def largest(number, top):
            row = pl.multiple_of(first + number * 16, 16)
            value = curve[pl.ds(row, 16), :] + bias_col[pl.ds(row, 16), 0:1]
            if group == OUT_GROUPS - 1:
                value = jnp.where(base + row < senones, value, -1e30)
            curve[pl.ds(row, 16), :] = value
            return jnp.maximum(top, value)

        top = lax.fori_loop(0, OUT_ROWS // 16, largest, jnp.full((16, frames), -1e30, F32))
        top = jnp.max(top, axis=0, keepdims=True)
        line = jnp.broadcast_to(own_row(all_tags()), (16, frames))

        def exponents(number, carry):
            total, picked = carry
            row = pl.multiple_of(first + number * 16, 16)
            value = curve[pl.ds(row, 16), :]
            power = jnp.exp(value - top)
            curve[pl.ds(row, 16), :] = power
            return total + power, picked + jnp.where(base + row == line, value, 0.0)

        blank = jnp.zeros((16, frames), F32)
        total, picked = lax.fori_loop(0, OUT_ROWS // 16, exponents, (blank, blank))
        sums[col, group : group + 1, :] = top
        sums[col, 4 + group : 5 + group, :] = jnp.sum(total, axis=0, keepdims=True)
        sums[col, 8 + group : 9 + group, :] = jnp.sum(picked, axis=0, keepdims=True)

    mom_copy = pltpu.make_async_remote_copy(
        src_ref=mom_ref,
        dst_ref=mom_far_ref,
        send_sem=mom_sems.at[0],
        recv_sem=mom_sems.at[1],
        device_id=across,
        device_id_type=MESH,
    )
    last_wave = RING_STARTS[-1] + STEPS
    for wave in range(2, last_wave + 1):
        ring_wave(wave)
        if 2 <= wave < 6:
            h_forward(0, wave - 2)
        if wave == LAYER_TWO_WAVE:
            for block in range(4):
                h_ready(0, block)
                layer(1, block, h_one, w_hid, h_two, slope_two)
            put(h_one, h_one_out)
            put(slope_two, slope_two_out)
            put(w_hid, w_hid_out)
        if LAYER_TWO_WAVE < wave <= LAYER_TWO_WAVE + 4:
            h_forward(1, wave - LAYER_TWO_WAVE - 1)
        for group, when in enumerate(LOGIT_WAVES):
            if wave == when:
                if group == 0:
                    for block in range(4):
                        h_ready(1, block)
                    put(h_two, h_two_out)
                    mom_copy.start()
                    for copy in tag_copies:
                        copy.wait_recv()
                rows = pl.ds(group * OUT_ROWS, OUT_ROWS)
                put(w_out.at[rows, :], w_out_out.at[rows, :])
                logits(group)

    sum_copies = [
        copy_to(target, sums.at[col], sum_send.at[number], sum_recv.at[number])
        for number, target in enumerate(others)
    ]
    for copy in sum_copies:
        copy.start()
    for copy in sum_copies:
        copy.wait_recv()

    def lines(first):
        return [sums[owner, first + group : first + group + 1, :] for owner in range(4) for group in range(4)]

    tops = lines(0)
    top = functools.reduce(jnp.maximum, tops)
    total = functools.reduce(
        jnp.add, [size * jnp.exp(own - top) for own, size in zip(tops, lines(4), strict=True)]
    )
    picked = functools.reduce(jnp.add, lines(8))
    line = all_tags()
    live = line >= 0
    loss = jnp.where(live, top + jnp.log(total) - picked, 0.0)
    loss = jnp.sum(loss, axis=1, keepdims=True)
    weight = jnp.where(live, 1.0 / slot_count, 0.0)
    line = jnp.broadcast_to(own_row(line), (16, frames))
    hit_weight = jnp.broadcast_to(weight, (16, frames))
    base = lax.broadcasted_iota(jnp.int32, (16, frames), 0)
    bias_col[...] = jnp.zeros_like(bias_col)
    for group in range(OUT_GROUPS):
        share = jnp.exp(sums[col, group : group + 1, :] - top) / total * weight

        def gradient(number, carry, first=group * OUT_ROWS, share=share):
            row = pl.multiple_of(first + number * 16, 16)
            value = curve[pl.ds(row, 16), :] * share - jnp.where(base + row == line, hit_weight, 0.0)
            value = value.astype(BF16)
            dl_ref[pl.ds(row, 16), :] = value
            value = value.astype(F32)
            bias_col[pl.ds(row, 16), :] = functools.reduce(
                jnp.add, [value[:, lane : lane + 128] for lane in range(0, frames, 128)]
            )
            return carry

        lax.fori_loop(0, OUT_ROWS // 16, gradient, 0)
    vec_ref[...] = jnp.zeros_like(vec_ref)
    row = 2 * units // 128
    for number in range(bias_out_ref.shape[0]):
        line = jnp.transpose(bias_col[number * 128 : (number + 1) * 128, :])
        line = jnp.sum(line, axis=0, keepdims=True)
        place = 128 * number + lax.broadcasted_iota(jnp.int32, line.shape, 1)
        line = jnp.where(place < senones, line, jnp.where(place == senones, loss, 0.0))
        vec_ref[row + number : row + number + 1, :] = line

    for group in range(len(RING_STARTS)):
        for way in range(2):
            for step in range(STEPS):
                ring_move(group, step, way).wait_send()
    for number in range(3):
        x_move(number).wait_send()
        for block in range(4):
            h_move(0, number, block).wait_send()
            h_move(1, number, block).wait_send()
    for copy in tag_copies + sum_copies:
        copy.wait_send()
    mom_copy.wait()
    for copy in outs:
        copy.wait()


def forward_pass(x, tags, w_in, w_hid, w_out, bias, bias_out, mom, slot_count):
    own_rows = x.shape[0]
    units = w_hid.shape[1]
    frames = 4 * own_rows
    wide = 4 * units
    rows = OUT_GROUPS * OUT_ROWS
    blocks = bias_out.shape[0]
    vmem = pl.BlockSpec(memory_space=pltpu.VMEM)
    hbm = pl.BlockSpec(memory_space=pl.ANY)
    sem = pltpu.SemaphoreType.DMA
    kept = (
        ((frames, 512), BF16),
        ((frames, wide), BF16),
        ((frames, wide), BF16),
        ((frames, units), F32),
        ((frames, units), F32),
        ((wide, units), BF16),
        ((rows, wide), BF16),
    )
    return pl.pallas_call(
        functools.partial(forward_kernel, slot_count),
        out_shape=tuple(jax.ShapeDtypeStruct(shape, kind) for shape, kind in kept)
        + (
            jax.ShapeDtypeStruct(mom.shape, F32),
            jax.ShapeDtypeStruct((rows, frames), BF16),
            jax.ShapeDtypeStruct((32, 128), F32),
        ),
        in_specs=[vmem] * 7 + [hbm],
        out_specs=(hbm,) * 8 + (vmem,) * 2,
        scratch_shapes=[pltpu.VMEM(shape, kind) for shape, kind in kept[:5]]
        + [
            pltpu.VMEM((512, units), BF16),
            pltpu.VMEM((wide, units), BF16),
            pltpu.VMEM((rows, wide), BF16),
            pltpu.VMEM((rows, frames), F32),
            pltpu.VMEM((blocks * 128, 128), F32),
            pltpu.VMEM((4,) + tags.shape, jnp.int32),
            pltpu.VMEM((4, 16, frames), F32),
            sem((5, 2, STEPS)),
            sem((5, 2, STEPS)),
            sem((3,)),
            sem((3,)),
            sem((2, 3, 4)),
            sem((2, 3, 4)),
            sem((3,)),
            sem((3,)),
            sem((3,)),
            sem((3,)),
            sem((16,)),
            sem((2,)),
        ],
        compiler_params=pltpu.CompilerParams(
            collective_id=2, has_side_effects=True, vmem_limit_bytes=60 * 1024 * 1024
        ),
    )(x, tags, w_in, w_hid, w_out, bias, bias_out, mom)


DIM_BITS = (2, 4, 8)
ORDERS = ((0, 1, 2), (1, 2, 0), (2, 0, 1))
PIECES = (
    ((0, 48, 0, 1792),),
    ((48, 96, 0, 1792),),
    ((96, 128, 0, 2048), (0, 96, 1792, 2048)),
)
SIZE_PIECE = 2
LIGHT_HID = 3
LIGHT_IN = 2


def stage_sends(stage, sources):
    moves = []
    for piece, order in enumerate(ORDERS):
        slot = sum(DIM_BITS[order[index]] for index in sources)
        moves.append((piece, slot, order[stage]))
    return moves


def landed(moves):
    return [(slot | DIM_BITS[dim], piece) for piece, slot, dim in moves]


FIRST = stage_sends(0, ())
SECOND = stage_sends(1, ())
SECOND_ON = stage_sends(1, (0,))
THIRD = stage_sends(2, ())
THIRD_A = stage_sends(2, (0,))
THIRD_B = stage_sends(2, (1,))
THIRD_C = stage_sends(2, (0, 1))
MOVES = FIRST + SECOND + SECOND_ON + THIRD + THIRD_A + THIRD_B + THIRD_C


def muon_kernel(
    stats_ref,
    red_hid_ref,
    mom_hid_ref,
    red_in_ref,
    mom_in_ref,
    red_far_ref,
    mom_far_ref,
    hid_ref,
    inp_ref,
    next_hid_ref,
    next_in_ref,
    norm_ref,
    codes,
    sizes,
    tops,
    lows,
    scales,
    weights,
    xs,
    us,
    vs,
    lhs,
    xin,
    xin_top,
    xin_low,
    gram,
    gram_got,
    back,
    sums,
    sums_got,
    spread_out,
    spread_got,
    spread_size_out,
    spread_size_got,
    send_sems,
    core_sems,
    recv_sems,
    back_send,
    back_recv,
    sums_send,
    sums_recv,
    spread_send,
    spread_recv,
    pair_send,
    pair_recv,
):
    blk = lax.axis_index("blk")
    col = lax.axis_index("col")
    rows, wide = xs.shape
    height = back.shape[2]
    deep = mom_in_ref.shape[0]
    part_wide = inp_ref.shape[1]
    other_core = {"col": col + 1 - 2 * (col % 2)}
    dims = (
        {"blk": blk + 1 - 2 * (blk % 2)},
        {"col": (col + 2) % 4},
        {"blk": blk + 2 - 4 * ((blk // 2) % 2)},
    )
    diagonal = {"blk": 4 * (blk // 4) + 3 - blk % 4}
    barrier = pltpu.get_barrier_semaphore()
    corner = {"col": (col + 2) % 4 + 1 - 2 * (col % 2)}
    cols = (other_core, dims[1], corner)
    for target in (*cols, *({"blk": (blk + away) % 8} for away in range(1, 8))):
        pl.semaphore_signal(barrier, inc=1, device_id=target, device_id_type=MESH)

    def fold(values):
        line = jnp.sum(values, axis=0, keepdims=True)
        return sum(line[:, lane : lane + 128] for lane in range(0, line.shape[1], 128))

    share = 0.125
    sums[blk, 0:1, :] = fold(stats_ref[...])
    sums[blk, 1:2, :] = fold(mom_hid_ref[...] * mom_hid_ref[...])
    red_hid = jnp.transpose(red_hid_ref[...])
    sums[blk, 2:3, :] = fold(mom_hid_ref[...] * red_hid)
    sums[blk, 3:4, :] = fold(red_hid_ref[...] * red_hid_ref[...])
    sums[blk, 4:5, :] = fold(mom_in_ref[...] * mom_in_ref[...]) * share
    sums[blk, 5:6, :] = fold(mom_in_ref[...] * red_in_ref[0:deep, :]) * share
    sums[blk, 6:7, :] = fold(red_in_ref[0:deep, :] * red_in_ref[0:deep, :]) * share
    sums[blk, 7:8, :] = jnp.zeros((1, 128), F32)
    eye = lax.broadcasted_iota(jnp.int32, (rows, rows), 0) == lax.broadcasted_iota(
        jnp.int32, (rows, rows), 1
    )
    pl.semaphore_wait(barrier, 10)

    def tell(own, targets, first):
        copies = []
        for number, target in enumerate(targets, start=first):
            copies.append(
                pltpu.make_async_remote_copy(
                    src_ref=own,
                    dst_ref=own,
                    send_sem=sums_send.at[number],
                    recv_sem=sums_recv.at[number],
                    device_id=target,
                    device_id_type=MESH,
                )
            )
            copies[-1].start()
        for copy in copies:
            copy.wait_recv()
        return copies

    told = tell(sums.at[blk], [{"blk": (blk + away) % 8} for away in range(1, 8)], 0)
    sums_got[col] = functools.reduce(jnp.add, [sums[number] for number in range(8)])
    told += tell(sums_got.at[col], cols, 7)
    whole = functools.reduce(jnp.add, [sums_got[number] for number in range(4)])
    whole = jnp.sum(whole, axis=1, keepdims=True)
    clip = jnp.sqrt(whole[0:1])
    factor = jnp.minimum(1.0, CLIP / clip)

    def norm_of(first):
        square = (
            0.25 * whole[first : first + 1]
            + factor * whole[first + 1 : first + 2]
            + factor * factor * whole[first + 2 : first + 3]
        )
        return 1.0 / (jnp.sqrt(jnp.maximum(square, 0.0)) + 1e-07)

    norm_ref[0:4, :] = jnp.broadcast_to(clip, (4, 128))
    norm_ref[4:8, :] = jnp.broadcast_to(factor, (4, 128))
    next_hid_ref[...] = 0.5 * mom_hid_ref[...] + factor * jnp.transpose(red_hid_ref[...])
    next_in_ref[...] = 0.5 * mom_in_ref[...] + factor * red_in_ref[0:deep, :]

    my_lanes = pl.ds(pl.multiple_of(blk * height, height), height)
    for number in range(4):
        there = slice(number * rows, (number + 1) * rows)
        value = jnp.transpose(next_hid_ref[:, there])
        largest = jnp.maximum(jnp.max(jnp.abs(value), axis=1, keepdims=True), 1e-30)
        spread_out[number] = to_codes(value * (TOP_CODE / largest))
        line = jnp.sum(jnp.where(eye, largest, 0.0), axis=0, keepdims=True)
        spread_size_out[number] = jnp.broadcast_to(line * (1.0 / TOP_CODE), (8, rows))
    spread = []
    for away in range(1, 8):
        target = (blk + away) % 8
        for kind, (src, dst) in enumerate(
            ((spread_out, spread_got), (spread_size_out, spread_size_got))
        ):
            spread.append(
                pltpu.make_async_remote_copy(
                    src_ref=src.at[target % 4],
                    dst_ref=dst.at[blk],
                    send_sem=spread_send.at[kind, away - 1],
                    recv_sem=spread_recv.at[kind, away - 1],
                    device_id={"blk": target},
                    device_id_type=MESH,
                )
            )
            spread[-1].start()
    high = col // 2
    my_half = pl.ds(pl.multiple_of(high * part_wide, part_wide), part_wide)
    far_half = pl.ds(pl.multiple_of((1 - high) * part_wide, part_wide), part_wide)
    in_scale = norm_of(4)
    xin[deep:, :] = jnp.zeros((xin.shape[0] - deep, xin.shape[1]), F32)
    xin[0:deep, my_half] = next_in_ref[...] * in_scale
    xin[0:deep, far_half] = (
        0.5 * mom_far_ref[...] + factor * red_far_ref[0:deep, :]
    ) * in_scale
    spread_got[blk] = spread_out[blk % 4]
    spread_size_got[blk] = spread_size_out[blk % 4]
    for copy in spread:
        copy.wait_recv()
    hid_scale = norm_of(1)
    for number in range(8):
        size = jnp.broadcast_to(spread_size_got[number, 0:1, :], (rows, rows))
        size = jnp.transpose(size) * hid_scale
        for lane in range(0, height, 128):
            xs[:, number * height + lane : number * height + lane + 128] = (
                from_codes(spread_got[number, :, lane : lane + 128]) * size
            )

    numbers = {move: number for number, move in enumerate(MOVES)}

    def parts(turn, slot, piece):
        refs = [
            codes.at[turn, slot, pl.ds(top, low - top), pl.ds(left, right - left)]
            for top, low, left, right in PIECES[piece]
        ]
        numbered = [(piece, refs[0])]
        if piece == SIZE_PIECE:
            numbered += [(3, refs[1]), (4, sizes.at[turn, slot])]
        return numbered

    def send(turn, move):
        piece, slot, dim = move
        there = slot | DIM_BITS[dim]
        return [
            pltpu.make_async_remote_copy(
                src_ref=src,
                dst_ref=dst,
                send_sem=send_sems.at[numbers[move], max(number - 2, 0)],
                recv_sem=recv_sems.at[turn, there, number],
                device_id=dims[dim],
                device_id_type=MESH,
            )
            for (number, src), (_, dst) in zip(
                parts(turn, slot, piece), parts(turn, there, piece), strict=True
            )
        ]

    def send_all(turn, moves):
        for move in moves:
            for copy in send(turn, move):
                copy.start()

    def to_core(turn, slot, piece):
        return [
            pltpu.make_async_remote_copy(
                src_ref=src,
                dst_ref=dst,
                send_sem=core_sems.at[slot // 2, number],
                recv_sem=recv_sems.at[turn, slot + 1, number],
                device_id=other_core,
                device_id_type=MESH,
            )
            for (number, src), (_, dst) in zip(
                parts(turn, slot, piece), parts(turn, slot + 1, piece), strict=True
            )
        ]

    def arrived(turn, slot, piece):
        for number, ref in parts(turn, slot, piece):
            pltpu.make_async_remote_copy(
                src_ref=ref,
                dst_ref=ref,
                send_sem=core_sems.at[0, 0],
                recv_sem=recv_sems.at[turn, slot, number],
                device_id=other_core,
                device_id_type=MESH,
            ).wait_recv()

    def forward(turn, moves, on=()):
        for number, (slot, piece) in enumerate(landed(moves)):
            arrived(turn, slot, piece)
            for copy in to_core(turn, slot, piece):
                copy.start()
            if on:
                send_all(turn, on[number : number + 1])

    def gram_copy():
        return pltpu.make_async_remote_copy(
            src_ref=gram,
            dst_ref=gram_got,
            send_sem=pair_send.at[1],
            recv_sem=pair_recv.at[1],
            device_id=other_core,
            device_id_type=MESH,
        )

    def unpack(turn, index, pair, light):
        for core in range(2):
            here = pl.ds(pl.multiple_of(index * 2 * rows + core * rows, rows), rows)
            slot = 2 * pair + core
            if light:
                tops[here, :] = from_codes(codes[turn, slot]).astype(BF16)
            else:
                top, low = halves(from_codes(codes[turn, slot]))
                tops[here, :] = top
                lows[here, :] = low
            size = sizes[turn, slot]
            scales[:, here] = size * size

    def inner(first, count, light):
        here = pl.ds(first, count)
        if light:
            values = dot_nt(lhs[0:rows, :], tops[here, :])
            weights[0:rows, here] = (values * scales[0:1, here]).astype(BF16)
        else:
            both = dot_nt(lhs[...], tops[here, :])
            values = both[:rows] + both[rows:] + dot_nt(lhs[0:rows, :], lows[here, :])
            top, low = halves(values * scales[0:1, here])
            weights[0:rows, here] = top
            weights[rows:, here] = low

    def outer(first, count, out, add, light):
        cut = 512
        here = slice(first, first + count)
        for start in range(0, wide, cut):
            lanes = slice(start, start + cut)
            if light:
                value = dot_nn(weights[0:rows, here], tops[here, lanes])
            else:
                both = dot_nn(weights[:, here], tops[here, lanes])
                value = both[:rows] + both[rows:] + dot_nn(weights[0:rows, here], lows[here, lanes])
            if add:
                value = value + out[:, lanes]
            out[:, lanes] = value

    def set_lhs(values):
        top, low = halves(values)
        lhs[0:rows, :] = top
        lhs[rows:, :] = low

    def input_gram(light):
        top, low = halves(xin[...])
        xin_top[...] = top
        if light:
            gram[...] = dot_nt(xin_top[...], xin_top[...])
        else:
            xin_low[...] = low
            cross = dot_nt(xin_top[...], xin_low[...])
            gram[...] = dot_nt(xin_top[...], xin_top[...]) + (cross + jnp.transpose(cross))
        gram_copy().start()

    def input_step(light):
        gram_copy().wait()
        square_of = gram[...] + gram_got[...]
        top, low = halves(square_of)
        if light:
            poly = NS_B * square_of + NS_C * dot_nn(top, top)
        else:
            cross = dot_nn(top, low)
            poly = NS_B * square_of + NS_C * (dot_nn(top, top) + (cross + jnp.transpose(cross)))
        top, low = halves(poly)
        cut = 512
        for start in range(0, xin.shape[1], cut):
            lanes = slice(start, start + cut)
            change = dot_nn(top, xin_top[:, lanes])
            if not light:
                change = change + dot_nn(low, xin_top[:, lanes]) + dot_nn(top, xin_low[:, lanes])
            xin[:, lanes] = NS_A * xin[:, lanes] + change

    def by_weight(number, limit, work):
        @pl.when(number < limit)
        def _():
            work(True)

        @pl.when(number >= limit)
        def _():
            work(False)

    def iteration(number, carry):
        turn = number % 2
        values = xs[...]
        largest = jnp.maximum(jnp.max(jnp.abs(values), axis=1, keepdims=True), 1e-30)
        codes[turn, 0] = to_codes(values * (TOP_CODE / largest))
        lane_size = jnp.sum(jnp.where(eye, largest, 0.0), axis=0, keepdims=True)
        sizes[turn, 0] = jnp.broadcast_to(lane_size * (1.0 / TOP_CODE), (8, rows))
        send_all(turn, FIRST)
        for piece in range(3):
            for copy in to_core(turn, 0, piece):
                copy.start()
        send_all(turn, SECOND)
        set_lhs(values)

        def first_pass(index, carry):
            pair = index + (index // 3) * (1 - index // 4) - (index // 4) * (1 - index // 5)

            @pl.when(index == 1)
            def _():
                forward(turn, FIRST, SECOND_ON)
                send_all(turn, THIRD)
                send_all(turn, THIRD_A)

                by_weight(number, LIGHT_IN, input_gram)

                forward(turn, SECOND, THIRD_B)
                forward(turn, SECOND_ON, THIRD_C)

                by_weight(number, LIGHT_IN, input_step)

                forward(turn, THIRD)

            @pl.when(index == 4)
            def _():
                forward(turn, THIRD_A)
                forward(turn, THIRD_B)

            @pl.when(index == 7)
            def _():
                forward(turn, THIRD_C)

            for piece in range(3):
                arrived(turn, 2 * pair + 1, piece)

            def work(light):
                unpack(turn, index, pair, light)
                inner(pl.multiple_of(index * 2 * rows, 2 * rows), 2 * rows, light)

            by_weight(number, LIGHT_HID, work)

            @pl.when(index == 3)
            def _():
                by_weight(number, LIGHT_HID, lambda light: outer(0, wide // 2, us, False, light))

            return carry

        lax.fori_loop(0, 8, first_pass, 0)

        def second_pass(light):
            outer(wide // 2, wide // 2, us, True, light)
            set_lhs(us[...])
            for first in range(0, wide, 512):
                inner(first, 512, light)
            outer(0, wide, vs, False, light)

        by_weight(number, LIGHT_HID, second_pass)
        xs[...] = NS_A * xs[...] + NS_B * us[...] + NS_C * vs[...]
        for move in MOVES:
            for copy in send(turn, move):
                copy.wait_send()
        for pair in range(8):
            for piece in range(3):
                for copy in to_core(turn, 2 * pair, piece):
                    copy.wait_send()
        return carry

    lax.fori_loop(0, NS, iteration, 0)

    place = blk % 4
    copies = []
    for rel, target in ((1, dims[0]), (2, dims[2]), (3, diagonal)):
        copies.append(
            pltpu.make_async_remote_copy(
                src_ref=xs.at[:, pl.ds(pl.multiple_of(target["blk"] * height, height), height)],
                dst_ref=back.at[place],
                send_sem=back_send.at[rel - 1],
                recv_sem=back_recv.at[rel - 1],
                device_id=target,
                device_id_type=MESH,
            )
        )
        copies[-1].start()
    back[place] = xs[:, my_lanes]
    inp_ref[...] = xin[0:deep, my_half]
    for copy in copies:
        copy.wait_recv()
    for number in range(4):
        hid_ref[:, number * rows : (number + 1) * rows] = jnp.transpose(back[number])
    for copy in copies + spread + told:
        copy.wait_send()


def muon(stats, red_hid, mom_hid, red_in, mom_in, red_far, mom_far, wide):
    rows = red_hid.shape[0] // 4
    height = red_hid.shape[1]
    deep, part_wide = red_in.shape
    vmem = pl.BlockSpec(memory_space=pltpu.VMEM)
    sem = pltpu.SemaphoreType.DMA
    return pl.pallas_call(
        muon_kernel,
        out_shape=(
            jax.ShapeDtypeStruct(mom_hid.shape, F32),
            jax.ShapeDtypeStruct(mom_in.shape, F32),
            jax.ShapeDtypeStruct(mom_hid.shape, F32),
            jax.ShapeDtypeStruct(mom_in.shape, F32),
            jax.ShapeDtypeStruct((8, 128), F32),
        ),
        in_specs=[vmem] * 7,
        out_specs=(vmem,) * 5,
        scratch_shapes=[
            pltpu.VMEM((2, 16, rows, wide), I16),
            pltpu.VMEM((2, 16, 8, rows), F32),
            pltpu.VMEM((wide, wide), BF16),
            pltpu.VMEM((wide, wide), BF16),
            pltpu.VMEM((8, wide), F32),
            pltpu.VMEM((2 * rows, wide), BF16),
            pltpu.VMEM((rows, wide), F32),
            pltpu.VMEM((rows, wide), F32),
            pltpu.VMEM((rows, wide), F32),
            pltpu.VMEM((2 * rows, wide), BF16),
            pltpu.VMEM((deep, 2 * part_wide), F32),
            pltpu.VMEM((deep, 2 * part_wide), BF16),
            pltpu.VMEM((deep, 2 * part_wide), BF16),
            pltpu.VMEM((deep, deep), F32),
            pltpu.VMEM((deep, deep), F32),
            pltpu.VMEM((4, rows, height), F32),
            pltpu.VMEM((8, 8, 128), F32),
            pltpu.VMEM((4, 8, 128), F32),
            pltpu.VMEM((4, rows, height), I16),
            pltpu.VMEM((8, rows, height), I16),
            pltpu.VMEM((4, 8, rows), F32),
            pltpu.VMEM((8, 8, rows), F32),
            sem((len(MOVES), 3)),
            sem((8, 5)),
            sem((2, 16, 5)),
            sem((3,)),
            sem((3,)),
            sem((10,)),
            sem((10,)),
            sem((2, 7)),
            sem((2, 7)),
            sem((2,)),
            sem((2,)),
        ],
        compiler_params=pltpu.CompilerParams(
            collective_id=0, has_side_effects=True, vmem_limit_bytes=60 * 1024 * 1024
        ),
    )(stats, red_hid, mom_hid, red_in, mom_in, red_far, mom_far)


def plain_body(
    frames,
    labels,
    mask,
    w_input,
    w_hidden,
    w_output,
    biases,
    mom_input,
    mom_hidden,
    out_first,
    out_second,
    bias_first,
    bias_second,
    res_input,
    res_hidden,
    res_output,
):
    ncol = lax.axis_size("col")
    nblk = lax.axis_size("blk")
    col_index = lax.axis_index("col")
    hcol = w_input.shape[1]
    scol = w_output.shape[1]
    micro = frames.shape[0]
    slot_count = frames.shape[1] * micro * nblk * ncol
    bias_row = biases[0]
    b_one = bias_row[:hcol]
    b_two = bias_row[hcol : 2 * hcol]
    b_out = bias_row[2 * hcol :]
    low_input = w_input.astype(jnp.bfloat16)
    row_tags = jnp.where(mask > 0, labels, -1)
    grad_input = jnp.zeros(w_input.shape, jnp.float32)
    grad_hidden = jnp.zeros((w_hidden.shape[0] * nblk, hcol), jnp.float32)
    grad_output = jnp.zeros((w_output.shape[0] * nblk, scol), jnp.float32)
    grad_bias = jnp.zeros(bias_row.shape, jnp.float32)
    loss_local = jnp.zeros((), jnp.float32)
    for micro_step in range(micro):
        low_hidden, low_output = (
            lax.all_gather(w_hidden.astype(jnp.bfloat16), "blk", axis=0, tiled=True),
            lax.all_gather(w_output.astype(jnp.bfloat16), "blk", axis=0, tiled=True),
        )
        inputs = lax.all_gather(frames[micro_step], "col", axis=0, tiled=True)
        tags_group = lax.all_gather(row_tags[micro_step], "col", axis=0, tiled=True)
        sig_one = jax.nn.sigmoid(matmul(inputs, low_input) + b_one)
        h_one = spread_cols(sig_one.astype(jnp.bfloat16))
        sig_two = jax.nn.sigmoid(matmul(h_one, low_hidden) + b_two)
        h_two = spread_cols(sig_two.astype(jnp.bfloat16))
        logits = matmul(h_two, low_output) + b_out
        row_top = lax.pmax(jnp.max(logits, axis=1), "col")
        exponent = jnp.exp(logits - row_top[:, None])
        target_hit = jnp.arange(scol)[None, :] == (tags_group - col_index * scol)[:, None]
        row_total, picked = lax.psum(
            (jnp.sum(exponent, axis=1), jnp.sum(jnp.where(target_hit, logits, 0.0), axis=1)), "col"
        )
        live_rows = tags_group >= 0
        loss_local = loss_local + jnp.sum(
            jnp.where(live_rows, row_top + jnp.log(row_total) - picked, 0.0)
        )
        probs = exponent / row_total[:, None]
        d_logits = (
            jnp.where(live_rows[:, None], probs - target_hit.astype(jnp.float32), 0.0) / slot_count
        ).astype(jnp.bfloat16)
        grad_output = grad_output + inner_rows(h_two, d_logits)
        d_h_two = reduce_cols(outer_cols(d_logits, low_output))
        d_z_two = (d_h_two * sig_two * (1.0 - sig_two)).astype(jnp.bfloat16)
        grad_hidden = grad_hidden + inner_rows(h_one, d_z_two)
        d_h_one = reduce_cols(outer_cols(d_z_two, low_hidden))
        d_z_one = (d_h_one * sig_one * (1.0 - sig_one)).astype(jnp.bfloat16)
        grad_input = grad_input + inner_rows(inputs, d_z_one)
        grad_bias = grad_bias + jnp.concatenate(
            [
                jnp.sum(d_z_one.astype(jnp.float32), axis=0),
                jnp.sum(d_z_two.astype(jnp.float32), axis=0),
                jnp.sum(d_logits.astype(jnp.float32), axis=0),
            ]
        )
    q_input, next_res_input = squash(grad_input, res_input[0])
    q_hidden, next_res_hidden = squash(grad_hidden, res_hidden[0])
    q_output, next_res_output = squash(grad_output, res_output[0])
    red_hidden, red_output = (
        lax.psum_scatter(q_hidden, "blk", scatter_dimension=0, tiled=True),
        lax.psum_scatter(q_output, "blk", scatter_dimension=0, tiled=True),
    )
    red_input, red_bias, loss_sum = lax.psum((q_input, grad_bias, loss_local), "blk")
    share_blk = 1.0 / nblk
    grad_square = (
        share_blk * (jnp.sum(red_input * red_input) + jnp.sum(red_bias * red_bias))
        + jnp.sum(red_hidden * red_hidden)
        + jnp.sum(red_output * red_output)
    )
    clip_norm = jnp.sqrt(lax.psum(grad_square, ("blk", "col")))
    factor = jnp.minimum(1.0, CLIP / clip_norm)
    next_mom_input = 0.5 * mom_input + factor * red_input
    next_mom_hidden = 0.5 * mom_hidden + factor * red_hidden
    square_input, square_hidden = lax.psum(
        (
            share_blk * jnp.sum(next_mom_input * next_mom_input),
            jnp.sum(next_mom_hidden * next_mom_hidden),
        ),
        ("blk", "col"),
    )
    iter_input = next_mom_input / (jnp.sqrt(square_input) + 1e-07)
    iter_hidden = next_mom_hidden / (jnp.sqrt(square_hidden) + 1e-07)
    for turn_index in range(NS):
        rows_hidden = collect_rows(iter_hidden)
        gram_input, gram_hidden = lax.psum(
            (precise(iter_input, iter_input.T), precise(iter_hidden, rows_hidden.T)), "col"
        )
        image_input = precise(gram_input, iter_input)
        image_hidden = precise(gram_hidden, rows_hidden)
        iter_input = (
            NS_A * iter_input + NS_B * image_input + NS_C * precise(gram_input, image_input)
        )
        iter_hidden = (
            NS_A * iter_hidden
            + NS_B * image_hidden
            + NS_C * precise(gram_hidden, collect_rows(image_hidden))
        )
    muon_scale = LR_MUON * 0.2 * math.sqrt(hcol * ncol)
    new_input = w_input * (1.0 - LR_MUON * WD_MUON) - muon_scale * iter_input
    new_hidden = w_hidden * (1.0 - LR_MUON * WD_MUON) - muon_scale * iter_hidden
    new_output, next_out_first, next_out_second = adam_step(
        w_output, factor * red_output, out_first, out_second
    )
    new_biases, next_bias_first, next_bias_second = adam_step(
        biases, factor * red_bias[None, :], bias_first, bias_second
    )
    return (
        loss_sum,
        clip_norm,
        new_input,
        new_hidden,
        new_output,
        new_biases,
        next_mom_input,
        next_mom_hidden,
        next_out_first,
        next_out_second,
        next_bias_first,
        next_bias_second,
        next_res_input[None],
        next_res_hidden[None],
        next_res_output[None],
    )


def fast_body(
    frames,
    labels,
    mask,
    w_input,
    w_hidden,
    w_output,
    biases,
    mom_input,
    mom_hidden,
    out_first,
    out_second,
    bias_first,
    bias_second,
    res_input,
    res_hidden,
    res_output,
):
    ncol = lax.axis_size("col")
    nblk = lax.axis_size("blk")
    col_index = lax.axis_index("col")
    blk_index = lax.axis_index("blk")
    hcol = w_input.shape[1]
    scol = w_output.shape[1]
    micro = frames.shape[0]
    slot_count = frames.shape[1] * micro * nblk * ncol
    bias_row = biases[0]
    deep = w_input.shape[0]
    padded = 512
    rows_out = OUT_GROUPS * OUT_ROWS
    own_tags = jnp.where(mask > 0, labels, -1).reshape(1, -1)
    layer_biases = jnp.pad(bias_row[: 2 * hcol].reshape(2, hcol), ((0, 6), (0, 0)))
    blocks = -(-rows_out // 128)
    out_biases = jnp.pad(bias_row[2 * hcol :], (0, blocks * 128 - scol)).reshape(blocks, 128)
    inputs, h_one, h_two, slope_one, slope_two, low_hidden, low_output, mom_far, d_logits, vec = (
        forward_pass(
            frames.reshape(-1, deep),
            jnp.broadcast_to(own_tags, (8, own_tags.shape[1])),
            w_input,
            w_hidden,
            w_output.T,
            layer_biases,
            out_biases,
            mom_input,
            slot_count,
        )
    )
    next_out, codes, sizes, partial = squash_out(d_logits, h_two, res_output[0].T, low_output)
    next_hid, next_in, red_out, red_hid, red_in, red_far, vec_sum, stats = reduce_grads(
        codes,
        sizes,
        h_one,
        inputs,
        partial,
        slope_two,
        slope_one,
        low_hidden,
        res_hidden[0],
        jnp.pad(res_input[0], ((0, padded - deep), (0, 0))).T,
        vec,
        scol,
        deep,
    )
    next_res_output = next_out.transpose(1, 2, 0)
    next_res_hidden = next_hid
    next_res_input = next_in[:, :deep].T
    red_output = red_out[:scol].T
    vec_sum = vec_sum.reshape(-1)
    red_bias = vec_sum[: bias_row.shape[0]]
    loss_sum = vec_sum[bias_row.shape[0]]
    done_hidden, done_input, next_mom_hidden, next_mom_input, norms = muon(
        stats,
        red_hid,
        mom_hidden,
        red_in,
        mom_input,
        red_far,
        mom_far,
        hcol * ncol,
    )
    clip_norm = norms[0, 0]
    factor = norms[4, 0]
    muon_scale = LR_MUON * 0.2 * math.sqrt(hcol * ncol)
    new_input = w_input * (1.0 - LR_MUON * WD_MUON) - muon_scale * done_input
    new_hidden = w_hidden * (1.0 - LR_MUON * WD_MUON) - muon_scale * done_hidden
    new_output, next_out_first, next_out_second = adam_step(
        w_output, factor * red_output, out_first, out_second
    )
    new_biases, next_bias_first, next_bias_second = adam_step(
        biases, factor * red_bias[None, :], bias_first, bias_second
    )
    return (
        loss_sum,
        clip_norm,
        new_input,
        new_hidden,
        new_output,
        new_biases,
        next_mom_input,
        next_mom_hidden,
        next_out_first,
        next_out_second,
        next_bias_first,
        next_bias_second,
        next_res_input[None],
        next_res_hidden[None],
        next_res_output,
    )


def solution(mesh):
    in_specs = (
        P(None, ("blk", "col"), None),
        P(None, ("blk", "col")),
        P(None, ("blk", "col")),
        P(None, "col"),
        P("blk", "col"),
        P("blk", "col"),
        P("col", None),
        P(None, "col"),
        P("blk", "col"),
        P("blk", "col"),
        P("blk", "col"),
        P("col", None),
        P("col", None),
        P("blk", None, "col"),
        P("blk", None, "col"),
        P("blk", None, "col"),
    )
    out_specs = (
        P(),
        P(),
        P(None, "col"),
        P("blk", "col"),
        P("blk", "col"),
        P("col", None),
        P(None, "col"),
        P("blk", "col"),
        P("blk", "col"),
        P("blk", "col"),
        P("col", None),
        P("col", None),
        P("blk", None, "col"),
        P("blk", None, "col"),
        P("blk", None, "col"),
    )
    cubes = mesh.shape["blk"] == 8 and mesh.shape["col"] == 4
    body = fast_body if cubes else plain_body
    return jax.shard_map(body, mesh=mesh, in_specs=in_specs, out_specs=out_specs, check_vma=False)
```

```python
import functools
import math

import jax
import jax.numpy as jnp
from jax import lax
from jax.experimental import pallas as pl
from jax.experimental.pallas import tpu as pltpu
from jax.sharding import PartitionSpec as P

NS = 5
STEP = 5


NS_A = 3.4445
NS_B = -4.775
NS_C = 2.0315
CLIP = 0.002
LR_MUON = 0.1
WD_MUON = 0.01
LR_ADAM = 0.03
WD_ADAM = 0.1

MESH = pl.DeviceIdType.MESH
F32 = jnp.float32
BF16 = jnp.bfloat16
I16 = jnp.int16
LN2 = math.log(2.0)
TOP_CODE = 32700.0
LEVELS = 64.0


def matmul(left_side, right_side):
    return jnp.dot(left_side, right_side, preferred_element_type=jnp.float32)


def inner_rows(left_side, right_side):
    return lax.dot_general(
        left_side, right_side, (((0,), (0,)), ((), ())), preferred_element_type=jnp.float32
    )


def outer_cols(left_side, right_side):
    return lax.dot_general(
        left_side, right_side, (((1,), (1,)), ((), ())), preferred_element_type=jnp.float32
    )


def precise(left_side, right_side):
    return jnp.dot(
        left_side, right_side, precision=lax.Precision.HIGHEST, preferred_element_type=jnp.float32
    )


def spread_cols(values):
    return lax.all_gather(values, "col", axis=1, tiled=True)


def reduce_cols(values):
    return lax.psum_scatter(values, "col", scatter_dimension=1, tiled=True)


def collect_rows(values):
    return lax.all_gather(values, "blk", axis=0, tiled=True)


def squash(gradient, resid):
    value = gradient + resid.astype(jnp.float32)
    scale = jnp.mean(jnp.abs(value), axis=0, keepdims=True) + 1e-12
    signed = scale * jnp.tanh(2.0 * value / scale)
    return (signed, value - signed)


def adam_step(weight, gradient, first, second):
    first = 0.5 * first + 0.5 * gradient
    second = 0.95 * second + 0.05 * gradient * gradient
    update = first / (1.0 - 0.5**STEP) / (jnp.sqrt(second / (1.0 - 0.95**STEP)) + 1e-08)
    return (weight - LR_ADAM * (update + WD_ADAM * weight), first, second)


def halves(values):
    top = values.astype(BF16)
    return top, (values - top.astype(F32)).astype(BF16)


def dot_nn(left_side, right_side):
    return lax.dot_general(
        left_side, right_side, (((1,), (0,)), ((), ())), preferred_element_type=F32
    )


def dot_nt(left_side, right_side):
    return lax.dot_general(
        left_side, right_side, (((1,), (1,)), ((), ())), preferred_element_type=F32
    )


RING = 8
STEPS = RING - 1
OUT_ROWS = 592
OUT_GROUPS = 4
HID_ROWS = 512
HID_GROUP = 4
IN_GROUP = 5
TURN_AT = 5
CROSS_AT = 6
HID_AT = 13
FINISH_AT = 14
IN_AT = 20
HID_HOP = 3


def ring_place(blk):
    odd = blk % 2
    return (blk // 2) * (1 - odd) + (7 - blk // 2) * odd


def ring_blk(place):
    back = place // 4
    return 2 * place * (1 - back) + (15 - 2 * place) * back


def scale_code(size):
    return jnp.ceil(jnp.log(jnp.maximum(size, 1e-30)) * (LEVELS / LN2))


def code_scale(code):
    return jnp.exp(code * (LN2 / LEVELS))


def to_codes(values):
    return jnp.round(values).astype(jnp.int32).astype(I16)


def from_codes(codes):
    return codes.astype(jnp.int32).astype(F32)


def chunk_of(lane):
    number = lane // 256
    return number // 2 if number % 2 == 0 else 7 - number // 2


def squash_kernel(senones, dl_ref, h_ref, res_ref, next_ref, codes_ref, size_ref, grad, cols, marks):
    group = pl.program_id(0)
    rows, wide = grad.shape
    valid = senones - group * rows
    for first, count in ((0, rows // 32 * 16), (rows // 32 * 16, rows - rows // 32 * 16)):
        there = slice(first, first + count)
        total = jnp.zeros((count, 128), F32)
        for lane in range(0, wide, 512):
            value = dot_nn(dl_ref[there, :], h_ref[:, lane : lane + 512])
            value = value + res_ref[there, lane : lane + 512].astype(F32)
            row = first + lax.broadcasted_iota(jnp.int32, value.shape, 0)
            value = jnp.where(row < valid, value, 0.0)
            grad[there, lane : lane + 512] = value
            value = jnp.abs(value)
            for part in range(0, 512, 128):
                total = total + value[:, part : part + 128]
        size = jnp.sum(total, axis=1, keepdims=True) * (1.0 / wide) + 1e-12
        size = jnp.broadcast_to(size, (count, 128))
        marks[there, :] = size
        cols[0, there, :] = size
        cols[1, there, :] = 2.0 / size

    def some(number, carry):
        row = pl.multiple_of(number * 16, 16)
        size = cols[0, pl.ds(row, 16), :]
        steep = cols[1, pl.ds(row, 16), :]
        for lane in range(0, wide, 128):
            piece = grad[pl.ds(row, 16), lane : lane + 128]
            curve = jnp.tanh(piece * steep)
            codes_ref[0, 2 * chunk_of(lane) + lane // 128 % 2, pl.ds(row, 16), :] = to_codes(
                curve * TOP_CODE
            )
            next_ref[pl.ds(row, 16), 0, lane : lane + 128] = piece - size * curve
        return carry

    lax.fori_loop(0, rows // 16, some, 0)
    marks[rows:, :] = jnp.zeros((marks.shape[0] - rows, 128), F32)
    lines = [jnp.transpose(marks[first : first + 128, :])[0:1, :] for first in range(0, rows, 128)]
    lines.append(jnp.zeros((8 - len(lines), 128), F32))
    size_ref[0] = jnp.concatenate(lines, axis=0)


def squash_out(dl, h_two, res_out):
    senones, wide = res_out.shape
    frames = dl.shape[1]
    return pl.pallas_call(
        functools.partial(squash_kernel, senones),
        grid=(OUT_GROUPS,),
        out_shape=(
            jax.ShapeDtypeStruct((senones, 1, wide), F32),
            jax.ShapeDtypeStruct((OUT_GROUPS, 2 * RING, OUT_ROWS, 128), I16),
            jax.ShapeDtypeStruct((OUT_GROUPS, 8, 128), F32),
        ),
        in_specs=[
            pl.BlockSpec((OUT_ROWS, frames), lambda group: (group, 0)),
            pl.BlockSpec((frames, wide), lambda group: (0, 0)),
            pl.BlockSpec((OUT_ROWS, wide), lambda group: (group, 0)),
        ],
        out_specs=(
            pl.BlockSpec((OUT_ROWS, 1, wide), lambda group: (group, 0, 0)),
            pl.BlockSpec((1, 2 * RING, OUT_ROWS, 128), lambda group: (group, 0, 0, 0)),
            pl.BlockSpec((1, 8, 128), lambda group: (group, 0, 0)),
        ),
        scratch_shapes=[
            pltpu.VMEM((OUT_ROWS, wide), F32),
            pltpu.VMEM((2, OUT_ROWS, 128), F32),
            pltpu.VMEM((640, 128), F32),
        ],
        compiler_params=pltpu.CompilerParams(vmem_limit_bytes=60 * 1024 * 1024),
    )(dl, h_two, res_out)


def reduce_kernel(
    deep,
    senones,
    codes_ref,
    sizes_ref,
    h_one_ref,
    x_ref,
    part_ref,
    slope_two_ref,
    slope_one_ref,
    w_hid_ref,
    res_hid_ref,
    res_in_ref,
    vec_ref,
    next_hid_ref,
    next_in_ref,
    red_out_ref,
    red_hid_ref,
    red_in_ref,
    red_far_ref,
    vec_sum_ref,
    stats_ref,
    grad,
    turned,
    res_buf,
    h_buf,
    slope_buf,
    marks,
    cols,
    keep_sums,
    dz,
    dz_two,
    dz_one,
    core_out,
    core_got,
    far_out,
    far_got,
    own_out,
    got_out,
    own_hid,
    got_hid,
    own_in,
    got_in,
    share_in,
    share_far,
    sizes,
    shares,
    vec,
    vecs,
    res_sems,
    load_sems,
    code_sems,
    slope_sems,
    core_send,
    core_recv,
    far_send,
    far_recv,
    out_send,
    out_recv,
    hid_send,
    hid_recv,
    in_send,
    in_recv,
    share_send,
    share_recv,
    vec_send,
    vec_recv,
    size_send,
    size_recv,
    share_far_send,
    share_far_recv,
):
    blk = lax.axis_index("blk")
    col = lax.axis_index("col")
    here = ring_place(blk)
    core, high = col % 2, col // 2
    cores = {"col": col + 1 - 2 * core}
    across = {"col": (col + 2) % 4}
    barrier = pltpu.get_barrier_semaphore()
    for target in (cores, across, *({"blk": (blk + away) % RING} for away in range(1, RING))):
        pl.semaphore_signal(barrier, inc=1, device_id=target, device_id_type=MESH)

    def code_copy(group):
        return pltpu.make_async_copy(codes_ref.at[group], own_out.at[group], code_sems.at[group])

    def hid_res_copy(part):
        return pltpu.make_async_copy(
            res_hid_ref.at[:, pl.ds(part * 256, 256)],
            res_buf.at[part],
            res_sems.at[part],
        )

    def hid_next_copy(part):
        return pltpu.make_async_copy(
            turned, next_hid_ref.at[:, pl.ds(part * 256, 256)], load_sems.at[1]
        )

    def load(src, dst):
        return pltpu.make_async_copy(src, dst, load_sems.at[0])

    for group in range(OUT_GROUPS):
        code_copy(group).start()
    for part in range(2):
        hid_res_copy(part).start()
    load(h_one_ref, h_buf).start()
    marks[...] = jnp.zeros_like(marks)
    stats_ref[...] = jnp.zeros_like(stats_ref)
    vec[...] = vec_ref[...]
    pl.semaphore_wait(barrier, RING + 1)

    CHUNK = 256
    units = slope_buf.shape[2]

    def slope_copy(layer, block):
        rows = pl.ds(pl.multiple_of(block * CHUNK, CHUNK), CHUNK)
        src = (slope_two_ref, slope_one_ref)[layer]
        return pltpu.make_async_copy(src.at[rows, :], slope_buf.at[block % 2], slope_sems.at[block % 2])

    def core_move(layer, block):
        return pltpu.make_async_remote_copy(
            src_ref=core_out.at[block % 2],
            dst_ref=core_got.at[layer, block],
            send_sem=core_send.at[block % 2],
            recv_sem=core_recv.at[layer, block],
            device_id=cores,
            device_id_type=MESH,
        )

    def far_move(layer, block):
        return pltpu.make_async_remote_copy(
            src_ref=far_out.at[block % 2],
            dst_ref=far_got.at[layer, block],
            send_sem=far_send.at[block % 2],
            recv_sem=far_recv.at[layer, block],
            device_id=across,
            device_id_type=MESH,
        )

    def lanes_of(number):
        return pl.ds(pl.multiple_of(number * units, units), units)

    def rows_at(number):
        return pl.ds(pl.multiple_of(number * 16, 16), 16)

    def free(copy, layer, block):
        @pl.when((layer > 0) | (block >= 2))
        def _():
            copy.wait_send()

    def lane_codes(first):
        return jnp.transpose(marks[first : first + 128, :])[0:1, :]

    def set_factors():
        top = jnp.max(cols[0, 0:CHUNK, :], axis=1, keepdims=True)
        code = scale_code(top)
        marks[0:CHUNK, :] = jnp.broadcast_to(code, (CHUNK, 128))
        cols[1, 0:CHUNK, :] = jnp.broadcast_to(TOP_CODE / code_scale(code), (CHUNK, 128))

    def largest(values):
        return functools.reduce(
            jnp.maximum,
            [
                jnp.abs(value[:, lane : lane + 128])
                for value in values
                for lane in range(0, value.shape[1], 128)
            ],
        )

    def scaled(values, factor):
        return jnp.concatenate(
            [values[:, lane : lane + 128] * factor for lane in range(0, values.shape[1], 128)], axis=1
        )

    def put_scale(out):
        codes = jnp.concatenate(
            [lane_codes(0), lane_codes(128), jnp.zeros((14, 128), F32)], axis=0
        )
        out[CHUNK : CHUNK + 16, 0:128] = codes.astype(jnp.int32).astype(I16)

    def read_scale(got):
        step = code_scale(from_codes(got[CHUNK : CHUNK + 16, 0:128])) * (1.0 / TOP_CODE)
        step = jnp.transpose(jnp.concatenate([step, jnp.zeros((112, 128), F32)], axis=0))
        for up in range(2):
            marks[CHUNK + up * 128 : CHUNK + (up + 1) * 128, :] = jnp.broadcast_to(
                step[:, up : up + 1], (128, 128)
            )

    def step_at(number):
        return marks[pl.ds(pl.multiple_of(CHUNK + number * 16, 16), 16), :]

    def split(layer, block):
        free(core_move(layer, block), layer, block)

        def measure(number, carry):
            rows = rows_at(number)
            cols[0, rows, :] = largest(
                [grad[rows, lanes_of(2 * half + 1 - core)] for half in range(2)]
            )
            return carry

        lax.fori_loop(0, CHUNK // 16, measure, 0)
        set_factors()

        def write(number, carry):
            rows = rows_at(number)
            factor = cols[1, rows, :]
            for half in range(2):
                there = slice(half * units, (half + 1) * units)
                core_out[block % 2, rows, there] = to_codes(
                    scaled(grad[rows, lanes_of(2 * half + 1 - core)], factor)
                )
                keep_sums[block, rows, there] = grad[rows, lanes_of(2 * half + core)]
            return carry

        lax.fori_loop(0, CHUNK // 16, write, 0)
        put_scale(core_out.at[block % 2])
        core_move(layer, block).start()

    def cross(layer, block):
        core_move(layer, block).wait_recv()
        free(far_move(layer, block), layer, block)
        got = core_got.at[layer, block]
        read_scale(got)

        def add(number, carry):
            rows = rows_at(number)
            near, away = lanes_of(high), lanes_of(1 - high)
            step = step_at(number)
            keep_sums[block, rows, near] += scaled(from_codes(got[rows, near]), step)
            value = keep_sums[block, rows, away] + scaled(from_codes(got[rows, away]), step)
            keep_sums[block, rows, away] = value
            cols[0, rows, :] = largest([value])
            return carry

        lax.fori_loop(0, CHUNK // 16, add, 0)
        set_factors()

        def write(number, carry):
            rows = rows_at(number)
            far_out[block % 2, rows, :] = to_codes(
                scaled(keep_sums[block, rows, lanes_of(1 - high)], cols[1, rows, :])
            )
            return carry

        lax.fori_loop(0, CHUNK // 16, write, 0)
        put_scale(far_out.at[block % 2])
        far_move(layer, block).start()

    def finish(layer, block):
        far_move(layer, block).wait_recv()
        slope_copy(layer, block).wait()
        got = far_got.at[layer, block]
        read_scale(got)

        def one(number, total):
            rows = rows_at(number)
            value = keep_sums[block, rows, lanes_of(high)] + scaled(
                from_codes(got[rows, :]), step_at(number)
            )
            value = (value * slope_buf[block % 2, rows, :]).astype(BF16)
            dz[rows, :] = value
            return total + value.astype(F32)

        total = lax.fori_loop(0, CHUNK // 16, one, jnp.zeros((16, units), F32))
        if layer == 0:

            @pl.when(block < 2)
            def _():
                slope_copy(0, block + 2).start()

            @pl.when(block >= 2)
            def _():
                slope_copy(1, block - 2).start()

        else:

            @pl.when(block < 2)
            def _():
                slope_copy(1, block + 2).start()

        total = jnp.sum(total, axis=0, keepdims=True)
        for number in range(units // 128):
            row = 4 * (1 - layer) + number
            vec[row : row + 1, :] += total[:, number * 128 : (number + 1) * 128]
        flipped = (dz_two, dz_one)[layer]
        for up in range(CHUNK // 128):
            there = pl.ds(pl.multiple_of(block * CHUNK + up * 128, 128), 128)
            for number in range(units // 128):
                tile = dz[up * 128 : (up + 1) * 128, number * 128 : (number + 1) * 128]
                flipped[number * 128 : (number + 1) * 128, there] = jnp.transpose(
                    tile.astype(F32)
                ).astype(BF16)

    def blocks(first, last, work):
        def one(block, carry):
            work(block)
            return carry

        lax.fori_loop(first, last, one, 0)

    def start_block(block):
        rows = pl.ds(pl.multiple_of(block * CHUNK, CHUNK), CHUNK)
        copy = pltpu.make_async_copy(part_ref.at[rows, :], grad.at[pl.ds(0, CHUNK), :], load_sems.at[1])
        copy.start()
        copy.wait()
        split(0, block)

    def turn_block(block):
        finish(0, block)
        for lane in range(0, grad.shape[1], 512):
            grad[0:CHUNK, lane : lane + 512] = dot_nt(dz[...], w_hid_ref[lane : lane + 512, :])
        split(1, block)

    core_out[:, CHUNK:, :] = jnp.zeros((2, 16, 2 * units), I16)
    far_out[:, CHUNK:, :] = jnp.zeros((2, 16, units), I16)
    slope_copy(0, 0).start()
    slope_copy(0, 1).start()
    def vec_copy(away):
        return pltpu.make_async_remote_copy(
            src_ref=vec,
            dst_ref=vecs.at[blk],
            send_sem=vec_send.at[away - 1],
            recv_sem=vec_recv.at[away - 1],
            device_id={"blk": (blk + away) % RING},
            device_id_type=MESH,
        )

    def set_rows(count, first_own, size):
        size = jnp.broadcast_to(size, (count, 128))
        marks[first_own : first_own + count, :] = size
        cols[0, 0:count, :] = size
        cols[1, 0:count, :] = 2.0 / size

    def tell_sizes(group):
        for away in range(1, RING):
            size_copy(group, away).start()

    def size_copy(group, away):
        return pltpu.make_async_remote_copy(
            src_ref=sizes.at[group, here],
            dst_ref=sizes.at[group, here],
            send_sem=size_send.at[group, away - 1],
            recv_sem=size_recv.at[group, away - 1],
            device_id={"blk": ring_blk((here + away) % RING)},
            device_id_type=MESH,
        )

    def set_sizes(rows, group):
        parts = [lane_codes(first) for first in range(0, rows, 128)]
        parts.append(jnp.zeros((8 - len(parts), 128), F32))
        sizes[group, here] = jnp.concatenate(parts, axis=0)
        tell_sizes(group)

    def make_shares(group, row_of):
        for away in range(1, RING):
            size_copy(group, away).wait_recv()
        for way in range(2):
            tiles = []
            for step in range(STEPS):
                mine = row_of(here, step, way)
                came = mine * 0.0
                for back in range(step + 1):
                    came = came + row_of((here - 1 - back + (2 + 2 * back) * way + RING) % RING, step, way)
                if step < STEPS - 1:
                    whole = 1.0 / jnp.maximum(came + mine, 1e-30)
                else:
                    whole = 1.0 / TOP_CODE
                tiles += [came * whole, mine * whole]
            tiles.append(jnp.zeros((16, 128), F32))
            shares[group, way] = jnp.transpose(jnp.concatenate(tiles, axis=0))

    def hid_group():
        load(h_one_ref, h_buf).wait()
        wide = grad.shape[1]
        for part in range(2):
            first = part * 256
            hid_res_copy(part).wait()
            total = jnp.zeros((256, 128), F32)
            for lane in range(0, wide, 512):
                value = dot_nn(dz_two[first : first + 256, :], h_buf[:, lane : lane + 512])
                value = value + jnp.transpose(res_buf[part, lane : lane + 512, :].astype(F32))
                grad[:, lane : lane + 512] = value
                value = jnp.abs(value)
                for more in range(0, 512, 128):
                    total = total + value[:, more : more + 128]
            set_rows(
                256, first, jnp.sum(total, axis=1, keepdims=True) * (1.0 / wide) + 1e-12
            )

            def some(number, carry, first=first):
                row = pl.multiple_of(number * 16, 16)
                size = cols[0, pl.ds(row, 16), :]
                steep = cols[1, pl.ds(row, 16), :]
                for lane in range(0, wide, 128):
                    piece = grad[pl.ds(row, 16), lane : lane + 128]
                    curve = jnp.tanh(piece * steep)
                    own_hid[2 * chunk_of(lane) + lane // 128 % 2, pl.ds(first + row, 16), :] = (
                        to_codes(curve * TOP_CODE)
                    )
                    grad[pl.ds(row, 16), lane : lane + 128] = piece - size * curve
                return carry

            lax.fori_loop(0, 16, some, 0)
            if part:
                hid_next_copy(part - 1).wait()
            for lane in range(0, wide, 128):
                turned[lane : lane + 128, :] = jnp.transpose(grad[:, lane : lane + 128])
            hid_next_copy(part).start()
        load(x_ref, h_buf.at[:, pl.ds(0, x_ref.shape[1])]).start()
        set_sizes(HID_ROWS, HID_GROUP)
        hid_next_copy(1).wait()

    def in_group():
        wide = x_ref.shape[1]
        load(x_ref, h_buf.at[:, pl.ds(0, wide)]).wait()
        for top in range(0, wide, 128):
            count = min(128, deep - top)
            for left in range(0, HID_ROWS, 128):
                tile = res_in_ref[top : top + count, left : left + 128].astype(F32)
                if count < 128:
                    tile = jnp.concatenate([tile, jnp.zeros((128 - count, 128), F32)], axis=0)
                place, lane = top // 256 * HID_ROWS + left, top % 256
                turned[place : place + 128, lane : lane + 128] = jnp.transpose(tile)
        for first in range(0, HID_ROWS, 256):
            grad[0:256, 0:wide] = dot_nn(dz_one[first : first + 256, :], h_buf[:, 0:wide])

            def add(number, carry, first=first):
                row = pl.multiple_of(number * 16, 16)
                place = pl.multiple_of(first + row, 16)
                value = grad[pl.ds(row, 16), 0:wide] + jnp.concatenate(
                    [turned[pl.ds(place, 16), :], turned[pl.ds(HID_ROWS + place, 16), :]], axis=1
                )
                grad[pl.ds(row, 16), 0:wide] = value
                value = jnp.abs(value)
                cols[0, pl.ds(row, 16), :] = functools.reduce(
                    jnp.add, [value[:, lane : lane + 128] for lane in range(0, wide, 128)]
                )
                return carry

            lax.fori_loop(0, 16, add, 0)
            set_rows(
                256,
                first,
                jnp.sum(cols[0, 0:256, :], axis=1, keepdims=True) * (1.0 / deep) + 1e-12,
            )

            def some(number, carry, first=first):
                row = pl.multiple_of(number * 16, 16)
                place = pl.multiple_of(first + row, 16)
                size = cols[0, pl.ds(row, 16), :]
                steep = cols[1, pl.ds(row, 16), :]
                chunk = first // 64 + number // 4
                inside = pl.multiple_of(number % 4 * 16, 16)
                for lane in range(0, wide, 128):
                    piece = grad[pl.ds(row, 16), lane : lane + 128]
                    curve = jnp.tanh(piece * steep)
                    turned[
                        pl.ds(lane // 256 * HID_ROWS + place, 16), lane % 256 : lane % 256 + 128
                    ] = piece - size * curve
                    own_in[
                        2 * chunk + lane // 256, pl.ds(inside, 16), lane % 256 : lane % 256 + 128
                    ] = to_codes(curve * TOP_CODE)
                return carry

            lax.fori_loop(0, 16, some, 0)
        for top in range(0, wide, 128):
            count = min(128, deep - top)
            for left in range(0, HID_ROWS, 128):
                place, lane = top // 256 * HID_ROWS + left, top % 256
                tile = jnp.transpose(turned[place : place + 128, lane : lane + 128])
                next_in_ref[top : top + count, left : left + 128] = tile[0:count, :]
        sizes[IN_GROUP, here] = jnp.concatenate(
            [lane_codes(64 * chunk) for chunk in range(RING)], axis=0
        )
        tell_sizes(IN_GROUP)

    def towards(way):
        return {"blk": ring_blk((here + 1 - 2 * way + RING) % RING)}

    def move(src, got, step, way, send_sem, recv_sem):
        return pltpu.make_async_remote_copy(
            src_ref=src,
            dst_ref=got.at[way, step],
            send_sem=send_sem.at[way, step],
            recv_sem=recv_sem.at[way, step],
            device_id=towards(way),
            device_id_type=MESH,
        )

    def first_moves(own, got, send_sem, recv_sem):
        for way in range(2):
            chunk = (here - 1 + 2 * way + RING) % RING
            move(own.at[2 * chunk + way], got, 0, way, send_sem, recv_sem).start()

    def hop(rows, own, got, group, step, send_sem, recv_sem, keep):
        for way in range(2):
            move(got.at[way, step], got, step, way, send_sem, recv_sem).wait_recv()

        def add(way, result):
            message = got.at[way, step]
            ahead = here - 2 - step + way * (4 + 2 * step) + 2 * RING
            mine = own.at[2 * (ahead % RING) + way]
            share = pltpu.roll(shares[group, way], (128 - 16 * step) % 128, 1)
            for number, first in enumerate(range(0, rows, 128)):
                count = min(128, rows - first)
                there = slice(first, first + count)
                result(
                    first,
                    count,
                    from_codes(message[there, :]) * share[0:count, number : number + 1]
                    + from_codes(mine[there, :]) * share[0:count, 8 + number : 9 + number],
                )

        @pl.when(step < STEPS - 1)
        def _():
            for way in range(2):

                def write(first, count, value, way=way):
                    got[way, step, first : first + count, :] = to_codes(value)

                add(way, write)
            for way in range(2):
                move(got.at[way, step], got, step + 1, way, send_sem, recv_sem).start()

        @pl.when(step == STEPS - 1)
        def _():
            for way in range(2):

                def finish_rows(first, count, value, way=way):
                    keep(way, first, count, value)
                    square = jnp.sum(value * value, axis=0, keepdims=True)
                    for lane in range(0, value.shape[1], 128):
                        stats_ref[0:1, :] += square[:, lane : lane + 128]

                add(way, finish_rows)

    def out_hop(group, step):
        def keep(way, first, count, value):
            row = pl.multiple_of(group * OUT_ROWS + first, 16)
            red_out_ref[pl.ds(row, count), way * 128 : (way + 1) * 128] = value

        hop(
            OUT_ROWS,
            own_out.at[group],
            got_out.at[group],
            group,
            step,
            out_send.at[group],
            out_recv.at[group],
            keep,
        )

    def hid_hop(step):
        def keep(way, first, count, value):
            red_hid_ref[first : first + count, way * 128 : (way + 1) * 128] = value

        hop(HID_ROWS, own_hid, got_hid, HID_GROUP, step, hid_send, hid_recv, keep)

    def share_move(step, way):
        place = (here - step + 2 * step * way + 2 * RING) % RING
        return pltpu.make_async_remote_copy(
            src_ref=share_in.at[way, place],
            dst_ref=share_in.at[way, place],
            send_sem=share_send.at[way, step],
            recv_sem=share_recv.at[way, step],
            device_id=towards(way),
            device_id_type=MESH,
        )

    def share_across(way, place):
        return pltpu.make_async_remote_copy(
            src_ref=share_in.at[way, place],
            dst_ref=share_far.at[way, place],
            send_sem=share_far_send.at[way, place],
            recv_sem=share_far_recv.at[way, place],
            device_id=across,
            device_id_type=MESH,
        )

    def in_hop(step):
        def keep(way, first, count, value):
            share_in[way, here] = value

        hop(64, own_in, got_in, IN_GROUP, step, in_send, in_recv, keep)

        @pl.when(step == STEPS - 1)
        def _():
            for way in range(2):
                share_move(0, way).start()
                share_across(way, here).start()

    def share_hop(step):
        for way in range(2):
            share_move(step, way).wait_recv()
            share_across(way, (here - 1 - step + (2 + 2 * step) * way + RING) % RING).start()

        @pl.when(step < STEPS - 1)
        def _():
            for way in range(2):
                share_move(step + 1, way).start()

    def in_step(index):
        @pl.when((index >= 0) & (index < STEPS))
        def _():
            in_hop(index)

        @pl.when((index >= STEPS) & (index < 2 * STEPS))
        def _():
            share_hop(index - STEPS)

    def chunk_row(place, step, way):
        chunk = (here - 2 - step + way * (4 + 2 * step) + 2 * RING) % RING
        line = sizes[IN_GROUP, place, pl.ds(chunk, 1), :]
        return jnp.broadcast_to(line, (8, 128))

    for group in range(OUT_GROUPS):
        sizes[group, here] = sizes_ref[group]
        tell_sizes(group)
        code_copy(group).wait()
        first_moves(own_out.at[group], got_out.at[group], out_send.at[group], out_recv.at[group])
    blocks(0, 4, start_block)

    def each(number, first, spacing, count, work):
        after = number - first

        @pl.when((after >= 0) & (after < spacing * count) & (after % spacing == 0))
        def _():
            work(after // spacing)

    def turn(number, carry):
        @pl.when(number < OUT_GROUPS)
        def _():
            make_shares(number, lambda place, step, way: sizes[number, place])

        @pl.when(number < OUT_GROUPS * STEPS)
        def _():
            out_hop(number % OUT_GROUPS, number // OUT_GROUPS)

        @pl.when(number == HID_AT + HID_HOP)
        def _():
            make_shares(HID_GROUP, lambda place, step, way: sizes[HID_GROUP, place])

        each(number, HID_AT + HID_HOP, HID_HOP, STEPS, hid_hop)

        @pl.when(number == IN_AT + 1)
        def _():
            make_shares(IN_GROUP, chunk_row)

        in_step(number - IN_AT - 1)
        each(number, 0, 1, 4, lambda block: cross(0, block))
        each(number, TURN_AT, 2, 4, turn_block)
        each(number, CROSS_AT, 2, 4, lambda block: cross(1, block))

        @pl.when(number == HID_AT)
        def _():
            hid_group()
            first_moves(own_hid, got_hid, hid_send, hid_recv)

        each(number, FINISH_AT, 2, 4, lambda block: finish(1, block))

        @pl.when(number == IN_AT)
        def _():
            in_group()
            first_moves(own_in, got_in, in_send, in_recv)
            for away in range(1, RING):
                vec_copy(away).start()

        return carry

    turns = max(IN_AT + 1 + 2 * STEPS, HID_AT + HID_HOP * STEPS + 1, OUT_GROUPS * STEPS)
    lax.fori_loop(0, turns, turn, 0)

    def unfold(shares_of, out):
        for place in range(0, RING, 2):
            for way in range(2):
                for lane in range(0, 256, 128):
                    tile = jnp.concatenate(
                        [shares_of[way, place + more, :, lane : lane + 128] for more in range(2)],
                        axis=0,
                    )
                    first = way * 256 + lane
                    out[first : first + 128, place * 64 : place * 64 + 128] = jnp.transpose(tile)

    unfold(share_in, red_in_ref)
    for place in range(RING):
        for way in range(2):
            share_across(way, place).wait_recv()
    unfold(share_far, red_far_ref)
    for away in range(1, RING):
        vec_copy(away).wait_recv()
    vecs[blk] = vec[...]
    total = vecs[0]
    for number in range(1, RING):
        total = total + vecs[number]
    vec_sum_ref[...] = total
    flat = 128 * lax.broadcasted_iota(jnp.int32, total.shape, 0) + lax.broadcasted_iota(
        jnp.int32, total.shape, 1
    )
    total = jnp.where(flat < 2 * units + senones, total, 0.0)
    stats_ref[1:2, :] = jnp.sum(total * total, axis=0, keepdims=True) * (1.0 / RING)
    for away in range(1, RING):
        vec_copy(away).wait_send()
        for group in range(OUT_GROUPS + 2):
            size_copy(group, away).wait_send()
    for slot in range(2):
        core_move(1, 2 + slot).wait_send()
        far_move(1, 2 + slot).wait_send()
    for way in range(2):
        for step in range(STEPS):
            for group in range(OUT_GROUPS):
                move(
                    got_out.at[group, way, step],
                    got_out.at[group],
                    step,
                    way,
                    out_send.at[group],
                    out_recv.at[group],
                ).wait_send()
            move(got_hid.at[way, step], got_hid, step, way, hid_send, hid_recv).wait_send()
            move(got_in.at[way, step], got_in, step, way, in_send, in_recv).wait_send()
            share_move(step, way).wait_send()
        for place in range(RING):
            share_across(way, place).wait_send()


def reduce_grads(
    codes, sizes, h_one, x, part, slope_two, slope_one, w_hid, res_hid, res_in, vec, senones, deep
):
    frames, wide = h_one.shape
    in_wide = x.shape[1]
    units = w_hid.shape[1]
    vmem = pl.BlockSpec(memory_space=pltpu.VMEM)
    hbm = pl.BlockSpec(memory_space=pl.ANY)
    message = OUT_ROWS
    hid_message = HID_ROWS
    in_message = 64
    sem = pltpu.SemaphoreType.DMA
    return pl.pallas_call(
        functools.partial(reduce_kernel, deep, senones),
        out_shape=(
            jax.ShapeDtypeStruct((wide, HID_ROWS), F32),
            jax.ShapeDtypeStruct(res_in.shape, F32),
            jax.ShapeDtypeStruct((OUT_GROUPS * OUT_ROWS, 256), F32),
            jax.ShapeDtypeStruct((HID_ROWS, 256), F32),
            jax.ShapeDtypeStruct((in_wide, HID_ROWS), F32),
            jax.ShapeDtypeStruct((in_wide, HID_ROWS), F32),
            jax.ShapeDtypeStruct(vec.shape, F32),
            jax.ShapeDtypeStruct((8, 128), F32),
        ),
        in_specs=[hbm, vmem] + [hbm] * 5 + [vmem, hbm, vmem, vmem],
        out_specs=(hbm,) + (vmem,) * 7,
        scratch_shapes=[
            pltpu.VMEM((256, wide), F32),
            pltpu.VMEM((wide, 256), F32),
            pltpu.VMEM((2, wide, 256), BF16),
            pltpu.VMEM((frames, wide), BF16),
            pltpu.VMEM((2, 256, units), F32),
            pltpu.VMEM((640, 128), F32),
            pltpu.VMEM((2, 256, 128), F32),
            pltpu.VMEM((4, 256, 2 * units), F32),
            pltpu.VMEM((256, units), BF16),
            pltpu.VMEM((units, frames), BF16),
            pltpu.VMEM((units, frames), BF16),
            pltpu.VMEM((2, 272, 2 * units), I16),
            pltpu.VMEM((2, 4, 272, 2 * units), I16),
            pltpu.VMEM((2, 272, units), I16),
            pltpu.VMEM((2, 4, 272, units), I16),
            pltpu.VMEM((OUT_GROUPS, 2 * RING, message, 128), I16),
            pltpu.VMEM((OUT_GROUPS, 2, STEPS, message, 128), I16),
            pltpu.VMEM((2 * RING, hid_message, 128), I16),
            pltpu.VMEM((2, STEPS, hid_message, 128), I16),
            pltpu.VMEM((2 * RING, in_message, 256), I16),
            pltpu.VMEM((2, STEPS, in_message, 256), I16),
            pltpu.VMEM((2, RING, 64, 256), F32),
            pltpu.VMEM((2, RING, 64, 256), F32),
            pltpu.VMEM((OUT_GROUPS + 2, RING, 8, 128), F32),
            pltpu.VMEM((OUT_GROUPS + 2, 2, 128, 128), F32),
            pltpu.VMEM(vec.shape, F32),
            pltpu.VMEM((RING,) + vec.shape, F32),
            sem((2,)),
            sem((2,)),
            sem((OUT_GROUPS,)),
            sem((2,)),
            sem((2,)),
            sem((2, 4)),
            sem((2,)),
            sem((2, 4)),
            sem((OUT_GROUPS, 2, STEPS)),
            sem((OUT_GROUPS, 2, STEPS)),
            sem((2, STEPS)),
            sem((2, STEPS)),
            sem((2, STEPS)),
            sem((2, STEPS)),
            sem((2, STEPS)),
            sem((2, STEPS)),
            sem((STEPS,)),
            sem((STEPS,)),
            sem((OUT_GROUPS + 2, STEPS)),
            sem((OUT_GROUPS + 2, STEPS)),
            sem((2, RING)),
            sem((2, RING)),
        ],
        compiler_params=pltpu.CompilerParams(
            collective_id=1, has_side_effects=True, vmem_limit_bytes=63 * 1024 * 1024
        ),
    )(codes, sizes, h_one, x, part, slope_two, slope_one, w_hid, res_hid, res_in, vec)


RING_STARTS = (0, 0, 5, 6, 7)
LAYER_TWO_WAVE = 7
LOGIT_WAVES = (11, 12, 13, 14)


def forward_kernel(
    slot_count,
    x_ref,
    labels_ref,
    mask_ref,
    w_in_ref,
    w_hid_ref,
    w_out_ref,
    bias_ref,
    mom_ref,
    x_out,
    h_one_out,
    h_two_out,
    slope_one_out,
    slope_two_out,
    w_hid_out,
    w_out_out,
    mom_far_ref,
    dl_ref,
    vec_ref,
    x_all,
    h_one,
    h_two,
    slope_one,
    slope_two,
    w_in,
    w_hid,
    w_out,
    curve,
    bias_line,
    bias_col,
    tags,
    sums,
    ring_send,
    ring_recv,
    x_send,
    x_recv,
    h_send,
    h_recv,
    tag_send,
    tag_recv,
    sum_send,
    sum_recv,
    out_sems,
    mom_sems,
):
    blk = lax.axis_index("blk")
    col = lax.axis_index("col")
    here = ring_place(blk)
    senones, depth = w_out_ref.shape
    own_rows, deep = x_ref.shape
    units = w_hid_ref.shape[1]
    frames = x_all.shape[0]
    cores = {"col": col + 1 - 2 * (col % 2)}
    across = {"col": (col + 2) % 4}
    corner = {"col": (col + 2) % 4 + 1 - 2 * (col % 2)}
    others = (cores, across, corner)

    barrier = pltpu.get_barrier_semaphore()
    for target in others + tuple({"blk": ring_blk((here + way) % RING)} for way in (1, 7)):
        pl.semaphore_signal(barrier, inc=1, device_id=target, device_id_type=MESH)

    w_hid[pl.ds(pl.multiple_of(blk * depth, depth), depth), :] = w_hid_ref[...].astype(BF16)
    own_lanes = pl.ds(pl.multiple_of(blk * depth, depth), depth)
    w_out[senones // 16 * 16 :, own_lanes] = jnp.zeros(
        (w_out.shape[0] - senones // 16 * 16, depth), BF16
    )
    w_out[0:senones, own_lanes] = w_out_ref[...].astype(BF16)
    own_frames = pl.ds(pl.multiple_of(col * own_rows, own_rows), own_rows)
    x_all[own_frames, :] = jnp.zeros((own_rows, x_all.shape[1]), BF16)
    x_all[own_frames, 0:deep] = x_ref[...]
    own_tags = jnp.where(mask_ref[...] > 0, labels_ref[...], -1)
    own_tags = jnp.concatenate([own_tags[row : row + 1, :] for row in range(own_tags.shape[0])], axis=1)
    tags[col] = jnp.broadcast_to(own_tags, (8, own_rows))
    bias_line[...] = jnp.zeros_like(bias_line)
    bias_line[:, 0 : bias_ref.shape[1]] = bias_ref[...]
    sums[...] = jnp.zeros_like(sums)
    pl.semaphore_wait(barrier, 5)

    def ring_part(group, origin, way):
        start = pl.multiple_of(origin * depth + way * 128, 128)
        if group == 0:
            return w_hid.at[pl.ds(start, 128), :]
        return w_out.at[pl.ds((group - 1) * OUT_ROWS, OUT_ROWS), pl.ds(start, 128)]

    def ring_move(group, step, way):
        origin = ring_blk((here - step + 2 * step * way + RING) % RING)
        part = ring_part(group, origin, way)
        return pltpu.make_async_remote_copy(
            src_ref=part,
            dst_ref=part,
            send_sem=ring_send.at[group, way, step],
            recv_sem=ring_recv.at[group, way, step],
            device_id={"blk": ring_blk((here + 1 - 2 * way + RING) % RING)},
            device_id_type=MESH,
        )

    def ring_wave(wave):
        for group, start in enumerate(RING_STARTS):
            step = wave - 1 - start
            for way in range(2):
                if step == -1:
                    ring_move(group, 0, way).start()
                if 0 <= step < STEPS:
                    ring_move(group, step, way).wait_recv()
                    if step < STEPS - 1:
                        ring_move(group, step + 1, way).start()

    def copy_to(target, src, send_sem, recv_sem):
        return pltpu.make_async_remote_copy(
            src_ref=src,
            dst_ref=src,
            send_sem=send_sem,
            recv_sem=recv_sem,
            device_id=target,
            device_id_type=MESH,
        )

    def rows_of(owner):
        return pl.ds(pl.multiple_of(owner * own_rows, own_rows), own_rows)

    def lanes_of(owner):
        return pl.ds(pl.multiple_of(owner * units, units), units)

    def x_move(number):
        owner = across["col"] if number == 2 else col
        target = across if number == 1 else cores
        return copy_to(target, x_all.at[rows_of(owner), :], x_send.at[number], x_recv.at[number])

    def h_move(layer, number, block):
        owner = across["col"] if number == 2 else col
        target = across if number == 1 else cores
        whole = (h_one, h_two)[layer]
        part = whole.at[pl.ds(block * own_rows, own_rows), lanes_of(owner)]
        return copy_to(
            target, part, h_send.at[layer, number, block], h_recv.at[layer, number, block]
        )

    def h_start(layer, block):
        h_move(layer, 0, block).start()
        h_move(layer, 1, block).start()

    def h_forward(layer, block):
        h_move(layer, 1, block).wait_recv()
        h_move(layer, 2, block).start()

    def h_ready(layer, block):
        h_move(layer, 0, block).wait_recv()
        h_move(layer, 2, block).wait_recv()

    ring_wave(0)
    x_move(0).start()
    x_move(1).start()
    tag_copies = [
        copy_to(target, tags.at[col], tag_send.at[number], tag_recv.at[number])
        for number, target in enumerate(others)
    ]
    for copy in tag_copies:
        copy.start()
    w_in[...] = jnp.zeros_like(w_in)
    w_in[0:deep, :] = w_in_ref[...].astype(BF16)
    for number in range(bias_col.shape[0] // 128):
        first = 2 * units + number * 128
        line = jnp.broadcast_to(bias_line[:, first : first + 128], (128, 128))
        bias_col[number * 128 : (number + 1) * 128, :] = jnp.transpose(line)
    ring_wave(1)
    x_move(1).wait_recv()
    x_move(2).start()
    x_move(0).wait_recv()
    x_move(2).wait_recv()

    def layer(number, block, inputs, weights, whole, slopes):
        there = slice(block * own_rows, (block + 1) * own_rows)
        value = jax.nn.sigmoid(
            dot_nn(inputs[there, :], weights[...])
            + bias_line[:, number * units : (number + 1) * units]
        )
        slopes[there, :] = value * (1.0 - value)
        whole[there, lanes_of(col)] = value.astype(BF16)
        h_start(number, block)

    outs = []

    def put(src, dst):
        copy = pltpu.make_async_copy(src, dst, out_sems.at[len(outs)])
        copy.start()
        outs.append(copy)

    for block in range(4):
        layer(0, block, x_all, w_in, h_one, slope_one)
    put(x_all, x_out)
    put(slope_one, slope_one_out)

    def all_tags():
        return jnp.concatenate([tags[owner, 0:1, :] for owner in range(4)], axis=1)

    def own_row(line):
        line = line - col * senones
        return jnp.where(line < senones, line, -1)

    def logits(group):
        first = group * OUT_ROWS
        half = frames // 2
        for part in range(2):
            curve[first : first + OUT_ROWS, part * half : (part + 1) * half] = dot_nt(
                w_out[first : first + OUT_ROWS, :], h_two[part * half : (part + 1) * half, :]
            )
        base = lax.broadcasted_iota(jnp.int32, (16, frames), 0)

        def largest(number, top):
            row = pl.multiple_of(first + number * 16, 16)
            value = curve[pl.ds(row, 16), :] + bias_col[pl.ds(row, 16), 0:1]
            if group == OUT_GROUPS - 1:
                value = jnp.where(base + row < senones, value, -1e30)
            curve[pl.ds(row, 16), :] = value
            return jnp.maximum(top, value)

        top = lax.fori_loop(0, OUT_ROWS // 16, largest, jnp.full((16, frames), -1e30, F32))
        top = jnp.max(top, axis=0, keepdims=True)
        line = jnp.broadcast_to(own_row(all_tags()), (16, frames))

        def exponents(number, carry):
            total, picked = carry
            row = pl.multiple_of(first + number * 16, 16)
            value = curve[pl.ds(row, 16), :]
            power = jnp.exp(value - top)
            curve[pl.ds(row, 16), :] = power
            return total + power, picked + jnp.where(base + row == line, value, 0.0)

        blank = jnp.zeros((16, frames), F32)
        total, picked = lax.fori_loop(0, OUT_ROWS // 16, exponents, (blank, blank))
        sums[col, group : group + 1, :] = top
        sums[col, 4 + group : 5 + group, :] = jnp.sum(total, axis=0, keepdims=True)
        sums[col, 8 + group : 9 + group, :] = jnp.sum(picked, axis=0, keepdims=True)

    mom_copy = pltpu.make_async_remote_copy(
        src_ref=mom_ref,
        dst_ref=mom_far_ref,
        send_sem=mom_sems.at[0],
        recv_sem=mom_sems.at[1],
        device_id=across,
        device_id_type=MESH,
    )
    last_wave = RING_STARTS[-1] + STEPS
    for wave in range(2, last_wave + 1):
        ring_wave(wave)
        if 2 <= wave < 6:
            h_forward(0, wave - 2)
        if wave == LAYER_TWO_WAVE:
            for block in range(4):
                h_ready(0, block)
                layer(1, block, h_one, w_hid, h_two, slope_two)
            put(h_one, h_one_out)
            put(slope_two, slope_two_out)
            put(w_hid, w_hid_out)
        if LAYER_TWO_WAVE < wave <= LAYER_TWO_WAVE + 4:
            h_forward(1, wave - LAYER_TWO_WAVE - 1)
        for group, when in enumerate(LOGIT_WAVES):
            if wave == when:
                if group == 0:
                    for block in range(4):
                        h_ready(1, block)
                    put(h_two, h_two_out)
                    mom_copy.start()
                    for copy in tag_copies:
                        copy.wait_recv()
                rows = pl.ds(group * OUT_ROWS, OUT_ROWS)
                put(w_out.at[rows, :], w_out_out.at[rows, :])
                logits(group)

    sum_copies = [
        copy_to(target, sums.at[col], sum_send.at[number], sum_recv.at[number])
        for number, target in enumerate(others)
    ]
    for copy in sum_copies:
        copy.start()
    for copy in sum_copies:
        copy.wait_recv()

    def lines(first):
        return [sums[owner, first + group : first + group + 1, :] for owner in range(4) for group in range(4)]

    tops = lines(0)
    top = functools.reduce(jnp.maximum, tops)
    total = functools.reduce(
        jnp.add, [size * jnp.exp(own - top) for own, size in zip(tops, lines(4), strict=True)]
    )
    picked = functools.reduce(jnp.add, lines(8))
    line = all_tags()
    live = line >= 0
    loss = jnp.where(live, top + jnp.log(total) - picked, 0.0)
    loss = jnp.sum(loss, axis=1, keepdims=True)
    weight = jnp.where(live, 1.0 / slot_count, 0.0)
    line = jnp.broadcast_to(own_row(line), (16, frames))
    hit_weight = jnp.broadcast_to(weight, (16, frames))
    base = lax.broadcasted_iota(jnp.int32, (16, frames), 0)
    bias_col[...] = jnp.zeros_like(bias_col)
    for group in range(OUT_GROUPS):
        share = jnp.exp(sums[col, group : group + 1, :] - top) / total * weight

        def gradient(number, carry, first=group * OUT_ROWS, share=share):
            row = pl.multiple_of(first + number * 16, 16)
            value = curve[pl.ds(row, 16), :] * share - jnp.where(base + row == line, hit_weight, 0.0)
            value = value.astype(BF16)
            dl_ref[pl.ds(row, 16), :] = value
            value = value.astype(F32)
            bias_col[pl.ds(row, 16), :] = functools.reduce(
                jnp.add, [value[:, lane : lane + 128] for lane in range(0, frames, 128)]
            )
            return carry

        lax.fori_loop(0, OUT_ROWS // 16, gradient, 0)
    vec_ref[...] = jnp.zeros_like(vec_ref)
    row = 2 * units // 128
    for number in range(bias_col.shape[0] // 128):
        line = jnp.transpose(bias_col[number * 128 : (number + 1) * 128, :])
        line = jnp.sum(line, axis=0, keepdims=True)
        place = 128 * number + lax.broadcasted_iota(jnp.int32, line.shape, 1)
        line = jnp.where(place < senones, line, jnp.where(place == senones, loss, 0.0))
        vec_ref[row + number : row + number + 1, :] = line

    for group in range(len(RING_STARTS)):
        for way in range(2):
            for step in range(STEPS):
                ring_move(group, step, way).wait_send()
    for number in range(3):
        x_move(number).wait_send()
        for block in range(4):
            h_move(0, number, block).wait_send()
            h_move(1, number, block).wait_send()
    for copy in tag_copies + sum_copies:
        copy.wait_send()
    mom_copy.wait()
    for copy in outs:
        copy.wait()


def forward_pass(x, labels, mask, w_in, w_hid, w_out, bias, mom, slot_count):
    own_rows = x.shape[0]
    units = w_hid.shape[1]
    frames = 4 * own_rows
    wide = 4 * units
    rows = OUT_GROUPS * OUT_ROWS
    blocks = -(-rows // 128)
    vmem = pl.BlockSpec(memory_space=pltpu.VMEM)
    hbm = pl.BlockSpec(memory_space=pl.ANY)
    sem = pltpu.SemaphoreType.DMA
    kept = (
        ((frames, 512), BF16),
        ((frames, wide), BF16),
        ((frames, wide), BF16),
        ((frames, units), F32),
        ((frames, units), F32),
        ((wide, units), BF16),
        ((rows, wide), BF16),
    )
    return pl.pallas_call(
        functools.partial(forward_kernel, slot_count),
        out_shape=tuple(jax.ShapeDtypeStruct(shape, kind) for shape, kind in kept)
        + (
            jax.ShapeDtypeStruct(mom.shape, F32),
            jax.ShapeDtypeStruct((rows, frames), BF16),
            jax.ShapeDtypeStruct((32, 128), F32),
        ),
        in_specs=[vmem] * 7 + [hbm],
        out_specs=(hbm,) * 8 + (vmem,) * 2,
        scratch_shapes=[pltpu.VMEM(shape, kind) for shape, kind in kept[:5]]
        + [
            pltpu.VMEM((512, units), BF16),
            pltpu.VMEM((wide, units), BF16),
            pltpu.VMEM((rows, wide), BF16),
            pltpu.VMEM((rows, frames), F32),
            pltpu.VMEM((1, 2 * units + blocks * 128), F32),
            pltpu.VMEM((blocks * 128, 128), F32),
            pltpu.VMEM((4, 8, own_rows), jnp.int32),
            pltpu.VMEM((4, 16, frames), F32),
            sem((5, 2, STEPS)),
            sem((5, 2, STEPS)),
            sem((3,)),
            sem((3,)),
            sem((2, 3, 4)),
            sem((2, 3, 4)),
            sem((3,)),
            sem((3,)),
            sem((3,)),
            sem((3,)),
            sem((16,)),
            sem((2,)),
        ],
        compiler_params=pltpu.CompilerParams(
            collective_id=2, has_side_effects=True, vmem_limit_bytes=60 * 1024 * 1024
        ),
    )(x, labels, mask, w_in, w_hid, w_out, bias, mom)


DIM_BITS = (2, 4, 8)
ORDERS = ((0, 1, 2), (1, 2, 0), (2, 0, 1))
PIECES = (
    ((0, 48, 0, 1792),),
    ((48, 96, 0, 1792),),
    ((96, 128, 0, 2048), (0, 96, 1792, 2048)),
)
SIZE_PIECE = 2
LIGHT_HID = 3
LIGHT_IN = 2


def stage_sends(stage, sources):
    moves = []
    for piece, order in enumerate(ORDERS):
        slot = sum(DIM_BITS[order[index]] for index in sources)
        moves.append((piece, slot, order[stage]))
    return moves


def landed(moves):
    return [(slot | DIM_BITS[dim], piece) for piece, slot, dim in moves]


FIRST = stage_sends(0, ())
SECOND = stage_sends(1, ())
SECOND_ON = stage_sends(1, (0,))
THIRD = stage_sends(2, ())
THIRD_A = stage_sends(2, (0,))
THIRD_B = stage_sends(2, (1,))
THIRD_C = stage_sends(2, (0, 1))
MOVES = FIRST + SECOND + SECOND_ON + THIRD + THIRD_A + THIRD_B + THIRD_C


def muon_kernel(
    stats_ref,
    red_hid_ref,
    mom_hid_ref,
    red_in_ref,
    mom_in_ref,
    red_far_ref,
    mom_far_ref,
    hid_ref,
    inp_ref,
    next_hid_ref,
    next_in_ref,
    norm_ref,
    codes,
    sizes,
    tops,
    lows,
    scales,
    weights,
    xs,
    us,
    vs,
    lhs,
    xin,
    xin_top,
    xin_low,
    gram,
    gram_got,
    back,
    sums,
    sums_got,
    spread_out,
    spread_got,
    spread_size_out,
    spread_size_got,
    send_sems,
    core_sems,
    recv_sems,
    back_send,
    back_recv,
    sums_send,
    sums_recv,
    spread_send,
    spread_recv,
    pair_send,
    pair_recv,
):
    blk = lax.axis_index("blk")
    col = lax.axis_index("col")
    rows, wide = xs.shape
    height = back.shape[2]
    deep = mom_in_ref.shape[0]
    part_wide = inp_ref.shape[1]
    other_core = {"col": col + 1 - 2 * (col % 2)}
    dims = (
        {"blk": blk + 1 - 2 * (blk % 2)},
        {"col": (col + 2) % 4},
        {"blk": blk + 2 - 4 * ((blk // 2) % 2)},
    )
    diagonal = {"blk": 4 * (blk // 4) + 3 - blk % 4}
    barrier = pltpu.get_barrier_semaphore()
    corner = {"col": (col + 2) % 4 + 1 - 2 * (col % 2)}
    cols = (other_core, dims[1], corner)
    for target in (*cols, *({"blk": (blk + away) % 8} for away in range(1, 8))):
        pl.semaphore_signal(barrier, inc=1, device_id=target, device_id_type=MESH)

    def fold(values):
        line = jnp.sum(values, axis=0, keepdims=True)
        return sum(line[:, lane : lane + 128] for lane in range(0, line.shape[1], 128))

    share = 0.125
    sums[blk, 0:1, :] = fold(stats_ref[...])
    sums[blk, 1:2, :] = fold(mom_hid_ref[...] * mom_hid_ref[...])
    red_hid = jnp.transpose(red_hid_ref[...])
    sums[blk, 2:3, :] = fold(mom_hid_ref[...] * red_hid)
    sums[blk, 3:4, :] = fold(red_hid_ref[...] * red_hid_ref[...])
    sums[blk, 4:5, :] = fold(mom_in_ref[...] * mom_in_ref[...]) * share
    sums[blk, 5:6, :] = fold(mom_in_ref[...] * red_in_ref[0:deep, :]) * share
    sums[blk, 6:7, :] = fold(red_in_ref[0:deep, :] * red_in_ref[0:deep, :]) * share
    sums[blk, 7:8, :] = jnp.zeros((1, 128), F32)
    eye = lax.broadcasted_iota(jnp.int32, (rows, rows), 0) == lax.broadcasted_iota(
        jnp.int32, (rows, rows), 1
    )
    pl.semaphore_wait(barrier, 10)

    def tell(own, targets, first):
        copies = []
        for number, target in enumerate(targets, start=first):
            copies.append(
                pltpu.make_async_remote_copy(
                    src_ref=own,
                    dst_ref=own,
                    send_sem=sums_send.at[number],
                    recv_sem=sums_recv.at[number],
                    device_id=target,
                    device_id_type=MESH,
                )
            )
            copies[-1].start()
        for copy in copies:
            copy.wait_recv()
        return copies

    told = tell(sums.at[blk], [{"blk": (blk + away) % 8} for away in range(1, 8)], 0)
    sums_got[col] = functools.reduce(jnp.add, [sums[number] for number in range(8)])
    told += tell(sums_got.at[col], cols, 7)
    whole = functools.reduce(jnp.add, [sums_got[number] for number in range(4)])
    whole = jnp.sum(whole, axis=1, keepdims=True)
    clip = jnp.sqrt(whole[0:1])
    factor = jnp.minimum(1.0, CLIP / clip)

    def norm_of(first):
        square = (
            0.25 * whole[first : first + 1]
            + factor * whole[first + 1 : first + 2]
            + factor * factor * whole[first + 2 : first + 3]
        )
        return 1.0 / (jnp.sqrt(jnp.maximum(square, 0.0)) + 1e-07)

    norm_ref[0:4, :] = jnp.broadcast_to(clip, (4, 128))
    norm_ref[4:8, :] = jnp.broadcast_to(factor, (4, 128))
    next_hid_ref[...] = 0.5 * mom_hid_ref[...] + factor * jnp.transpose(red_hid_ref[...])
    next_in_ref[...] = 0.5 * mom_in_ref[...] + factor * red_in_ref[0:deep, :]

    my_lanes = pl.ds(pl.multiple_of(blk * height, height), height)
    for number in range(4):
        there = slice(number * rows, (number + 1) * rows)
        value = jnp.transpose(next_hid_ref[:, there])
        largest = jnp.maximum(jnp.max(jnp.abs(value), axis=1, keepdims=True), 1e-30)
        spread_out[number] = to_codes(value * (TOP_CODE / largest))
        line = jnp.sum(jnp.where(eye, largest, 0.0), axis=0, keepdims=True)
        spread_size_out[number] = jnp.broadcast_to(line * (1.0 / TOP_CODE), (8, rows))
    spread = []
    for away in range(1, 8):
        target = (blk + away) % 8
        for kind, (src, dst) in enumerate(
            ((spread_out, spread_got), (spread_size_out, spread_size_got))
        ):
            spread.append(
                pltpu.make_async_remote_copy(
                    src_ref=src.at[target % 4],
                    dst_ref=dst.at[blk],
                    send_sem=spread_send.at[kind, away - 1],
                    recv_sem=spread_recv.at[kind, away - 1],
                    device_id={"blk": target},
                    device_id_type=MESH,
                )
            )
            spread[-1].start()
    high = col // 2
    my_half = pl.ds(pl.multiple_of(high * part_wide, part_wide), part_wide)
    far_half = pl.ds(pl.multiple_of((1 - high) * part_wide, part_wide), part_wide)
    in_scale = norm_of(4)
    xin[deep:, :] = jnp.zeros((xin.shape[0] - deep, xin.shape[1]), F32)
    xin[0:deep, my_half] = next_in_ref[...] * in_scale
    xin[0:deep, far_half] = (
        0.5 * mom_far_ref[...] + factor * red_far_ref[0:deep, :]
    ) * in_scale
    spread_got[blk] = spread_out[blk % 4]
    spread_size_got[blk] = spread_size_out[blk % 4]
    for copy in spread:
        copy.wait_recv()
    hid_scale = norm_of(1)
    for number in range(8):
        size = jnp.broadcast_to(spread_size_got[number, 0:1, :], (rows, rows))
        size = jnp.transpose(size) * hid_scale
        for lane in range(0, height, 128):
            xs[:, number * height + lane : number * height + lane + 128] = (
                from_codes(spread_got[number, :, lane : lane + 128]) * size
            )

    numbers = {move: number for number, move in enumerate(MOVES)}

    def parts(turn, slot, piece):
        refs = [
            codes.at[turn, slot, pl.ds(top, low - top), pl.ds(left, right - left)]
            for top, low, left, right in PIECES[piece]
        ]
        numbered = [(piece, refs[0])]
        if piece == SIZE_PIECE:
            numbered += [(3, refs[1]), (4, sizes.at[turn, slot])]
        return numbered

    def send(turn, move):
        piece, slot, dim = move
        there = slot | DIM_BITS[dim]
        return [
            pltpu.make_async_remote_copy(
                src_ref=src,
                dst_ref=dst,
                send_sem=send_sems.at[numbers[move], max(number - 2, 0)],
                recv_sem=recv_sems.at[turn, there, number],
                device_id=dims[dim],
                device_id_type=MESH,
            )
            for (number, src), (_, dst) in zip(
                parts(turn, slot, piece), parts(turn, there, piece), strict=True
            )
        ]

    def send_all(turn, moves):
        for move in moves:
            for copy in send(turn, move):
                copy.start()

    def to_core(turn, slot, piece):
        return [
            pltpu.make_async_remote_copy(
                src_ref=src,
                dst_ref=dst,
                send_sem=core_sems.at[slot // 2, number],
                recv_sem=recv_sems.at[turn, slot + 1, number],
                device_id=other_core,
                device_id_type=MESH,
            )
            for (number, src), (_, dst) in zip(
                parts(turn, slot, piece), parts(turn, slot + 1, piece), strict=True
            )
        ]

    def arrived(turn, slot, piece):
        for number, ref in parts(turn, slot, piece):
            pltpu.make_async_remote_copy(
                src_ref=ref,
                dst_ref=ref,
                send_sem=core_sems.at[0, 0],
                recv_sem=recv_sems.at[turn, slot, number],
                device_id=other_core,
                device_id_type=MESH,
            ).wait_recv()

    def forward(turn, moves, on=()):
        for number, (slot, piece) in enumerate(landed(moves)):
            arrived(turn, slot, piece)
            for copy in to_core(turn, slot, piece):
                copy.start()
            if on:
                send_all(turn, on[number : number + 1])

    def gram_copy():
        return pltpu.make_async_remote_copy(
            src_ref=gram,
            dst_ref=gram_got,
            send_sem=pair_send.at[1],
            recv_sem=pair_recv.at[1],
            device_id=other_core,
            device_id_type=MESH,
        )

    def unpack(turn, index, pair, light):
        for core in range(2):
            here = pl.ds(pl.multiple_of(index * 2 * rows + core * rows, rows), rows)
            slot = 2 * pair + core
            if light:
                tops[here, :] = from_codes(codes[turn, slot]).astype(BF16)
            else:
                top, low = halves(from_codes(codes[turn, slot]))
                tops[here, :] = top
                lows[here, :] = low
            size = sizes[turn, slot]
            scales[:, here] = size * size

    def inner(first, count, light):
        here = pl.ds(first, count)
        if light:
            values = dot_nt(lhs[0:rows, :], tops[here, :])
            weights[0:rows, here] = (values * scales[0:1, here]).astype(BF16)
        else:
            both = dot_nt(lhs[...], tops[here, :])
            values = both[:rows] + both[rows:] + dot_nt(lhs[0:rows, :], lows[here, :])
            top, low = halves(values * scales[0:1, here])
            weights[0:rows, here] = top
            weights[rows:, here] = low

    def outer(first, count, out, add, light):
        cut = 512
        here = slice(first, first + count)
        for start in range(0, wide, cut):
            lanes = slice(start, start + cut)
            if light:
                value = dot_nn(weights[0:rows, here], tops[here, lanes])
            else:
                both = dot_nn(weights[:, here], tops[here, lanes])
                value = both[:rows] + both[rows:] + dot_nn(weights[0:rows, here], lows[here, lanes])
            if add:
                value = value + out[:, lanes]
            out[:, lanes] = value

    def set_lhs(values):
        top, low = halves(values)
        lhs[0:rows, :] = top
        lhs[rows:, :] = low

    def input_gram(light):
        top, low = halves(xin[...])
        xin_top[...] = top
        if light:
            gram[...] = dot_nt(xin_top[...], xin_top[...])
        else:
            xin_low[...] = low
            cross = dot_nt(xin_top[...], xin_low[...])
            gram[...] = dot_nt(xin_top[...], xin_top[...]) + (cross + jnp.transpose(cross))
        gram_copy().start()

    def input_step(light):
        gram_copy().wait()
        square_of = gram[...] + gram_got[...]
        top, low = halves(square_of)
        if light:
            poly = NS_B * square_of + NS_C * dot_nn(top, top)
        else:
            cross = dot_nn(top, low)
            poly = NS_B * square_of + NS_C * (dot_nn(top, top) + (cross + jnp.transpose(cross)))
        top, low = halves(poly)
        cut = 512
        for start in range(0, xin.shape[1], cut):
            lanes = slice(start, start + cut)
            change = dot_nn(top, xin_top[:, lanes])
            if not light:
                change = change + dot_nn(low, xin_top[:, lanes]) + dot_nn(top, xin_low[:, lanes])
            xin[:, lanes] = NS_A * xin[:, lanes] + change

    def by_weight(number, limit, work):
        @pl.when(number < limit)
        def _():
            work(True)

        @pl.when(number >= limit)
        def _():
            work(False)

    def iteration(number, carry):
        turn = number % 2
        values = xs[...]
        largest = jnp.maximum(jnp.max(jnp.abs(values), axis=1, keepdims=True), 1e-30)
        codes[turn, 0] = to_codes(values * (TOP_CODE / largest))
        lane_size = jnp.sum(jnp.where(eye, largest, 0.0), axis=0, keepdims=True)
        sizes[turn, 0] = jnp.broadcast_to(lane_size * (1.0 / TOP_CODE), (8, rows))
        send_all(turn, FIRST)
        for piece in range(3):
            for copy in to_core(turn, 0, piece):
                copy.start()
        send_all(turn, SECOND)
        set_lhs(values)

        def first_pass(index, carry):
            pair = index + (index // 3) * (1 - index // 4) - (index // 4) * (1 - index // 5)

            @pl.when(index == 1)
            def _():
                forward(turn, FIRST, SECOND_ON)
                send_all(turn, THIRD)
                send_all(turn, THIRD_A)

                by_weight(number, LIGHT_IN, input_gram)

                forward(turn, SECOND, THIRD_B)
                forward(turn, SECOND_ON, THIRD_C)

                by_weight(number, LIGHT_IN, input_step)

                forward(turn, THIRD)

            @pl.when(index == 4)
            def _():
                forward(turn, THIRD_A)
                forward(turn, THIRD_B)

            @pl.when(index == 7)
            def _():
                forward(turn, THIRD_C)

            for piece in range(3):
                arrived(turn, 2 * pair + 1, piece)

            def work(light):
                unpack(turn, index, pair, light)
                inner(pl.multiple_of(index * 2 * rows, 2 * rows), 2 * rows, light)

            by_weight(number, LIGHT_HID, work)

            @pl.when(index == 3)
            def _():
                by_weight(number, LIGHT_HID, lambda light: outer(0, wide // 2, us, False, light))

            return carry

        lax.fori_loop(0, 8, first_pass, 0)

        def second_pass(light):
            outer(wide // 2, wide // 2, us, True, light)
            set_lhs(us[...])
            for first in range(0, wide, 512):
                inner(first, 512, light)
            outer(0, wide, vs, False, light)

        by_weight(number, LIGHT_HID, second_pass)
        xs[...] = NS_A * xs[...] + NS_B * us[...] + NS_C * vs[...]
        for move in MOVES:
            for copy in send(turn, move):
                copy.wait_send()
        for pair in range(8):
            for piece in range(3):
                for copy in to_core(turn, 2 * pair, piece):
                    copy.wait_send()
        return carry

    lax.fori_loop(0, NS, iteration, 0)

    place = blk % 4
    copies = []
    for rel, target in ((1, dims[0]), (2, dims[2]), (3, diagonal)):
        copies.append(
            pltpu.make_async_remote_copy(
                src_ref=xs.at[:, pl.ds(pl.multiple_of(target["blk"] * height, height), height)],
                dst_ref=back.at[place],
                send_sem=back_send.at[rel - 1],
                recv_sem=back_recv.at[rel - 1],
                device_id=target,
                device_id_type=MESH,
            )
        )
        copies[-1].start()
    back[place] = xs[:, my_lanes]
    inp_ref[...] = xin[0:deep, my_half]
    for copy in copies:
        copy.wait_recv()
    for number in range(4):
        hid_ref[:, number * rows : (number + 1) * rows] = jnp.transpose(back[number])
    for copy in copies + spread + told:
        copy.wait_send()


def muon(stats, red_hid, mom_hid, red_in, mom_in, red_far, mom_far, wide):
    rows = red_hid.shape[0] // 4
    height = red_hid.shape[1]
    deep, part_wide = red_in.shape
    vmem = pl.BlockSpec(memory_space=pltpu.VMEM)
    sem = pltpu.SemaphoreType.DMA
    return pl.pallas_call(
        muon_kernel,
        out_shape=(
            jax.ShapeDtypeStruct(mom_hid.shape, F32),
            jax.ShapeDtypeStruct(mom_in.shape, F32),
            jax.ShapeDtypeStruct(mom_hid.shape, F32),
            jax.ShapeDtypeStruct(mom_in.shape, F32),
            jax.ShapeDtypeStruct((8, 128), F32),
        ),
        in_specs=[vmem] * 7,
        out_specs=(vmem,) * 5,
        scratch_shapes=[
            pltpu.VMEM((2, 16, rows, wide), I16),
            pltpu.VMEM((2, 16, 8, rows), F32),
            pltpu.VMEM((wide, wide), BF16),
            pltpu.VMEM((wide, wide), BF16),
            pltpu.VMEM((8, wide), F32),
            pltpu.VMEM((2 * rows, wide), BF16),
            pltpu.VMEM((rows, wide), F32),
            pltpu.VMEM((rows, wide), F32),
            pltpu.VMEM((rows, wide), F32),
            pltpu.VMEM((2 * rows, wide), BF16),
            pltpu.VMEM((deep, 2 * part_wide), F32),
            pltpu.VMEM((deep, 2 * part_wide), BF16),
            pltpu.VMEM((deep, 2 * part_wide), BF16),
            pltpu.VMEM((deep, deep), F32),
            pltpu.VMEM((deep, deep), F32),
            pltpu.VMEM((4, rows, height), F32),
            pltpu.VMEM((8, 8, 128), F32),
            pltpu.VMEM((4, 8, 128), F32),
            pltpu.VMEM((4, rows, height), I16),
            pltpu.VMEM((8, rows, height), I16),
            pltpu.VMEM((4, 8, rows), F32),
            pltpu.VMEM((8, 8, rows), F32),
            sem((len(MOVES), 3)),
            sem((8, 5)),
            sem((2, 16, 5)),
            sem((3,)),
            sem((3,)),
            sem((10,)),
            sem((10,)),
            sem((2, 7)),
            sem((2, 7)),
            sem((2,)),
            sem((2,)),
        ],
        compiler_params=pltpu.CompilerParams(
            collective_id=0, has_side_effects=True, vmem_limit_bytes=60 * 1024 * 1024
        ),
    )(stats, red_hid, mom_hid, red_in, mom_in, red_far, mom_far)


def finish_kernel(
    scale,
    red_ref,
    w_out_ref,
    first_ref,
    second_ref,
    norm_ref,
    hid_ref,
    w_hid_ref,
    inp_ref,
    w_in_ref,
    res_hid_ref,
    res_in_ref,
    mom_hid_ref,
    mom_in_ref,
    new_out_ref,
    next_first_ref,
    next_second_ref,
    new_hid_ref,
    new_in_ref,
    next_res_hid_ref,
    next_res_in_ref,
    next_mom_hid_ref,
    next_mom_in_ref,
    sems,
):
    step = pl.program_id(0)
    pairs = (
        (res_hid_ref, next_res_hid_ref),
        (res_in_ref, next_res_in_ref),
        (mom_hid_ref, next_mom_hid_ref),
        (mom_in_ref, next_mom_in_ref),
    )
    copies = [
        pltpu.make_async_copy(src, dst, sems.at[number]) for number, (src, dst) in enumerate(pairs)
    ]

    @pl.when(step == 0)
    def _():
        for copy in copies:
            copy.start()
        new_hid_ref[...] = w_hid_ref[...] * (1.0 - LR_MUON * WD_MUON) - scale * hid_ref[...]
        new_in_ref[...] = w_in_ref[...] * (1.0 - LR_MUON * WD_MUON) - scale * inp_ref[...]

    new_out_ref[...], next_first_ref[...], next_second_ref[...] = adam_step(
        w_out_ref[...], norm_ref[4:5, 0:1] * red_ref[...], first_ref[...], second_ref[...]
    )

    @pl.when(step == pl.num_programs(0) - 1)
    def _():
        for copy in copies:
            copy.wait()


def finish(red, w_out, first, second, norms, hid, w_hid, inp, w_in, kept, scale):
    senones, depth = w_out.shape
    rows = OUT_ROWS // 2
    streamed = pl.BlockSpec((rows, depth), lambda step: (step, 0))
    hbm = pl.BlockSpec(memory_space=pl.ANY)

    def whole(array):
        return pl.BlockSpec(array.shape, lambda step: (0, 0))

    small = (norms, hid, w_hid, inp, w_in)
    return pl.pallas_call(
        functools.partial(finish_kernel, scale),
        grid=(2 * OUT_GROUPS,),
        out_shape=tuple(
            jax.ShapeDtypeStruct(array.shape, F32)
            for array in (w_out, w_out, w_out, w_hid, w_in, *kept)
        ),
        in_specs=[streamed] * 4 + [whole(array) for array in small] + [hbm] * 4,
        out_specs=(streamed,) * 3 + (whole(w_hid), whole(w_in)) + (hbm,) * 4,
        scratch_shapes=[pltpu.SemaphoreType.DMA((4,))],
        compiler_params=pltpu.CompilerParams(vmem_limit_bytes=40 * 1024 * 1024),
    )(red, w_out, first, second, *small, *kept)


def plain_body(
    frames,
    labels,
    mask,
    w_input,
    w_hidden,
    w_output,
    biases,
    mom_input,
    mom_hidden,
    out_first,
    out_second,
    bias_first,
    bias_second,
    res_input,
    res_hidden,
    res_output,
):
    ncol = lax.axis_size("col")
    nblk = lax.axis_size("blk")
    col_index = lax.axis_index("col")
    hcol = w_input.shape[1]
    scol = w_output.shape[1]
    micro = frames.shape[0]
    slot_count = frames.shape[1] * micro * nblk * ncol
    bias_row = biases[0]
    b_one = bias_row[:hcol]
    b_two = bias_row[hcol : 2 * hcol]
    b_out = bias_row[2 * hcol :]
    low_input = w_input.astype(jnp.bfloat16)
    row_tags = jnp.where(mask > 0, labels, -1)
    grad_input = jnp.zeros(w_input.shape, jnp.float32)
    grad_hidden = jnp.zeros((w_hidden.shape[0] * nblk, hcol), jnp.float32)
    grad_output = jnp.zeros((w_output.shape[0] * nblk, scol), jnp.float32)
    grad_bias = jnp.zeros(bias_row.shape, jnp.float32)
    loss_local = jnp.zeros((), jnp.float32)
    for micro_step in range(micro):
        low_hidden, low_output = (
            lax.all_gather(w_hidden.astype(jnp.bfloat16), "blk", axis=0, tiled=True),
            lax.all_gather(w_output.astype(jnp.bfloat16), "blk", axis=0, tiled=True),
        )
        inputs = lax.all_gather(frames[micro_step], "col", axis=0, tiled=True)
        tags_group = lax.all_gather(row_tags[micro_step], "col", axis=0, tiled=True)
        sig_one = jax.nn.sigmoid(matmul(inputs, low_input) + b_one)
        h_one = spread_cols(sig_one.astype(jnp.bfloat16))
        sig_two = jax.nn.sigmoid(matmul(h_one, low_hidden) + b_two)
        h_two = spread_cols(sig_two.astype(jnp.bfloat16))
        logits = matmul(h_two, low_output) + b_out
        row_top = lax.pmax(jnp.max(logits, axis=1), "col")
        exponent = jnp.exp(logits - row_top[:, None])
        target_hit = jnp.arange(scol)[None, :] == (tags_group - col_index * scol)[:, None]
        row_total, picked = lax.psum(
            (jnp.sum(exponent, axis=1), jnp.sum(jnp.where(target_hit, logits, 0.0), axis=1)), "col"
        )
        live_rows = tags_group >= 0
        loss_local = loss_local + jnp.sum(
            jnp.where(live_rows, row_top + jnp.log(row_total) - picked, 0.0)
        )
        probs = exponent / row_total[:, None]
        d_logits = (
            jnp.where(live_rows[:, None], probs - target_hit.astype(jnp.float32), 0.0) / slot_count
        ).astype(jnp.bfloat16)
        grad_output = grad_output + inner_rows(h_two, d_logits)
        d_h_two = reduce_cols(outer_cols(d_logits, low_output))
        d_z_two = (d_h_two * sig_two * (1.0 - sig_two)).astype(jnp.bfloat16)
        grad_hidden = grad_hidden + inner_rows(h_one, d_z_two)
        d_h_one = reduce_cols(outer_cols(d_z_two, low_hidden))
        d_z_one = (d_h_one * sig_one * (1.0 - sig_one)).astype(jnp.bfloat16)
        grad_input = grad_input + inner_rows(inputs, d_z_one)
        grad_bias = grad_bias + jnp.concatenate(
            [
                jnp.sum(d_z_one.astype(jnp.float32), axis=0),
                jnp.sum(d_z_two.astype(jnp.float32), axis=0),
                jnp.sum(d_logits.astype(jnp.float32), axis=0),
            ]
        )
    q_input, next_res_input = squash(grad_input, res_input[0])
    q_hidden, next_res_hidden = squash(grad_hidden, res_hidden[0])
    q_output, next_res_output = squash(grad_output, res_output[0])
    red_hidden, red_output = (
        lax.psum_scatter(q_hidden, "blk", scatter_dimension=0, tiled=True),
        lax.psum_scatter(q_output, "blk", scatter_dimension=0, tiled=True),
    )
    red_input, red_bias, loss_sum = lax.psum((q_input, grad_bias, loss_local), "blk")
    share_blk = 1.0 / nblk
    grad_square = (
        share_blk * (jnp.sum(red_input * red_input) + jnp.sum(red_bias * red_bias))
        + jnp.sum(red_hidden * red_hidden)
        + jnp.sum(red_output * red_output)
    )
    clip_norm = jnp.sqrt(lax.psum(grad_square, ("blk", "col")))
    factor = jnp.minimum(1.0, CLIP / clip_norm)
    next_mom_input = 0.5 * mom_input + factor * red_input
    next_mom_hidden = 0.5 * mom_hidden + factor * red_hidden
    square_input, square_hidden = lax.psum(
        (
            share_blk * jnp.sum(next_mom_input * next_mom_input),
            jnp.sum(next_mom_hidden * next_mom_hidden),
        ),
        ("blk", "col"),
    )
    iter_input = next_mom_input / (jnp.sqrt(square_input) + 1e-07)
    iter_hidden = next_mom_hidden / (jnp.sqrt(square_hidden) + 1e-07)
    for turn_index in range(NS):
        rows_hidden = collect_rows(iter_hidden)
        gram_input, gram_hidden = lax.psum(
            (precise(iter_input, iter_input.T), precise(iter_hidden, rows_hidden.T)), "col"
        )
        image_input = precise(gram_input, iter_input)
        image_hidden = precise(gram_hidden, rows_hidden)
        iter_input = (
            NS_A * iter_input + NS_B * image_input + NS_C * precise(gram_input, image_input)
        )
        iter_hidden = (
            NS_A * iter_hidden
            + NS_B * image_hidden
            + NS_C * precise(gram_hidden, collect_rows(image_hidden))
        )
    muon_scale = LR_MUON * 0.2 * math.sqrt(hcol * ncol)
    new_input = w_input * (1.0 - LR_MUON * WD_MUON) - muon_scale * iter_input
    new_hidden = w_hidden * (1.0 - LR_MUON * WD_MUON) - muon_scale * iter_hidden
    new_output, next_out_first, next_out_second = adam_step(
        w_output, factor * red_output, out_first, out_second
    )
    new_biases, next_bias_first, next_bias_second = adam_step(
        biases, factor * red_bias[None, :], bias_first, bias_second
    )
    return (
        loss_sum,
        clip_norm,
        new_input,
        new_hidden,
        new_output,
        new_biases,
        next_mom_input,
        next_mom_hidden,
        next_out_first,
        next_out_second,
        next_bias_first,
        next_bias_second,
        next_res_input[None],
        next_res_hidden[None],
        next_res_output[None],
    )


def fast_body(
    frames,
    labels,
    mask,
    w_input,
    w_hidden,
    w_output,
    biases,
    mom_input,
    mom_hidden,
    out_first,
    out_second,
    bias_first,
    bias_second,
    res_input,
    res_hidden,
    res_output,
):
    ncol = lax.axis_size("col")
    nblk = lax.axis_size("blk")
    col_index = lax.axis_index("col")
    blk_index = lax.axis_index("blk")
    hcol = w_input.shape[1]
    scol = w_output.shape[1]
    micro = frames.shape[0]
    slot_count = frames.shape[1] * micro * nblk * ncol
    bias_row = biases[0]
    deep = w_input.shape[0]
    rows_out = OUT_GROUPS * OUT_ROWS
    inputs, h_one, h_two, slope_one, slope_two, low_hidden, low_output, mom_far, d_logits, vec = (
        forward_pass(
            frames.reshape(-1, deep),
            labels,
            mask,
            w_input,
            w_hidden,
            w_output.T,
            biases,
            mom_input,
            slot_count,
        )
    )
    partial = inner_rows(d_logits, low_output)
    next_out, codes, sizes = squash_out(d_logits, h_two, res_output[0].T)
    next_hid, next_in, red_out, red_hid, red_in, red_far, vec_sum, stats = reduce_grads(
        codes,
        sizes,
        h_one,
        inputs,
        partial,
        slope_two,
        slope_one,
        low_hidden,
        res_hidden[0],
        res_input[0],
        vec,
        scol,
        deep,
    )
    next_res_output = next_out.transpose(1, 2, 0)
    vec_sum = vec_sum.reshape(-1)
    red_bias = vec_sum[: bias_row.shape[0]]
    loss_sum = vec_sum[bias_row.shape[0]]
    done_hidden, done_input, mom_hid_next, mom_in_next, norms = muon(
        stats,
        red_hid,
        mom_hidden,
        red_in,
        mom_input,
        red_far,
        mom_far,
        hcol * ncol,
    )
    clip_norm = norms[0, 0]
    factor = norms[4, 0]
    muon_scale = LR_MUON * 0.2 * math.sqrt(hcol * ncol)
    (
        new_output,
        next_out_first,
        next_out_second,
        new_hidden,
        new_input,
        next_res_hidden,
        next_res_input,
        next_mom_hidden,
        next_mom_input,
    ) = finish(
        red_out,
        w_output.T,
        out_first.T,
        out_second.T,
        norms,
        done_hidden,
        w_hidden,
        done_input,
        w_input,
        (next_hid, next_in, mom_hid_next, mom_in_next),
        muon_scale,
    )
    new_biases, next_bias_first, next_bias_second = adam_step(
        biases, factor * red_bias[None, :], bias_first, bias_second
    )
    return (
        loss_sum,
        clip_norm,
        new_input,
        new_hidden,
        new_output.T,
        new_biases,
        next_mom_input,
        next_mom_hidden,
        next_out_first.T,
        next_out_second.T,
        next_bias_first,
        next_bias_second,
        next_res_input[None],
        next_res_hidden[None],
        next_res_output,
    )


def solution(mesh):
    in_specs = (
        P(None, ("blk", "col"), None),
        P(None, ("blk", "col")),
        P(None, ("blk", "col")),
        P(None, "col"),
        P("blk", "col"),
        P("blk", "col"),
        P("col", None),
        P(None, "col"),
        P("blk", "col"),
        P("blk", "col"),
        P("blk", "col"),
        P("col", None),
        P("col", None),
        P("blk", None, "col"),
        P("blk", None, "col"),
        P("blk", None, "col"),
    )
    out_specs = (
        P(),
        P(),
        P(None, "col"),
        P("blk", "col"),
        P("blk", "col"),
        P("col", None),
        P(None, "col"),
        P("blk", "col"),
        P("blk", "col"),
        P("blk", "col"),
        P("col", None),
        P("col", None),
        P("blk", None, "col"),
        P("blk", None, "col"),
        P("blk", None, "col"),
    )
    cubes = mesh.shape["blk"] == 8 and mesh.shape["col"] == 4
    body = fast_body if cubes else plain_body
    return jax.shard_map(body, mesh=mesh, in_specs=in_specs, out_specs=out_specs, check_vma=False)
```

```python
import functools
import math

import jax
import jax.numpy as jnp
from jax import lax
from jax.experimental import pallas as pl
from jax.experimental.pallas import tpu as pltpu
from jax.sharding import PartitionSpec as P

NS = 5
STEP = 5


NS_A = 3.4445
NS_B = -4.775
NS_C = 2.0315
CLIP = 0.002
LR_MUON = 0.1
WD_MUON = 0.01
LR_ADAM = 0.03
WD_ADAM = 0.1

MESH = pl.DeviceIdType.MESH
F32 = jnp.float32
BF16 = jnp.bfloat16
I16 = jnp.int16
LN2 = math.log(2.0)
TOP_CODE = 32700.0
LEVELS = 64.0


def matmul(left_side, right_side):
    return jnp.dot(left_side, right_side, preferred_element_type=jnp.float32)


def inner_rows(left_side, right_side):
    return lax.dot_general(
        left_side, right_side, (((0,), (0,)), ((), ())), preferred_element_type=jnp.float32
    )


def outer_cols(left_side, right_side):
    return lax.dot_general(
        left_side, right_side, (((1,), (1,)), ((), ())), preferred_element_type=jnp.float32
    )


def precise(left_side, right_side):
    return jnp.dot(
        left_side, right_side, precision=lax.Precision.HIGHEST, preferred_element_type=jnp.float32
    )


def spread_cols(values):
    return lax.all_gather(values, "col", axis=1, tiled=True)


def reduce_cols(values):
    return lax.psum_scatter(values, "col", scatter_dimension=1, tiled=True)


def collect_rows(values):
    return lax.all_gather(values, "blk", axis=0, tiled=True)


def squash(gradient, resid):
    value = gradient + resid.astype(jnp.float32)
    scale = jnp.mean(jnp.abs(value), axis=0, keepdims=True) + 1e-12
    signed = scale * jnp.tanh(2.0 * value / scale)
    return (signed, value - signed)


def adam_step(weight, gradient, first, second):
    first = 0.5 * first + 0.5 * gradient
    second = 0.95 * second + 0.05 * gradient * gradient
    update = first / (1.0 - 0.5**STEP) / (jnp.sqrt(second / (1.0 - 0.95**STEP)) + 1e-08)
    return (weight - LR_ADAM * (update + WD_ADAM * weight), first, second)


def halves(values):
    top = values.astype(BF16)
    return top, (values - top.astype(F32)).astype(BF16)


def dot_nn(left_side, right_side):
    return lax.dot_general(
        left_side, right_side, (((1,), (0,)), ((), ())), preferred_element_type=F32
    )


def dot_nt(left_side, right_side):
    return lax.dot_general(
        left_side, right_side, (((1,), (1,)), ((), ())), preferred_element_type=F32
    )


RING = 8
STEPS = RING - 1
OUT_ROWS = 592
OUT_GROUPS = 4
HID_ROWS = 512
HID_GROUP = 4
IN_GROUP = 5
TURN_AT = 5
CROSS_AT = 6
HID_AT = 13
FINISH_AT = 14
IN_AT = 20
HID_HOP = 3


def ring_place(blk):
    odd = blk % 2
    return (blk // 2) * (1 - odd) + (7 - blk // 2) * odd


def ring_blk(place):
    back = place // 4
    return 2 * place * (1 - back) + (15 - 2 * place) * back


def scale_code(size):
    return jnp.ceil(jnp.log(jnp.maximum(size, 1e-30)) * (LEVELS / LN2))


def code_scale(code):
    return jnp.exp(code * (LN2 / LEVELS))


def to_codes(values):
    return jnp.round(values).astype(jnp.int32).astype(I16)


def from_codes(codes):
    return codes.astype(jnp.int32).astype(F32)


def chunk_of(lane):
    number = lane // 256
    return number // 2 if number % 2 == 0 else 7 - number // 2


def squash_kernel(senones, dl_ref, h_ref, res_ref, next_ref, codes_ref, size_ref, grad, cols, marks):
    group = pl.program_id(0)
    rows, wide = grad.shape
    valid = senones - group * rows
    for first, count in ((0, rows // 32 * 16), (rows // 32 * 16, rows - rows // 32 * 16)):
        there = slice(first, first + count)
        total = jnp.zeros((count, 128), F32)
        for lane in range(0, wide, 512):
            value = dot_nn(dl_ref[there, :], h_ref[:, lane : lane + 512])
            value = value + res_ref[there, lane : lane + 512].astype(F32)
            row = first + lax.broadcasted_iota(jnp.int32, value.shape, 0)
            value = jnp.where(row < valid, value, 0.0)
            grad[there, lane : lane + 512] = value
            value = jnp.abs(value)
            for part in range(0, 512, 128):
                total = total + value[:, part : part + 128]
        size = jnp.sum(total, axis=1, keepdims=True) * (1.0 / wide) + 1e-12
        size = jnp.broadcast_to(size, (count, 128))
        marks[there, :] = size
        cols[0, there, :] = size
        cols[1, there, :] = 2.0 / size

    def some(number, carry):
        row = pl.multiple_of(number * 16, 16)
        size = cols[0, pl.ds(row, 16), :]
        steep = cols[1, pl.ds(row, 16), :]
        for lane in range(0, wide, 128):
            piece = grad[pl.ds(row, 16), lane : lane + 128]
            curve = jnp.tanh(piece * steep)
            codes_ref[0, 2 * chunk_of(lane) + lane // 128 % 2, pl.ds(row, 16), :] = to_codes(
                curve * TOP_CODE
            )
            next_ref[pl.ds(row, 16), 0, lane : lane + 128] = piece - size * curve
        return carry

    lax.fori_loop(0, rows // 16, some, 0)
    marks[rows:, :] = jnp.zeros((marks.shape[0] - rows, 128), F32)
    lines = [jnp.transpose(marks[first : first + 128, :])[0:1, :] for first in range(0, rows, 128)]
    lines.append(jnp.zeros((8 - len(lines), 128), F32))
    size_ref[0] = jnp.concatenate(lines, axis=0)


def squash_out(dl, h_two, res_out):
    senones, wide = res_out.shape
    frames = dl.shape[1]
    return pl.pallas_call(
        functools.partial(squash_kernel, senones),
        grid=(OUT_GROUPS,),
        out_shape=(
            jax.ShapeDtypeStruct((senones, 1, wide), F32),
            jax.ShapeDtypeStruct((OUT_GROUPS, 2 * RING, OUT_ROWS, 128), I16),
            jax.ShapeDtypeStruct((OUT_GROUPS, 8, 128), F32),
        ),
        in_specs=[
            pl.BlockSpec((OUT_ROWS, frames), lambda group: (group, 0)),
            pl.BlockSpec((frames, wide), lambda group: (0, 0)),
            pl.BlockSpec((OUT_ROWS, wide), lambda group: (group, 0)),
        ],
        out_specs=(
            pl.BlockSpec((OUT_ROWS, 1, wide), lambda group: (group, 0, 0)),
            pl.BlockSpec((1, 2 * RING, OUT_ROWS, 128), lambda group: (group, 0, 0, 0)),
            pl.BlockSpec((1, 8, 128), lambda group: (group, 0, 0)),
        ),
        scratch_shapes=[
            pltpu.VMEM((OUT_ROWS, wide), F32),
            pltpu.VMEM((2, OUT_ROWS, 128), F32),
            pltpu.VMEM((640, 128), F32),
        ],
        compiler_params=pltpu.CompilerParams(vmem_limit_bytes=60 * 1024 * 1024),
    )(dl, h_two, res_out)


def reduce_kernel(
    deep,
    senones,
    codes_ref,
    sizes_ref,
    h_one_ref,
    x_ref,
    part_ref,
    slope_two_ref,
    slope_one_ref,
    w_hid_ref,
    res_hid_ref,
    res_in_ref,
    vec_ref,
    next_hid_ref,
    next_in_ref,
    red_out_ref,
    red_hid_ref,
    red_in_ref,
    red_far_ref,
    vec_sum_ref,
    stats_ref,
    grad,
    turned,
    res_buf,
    h_buf,
    slope_buf,
    marks,
    cols,
    keep_sums,
    dz,
    dz_two,
    dz_one,
    core_out,
    core_got,
    far_out,
    far_got,
    own_out,
    got_out,
    own_hid,
    got_hid,
    own_in,
    got_in,
    share_in,
    share_far,
    sizes,
    shares,
    vec,
    vecs,
    res_sems,
    load_sems,
    code_sems,
    slope_sems,
    core_send,
    core_recv,
    far_send,
    far_recv,
    out_send,
    out_recv,
    hid_send,
    hid_recv,
    in_send,
    in_recv,
    share_send,
    share_recv,
    vec_send,
    vec_recv,
    size_send,
    size_recv,
    share_far_send,
    share_far_recv,
):
    blk = lax.axis_index("blk")
    col = lax.axis_index("col")
    here = ring_place(blk)
    core, high = col % 2, col // 2
    cores = {"col": col + 1 - 2 * core}
    across = {"col": (col + 2) % 4}
    barrier = pltpu.get_barrier_semaphore()
    for target in (cores, across, *({"blk": (blk + away) % RING} for away in range(1, RING))):
        pl.semaphore_signal(barrier, inc=1, device_id=target, device_id_type=MESH)

    def code_copy(group):
        return pltpu.make_async_copy(codes_ref.at[group], own_out.at[group], code_sems.at[group])

    def hid_res_copy(part):
        return pltpu.make_async_copy(
            res_hid_ref.at[:, pl.ds(part * 256, 256)],
            res_buf.at[part],
            res_sems.at[part],
        )

    def hid_next_copy(part):
        return pltpu.make_async_copy(
            turned, next_hid_ref.at[:, pl.ds(part * 256, 256)], load_sems.at[1]
        )

    def load(src, dst):
        return pltpu.make_async_copy(src, dst, load_sems.at[0])

    for group in range(OUT_GROUPS):
        code_copy(group).start()
    for part in range(2):
        hid_res_copy(part).start()
    load(h_one_ref, h_buf).start()
    marks[...] = jnp.zeros_like(marks)
    stats_ref[...] = jnp.zeros_like(stats_ref)
    vec[...] = vec_ref[...]
    pl.semaphore_wait(barrier, RING + 1)

    CHUNK = 256
    units = slope_buf.shape[2]

    def slope_copy(layer, block):
        rows = pl.ds(pl.multiple_of(block * CHUNK, CHUNK), CHUNK)
        src = (slope_two_ref, slope_one_ref)[layer]
        return pltpu.make_async_copy(src.at[rows, :], slope_buf.at[block % 2], slope_sems.at[block % 2])

    def core_move(layer, block):
        return pltpu.make_async_remote_copy(
            src_ref=core_out.at[block % 2],
            dst_ref=core_got.at[layer, block],
            send_sem=core_send.at[block % 2],
            recv_sem=core_recv.at[layer, block],
            device_id=cores,
            device_id_type=MESH,
        )

    def far_move(layer, block):
        return pltpu.make_async_remote_copy(
            src_ref=far_out.at[block % 2],
            dst_ref=far_got.at[layer, block],
            send_sem=far_send.at[block % 2],
            recv_sem=far_recv.at[layer, block],
            device_id=across,
            device_id_type=MESH,
        )

    def lanes_of(number):
        return pl.ds(pl.multiple_of(number * units, units), units)

    def rows_at(number):
        return pl.ds(pl.multiple_of(number * 16, 16), 16)

    def free(copy, layer, block):
        @pl.when((layer > 0) | (block >= 2))
        def _():
            copy.wait_send()

    def lane_codes(first):
        return jnp.transpose(marks[first : first + 128, :])[0:1, :]

    def set_factors():
        top = jnp.max(cols[0, 0:CHUNK, :], axis=1, keepdims=True)
        code = scale_code(top)
        marks[0:CHUNK, :] = jnp.broadcast_to(code, (CHUNK, 128))
        cols[1, 0:CHUNK, :] = jnp.broadcast_to(TOP_CODE / code_scale(code), (CHUNK, 128))

    def largest(values):
        return functools.reduce(
            jnp.maximum,
            [
                jnp.abs(value[:, lane : lane + 128])
                for value in values
                for lane in range(0, value.shape[1], 128)
            ],
        )

    def scaled(values, factor):
        return jnp.concatenate(
            [values[:, lane : lane + 128] * factor for lane in range(0, values.shape[1], 128)], axis=1
        )

    def put_scale(out):
        codes = jnp.concatenate(
            [lane_codes(0), lane_codes(128), jnp.zeros((14, 128), F32)], axis=0
        )
        out[CHUNK : CHUNK + 16, 0:128] = codes.astype(jnp.int32).astype(I16)

    def read_scale(got):
        step = code_scale(from_codes(got[CHUNK : CHUNK + 16, 0:128])) * (1.0 / TOP_CODE)
        step = jnp.transpose(jnp.concatenate([step, jnp.zeros((112, 128), F32)], axis=0))
        for up in range(2):
            marks[CHUNK + up * 128 : CHUNK + (up + 1) * 128, :] = jnp.broadcast_to(
                step[:, up : up + 1], (128, 128)
            )

    def step_at(number):
        return marks[pl.ds(pl.multiple_of(CHUNK + number * 16, 16), 16), :]

    def split(layer, block):
        free(core_move(layer, block), layer, block)

        def measure(number, carry):
            rows = rows_at(number)
            cols[0, rows, :] = largest(
                [grad[rows, lanes_of(2 * half + 1 - core)] for half in range(2)]
            )
            return carry

        lax.fori_loop(0, CHUNK // 16, measure, 0)
        set_factors()

        def write(number, carry):
            rows = rows_at(number)
            factor = cols[1, rows, :]
            for half in range(2):
                there = slice(half * units, (half + 1) * units)
                core_out[block % 2, rows, there] = to_codes(
                    scaled(grad[rows, lanes_of(2 * half + 1 - core)], factor)
                )
                keep_sums[block, rows, there] = grad[rows, lanes_of(2 * half + core)]
            return carry

        lax.fori_loop(0, CHUNK // 16, write, 0)
        put_scale(core_out.at[block % 2])
        core_move(layer, block).start()

    def cross(layer, block):
        core_move(layer, block).wait_recv()
        free(far_move(layer, block), layer, block)
        got = core_got.at[layer, block]
        read_scale(got)

        def add(number, carry):
            rows = rows_at(number)
            near, away = lanes_of(high), lanes_of(1 - high)
            step = step_at(number)
            keep_sums[block, rows, near] += scaled(from_codes(got[rows, near]), step)
            value = keep_sums[block, rows, away] + scaled(from_codes(got[rows, away]), step)
            keep_sums[block, rows, away] = value
            cols[0, rows, :] = largest([value])
            return carry

        lax.fori_loop(0, CHUNK // 16, add, 0)
        set_factors()

        def write(number, carry):
            rows = rows_at(number)
            far_out[block % 2, rows, :] = to_codes(
                scaled(keep_sums[block, rows, lanes_of(1 - high)], cols[1, rows, :])
            )
            return carry

        lax.fori_loop(0, CHUNK // 16, write, 0)
        put_scale(far_out.at[block % 2])
        far_move(layer, block).start()

    def finish(layer, block):
        far_move(layer, block).wait_recv()
        slope_copy(layer, block).wait()
        got = far_got.at[layer, block]
        read_scale(got)

        def one(number, total):
            rows = rows_at(number)
            value = keep_sums[block, rows, lanes_of(high)] + scaled(
                from_codes(got[rows, :]), step_at(number)
            )
            value = (value * slope_buf[block % 2, rows, :]).astype(BF16)
            dz[rows, :] = value
            return total + value.astype(F32)

        total = lax.fori_loop(0, CHUNK // 16, one, jnp.zeros((16, units), F32))
        if layer == 0:

            @pl.when(block < 2)
            def _():
                slope_copy(0, block + 2).start()

            @pl.when(block >= 2)
            def _():
                slope_copy(1, block - 2).start()

        else:

            @pl.when(block < 2)
            def _():
                slope_copy(1, block + 2).start()

        total = jnp.sum(total, axis=0, keepdims=True)
        for number in range(units // 128):
            row = 4 * (1 - layer) + number
            vec[row : row + 1, :] += total[:, number * 128 : (number + 1) * 128]
        flipped = (dz_two, dz_one)[layer]
        for up in range(CHUNK // 128):
            there = pl.ds(pl.multiple_of(block * CHUNK + up * 128, 128), 128)
            for number in range(units // 128):
                tile = dz[up * 128 : (up + 1) * 128, number * 128 : (number + 1) * 128]
                flipped[number * 128 : (number + 1) * 128, there] = jnp.transpose(
                    tile.astype(F32)
                ).astype(BF16)

    def blocks(first, last, work):
        def one(block, carry):
            work(block)
            return carry

        lax.fori_loop(first, last, one, 0)

    def start_block(block):
        rows = pl.ds(pl.multiple_of(block * CHUNK, CHUNK), CHUNK)
        copy = pltpu.make_async_copy(part_ref.at[rows, :], grad.at[pl.ds(0, CHUNK), :], load_sems.at[1])
        copy.start()
        copy.wait()
        split(0, block)

    def turn_block(block):
        finish(0, block)
        for lane in range(0, grad.shape[1], 512):
            grad[0:CHUNK, lane : lane + 512] = dot_nt(dz[...], w_hid_ref[lane : lane + 512, :])
        split(1, block)

    core_out[:, CHUNK:, :] = jnp.zeros((2, 16, 2 * units), I16)
    far_out[:, CHUNK:, :] = jnp.zeros((2, 16, units), I16)
    slope_copy(0, 0).start()
    slope_copy(0, 1).start()
    def vec_copy(away):
        return pltpu.make_async_remote_copy(
            src_ref=vec,
            dst_ref=vecs.at[blk],
            send_sem=vec_send.at[away - 1],
            recv_sem=vec_recv.at[away - 1],
            device_id={"blk": (blk + away) % RING},
            device_id_type=MESH,
        )

    def set_rows(count, first_own, size):
        size = jnp.broadcast_to(size, (count, 128))
        marks[first_own : first_own + count, :] = size
        cols[0, 0:count, :] = size
        cols[1, 0:count, :] = 2.0 / size

    def tell_sizes(group):
        for away in range(1, RING):
            size_copy(group, away).start()

    def size_copy(group, away):
        return pltpu.make_async_remote_copy(
            src_ref=sizes.at[group, here],
            dst_ref=sizes.at[group, here],
            send_sem=size_send.at[group, away - 1],
            recv_sem=size_recv.at[group, away - 1],
            device_id={"blk": ring_blk((here + away) % RING)},
            device_id_type=MESH,
        )

    def set_sizes(rows, group):
        parts = [lane_codes(first) for first in range(0, rows, 128)]
        parts.append(jnp.zeros((8 - len(parts), 128), F32))
        sizes[group, here] = jnp.concatenate(parts, axis=0)
        tell_sizes(group)

    def make_shares(group, row_of):
        for away in range(1, RING):
            size_copy(group, away).wait_recv()
        for way in range(2):
            tiles = []
            for step in range(STEPS):
                mine = row_of(here, step, way)
                came = mine * 0.0
                for back in range(step + 1):
                    came = came + row_of((here - 1 - back + (2 + 2 * back) * way + RING) % RING, step, way)
                if step < STEPS - 1:
                    whole = 1.0 / jnp.maximum(came + mine, 1e-30)
                else:
                    whole = 1.0 / TOP_CODE
                tiles += [came * whole, mine * whole]
            tiles.append(jnp.zeros((16, 128), F32))
            shares[group, way] = jnp.transpose(jnp.concatenate(tiles, axis=0))

    def hid_group():
        load(h_one_ref, h_buf).wait()
        wide = grad.shape[1]
        for part in range(2):
            first = part * 256
            hid_res_copy(part).wait()
            total = jnp.zeros((256, 128), F32)
            for lane in range(0, wide, 512):
                value = dot_nn(dz_two[first : first + 256, :], h_buf[:, lane : lane + 512])
                value = value + jnp.transpose(res_buf[part, lane : lane + 512, :].astype(F32))
                grad[:, lane : lane + 512] = value
                value = jnp.abs(value)
                for more in range(0, 512, 128):
                    total = total + value[:, more : more + 128]
            set_rows(
                256, first, jnp.sum(total, axis=1, keepdims=True) * (1.0 / wide) + 1e-12
            )

            def some(number, carry, first=first):
                row = pl.multiple_of(number * 16, 16)
                size = cols[0, pl.ds(row, 16), :]
                steep = cols[1, pl.ds(row, 16), :]
                for lane in range(0, wide, 128):
                    piece = grad[pl.ds(row, 16), lane : lane + 128]
                    curve = jnp.tanh(piece * steep)
                    own_hid[2 * chunk_of(lane) + lane // 128 % 2, pl.ds(first + row, 16), :] = (
                        to_codes(curve * TOP_CODE)
                    )
                    grad[pl.ds(row, 16), lane : lane + 128] = piece - size * curve
                return carry

            lax.fori_loop(0, 16, some, 0)
            if part:
                hid_next_copy(part - 1).wait()
            for lane in range(0, wide, 128):
                turned[lane : lane + 128, :] = jnp.transpose(grad[:, lane : lane + 128])
            hid_next_copy(part).start()
        load(x_ref, h_buf.at[:, pl.ds(0, x_ref.shape[1])]).start()
        set_sizes(HID_ROWS, HID_GROUP)
        hid_next_copy(1).wait()

    def in_group():
        wide = x_ref.shape[1]
        load(x_ref, h_buf.at[:, pl.ds(0, wide)]).wait()
        for top in range(0, wide, 128):
            count = min(128, deep - top)
            for left in range(0, HID_ROWS, 128):
                tile = res_in_ref[top : top + count, left : left + 128].astype(F32)
                if count < 128:
                    tile = jnp.concatenate([tile, jnp.zeros((128 - count, 128), F32)], axis=0)
                place, lane = top // 256 * HID_ROWS + left, top % 256
                turned[place : place + 128, lane : lane + 128] = jnp.transpose(tile)
        for first in range(0, HID_ROWS, 256):
            grad[0:256, 0:wide] = dot_nn(dz_one[first : first + 256, :], h_buf[:, 0:wide])

            def add(number, carry, first=first):
                row = pl.multiple_of(number * 16, 16)
                place = pl.multiple_of(first + row, 16)
                value = grad[pl.ds(row, 16), 0:wide] + jnp.concatenate(
                    [turned[pl.ds(place, 16), :], turned[pl.ds(HID_ROWS + place, 16), :]], axis=1
                )
                grad[pl.ds(row, 16), 0:wide] = value
                value = jnp.abs(value)
                cols[0, pl.ds(row, 16), :] = functools.reduce(
                    jnp.add, [value[:, lane : lane + 128] for lane in range(0, wide, 128)]
                )
                return carry

            lax.fori_loop(0, 16, add, 0)
            set_rows(
                256,
                first,
                jnp.sum(cols[0, 0:256, :], axis=1, keepdims=True) * (1.0 / deep) + 1e-12,
            )

            def some(number, carry, first=first):
                row = pl.multiple_of(number * 16, 16)
                place = pl.multiple_of(first + row, 16)
                size = cols[0, pl.ds(row, 16), :]
                steep = cols[1, pl.ds(row, 16), :]
                chunk = first // 64 + number // 4
                inside = pl.multiple_of(number % 4 * 16, 16)
                for lane in range(0, wide, 128):
                    piece = grad[pl.ds(row, 16), lane : lane + 128]
                    curve = jnp.tanh(piece * steep)
                    turned[
                        pl.ds(lane // 256 * HID_ROWS + place, 16), lane % 256 : lane % 256 + 128
                    ] = piece - size * curve
                    own_in[
                        2 * chunk + lane // 256, pl.ds(inside, 16), lane % 256 : lane % 256 + 128
                    ] = to_codes(curve * TOP_CODE)
                return carry

            lax.fori_loop(0, 16, some, 0)
        for top in range(0, wide, 128):
            count = min(128, deep - top)
            for left in range(0, HID_ROWS, 128):
                place, lane = top // 256 * HID_ROWS + left, top % 256
                tile = jnp.transpose(turned[place : place + 128, lane : lane + 128])
                next_in_ref[top : top + count, left : left + 128] = tile[0:count, :]
        sizes[IN_GROUP, here] = jnp.concatenate(
            [lane_codes(64 * chunk) for chunk in range(RING)], axis=0
        )
        tell_sizes(IN_GROUP)

    def towards(way):
        return {"blk": ring_blk((here + 1 - 2 * way + RING) % RING)}

    def move(src, got, step, way, send_sem, recv_sem):
        return pltpu.make_async_remote_copy(
            src_ref=src,
            dst_ref=got.at[way, step],
            send_sem=send_sem.at[way, step],
            recv_sem=recv_sem.at[way, step],
            device_id=towards(way),
            device_id_type=MESH,
        )

    def first_moves(own, got, send_sem, recv_sem):
        for way in range(2):
            chunk = (here - 1 + 2 * way + RING) % RING
            move(own.at[2 * chunk + way], got, 0, way, send_sem, recv_sem).start()

    def hop(rows, own, got, group, step, send_sem, recv_sem, keep):
        for way in range(2):
            move(got.at[way, step], got, step, way, send_sem, recv_sem).wait_recv()

        def add(way, result):
            message = got.at[way, step]
            ahead = here - 2 - step + way * (4 + 2 * step) + 2 * RING
            mine = own.at[2 * (ahead % RING) + way]
            share = pltpu.roll(shares[group, way], (128 - 16 * step) % 128, 1)
            for number, first in enumerate(range(0, rows, 128)):
                count = min(128, rows - first)
                there = slice(first, first + count)
                result(
                    first,
                    count,
                    from_codes(message[there, :]) * share[0:count, number : number + 1]
                    + from_codes(mine[there, :]) * share[0:count, 8 + number : 9 + number],
                )

        @pl.when(step < STEPS - 1)
        def _():
            for way in range(2):

                def write(first, count, value, way=way):
                    got[way, step, first : first + count, :] = to_codes(value)

                add(way, write)
            for way in range(2):
                move(got.at[way, step], got, step + 1, way, send_sem, recv_sem).start()

        @pl.when(step == STEPS - 1)
        def _():
            for way in range(2):

                def finish_rows(first, count, value, way=way):
                    keep(way, first, count, value)
                    square = jnp.sum(value * value, axis=0, keepdims=True)
                    for lane in range(0, value.shape[1], 128):
                        stats_ref[0:1, :] += square[:, lane : lane + 128]

                add(way, finish_rows)

    def out_hop(group, step):
        def keep(way, first, count, value):
            row = pl.multiple_of(group * OUT_ROWS + first, 16)
            red_out_ref[pl.ds(row, count), way * 128 : (way + 1) * 128] = value

        hop(
            OUT_ROWS,
            own_out.at[group],
            got_out.at[group],
            group,
            step,
            out_send.at[group],
            out_recv.at[group],
            keep,
        )

    def hid_hop(step):
        def keep(way, first, count, value):
            red_hid_ref[first : first + count, way * 128 : (way + 1) * 128] = value

        hop(HID_ROWS, own_hid, got_hid, HID_GROUP, step, hid_send, hid_recv, keep)

    def share_move(step, way):
        place = (here - step + 2 * step * way + 2 * RING) % RING
        return pltpu.make_async_remote_copy(
            src_ref=share_in.at[way, place],
            dst_ref=share_in.at[way, place],
            send_sem=share_send.at[way, step],
            recv_sem=share_recv.at[way, step],
            device_id=towards(way),
            device_id_type=MESH,
        )

    def share_across(way, place):
        return pltpu.make_async_remote_copy(
            src_ref=share_in.at[way, place],
            dst_ref=share_far.at[way, place],
            send_sem=share_far_send.at[way, place],
            recv_sem=share_far_recv.at[way, place],
            device_id=across,
            device_id_type=MESH,
        )

    def in_hop(step):
        def keep(way, first, count, value):
            share_in[way, here] = value

        hop(64, own_in, got_in, IN_GROUP, step, in_send, in_recv, keep)

        @pl.when(step == STEPS - 1)
        def _():
            for way in range(2):
                share_move(0, way).start()
                share_across(way, here).start()

    def share_hop(step):
        for way in range(2):
            share_move(step, way).wait_recv()
            share_across(way, (here - 1 - step + (2 + 2 * step) * way + RING) % RING).start()

        @pl.when(step < STEPS - 1)
        def _():
            for way in range(2):
                share_move(step + 1, way).start()

    def in_step(index):
        @pl.when((index >= 0) & (index < STEPS))
        def _():
            in_hop(index)

        @pl.when((index >= STEPS) & (index < 2 * STEPS))
        def _():
            share_hop(index - STEPS)

    def chunk_row(place, step, way):
        chunk = (here - 2 - step + way * (4 + 2 * step) + 2 * RING) % RING
        line = sizes[IN_GROUP, place, pl.ds(chunk, 1), :]
        return jnp.broadcast_to(line, (8, 128))

    for group in range(OUT_GROUPS):
        sizes[group, here] = sizes_ref[group]
        tell_sizes(group)
        code_copy(group).wait()
        first_moves(own_out.at[group], got_out.at[group], out_send.at[group], out_recv.at[group])
    blocks(0, 4, start_block)

    def each(number, first, spacing, count, work):
        after = number - first

        @pl.when((after >= 0) & (after < spacing * count) & (after % spacing == 0))
        def _():
            work(after // spacing)

    def turn(number, carry):
        @pl.when(number < OUT_GROUPS)
        def _():
            make_shares(number, lambda place, step, way: sizes[number, place])

        @pl.when(number < OUT_GROUPS * STEPS)
        def _():
            out_hop(number % OUT_GROUPS, number // OUT_GROUPS)

        @pl.when(number == HID_AT + HID_HOP)
        def _():
            make_shares(HID_GROUP, lambda place, step, way: sizes[HID_GROUP, place])

        each(number, HID_AT + HID_HOP, HID_HOP, STEPS, hid_hop)

        @pl.when(number == IN_AT + 1)
        def _():
            make_shares(IN_GROUP, chunk_row)

        in_step(number - IN_AT - 1)
        each(number, 0, 1, 4, lambda block: cross(0, block))
        each(number, TURN_AT, 2, 4, turn_block)
        each(number, CROSS_AT, 2, 4, lambda block: cross(1, block))

        @pl.when(number == HID_AT)
        def _():
            hid_group()
            first_moves(own_hid, got_hid, hid_send, hid_recv)

        each(number, FINISH_AT, 2, 4, lambda block: finish(1, block))

        @pl.when(number == IN_AT)
        def _():
            in_group()
            first_moves(own_in, got_in, in_send, in_recv)
            for away in range(1, RING):
                vec_copy(away).start()

        return carry

    turns = max(IN_AT + 1 + 2 * STEPS, HID_AT + HID_HOP * STEPS + 1, OUT_GROUPS * STEPS)
    lax.fori_loop(0, turns, turn, 0)

    def unfold(shares_of, out):
        for place in range(0, RING, 2):
            for way in range(2):
                for lane in range(0, 256, 128):
                    tile = jnp.concatenate(
                        [shares_of[way, place + more, :, lane : lane + 128] for more in range(2)],
                        axis=0,
                    )
                    first = way * 256 + lane
                    out[first : first + 128, place * 64 : place * 64 + 128] = jnp.transpose(tile)

    unfold(share_in, red_in_ref)
    for place in range(RING):
        for way in range(2):
            share_across(way, place).wait_recv()
    unfold(share_far, red_far_ref)
    for away in range(1, RING):
        vec_copy(away).wait_recv()
    vecs[blk] = vec[...]
    total = vecs[0]
    for number in range(1, RING):
        total = total + vecs[number]
    vec_sum_ref[...] = total
    flat = 128 * lax.broadcasted_iota(jnp.int32, total.shape, 0) + lax.broadcasted_iota(
        jnp.int32, total.shape, 1
    )
    total = jnp.where(flat < 2 * units + senones, total, 0.0)
    stats_ref[1:2, :] = jnp.sum(total * total, axis=0, keepdims=True) * (1.0 / RING)
    for away in range(1, RING):
        vec_copy(away).wait_send()
        for group in range(OUT_GROUPS + 2):
            size_copy(group, away).wait_send()
    for slot in range(2):
        core_move(1, 2 + slot).wait_send()
        far_move(1, 2 + slot).wait_send()
    for way in range(2):
        for step in range(STEPS):
            for group in range(OUT_GROUPS):
                move(
                    got_out.at[group, way, step],
                    got_out.at[group],
                    step,
                    way,
                    out_send.at[group],
                    out_recv.at[group],
                ).wait_send()
            move(got_hid.at[way, step], got_hid, step, way, hid_send, hid_recv).wait_send()
            move(got_in.at[way, step], got_in, step, way, in_send, in_recv).wait_send()
            share_move(step, way).wait_send()
        for place in range(RING):
            share_across(way, place).wait_send()


def reduce_grads(
    codes, sizes, h_one, x, part, slope_two, slope_one, w_hid, res_hid, res_in, vec, senones, deep
):
    frames, wide = h_one.shape
    in_wide = x.shape[1]
    units = w_hid.shape[1]
    vmem = pl.BlockSpec(memory_space=pltpu.VMEM)
    hbm = pl.BlockSpec(memory_space=pl.ANY)
    message = OUT_ROWS
    hid_message = HID_ROWS
    in_message = 64
    sem = pltpu.SemaphoreType.DMA
    return pl.pallas_call(
        functools.partial(reduce_kernel, deep, senones),
        out_shape=(
            jax.ShapeDtypeStruct((wide, HID_ROWS), F32),
            jax.ShapeDtypeStruct(res_in.shape, F32),
            jax.ShapeDtypeStruct((OUT_GROUPS * OUT_ROWS, 256), F32),
            jax.ShapeDtypeStruct((HID_ROWS, 256), F32),
            jax.ShapeDtypeStruct((in_wide, HID_ROWS), F32),
            jax.ShapeDtypeStruct((in_wide, HID_ROWS), F32),
            jax.ShapeDtypeStruct(vec.shape, F32),
            jax.ShapeDtypeStruct((8, 128), F32),
        ),
        in_specs=[hbm, vmem] + [hbm] * 5 + [vmem, hbm, vmem, vmem],
        out_specs=(hbm,) + (vmem,) * 7,
        scratch_shapes=[
            pltpu.VMEM((256, wide), F32),
            pltpu.VMEM((wide, 256), F32),
            pltpu.VMEM((2, wide, 256), BF16),
            pltpu.VMEM((frames, wide), BF16),
            pltpu.VMEM((2, 256, units), F32),
            pltpu.VMEM((640, 128), F32),
            pltpu.VMEM((2, 256, 128), F32),
            pltpu.VMEM((4, 256, 2 * units), F32),
            pltpu.VMEM((256, units), BF16),
            pltpu.VMEM((units, frames), BF16),
            pltpu.VMEM((units, frames), BF16),
            pltpu.VMEM((2, 272, 2 * units), I16),
            pltpu.VMEM((2, 4, 272, 2 * units), I16),
            pltpu.VMEM((2, 272, units), I16),
            pltpu.VMEM((2, 4, 272, units), I16),
            pltpu.VMEM((OUT_GROUPS, 2 * RING, message, 128), I16),
            pltpu.VMEM((OUT_GROUPS, 2, STEPS, message, 128), I16),
            pltpu.VMEM((2 * RING, hid_message, 128), I16),
            pltpu.VMEM((2, STEPS, hid_message, 128), I16),
            pltpu.VMEM((2 * RING, in_message, 256), I16),
            pltpu.VMEM((2, STEPS, in_message, 256), I16),
            pltpu.VMEM((2, RING, 64, 256), F32),
            pltpu.VMEM((2, RING, 64, 256), F32),
            pltpu.VMEM((OUT_GROUPS + 2, RING, 8, 128), F32),
            pltpu.VMEM((OUT_GROUPS + 2, 2, 128, 128), F32),
            pltpu.VMEM(vec.shape, F32),
            pltpu.VMEM((RING,) + vec.shape, F32),
            sem((2,)),
            sem((2,)),
            sem((OUT_GROUPS,)),
            sem((2,)),
            sem((2,)),
            sem((2, 4)),
            sem((2,)),
            sem((2, 4)),
            sem((OUT_GROUPS, 2, STEPS)),
            sem((OUT_GROUPS, 2, STEPS)),
            sem((2, STEPS)),
            sem((2, STEPS)),
            sem((2, STEPS)),
            sem((2, STEPS)),
            sem((2, STEPS)),
            sem((2, STEPS)),
            sem((STEPS,)),
            sem((STEPS,)),
            sem((OUT_GROUPS + 2, STEPS)),
            sem((OUT_GROUPS + 2, STEPS)),
            sem((2, RING)),
            sem((2, RING)),
        ],
        compiler_params=pltpu.CompilerParams(
            collective_id=1, has_side_effects=True, vmem_limit_bytes=63 * 1024 * 1024
        ),
    )(codes, sizes, h_one, x, part, slope_two, slope_one, w_hid, res_hid, res_in, vec)


RING_STARTS = (0, 0, 5, 6, 7)
LAYER_TWO_WAVE = 7
LOGIT_WAVES = (11, 12, 13, 14)


def forward_kernel(
    slot_count,
    x_ref,
    labels_ref,
    mask_ref,
    w_in_ref,
    w_hid_ref,
    w_out_ref,
    bias_ref,
    mom_ref,
    x_out,
    h_one_out,
    h_two_out,
    slope_one_out,
    slope_two_out,
    w_hid_out,
    w_out_out,
    mom_far_ref,
    dl_ref,
    vec_ref,
    x_all,
    h_one,
    h_two,
    slope_one,
    slope_two,
    w_in,
    w_hid,
    w_out,
    curve,
    bias_line,
    bias_col,
    tags,
    sums,
    ring_send,
    ring_recv,
    x_send,
    x_recv,
    h_send,
    h_recv,
    tag_send,
    tag_recv,
    sum_send,
    sum_recv,
    out_sems,
    mom_sems,
):
    blk = lax.axis_index("blk")
    col = lax.axis_index("col")
    here = ring_place(blk)
    senones, depth = w_out_ref.shape
    own_rows, deep = x_ref.shape
    units = w_hid_ref.shape[1]
    frames = x_all.shape[0]
    cores = {"col": col + 1 - 2 * (col % 2)}
    across = {"col": (col + 2) % 4}
    corner = {"col": (col + 2) % 4 + 1 - 2 * (col % 2)}
    others = (cores, across, corner)

    barrier = pltpu.get_barrier_semaphore()
    for target in others + tuple({"blk": ring_blk((here + way) % RING)} for way in (1, 7)):
        pl.semaphore_signal(barrier, inc=1, device_id=target, device_id_type=MESH)

    w_hid[pl.ds(pl.multiple_of(blk * depth, depth), depth), :] = w_hid_ref[...].astype(BF16)
    own_lanes = pl.ds(pl.multiple_of(blk * depth, depth), depth)
    w_out[senones // 16 * 16 :, own_lanes] = jnp.zeros(
        (w_out.shape[0] - senones // 16 * 16, depth), BF16
    )
    w_out[0:senones, own_lanes] = w_out_ref[...].astype(BF16)
    own_frames = pl.ds(pl.multiple_of(col * own_rows, own_rows), own_rows)
    x_all[own_frames, :] = jnp.zeros((own_rows, x_all.shape[1]), BF16)
    x_all[own_frames, 0:deep] = x_ref[...]
    own_tags = jnp.where(mask_ref[...] > 0, labels_ref[...], -1)
    own_tags = jnp.concatenate([own_tags[row : row + 1, :] for row in range(own_tags.shape[0])], axis=1)
    tags[col] = jnp.broadcast_to(own_tags, (8, own_rows))
    bias_line[...] = jnp.zeros_like(bias_line)
    bias_line[:, 0 : bias_ref.shape[1]] = bias_ref[...]
    sums[...] = jnp.zeros_like(sums)
    pl.semaphore_wait(barrier, 5)

    def ring_part(group, origin, way):
        start = pl.multiple_of(origin * depth + way * 128, 128)
        if group == 0:
            return w_hid.at[pl.ds(start, 128), :]
        return w_out.at[pl.ds((group - 1) * OUT_ROWS, OUT_ROWS), pl.ds(start, 128)]

    def ring_move(group, step, way):
        origin = ring_blk((here - step + 2 * step * way + RING) % RING)
        part = ring_part(group, origin, way)
        return pltpu.make_async_remote_copy(
            src_ref=part,
            dst_ref=part,
            send_sem=ring_send.at[group, way, step],
            recv_sem=ring_recv.at[group, way, step],
            device_id={"blk": ring_blk((here + 1 - 2 * way + RING) % RING)},
            device_id_type=MESH,
        )

    def ring_wave(wave):
        for group, start in enumerate(RING_STARTS):
            step = wave - 1 - start
            for way in range(2):
                if step == -1:
                    ring_move(group, 0, way).start()
                if 0 <= step < STEPS:
                    ring_move(group, step, way).wait_recv()
                    if step < STEPS - 1:
                        ring_move(group, step + 1, way).start()

    def copy_to(target, src, send_sem, recv_sem):
        return pltpu.make_async_remote_copy(
            src_ref=src,
            dst_ref=src,
            send_sem=send_sem,
            recv_sem=recv_sem,
            device_id=target,
            device_id_type=MESH,
        )

    def rows_of(owner):
        return pl.ds(pl.multiple_of(owner * own_rows, own_rows), own_rows)

    def lanes_of(owner):
        return pl.ds(pl.multiple_of(owner * units, units), units)

    def x_move(number):
        owner = across["col"] if number == 2 else col
        target = across if number == 1 else cores
        return copy_to(target, x_all.at[rows_of(owner), :], x_send.at[number], x_recv.at[number])

    def h_move(layer, number, block):
        owner = across["col"] if number == 2 else col
        target = across if number == 1 else cores
        whole = (h_one, h_two)[layer]
        part = whole.at[pl.ds(block * own_rows, own_rows), lanes_of(owner)]
        return copy_to(
            target, part, h_send.at[layer, number, block], h_recv.at[layer, number, block]
        )

    def h_start(layer, block):
        h_move(layer, 0, block).start()
        h_move(layer, 1, block).start()

    def h_forward(layer, block):
        h_move(layer, 1, block).wait_recv()
        h_move(layer, 2, block).start()

    def h_ready(layer, block):
        h_move(layer, 0, block).wait_recv()
        h_move(layer, 2, block).wait_recv()

    ring_wave(0)
    x_move(0).start()
    x_move(1).start()
    tag_copies = [
        copy_to(target, tags.at[col], tag_send.at[number], tag_recv.at[number])
        for number, target in enumerate(others)
    ]
    for copy in tag_copies:
        copy.start()
    w_in[...] = jnp.zeros_like(w_in)
    w_in[0:deep, :] = w_in_ref[...].astype(BF16)
    for number in range(bias_col.shape[0] // 128):
        first = 2 * units + number * 128
        line = jnp.broadcast_to(bias_line[:, first : first + 128], (128, 128))
        bias_col[number * 128 : (number + 1) * 128, :] = jnp.transpose(line)
    ring_wave(1)
    x_move(1).wait_recv()
    x_move(2).start()
    x_move(0).wait_recv()
    x_move(2).wait_recv()

    def layer(number, block, inputs, weights, whole, slopes):
        there = slice(block * own_rows, (block + 1) * own_rows)
        value = jax.nn.sigmoid(
            dot_nn(inputs[there, :], weights[...])
            + bias_line[:, number * units : (number + 1) * units]
        )
        slopes[there, :] = value * (1.0 - value)
        whole[there, lanes_of(col)] = value.astype(BF16)
        h_start(number, block)

    outs = []

    def put(src, dst):
        copy = pltpu.make_async_copy(src, dst, out_sems.at[len(outs)])
        copy.start()
        outs.append(copy)

    for block in range(4):
        layer(0, block, x_all, w_in, h_one, slope_one)
    put(x_all, x_out)
    put(slope_one, slope_one_out)

    def all_tags():
        return jnp.concatenate([tags[owner, 0:1, :] for owner in range(4)], axis=1)

    def own_row(line):
        line = line - col * senones
        return jnp.where(line < senones, line, -1)

    def logits(group):
        first = group * OUT_ROWS
        half = frames // 2
        for part in range(2):
            curve[first : first + OUT_ROWS, part * half : (part + 1) * half] = dot_nt(
                w_out[first : first + OUT_ROWS, :], h_two[part * half : (part + 1) * half, :]
            )
        base = lax.broadcasted_iota(jnp.int32, (16, frames), 0)

        def largest(number, top):
            row = pl.multiple_of(first + number * 16, 16)
            value = curve[pl.ds(row, 16), :] + bias_col[pl.ds(row, 16), 0:1]
            if group == OUT_GROUPS - 1:
                value = jnp.where(base + row < senones, value, -1e30)
            curve[pl.ds(row, 16), :] = value
            return jnp.maximum(top, value)

        top = lax.fori_loop(0, OUT_ROWS // 16, largest, jnp.full((16, frames), -1e30, F32))
        top = jnp.max(top, axis=0, keepdims=True)
        line = jnp.broadcast_to(own_row(all_tags()), (16, frames))

        def exponents(number, carry):
            total, picked = carry
            row = pl.multiple_of(first + number * 16, 16)
            value = curve[pl.ds(row, 16), :]
            power = jnp.exp(value - top)
            curve[pl.ds(row, 16), :] = power
            return total + power, picked + jnp.where(base + row == line, value, 0.0)

        blank = jnp.zeros((16, frames), F32)
        total, picked = lax.fori_loop(0, OUT_ROWS // 16, exponents, (blank, blank))
        sums[col, group : group + 1, :] = top
        sums[col, 4 + group : 5 + group, :] = jnp.sum(total, axis=0, keepdims=True)
        sums[col, 8 + group : 9 + group, :] = jnp.sum(picked, axis=0, keepdims=True)

    mom_copy = pltpu.make_async_remote_copy(
        src_ref=mom_ref,
        dst_ref=mom_far_ref,
        send_sem=mom_sems.at[0],
        recv_sem=mom_sems.at[1],
        device_id=across,
        device_id_type=MESH,
    )
    last_wave = RING_STARTS[-1] + STEPS
    for wave in range(2, last_wave + 1):
        ring_wave(wave)
        if 2 <= wave < 6:
            h_forward(0, wave - 2)
        if wave == LAYER_TWO_WAVE:
            for block in range(4):
                h_ready(0, block)
                layer(1, block, h_one, w_hid, h_two, slope_two)
            put(h_one, h_one_out)
            put(slope_two, slope_two_out)
            put(w_hid, w_hid_out)
        if LAYER_TWO_WAVE < wave <= LAYER_TWO_WAVE + 4:
            h_forward(1, wave - LAYER_TWO_WAVE - 1)
        for group, when in enumerate(LOGIT_WAVES):
            if wave == when:
                if group == 0:
                    for block in range(4):
                        h_ready(1, block)
                    put(h_two, h_two_out)
                    mom_copy.start()
                    for copy in tag_copies:
                        copy.wait_recv()
                rows = pl.ds(group * OUT_ROWS, OUT_ROWS)
                put(w_out.at[rows, :], w_out_out.at[rows, :])
                logits(group)

    sum_copies = [
        copy_to(target, sums.at[col], sum_send.at[number], sum_recv.at[number])
        for number, target in enumerate(others)
    ]
    for copy in sum_copies:
        copy.start()
    for copy in sum_copies:
        copy.wait_recv()

    def lines(first):
        return [sums[owner, first + group : first + group + 1, :] for owner in range(4) for group in range(4)]

    tops = lines(0)
    top = functools.reduce(jnp.maximum, tops)
    total = functools.reduce(
        jnp.add, [size * jnp.exp(own - top) for own, size in zip(tops, lines(4), strict=True)]
    )
    picked = functools.reduce(jnp.add, lines(8))
    line = all_tags()
    live = line >= 0
    loss = jnp.where(live, top + jnp.log(total) - picked, 0.0)
    loss = jnp.sum(loss, axis=1, keepdims=True)
    weight = jnp.where(live, 1.0 / slot_count, 0.0)
    line = jnp.broadcast_to(own_row(line), (16, frames))
    hit_weight = jnp.broadcast_to(weight, (16, frames))
    base = lax.broadcasted_iota(jnp.int32, (16, frames), 0)
    bias_col[...] = jnp.zeros_like(bias_col)
    for group in range(OUT_GROUPS):
        share = jnp.exp(sums[col, group : group + 1, :] - top) / total * weight

        def gradient(number, carry, first=group * OUT_ROWS, share=share):
            row = pl.multiple_of(first + number * 16, 16)
            value = curve[pl.ds(row, 16), :] * share - jnp.where(base + row == line, hit_weight, 0.0)
            value = value.astype(BF16)
            dl_ref[pl.ds(row, 16), :] = value
            value = value.astype(F32)
            bias_col[pl.ds(row, 16), :] = functools.reduce(
                jnp.add, [value[:, lane : lane + 128] for lane in range(0, frames, 128)]
            )
            return carry

        lax.fori_loop(0, OUT_ROWS // 16, gradient, 0)
    vec_ref[...] = jnp.zeros_like(vec_ref)
    row = 2 * units // 128
    for number in range(bias_col.shape[0] // 128):
        line = jnp.transpose(bias_col[number * 128 : (number + 1) * 128, :])
        line = jnp.sum(line, axis=0, keepdims=True)
        place = 128 * number + lax.broadcasted_iota(jnp.int32, line.shape, 1)
        line = jnp.where(place < senones, line, jnp.where(place == senones, loss, 0.0))
        vec_ref[row + number : row + number + 1, :] = line

    for group in range(len(RING_STARTS)):
        for way in range(2):
            for step in range(STEPS):
                ring_move(group, step, way).wait_send()
    for number in range(3):
        x_move(number).wait_send()
        for block in range(4):
            h_move(0, number, block).wait_send()
            h_move(1, number, block).wait_send()
    for copy in tag_copies + sum_copies:
        copy.wait_send()
    mom_copy.wait()
    for copy in outs:
        copy.wait()


def forward_pass(x, labels, mask, w_in, w_hid, w_out, bias, mom, slot_count):
    own_rows = x.shape[0]
    units = w_hid.shape[1]
    frames = 4 * own_rows
    wide = 4 * units
    rows = OUT_GROUPS * OUT_ROWS
    blocks = -(-rows // 128)
    vmem = pl.BlockSpec(memory_space=pltpu.VMEM)
    hbm = pl.BlockSpec(memory_space=pl.ANY)
    sem = pltpu.SemaphoreType.DMA
    kept = (
        ((frames, 512), BF16),
        ((frames, wide), BF16),
        ((frames, wide), BF16),
        ((frames, units), F32),
        ((frames, units), F32),
        ((wide, units), BF16),
        ((rows, wide), BF16),
    )
    return pl.pallas_call(
        functools.partial(forward_kernel, slot_count),
        out_shape=tuple(jax.ShapeDtypeStruct(shape, kind) for shape, kind in kept)
        + (
            jax.ShapeDtypeStruct(mom.shape, F32),
            jax.ShapeDtypeStruct((rows, frames), BF16),
            jax.ShapeDtypeStruct((32, 128), F32),
        ),
        in_specs=[vmem] * 7 + [hbm],
        out_specs=(hbm,) * 8 + (vmem,) * 2,
        scratch_shapes=[pltpu.VMEM(shape, kind) for shape, kind in kept[:5]]
        + [
            pltpu.VMEM((512, units), BF16),
            pltpu.VMEM((wide, units), BF16),
            pltpu.VMEM((rows, wide), BF16),
            pltpu.VMEM((rows, frames), F32),
            pltpu.VMEM((1, 2 * units + blocks * 128), F32),
            pltpu.VMEM((blocks * 128, 128), F32),
            pltpu.VMEM((4, 8, own_rows), jnp.int32),
            pltpu.VMEM((4, 16, frames), F32),
            sem((5, 2, STEPS)),
            sem((5, 2, STEPS)),
            sem((3,)),
            sem((3,)),
            sem((2, 3, 4)),
            sem((2, 3, 4)),
            sem((3,)),
            sem((3,)),
            sem((3,)),
            sem((3,)),
            sem((16,)),
            sem((2,)),
        ],
        compiler_params=pltpu.CompilerParams(
            collective_id=2, has_side_effects=True, vmem_limit_bytes=60 * 1024 * 1024
        ),
    )(x, labels, mask, w_in, w_hid, w_out, bias, mom)


DIM_BITS = (2, 4, 8)
ORDERS = ((0, 1, 2), (1, 2, 0), (2, 0, 1))
PIECES = (
    ((0, 48, 0, 1792),),
    ((48, 96, 0, 1792),),
    ((96, 128, 0, 2048), (0, 96, 1792, 2048)),
)
SIZE_PIECE = 2
LIGHT_HID = 3
LIGHT_IN = 2


def stage_sends(stage, sources):
    moves = []
    for piece, order in enumerate(ORDERS):
        slot = sum(DIM_BITS[order[index]] for index in sources)
        moves.append((piece, slot, order[stage]))
    return moves


def landed(moves):
    return [(slot | DIM_BITS[dim], piece) for piece, slot, dim in moves]


FIRST = stage_sends(0, ())
SECOND = stage_sends(1, ())
SECOND_ON = stage_sends(1, (0,))
THIRD = stage_sends(2, ())
THIRD_A = stage_sends(2, (0,))
THIRD_B = stage_sends(2, (1,))
THIRD_C = stage_sends(2, (0, 1))
MOVES = FIRST + SECOND + SECOND_ON + THIRD + THIRD_A + THIRD_B + THIRD_C


def muon_kernel(
    stats_ref,
    red_hid_ref,
    mom_hid_ref,
    red_in_ref,
    mom_in_ref,
    red_far_ref,
    mom_far_ref,
    hid_ref,
    inp_ref,
    next_hid_ref,
    next_in_ref,
    norm_ref,
    codes,
    sizes,
    tops,
    lows,
    scales,
    weights,
    xs,
    us,
    vs,
    lhs,
    xin,
    xin_top,
    xin_low,
    gram,
    gram_got,
    back,
    sums,
    sums_got,
    spread_out,
    spread_got,
    spread_size_out,
    spread_size_got,
    send_sems,
    core_sems,
    recv_sems,
    back_send,
    back_recv,
    sums_send,
    sums_recv,
    spread_send,
    spread_recv,
    pair_send,
    pair_recv,
):
    blk = lax.axis_index("blk")
    col = lax.axis_index("col")
    rows, wide = xs.shape
    height = back.shape[2]
    deep = mom_in_ref.shape[0]
    part_wide = inp_ref.shape[1]
    other_core = {"col": col + 1 - 2 * (col % 2)}
    dims = (
        {"blk": blk + 1 - 2 * (blk % 2)},
        {"col": (col + 2) % 4},
        {"blk": blk + 2 - 4 * ((blk // 2) % 2)},
    )
    diagonal = {"blk": 4 * (blk // 4) + 3 - blk % 4}
    barrier = pltpu.get_barrier_semaphore()
    corner = {"col": (col + 2) % 4 + 1 - 2 * (col % 2)}
    cols = (other_core, dims[1], corner)
    for target in (*cols, *({"blk": (blk + away) % 8} for away in range(1, 8))):
        pl.semaphore_signal(barrier, inc=1, device_id=target, device_id_type=MESH)

    def fold(values):
        line = jnp.sum(values, axis=0, keepdims=True)
        return sum(line[:, lane : lane + 128] for lane in range(0, line.shape[1], 128))

    share = 0.125
    sums[blk, 0:1, :] = fold(stats_ref[...])
    sums[blk, 1:2, :] = fold(mom_hid_ref[...] * mom_hid_ref[...])
    red_hid = jnp.transpose(red_hid_ref[...])
    sums[blk, 2:3, :] = fold(mom_hid_ref[...] * red_hid)
    sums[blk, 3:4, :] = fold(red_hid_ref[...] * red_hid_ref[...])
    sums[blk, 4:5, :] = fold(mom_in_ref[...] * mom_in_ref[...]) * share
    sums[blk, 5:6, :] = fold(mom_in_ref[...] * red_in_ref[0:deep, :]) * share
    sums[blk, 6:7, :] = fold(red_in_ref[0:deep, :] * red_in_ref[0:deep, :]) * share
    sums[blk, 7:8, :] = jnp.zeros((1, 128), F32)
    eye = lax.broadcasted_iota(jnp.int32, (rows, rows), 0) == lax.broadcasted_iota(
        jnp.int32, (rows, rows), 1
    )
    pl.semaphore_wait(barrier, 10)

    def tell(own, targets, first):
        copies = []
        for number, target in enumerate(targets, start=first):
            copies.append(
                pltpu.make_async_remote_copy(
                    src_ref=own,
                    dst_ref=own,
                    send_sem=sums_send.at[number],
                    recv_sem=sums_recv.at[number],
                    device_id=target,
                    device_id_type=MESH,
                )
            )
            copies[-1].start()
        for copy in copies:
            copy.wait_recv()
        return copies

    told = tell(sums.at[blk], [{"blk": (blk + away) % 8} for away in range(1, 8)], 0)
    sums_got[col] = functools.reduce(jnp.add, [sums[number] for number in range(8)])
    told += tell(sums_got.at[col], cols, 7)
    whole = functools.reduce(jnp.add, [sums_got[number] for number in range(4)])
    whole = jnp.sum(whole, axis=1, keepdims=True)
    clip = jnp.sqrt(whole[0:1])
    factor = jnp.minimum(1.0, CLIP / clip)

    def norm_of(first):
        square = (
            0.25 * whole[first : first + 1]
            + factor * whole[first + 1 : first + 2]
            + factor * factor * whole[first + 2 : first + 3]
        )
        return 1.0 / (jnp.sqrt(jnp.maximum(square, 0.0)) + 1e-07)

    norm_ref[0:4, :] = jnp.broadcast_to(clip, (4, 128))
    norm_ref[4:8, :] = jnp.broadcast_to(factor, (4, 128))
    next_hid_ref[...] = 0.5 * mom_hid_ref[...] + factor * jnp.transpose(red_hid_ref[...])
    next_in_ref[...] = 0.5 * mom_in_ref[...] + factor * red_in_ref[0:deep, :]

    my_lanes = pl.ds(pl.multiple_of(blk * height, height), height)
    for number in range(4):
        there = slice(number * rows, (number + 1) * rows)
        value = jnp.transpose(next_hid_ref[:, there])
        largest = jnp.maximum(jnp.max(jnp.abs(value), axis=1, keepdims=True), 1e-30)
        spread_out[number] = to_codes(value * (TOP_CODE / largest))
        line = jnp.sum(jnp.where(eye, largest, 0.0), axis=0, keepdims=True)
        spread_size_out[number] = jnp.broadcast_to(line * (1.0 / TOP_CODE), (8, rows))
    spread = []
    for away in range(1, 8):
        target = (blk + away) % 8
        for kind, (src, dst) in enumerate(
            ((spread_out, spread_got), (spread_size_out, spread_size_got))
        ):
            spread.append(
                pltpu.make_async_remote_copy(
                    src_ref=src.at[target % 4],
                    dst_ref=dst.at[blk],
                    send_sem=spread_send.at[kind, away - 1],
                    recv_sem=spread_recv.at[kind, away - 1],
                    device_id={"blk": target},
                    device_id_type=MESH,
                )
            )
            spread[-1].start()
    high = col // 2
    my_half = pl.ds(pl.multiple_of(high * part_wide, part_wide), part_wide)
    far_half = pl.ds(pl.multiple_of((1 - high) * part_wide, part_wide), part_wide)
    in_scale = norm_of(4)
    xin[deep:, :] = jnp.zeros((xin.shape[0] - deep, xin.shape[1]), F32)
    xin[0:deep, my_half] = next_in_ref[...] * in_scale
    xin[0:deep, far_half] = (
        0.5 * mom_far_ref[...] + factor * red_far_ref[0:deep, :]
    ) * in_scale
    spread_got[blk] = spread_out[blk % 4]
    spread_size_got[blk] = spread_size_out[blk % 4]
    for copy in spread:
        copy.wait_recv()
    hid_scale = norm_of(1)
    for number in range(8):
        size = jnp.broadcast_to(spread_size_got[number, 0:1, :], (rows, rows))
        size = jnp.transpose(size) * hid_scale
        for lane in range(0, height, 128):
            xs[:, number * height + lane : number * height + lane + 128] = (
                from_codes(spread_got[number, :, lane : lane + 128]) * size
            )

    numbers = {move: number for number, move in enumerate(MOVES)}

    def parts(turn, slot, piece):
        refs = [
            codes.at[turn, slot, pl.ds(top, low - top), pl.ds(left, right - left)]
            for top, low, left, right in PIECES[piece]
        ]
        numbered = [(piece, refs[0])]
        if piece == SIZE_PIECE:
            numbered += [(3, refs[1]), (4, sizes.at[turn, slot])]
        return numbered

    def send(turn, move):
        piece, slot, dim = move
        there = slot | DIM_BITS[dim]
        return [
            pltpu.make_async_remote_copy(
                src_ref=src,
                dst_ref=dst,
                send_sem=send_sems.at[numbers[move], max(number - 2, 0)],
                recv_sem=recv_sems.at[turn, there, number],
                device_id=dims[dim],
                device_id_type=MESH,
            )
            for (number, src), (_, dst) in zip(
                parts(turn, slot, piece), parts(turn, there, piece), strict=True
            )
        ]

    def send_all(turn, moves):
        for move in moves:
            for copy in send(turn, move):
                copy.start()

    def to_core(turn, slot, piece):
        return [
            pltpu.make_async_remote_copy(
                src_ref=src,
                dst_ref=dst,
                send_sem=core_sems.at[slot // 2, number],
                recv_sem=recv_sems.at[turn, slot + 1, number],
                device_id=other_core,
                device_id_type=MESH,
            )
            for (number, src), (_, dst) in zip(
                parts(turn, slot, piece), parts(turn, slot + 1, piece), strict=True
            )
        ]

    def arrived(turn, slot, piece):
        for number, ref in parts(turn, slot, piece):
            pltpu.make_async_remote_copy(
                src_ref=ref,
                dst_ref=ref,
                send_sem=core_sems.at[0, 0],
                recv_sem=recv_sems.at[turn, slot, number],
                device_id=other_core,
                device_id_type=MESH,
            ).wait_recv()

    def forward(turn, moves, on=()):
        for number, (slot, piece) in enumerate(landed(moves)):
            arrived(turn, slot, piece)
            for copy in to_core(turn, slot, piece):
                copy.start()
            if on:
                send_all(turn, on[number : number + 1])

    def gram_copy():
        return pltpu.make_async_remote_copy(
            src_ref=gram,
            dst_ref=gram_got,
            send_sem=pair_send.at[1],
            recv_sem=pair_recv.at[1],
            device_id=other_core,
            device_id_type=MESH,
        )

    def unpack(turn, index, pair, light):
        for core in range(2):
            here = pl.ds(pl.multiple_of(index * 2 * rows + core * rows, rows), rows)
            slot = 2 * pair + core
            if light:
                tops[here, :] = from_codes(codes[turn, slot]).astype(BF16)
            else:
                top, low = halves(from_codes(codes[turn, slot]))
                tops[here, :] = top
                lows[here, :] = low
            size = sizes[turn, slot]
            scales[:, here] = size * size

    def inner(first, count, light):
        here = pl.ds(first, count)
        if light:
            values = dot_nt(lhs[0:rows, :], tops[here, :])
            weights[0:rows, here] = (values * scales[0:1, here]).astype(BF16)
        else:
            both = dot_nt(lhs[...], tops[here, :])
            values = both[:rows] + both[rows:] + dot_nt(lhs[0:rows, :], lows[here, :])
            top, low = halves(values * scales[0:1, here])
            weights[0:rows, here] = top
            weights[rows:, here] = low

    def outer(first, count, out, add, light):
        cut = 512
        here = slice(first, first + count)
        for start in range(0, wide, cut):
            lanes = slice(start, start + cut)
            if light:
                value = dot_nn(weights[0:rows, here], tops[here, lanes])
            else:
                both = dot_nn(weights[:, here], tops[here, lanes])
                value = both[:rows] + both[rows:] + dot_nn(weights[0:rows, here], lows[here, lanes])
            if add:
                value = value + out[:, lanes]
            out[:, lanes] = value

    def set_lhs(values):
        top, low = halves(values)
        lhs[0:rows, :] = top
        lhs[rows:, :] = low

    def input_gram(light):
        top, low = halves(xin[...])
        xin_top[...] = top
        if light:
            gram[...] = dot_nt(xin_top[...], xin_top[...])
        else:
            xin_low[...] = low
            cross = dot_nt(xin_top[...], xin_low[...])
            gram[...] = dot_nt(xin_top[...], xin_top[...]) + (cross + jnp.transpose(cross))
        gram_copy().start()

    def input_step(light):
        gram_copy().wait()
        square_of = gram[...] + gram_got[...]
        top, low = halves(square_of)
        if light:
            poly = NS_B * square_of + NS_C * dot_nn(top, top)
        else:
            cross = dot_nn(top, low)
            poly = NS_B * square_of + NS_C * (dot_nn(top, top) + (cross + jnp.transpose(cross)))
        top, low = halves(poly)
        cut = 512
        for start in range(0, xin.shape[1], cut):
            lanes = slice(start, start + cut)
            change = dot_nn(top, xin_top[:, lanes])
            if not light:
                change = change + dot_nn(low, xin_top[:, lanes]) + dot_nn(top, xin_low[:, lanes])
            xin[:, lanes] = NS_A * xin[:, lanes] + change

    def by_weight(number, limit, work):
        @pl.when(number < limit)
        def _():
            work(True)

        @pl.when(number >= limit)
        def _():
            work(False)

    def iteration(number, carry):
        turn = number % 2
        values = xs[...]
        largest = jnp.maximum(jnp.max(jnp.abs(values), axis=1, keepdims=True), 1e-30)
        codes[turn, 0] = to_codes(values * (TOP_CODE / largest))
        lane_size = jnp.sum(jnp.where(eye, largest, 0.0), axis=0, keepdims=True)
        sizes[turn, 0] = jnp.broadcast_to(lane_size * (1.0 / TOP_CODE), (8, rows))
        send_all(turn, FIRST)
        for piece in range(3):
            for copy in to_core(turn, 0, piece):
                copy.start()
        send_all(turn, SECOND)
        set_lhs(values)

        def first_pass(index, carry):
            pair = index + (index // 3) * (1 - index // 4) - (index // 4) * (1 - index // 5)

            @pl.when(index == 1)
            def _():
                forward(turn, FIRST, SECOND_ON)
                send_all(turn, THIRD)
                send_all(turn, THIRD_A)

                by_weight(number, LIGHT_IN, input_gram)

                forward(turn, SECOND, THIRD_B)
                forward(turn, SECOND_ON, THIRD_C)

                by_weight(number, LIGHT_IN, input_step)

                forward(turn, THIRD)

            @pl.when(index == 4)
            def _():
                forward(turn, THIRD_A)
                forward(turn, THIRD_B)

            @pl.when(index == 7)
            def _():
                forward(turn, THIRD_C)

            for piece in range(3):
                arrived(turn, 2 * pair + 1, piece)

            def work(light):
                unpack(turn, index, pair, light)
                inner(pl.multiple_of(index * 2 * rows, 2 * rows), 2 * rows, light)

            by_weight(number, LIGHT_HID, work)

            @pl.when(index == 3)
            def _():
                by_weight(number, LIGHT_HID, lambda light: outer(0, wide // 2, us, False, light))

            return carry

        lax.fori_loop(0, 8, first_pass, 0)

        def second_pass(light):
            outer(wide // 2, wide // 2, us, True, light)
            set_lhs(us[...])
            for first in range(0, wide, 512):
                inner(first, 512, light)
            outer(0, wide, vs, False, light)

        by_weight(number, LIGHT_HID, second_pass)
        xs[...] = NS_A * xs[...] + NS_B * us[...] + NS_C * vs[...]
        for move in MOVES:
            for copy in send(turn, move):
                copy.wait_send()
        for pair in range(8):
            for piece in range(3):
                for copy in to_core(turn, 2 * pair, piece):
                    copy.wait_send()
        return carry

    lax.fori_loop(0, NS, iteration, 0)

    place = blk % 4
    copies = []
    for rel, target in ((1, dims[0]), (2, dims[2]), (3, diagonal)):
        copies.append(
            pltpu.make_async_remote_copy(
                src_ref=xs.at[:, pl.ds(pl.multiple_of(target["blk"] * height, height), height)],
                dst_ref=back.at[place],
                send_sem=back_send.at[rel - 1],
                recv_sem=back_recv.at[rel - 1],
                device_id=target,
                device_id_type=MESH,
            )
        )
        copies[-1].start()
    back[place] = xs[:, my_lanes]
    inp_ref[...] = xin[0:deep, my_half]
    for copy in copies:
        copy.wait_recv()
    for number in range(4):
        hid_ref[:, number * rows : (number + 1) * rows] = jnp.transpose(back[number])
    for copy in copies + spread + told:
        copy.wait_send()


def muon(stats, red_hid, mom_hid, red_in, mom_in, red_far, mom_far, wide):
    rows = red_hid.shape[0] // 4
    height = red_hid.shape[1]
    deep, part_wide = red_in.shape
    vmem = pl.BlockSpec(memory_space=pltpu.VMEM)
    sem = pltpu.SemaphoreType.DMA
    return pl.pallas_call(
        muon_kernel,
        out_shape=(
            jax.ShapeDtypeStruct(mom_hid.shape, F32),
            jax.ShapeDtypeStruct(mom_in.shape, F32),
            jax.ShapeDtypeStruct(mom_hid.shape, F32),
            jax.ShapeDtypeStruct(mom_in.shape, F32),
            jax.ShapeDtypeStruct((8, 128), F32),
        ),
        in_specs=[vmem] * 7,
        out_specs=(vmem,) * 5,
        scratch_shapes=[
            pltpu.VMEM((2, 16, rows, wide), I16),
            pltpu.VMEM((2, 16, 8, rows), F32),
            pltpu.VMEM((wide, wide), BF16),
            pltpu.VMEM((wide, wide), BF16),
            pltpu.VMEM((8, wide), F32),
            pltpu.VMEM((2 * rows, wide), BF16),
            pltpu.VMEM((rows, wide), F32),
            pltpu.VMEM((rows, wide), F32),
            pltpu.VMEM((rows, wide), F32),
            pltpu.VMEM((2 * rows, wide), BF16),
            pltpu.VMEM((deep, 2 * part_wide), F32),
            pltpu.VMEM((deep, 2 * part_wide), BF16),
            pltpu.VMEM((deep, 2 * part_wide), BF16),
            pltpu.VMEM((deep, deep), F32),
            pltpu.VMEM((deep, deep), F32),
            pltpu.VMEM((4, rows, height), F32),
            pltpu.VMEM((8, 8, 128), F32),
            pltpu.VMEM((4, 8, 128), F32),
            pltpu.VMEM((4, rows, height), I16),
            pltpu.VMEM((8, rows, height), I16),
            pltpu.VMEM((4, 8, rows), F32),
            pltpu.VMEM((8, 8, rows), F32),
            sem((len(MOVES), 3)),
            sem((8, 5)),
            sem((2, 16, 5)),
            sem((3,)),
            sem((3,)),
            sem((10,)),
            sem((10,)),
            sem((2, 7)),
            sem((2, 7)),
            sem((2,)),
            sem((2,)),
        ],
        compiler_params=pltpu.CompilerParams(
            collective_id=0, has_side_effects=True, vmem_limit_bytes=60 * 1024 * 1024
        ),
    )(stats, red_hid, mom_hid, red_in, mom_in, red_far, mom_far)


def plain_body(
    frames,
    labels,
    mask,
    w_input,
    w_hidden,
    w_output,
    biases,
    mom_input,
    mom_hidden,
    out_first,
    out_second,
    bias_first,
    bias_second,
    res_input,
    res_hidden,
    res_output,
):
    ncol = lax.axis_size("col")
    nblk = lax.axis_size("blk")
    col_index = lax.axis_index("col")
    hcol = w_input.shape[1]
    scol = w_output.shape[1]
    micro = frames.shape[0]
    slot_count = frames.shape[1] * micro * nblk * ncol
    bias_row = biases[0]
    b_one = bias_row[:hcol]
    b_two = bias_row[hcol : 2 * hcol]
    b_out = bias_row[2 * hcol :]
    low_input = w_input.astype(jnp.bfloat16)
    row_tags = jnp.where(mask > 0, labels, -1)
    grad_input = jnp.zeros(w_input.shape, jnp.float32)
    grad_hidden = jnp.zeros((w_hidden.shape[0] * nblk, hcol), jnp.float32)
    grad_output = jnp.zeros((w_output.shape[0] * nblk, scol), jnp.float32)
    grad_bias = jnp.zeros(bias_row.shape, jnp.float32)
    loss_local = jnp.zeros((), jnp.float32)
    for micro_step in range(micro):
        low_hidden, low_output = (
            lax.all_gather(w_hidden.astype(jnp.bfloat16), "blk", axis=0, tiled=True),
            lax.all_gather(w_output.astype(jnp.bfloat16), "blk", axis=0, tiled=True),
        )
        inputs = lax.all_gather(frames[micro_step], "col", axis=0, tiled=True)
        tags_group = lax.all_gather(row_tags[micro_step], "col", axis=0, tiled=True)
        sig_one = jax.nn.sigmoid(matmul(inputs, low_input) + b_one)
        h_one = spread_cols(sig_one.astype(jnp.bfloat16))
        sig_two = jax.nn.sigmoid(matmul(h_one, low_hidden) + b_two)
        h_two = spread_cols(sig_two.astype(jnp.bfloat16))
        logits = matmul(h_two, low_output) + b_out
        row_top = lax.pmax(jnp.max(logits, axis=1), "col")
        exponent = jnp.exp(logits - row_top[:, None])
        target_hit = jnp.arange(scol)[None, :] == (tags_group - col_index * scol)[:, None]
        row_total, picked = lax.psum(
            (jnp.sum(exponent, axis=1), jnp.sum(jnp.where(target_hit, logits, 0.0), axis=1)), "col"
        )
        live_rows = tags_group >= 0
        loss_local = loss_local + jnp.sum(
            jnp.where(live_rows, row_top + jnp.log(row_total) - picked, 0.0)
        )
        probs = exponent / row_total[:, None]
        d_logits = (
            jnp.where(live_rows[:, None], probs - target_hit.astype(jnp.float32), 0.0) / slot_count
        ).astype(jnp.bfloat16)
        grad_output = grad_output + inner_rows(h_two, d_logits)
        d_h_two = reduce_cols(outer_cols(d_logits, low_output))
        d_z_two = (d_h_two * sig_two * (1.0 - sig_two)).astype(jnp.bfloat16)
        grad_hidden = grad_hidden + inner_rows(h_one, d_z_two)
        d_h_one = reduce_cols(outer_cols(d_z_two, low_hidden))
        d_z_one = (d_h_one * sig_one * (1.0 - sig_one)).astype(jnp.bfloat16)
        grad_input = grad_input + inner_rows(inputs, d_z_one)
        grad_bias = grad_bias + jnp.concatenate(
            [
                jnp.sum(d_z_one.astype(jnp.float32), axis=0),
                jnp.sum(d_z_two.astype(jnp.float32), axis=0),
                jnp.sum(d_logits.astype(jnp.float32), axis=0),
            ]
        )
    q_input, next_res_input = squash(grad_input, res_input[0])
    q_hidden, next_res_hidden = squash(grad_hidden, res_hidden[0])
    q_output, next_res_output = squash(grad_output, res_output[0])
    red_hidden, red_output = (
        lax.psum_scatter(q_hidden, "blk", scatter_dimension=0, tiled=True),
        lax.psum_scatter(q_output, "blk", scatter_dimension=0, tiled=True),
    )
    red_input, red_bias, loss_sum = lax.psum((q_input, grad_bias, loss_local), "blk")
    share_blk = 1.0 / nblk
    grad_square = (
        share_blk * (jnp.sum(red_input * red_input) + jnp.sum(red_bias * red_bias))
        + jnp.sum(red_hidden * red_hidden)
        + jnp.sum(red_output * red_output)
    )
    clip_norm = jnp.sqrt(lax.psum(grad_square, ("blk", "col")))
    factor = jnp.minimum(1.0, CLIP / clip_norm)
    next_mom_input = 0.5 * mom_input + factor * red_input
    next_mom_hidden = 0.5 * mom_hidden + factor * red_hidden
    square_input, square_hidden = lax.psum(
        (
            share_blk * jnp.sum(next_mom_input * next_mom_input),
            jnp.sum(next_mom_hidden * next_mom_hidden),
        ),
        ("blk", "col"),
    )
    iter_input = next_mom_input / (jnp.sqrt(square_input) + 1e-07)
    iter_hidden = next_mom_hidden / (jnp.sqrt(square_hidden) + 1e-07)
    for turn_index in range(NS):
        rows_hidden = collect_rows(iter_hidden)
        gram_input, gram_hidden = lax.psum(
            (precise(iter_input, iter_input.T), precise(iter_hidden, rows_hidden.T)), "col"
        )
        image_input = precise(gram_input, iter_input)
        image_hidden = precise(gram_hidden, rows_hidden)
        iter_input = (
            NS_A * iter_input + NS_B * image_input + NS_C * precise(gram_input, image_input)
        )
        iter_hidden = (
            NS_A * iter_hidden
            + NS_B * image_hidden
            + NS_C * precise(gram_hidden, collect_rows(image_hidden))
        )
    muon_scale = LR_MUON * 0.2 * math.sqrt(hcol * ncol)
    new_input = w_input * (1.0 - LR_MUON * WD_MUON) - muon_scale * iter_input
    new_hidden = w_hidden * (1.0 - LR_MUON * WD_MUON) - muon_scale * iter_hidden
    new_output, next_out_first, next_out_second = adam_step(
        w_output, factor * red_output, out_first, out_second
    )
    new_biases, next_bias_first, next_bias_second = adam_step(
        biases, factor * red_bias[None, :], bias_first, bias_second
    )
    return (
        loss_sum,
        clip_norm,
        new_input,
        new_hidden,
        new_output,
        new_biases,
        next_mom_input,
        next_mom_hidden,
        next_out_first,
        next_out_second,
        next_bias_first,
        next_bias_second,
        next_res_input[None],
        next_res_hidden[None],
        next_res_output[None],
    )


def fast_body(
    frames,
    labels,
    mask,
    w_input,
    w_hidden,
    w_output,
    biases,
    mom_input,
    mom_hidden,
    out_first,
    out_second,
    bias_first,
    bias_second,
    res_input,
    res_hidden,
    res_output,
):
    ncol = lax.axis_size("col")
    nblk = lax.axis_size("blk")
    col_index = lax.axis_index("col")
    blk_index = lax.axis_index("blk")
    hcol = w_input.shape[1]
    scol = w_output.shape[1]
    micro = frames.shape[0]
    slot_count = frames.shape[1] * micro * nblk * ncol
    bias_row = biases[0]
    deep = w_input.shape[0]
    rows_out = OUT_GROUPS * OUT_ROWS
    inputs, h_one, h_two, slope_one, slope_two, low_hidden, low_output, mom_far, d_logits, vec = (
        forward_pass(
            frames.reshape(-1, deep),
            labels,
            mask,
            w_input,
            w_hidden,
            w_output.T,
            biases,
            mom_input,
            slot_count,
        )
    )
    partial = inner_rows(d_logits, low_output)
    next_out, codes, sizes = squash_out(d_logits, h_two, res_output[0].T)
    next_hid, next_in, red_out, red_hid, red_in, red_far, vec_sum, stats = reduce_grads(
        codes,
        sizes,
        h_one,
        inputs,
        partial,
        slope_two,
        slope_one,
        low_hidden,
        res_hidden[0],
        res_input[0],
        vec,
        scol,
        deep,
    )
    next_res_output = next_out.transpose(1, 2, 0)
    vec_sum = vec_sum.reshape(-1)
    red_bias = vec_sum[: bias_row.shape[0]]
    loss_sum = vec_sum[bias_row.shape[0]]
    done_hidden, done_input, next_mom_hidden, next_mom_input, norms = muon(
        stats,
        red_hid,
        mom_hidden,
        red_in,
        mom_input,
        red_far,
        mom_far,
        hcol * ncol,
    )
    clip_norm = norms[0, 0]
    factor = norms[4, 0]
    muon_scale = LR_MUON * 0.2 * math.sqrt(hcol * ncol)
    new_input = w_input * (1.0 - LR_MUON * WD_MUON) - muon_scale * done_input
    new_hidden = w_hidden * (1.0 - LR_MUON * WD_MUON) - muon_scale * done_hidden
    new_output, next_out_first, next_out_second = adam_step(
        w_output, factor * red_out[:scol].T, out_first, out_second
    )
    new_biases, next_bias_first, next_bias_second = adam_step(
        biases, factor * red_bias[None, :], bias_first, bias_second
    )
    return (
        loss_sum,
        clip_norm,
        new_input,
        new_hidden,
        new_output,
        new_biases,
        next_mom_input,
        next_mom_hidden,
        next_out_first,
        next_out_second,
        next_bias_first,
        next_bias_second,
        next_in[None],
        next_hid[None],
        next_res_output,
    )


def solution(mesh):
    in_specs = (
        P(None, ("blk", "col"), None),
        P(None, ("blk", "col")),
        P(None, ("blk", "col")),
        P(None, "col"),
        P("blk", "col"),
        P("blk", "col"),
        P("col", None),
        P(None, "col"),
        P("blk", "col"),
        P("blk", "col"),
        P("blk", "col"),
        P("col", None),
        P("col", None),
        P("blk", None, "col"),
        P("blk", None, "col"),
        P("blk", None, "col"),
    )
    out_specs = (
        P(),
        P(),
        P(None, "col"),
        P("blk", "col"),
        P("blk", "col"),
        P("col", None),
        P(None, "col"),
        P("blk", "col"),
        P("blk", "col"),
        P("blk", "col"),
        P("col", None),
        P("col", None),
        P("blk", None, "col"),
        P("blk", None, "col"),
        P("blk", None, "col"),
    )
    cubes = mesh.shape["blk"] == 8 and mesh.shape["col"] == 4
    body = fast_body if cubes else plain_body
    return jax.shard_map(body, mesh=mesh, in_specs=in_specs, out_specs=out_specs, check_vma=False)
```

```python
import functools
import math

import jax
import jax.numpy as jnp
from jax import lax
from jax.experimental import pallas as pl
from jax.experimental.pallas import tpu as pltpu
from jax.sharding import PartitionSpec as P

NS = 5
STEP = 5


NS_A = 3.4445
NS_B = -4.775
NS_C = 2.0315
CLIP = 0.002
LR_MUON = 0.1
WD_MUON = 0.01
LR_ADAM = 0.03
WD_ADAM = 0.1

MESH = pl.DeviceIdType.MESH
F32 = jnp.float32
BF16 = jnp.bfloat16
I16 = jnp.int16
LN2 = math.log(2.0)
TOP_CODE = 32700.0
LEVELS = 64.0


def matmul(left_side, right_side):
    return jnp.dot(left_side, right_side, preferred_element_type=jnp.float32)


def inner_rows(left_side, right_side):
    return lax.dot_general(
        left_side, right_side, (((0,), (0,)), ((), ())), preferred_element_type=jnp.float32
    )


def outer_cols(left_side, right_side):
    return lax.dot_general(
        left_side, right_side, (((1,), (1,)), ((), ())), preferred_element_type=jnp.float32
    )


def precise(left_side, right_side):
    return jnp.dot(
        left_side, right_side, precision=lax.Precision.HIGHEST, preferred_element_type=jnp.float32
    )


def spread_cols(values):
    return lax.all_gather(values, "col", axis=1, tiled=True)


def reduce_cols(values):
    return lax.psum_scatter(values, "col", scatter_dimension=1, tiled=True)


def collect_rows(values):
    return lax.all_gather(values, "blk", axis=0, tiled=True)


def squash(gradient, resid):
    value = gradient + resid.astype(jnp.float32)
    scale = jnp.mean(jnp.abs(value), axis=0, keepdims=True) + 1e-12
    signed = scale * jnp.tanh(2.0 * value / scale)
    return (signed, value - signed)


def adam_step(weight, gradient, first, second):
    first = 0.5 * first + 0.5 * gradient
    second = 0.95 * second + 0.05 * gradient * gradient
    update = first / (1.0 - 0.5**STEP) / (jnp.sqrt(second / (1.0 - 0.95**STEP)) + 1e-08)
    return (weight - LR_ADAM * (update + WD_ADAM * weight), first, second)


def halves(values):
    top = values.astype(BF16)
    return top, (values - top.astype(F32)).astype(BF16)


def dot_nn(left_side, right_side):
    return lax.dot_general(
        left_side, right_side, (((1,), (0,)), ((), ())), preferred_element_type=F32
    )


def dot_nt(left_side, right_side):
    return lax.dot_general(
        left_side, right_side, (((1,), (1,)), ((), ())), preferred_element_type=F32
    )


RING = 8
STEPS = RING - 1
OUT_ROWS = 592
OUT_GROUPS = 4
HID_ROWS = 512
HID_GROUP = 4
IN_GROUP = 5
TURN_AT = 5
CROSS_AT = 6
HID_AT = 13
FINISH_AT = 14
IN_AT = 20
HID_HOP = 2


def ring_place(blk):
    odd = blk % 2
    return (blk // 2) * (1 - odd) + (7 - blk // 2) * odd


def ring_blk(place):
    back = place // 4
    return 2 * place * (1 - back) + (15 - 2 * place) * back


def scale_code(size):
    return jnp.ceil(jnp.log(jnp.maximum(size, 1e-30)) * (LEVELS / LN2))


def code_scale(code):
    return jnp.exp(code * (LN2 / LEVELS))


def to_codes(values):
    return jnp.round(values).astype(jnp.int32).astype(I16)


def from_codes(codes):
    return codes.astype(jnp.int32).astype(F32)


def chunk_of(lane):
    number = lane // 256
    return number // 2 if number % 2 == 0 else 7 - number // 2


def squash_kernel(senones, dl_ref, h_ref, res_ref, next_ref, codes_ref, size_ref, grad, cols, marks):
    group = pl.program_id(0)
    rows, wide = grad.shape
    valid = senones - group * rows
    for first, count in ((0, rows // 32 * 16), (rows // 32 * 16, rows - rows // 32 * 16)):
        there = slice(first, first + count)
        total = jnp.zeros((count, 128), F32)
        for lane in range(0, wide, 512):
            value = dot_nn(dl_ref[there, :], h_ref[:, lane : lane + 512])
            value = value + res_ref[there, lane : lane + 512].astype(F32)
            row = first + lax.broadcasted_iota(jnp.int32, value.shape, 0)
            value = jnp.where(row < valid, value, 0.0)
            grad[there, lane : lane + 512] = value
            value = jnp.abs(value)
            for part in range(0, 512, 128):
                total = total + value[:, part : part + 128]
        size = jnp.sum(total, axis=1, keepdims=True) * (1.0 / wide) + 1e-12
        size = jnp.broadcast_to(size, (count, 128))
        marks[there, :] = size
        cols[0, there, :] = size
        cols[1, there, :] = 2.0 / size

    def some(number, carry):
        row = pl.multiple_of(number * 16, 16)
        size = cols[0, pl.ds(row, 16), :]
        steep = cols[1, pl.ds(row, 16), :]
        for lane in range(0, wide, 128):
            piece = grad[pl.ds(row, 16), lane : lane + 128]
            curve = jnp.tanh(piece * steep)
            codes_ref[0, 2 * chunk_of(lane) + lane // 128 % 2, pl.ds(row, 16), :] = to_codes(
                curve * TOP_CODE
            )
            next_ref[pl.ds(row, 16), 0, lane : lane + 128] = piece - size * curve
        return carry

    lax.fori_loop(0, rows // 16, some, 0)
    marks[rows:, :] = jnp.zeros((marks.shape[0] - rows, 128), F32)
    lines = [jnp.transpose(marks[first : first + 128, :])[0:1, :] for first in range(0, rows, 128)]
    lines.append(jnp.zeros((8 - len(lines), 128), F32))
    size_ref[0] = jnp.concatenate(lines, axis=0)


def squash_out(dl, h_two, res_out):
    senones, wide = res_out.shape
    frames = dl.shape[1]
    return pl.pallas_call(
        functools.partial(squash_kernel, senones),
        grid=(OUT_GROUPS,),
        out_shape=(
            jax.ShapeDtypeStruct((senones, 1, wide), F32),
            jax.ShapeDtypeStruct((OUT_GROUPS, 2 * RING, OUT_ROWS, 128), I16),
            jax.ShapeDtypeStruct((OUT_GROUPS, 8, 128), F32),
        ),
        in_specs=[
            pl.BlockSpec((OUT_ROWS, frames), lambda group: (group, 0)),
            pl.BlockSpec((frames, wide), lambda group: (0, 0)),
            pl.BlockSpec((OUT_ROWS, wide), lambda group: (group, 0)),
        ],
        out_specs=(
            pl.BlockSpec((OUT_ROWS, 1, wide), lambda group: (group, 0, 0)),
            pl.BlockSpec((1, 2 * RING, OUT_ROWS, 128), lambda group: (group, 0, 0, 0)),
            pl.BlockSpec((1, 8, 128), lambda group: (group, 0, 0)),
        ),
        scratch_shapes=[
            pltpu.VMEM((OUT_ROWS, wide), F32),
            pltpu.VMEM((2, OUT_ROWS, 128), F32),
            pltpu.VMEM((640, 128), F32),
        ],
        compiler_params=pltpu.CompilerParams(vmem_limit_bytes=60 * 1024 * 1024),
    )(dl, h_two, res_out)


def reduce_kernel(
    deep,
    senones,
    codes_ref,
    sizes_ref,
    h_one_ref,
    x_ref,
    part_ref,
    slope_two_ref,
    slope_one_ref,
    w_hid_ref,
    res_hid_ref,
    res_in_ref,
    vec_ref,
    next_hid_ref,
    next_in_ref,
    red_out_ref,
    red_hid_ref,
    red_in_ref,
    red_far_ref,
    vec_sum_ref,
    stats_ref,
    grad,
    turned,
    res_buf,
    h_buf,
    slope_buf,
    marks,
    cols,
    keep_sums,
    dz,
    dz_two,
    dz_one,
    core_out,
    core_got,
    far_out,
    far_got,
    own_out,
    got_out,
    own_hid,
    got_hid,
    own_in,
    got_in,
    share_in,
    share_far,
    sizes,
    shares,
    vec,
    vecs,
    res_sems,
    load_sems,
    code_sems,
    slope_sems,
    core_send,
    core_recv,
    far_send,
    far_recv,
    out_send,
    out_recv,
    hid_send,
    hid_recv,
    in_send,
    in_recv,
    share_send,
    share_recv,
    vec_send,
    vec_recv,
    size_send,
    size_recv,
    share_far_send,
    share_far_recv,
):
    blk = lax.axis_index("blk")
    col = lax.axis_index("col")
    here = ring_place(blk)
    core, high = col % 2, col // 2
    cores = {"col": col + 1 - 2 * core}
    across = {"col": (col + 2) % 4}
    barrier = pltpu.get_barrier_semaphore()
    for target in (cores, across, *({"blk": (blk + away) % RING} for away in range(1, RING))):
        pl.semaphore_signal(barrier, inc=1, device_id=target, device_id_type=MESH)

    def code_copy(group):
        return pltpu.make_async_copy(codes_ref.at[group], own_out.at[group], code_sems.at[group])

    def hid_res_copy(part):
        return pltpu.make_async_copy(
            res_hid_ref.at[:, pl.ds(part * 256, 256)],
            res_buf.at[part],
            res_sems.at[part],
        )

    def hid_next_copy(part):
        return pltpu.make_async_copy(
            turned, next_hid_ref.at[:, pl.ds(part * 256, 256)], load_sems.at[1]
        )

    def load(src, dst):
        return pltpu.make_async_copy(src, dst, load_sems.at[0])

    for group in range(OUT_GROUPS):
        code_copy(group).start()
    for part in range(2):
        hid_res_copy(part).start()
    load(h_one_ref, h_buf).start()
    marks[...] = jnp.zeros_like(marks)
    stats_ref[...] = jnp.zeros_like(stats_ref)
    vec[...] = vec_ref[...]
    pl.semaphore_wait(barrier, RING + 1)

    CHUNK = 256
    units = slope_buf.shape[2]

    def slope_copy(layer, block):
        rows = pl.ds(pl.multiple_of(block * CHUNK, CHUNK), CHUNK)
        src = (slope_two_ref, slope_one_ref)[layer]
        return pltpu.make_async_copy(src.at[rows, :], slope_buf.at[block % 2], slope_sems.at[block % 2])

    def core_move(layer, block):
        return pltpu.make_async_remote_copy(
            src_ref=core_out.at[block % 2],
            dst_ref=core_got.at[layer, block],
            send_sem=core_send.at[block % 2],
            recv_sem=core_recv.at[layer, block],
            device_id=cores,
            device_id_type=MESH,
        )

    def far_move(layer, block):
        return pltpu.make_async_remote_copy(
            src_ref=far_out.at[block % 2],
            dst_ref=far_got.at[layer, block],
            send_sem=far_send.at[block % 2],
            recv_sem=far_recv.at[layer, block],
            device_id=across,
            device_id_type=MESH,
        )

    def lanes_of(number):
        return pl.ds(pl.multiple_of(number * units, units), units)

    def rows_at(number):
        return pl.ds(pl.multiple_of(number * 16, 16), 16)

    def free(copy, layer, block):
        @pl.when((layer > 0) | (block >= 2))
        def _():
            copy.wait_send()

    def lane_codes(first):
        return jnp.transpose(marks[first : first + 128, :])[0:1, :]

    def set_factors():
        top = jnp.max(cols[0, 0:CHUNK, :], axis=1, keepdims=True)
        code = scale_code(top)
        marks[0:CHUNK, :] = jnp.broadcast_to(code, (CHUNK, 128))
        cols[1, 0:CHUNK, :] = jnp.broadcast_to(TOP_CODE / code_scale(code), (CHUNK, 128))

    def largest(values):
        return functools.reduce(
            jnp.maximum,
            [
                jnp.abs(value[:, lane : lane + 128])
                for value in values
                for lane in range(0, value.shape[1], 128)
            ],
        )

    def scaled(values, factor):
        return jnp.concatenate(
            [values[:, lane : lane + 128] * factor for lane in range(0, values.shape[1], 128)], axis=1
        )

    def put_scale(out):
        codes = jnp.concatenate(
            [lane_codes(0), lane_codes(128), jnp.zeros((14, 128), F32)], axis=0
        )
        out[CHUNK : CHUNK + 16, 0:128] = codes.astype(jnp.int32).astype(I16)

    def read_scale(got):
        step = code_scale(from_codes(got[CHUNK : CHUNK + 16, 0:128])) * (1.0 / TOP_CODE)
        step = jnp.transpose(jnp.concatenate([step, jnp.zeros((112, 128), F32)], axis=0))
        for up in range(2):
            marks[CHUNK + up * 128 : CHUNK + (up + 1) * 128, :] = jnp.broadcast_to(
                step[:, up : up + 1], (128, 128)
            )

    def step_at(number):
        return marks[pl.ds(pl.multiple_of(CHUNK + number * 16, 16), 16), :]

    def split(layer, block):
        free(core_move(layer, block), layer, block)

        def measure(number, carry):
            rows = rows_at(number)
            cols[0, rows, :] = largest(
                [grad[rows, lanes_of(2 * half + 1 - core)] for half in range(2)]
            )
            return carry

        lax.fori_loop(0, CHUNK // 16, measure, 0)
        set_factors()

        def write(number, carry):
            rows = rows_at(number)
            factor = cols[1, rows, :]
            for half in range(2):
                there = slice(half * units, (half + 1) * units)
                core_out[block % 2, rows, there] = to_codes(
                    scaled(grad[rows, lanes_of(2 * half + 1 - core)], factor)
                )
                keep_sums[block, rows, there] = grad[rows, lanes_of(2 * half + core)]
            return carry

        lax.fori_loop(0, CHUNK // 16, write, 0)
        put_scale(core_out.at[block % 2])
        core_move(layer, block).start()

    def cross(layer, block):
        core_move(layer, block).wait_recv()
        free(far_move(layer, block), layer, block)
        got = core_got.at[layer, block]
        read_scale(got)

        def add(number, carry):
            rows = rows_at(number)
            near, away = lanes_of(high), lanes_of(1 - high)
            step = step_at(number)
            keep_sums[block, rows, near] += scaled(from_codes(got[rows, near]), step)
            value = keep_sums[block, rows, away] + scaled(from_codes(got[rows, away]), step)
            keep_sums[block, rows, away] = value
            cols[0, rows, :] = largest([value])
            return carry

        lax.fori_loop(0, CHUNK // 16, add, 0)
        set_factors()

        def write(number, carry):
            rows = rows_at(number)
            far_out[block % 2, rows, :] = to_codes(
                scaled(keep_sums[block, rows, lanes_of(1 - high)], cols[1, rows, :])
            )
            return carry

        lax.fori_loop(0, CHUNK // 16, write, 0)
        put_scale(far_out.at[block % 2])
        far_move(layer, block).start()

    def finish(layer, block):
        far_move(layer, block).wait_recv()
        slope_copy(layer, block).wait()
        got = far_got.at[layer, block]
        read_scale(got)

        def one(number, total):
            rows = rows_at(number)
            value = keep_sums[block, rows, lanes_of(high)] + scaled(
                from_codes(got[rows, :]), step_at(number)
            )
            value = (value * slope_buf[block % 2, rows, :]).astype(BF16)
            dz[rows, :] = value
            return total + value.astype(F32)

        total = lax.fori_loop(0, CHUNK // 16, one, jnp.zeros((16, units), F32))
        if layer == 0:

            @pl.when(block < 2)
            def _():
                slope_copy(0, block + 2).start()

            @pl.when(block >= 2)
            def _():
                slope_copy(1, block - 2).start()

        else:

            @pl.when(block < 2)
            def _():
                slope_copy(1, block + 2).start()

        total = jnp.sum(total, axis=0, keepdims=True)
        for number in range(units // 128):
            row = 4 * (1 - layer) + number
            vec[row : row + 1, :] += total[:, number * 128 : (number + 1) * 128]
        flipped = (dz_two, dz_one)[layer]
        for up in range(CHUNK // 128):
            there = pl.ds(pl.multiple_of(block * CHUNK + up * 128, 128), 128)
            for number in range(units // 128):
                tile = dz[up * 128 : (up + 1) * 128, number * 128 : (number + 1) * 128]
                flipped[number * 128 : (number + 1) * 128, there] = jnp.transpose(
                    tile.astype(F32)
                ).astype(BF16)

    def blocks(first, last, work):
        def one(block, carry):
            work(block)
            return carry

        lax.fori_loop(first, last, one, 0)

    def start_block(block):
        rows = pl.ds(pl.multiple_of(block * CHUNK, CHUNK), CHUNK)
        copy = pltpu.make_async_copy(part_ref.at[rows, :], grad.at[pl.ds(0, CHUNK), :], load_sems.at[1])
        copy.start()
        copy.wait()
        split(0, block)

    def turn_block(block):
        finish(0, block)
        for lane in range(0, grad.shape[1], 512):
            grad[0:CHUNK, lane : lane + 512] = dot_nt(dz[...], w_hid_ref[lane : lane + 512, :])
        split(1, block)

    core_out[:, CHUNK:, :] = jnp.zeros((2, 16, 2 * units), I16)
    far_out[:, CHUNK:, :] = jnp.zeros((2, 16, units), I16)
    slope_copy(0, 0).start()
    slope_copy(0, 1).start()
    def vec_copy(away):
        return pltpu.make_async_remote_copy(
            src_ref=vec,
            dst_ref=vecs.at[blk],
            send_sem=vec_send.at[away - 1],
            recv_sem=vec_recv.at[away - 1],
            device_id={"blk": (blk + away) % RING},
            device_id_type=MESH,
        )

    def set_rows(count, first_own, size):
        size = jnp.broadcast_to(size, (count, 128))
        marks[first_own : first_own + count, :] = size
        cols[0, 0:count, :] = size
        cols[1, 0:count, :] = 2.0 / size

    def tell_sizes(group):
        for away in range(1, RING):
            size_copy(group, away).start()

    def size_copy(group, away):
        return pltpu.make_async_remote_copy(
            src_ref=sizes.at[group, here],
            dst_ref=sizes.at[group, here],
            send_sem=size_send.at[group, away - 1],
            recv_sem=size_recv.at[group, away - 1],
            device_id={"blk": ring_blk((here + away) % RING)},
            device_id_type=MESH,
        )

    def set_sizes(rows, group):
        parts = [lane_codes(first) for first in range(0, rows, 128)]
        parts.append(jnp.zeros((8 - len(parts), 128), F32))
        sizes[group, here] = jnp.concatenate(parts, axis=0)
        tell_sizes(group)

    def make_shares(group, row_of):
        for away in range(1, RING):
            size_copy(group, away).wait_recv()
        for way in range(2):
            tiles = []
            for step in range(STEPS):
                mine = row_of(here, step, way)
                came = mine * 0.0
                for back in range(step + 1):
                    came = came + row_of((here - 1 - back + (2 + 2 * back) * way + RING) % RING, step, way)
                if step < STEPS - 1:
                    whole = 1.0 / jnp.maximum(came + mine, 1e-30)
                else:
                    whole = 1.0 / TOP_CODE
                tiles += [came * whole, mine * whole]
            tiles.append(jnp.zeros((16, 128), F32))
            shares[group, way] = jnp.transpose(jnp.concatenate(tiles, axis=0))

    def hid_group():
        load(h_one_ref, h_buf).wait()
        wide = grad.shape[1]
        for part in range(2):
            first = part * 256
            hid_res_copy(part).wait()
            total = jnp.zeros((256, 128), F32)
            for lane in range(0, wide, 512):
                value = dot_nn(dz_two[first : first + 256, :], h_buf[:, lane : lane + 512])
                value = value + jnp.transpose(res_buf[part, lane : lane + 512, :].astype(F32))
                grad[:, lane : lane + 512] = value
                value = jnp.abs(value)
                for more in range(0, 512, 128):
                    total = total + value[:, more : more + 128]
            set_rows(
                256, first, jnp.sum(total, axis=1, keepdims=True) * (1.0 / wide) + 1e-12
            )

            def some(number, carry, first=first):
                row = pl.multiple_of(number * 16, 16)
                size = cols[0, pl.ds(row, 16), :]
                steep = cols[1, pl.ds(row, 16), :]
                for lane in range(0, wide, 128):
                    piece = grad[pl.ds(row, 16), lane : lane + 128]
                    curve = jnp.tanh(piece * steep)
                    own_hid[2 * chunk_of(lane) + lane // 128 % 2, pl.ds(first + row, 16), :] = (
                        to_codes(curve * TOP_CODE)
                    )
                    grad[pl.ds(row, 16), lane : lane + 128] = piece - size * curve
                return carry

            lax.fori_loop(0, 16, some, 0)
            if part:
                hid_next_copy(part - 1).wait()
            for lane in range(0, wide, 128):
                turned[lane : lane + 128, :] = jnp.transpose(grad[:, lane : lane + 128])
            hid_next_copy(part).start()
        load(x_ref, h_buf.at[:, pl.ds(0, x_ref.shape[1])]).start()
        set_sizes(HID_ROWS, HID_GROUP)
        hid_next_copy(1).wait()

    def in_group():
        wide = x_ref.shape[1]
        load(x_ref, h_buf.at[:, pl.ds(0, wide)]).wait()
        for top in range(0, wide, 128):
            count = min(128, deep - top)
            for left in range(0, HID_ROWS, 128):
                tile = res_in_ref[top : top + count, left : left + 128].astype(F32)
                if count < 128:
                    tile = jnp.concatenate([tile, jnp.zeros((128 - count, 128), F32)], axis=0)
                place, lane = top // 256 * HID_ROWS + left, top % 256
                turned[place : place + 128, lane : lane + 128] = jnp.transpose(tile)
        for first in range(0, HID_ROWS, 256):
            grad[0:256, 0:wide] = dot_nn(dz_one[first : first + 256, :], h_buf[:, 0:wide])

            def add(number, carry, first=first):
                row = pl.multiple_of(number * 16, 16)
                place = pl.multiple_of(first + row, 16)
                value = grad[pl.ds(row, 16), 0:wide] + jnp.concatenate(
                    [turned[pl.ds(place, 16), :], turned[pl.ds(HID_ROWS + place, 16), :]], axis=1
                )
                grad[pl.ds(row, 16), 0:wide] = value
                value = jnp.abs(value)
                cols[0, pl.ds(row, 16), :] = functools.reduce(
                    jnp.add, [value[:, lane : lane + 128] for lane in range(0, wide, 128)]
                )
                return carry

            lax.fori_loop(0, 16, add, 0)
            set_rows(
                256,
                first,
                jnp.sum(cols[0, 0:256, :], axis=1, keepdims=True) * (1.0 / deep) + 1e-12,
            )

            def some(number, carry, first=first):
                row = pl.multiple_of(number * 16, 16)
                place = pl.multiple_of(first + row, 16)
                size = cols[0, pl.ds(row, 16), :]
                steep = cols[1, pl.ds(row, 16), :]
                chunk = first // 64 + number // 4
                inside = pl.multiple_of(number % 4 * 16, 16)
                for lane in range(0, wide, 128):
                    piece = grad[pl.ds(row, 16), lane : lane + 128]
                    curve = jnp.tanh(piece * steep)
                    turned[
                        pl.ds(lane // 256 * HID_ROWS + place, 16), lane % 256 : lane % 256 + 128
                    ] = piece - size * curve
                    own_in[
                        2 * chunk + lane // 256, pl.ds(inside, 16), lane % 256 : lane % 256 + 128
                    ] = to_codes(curve * TOP_CODE)
                return carry

            lax.fori_loop(0, 16, some, 0)
        for top in range(0, wide, 128):
            count = min(128, deep - top)
            for left in range(0, HID_ROWS, 128):
                place, lane = top // 256 * HID_ROWS + left, top % 256
                tile = jnp.transpose(turned[place : place + 128, lane : lane + 128])
                next_in_ref[top : top + count, left : left + 128] = tile[0:count, :]
        sizes[IN_GROUP, here] = jnp.concatenate(
            [lane_codes(64 * chunk) for chunk in range(RING)], axis=0
        )
        tell_sizes(IN_GROUP)

    def towards(way):
        return {"blk": ring_blk((here + 1 - 2 * way + RING) % RING)}

    def move(src, got, step, way, send_sem, recv_sem):
        return pltpu.make_async_remote_copy(
            src_ref=src,
            dst_ref=got.at[way, step],
            send_sem=send_sem.at[way, step],
            recv_sem=recv_sem.at[way, step],
            device_id=towards(way),
            device_id_type=MESH,
        )

    def first_moves(own, got, send_sem, recv_sem):
        for way in range(2):
            chunk = (here - 1 + 2 * way + RING) % RING
            move(own.at[2 * chunk + way], got, 0, way, send_sem, recv_sem).start()

    def hop(rows, own, got, group, step, send_sem, recv_sem, keep):
        for way in range(2):
            move(got.at[way, step], got, step, way, send_sem, recv_sem).wait_recv()

        def add(way, result):
            message = got.at[way, step]
            ahead = here - 2 - step + way * (4 + 2 * step) + 2 * RING
            mine = own.at[2 * (ahead % RING) + way]
            share = pltpu.roll(shares[group, way], (128 - 16 * step) % 128, 1)
            for number, first in enumerate(range(0, rows, 128)):
                count = min(128, rows - first)
                there = slice(first, first + count)
                result(
                    first,
                    count,
                    from_codes(message[there, :]) * share[0:count, number : number + 1]
                    + from_codes(mine[there, :]) * share[0:count, 8 + number : 9 + number],
                )

        @pl.when(step < STEPS - 1)
        def _():
            for way in range(2):

                def write(first, count, value, way=way):
                    got[way, step, first : first + count, :] = to_codes(value)

                add(way, write)
            for way in range(2):
                move(got.at[way, step], got, step + 1, way, send_sem, recv_sem).start()

        @pl.when(step == STEPS - 1)
        def _():
            for way in range(2):

                def finish_rows(first, count, value, way=way):
                    keep(way, first, count, value)
                    square = jnp.sum(value * value, axis=0, keepdims=True)
                    for lane in range(0, value.shape[1], 128):
                        stats_ref[0:1, :] += square[:, lane : lane + 128]

                add(way, finish_rows)

    def out_hop(group, step):
        def keep(way, first, count, value):
            row = pl.multiple_of(group * OUT_ROWS + first, 16)
            red_out_ref[pl.ds(row, count), way * 128 : (way + 1) * 128] = value

        hop(
            OUT_ROWS,
            own_out.at[group],
            got_out.at[group],
            group,
            step,
            out_send.at[group],
            out_recv.at[group],
            keep,
        )

    def hid_hop(step):
        def keep(way, first, count, value):
            red_hid_ref[first : first + count, way * 128 : (way + 1) * 128] = value

        hop(HID_ROWS, own_hid, got_hid, HID_GROUP, step, hid_send, hid_recv, keep)

    def share_move(step, way):
        place = (here - step + 2 * step * way + 2 * RING) % RING
        return pltpu.make_async_remote_copy(
            src_ref=share_in.at[way, place],
            dst_ref=share_in.at[way, place],
            send_sem=share_send.at[way, step],
            recv_sem=share_recv.at[way, step],
            device_id=towards(way),
            device_id_type=MESH,
        )

    def share_across(way, place):
        return pltpu.make_async_remote_copy(
            src_ref=share_in.at[way, place],
            dst_ref=share_far.at[way, place],
            send_sem=share_far_send.at[way, place],
            recv_sem=share_far_recv.at[way, place],
            device_id=across,
            device_id_type=MESH,
        )

    def in_hop(step):
        def keep(way, first, count, value):
            share_in[way, here] = value

        hop(64, own_in, got_in, IN_GROUP, step, in_send, in_recv, keep)

        @pl.when(step == STEPS - 1)
        def _():
            for way in range(2):
                share_move(0, way).start()
                share_across(way, here).start()

    def share_hop(step):
        for way in range(2):
            share_move(step, way).wait_recv()
            share_across(way, (here - 1 - step + (2 + 2 * step) * way + RING) % RING).start()

        @pl.when(step < STEPS - 1)
        def _():
            for way in range(2):
                share_move(step + 1, way).start()

    def in_step(index):
        @pl.when((index >= 0) & (index < STEPS))
        def _():
            in_hop(index)

        @pl.when((index >= STEPS) & (index < 2 * STEPS))
        def _():
            share_hop(index - STEPS)

    def chunk_row(place, step, way):
        chunk = (here - 2 - step + way * (4 + 2 * step) + 2 * RING) % RING
        line = sizes[IN_GROUP, place, pl.ds(chunk, 1), :]
        return jnp.broadcast_to(line, (8, 128))

    for group in range(OUT_GROUPS):
        sizes[group, here] = sizes_ref[group]
        tell_sizes(group)
        code_copy(group).wait()
        first_moves(own_out.at[group], got_out.at[group], out_send.at[group], out_recv.at[group])
    blocks(0, 4, start_block)

    def each(number, first, spacing, count, work):
        after = number - first

        @pl.when((after >= 0) & (after < spacing * count) & (after % spacing == 0))
        def _():
            work(after // spacing)

    def turn(number, carry):
        @pl.when(number < OUT_GROUPS)
        def _():
            make_shares(number, lambda place, step, way: sizes[number, place])

        @pl.when(number < OUT_GROUPS * STEPS)
        def _():
            out_hop(number % OUT_GROUPS, number // OUT_GROUPS)

        @pl.when(number == HID_AT + HID_HOP)
        def _():
            make_shares(HID_GROUP, lambda place, step, way: sizes[HID_GROUP, place])

        each(number, HID_AT + HID_HOP, HID_HOP, STEPS, hid_hop)

        @pl.when(number == IN_AT + 1)
        def _():
            make_shares(IN_GROUP, chunk_row)

        index = 2 * (number - IN_AT - 1)
        in_step(index)
        each(number, 0, 1, 4, lambda block: cross(0, block))
        each(number, TURN_AT, 2, 4, turn_block)
        each(number, CROSS_AT, 2, 4, lambda block: cross(1, block))

        @pl.when(number == HID_AT)
        def _():
            hid_group()
            first_moves(own_hid, got_hid, hid_send, hid_recv)

        each(number, FINISH_AT, 2, 4, lambda block: finish(1, block))

        @pl.when(number == IN_AT)
        def _():
            in_group()
            first_moves(own_in, got_in, in_send, in_recv)
            for away in range(1, RING):
                vec_copy(away).start()

        in_step(index + 1)
        return carry

    turns = max(IN_AT + 1 + STEPS, HID_AT + HID_HOP * STEPS + 1, OUT_GROUPS * STEPS)
    lax.fori_loop(0, turns, turn, 0)

    def unfold(shares_of, out):
        for place in range(0, RING, 2):
            for way in range(2):
                for lane in range(0, 256, 128):
                    tile = jnp.concatenate(
                        [shares_of[way, place + more, :, lane : lane + 128] for more in range(2)],
                        axis=0,
                    )
                    first = way * 256 + lane
                    out[first : first + 128, place * 64 : place * 64 + 128] = jnp.transpose(tile)

    unfold(share_in, red_in_ref)
    for place in range(RING):
        for way in range(2):
            share_across(way, place).wait_recv()
    unfold(share_far, red_far_ref)
    for away in range(1, RING):
        vec_copy(away).wait_recv()
    vecs[blk] = vec[...]
    total = vecs[0]
    for number in range(1, RING):
        total = total + vecs[number]
    vec_sum_ref[...] = total
    flat = 128 * lax.broadcasted_iota(jnp.int32, total.shape, 0) + lax.broadcasted_iota(
        jnp.int32, total.shape, 1
    )
    total = jnp.where(flat < 2 * units + senones, total, 0.0)
    stats_ref[1:2, :] = jnp.sum(total * total, axis=0, keepdims=True) * (1.0 / RING)
    for away in range(1, RING):
        vec_copy(away).wait_send()
        for group in range(OUT_GROUPS + 2):
            size_copy(group, away).wait_send()
    for slot in range(2):
        core_move(1, 2 + slot).wait_send()
        far_move(1, 2 + slot).wait_send()
    for way in range(2):
        for step in range(STEPS):
            for group in range(OUT_GROUPS):
                move(
                    got_out.at[group, way, step],
                    got_out.at[group],
                    step,
                    way,
                    out_send.at[group],
                    out_recv.at[group],
                ).wait_send()
            move(got_hid.at[way, step], got_hid, step, way, hid_send, hid_recv).wait_send()
            move(got_in.at[way, step], got_in, step, way, in_send, in_recv).wait_send()
            share_move(step, way).wait_send()
        for place in range(RING):
            share_across(way, place).wait_send()


def reduce_grads(
    codes, sizes, h_one, x, part, slope_two, slope_one, w_hid, res_hid, res_in, vec, senones, deep
):
    frames, wide = h_one.shape
    in_wide = x.shape[1]
    units = w_hid.shape[1]
    vmem = pl.BlockSpec(memory_space=pltpu.VMEM)
    hbm = pl.BlockSpec(memory_space=pl.ANY)
    message = OUT_ROWS
    hid_message = HID_ROWS
    in_message = 64
    sem = pltpu.SemaphoreType.DMA
    return pl.pallas_call(
        functools.partial(reduce_kernel, deep, senones),
        out_shape=(
            jax.ShapeDtypeStruct((wide, HID_ROWS), F32),
            jax.ShapeDtypeStruct(res_in.shape, F32),
            jax.ShapeDtypeStruct((OUT_GROUPS * OUT_ROWS, 256), F32),
            jax.ShapeDtypeStruct((HID_ROWS, 256), F32),
            jax.ShapeDtypeStruct((in_wide, HID_ROWS), F32),
            jax.ShapeDtypeStruct((in_wide, HID_ROWS), F32),
            jax.ShapeDtypeStruct(vec.shape, F32),
            jax.ShapeDtypeStruct((8, 128), F32),
        ),
        in_specs=[hbm, vmem] + [hbm] * 5 + [vmem, hbm, vmem, vmem],
        out_specs=(hbm,) + (vmem,) * 7,
        scratch_shapes=[
            pltpu.VMEM((256, wide), F32),
            pltpu.VMEM((wide, 256), F32),
            pltpu.VMEM((2, wide, 256), BF16),
            pltpu.VMEM((frames, wide), BF16),
            pltpu.VMEM((2, 256, units), F32),
            pltpu.VMEM((640, 128), F32),
            pltpu.VMEM((2, 256, 128), F32),
            pltpu.VMEM((4, 256, 2 * units), F32),
            pltpu.VMEM((256, units), BF16),
            pltpu.VMEM((units, frames), BF16),
            pltpu.VMEM((units, frames), BF16),
            pltpu.VMEM((2, 272, 2 * units), I16),
            pltpu.VMEM((2, 4, 272, 2 * units), I16),
            pltpu.VMEM((2, 272, units), I16),
            pltpu.VMEM((2, 4, 272, units), I16),
            pltpu.VMEM((OUT_GROUPS, 2 * RING, message, 128), I16),
            pltpu.VMEM((OUT_GROUPS, 2, STEPS, message, 128), I16),
            pltpu.VMEM((2 * RING, hid_message, 128), I16),
            pltpu.VMEM((2, STEPS, hid_message, 128), I16),
            pltpu.VMEM((2 * RING, in_message, 256), I16),
            pltpu.VMEM((2, STEPS, in_message, 256), I16),
            pltpu.VMEM((2, RING, 64, 256), F32),
            pltpu.VMEM((2, RING, 64, 256), F32),
            pltpu.VMEM((OUT_GROUPS + 2, RING, 8, 128), F32),
            pltpu.VMEM((OUT_GROUPS + 2, 2, 128, 128), F32),
            pltpu.VMEM(vec.shape, F32),
            pltpu.VMEM((RING,) + vec.shape, F32),
            sem((2,)),
            sem((2,)),
            sem((OUT_GROUPS,)),
            sem((2,)),
            sem((2,)),
            sem((2, 4)),
            sem((2,)),
            sem((2, 4)),
            sem((OUT_GROUPS, 2, STEPS)),
            sem((OUT_GROUPS, 2, STEPS)),
            sem((2, STEPS)),
            sem((2, STEPS)),
            sem((2, STEPS)),
            sem((2, STEPS)),
            sem((2, STEPS)),
            sem((2, STEPS)),
            sem((STEPS,)),
            sem((STEPS,)),
            sem((OUT_GROUPS + 2, STEPS)),
            sem((OUT_GROUPS + 2, STEPS)),
            sem((2, RING)),
            sem((2, RING)),
        ],
        compiler_params=pltpu.CompilerParams(
            collective_id=1, has_side_effects=True, vmem_limit_bytes=63 * 1024 * 1024
        ),
    )(codes, sizes, h_one, x, part, slope_two, slope_one, w_hid, res_hid, res_in, vec)


RING_STARTS = (0, 0, 5, 6, 7)
LAYER_TWO_WAVE = 7
LOGIT_WAVES = (11, 12, 13, 14)


def forward_kernel(
    slot_count,
    x_ref,
    labels_ref,
    mask_ref,
    w_in_ref,
    w_hid_ref,
    w_out_ref,
    bias_ref,
    mom_ref,
    x_out,
    h_one_out,
    h_two_out,
    slope_one_out,
    slope_two_out,
    w_hid_out,
    w_out_out,
    mom_far_ref,
    dl_ref,
    vec_ref,
    x_all,
    h_one,
    h_two,
    slope_one,
    slope_two,
    w_in,
    w_hid,
    w_out,
    curve,
    bias_line,
    bias_col,
    tags,
    sums,
    ring_send,
    ring_recv,
    x_send,
    x_recv,
    h_send,
    h_recv,
    tag_send,
    tag_recv,
    sum_send,
    sum_recv,
    out_sems,
    mom_sems,
):
    blk = lax.axis_index("blk")
    col = lax.axis_index("col")
    here = ring_place(blk)
    senones, depth = w_out_ref.shape
    own_rows, deep = x_ref.shape
    units = w_hid_ref.shape[1]
    frames = x_all.shape[0]
    cores = {"col": col + 1 - 2 * (col % 2)}
    across = {"col": (col + 2) % 4}
    corner = {"col": (col + 2) % 4 + 1 - 2 * (col % 2)}
    others = (cores, across, corner)

    barrier = pltpu.get_barrier_semaphore()
    for target in others + tuple({"blk": ring_blk((here + way) % RING)} for way in (1, 7)):
        pl.semaphore_signal(barrier, inc=1, device_id=target, device_id_type=MESH)

    w_hid[pl.ds(pl.multiple_of(blk * depth, depth), depth), :] = w_hid_ref[...].astype(BF16)
    own_lanes = pl.ds(pl.multiple_of(blk * depth, depth), depth)
    w_out[senones // 16 * 16 :, own_lanes] = jnp.zeros(
        (w_out.shape[0] - senones // 16 * 16, depth), BF16
    )
    w_out[0:senones, own_lanes] = w_out_ref[...].astype(BF16)
    own_frames = pl.ds(pl.multiple_of(col * own_rows, own_rows), own_rows)
    x_all[own_frames, :] = jnp.zeros((own_rows, x_all.shape[1]), BF16)
    x_all[own_frames, 0:deep] = x_ref[...]
    own_tags = jnp.where(mask_ref[...] > 0, labels_ref[...], -1)
    own_tags = jnp.concatenate([own_tags[row : row + 1, :] for row in range(own_tags.shape[0])], axis=1)
    tags[col] = jnp.broadcast_to(own_tags, (8, own_rows))
    bias_line[...] = jnp.zeros_like(bias_line)
    bias_line[:, 0 : bias_ref.shape[1]] = bias_ref[...]
    sums[...] = jnp.zeros_like(sums)
    pl.semaphore_wait(barrier, 5)

    def ring_part(group, origin, way):
        start = pl.multiple_of(origin * depth + way * 128, 128)
        if group == 0:
            return w_hid.at[pl.ds(start, 128), :]
        return w_out.at[pl.ds((group - 1) * OUT_ROWS, OUT_ROWS), pl.ds(start, 128)]

    def ring_move(group, step, way):
        origin = ring_blk((here - step + 2 * step * way + RING) % RING)
        part = ring_part(group, origin, way)
        return pltpu.make_async_remote_copy(
            src_ref=part,
            dst_ref=part,
            send_sem=ring_send.at[group, way, step],
            recv_sem=ring_recv.at[group, way, step],
            device_id={"blk": ring_blk((here + 1 - 2 * way + RING) % RING)},
            device_id_type=MESH,
        )

    def ring_wave(wave):
        for group, start in enumerate(RING_STARTS):
            step = wave - 1 - start
            for way in range(2):
                if step == -1:
                    ring_move(group, 0, way).start()
                if 0 <= step < STEPS:
                    ring_move(group, step, way).wait_recv()
                    if step < STEPS - 1:
                        ring_move(group, step + 1, way).start()

    def copy_to(target, src, send_sem, recv_sem):
        return pltpu.make_async_remote_copy(
            src_ref=src,
            dst_ref=src,
            send_sem=send_sem,
            recv_sem=recv_sem,
            device_id=target,
            device_id_type=MESH,
        )

    def rows_of(owner):
        return pl.ds(pl.multiple_of(owner * own_rows, own_rows), own_rows)

    def lanes_of(owner):
        return pl.ds(pl.multiple_of(owner * units, units), units)

    def x_move(number):
        owner = across["col"] if number == 2 else col
        target = across if number == 1 else cores
        return copy_to(target, x_all.at[rows_of(owner), :], x_send.at[number], x_recv.at[number])

    def h_move(layer, number, block):
        owner = across["col"] if number == 2 else col
        target = across if number == 1 else cores
        whole = (h_one, h_two)[layer]
        part = whole.at[pl.ds(block * own_rows, own_rows), lanes_of(owner)]
        return copy_to(
            target, part, h_send.at[layer, number, block], h_recv.at[layer, number, block]
        )

    def h_start(layer, block):
        h_move(layer, 0, block).start()
        h_move(layer, 1, block).start()

    def h_forward(layer, block):
        h_move(layer, 1, block).wait_recv()
        h_move(layer, 2, block).start()

    def h_ready(layer, block):
        h_move(layer, 0, block).wait_recv()
        h_move(layer, 2, block).wait_recv()

    ring_wave(0)
    x_move(0).start()
    x_move(1).start()
    tag_copies = [
        copy_to(target, tags.at[col], tag_send.at[number], tag_recv.at[number])
        for number, target in enumerate(others)
    ]
    for copy in tag_copies:
        copy.start()
    w_in[...] = jnp.zeros_like(w_in)
    w_in[0:deep, :] = w_in_ref[...].astype(BF16)
    for number in range(bias_col.shape[0] // 128):
        first = 2 * units + number * 128
        line = jnp.broadcast_to(bias_line[:, first : first + 128], (128, 128))
        bias_col[number * 128 : (number + 1) * 128, :] = jnp.transpose(line)
    ring_wave(1)
    x_move(1).wait_recv()
    x_move(2).start()
    x_move(0).wait_recv()
    x_move(2).wait_recv()

    def layer(number, block, inputs, weights, whole, slopes):
        there = slice(block * own_rows, (block + 1) * own_rows)
        value = jax.nn.sigmoid(
            dot_nn(inputs[there, :], weights[...])
            + bias_line[:, number * units : (number + 1) * units]
        )
        slopes[there, :] = value * (1.0 - value)
        whole[there, lanes_of(col)] = value.astype(BF16)
        h_start(number, block)

    outs = []

    def put(src, dst):
        copy = pltpu.make_async_copy(src, dst, out_sems.at[len(outs)])
        copy.start()
        outs.append(copy)

    for block in range(4):
        layer(0, block, x_all, w_in, h_one, slope_one)
    put(x_all, x_out)
    put(slope_one, slope_one_out)

    def all_tags():
        return jnp.concatenate([tags[owner, 0:1, :] for owner in range(4)], axis=1)

    def own_row(line):
        line = line - col * senones
        return jnp.where(line < senones, line, -1)

    def logits(group):
        first = group * OUT_ROWS
        half = frames // 2
        for part in range(2):
            curve[first : first + OUT_ROWS, part * half : (part + 1) * half] = dot_nt(
                w_out[first : first + OUT_ROWS, :], h_two[part * half : (part + 1) * half, :]
            )
        base = lax.broadcasted_iota(jnp.int32, (16, frames), 0)

        def largest(number, top):
            row = pl.multiple_of(first + number * 16, 16)
            value = curve[pl.ds(row, 16), :] + bias_col[pl.ds(row, 16), 0:1]
            if group == OUT_GROUPS - 1:
                value = jnp.where(base + row < senones, value, -1e30)
            curve[pl.ds(row, 16), :] = value
            return jnp.maximum(top, value)

        top = lax.fori_loop(0, OUT_ROWS // 16, largest, jnp.full((16, frames), -1e30, F32))
        top = jnp.max(top, axis=0, keepdims=True)
        line = jnp.broadcast_to(own_row(all_tags()), (16, frames))

        def exponents(number, carry):
            total, picked = carry
            row = pl.multiple_of(first + number * 16, 16)
            value = curve[pl.ds(row, 16), :]
            power = jnp.exp(value - top)
            curve[pl.ds(row, 16), :] = power
            return total + power, picked + jnp.where(base + row == line, value, 0.0)

        blank = jnp.zeros((16, frames), F32)
        total, picked = lax.fori_loop(0, OUT_ROWS // 16, exponents, (blank, blank))
        sums[col, group : group + 1, :] = top
        sums[col, 4 + group : 5 + group, :] = jnp.sum(total, axis=0, keepdims=True)
        sums[col, 8 + group : 9 + group, :] = jnp.sum(picked, axis=0, keepdims=True)

    mom_copy = pltpu.make_async_remote_copy(
        src_ref=mom_ref,
        dst_ref=mom_far_ref,
        send_sem=mom_sems.at[0],
        recv_sem=mom_sems.at[1],
        device_id=across,
        device_id_type=MESH,
    )
    last_wave = RING_STARTS[-1] + STEPS
    for wave in range(2, last_wave + 1):
        ring_wave(wave)
        if 2 <= wave < 6:
            h_forward(0, wave - 2)
        if wave == LAYER_TWO_WAVE:
            for block in range(4):
                h_ready(0, block)
                layer(1, block, h_one, w_hid, h_two, slope_two)
            put(h_one, h_one_out)
            put(slope_two, slope_two_out)
            put(w_hid, w_hid_out)
        if LAYER_TWO_WAVE < wave <= LAYER_TWO_WAVE + 4:
            h_forward(1, wave - LAYER_TWO_WAVE - 1)
        for group, when in enumerate(LOGIT_WAVES):
            if wave == when:
                if group == 0:
                    for block in range(4):
                        h_ready(1, block)
                    put(h_two, h_two_out)
                    mom_copy.start()
                    for copy in tag_copies:
                        copy.wait_recv()
                rows = pl.ds(group * OUT_ROWS, OUT_ROWS)
                put(w_out.at[rows, :], w_out_out.at[rows, :])
                logits(group)

    sum_copies = [
        copy_to(target, sums.at[col], sum_send.at[number], sum_recv.at[number])
        for number, target in enumerate(others)
    ]
    for copy in sum_copies:
        copy.start()
    for copy in sum_copies:
        copy.wait_recv()

    def lines(first):
        return [sums[owner, first + group : first + group + 1, :] for owner in range(4) for group in range(4)]

    tops = lines(0)
    top = functools.reduce(jnp.maximum, tops)
    total = functools.reduce(
        jnp.add, [size * jnp.exp(own - top) for own, size in zip(tops, lines(4), strict=True)]
    )
    picked = functools.reduce(jnp.add, lines(8))
    line = all_tags()
    live = line >= 0
    loss = jnp.where(live, top + jnp.log(total) - picked, 0.0)
    loss = jnp.sum(loss, axis=1, keepdims=True)
    weight = jnp.where(live, 1.0 / slot_count, 0.0)
    line = jnp.broadcast_to(own_row(line), (16, frames))
    hit_weight = jnp.broadcast_to(weight, (16, frames))
    base = lax.broadcasted_iota(jnp.int32, (16, frames), 0)
    bias_col[...] = jnp.zeros_like(bias_col)
    for group in range(OUT_GROUPS):
        share = jnp.exp(sums[col, group : group + 1, :] - top) / total * weight

        def gradient(number, carry, first=group * OUT_ROWS, share=share):
            row = pl.multiple_of(first + number * 16, 16)
            value = curve[pl.ds(row, 16), :] * share - jnp.where(base + row == line, hit_weight, 0.0)
            value = value.astype(BF16)
            dl_ref[pl.ds(row, 16), :] = value
            value = value.astype(F32)
            bias_col[pl.ds(row, 16), :] = functools.reduce(
                jnp.add, [value[:, lane : lane + 128] for lane in range(0, frames, 128)]
            )
            return carry

        lax.fori_loop(0, OUT_ROWS // 16, gradient, 0)
    vec_ref[...] = jnp.zeros_like(vec_ref)
    row = 2 * units // 128
    for number in range(bias_col.shape[0] // 128):
        line = jnp.transpose(bias_col[number * 128 : (number + 1) * 128, :])
        line = jnp.sum(line, axis=0, keepdims=True)
        place = 128 * number + lax.broadcasted_iota(jnp.int32, line.shape, 1)
        line = jnp.where(place < senones, line, jnp.where(place == senones, loss, 0.0))
        vec_ref[row + number : row + number + 1, :] = line

    for group in range(len(RING_STARTS)):
        for way in range(2):
            for step in range(STEPS):
                ring_move(group, step, way).wait_send()
    for number in range(3):
        x_move(number).wait_send()
        for block in range(4):
            h_move(0, number, block).wait_send()
            h_move(1, number, block).wait_send()
    for copy in tag_copies + sum_copies:
        copy.wait_send()
    mom_copy.wait()
    for copy in outs:
        copy.wait()


def forward_pass(x, labels, mask, w_in, w_hid, w_out, bias, mom, slot_count):
    own_rows = x.shape[0]
    units = w_hid.shape[1]
    frames = 4 * own_rows
    wide = 4 * units
    rows = OUT_GROUPS * OUT_ROWS
    blocks = -(-rows // 128)
    vmem = pl.BlockSpec(memory_space=pltpu.VMEM)
    hbm = pl.BlockSpec(memory_space=pl.ANY)
    sem = pltpu.SemaphoreType.DMA
    kept = (
        ((frames, 512), BF16),
        ((frames, wide), BF16),
        ((frames, wide), BF16),
        ((frames, units), F32),
        ((frames, units), F32),
        ((wide, units), BF16),
        ((rows, wide), BF16),
    )
    return pl.pallas_call(
        functools.partial(forward_kernel, slot_count),
        out_shape=tuple(jax.ShapeDtypeStruct(shape, kind) for shape, kind in kept)
        + (
            jax.ShapeDtypeStruct(mom.shape, F32),
            jax.ShapeDtypeStruct((rows, frames), BF16),
            jax.ShapeDtypeStruct((32, 128), F32),
        ),
        in_specs=[vmem] * 7 + [hbm],
        out_specs=(hbm,) * 8 + (vmem,) * 2,
        scratch_shapes=[pltpu.VMEM(shape, kind) for shape, kind in kept[:5]]
        + [
            pltpu.VMEM((512, units), BF16),
            pltpu.VMEM((wide, units), BF16),
            pltpu.VMEM((rows, wide), BF16),
            pltpu.VMEM((rows, frames), F32),
            pltpu.VMEM((1, 2 * units + blocks * 128), F32),
            pltpu.VMEM((blocks * 128, 128), F32),
            pltpu.VMEM((4, 8, own_rows), jnp.int32),
            pltpu.VMEM((4, 16, frames), F32),
            sem((5, 2, STEPS)),
            sem((5, 2, STEPS)),
            sem((3,)),
            sem((3,)),
            sem((2, 3, 4)),
            sem((2, 3, 4)),
            sem((3,)),
            sem((3,)),
            sem((3,)),
            sem((3,)),
            sem((16,)),
            sem((2,)),
        ],
        compiler_params=pltpu.CompilerParams(
            collective_id=2, has_side_effects=True, vmem_limit_bytes=60 * 1024 * 1024
        ),
    )(x, labels, mask, w_in, w_hid, w_out, bias, mom)


DIM_BITS = (2, 4, 8)
ORDERS = ((0, 1, 2), (1, 2, 0), (2, 0, 1))
PIECES = (
    ((0, 48, 0, 1792),),
    ((48, 96, 0, 1792),),
    ((96, 128, 0, 2048), (0, 96, 1792, 2048)),
)
SIZE_PIECE = 2
LIGHT_HID = 3
LIGHT_IN = 2


def stage_sends(stage, sources):
    moves = []
    for piece, order in enumerate(ORDERS):
        slot = sum(DIM_BITS[order[index]] for index in sources)
        moves.append((piece, slot, order[stage]))
    return moves


def landed(moves):
    return [(slot | DIM_BITS[dim], piece) for piece, slot, dim in moves]


FIRST = stage_sends(0, ())
SECOND = stage_sends(1, ())
SECOND_ON = stage_sends(1, (0,))
THIRD = stage_sends(2, ())
THIRD_A = stage_sends(2, (0,))
THIRD_B = stage_sends(2, (1,))
THIRD_C = stage_sends(2, (0, 1))
MOVES = FIRST + SECOND + SECOND_ON + THIRD + THIRD_A + THIRD_B + THIRD_C


def muon_kernel(
    stats_ref,
    red_hid_ref,
    mom_hid_ref,
    red_in_ref,
    mom_in_ref,
    red_far_ref,
    mom_far_ref,
    hid_ref,
    inp_ref,
    next_hid_ref,
    next_in_ref,
    norm_ref,
    codes,
    sizes,
    tops,
    lows,
    scales,
    weights,
    xs,
    us,
    vs,
    lhs,
    xin,
    xin_top,
    xin_low,
    gram,
    gram_got,
    back,
    sums,
    sums_got,
    spread_out,
    spread_got,
    spread_size_out,
    spread_size_got,
    send_sems,
    core_sems,
    recv_sems,
    back_send,
    back_recv,
    sums_send,
    sums_recv,
    spread_send,
    spread_recv,
    pair_send,
    pair_recv,
):
    blk = lax.axis_index("blk")
    col = lax.axis_index("col")
    rows, wide = xs.shape
    height = back.shape[2]
    deep = mom_in_ref.shape[0]
    part_wide = inp_ref.shape[1]
    other_core = {"col": col + 1 - 2 * (col % 2)}
    dims = (
        {"blk": blk + 1 - 2 * (blk % 2)},
        {"col": (col + 2) % 4},
        {"blk": blk + 2 - 4 * ((blk // 2) % 2)},
    )
    diagonal = {"blk": 4 * (blk // 4) + 3 - blk % 4}
    barrier = pltpu.get_barrier_semaphore()
    corner = {"col": (col + 2) % 4 + 1 - 2 * (col % 2)}
    cols = (other_core, dims[1], corner)
    for target in (*cols, *({"blk": (blk + away) % 8} for away in range(1, 8))):
        pl.semaphore_signal(barrier, inc=1, device_id=target, device_id_type=MESH)

    def fold(values):
        line = jnp.sum(values, axis=0, keepdims=True)
        return sum(line[:, lane : lane + 128] for lane in range(0, line.shape[1], 128))

    share = 0.125
    sums[blk, 0:1, :] = fold(stats_ref[...])
    sums[blk, 1:2, :] = fold(mom_hid_ref[...] * mom_hid_ref[...])
    red_hid = jnp.transpose(red_hid_ref[...])
    sums[blk, 2:3, :] = fold(mom_hid_ref[...] * red_hid)
    sums[blk, 3:4, :] = fold(red_hid_ref[...] * red_hid_ref[...])
    sums[blk, 4:5, :] = fold(mom_in_ref[...] * mom_in_ref[...]) * share
    sums[blk, 5:6, :] = fold(mom_in_ref[...] * red_in_ref[0:deep, :]) * share
    sums[blk, 6:7, :] = fold(red_in_ref[0:deep, :] * red_in_ref[0:deep, :]) * share
    sums[blk, 7:8, :] = jnp.zeros((1, 128), F32)
    eye = lax.broadcasted_iota(jnp.int32, (rows, rows), 0) == lax.broadcasted_iota(
        jnp.int32, (rows, rows), 1
    )
    pl.semaphore_wait(barrier, 10)

    def tell(own, targets, first):
        copies = []
        for number, target in enumerate(targets, start=first):
            copies.append(
                pltpu.make_async_remote_copy(
                    src_ref=own,
                    dst_ref=own,
                    send_sem=sums_send.at[number],
                    recv_sem=sums_recv.at[number],
                    device_id=target,
                    device_id_type=MESH,
                )
            )
            copies[-1].start()
        for copy in copies:
            copy.wait_recv()
        return copies

    told = tell(sums.at[blk], [{"blk": (blk + away) % 8} for away in range(1, 8)], 0)
    sums_got[col] = functools.reduce(jnp.add, [sums[number] for number in range(8)])
    told += tell(sums_got.at[col], cols, 7)
    whole = functools.reduce(jnp.add, [sums_got[number] for number in range(4)])
    whole = jnp.sum(whole, axis=1, keepdims=True)
    clip = jnp.sqrt(whole[0:1])
    factor = jnp.minimum(1.0, CLIP / clip)

    def norm_of(first):
        square = (
            0.25 * whole[first : first + 1]
            + factor * whole[first + 1 : first + 2]
            + factor * factor * whole[first + 2 : first + 3]
        )
        return 1.0 / (jnp.sqrt(jnp.maximum(square, 0.0)) + 1e-07)

    norm_ref[0:4, :] = jnp.broadcast_to(clip, (4, 128))
    norm_ref[4:8, :] = jnp.broadcast_to(factor, (4, 128))
    next_hid_ref[...] = 0.5 * mom_hid_ref[...] + factor * jnp.transpose(red_hid_ref[...])
    next_in_ref[...] = 0.5 * mom_in_ref[...] + factor * red_in_ref[0:deep, :]

    my_lanes = pl.ds(pl.multiple_of(blk * height, height), height)
    for number in range(4):
        there = slice(number * rows, (number + 1) * rows)
        value = jnp.transpose(next_hid_ref[:, there])
        largest = jnp.maximum(jnp.max(jnp.abs(value), axis=1, keepdims=True), 1e-30)
        spread_out[number] = to_codes(value * (TOP_CODE / largest))
        line = jnp.sum(jnp.where(eye, largest, 0.0), axis=0, keepdims=True)
        spread_size_out[number] = jnp.broadcast_to(line * (1.0 / TOP_CODE), (8, rows))
    spread = []
    for away in range(1, 8):
        target = (blk + away) % 8
        for kind, (src, dst) in enumerate(
            ((spread_out, spread_got), (spread_size_out, spread_size_got))
        ):
            spread.append(
                pltpu.make_async_remote_copy(
                    src_ref=src.at[target % 4],
                    dst_ref=dst.at[blk],
                    send_sem=spread_send.at[kind, away - 1],
                    recv_sem=spread_recv.at[kind, away - 1],
                    device_id={"blk": target},
                    device_id_type=MESH,
                )
            )
            spread[-1].start()
    high = col // 2
    my_half = pl.ds(pl.multiple_of(high * part_wide, part_wide), part_wide)
    far_half = pl.ds(pl.multiple_of((1 - high) * part_wide, part_wide), part_wide)
    in_scale = norm_of(4)
    xin[deep:, :] = jnp.zeros((xin.shape[0] - deep, xin.shape[1]), F32)
    xin[0:deep, my_half] = next_in_ref[...] * in_scale
    xin[0:deep, far_half] = (
        0.5 * mom_far_ref[...] + factor * red_far_ref[0:deep, :]
    ) * in_scale
    spread_got[blk] = spread_out[blk % 4]
    spread_size_got[blk] = spread_size_out[blk % 4]
    for copy in spread:
        copy.wait_recv()
    hid_scale = norm_of(1)
    for number in range(8):
        size = jnp.broadcast_to(spread_size_got[number, 0:1, :], (rows, rows))
        size = jnp.transpose(size) * hid_scale
        for lane in range(0, height, 128):
            xs[:, number * height + lane : number * height + lane + 128] = (
                from_codes(spread_got[number, :, lane : lane + 128]) * size
            )

    numbers = {move: number for number, move in enumerate(MOVES)}

    def parts(turn, slot, piece):
        refs = [
            codes.at[turn, slot, pl.ds(top, low - top), pl.ds(left, right - left)]
            for top, low, left, right in PIECES[piece]
        ]
        numbered = [(piece, refs[0])]
        if piece == SIZE_PIECE:
            numbered += [(3, refs[1]), (4, sizes.at[turn, slot])]
        return numbered

    def send(turn, move):
        piece, slot, dim = move
        there = slot | DIM_BITS[dim]
        return [
            pltpu.make_async_remote_copy(
                src_ref=src,
                dst_ref=dst,
                send_sem=send_sems.at[numbers[move], max(number - 2, 0)],
                recv_sem=recv_sems.at[turn, there, number],
                device_id=dims[dim],
                device_id_type=MESH,
            )
            for (number, src), (_, dst) in zip(
                parts(turn, slot, piece), parts(turn, there, piece), strict=True
            )
        ]

    def send_all(turn, moves):
        for move in moves:
            for copy in send(turn, move):
                copy.start()

    def to_core(turn, slot, piece):
        return [
            pltpu.make_async_remote_copy(
                src_ref=src,
                dst_ref=dst,
                send_sem=core_sems.at[slot // 2, number],
                recv_sem=recv_sems.at[turn, slot + 1, number],
                device_id=other_core,
                device_id_type=MESH,
            )
            for (number, src), (_, dst) in zip(
                parts(turn, slot, piece), parts(turn, slot + 1, piece), strict=True
            )
        ]

    def arrived(turn, slot, piece):
        for number, ref in parts(turn, slot, piece):
            pltpu.make_async_remote_copy(
                src_ref=ref,
                dst_ref=ref,
                send_sem=core_sems.at[0, 0],
                recv_sem=recv_sems.at[turn, slot, number],
                device_id=other_core,
                device_id_type=MESH,
            ).wait_recv()

    def forward(turn, moves, on=()):
        for number, (slot, piece) in enumerate(landed(moves)):
            arrived(turn, slot, piece)
            for copy in to_core(turn, slot, piece):
                copy.start()
            if on:
                send_all(turn, on[number : number + 1])

    def gram_copy():
        return pltpu.make_async_remote_copy(
            src_ref=gram,
            dst_ref=gram_got,
            send_sem=pair_send.at[1],
            recv_sem=pair_recv.at[1],
            device_id=other_core,
            device_id_type=MESH,
        )

    def unpack(turn, index, pair, light):
        for core in range(2):
            here = pl.ds(pl.multiple_of(index * 2 * rows + core * rows, rows), rows)
            slot = 2 * pair + core
            if light:
                tops[here, :] = from_codes(codes[turn, slot]).astype(BF16)
            else:
                top, low = halves(from_codes(codes[turn, slot]))
                tops[here, :] = top
                lows[here, :] = low
            size = sizes[turn, slot]
            scales[:, here] = size * size

    def inner(first, count, light):
        here = pl.ds(first, count)
        if light:
            values = dot_nt(lhs[0:rows, :], tops[here, :])
            weights[0:rows, here] = (values * scales[0:1, here]).astype(BF16)
        else:
            both = dot_nt(lhs[...], tops[here, :])
            values = both[:rows] + both[rows:] + dot_nt(lhs[0:rows, :], lows[here, :])
            top, low = halves(values * scales[0:1, here])
            weights[0:rows, here] = top
            weights[rows:, here] = low

    def outer(first, count, out, add, light):
        cut = 512
        here = slice(first, first + count)
        for start in range(0, wide, cut):
            lanes = slice(start, start + cut)
            if light:
                value = dot_nn(weights[0:rows, here], tops[here, lanes])
            else:
                both = dot_nn(weights[:, here], tops[here, lanes])
                value = both[:rows] + both[rows:] + dot_nn(weights[0:rows, here], lows[here, lanes])
            if add:
                value = value + out[:, lanes]
            out[:, lanes] = value

    def set_lhs(values):
        top, low = halves(values)
        lhs[0:rows, :] = top
        lhs[rows:, :] = low

    def input_gram(light):
        top, low = halves(xin[...])
        xin_top[...] = top
        if light:
            gram[...] = dot_nt(xin_top[...], xin_top[...])
        else:
            xin_low[...] = low
            cross = dot_nt(xin_top[...], xin_low[...])
            gram[...] = dot_nt(xin_top[...], xin_top[...]) + (cross + jnp.transpose(cross))
        gram_copy().start()

    def input_step(light):
        gram_copy().wait()
        square_of = gram[...] + gram_got[...]
        top, low = halves(square_of)
        if light:
            poly = NS_B * square_of + NS_C * dot_nn(top, top)
        else:
            cross = dot_nn(top, low)
            poly = NS_B * square_of + NS_C * (dot_nn(top, top) + (cross + jnp.transpose(cross)))
        top, low = halves(poly)
        cut = 512
        for start in range(0, xin.shape[1], cut):
            lanes = slice(start, start + cut)
            change = dot_nn(top, xin_top[:, lanes])
            if not light:
                change = change + dot_nn(low, xin_top[:, lanes]) + dot_nn(top, xin_low[:, lanes])
            xin[:, lanes] = NS_A * xin[:, lanes] + change

    def by_weight(number, limit, work):
        @pl.when(number < limit)
        def _():
            work(True)

        @pl.when(number >= limit)
        def _():
            work(False)

    def iteration(number, carry):
        turn = number % 2
        values = xs[...]
        largest = jnp.maximum(jnp.max(jnp.abs(values), axis=1, keepdims=True), 1e-30)
        codes[turn, 0] = to_codes(values * (TOP_CODE / largest))
        lane_size = jnp.sum(jnp.where(eye, largest, 0.0), axis=0, keepdims=True)
        sizes[turn, 0] = jnp.broadcast_to(lane_size * (1.0 / TOP_CODE), (8, rows))
        send_all(turn, FIRST)
        for piece in range(3):
            for copy in to_core(turn, 0, piece):
                copy.start()
        send_all(turn, SECOND)
        set_lhs(values)

        def first_pass(index, carry):
            pair = index + (index // 3) * (1 - index // 4) - (index // 4) * (1 - index // 5)

            @pl.when(index == 1)
            def _():
                forward(turn, FIRST, SECOND_ON)
                send_all(turn, THIRD)
                send_all(turn, THIRD_A)

                by_weight(number, LIGHT_IN, input_gram)

                forward(turn, SECOND, THIRD_B)
                forward(turn, SECOND_ON, THIRD_C)

                by_weight(number, LIGHT_IN, input_step)

                forward(turn, THIRD)

            @pl.when(index == 4)
            def _():
                forward(turn, THIRD_A)
                forward(turn, THIRD_B)

            @pl.when(index == 7)
            def _():
                forward(turn, THIRD_C)

            for piece in range(3):
                arrived(turn, 2 * pair + 1, piece)

            def work(light):
                unpack(turn, index, pair, light)
                inner(pl.multiple_of(index * 2 * rows, 2 * rows), 2 * rows, light)

            by_weight(number, LIGHT_HID, work)

            @pl.when(index == 3)
            def _():
                by_weight(number, LIGHT_HID, lambda light: outer(0, wide // 2, us, False, light))

            return carry

        lax.fori_loop(0, 8, first_pass, 0)

        def second_pass(light):
            outer(wide // 2, wide // 2, us, True, light)
            set_lhs(us[...])
            for first in range(0, wide, 512):
                inner(first, 512, light)
            outer(0, wide, vs, False, light)

        by_weight(number, LIGHT_HID, second_pass)
        xs[...] = NS_A * xs[...] + NS_B * us[...] + NS_C * vs[...]
        for move in MOVES:
            for copy in send(turn, move):
                copy.wait_send()
        for pair in range(8):
            for piece in range(3):
                for copy in to_core(turn, 2 * pair, piece):
                    copy.wait_send()
        return carry

    lax.fori_loop(0, NS, iteration, 0)

    place = blk % 4
    copies = []
    for rel, target in ((1, dims[0]), (2, dims[2]), (3, diagonal)):
        copies.append(
            pltpu.make_async_remote_copy(
                src_ref=xs.at[:, pl.ds(pl.multiple_of(target["blk"] * height, height), height)],
                dst_ref=back.at[place],
                send_sem=back_send.at[rel - 1],
                recv_sem=back_recv.at[rel - 1],
                device_id=target,
                device_id_type=MESH,
            )
        )
        copies[-1].start()
    back[place] = xs[:, my_lanes]
    inp_ref[...] = xin[0:deep, my_half]
    for copy in copies:
        copy.wait_recv()
    for number in range(4):
        hid_ref[:, number * rows : (number + 1) * rows] = jnp.transpose(back[number])
    for copy in copies + spread + told:
        copy.wait_send()


def muon(stats, red_hid, mom_hid, red_in, mom_in, red_far, mom_far, wide):
    rows = red_hid.shape[0] // 4
    height = red_hid.shape[1]
    deep, part_wide = red_in.shape
    vmem = pl.BlockSpec(memory_space=pltpu.VMEM)
    sem = pltpu.SemaphoreType.DMA
    return pl.pallas_call(
        muon_kernel,
        out_shape=(
            jax.ShapeDtypeStruct(mom_hid.shape, F32),
            jax.ShapeDtypeStruct(mom_in.shape, F32),
            jax.ShapeDtypeStruct(mom_hid.shape, F32),
            jax.ShapeDtypeStruct(mom_in.shape, F32),
            jax.ShapeDtypeStruct((8, 128), F32),
        ),
        in_specs=[vmem] * 7,
        out_specs=(vmem,) * 5,
        scratch_shapes=[
            pltpu.VMEM((2, 16, rows, wide), I16),
            pltpu.VMEM((2, 16, 8, rows), F32),
            pltpu.VMEM((wide, wide), BF16),
            pltpu.VMEM((wide, wide), BF16),
            pltpu.VMEM((8, wide), F32),
            pltpu.VMEM((2 * rows, wide), BF16),
            pltpu.VMEM((rows, wide), F32),
            pltpu.VMEM((rows, wide), F32),
            pltpu.VMEM((rows, wide), F32),
            pltpu.VMEM((2 * rows, wide), BF16),
            pltpu.VMEM((deep, 2 * part_wide), F32),
            pltpu.VMEM((deep, 2 * part_wide), BF16),
            pltpu.VMEM((deep, 2 * part_wide), BF16),
            pltpu.VMEM((deep, deep), F32),
            pltpu.VMEM((deep, deep), F32),
            pltpu.VMEM((4, rows, height), F32),
            pltpu.VMEM((8, 8, 128), F32),
            pltpu.VMEM((4, 8, 128), F32),
            pltpu.VMEM((4, rows, height), I16),
            pltpu.VMEM((8, rows, height), I16),
            pltpu.VMEM((4, 8, rows), F32),
            pltpu.VMEM((8, 8, rows), F32),
            sem((len(MOVES), 3)),
            sem((8, 5)),
            sem((2, 16, 5)),
            sem((3,)),
            sem((3,)),
            sem((10,)),
            sem((10,)),
            sem((2, 7)),
            sem((2, 7)),
            sem((2,)),
            sem((2,)),
        ],
        compiler_params=pltpu.CompilerParams(
            collective_id=0, has_side_effects=True, vmem_limit_bytes=60 * 1024 * 1024
        ),
    )(stats, red_hid, mom_hid, red_in, mom_in, red_far, mom_far)


def plain_body(
    frames,
    labels,
    mask,
    w_input,
    w_hidden,
    w_output,
    biases,
    mom_input,
    mom_hidden,
    out_first,
    out_second,
    bias_first,
    bias_second,
    res_input,
    res_hidden,
    res_output,
):
    ncol = lax.axis_size("col")
    nblk = lax.axis_size("blk")
    col_index = lax.axis_index("col")
    hcol = w_input.shape[1]
    scol = w_output.shape[1]
    micro = frames.shape[0]
    slot_count = frames.shape[1] * micro * nblk * ncol
    bias_row = biases[0]
    b_one = bias_row[:hcol]
    b_two = bias_row[hcol : 2 * hcol]
    b_out = bias_row[2 * hcol :]
    low_input = w_input.astype(jnp.bfloat16)
    row_tags = jnp.where(mask > 0, labels, -1)
    grad_input = jnp.zeros(w_input.shape, jnp.float32)
    grad_hidden = jnp.zeros((w_hidden.shape[0] * nblk, hcol), jnp.float32)
    grad_output = jnp.zeros((w_output.shape[0] * nblk, scol), jnp.float32)
    grad_bias = jnp.zeros(bias_row.shape, jnp.float32)
    loss_local = jnp.zeros((), jnp.float32)
    for micro_step in range(micro):
        low_hidden, low_output = (
            lax.all_gather(w_hidden.astype(jnp.bfloat16), "blk", axis=0, tiled=True),
            lax.all_gather(w_output.astype(jnp.bfloat16), "blk", axis=0, tiled=True),
        )
        inputs = lax.all_gather(frames[micro_step], "col", axis=0, tiled=True)
        tags_group = lax.all_gather(row_tags[micro_step], "col", axis=0, tiled=True)
        sig_one = jax.nn.sigmoid(matmul(inputs, low_input) + b_one)
        h_one = spread_cols(sig_one.astype(jnp.bfloat16))
        sig_two = jax.nn.sigmoid(matmul(h_one, low_hidden) + b_two)
        h_two = spread_cols(sig_two.astype(jnp.bfloat16))
        logits = matmul(h_two, low_output) + b_out
        row_top = lax.pmax(jnp.max(logits, axis=1), "col")
        exponent = jnp.exp(logits - row_top[:, None])
        target_hit = jnp.arange(scol)[None, :] == (tags_group - col_index * scol)[:, None]
        row_total, picked = lax.psum(
            (jnp.sum(exponent, axis=1), jnp.sum(jnp.where(target_hit, logits, 0.0), axis=1)), "col"
        )
        live_rows = tags_group >= 0
        loss_local = loss_local + jnp.sum(
            jnp.where(live_rows, row_top + jnp.log(row_total) - picked, 0.0)
        )
        probs = exponent / row_total[:, None]
        d_logits = (
            jnp.where(live_rows[:, None], probs - target_hit.astype(jnp.float32), 0.0) / slot_count
        ).astype(jnp.bfloat16)
        grad_output = grad_output + inner_rows(h_two, d_logits)
        d_h_two = reduce_cols(outer_cols(d_logits, low_output))
        d_z_two = (d_h_two * sig_two * (1.0 - sig_two)).astype(jnp.bfloat16)
        grad_hidden = grad_hidden + inner_rows(h_one, d_z_two)
        d_h_one = reduce_cols(outer_cols(d_z_two, low_hidden))
        d_z_one = (d_h_one * sig_one * (1.0 - sig_one)).astype(jnp.bfloat16)
        grad_input = grad_input + inner_rows(inputs, d_z_one)
        grad_bias = grad_bias + jnp.concatenate(
            [
                jnp.sum(d_z_one.astype(jnp.float32), axis=0),
                jnp.sum(d_z_two.astype(jnp.float32), axis=0),
                jnp.sum(d_logits.astype(jnp.float32), axis=0),
            ]
        )
    q_input, next_res_input = squash(grad_input, res_input[0])
    q_hidden, next_res_hidden = squash(grad_hidden, res_hidden[0])
    q_output, next_res_output = squash(grad_output, res_output[0])
    red_hidden, red_output = (
        lax.psum_scatter(q_hidden, "blk", scatter_dimension=0, tiled=True),
        lax.psum_scatter(q_output, "blk", scatter_dimension=0, tiled=True),
    )
    red_input, red_bias, loss_sum = lax.psum((q_input, grad_bias, loss_local), "blk")
    share_blk = 1.0 / nblk
    grad_square = (
        share_blk * (jnp.sum(red_input * red_input) + jnp.sum(red_bias * red_bias))
        + jnp.sum(red_hidden * red_hidden)
        + jnp.sum(red_output * red_output)
    )
    clip_norm = jnp.sqrt(lax.psum(grad_square, ("blk", "col")))
    factor = jnp.minimum(1.0, CLIP / clip_norm)
    next_mom_input = 0.5 * mom_input + factor * red_input
    next_mom_hidden = 0.5 * mom_hidden + factor * red_hidden
    square_input, square_hidden = lax.psum(
        (
            share_blk * jnp.sum(next_mom_input * next_mom_input),
            jnp.sum(next_mom_hidden * next_mom_hidden),
        ),
        ("blk", "col"),
    )
    iter_input = next_mom_input / (jnp.sqrt(square_input) + 1e-07)
    iter_hidden = next_mom_hidden / (jnp.sqrt(square_hidden) + 1e-07)
    for turn_index in range(NS):
        rows_hidden = collect_rows(iter_hidden)
        gram_input, gram_hidden = lax.psum(
            (precise(iter_input, iter_input.T), precise(iter_hidden, rows_hidden.T)), "col"
        )
        image_input = precise(gram_input, iter_input)
        image_hidden = precise(gram_hidden, rows_hidden)
        iter_input = (
            NS_A * iter_input + NS_B * image_input + NS_C * precise(gram_input, image_input)
        )
        iter_hidden = (
            NS_A * iter_hidden
            + NS_B * image_hidden
            + NS_C * precise(gram_hidden, collect_rows(image_hidden))
        )
    muon_scale = LR_MUON * 0.2 * math.sqrt(hcol * ncol)
    new_input = w_input * (1.0 - LR_MUON * WD_MUON) - muon_scale * iter_input
    new_hidden = w_hidden * (1.0 - LR_MUON * WD_MUON) - muon_scale * iter_hidden
    new_output, next_out_first, next_out_second = adam_step(
        w_output, factor * red_output, out_first, out_second
    )
    new_biases, next_bias_first, next_bias_second = adam_step(
        biases, factor * red_bias[None, :], bias_first, bias_second
    )
    return (
        loss_sum,
        clip_norm,
        new_input,
        new_hidden,
        new_output,
        new_biases,
        next_mom_input,
        next_mom_hidden,
        next_out_first,
        next_out_second,
        next_bias_first,
        next_bias_second,
        next_res_input[None],
        next_res_hidden[None],
        next_res_output[None],
    )


def fast_body(
    frames,
    labels,
    mask,
    w_input,
    w_hidden,
    w_output,
    biases,
    mom_input,
    mom_hidden,
    out_first,
    out_second,
    bias_first,
    bias_second,
    res_input,
    res_hidden,
    res_output,
):
    ncol = lax.axis_size("col")
    nblk = lax.axis_size("blk")
    col_index = lax.axis_index("col")
    blk_index = lax.axis_index("blk")
    hcol = w_input.shape[1]
    scol = w_output.shape[1]
    micro = frames.shape[0]
    slot_count = frames.shape[1] * micro * nblk * ncol
    bias_row = biases[0]
    deep = w_input.shape[0]
    rows_out = OUT_GROUPS * OUT_ROWS
    inputs, h_one, h_two, slope_one, slope_two, low_hidden, low_output, mom_far, d_logits, vec = (
        forward_pass(
            frames.reshape(-1, deep),
            labels,
            mask,
            w_input,
            w_hidden,
            w_output.T,
            biases,
            mom_input,
            slot_count,
        )
    )
    partial = inner_rows(d_logits, low_output)
    next_out, codes, sizes = squash_out(d_logits, h_two, res_output[0].T)
    next_hid, next_in, red_out, red_hid, red_in, red_far, vec_sum, stats = reduce_grads(
        codes,
        sizes,
        h_one,
        inputs,
        partial,
        slope_two,
        slope_one,
        low_hidden,
        res_hidden[0],
        res_input[0],
        vec,
        scol,
        deep,
    )
    next_res_output = next_out.transpose(1, 2, 0)
    vec_sum = vec_sum.reshape(-1)
    red_bias = vec_sum[: bias_row.shape[0]]
    loss_sum = vec_sum[bias_row.shape[0]]
    done_hidden, done_input, next_mom_hidden, next_mom_input, norms = muon(
        stats,
        red_hid,
        mom_hidden,
        red_in,
        mom_input,
        red_far,
        mom_far,
        hcol * ncol,
    )
    clip_norm = norms[0, 0]
    factor = norms[4, 0]
    muon_scale = LR_MUON * 0.2 * math.sqrt(hcol * ncol)
    new_input = w_input * (1.0 - LR_MUON * WD_MUON) - muon_scale * done_input
    new_hidden = w_hidden * (1.0 - LR_MUON * WD_MUON) - muon_scale * done_hidden
    new_output, next_out_first, next_out_second = adam_step(
        w_output, factor * red_out[:scol].T, out_first, out_second
    )
    new_biases, next_bias_first, next_bias_second = adam_step(
        biases, factor * red_bias[None, :], bias_first, bias_second
    )
    return (
        loss_sum,
        clip_norm,
        new_input,
        new_hidden,
        new_output,
        new_biases,
        next_mom_input,
        next_mom_hidden,
        next_out_first,
        next_out_second,
        next_bias_first,
        next_bias_second,
        next_in[None],
        next_hid[None],
        next_res_output,
    )


def solution(mesh):
    in_specs = (
        P(None, ("blk", "col"), None),
        P(None, ("blk", "col")),
        P(None, ("blk", "col")),
        P(None, "col"),
        P("blk", "col"),
        P("blk", "col"),
        P("col", None),
        P(None, "col"),
        P("blk", "col"),
        P("blk", "col"),
        P("blk", "col"),
        P("col", None),
        P("col", None),
        P("blk", None, "col"),
        P("blk", None, "col"),
        P("blk", None, "col"),
    )
    out_specs = (
        P(),
        P(),
        P(None, "col"),
        P("blk", "col"),
        P("blk", "col"),
        P("col", None),
        P(None, "col"),
        P("blk", "col"),
        P("blk", "col"),
        P("blk", "col"),
        P("col", None),
        P("col", None),
        P("blk", None, "col"),
        P("blk", None, "col"),
        P("blk", None, "col"),
    )
    cubes = mesh.shape["blk"] == 8 and mesh.shape["col"] == 4
    body = fast_body if cubes else plain_body
    return jax.shard_map(body, mesh=mesh, in_specs=in_specs, out_specs=out_specs, check_vma=False)
```
